32 devices in a mesh: dp: 32 (over z, y, x, core).
Axes of the slice: x: 2, y: 2, z: 4, core: 2. Of those that a mesh axis runs over, the one named last changes fastest.
Arguments:
- actions: float32 [16384, 256], P('dp'), may hold values from -6 to 6
- observed: bfloat16 [1024, 196, 256], P('dp'), may hold values from -6 to 6
- camera_flags: int32 [1024], P('dp'), may hold values 0 or 1
- noise_levels: int32 [1024], P('dp'), may hold values from 0 to 99
- cotangent: float32 [16384, 256], P('dp'), may hold values from -6 to 6
- square_weights: float32 [5, 256, 256], P(None, 'dp'), may hold values from -2 to 2
- mlp_weights: float32 [2, 256, 1024], P(None, 'dp'), may hold values from -0.25 to 0.25
- gains: float32 [2, 256], P(None, 'dp'), may hold values from 0.5 to 1.5
- square_moment: float32 [5, 256, 256], P(None, 'dp'), may hold values from -563.2 to 563.2
- mlp_moment: float32 [2, 256, 1024], P(None, 'dp'), may hold values from -307.2 to 307.2
- gain_moment: float32 [2, 256], P(None, 'dp'), may hold values from -640 to 640
Outputs:
- output: float32 [16384, 256], P('dp')
- actions_grad: float32 [16384, 256], P('dp')
- observed_grad: float32 [1024, 196, 256], P('dp')
- square_grad: float32 [5, 256, 256], P(None, 'dp')
- square_moment_new: float32 [5, 256, 256], P(None, 'dp')
- updated_square_projections: float32 [5, 256, 256], P(None, 'dp')
- square_copy: bfloat16 [5, 256, 256], P(None, 'dp')
- mlp_grad: float32 [2, 256, 1024], P(None, 'dp')
- mlp_moment_new: float32 [2, 256, 1024], P(None, 'dp')
- mlp_new: float32 [2, 256, 1024], P(None, 'dp')
- mlp_copy: bfloat16 [2, 256, 1024], P(None, 'dp')
- gain_grad: float32 [2, 256], P(None, 'dp')
- gain_moment_new: float32 [2, 256], P(None, 'dp')
- gains_new: float32 [2, 256], P(None, 'dp')
The draws below stay inside these ranges and needn't reach their ends.
All inputs are finite; a program needn't handle non-finite values. No bound on the sum of `camera_flags` on one device may be relied on, other than what follows from the above.
Results may differ from the reference program's by a relative error of at most 0.013.
Values may be sent and summed in bfloat16 or wider, within the bound.
A program may use at most 128 MiB of HBM per device.

```python
import math
import jax
import jax.numpy as jnp
from jax import lax

D = 256
HEADS = 4
FF = 1024
HEAD_DIM = 64
ACT = 16
OBS_FULL = 196
OBS_FEW = 49
KEYS = 197
SAMP_DEV = 32
SAMPLES = 1024
TOKENS = 16384


def scaled_normal(key, shape, scales):
    values = jax.random.truncated_normal(key, -4.0, 4.0, shape, jnp.float32)
    return values * scales


def draw_square_weights(key, part):
    key = jax.random.fold_in(key, 11)
    scales = jnp.array([1.0, 1.0, 1.0, 1.0, 8.0], jnp.float32)[:, None, None] * D ** (-0.5)
    return scaled_normal(key, (5, D, D), scales)


def draw_mlp_weights(key, part):
    key = jax.random.fold_in(key, 12)
    scales = jnp.array([D ** (-0.5), FF ** (-0.5)], jnp.float32)[:, None, None]
    return scaled_normal(key, (2, D, FF), scales)


def draw_square_moment(key, part):
    key = jax.random.fold_in(key, 13)
    scales = jnp.array([0.1, 1.0, 1.1, 1.1, 0.15], jnp.float32)[:, None, None] * TOKENS ** 0.5
    return scaled_normal(key, (5, D, D), scales)


def draw_mlp_moment(key, part):
    key = jax.random.fold_in(key, 14)
    scales = jnp.array([0.3, 0.6], jnp.float32)[:, None, None] * TOKENS ** 0.5
    return scaled_normal(key, (2, D, FF), scales)


def plant(entries, own_key, low, largest):
    dims = entries.shape
    place = [jax.random.randint(jax.random.fold_in(own_key, axis), (), 0, dims[axis]) for axis in range(len(dims))]
    entries = entries.at[tuple(place)].set(low)
    longest = dims.index(max(dims))
    place[longest] = (place[longest] + 1) % dims[longest]
    return entries.at[tuple(place)].set(largest)


def shard_levels(stream_key, dims, cuts, least, largest):
    factor_of, own = 1.0, jax.random.fold_in(stream_key, 6)
    for axis_at, shards_of in cuts:
        draws = jnp.exp(jax.random.uniform(jax.random.fold_in(own, axis_at), (shards_of,), jnp.float32, least / len(cuts), largest / len(cuts)))
        factor_of = factor_of * jnp.repeat(draws, dims[axis_at] // shards_of).reshape([-1 if axis == axis_at else 1 for axis in range(len(dims))])
    return factor_of


def normal_values(stream_key, extent, deviation, reach, cuts=(), held_as=jnp.bfloat16):
    result = jax.random.normal(stream_key, extent, jnp.float32) * deviation
    if len(cuts) > 0:
        result = shard_levels(stream_key, extent, cuts, -0.22, 0.18) * result
    return jnp.clip(result, min=-reach, max=reach).astype(held_as)


def setup_inputs(seed: int = 0) -> dict:
    streams_of = jax.random.split(jax.random.key(seed), 12)
    actions = normal_values(streams_of[0], (TOKENS, D), 1.0, 6.0, ((0, 32),), jnp.float32)
    observed = normal_values(streams_of[1], (SAMPLES, OBS_FULL, D), 1.0, 6.0, ((0, 32),))
    camera_flags = plant((jax.random.randint(streams_of[2], (SAMPLES,), 0, 2) < 1).astype(jnp.int32), jax.random.fold_in(streams_of[2], 1), 0, 1)
    noise_levels = plant(jax.random.randint(streams_of[3], (SAMPLES,), 0, 100), jax.random.fold_in(streams_of[3], 1), 0, 99).astype(jnp.int32)
    cotangent = normal_values(streams_of[4], (TOKENS, D), 1.0, 6.0, ((0, 32),), jnp.float32)
    square_weights = draw_square_weights(jax.random.fold_in(streams_of[11], 71), 0)
    mlp_weights = draw_mlp_weights(jax.random.fold_in(streams_of[11], 71), 0)
    gains = jnp.clip(1.0 + 0.1 * jax.random.normal(streams_of[7], (2, D), jnp.float32), 0.5, 1.5)
    square_moment = draw_square_moment(jax.random.fold_in(streams_of[11], 71), 0)
    mlp_moment = draw_mlp_moment(jax.random.fold_in(streams_of[11], 71), 0)
    gain_moment = normal_values(streams_of[10], (2, D), (0.8 * TOKENS ** 0.5), 640.0, ((1, 32),), jnp.float32)
    return dict(actions=actions, observed=observed, camera_flags=camera_flags, noise_levels=noise_levels, cotangent=cotangent, square_weights=square_weights, mlp_weights=mlp_weights, gains=gains, square_moment=square_moment, mlp_moment=mlp_moment, gain_moment=gain_moment)


@jax.custom_vjp
def low(v):
    return lax.optimization_barrier(v.astype(jnp.bfloat16)).astype(jnp.float32)

@jax.custom_vjp
def low_back(v):
    return v

def low_keep(v):
    return (low(v), None)

def low_pass(kept, grad):
    return (grad,)

def back_keep(v):
    return (v, None)

def back_low(kept, grad):
    return (low(grad),)
low.defvjp(low_keep, low_pass)
low_back.defvjp(back_keep, back_low)
HIGH_PRECISION = lax.Precision.HIGHEST
COEF_A = 3.4445
COEF_B = -4.775
COEF_C = 2.0315

def forward_and_backward(values):
    return low(low_back(values))

def sinusoid(levels, width):
    half = width // 2
    freqs = jnp.exp(-math.log(10000.0) * jnp.arange(half, dtype=jnp.float32) / half)
    angle = levels.astype(jnp.float32)[:, None] * freqs[None, :]
    return jnp.concatenate([jnp.sin(angle), jnp.cos(angle)], axis=-1)

def layer_norm(values, gain):
    centred = values - lax.optimization_barrier(jnp.mean(values, -1, keepdims=True))
    spread = lax.optimization_barrier(jnp.mean(centred * centred, -1, keepdims=True))
    return centred * lax.rsqrt(spread + 1e-05) * gain

def gelu_tanh(values):
    return 0.5 * values * (1.0 + jnp.tanh(0.7978845608 * (values + 0.044715 * values * values * values)))

def orthogonalize(matrix):
    current = matrix / (jnp.sqrt(jnp.sum(matrix * matrix)) + 1e-07)
    for turn in range(5):
        gram = jnp.dot(current, current.T, precision=HIGH_PRECISION)
        poly = COEF_B * gram + COEF_C * jnp.dot(gram, gram, precision=HIGH_PRECISION)
        current = COEF_A * current + jnp.dot(poly, current, precision=HIGH_PRECISION)
    return current

def block_forward(square_reduced_precision, mlp_low, gain_full, acts, obs, counts, embed):
    batch = acts.shape[0]
    first = low(layer_norm(acts, gain_full[0]))
    queries = forward_and_backward(jnp.einsum('bad,de->bae', first, square_reduced_precision[1], precision=HIGH_PRECISION))
    stamp = forward_and_backward(jnp.einsum('bd,de->be', embed, square_reduced_precision[0], precision=HIGH_PRECISION))
    context_memory = jnp.concatenate([stamp[:, None, :], obs], axis=1)
    gathered_keys = forward_and_backward(jnp.einsum('rjv,vf->rjf', context_memory, square_reduced_precision[2], precision=HIGH_PRECISION))
    gathered_values = forward_and_backward(jnp.einsum('rjv,vf->rjf', context_memory, square_reduced_precision[3], precision=HIGH_PRECISION))
    query_heads = queries.reshape(batch, ACT, HEADS, HEAD_DIM)
    key_heads = gathered_keys.reshape(batch, KEYS, HEADS, HEAD_DIM)
    value_heads = gathered_values.reshape(batch, KEYS, HEADS, HEAD_DIM)
    scores = jnp.einsum('bqhd,bkhd->bhqk', query_heads, key_heads, precision=HIGH_PRECISION) * 0.125
    position = jnp.arange(KEYS)[None, :]
    valid = position <= counts[:, None]
    scores = jnp.where(valid[:, None, None, :], scores, -1000000000.0)
    scores = low_back(scores)
    top = lax.optimization_barrier(jnp.max(scores, -1, keepdims=True))
    expo = jnp.exp(scores - top)
    probs = expo / lax.optimization_barrier(jnp.sum(expo, -1, keepdims=True))
    mixed = jnp.einsum('bhqk,bkhd->bqhd', low(probs), value_heads, precision=HIGH_PRECISION)
    mixed = forward_and_backward(mixed.reshape(batch, ACT, D))
    branch = low_back(jnp.einsum('bad,de->bae', mixed, square_reduced_precision[4], precision=HIGH_PRECISION))
    resid = acts + branch
    second = low(layer_norm(resid, gain_full[1]))
    hidden = low_back(jnp.einsum('bad,df->baf', second, mlp_low[0], precision=HIGH_PRECISION))
    active = low(gelu_tanh(hidden))
    update = low_back(jnp.einsum('baf,df->bad', active, mlp_low[1], precision=HIGH_PRECISION))
    return resid + update

def reference(actions, observed, camera_flags, noise_levels, cotangent, square_weights, mlp_weights, gains, square_moment, mlp_moment, gain_moment):
    counts = OBS_FEW + (OBS_FULL - OBS_FEW) * camera_flags
    embed = low(sinusoid(noise_levels, D))
    blocks = SAMPLES // SAMP_DEV

    def forward_block_pass(square_full, mlp_full, gain_full, acts, obs):
        square_reduced_precision = low(square_full)
        mlp_low = low(mlp_full)

        def run(piece):
            return jax.checkpoint(block_forward)(square_reduced_precision, mlp_low, gain_full, *piece)
        stacked = (acts.reshape(blocks, SAMP_DEV, ACT, D), obs.reshape(blocks, SAMP_DEV, OBS_FULL, D), counts.reshape(blocks, SAMP_DEV), embed.reshape(blocks, SAMP_DEV, D))
        return lax.map(run, stacked).reshape(TOKENS, D)
    output, pullback = jax.vjp(forward_block_pass, square_weights, mlp_weights, gains, actions, observed.astype(jnp.float32))
    square_grad, mlp_grad, gain_grad, actions_grad, observed_grad = pullback(cotangent)
    square_moment_new = 0.5 * square_moment + square_grad
    mlp_moment_new = 0.5 * mlp_moment + mlp_grad
    gain_moment_new = 0.5 * gain_moment + gain_grad
    square_ortho = jnp.stack([orthogonalize(square_moment_new[index]) for index in range(5)])
    mlp_ortho = jnp.stack([orthogonalize(mlp_moment_new[index]) for index in range(2)])
    square_rates = jnp.array([0.5, 0.5, 0.5, 0.5, 4.0], jnp.float32)
    mlp_rates = jnp.array([1.0, 0.5], jnp.float32)
    updated_square_projections = square_weights - square_rates[:, None, None] * square_ortho
    mlp_new = mlp_weights - mlp_rates[:, None, None] * mlp_ortho
    gains_new = gains - 0.1 / math.sqrt(TOKENS) * gain_moment_new
    return (output, actions_grad, observed_grad, square_grad, square_moment_new, updated_square_projections, updated_square_projections.astype(jnp.bfloat16), mlp_grad, mlp_moment_new, mlp_new, mlp_new.astype(jnp.bfloat16), gain_grad, gain_moment_new, gains_new)
```

```python
import functools
import math

import jax
import jax.numpy as jnp
from jax import lax
from jax.experimental import pallas as pl
from jax.experimental.pallas import tpu as pltpu
from jax.sharding import PartitionSpec as P

HEADS = 4
ACT = 16
OBS_FULL = 196
OBS_FEW = 49
COEF_A = 3.4445
COEF_B = -4.775
COEF_C = 2.0315
F32 = jnp.float32
BF16 = jnp.bfloat16
MESH = pl.DeviceIdType.MESH
VMEM = pltpu.VMEM
NN = (((1,), (0,)), ((), ()))
NT = (((1,), (1,)), ((), ()))
TN = (((0,), (0,)), ((), ()))

LANES = 128
TILE = 8
MLP_ROWS = 64
SQ_ROWS = 16
SQ_BASE = 2 * MLP_ROWS
GAIN_BASE = SQ_BASE + 5 * SQ_ROWS
WIRE = GAIN_BASE + 16
CHUNKS = ((0, 64), (64, 64), (128, 48), (176, 48))
MLP_RATES = (1.0, 0.5)
SQ_RATES = (0.5, 0.5, 0.5, 0.5, 4.0)
GRID = (4, 2, 2, 2)
OWNERS = (8, 22, 14, 16, 11, 21, 13)


def dot(left, right, dims=NN):
    return lax.dot_general(left, right, dims, preferred_element_type=F32)


def place():
    me = lax.axis_index("dp")
    return me, me // 8, (me // 4) % 2, (me // 2) % 2, me % 2


def device_at(z, y, x, c):
    return ((z * 2 + y) * 2 + x) * 2 + c


def link(src, dst, send, recv, device):
    return pltpu.make_async_remote_copy(
        src_ref=src,
        dst_ref=dst,
        send_sem=send,
        recv_sem=recv,
        device_id=(device,),
        device_id_type=MESH,
    )


def greet(device):
    pl.semaphore_signal(
        pltpu.get_barrier_semaphore(), inc=1, device_id=(device,), device_id_type=MESH
    )


def greet_partners(z, y, x, c):
    greet(device_at(z, y, x, 1 - c))
    greet(device_at(z, y, 1 - x, c))
    greet(device_at(z, 1 - y, x, c))
    for step in range(1, 4):
        greet(device_at((z + step) % 4, y, x, c))


def gather_kernel(sq_ref, mlp_ref, gain_ref, sq_out, mlp_out, gain_out, wire, edge, send, recv):
    me, z, y, x, c = place()
    greet_partners(z, y, x, c)
    for m in range(2):
        for j in range(4):
            pair = [mlp_ref[m, :, pl.ds((2 * j + k) * LANES, LANES)] for k in range(2)]
            rows = pl.ds(m * MLP_ROWS + j * 16, 16)
            wire[z, y, x, c, rows, :] = jnp.concatenate(pair, axis=0).astype(BF16)
    for m in range(5):
        pair = [sq_ref[m, :, pl.ds(k * LANES, LANES)] for k in range(2)]
        rows = pl.ds(SQ_BASE + m * SQ_ROWS, 16)
        wire[z, y, x, c, rows, :] = jnp.concatenate(pair, axis=0).astype(BF16)
    gains = gain_ref[...]
    high = gains.astype(BF16).astype(F32)
    middle = (gains - high).astype(BF16).astype(F32)
    low = (gains - high - middle).astype(BF16).astype(F32)
    edge[...] = jnp.zeros_like(edge)
    edge[0:2, 0:TILE] = high
    edge[2:4, 0:TILE] = middle
    edge[4:6, 0:TILE] = low
    wire[z, y, x, c, pl.ds(GAIN_BASE, 16), :] = edge[...].astype(BF16)
    pl.semaphore_wait(pltpu.get_barrier_semaphore(), 6)

    def along_z(k, step):
        rows = pl.ds(*CHUNKS[k])
        mine = wire.at[z, y, x, c, rows]
        return link(mine, mine, send.at[k, step], recv.at[k, step], device_at((z + step + 1) % 4, y, x, c))

    def from_z(k, step):
        rows = pl.ds(*CHUNKS[k])
        there = wire.at[(z + 3 - step) % 4, y, x, c, rows]
        return link(there, there, send.at[k, step], recv.at[k, step], device_at((z + 3 - step) % 4, y, x, c))

    def second(k, px, py):
        rows = pl.ds(*CHUNKS[k])
        if k % 2 == 0:
            part, to = wire.at[:, y, px, c, rows], device_at(z, y, 1 - x, c)
        else:
            part, to = wire.at[:, py, x, c, rows], device_at(z, 1 - y, x, c)
        return link(part, part, send.at[k, 3], recv.at[k, 3], to)

    def third(k, px, py):
        rows = pl.ds(*CHUNKS[k])
        if k % 2 == 0:
            part, to = wire.at[:, py, :, c, rows], device_at(z, 1 - y, x, c)
        else:
            part, to = wire.at[:, :, px, c, rows], device_at(z, y, 1 - x, c)
        return link(part, part, send.at[k, 4], recv.at[k, 4], to)

    def fourth(k, pc):
        rows = pl.ds(*CHUNKS[k])
        part = wire.at[:, :, :, pc, rows]
        return link(part, part, send.at[k, 5], recv.at[k, 5], device_at(z, y, x, 1 - c))

    number = len(CHUNKS)
    order = (2, 3, 0, 1)
    for k in order:
        for step in range(3):
            along_z(k, step).start()
    for k in order:
        for step in range(3):
            from_z(k, step).wait_recv()
        second(k, x, y).start()
    for k in order:
        second(k, 1 - x, 1 - y).wait_recv()
        third(k, x, y).start()
    for k in order:
        third(k, 1 - x, 1 - y).wait_recv()
        fourth(k, c).start()
    for k in order:
        fourth(k, 1 - c).wait_recv()
        if k < 2:
            for j in range(4):
                block = wire[:, :, :, :, pl.ds(k * MLP_ROWS + j * 16, 16), :].reshape(32, 16, LANES).astype(F32)
                for half in range(2):
                    columns = pl.ds((2 * j + half) * LANES, LANES)
                    mlp_out[k, :, columns] = block[:, half * 8 : half * 8 + 8, :].reshape(256, LANES).astype(BF16)
        else:
            for m in ((0, 1, 2), (3, 4))[k - 2]:
                block = wire[:, :, :, :, pl.ds(SQ_BASE + m * SQ_ROWS, 16), :].reshape(32, 16, LANES).astype(F32)
                for half in range(2):
                    columns = pl.ds(half * LANES, LANES)
                    sq_out[m, :, columns] = block[:, half * 8 : half * 8 + 8, :].reshape(256, LANES).astype(BF16)
    for half in range(2):
        total = jnp.zeros((16, LANES), F32)
        for at in range(16):
            d = half * 16 + at
            tile = wire[d // 8, (d // 4) % 2, (d // 2) % 2, d % 2, pl.ds(GAIN_BASE, 16), :].astype(F32)
            total = total + (tile if at == 0 else pltpu.roll(tile, at * TILE, 1))
        edge[...] = total
        gain_out[:, pl.ds(half * LANES, LANES)] = edge[0:2, :] + edge[2:4, :] + edge[4:6, :]
    for k in range(number):
        for step in range(3):
            along_z(k, step).wait_send()
        second(k, x, y).wait_send()
        third(k, x, y).wait_send()
        fourth(k, c).wait_send()


def gather_weights(square_weights, mlp_weights, gains):
    spec = pl.BlockSpec(memory_space=VMEM)
    return pl.pallas_call(
        gather_kernel,
        out_shape=(
            jax.ShapeDtypeStruct((5, 256, 256), BF16),
            jax.ShapeDtypeStruct((2, 256, 1024), BF16),
            jax.ShapeDtypeStruct((2, 256), F32),
        ),
        in_specs=[spec] * 3,
        out_specs=[spec] * 3,
        scratch_shapes=[
            VMEM(GRID + (WIRE, LANES), BF16),
            VMEM((16, LANES), F32),
            pltpu.SemaphoreType.DMA((4, 6)),
            pltpu.SemaphoreType.DMA((4, 6)),
        ],
        compiler_params=pltpu.CompilerParams(
            collective_id=0, has_side_effects=True, vmem_limit_bytes=24 << 20
        ),
        name="gather_weights",
    )(square_weights, mlp_weights, gains)


KEYS_PAD = 208
GROUP = 4
ROWS = 256


def block_kernel(
    acts_ref, cot_ref, obs_ref, flags_ref, levels_ref, sq_ref, mlp_ref, gain_ref,
    out_ref, ag_ref, og_ref, grad_ref,
    mem, tail, og, wkh, wvh, q_s, qp, p_s, u_s, dup, dq_s, first_s, xhat, rstd, mixed_s, second_s,
    act_s, dh_s, outlow_s, rl_s, gm_s, angle, embed_s, stamp_s, dres_s, gain_acc, sems,
):
    samples = obs_ref.shape[0]
    tokens = acts_ref.shape[0]
    width = acts_ref.shape[1]
    wide = mlp_ref.shape[2]
    head_dim = width // HEADS
    half = width // 2

    lane = lax.broadcasted_iota(jnp.int32, (width, width), 1)
    for h in range(HEADS):
        inside = lane // head_dim == h
        block = pl.ds(h * width, width)
        wkh[block, :] = jnp.where(inside, sq_ref[2].astype(F32), 0.0).astype(BF16)
        wvh[block, :] = jnp.where(inside, sq_ref[3].astype(F32), 0.0).astype(BF16)

    freqs = jnp.exp(
        lax.broadcasted_iota(jnp.int32, (1, half), 1).astype(F32) * F32(-math.log(10000.0)) / half
    )
    for s in range(samples):
        angle[s : s + 1, :] = levels_ref[s].astype(F32) * freqs
    embed_s[:, 0:half] = jnp.sin(angle[...]).astype(BF16)
    embed_s[:, half:width] = jnp.cos(angle[...]).astype(BF16)
    stamp = dot(embed_s[...], sq_ref[0]).astype(BF16).astype(F32)
    tail[...] = jnp.zeros_like(tail)
    for s in range(samples):
        tail[s, 0:4, :] = obs_ref[s, 192:196, :].astype(F32)
        tail[s, 4:5, :] = stamp[s : s + 1, :]

    def fill(s, _):
        mem[s, 0:192, :] = obs_ref[s, 0:192, :]
        mem[s, 192:208, :] = tail[s].astype(BF16)
        return 0

    lax.fori_loop(0, samples, fill, 0)

    g1 = gain_ref[0:1, :]
    g2 = gain_ref[1:2, :]

    def normalize(values):
        centred = values - jnp.mean(values, -1, keepdims=True)
        scale = lax.rsqrt(jnp.mean(centred * centred, -1, keepdims=True) + 1e-05)
        return centred * scale, scale

    def norm_back(grad, hat, scale):
        mean_one = jnp.mean(grad, -1, keepdims=True)
        mean_two = jnp.mean(grad * hat, -1, keepdims=True)
        return scale * (grad - mean_one - hat * mean_two)

    per = ROWS // ACT

    def make_queries(r, _):
        rows = pl.ds(pl.multiple_of(r * ROWS, ROWS), ROWS)
        hat, scale = normalize(acts_ref[rows, :])
        xhat[rows, :] = hat
        rstd[rows, :] = scale
        first = (hat * g1).astype(BF16)
        first_s[rows, :] = first
        q = dot(first, sq_ref[1]).astype(BF16)
        q_s[rows, :] = q
        here = pl.ds(r * per, per)
        for h in range(HEADS):
            wk = wkh[pl.ds(h * width, width), :]
            qp[here, pl.ds(h * ACT, ACT), :] = (dot(q, wk, NT) * 0.125).astype(BF16).reshape(per, ACT, width)
        return 0

    lax.fori_loop(0, tokens // ROWS, make_queries, 0)

    key = lax.broadcasted_iota(jnp.int32, (HEADS * ACT, KEYS_PAD), 1)

    def attend(g, _):
        ids = [g * GROUP + k for k in range(GROUP)]
        scores = [dot(qp[s], mem[s], NT) for s in ids]
        lows = []
        for s, score in zip(ids, scores):
            count = OBS_FEW + (OBS_FULL - OBS_FEW) * flags_ref[s]
            score = jnp.where((key < count) | (key == OBS_FULL), score, -1000000000.0)
            expo = jnp.exp(score - jnp.max(score, -1, keepdims=True))
            probs = expo / jnp.sum(expo, -1, keepdims=True)
            p_s[s] = probs
            lows.append(probs.astype(BF16))
        for s, low in zip(ids, lows):
            u = dot(low, mem[s]).astype(BF16)
            rows = pl.ds(pl.multiple_of(s * ACT, ACT), ACT)
            for h in range(HEADS):
                u_s[rows, pl.ds(h * width, width)] = u[h * ACT : (h + 1) * ACT, :]
        return 0

    lax.fori_loop(0, samples // GROUP, attend, 0)

    gain_acc[...] = jnp.zeros_like(gain_acc)

    def feed(r, _):
        rows = pl.ds(pl.multiple_of(r * ROWS, ROWS), ROWS)
        mixed = dot(u_s[rows, :], wvh[...]).astype(BF16)
        mixed_s[rows, :] = mixed
        resid = acts_ref[rows, :] + dot(mixed, sq_ref[4])
        hat, scale = normalize(resid)
        second = (hat * g2).astype(BF16)
        second_s[rows, :] = second
        cot = cot_ref[rows, :]
        out_low = cot.astype(BF16)
        outlow_s[rows, :] = out_low
        for c in range(wide // 256):
            columns = pl.ds(c * 256, 256)
            v = dot(second, mlp_ref[0, :, columns])
            square = v * v
            t = jnp.tanh(0.7978845608 * (v + 0.044715 * square * v))
            act_s[rows, columns] = (0.5 * v * (1.0 + t)).astype(BF16)
            slope = 0.5 * (1.0 + t) + 0.5 * v * (1.0 - t * t) * (0.7978845608 * (1.0 + 0.134145 * square))
            dh_s[rows, columns] = (slope * dot(out_low, mlp_ref[1, :, columns])).astype(BF16)
        out_ref[rows, :] = resid + dot(act_s[rows, :], mlp_ref[1], NT)
        grad_second = dot(dh_s[rows, :], mlp_ref[0], NT)
        gain_acc[1:2, :] += jnp.sum(grad_second * hat, 0, keepdims=True)
        dres = cot + norm_back(grad_second * g2, hat, scale)
        dres_s[rows, :] = dres
        low = dres.astype(BF16)
        rl_s[rows, :] = low
        gm = dot(low, sq_ref[4], NT).astype(BF16)
        gm_s[rows, :] = gm
        here = pl.ds(r * per, per)
        for h in range(HEADS):
            wv = wvh[pl.ds(h * width, width), :]
            dup[here, pl.ds(h * ACT, ACT), :] = dot(gm, wv, NT).astype(BF16).reshape(per, ACT, width)
        return 0

    lax.fori_loop(0, tokens // ROWS, feed, 0)

    def attend_back(g, _):
        ids = [g * GROUP + k for k in range(GROUP)]
        grads = [dot(dup[s], mem[s], NT) for s in ids]
        pairs = []
        for s, grad in zip(ids, grads):
            probs = p_s[s]
            both = probs * grad
            dscore = (both - probs * jnp.sum(both, -1, keepdims=True)).astype(BF16)
            pairs.append((probs.astype(BF16), dscore))
        for s, (low, dscore) in zip(ids, pairs):
            dq = (dot(dscore, mem[s]) * 0.125).astype(BF16)
            rows = pl.ds(pl.multiple_of(s * ACT, ACT), ACT)
            for h in range(HEADS):
                dq_s[rows, pl.ds(h * width, width)] = dq[h * ACT : (h + 1) * ACT, :]
            both = jnp.concatenate([low, dscore], axis=0)
            sides = jnp.concatenate([dup[s], qp[s]], axis=0)
            dmem = dot(both, sides, TN)
            og[s] = dmem[0:OBS_FULL, :]
            stamp_s[s] = dmem[192:200, :]
        block = pl.ds(g * GROUP, GROUP)
        pltpu.make_async_copy(og.at[block], og_ref.at[block], sems.at[g]).start()
        return 0

    lax.fori_loop(0, samples // GROUP, attend_back, 0)

    def put(base, tiles, value):
        blocks = value.shape[0] // TILE
        for j in range(tiles):
            part = value[:, j * LANES : (j + 1) * LANES].reshape(blocks, TILE, LANES)
            grad_ref[:, pl.ds(base + j * TILE, TILE), :] = part

    put(0, 8, dot(second_s[...], dh_s[...], TN))
    put(MLP_ROWS, 8, dot(outlow_s[...], act_s[...], TN))
    put(SQ_BASE + 4 * SQ_ROWS, 2, dot(mixed_s[...], rl_s[...], TN))

    def by_head(left, right):
        turned = left.T
        parts = [
            dot(turned[h * head_dim : (h + 1) * head_dim, :], right[:, pl.ds(h * width, width)])
            for h in range(HEADS)
        ]
        return jnp.concatenate(parts, axis=0).T

    put(SQ_BASE + 3 * SQ_ROWS, 2, by_head(gm_s[...], u_s))
    put(SQ_BASE + 2 * SQ_ROWS, 2, by_head(q_s[...], dq_s))

    def queries_back(r, _):
        rows = pl.ds(pl.multiple_of(r * ROWS, ROWS), ROWS)
        dq = dot(dq_s[rows, :], wkh[...]).astype(BF16)
        rl_s[rows, :] = dq
        grad_first = dot(dq, sq_ref[1], NT)
        hat = xhat[rows, :]
        gain_acc[0:1, :] += jnp.sum(grad_first * hat, 0, keepdims=True)
        ag_ref[rows, :] = dres_s[rows, :] + norm_back(grad_first * g1, hat, rstd[rows, :])
        return 0

    lax.fori_loop(0, tokens // ROWS, queries_back, 0)
    put(SQ_BASE + SQ_ROWS, 2, dot(first_s[...], rl_s[...], TN))
    stamp_low = stamp_s[:, 4:5, :].reshape(samples, width).astype(BF16)
    put(SQ_BASE, 2, dot(embed_s[...], stamp_low, TN))
    blocks = width // TILE
    for norm in range(2):
        for j in range(2):
            row = gain_acc[norm : norm + 1, j * LANES : (j + 1) * LANES]
            at = GAIN_BASE + norm * 2 + j
            grad_ref[:, at : at + 1, :] = jnp.broadcast_to(row.reshape(1, 1, LANES), (blocks, 1, LANES))
    grad_ref[:, GAIN_BASE + 4 : WIRE, :] = jnp.zeros((blocks, WIRE - GAIN_BASE - 4, LANES), F32)

    def finish(g, _):
        block = pl.ds(g * GROUP, GROUP)
        pltpu.make_async_copy(og.at[block], og_ref.at[block], sems.at[g]).wait()
        return 0

    lax.fori_loop(0, samples // GROUP, finish, 0)


def block_and_back(actions, observed, camera_flags, noise_levels, cotangent, square, mlp, gains):
    tokens, width = actions.shape
    samples = observed.shape[0]
    wide = mlp.shape[2]
    spec = pl.BlockSpec(memory_space=VMEM)
    scalars = pl.BlockSpec(memory_space=pltpu.SMEM)
    rows = HEADS * ACT
    return pl.pallas_call(
        block_kernel,
        out_shape=(
            jax.ShapeDtypeStruct(actions.shape, F32),
            jax.ShapeDtypeStruct(actions.shape, F32),
            jax.ShapeDtypeStruct(observed.shape, F32),
            jax.ShapeDtypeStruct((width // TILE, WIRE, LANES), F32),
        ),
        in_specs=[spec, spec, spec, scalars, scalars, spec, spec, spec],
        out_specs=[spec, spec, pl.BlockSpec(memory_space=pl.ANY), spec],
        scratch_shapes=[
            VMEM((samples, KEYS_PAD, width), BF16),
            VMEM((samples, 16, width), F32),
            VMEM((samples, OBS_FULL, width), F32),
            VMEM((HEADS * width, width), BF16),
            VMEM((HEADS * width, width), BF16),
            VMEM((tokens, width), BF16),
            VMEM((samples, rows, width), BF16),
            VMEM((samples, rows, KEYS_PAD), F32),
            VMEM((tokens, HEADS * width), BF16),
            VMEM((samples, rows, width), BF16),
            VMEM((tokens, HEADS * width), BF16),
            VMEM((tokens, width), BF16),
            VMEM((tokens, width), F32),
            VMEM((tokens, 1), F32),
            VMEM((tokens, width), BF16),
            VMEM((tokens, width), BF16),
            VMEM((tokens, wide), BF16),
            VMEM((tokens, wide), BF16),
            VMEM((tokens, width), BF16),
            VMEM((tokens, width), BF16),
            VMEM((tokens, width), BF16),
            VMEM((samples, width // 2), F32),
            VMEM((samples, width), BF16),
            VMEM((samples, 8, width), F32),
            VMEM((tokens, width), F32),
            VMEM((8, width), F32),
            pltpu.SemaphoreType.DMA((samples // GROUP,)),
        ],
        compiler_params=pltpu.CompilerParams(vmem_limit_bytes=56 << 20),
        name="block_and_back",
    )(actions, cotangent, observed, camera_flags, noise_levels, square, mlp, gains)


def halves(value):
    high = value.astype(BF16)
    return high, (value - high.astype(F32)).astype(BF16)


def dot3(left, right, dims=NN):
    lh, ll = halves(left)
    rh, rl = halves(right)
    return dot(lh, rh, dims) + (dot(lh, rl, dims) + dot(ll, rh, dims))


def orthogonalize(read, columns, store, cur, gram_s, prod_s):
    total = jnp.zeros((1, 1), F32)
    for j in range(columns // LANES):
        part = read(j)
        cur[:, pl.ds(j * LANES, LANES)] = part
        total = total + jnp.sum(jnp.sum(part * part, axis=0, keepdims=True), axis=1, keepdims=True)
    scale = 1.0 / (jnp.sqrt(total) + 1e-07)
    cur[:, 0:columns] = cur[:, 0:columns] * scale
    x = cur[:, 0:columns]
    gram_s[...] = dot3(x, x, NT)
    one = (
        lax.broadcasted_iota(jnp.int32, (256, 256), 0) == lax.broadcasted_iota(jnp.int32, (256, 256), 1)
    ).astype(F32)
    prod_s[...] = one

    def turn(k, _):
        gram = gram_s[...]
        poly = COEF_A * one + COEF_B * gram + COEF_C * dot3(gram, gram)
        prod_s[...] = dot3(poly, prod_s[...])
        gram_s[...] = dot3(dot3(poly, gram), poly)
        return 0

    lax.fori_loop(0, 5, turn, 0)
    store(prod_s)


def update_kernel(
    grad_ref, sqm_ref, mlpm_ref, out_ref,
    got_core, sum1, send1, got1, sum2, send2, got2, sum3, send3, got3, moment, slabs_sq, slabs_mlp,
    result_sq, result_mlp, cur, gram_s, prod_s,
    send, recv, own_send, own_recv, back_send, back_recv,
):
    me, z, y, x, c = place()
    greet_partners(z, y, x, c)
    owner = me < 0
    for device in OWNERS:
        owner = jnp.logical_or(owner, me == device)

        @pl.when(me != device)
        def _():
            greet(device)

    @pl.when(owner)
    def _():
        def greet_other(step, _):
            greet((me + step) % 32)
            return 0

        lax.fori_loop(1, 32, greet_other, 0)

    is_owner = owner.astype(jnp.int32)
    pl.semaphore_wait(pltpu.get_barrier_semaphore(), 6 + 7 - is_owner + 31 * is_owner)

    def core_copy(k, pc):
        rows = pl.ds(*CHUNKS[k])
        return link(
            grad_ref.at[:, :, :, 1 - c, rows], got_core.at[:, :, :, rows],
            send.at[k, 0], recv.at[k, 0], device_at(z, y, x, 1 - c),
        )

    def first_copy(k):
        rows = pl.ds(*CHUNKS[k])
        to = device_at(z, y, 1 - x, c) if k % 2 == 0 else device_at(z, 1 - y, x, c)
        return link(send1.at[:, :, rows], got1.at[:, :, rows], send.at[k, 1], recv.at[k, 1], to)

    def second_copy(k):
        rows = pl.ds(*CHUNKS[k])
        to = device_at(z, 1 - y, x, c) if k % 2 == 0 else device_at(z, y, 1 - x, c)
        return link(send2.at[:, rows], got2.at[:, rows], send.at[k, 2], recv.at[k, 2], to)

    def third_copy(k, step):
        rows = pl.ds(*CHUNKS[k])
        to = device_at((z + step + 1) % 4, y, x, c)
        return link(
            send3.at[step, rows], got3.at[step, rows], send.at[k, 3 + step], recv.at[k, 3 + step], to
        )

    number = len(CHUNKS)
    for k in range(number):
        core_copy(k, c).start()
    for k in range(number):
        rows = pl.ds(*CHUNKS[k])
        core_copy(k, c).wait_recv()
        sum1[:, :, :, rows, :] = grad_ref[:, :, :, c, rows, :] + got_core[:, :, :, rows, :]
        if k % 2 == 0:
            send1[:, :, rows, :] = sum1[:, :, 1 - x, rows, :].astype(BF16)
        else:
            send1[:, :, rows, :] = sum1[:, 1 - y, :, rows, :].astype(BF16)
        first_copy(k).start()
    for k in range(number):
        rows = pl.ds(*CHUNKS[k])
        first_copy(k).wait_recv()
        if k % 2 == 0:
            sum2[:, :, rows, :] = sum1[:, :, x, rows, :] + got1[:, :, rows, :].astype(F32)
            send2[:, rows, :] = sum2[:, 1 - y, rows, :].astype(BF16)
        else:
            sum2[:, :, rows, :] = sum1[:, y, :, rows, :] + got1[:, :, rows, :].astype(F32)
            send2[:, rows, :] = sum2[:, 1 - x, rows, :].astype(BF16)
        second_copy(k).start()
    for k in range(number):
        rows = pl.ds(*CHUNKS[k])
        second_copy(k).wait_recv()
        mine = y if k % 2 == 0 else x
        sum3[:, rows, :] = sum2[:, mine, rows, :] + got2[:, rows, :].astype(F32)
        for step in range(3):
            send3[step, rows, :] = sum3[(z + step + 1) % 4, rows, :].astype(BF16)
            third_copy(k, step).start()

    for m in range(2):
        for j in range(8):
            moment[pl.ds(m * MLP_ROWS + j * TILE, TILE), :] = mlpm_ref[m, :, pl.ds(j * LANES, LANES)]
    for m in range(5):
        for j in range(2):
            moment[pl.ds(SQ_BASE + m * SQ_ROWS + j * TILE, TILE), :] = sqm_ref[m, :, pl.ds(j * LANES, LANES)]

    def slab(index):
        if index < 2:
            return pl.ds(index * MLP_ROWS, MLP_ROWS), slabs_mlp, result_mlp
        return pl.ds(SQ_BASE + (index - 2) * SQ_ROWS, SQ_ROWS), slabs_sq, result_sq

    def to_owner(index):
        rows, slabs, _ = slab(index)
        return link(
            moment.at[rows], slabs.at[me], own_send.at[index], own_recv.at[0], OWNERS[index]
        )

    for k in range(number):
        rows = pl.ds(*CHUNKS[k])
        total = sum3[z, rows, :]
        for step in range(3):
            third_copy(k, step).wait_recv()
            total = total + got3[step, rows, :].astype(F32)
        out_ref[0, rows, :] = total
        moment[rows, :] = 0.5 * moment[rows, :] + total
        for index in ((0,), (1,), (2, 3, 4), (5, 6))[k]:
            rows_m, slabs, _ = slab(index)

            @pl.when(me != OWNERS[index])
            def _():
                to_owner(index).start()

            @pl.when(me == OWNERS[index])
            def _():
                pltpu.make_async_copy(moment.at[rows_m], slabs.at[me], own_recv.at[0]).start()

    for index in range(7):
        rows_m, slabs, result = slab(index)
        tiles = 8 if index < 2 else 2

        @pl.when(me == OWNERS[index])
        def _():
            pltpu.make_async_copy(slabs, slabs, own_recv.at[0]).wait()

    for kind in range(2):
        mine = me < 0
        for index in range(7):
            if (index < 2) == (kind == 0):
                mine = jnp.logical_or(mine, me == OWNERS[index])
        slabs, result, tiles = (slabs_mlp, result_mlp, 8) if kind == 0 else (slabs_sq, result_sq, 2)

        @pl.when(mine)
        def _():
            def read(j):
                return slabs[:, pl.ds(j * TILE, TILE), :].reshape(256, LANES)

            def store(prod):
                for j in range(tiles):
                    part = dot3(prod[...], cur[:, pl.ds(j * LANES, LANES)])
                    result[:, pl.ds(j * TILE, TILE), :] = part.reshape(32, TILE, LANES)

            orthogonalize(read, tiles * LANES, store, cur, gram_s, prod_s)

    def give_back(index, device):
        rows, _, result = slab(index)
        return link(
            result.at[device], out_ref.at[2, rows], back_send.at[device], back_recv.at[index], device
        )

    for index in range(7):
        rows, _, result = slab(index)

        @pl.when(me == OWNERS[index])
        def _():
            def send_one(step, _):
                give_back(index, (me + step) % 32).start()
                return 0

            lax.fori_loop(1, 32, send_one, 0)
            pltpu.make_async_copy(result.at[me], out_ref.at[2, rows], back_recv.at[index]).start()

    out_ref[0, pl.ds(GAIN_BASE, 16), :] = out_ref[0, pl.ds(GAIN_BASE, 16), :]
    out_ref[1, pl.ds(0, WIRE), :] = moment[...]
    out_ref[2, pl.ds(GAIN_BASE, 16), :] = jnp.zeros((16, LANES), F32)
    for index in range(7):
        rows, _, result = slab(index)
        pltpu.make_async_copy(result.at[0], out_ref.at[2, rows], back_recv.at[index]).wait()

    for index in range(7):
        @pl.when(me != OWNERS[index])
        def _():
            to_owner(index).wait_send()

        @pl.when(me == OWNERS[index])
        def _():
            def wait_one(step, _):
                give_back(index, (me + step) % 32).wait_send()
                return 0

            lax.fori_loop(1, 32, wait_one, 0)

    for k in range(number):
        core_copy(k, c).wait_send()
        first_copy(k).wait_send()
        second_copy(k).wait_send()
        for step in range(3):
            third_copy(k, step).wait_send()


def reduce_and_orthogonalize(grads, square_moment, mlp_moment):
    spec = pl.BlockSpec(memory_space=VMEM)
    sem = pltpu.SemaphoreType.DMA
    return pl.pallas_call(
        update_kernel,
        out_shape=jax.ShapeDtypeStruct((3, WIRE, LANES), F32),
        in_specs=[spec] * 3,
        out_specs=spec,
        scratch_shapes=[
            VMEM((4, 2, 2, WIRE, LANES), F32),
            VMEM((4, 2, 2, WIRE, LANES), F32),
            VMEM((4, 2, WIRE, LANES), BF16),
            VMEM((4, 2, WIRE, LANES), BF16),
            VMEM((4, 2, WIRE, LANES), F32),
            VMEM((4, WIRE, LANES), BF16),
            VMEM((4, WIRE, LANES), BF16),
            VMEM((4, WIRE, LANES), F32),
            VMEM((3, WIRE, LANES), BF16),
            VMEM((3, WIRE, LANES), BF16),
            VMEM((WIRE, LANES), F32),
            VMEM((32, SQ_ROWS, LANES), F32),
            VMEM((32, MLP_ROWS, LANES), F32),
            VMEM((32, SQ_ROWS, LANES), F32),
            VMEM((32, MLP_ROWS, LANES), F32),
            VMEM((256, 1024), F32),
            VMEM((256, 256), F32),
            VMEM((256, 256), F32),
            sem((4, 6)),
            sem((4, 6)),
            sem((7,)),
            sem((1,)),
            sem((32,)),
            sem((7,)),
        ],
        compiler_params=pltpu.CompilerParams(
            collective_id=1, has_side_effects=True, vmem_limit_bytes=40 << 20
        ),
        name="reduce_and_orthogonalize",
    )(grads.reshape(GRID + (WIRE, LANES)), square_moment, mlp_moment)


def finish_kernel(
    rate, wire_ref, sqw_ref, mlpw_ref, gain_ref, gainm_ref,
    sqg, sqm, sqn, sqc, mlpg, mlpm, mlpn, mlpc, gg, gm, gn,
):
    me = lax.axis_index("dp")
    for m in range(5):
        for j in range(2):
            rows, columns = pl.ds(SQ_BASE + m * SQ_ROWS + j * TILE, TILE), pl.ds(j * LANES, LANES)
            sqg[m, :, columns] = wire_ref[0, rows, :]
            sqm[m, :, columns] = wire_ref[1, rows, :]
            sqn[m, :, columns] = sqw_ref[m, :, columns] - SQ_RATES[m] * wire_ref[2, rows, :]
    sqc[...] = sqn[...].astype(BF16)
    for m in range(2):
        for j in range(8):
            rows, columns = pl.ds(m * MLP_ROWS + j * TILE, TILE), pl.ds(j * LANES, LANES)
            mlpg[m, :, columns] = wire_ref[0, rows, :]
            mlpm[m, :, columns] = wire_ref[1, rows, :]
            mlpn[m, :, columns] = mlpw_ref[m, :, columns] - MLP_RATES[m] * wire_ref[2, rows, :]
    mlpc[...] = mlpn[...].astype(BF16)
    tile = wire_ref[0, pl.ds(GAIN_BASE, TILE), :]
    turned = pltpu.roll(tile, (LANES - (me % 16) * TILE) % LANES, 1)
    at = me // 16
    for norm in range(2):
        pair = turned[2 * norm : 2 * norm + 2, 0:TILE]
        row = jnp.where(at == 0, pair[0:1, :], pair[1:2, :])
        new = 0.5 * gainm_ref[norm : norm + 1, :] + row
        gg[norm : norm + 1, :] = row
        gm[norm : norm + 1, :] = new
        gn[norm : norm + 1, :] = gain_ref[norm : norm + 1, :] - rate * new


def finish(wire, square_weights, mlp_weights, gains, gain_moment, rate):
    spec = pl.BlockSpec(memory_space=VMEM)
    square = jax.ShapeDtypeStruct(square_weights.shape, F32)
    square_low = jax.ShapeDtypeStruct(square_weights.shape, BF16)
    mlp = jax.ShapeDtypeStruct(mlp_weights.shape, F32)
    mlp_low = jax.ShapeDtypeStruct(mlp_weights.shape, BF16)
    gain = jax.ShapeDtypeStruct(gains.shape, F32)
    return pl.pallas_call(
        functools.partial(finish_kernel, rate),
        out_shape=(square, square, square, square_low, mlp, mlp, mlp, mlp_low, gain, gain, gain),
        in_specs=[spec] * 5,
        out_specs=[spec] * 11,
        name="finish",
    )(wire, square_weights, mlp_weights, gains, gain_moment)


HIGH_PRECISION = lax.Precision.HIGHEST


def plain_orthogonalize(matrix):
    current = matrix / (jnp.sqrt(jnp.sum(matrix * matrix)) + 1e-07)
    for turn in range(5):
        gram = jnp.dot(current, current.T, precision=HIGH_PRECISION)
        poly = COEF_B * gram + COEF_C * jnp.dot(gram, gram, precision=HIGH_PRECISION)
        current = COEF_A * current + jnp.dot(poly, current, precision=HIGH_PRECISION)
    return current


def pick_owned(stack, owners, device):
    chosen = jnp.zeros_like(stack[0])
    for index in range(len(owners)):
        chosen = jnp.where(device == owners[index], stack[index], chosen)
    return chosen


def is_owner(owners, device):
    flag = device < 0
    for owner in owners:
        flag = jnp.logical_or(flag, device == owner)
    return flag


def from_wire(grads):
    def matrix(base, tiles):
        part = grads[:, base : base + tiles * TILE, :].reshape(-1, tiles, TILE, LANES)
        return part.transpose(0, 2, 1, 3).reshape(-1, tiles * LANES)

    square = jnp.stack([matrix(SQ_BASE + m * SQ_ROWS, 2) for m in range(5)])
    mlp = jnp.stack([matrix(m * MLP_ROWS, 8) for m in range(2)])
    return square, mlp, grads[0, GAIN_BASE : GAIN_BASE + 4, :].reshape(2, 2 * LANES)


def update_by_collectives(
    grads, square_weights, mlp_weights, gains, square_moment, mlp_moment, gain_moment, rate
):
    square_local, mlp_local, gain_local = from_wire(grads)
    square_grad, mlp_grad, gain_grad = (
        lax.psum_scatter(square_local, "dp", scatter_dimension=1, tiled=True),
        lax.psum_scatter(mlp_local, "dp", scatter_dimension=1, tiled=True),
        lax.psum_scatter(gain_local, "dp", scatter_dimension=1, tiled=True),
    )
    square_moment_new = 0.5 * square_moment + square_grad
    mlp_moment_new = 0.5 * mlp_moment + mlp_grad
    gain_moment_new = 0.5 * gain_moment + gain_grad
    device = lax.axis_index("dp")
    count = lax.axis_size("dp")
    square_owners = [index * count // 7 for index in range(5)]
    mlp_owners = [(index + 5) * count // 7 for index in range(2)]
    square_full, mlp_full = (
        lax.all_gather(square_moment_new, "dp", axis=1, tiled=True),
        lax.all_gather(mlp_moment_new, "dp", axis=1, tiled=True),
    )
    mine_square = pick_owned(square_full, square_owners, device)
    mine_mlp = pick_owned(mlp_full, mlp_owners, device)
    made_square = lax.cond(
        is_owner(square_owners, device), plain_orthogonalize, jnp.zeros_like, mine_square
    )
    made_mlp = lax.cond(is_owner(mlp_owners, device), plain_orthogonalize, jnp.zeros_like, mine_mlp)
    stack_square = jnp.stack(
        [jnp.where(device == owner, made_square, 0.0) for owner in square_owners]
    )
    stack_mlp = jnp.stack([jnp.where(device == owner, made_mlp, 0.0) for owner in mlp_owners])
    square_ortho, mlp_ortho = (
        lax.psum_scatter(stack_square, "dp", scatter_dimension=1, tiled=True),
        lax.psum_scatter(stack_mlp, "dp", scatter_dimension=1, tiled=True),
    )
    square_new = square_weights - jnp.array(SQ_RATES, F32)[:, None, None] * square_ortho
    mlp_new = mlp_weights - jnp.array(MLP_RATES, F32)[:, None, None] * mlp_ortho
    gains_new = gains - rate * gain_moment_new
    return (
        square_grad,
        square_moment_new,
        square_new,
        square_new.astype(BF16),
        mlp_grad,
        mlp_moment_new,
        mlp_new,
        mlp_new.astype(BF16),
        gain_grad,
        gain_moment_new,
        gains_new,
    )


def per_device(
    actions,
    observed,
    camera_flags,
    noise_levels,
    cotangent,
    square_weights,
    mlp_weights,
    gains,
    square_moment,
    mlp_moment,
    gain_moment,
):
    count = lax.axis_size("dp")
    rate = 0.1 / math.sqrt(actions.shape[0] * count)
    kernels = count == math.prod(GRID)
    if kernels:
        square_all, mlp_all, gain_all = gather_weights(square_weights, mlp_weights, gains)
    else:
        square_all, mlp_all = (
            lax.all_gather(square_weights.astype(BF16), "dp", axis=1, tiled=True),
            lax.all_gather(mlp_weights.astype(BF16), "dp", axis=1, tiled=True),
        )
        gain_all = lax.all_gather(gains, "dp", axis=1, tiled=True)
    output, actions_grad, observed_grad, grads = block_and_back(
        actions, observed, camera_flags, noise_levels, cotangent, square_all, mlp_all, gain_all
    )
    if kernels:
        wire = reduce_and_orthogonalize(grads, square_moment, mlp_moment)
        rest = finish(wire, square_weights, mlp_weights, gains, gain_moment, rate)
    else:
        rest = update_by_collectives(
            grads, square_weights, mlp_weights, gains, square_moment, mlp_moment, gain_moment, rate
        )
    return (output, actions_grad, observed_grad) + tuple(rest)


def solution(mesh):
    rows, cube, flat = P("dp", None), P("dp", None, None), P("dp")
    stacked, pair = P(None, "dp", None), P(None, "dp")
    return jax.shard_map(
        per_device,
        mesh=mesh,
        in_specs=(rows, cube, flat, flat, rows, stacked, stacked, pair, stacked, stacked, pair),
        out_specs=(rows, rows, cube) + (stacked,) * 8 + (pair,) * 3,
        check_vma=False,
    )
```

```python
import functools
import math

import jax
import jax.numpy as jnp
from jax import lax
from jax.experimental import pallas as pl
from jax.experimental.pallas import tpu as pltpu
from jax.sharding import PartitionSpec as P

HEADS = 4
ACT = 16
OBS_FULL = 196
OBS_FEW = 49
COEF_A = 3.4445
COEF_B = -4.775
COEF_C = 2.0315
F32 = jnp.float32
BF16 = jnp.bfloat16
MESH = pl.DeviceIdType.MESH
VMEM = pltpu.VMEM
NN = (((1,), (0,)), ((), ()))
NT = (((1,), (1,)), ((), ()))
TN = (((0,), (0,)), ((), ()))

LANES = 128
TILE = 8
MLP_ROWS = 64
SQ_ROWS = 16
SQ_AT = (160, 176, 192, 128, 144)
GAIN_BASE = 208
WIRE = 224
CHUNKS = ((0, 64), (64, 64), (128, 32), (160, 32), (192, 32))
X_FIRST = (True, False, True, True, False)
MLP_RATES = (1.0, 0.5)
SQ_RATES = (0.5, 0.5, 0.5, 0.5, 4.0)
GRID = (4, 2, 2, 2)
OWNERS = (8, 22, 14, 16, 11, 21, 13)
KEYS_PAD = 208
GROUP = 4
ROWS = 256


def dot(left, right, dims=NN):
    return lax.dot_general(left, right, dims, preferred_element_type=F32)


def place():
    me = lax.axis_index("dp")
    return me, me // 8, (me // 4) % 2, (me // 2) % 2, me % 2


def device_at(z, y, x, c):
    return ((z * 2 + y) * 2 + x) * 2 + c


def link(src, dst, send, recv, device):
    return pltpu.make_async_remote_copy(
        src_ref=src,
        dst_ref=dst,
        send_sem=send,
        recv_sem=recv,
        device_id=(device,),
        device_id_type=MESH,
    )


def greet(device):
    pl.semaphore_signal(
        pltpu.get_barrier_semaphore(), inc=1, device_id=(device,), device_id_type=MESH
    )


def halves(value):
    high = value.astype(BF16)
    return high, (value - high.astype(F32)).astype(BF16)


def dot3(left, right, dims=NN):
    (lh, ll), (rh, rl) = left, right
    return dot(lh, rh, dims) + (dot(lh, rl, dims) + dot(ll, rh, dims))


def normalize(values):
    centred = values - jnp.mean(values, -1, keepdims=True)
    scale = lax.rsqrt(jnp.mean(centred * centred, -1, keepdims=True) + 1e-05)
    return centred * scale, scale


def norm_back(grad, hat, scale):
    mean_one = jnp.mean(grad, -1, keepdims=True)
    mean_two = jnp.mean(grad * hat, -1, keepdims=True)
    return scale * (grad - mean_one - hat * mean_two)


class Gather:
    def __init__(self, r):
        self.r = r
        self.me, self.z, self.y, self.x, self.c = place()

    def hop(self, k, step, part, device):
        return link(part, part, self.r["gsend"].at[k, step], self.r["grecv"].at[k, step], device)

    def along_z(self, k, step):
        part = self.r["wire"].at[self.z, self.y, self.x, self.c, pl.ds(*CHUNKS[k])]
        return self.hop(k, step, part, device_at((self.z + step + 1) % 4, self.y, self.x, self.c))

    def from_z(self, k, step):
        there = (self.z + 3 - step) % 4
        part = self.r["wire"].at[there, self.y, self.x, self.c, pl.ds(*CHUNKS[k])]
        return self.hop(k, step, part, device_at(there, self.y, self.x, self.c))

    def plane(self, k, second, mine):
        z, y, x, c = self.z, self.y, self.x, self.c
        rows, wire = pl.ds(*CHUNKS[k]), self.r["wire"]
        py, px = (y, x) if mine else (1 - y, 1 - x)
        along_x = X_FIRST[k] == second
        if along_x:
            part = wire.at[:, y, px, c, rows] if second else wire.at[:, :, px, c, rows]
            return self.hop(k, 3 if second else 4, part, device_at(z, y, 1 - x, c))
        part = wire.at[:, py, x, c, rows] if second else wire.at[:, py, :, c, rows]
        return self.hop(k, 3 if second else 4, part, device_at(z, 1 - y, x, c))

    def core(self, k, mine):
        part = self.r["wire"].at[:, :, :, self.c if mine else 1 - self.c, pl.ds(*CHUNKS[k])]
        return self.hop(k, 5, part, device_at(self.z, self.y, self.x, 1 - self.c))

    def first(self, *chunks):
        for k in chunks:
            for step in range(3):
                self.along_z(k, step).start()

    def second(self, *chunks):
        for k in chunks:
            for step in range(3):
                self.from_z(k, step).wait_recv()
            self.plane(k, True, True).start()

    def third(self, *chunks):
        for k in chunks:
            self.plane(k, True, False).wait_recv()
            self.plane(k, False, True).start()

    def fourth(self, *chunks):
        for k in chunks:
            self.plane(k, False, False).wait_recv()
            self.core(k, True).start()

    def last(self, *chunks):
        for k in chunks:
            self.core(k, False).wait_recv()

    def drain(self):
        for k in range(len(CHUNKS)):
            for step in range(3):
                self.along_z(k, step).wait_send()
            self.plane(k, True, True).wait_send()
            self.plane(k, False, True).wait_send()
            self.core(k, True).wait_send()

    def fill(self):
        r = self.r
        spot = (self.z, self.y, self.x, self.c)

        def tiles(source, m, base, number):
            for j in range(number):
                pair = [source[m, :, pl.ds((2 * j + k) * LANES, LANES)] for k in range(2)]
                r["wire"][spot + (pl.ds(base + j * 16, 16),)] = jnp.concatenate(pair, axis=0).astype(BF16)

        for m in range(5):
            tiles(r["sqw_v"], m, SQ_AT[m], 1)
        for m in range(2):
            tiles(r["mlpw_v"], m, m * MLP_ROWS, 4)
        gains, edge = r["gain_v"][...], r["edge"]
        high = gains.astype(BF16).astype(F32)
        middle = (gains - high).astype(BF16).astype(F32)
        edge[...] = jnp.zeros_like(edge)
        edge[0:2, 0:TILE] = high
        edge[2:4, 0:TILE] = middle
        edge[4:6, 0:TILE] = (gains - high - middle).astype(BF16).astype(F32)
        r["wire"][spot + (pl.ds(GAIN_BASE, 16),)] = edge[...].astype(BF16)

    def unpack(self, base, number, out, m):
        for j in range(number):
            block = self.r["wire"][:, :, :, :, pl.ds(base + j * 16, 16), :].reshape(32, 16, LANES).astype(F32)
            for half in range(2):
                columns = pl.ds((2 * j + half) * LANES, LANES)
                out[m, :, columns] = block[:, half * 8 : half * 8 + 8, :].reshape(256, LANES).astype(BF16)

    def unpack_gains(self):
        edge, wire = self.r["edge"], self.r["wire"]
        for half in range(2):
            total = jnp.zeros((16, LANES), F32)
            for at in range(16):
                d = half * 16 + at
                tile = wire[d // 8, (d // 4) % 2, (d // 2) % 2, d % 2, pl.ds(GAIN_BASE, 16), :].astype(F32)
                total = total + (tile if at == 0 else pltpu.roll(tile, at * TILE, 1))
            edge[...] = total
            self.r["gain_all"][:, pl.ds(half * LANES, LANES)] = edge[0:2, :] + edge[2:4, :] + edge[4:6, :]


class Update:
    def __init__(self, r):
        self.r = r
        self.me, self.z, self.y, self.x, self.c = place()

    def hop(self, k, step, src, dst, device):
        return link(src, dst, self.r["send"].at[k, step], self.r["recv"].at[k, step], device)

    def core(self, k):
        rows = pl.ds(*CHUNKS[k])
        src, dst = self.r["grads"].at[:, :, :, 1 - self.c, rows], self.r["got_core"].at[:, :, :, rows]
        return self.hop(k, 0, src, dst, device_at(self.z, self.y, self.x, 1 - self.c))

    def plane(self, k, first):
        rows = pl.ds(*CHUNKS[k])
        to = (self.z, self.y, 1 - self.x, self.c) if X_FIRST[k] == first else (self.z, 1 - self.y, self.x, self.c)
        if first:
            src, dst = self.r["send1"].at[:, :, rows], self.r["got1"].at[:, :, rows]
        else:
            src, dst = self.r["send2"].at[:, rows], self.r["got2"].at[:, rows]
        return self.hop(k, 1 if first else 2, src, dst, device_at(*to))

    def along_z(self, k, step):
        rows = pl.ds(*CHUNKS[k])
        to = device_at((self.z + step + 1) % 4, self.y, self.x, self.c)
        return self.hop(k, 3 + step, self.r["send3"].at[step, rows], self.r["got3"].at[step, rows], to)

    def start(self, k):
        self.core(k).start()

    def one(self, *chunks):
        r = self.r
        for k in chunks:
            rows = pl.ds(*CHUNKS[k])
            self.core(k).wait_recv()
            sum1 = r["sum1"]
            sum1[:, :, :, rows, :] = r["grads"][:, :, :, self.c, rows, :] + r["got_core"][:, :, :, rows, :]
            other = sum1[:, :, 1 - self.x, rows, :] if X_FIRST[k] else sum1[:, 1 - self.y, :, rows, :]
            r["send1"][:, :, rows, :] = other.astype(BF16)
            self.plane(k, True).start()

    def two(self, *chunks):
        r = self.r
        for k in chunks:
            rows = pl.ds(*CHUNKS[k])
            self.plane(k, True).wait_recv()
            sum1, sum2 = r["sum1"], r["sum2"]
            mine = sum1[:, :, self.x, rows, :] if X_FIRST[k] else sum1[:, self.y, :, rows, :]
            sum2[:, :, rows, :] = mine + r["got1"][:, :, rows, :].astype(F32)
            other = 1 - self.y if X_FIRST[k] else 1 - self.x
            r["send2"][:, rows, :] = sum2[:, other, rows, :].astype(BF16)
            self.plane(k, False).start()

    def three(self, *chunks):
        r = self.r
        for k in chunks:
            rows = pl.ds(*CHUNKS[k])
            self.plane(k, False).wait_recv()
            mine = self.y if X_FIRST[k] else self.x
            r["sum3"][:, rows, :] = r["sum2"][:, mine, rows, :] + r["got2"][:, rows, :].astype(F32)
            for step in range(3):
                r["send3"][step, rows, :] = r["sum3"][(self.z + step + 1) % 4, rows, :].astype(BF16)
                self.along_z(k, step).start()

    def slab(self, index):
        if index < 2:
            return pl.ds(index * MLP_ROWS, MLP_ROWS), self.r["slabs_mlp"], self.r["result_mlp"]
        return pl.ds(SQ_AT[index - 2], SQ_ROWS), self.r["slabs_sq"], self.r["result_sq"]

    def to_owner(self, index):
        rows, slabs, _ = self.slab(index)
        return link(
            self.r["moment"].at[rows], slabs.at[self.me],
            self.r["own_send"].at[index], self.r["own_recv"].at[0], OWNERS[index],
        )

    def four(self, *chunks):
        r = self.r
        moment, out = r["moment"], r["out"]
        for k in chunks:
            rows = pl.ds(*CHUNKS[k])
            total = r["sum3"][self.z, rows, :]
            for step in range(3):
                self.along_z(k, step).wait_recv()
                total = total + r["got3"][step, rows, :].astype(F32)
            out[0, rows, :] = total
            moment[rows, :] = 0.5 * moment[rows, :] + total
            for index in ((0,), (1,), (5, 6), (2, 3), (4,))[k]:
                rows_m, slabs, _ = self.slab(index)

                @pl.when(self.me != OWNERS[index])
                def _():
                    self.to_owner(index).start()

                @pl.when(self.me == OWNERS[index])
                def _():
                    pltpu.make_async_copy(moment.at[rows_m], slabs.at[self.me], r["own_recv"].at[0]).start()

    def old_moment(self):
        r = self.r
        moment = r["moment"]
        for m in range(2):
            for j in range(8):
                moment[pl.ds(m * MLP_ROWS + j * TILE, TILE), :] = r["mlpm_v"][m, :, pl.ds(j * LANES, LANES)]
        for m in range(5):
            for j in range(2):
                moment[pl.ds(SQ_AT[m] + j * TILE, TILE), :] = r["sqm_v"][m, :, pl.ds(j * LANES, LANES)]
        moment[pl.ds(GAIN_BASE, 16), :] = jnp.zeros((16, LANES), F32)

    def orthogonalize(self):
        r = self.r
        cur, gram_s, prod_s = r["cur"], r["gram_s"], r["prod_s"]

        def load(slabs, tiles):
            total = jnp.zeros((1, 1), F32)
            for j in range(tiles):
                part = slabs[:, pl.ds(j * TILE, TILE), :].reshape(256, LANES)
                cur[:, pl.ds(j * LANES, LANES)] = part
                total = total + jnp.sum(jnp.sum(part * part, axis=0, keepdims=True), axis=1, keepdims=True)
            width = tiles * LANES
            cur[:, 0:width] = cur[:, 0:width] * (1.0 / (jnp.sqrt(total) + 1e-07))

        mine_mlp = jnp.logical_or(self.me == OWNERS[0], self.me == OWNERS[1])
        mine_sq = self.me < 0
        for device in OWNERS[2:]:
            mine_sq = jnp.logical_or(mine_sq, self.me == device)

        @pl.when(mine_mlp)
        def _():
            slabs, result = r["slabs_mlp"], r["result_mlp"]
            pltpu.make_async_copy(slabs, slabs, r["own_recv"].at[0]).wait()
            load(slabs, 8)
            x = halves(cur[...])
            gram_s[...] = dot3(x, x, NT)
            rows = lax.broadcasted_iota(jnp.int32, (256, 256), 0)
            one = (rows == lax.broadcasted_iota(jnp.int32, (256, 256), 1)).astype(F32)
            prod_s[...] = one

            def turn(k, _):
                gram = gram_s[...]
                g = halves(gram)
                p = halves(COEF_A * one + COEF_B * gram + COEF_C * dot3(g, g))
                prod_s[...] = dot3(p, halves(prod_s[...]))
                gram_s[...] = dot3(halves(dot3(p, g)), p)
                return 0

            lax.fori_loop(0, 5, turn, 0)
            prod = halves(prod_s[...])
            for j in range(8):
                part = dot3(prod, halves(cur[:, pl.ds(j * LANES, LANES)]))
                result[:, pl.ds(j * TILE, TILE), :] = part.reshape(32, TILE, LANES)

        @pl.when(mine_sq)
        def _():
            slabs, result = r["slabs_sq"], r["result_sq"]
            pltpu.make_async_copy(slabs, slabs, r["own_recv"].at[0]).wait()
            load(slabs, 2)

            def turn(k, _):
                now = cur[:, 0:256]
                x = halves(now)
                gram = dot3(x, x, NT)
                g = halves(gram)
                p = halves(COEF_B * gram + COEF_C * dot3(g, g))
                cur[:, 0:256] = COEF_A * now + dot3(p, x)
                return 0

            lax.fori_loop(0, 5, turn, 0)
            for j in range(2):
                part = cur[:, pl.ds(j * LANES, LANES)]
                result[:, pl.ds(j * TILE, TILE), :] = part.reshape(32, TILE, LANES)

    def give_back(self, index, device):
        rows, _, result = self.slab(index)
        return link(
            result.at[device], self.r["out"].at[2, rows],
            self.r["back_send"].at[device], self.r["back_recv"].at[index], device,
        )

    def give_all(self):
        r = self.r
        for index in range(7):
            rows, _, result = self.slab(index)

            @pl.when(self.me == OWNERS[index])
            def _():
                def send_one(step, _):
                    self.give_back(index, (self.me + step) % 32).start()
                    return 0

                lax.fori_loop(1, 32, send_one, 0)
                pltpu.make_async_copy(result.at[self.me], r["out"].at[2, rows], r["back_recv"].at[index]).start()

    def take_all(self):
        for index in range(7):
            rows, _, result = self.slab(index)
            pltpu.make_async_copy(result.at[0], self.r["out"].at[2, rows], self.r["back_recv"].at[index]).wait()

    def drain(self):
        for index in range(7):

            @pl.when(self.me != OWNERS[index])
            def _():
                self.to_owner(index).wait_send()

            @pl.when(self.me == OWNERS[index])
            def _():
                def wait_one(step, _):
                    self.give_back(index, (self.me + step) % 32).wait_send()
                    return 0

                lax.fori_loop(1, 32, wait_one, 0)

        for k in range(len(CHUNKS)):
            self.core(k).wait_send()
            self.plane(k, True).wait_send()
            self.plane(k, False).wait_send()
            for step in range(3):
                self.along_z(k, step).wait_send()


def greet_all():
    me, z, y, x, c = place()
    greet(device_at(z, y, x, 1 - c))
    greet(device_at(z, y, 1 - x, c))
    greet(device_at(z, 1 - y, x, c))
    for step in range(1, 4):
        greet(device_at((z + step) % 4, y, x, c))
    owner = me < 0
    for device in OWNERS:
        owner = jnp.logical_or(owner, me == device)

        @pl.when(me != device)
        def _():
            greet(device)

    @pl.when(owner)
    def _():
        def greet_other(step, _):
            greet((me + step) % 32)
            return 0

        lax.fori_loop(1, 32, greet_other, 0)

    is_owner = owner.astype(jnp.int32)
    return 6 + 7 - is_owner + 31 * is_owner


def block_kernel(names, remote, *args):
    r = dict(zip(names, args))
    keys, samples = r["obs"].shape[0], r["obs"].shape[1]
    tokens, width = r["acts"].shape
    head_dim, half, per = width // HEADS, width // 2, ROWS // ACT
    wide = r["mlp_all"].shape[2]
    groups = samples // GROUP
    in_sems, out_sems = r["in_sems"], r["out_sems"]

    loads = [("obs", "obs_v"), ("acts", "acts_v"), ("cot", "cot_v")]
    if remote:
        loads = [("sqw", "sqw_v"), ("mlpw", "mlpw_v"), ("gain", "gain_v")] + loads
        loads += [("sqm", "sqm_v"), ("mlpm", "mlpm_v")]
    else:
        loads += [("sqw", "sq_all"), ("mlpw", "mlp_all"), ("gain", "gain_all")]
    copies = {a: pltpu.make_async_copy(r[a], r[b], in_sems.at[i]) for i, (a, b) in enumerate(loads)}

    def arrive(*which):
        for name in which:
            copies[name].wait()

    for copy in copies.values():
        copy.start()
    if remote:
        gather, update = Gather(r), Update(r)
        expected = greet_all()
        arrive("sqw", "mlpw", "gain")
        gather.fill()
        pl.semaphore_wait(pltpu.get_barrier_semaphore(), expected)
        gather.first(3, 4, 2)

    arrive("acts")

    def hats(i, _):
        rows = pl.ds(pl.multiple_of(i * ROWS, ROWS), ROWS)
        hat, scale = normalize(r["acts_v"][rows, :])
        r["xhat"][rows, :] = hat
        r["rstd"][rows, :] = scale
        return 0

    lax.fori_loop(0, tokens // ROWS, hats, 0)

    spread, mem, tail = r["spread"], r["mem"], r["tail"]
    batch = 16

    def turn_in(part):
        def one_key(j, _):
            value = r["obs_v"][j, part * batch : (part + 1) * batch, :].astype(F32)
            at = pl.multiple_of(j * batch, batch)
            for side in range(2):
                spread[pl.ds(side * keys * batch + at, batch), :] = value[:, side * LANES : (side + 1) * LANES]
            return 0

        lax.fori_loop(0, keys, one_key, 0, unroll=4)

    def turn_out(part):
        def one_sample(s, _):
            for side in range(2):
                value = spread[pl.ds(side * keys * batch + s, keys, stride=batch), :]
                columns = pl.ds(side * LANES, LANES)
                mem[part * batch + s, 0:192, columns] = value[0:192].astype(BF16)
                tail[part * batch + s, 0:4, columns] = value[192:196]
            return 0

        lax.fori_loop(0, batch, one_sample, 0)

    tail[...] = jnp.zeros_like(tail)
    arrive("obs")
    turn_in(0)
    if remote:
        gather.second(3, 4, 2)
        gather.first(0, 1)
    turn_out(0)
    if remote:
        gather.third(3, 4, 2)
    turn_in(1)
    if remote:
        gather.second(0, 1)
        gather.fourth(3, 4, 2)
    turn_out(1)
    freqs = jnp.exp(
        lax.broadcasted_iota(jnp.int32, (1, half), 1).astype(F32) * F32(-math.log(10000.0)) / half
    )
    for s in range(samples):
        r["angle"][s : s + 1, :] = r["levels"][s].astype(F32) * freqs
    r["embed"][:, 0:half] = jnp.sin(r["angle"][...]).astype(BF16)
    r["embed"][:, half:width] = jnp.cos(r["angle"][...]).astype(BF16)
    if remote:
        arrive("sqm", "mlpm")
        update.old_moment()
        gather.third(0, 1)
        gather.last(3, 4, 2)
        for m in range(5):
            gather.unpack(SQ_AT[m], 1, r["sq_all"], m)
        gather.unpack_gains()
    else:
        arrive("sqw", "mlpw", "gain")

    sq, mlp = r["sq_all"], r["mlp_all"]
    wkh, wvh = r["wkh"], r["wvh"]
    lane = lax.broadcasted_iota(jnp.int32, (width, width), 1)
    for h in range(HEADS):
        inside = lane // head_dim == h
        block = pl.ds(h * width, width)
        wkh[block, :] = jnp.where(inside, sq[2].astype(F32), 0.0).astype(BF16)
        wvh[block, :] = jnp.where(inside, sq[3].astype(F32), 0.0).astype(BF16)
    g1, g2 = r["gain_all"][0:1, :], r["gain_all"][1:2, :]

    stamp = dot(r["embed"][...], sq[0]).astype(BF16).astype(F32)
    for s in range(samples):
        tail[s, 4:5, :] = stamp[s : s + 1, :]

    def close(s, _):
        mem[s, 192:208, :] = tail[s].astype(BF16)
        return 0

    lax.fori_loop(0, samples, close, 0)

    sides, weights = r["sides_v"], r["pds_v"]

    def make_queries(i, _):
        rows = pl.ds(pl.multiple_of(i * ROWS, ROWS), ROWS)
        first = (r["xhat"][rows, :] * g1).astype(BF16)
        r["first"][rows, :] = first
        q = dot(first, sq[1]).astype(BF16)
        r["query"][rows, :] = q
        here = pl.ds(i * per, per)
        for h in range(HEADS):
            wk = wkh[pl.ds(h * width, width), :]
            value = (dot(q, wk, NT) * 0.125).astype(BF16).reshape(per, ACT, width)
            sides[here, pl.ds((HEADS + h) * ACT, ACT), :] = value
        return 0

    lax.fori_loop(0, tokens // ROWS, make_queries, 0)

    key = lax.broadcasted_iota(jnp.int32, (HEADS * ACT, KEYS_PAD), 1)
    low_rows, high_rows = pl.ds(0, HEADS * ACT), pl.ds(HEADS * ACT, HEADS * ACT)

    def attend(g, _):
        ids = [g * GROUP + k for k in range(GROUP)]
        scores = [dot(sides[s, high_rows, :], mem[s], NT) for s in ids]
        lows = []
        for s, score in zip(ids, scores):
            count = OBS_FEW + (OBS_FULL - OBS_FEW) * r["flags"][s]
            score = jnp.where((key < count) | (key == OBS_FULL), score, -1000000000.0)
            expo = jnp.exp(score - jnp.max(score, -1, keepdims=True))
            probs = expo / jnp.sum(expo, -1, keepdims=True)
            r["probs"][s] = probs
            low = probs.astype(BF16)
            weights[s, low_rows, :] = low
            lows.append(low)
        for s, low in zip(ids, lows):
            u = dot(low, mem[s]).astype(BF16)
            rows = pl.ds(pl.multiple_of(s * ACT, ACT), ACT)
            for h in range(HEADS):
                r["u"][rows, pl.ds(h * width, width)] = u[h * ACT : (h + 1) * ACT, :]
        return 0

    lax.fori_loop(0, groups // 2, attend, 0)
    if remote:
        gather.fourth(0, 1)
    lax.fori_loop(groups // 2, groups, attend, 0)
    if remote:
        gather.last(0, 1)
        for m in range(2):
            gather.unpack(m * MLP_ROWS, 4, mlp, m)

    gain_acc = r["gain_acc"]
    gain_acc[...] = jnp.zeros_like(gain_acc)
    arrive("cot")

    def feed(i, _):
        rows = pl.ds(pl.multiple_of(i * ROWS, ROWS), ROWS)
        mixed = dot(r["u"][rows, :], wvh[...]).astype(BF16)
        r["mixed"][rows, :] = mixed
        resid = r["acts_v"][rows, :] + dot(mixed, sq[4])
        hat, scale = normalize(resid)
        second = (hat * g2).astype(BF16)
        r["second"][rows, :] = second
        cot = r["cot_v"][rows, :]
        out_low = cot.astype(BF16)
        r["out_low"][rows, :] = out_low
        for c in range(wide // 256):
            columns = pl.ds(c * 256, 256)
            v = dot(second, mlp[0, :, columns])
            square = v * v
            t = jnp.tanh(0.7978845608 * (v + 0.044715 * square * v))
            r["active"][rows, columns] = (0.5 * v * (1.0 + t)).astype(BF16)
            slope = 0.5 * (1.0 + t) + 0.5 * v * (1.0 - t * t) * (0.7978845608 * (1.0 + 0.134145 * square))
            r["dhidden"][rows, columns] = (slope * dot(out_low, mlp[1, :, columns])).astype(BF16)
        r["out_v"][rows, :] = resid + dot(r["active"][rows, :], mlp[1], NT)
        grad_second = dot(r["dhidden"][rows, :], mlp[0], NT)
        gain_acc[1:2, :] += jnp.sum(grad_second * hat, 0, keepdims=True)
        dres = cot + norm_back(grad_second * g2, hat, scale)
        r["dres"][rows, :] = dres
        low = dres.astype(BF16)
        r["dres_low"][rows, :] = low
        gm = dot(low, sq[4], NT).astype(BF16)
        r["dmixed"][rows, :] = gm
        here = pl.ds(i * per, per)
        for h in range(HEADS):
            wv = wvh[pl.ds(h * width, width), :]
            sides[here, pl.ds(h * ACT, ACT), :] = dot(gm, wv, NT).astype(BF16).reshape(per, ACT, width)
        return 0

    lax.fori_loop(0, tokens // ROWS, feed, 0)
    keep_out = pltpu.make_async_copy(r["out_v"], r["output"], out_sems.at[0])
    keep_out.start()
    keep_sides = pltpu.make_async_copy(sides, r["sides"], out_sems.at[1])
    keep_sides.start()

    grads = r["grads"]

    def put(base, tiles, value):
        for j in range(tiles):
            part = value[:, j * LANES : (j + 1) * LANES].reshape(GRID + (TILE, LANES))
            grads[:, :, :, :, pl.ds(base + j * TILE, TILE), :] = part

    def by_head(left, right):
        turned = left.T
        parts = [
            dot(turned[h * head_dim : (h + 1) * head_dim, :], right[:, pl.ds(h * width, width)])
            for h in range(HEADS)
        ]
        return jnp.concatenate(parts, axis=0).T

    put(0, 8, dot(r["second"][...], r["dhidden"][...], TN))
    if remote:
        update.start(0)
    put(MLP_ROWS, 8, dot(r["out_low"][...], r["active"][...], TN))
    if remote:
        update.start(1)
    put(SQ_AT[4], 2, dot(r["mixed"][...], r["dres_low"][...], TN))
    put(SQ_AT[3], 2, by_head(r["dmixed"][...], r["u"]))
    if remote:
        update.start(2)

    def attend_back(g, _):
        ids = [g * GROUP + k for k in range(GROUP)]
        rises = [dot(sides[s, low_rows, :], mem[s], NT) for s in ids]
        for s, rise in zip(ids, rises):
            probs = r["probs"][s]
            both = probs * rise
            weights[s, high_rows, :] = (both - probs * jnp.sum(both, -1, keepdims=True)).astype(BF16)
        for s in ids:
            dq = (dot(weights[s, high_rows, :], mem[s]) * 0.125).astype(BF16)
            rows = pl.ds(pl.multiple_of(s * ACT, ACT), ACT)
            for h in range(HEADS):
                r["dq_wide"][rows, pl.ds(h * width, width)] = dq[h * ACT : (h + 1) * ACT, :]
            end = dot(weights[s, :, LANES:KEYS_PAD], sides[s], TN)
            r["stamps"][s] = end[64:72, :]
        return 0

    quarter = groups // 4
    lax.fori_loop(0, quarter, attend_back, 0)
    if remote:
        update.one(0, 1)
    lax.fori_loop(quarter, 2 * quarter, attend_back, 0)
    if remote:
        update.two(0, 1)
        update.one(2)
    lax.fori_loop(2 * quarter, 3 * quarter, attend_back, 0)
    if remote:
        update.three(0, 1)
        update.two(2)
    lax.fori_loop(3 * quarter, groups, attend_back, 0)
    keep_pds = pltpu.make_async_copy(weights, r["pds"], out_sems.at[2])
    keep_pds.start()

    def queries_back(i, _):
        rows = pl.ds(pl.multiple_of(i * ROWS, ROWS), ROWS)
        r["dquery"][rows, :] = dot(r["dq_wide"][rows, :], wkh[...]).astype(BF16)
        return 0

    lax.fori_loop(0, tokens // ROWS, queries_back, 0)
    put(SQ_AT[1], 2, dot(r["first"][...], r["dquery"][...], TN))
    stamp_low = r["stamps"][:, 4:5, :].reshape(samples, width).astype(BF16)
    put(SQ_AT[0], 2, dot(r["embed"][...], stamp_low, TN))
    if remote:
        update.start(3)

    def acts_back(i, _):
        rows = pl.ds(pl.multiple_of(i * ROWS, ROWS), ROWS)
        grad_first = dot(r["dquery"][rows, :], sq[1], NT)
        hat = r["xhat"][rows, :]
        gain_acc[0:1, :] += jnp.sum(grad_first * hat, 0, keepdims=True)
        r["ag_v"][rows, :] = r["dres"][rows, :] + norm_back(grad_first * g1, hat, r["rstd"][rows, :])
        return 0

    lax.fori_loop(0, tokens // ROWS, acts_back, 0)
    put(SQ_AT[2], 2, by_head(r["query"][...], r["dq_wide"]))
    for norm in range(2):
        for j in range(2):
            row = gain_acc[norm : norm + 1, j * LANES : (j + 1) * LANES]
            at = GAIN_BASE + norm * 2 + j
            value = jnp.broadcast_to(row.reshape(1, 1, 1, 1, 1, LANES), GRID + (1, LANES))
            grads[:, :, :, :, at : at + 1, :] = value
    rest = WIRE - GAIN_BASE - 4
    grads[:, :, :, :, GAIN_BASE + 4 : WIRE, :] = jnp.zeros(GRID + (rest, LANES), F32)
    keep_ag = pltpu.make_async_copy(r["ag_v"], r["ag"], out_sems.at[3])
    keep_ag.start()
    if remote:
        update.start(4)
        update.three(2)
        update.one(3, 4)
        update.four(0, 1)
        update.two(3, 4)
        update.four(2)
        update.three(3, 4)
        update.four(3, 4)
        update.orthogonalize()
        update.give_all()
        out = r["out"]
        out[1, :, :] = r["moment"][...]
        out[2, pl.ds(GAIN_BASE, 16), :] = jnp.zeros((16, LANES), F32)
        update.take_all()
        gather.drain()
        update.drain()
    for copy in (keep_out, keep_sides, keep_pds, keep_ag):
        copy.wait()


def block_and_back(remote, acts, obs, flags, levels, cot, sqw, mlpw, gain, sqm=None, mlpm=None):
    tokens, width = acts.shape
    keys, samples = obs.shape[0], obs.shape[1]
    rows = HEADS * ACT
    wide = mlpw.shape[2]
    any_space = pl.BlockSpec(memory_space=pl.ANY)
    in_vmem = pl.BlockSpec(memory_space=VMEM)
    scalars = pl.BlockSpec(memory_space=pltpu.SMEM)
    sem = pltpu.SemaphoreType.DMA
    ins = dict(flags=flags, levels=levels, acts=acts, obs=obs, cot=cot, sqw=sqw, mlpw=mlpw, gain=gain)
    outs = dict(
        output=jax.ShapeDtypeStruct(acts.shape, F32),
        ag=jax.ShapeDtypeStruct(acts.shape, F32),
        pds=jax.ShapeDtypeStruct((samples, 2 * rows, KEYS_PAD), BF16),
        sides=jax.ShapeDtypeStruct((samples, 2 * rows, width), BF16),
    )
    grads = GRID + (WIRE, LANES)
    scratch = dict(
        obs_v=VMEM(obs.shape, BF16),
        acts_v=VMEM(acts.shape, F32),
        cot_v=VMEM(acts.shape, F32),
        spread=VMEM((2 * keys * 16, LANES), F32),
        mem=VMEM((samples, KEYS_PAD, width), BF16),
        tail=VMEM((samples, 16, width), F32),
        sq_all=VMEM((5, width, width), BF16),
        mlp_all=VMEM((2, width, wide), BF16),
        gain_all=VMEM((2, width), F32),
        wkh=VMEM((HEADS * width, width), BF16),
        wvh=VMEM((HEADS * width, width), BF16),
        first=VMEM((tokens, width), BF16),
        query=VMEM((tokens, width), BF16),
        xhat=VMEM((tokens, width), F32),
        rstd=VMEM((tokens, 1), F32),
        probs=VMEM((samples, rows, KEYS_PAD), F32),
        pds_v=VMEM((samples, 2 * rows, KEYS_PAD), BF16),
        sides_v=VMEM((samples, 2 * rows, width), BF16),
        u=VMEM((tokens, HEADS * width), BF16),
        dq_wide=VMEM((tokens, HEADS * width), BF16),
        mixed=VMEM((tokens, width), BF16),
        second=VMEM((tokens, width), BF16),
        active=VMEM((tokens, wide), BF16),
        dhidden=VMEM((tokens, wide), BF16),
        out_low=VMEM((tokens, width), BF16),
        dres_low=VMEM((tokens, width), BF16),
        dres=VMEM((tokens, width), F32),
        dmixed=VMEM((tokens, width), BF16),
        dquery=VMEM((tokens, width), BF16),
        out_v=VMEM((tokens, width), F32),
        ag_v=VMEM((tokens, width), F32),
        angle=VMEM((samples, width // 2), F32),
        embed=VMEM((samples, width), BF16),
        stamps=VMEM((samples, 8, width), F32),
        gain_acc=VMEM((8, width), F32),
        in_sems=sem((8,)),
        out_sems=sem((4,)),
    )
    extra = {}
    if remote:
        ins.update(sqm=sqm, mlpm=mlpm)
        outs.update(out=jax.ShapeDtypeStruct((3, WIRE, LANES), F32))
        chunks = len(CHUNKS)
        scratch.update(
            grads=VMEM(grads, F32),
            sqw_v=VMEM(sqw.shape, F32),
            mlpw_v=VMEM(mlpw.shape, F32),
            gain_v=VMEM(gain.shape, F32),
            sqm_v=VMEM(sqm.shape, F32),
            mlpm_v=VMEM(mlpm.shape, F32),
            wire=VMEM(grads, BF16),
            edge=VMEM((16, LANES), F32),
            gsend=sem((chunks, 6)),
            grecv=sem((chunks, 6)),
            got_core=VMEM((4, 2, 2, WIRE, LANES), F32),
            sum1=VMEM((4, 2, 2, WIRE, LANES), F32),
            send1=VMEM((4, 2, WIRE, LANES), BF16),
            got1=VMEM((4, 2, WIRE, LANES), BF16),
            sum2=VMEM((4, 2, WIRE, LANES), F32),
            send2=VMEM((4, WIRE, LANES), BF16),
            got2=VMEM((4, WIRE, LANES), BF16),
            sum3=VMEM((4, WIRE, LANES), F32),
            send3=VMEM((3, WIRE, LANES), BF16),
            got3=VMEM((3, WIRE, LANES), BF16),
            moment=VMEM((WIRE, LANES), F32),
            slabs_sq=VMEM((32, SQ_ROWS, LANES), F32),
            slabs_mlp=VMEM((32, MLP_ROWS, LANES), F32),
            result_sq=VMEM((32, SQ_ROWS, LANES), F32),
            result_mlp=VMEM((32, MLP_ROWS, LANES), F32),
            cur=VMEM((width, wide), F32),
            gram_s=VMEM((width, width), F32),
            prod_s=VMEM((width, width), F32),
            send=sem((chunks, 6)),
            recv=sem((chunks, 6)),
            own_send=sem((7,)),
            own_recv=sem((1,)),
            back_send=sem((32,)),
            back_recv=sem((7,)),
        )
        extra = dict(collective_id=0, has_side_effects=True)
    else:
        outs.update(grads=jax.ShapeDtypeStruct(grads, F32))
    names = tuple(ins) + tuple(outs) + tuple(scratch)
    results = pl.pallas_call(
        functools.partial(block_kernel, names, remote),
        out_shape=tuple(outs.values()),
        in_specs=[scalars if name in ("flags", "levels") else any_space for name in ins],
        out_specs=[in_vmem if name in ("out", "grads") else any_space for name in outs],
        scratch_shapes=list(scratch.values()),
        compiler_params=pltpu.CompilerParams(vmem_limit_bytes=56 << 20, **extra),
        name="block_and_back",
    )(*ins.values())
    return dict(zip(outs, results))


def finish_kernel(names, rate, *args):
    r = dict(zip(names, args))
    samples, rows, _ = r["pds"].shape
    keys = r["og"].shape[0] // samples
    groups = samples // GROUP
    sems = r["sems"]
    moves = []
    for i in range(groups):
        block = pl.ds(i * GROUP, GROUP)
        moves.append(
            (
                pltpu.make_async_copy(r["pds"].at[block], r["pds_v"].at[block], sems.at[2 * i]),
                pltpu.make_async_copy(r["sides"].at[block], r["sides_v"].at[block], sems.at[2 * i + 1]),
            )
        )
    for pair in moves:
        for copy in pair:
            copy.start()
    more = 2 * groups
    passes = [pltpu.make_async_copy(r[a], r[b], sems.at[more + i]) for i, (a, b) in enumerate((("output", "output_f"), ("ag", "ag_f")))] if "ag_f" in r else []
    for copy in passes:
        copy.start()
    more += 2
    small = []
    if "wire" in r:
        for i, name in enumerate(("wire", "sqw", "mlpw", "gain", "gainm")):
            small.append(pltpu.make_async_copy(r[name], r[name + "_v"], sems.at[more + i]))
            small[-1].start()
        more += 5

    spread = r["spread"]

    def observed(part, g):
        low, high, end = ((0, LANES, LANES), (LANES, KEYS_PAD, keys))[part]
        for k in range(GROUP):
            s = g * GROUP + k
            value = dot(r["pds_v"][s, :, low:high], r["sides_v"][s], TN)
            for side in range(2):
                at = side * keys * samples + low * samples + s
                spread[pl.ds(at, end - low, stride=samples), :] = value[0 : end - low, side * LANES : (side + 1) * LANES]

    def leave(part, side):
        low, end = ((0, LANES), (LANES, keys))[part]
        there = pl.ds(low * samples, (end - low) * samples)
        here = pl.ds(side * keys * samples + low * samples, (end - low) * samples)
        target = r["og"].at[there, pl.ds(side * LANES, LANES)]
        return pltpu.make_async_copy(spread.at[here], target, sems.at[more + 2 * part + side])

    for g, pair in enumerate(moves):
        for copy in pair:
            copy.wait()
        observed(0, g)
    for side in range(2):
        leave(0, side).start()
    for g in range(groups):
        observed(1, g)
    for side in range(2):
        leave(1, side).start()

    if "wire" in r:
        for copy in small:
            copy.wait()
        finish_weights(r, rate)
    for part in range(2):
        for side in range(2):
            leave(part, side).wait()
    for copy in passes:
        copy.wait()


def finish_weights(r, rate):
    wire = r["wire_v"]
    me = lax.axis_index("dp")
    for m in range(5):
        for j in range(2):
            rows, columns = pl.ds(SQ_AT[m] + j * TILE, TILE), pl.ds(j * LANES, LANES)
            r["sqg"][m, :, columns] = wire[0, rows, :]
            r["sqm"][m, :, columns] = wire[1, rows, :]
            r["sqn"][m, :, columns] = r["sqw_v"][m, :, columns] - SQ_RATES[m] * wire[2, rows, :]
    r["sqc"][...] = r["sqn"][...].astype(BF16)
    for m in range(2):
        for j in range(8):
            rows, columns = pl.ds(m * MLP_ROWS + j * TILE, TILE), pl.ds(j * LANES, LANES)
            r["mlpg"][m, :, columns] = wire[0, rows, :]
            r["mlpm"][m, :, columns] = wire[1, rows, :]
            r["mlpn"][m, :, columns] = r["mlpw_v"][m, :, columns] - MLP_RATES[m] * wire[2, rows, :]
    r["mlpc"][...] = r["mlpn"][...].astype(BF16)
    tile = wire[0, pl.ds(GAIN_BASE, TILE), :]
    turned = pltpu.roll(tile, (LANES - (me % 16) * TILE) % LANES, 1)
    at = me // 16
    for norm in range(2):
        pair = turned[2 * norm : 2 * norm + 2, 0:TILE]
        row = jnp.where(at == 0, pair[0:1, :], pair[1:2, :])
        new = 0.5 * r["gainm_v"][norm : norm + 1, :] + row
        r["gg"][norm : norm + 1, :] = row
        r["gm"][norm : norm + 1, :] = new
        r["gn"][norm : norm + 1, :] = r["gain_v"][norm : norm + 1, :] - rate * new


def finish(rate, keys, made, sqw=None, mlpw=None, gain=None, gainm=None):
    any_space = pl.BlockSpec(memory_space=pl.ANY)
    in_vmem = pl.BlockSpec(memory_space=VMEM)
    pds, sides = made["pds"], made["sides"]
    samples, rows, width = sides.shape
    ins = dict(pds=pds, sides=sides)
    outs = dict(og=jax.ShapeDtypeStruct((keys * samples, width), F32))
    far = set(ins) | set(outs) | {"output", "ag", "output_f", "ag_f"}
    if "out" in made:
        ins.update(output=made["output"], ag=made["ag"], wire=made["out"], sqw=sqw, mlpw=mlpw, gain=gain, gainm=gainm)
        like = jax.ShapeDtypeStruct
        outs.update(
            output_f=like(made["output"].shape, F32),
            ag_f=like(made["ag"].shape, F32),
            sqg=like(sqw.shape, F32),
            sqm=like(sqw.shape, F32),
            sqn=like(sqw.shape, F32),
            sqc=like(sqw.shape, BF16),
            mlpg=like(mlpw.shape, F32),
            mlpm=like(mlpw.shape, F32),
            mlpn=like(mlpw.shape, F32),
            mlpc=like(mlpw.shape, BF16),
            gg=like(gain.shape, F32),
            gm=like(gain.shape, F32),
            gn=like(gain.shape, F32),
        )
    scratch = dict(
        pds_v=VMEM(pds.shape, BF16),
        sides_v=VMEM(sides.shape, BF16),
        spread=VMEM((2 * keys * samples, LANES), F32),
        sems=pltpu.SemaphoreType.DMA((2 * (samples // GROUP) + 11,)),
    )
    if "out" in made:
        for name in ("wire", "sqw", "mlpw", "gain", "gainm"):
            scratch[name + "_v"] = VMEM(ins[name].shape, F32)
            far.add(name)
    names = tuple(ins) + tuple(outs) + tuple(scratch)
    results = pl.pallas_call(
        functools.partial(finish_kernel, names, rate),
        out_shape=tuple(outs.values()),
        in_specs=[any_space if name in far else in_vmem for name in ins],
        out_specs=[any_space if name in far else in_vmem for name in outs],
        scratch_shapes=list(scratch.values()),
        compiler_params=pltpu.CompilerParams(vmem_limit_bytes=60 << 20),
        name="finish",
    )(*ins.values())
    return dict(zip(outs, results))


HIGH_PRECISION = lax.Precision.HIGHEST


def plain_orthogonalize(matrix):
    current = matrix / (jnp.sqrt(jnp.sum(matrix * matrix)) + 1e-07)
    for turn in range(5):
        gram = jnp.dot(current, current.T, precision=HIGH_PRECISION)
        poly = COEF_B * gram + COEF_C * jnp.dot(gram, gram, precision=HIGH_PRECISION)
        current = COEF_A * current + jnp.dot(poly, current, precision=HIGH_PRECISION)
    return current


def pick_owned(stack, owners, device):
    chosen = jnp.zeros_like(stack[0])
    for index in range(len(owners)):
        chosen = jnp.where(device == owners[index], stack[index], chosen)
    return chosen


def is_owner(owners, device):
    flag = device < 0
    for owner in owners:
        flag = jnp.logical_or(flag, device == owner)
    return flag


def from_wire(grads):
    def matrix(base, tiles):
        part = grads[:, base : base + tiles * TILE, :].reshape(-1, tiles, TILE, LANES)
        return part.transpose(0, 2, 1, 3).reshape(-1, tiles * LANES)

    square = jnp.stack([matrix(SQ_AT[m], 2) for m in range(5)])
    mlp = jnp.stack([matrix(m * MLP_ROWS, 8) for m in range(2)])
    return square, mlp, grads[0, GAIN_BASE : GAIN_BASE + 4, :].reshape(2, 2 * LANES)


def update_by_collectives(
    grads, square_weights, mlp_weights, gains, square_moment, mlp_moment, gain_moment, rate
):
    square_local, mlp_local, gain_local = from_wire(grads)
    square_grad, mlp_grad, gain_grad = (
        lax.psum_scatter(square_local, "dp", scatter_dimension=1, tiled=True),
        lax.psum_scatter(mlp_local, "dp", scatter_dimension=1, tiled=True),
        lax.psum_scatter(gain_local, "dp", scatter_dimension=1, tiled=True),
    )
    square_moment_new = 0.5 * square_moment + square_grad
    mlp_moment_new = 0.5 * mlp_moment + mlp_grad
    gain_moment_new = 0.5 * gain_moment + gain_grad
    device = lax.axis_index("dp")
    count = lax.axis_size("dp")
    square_owners = [index * count // 7 for index in range(5)]
    mlp_owners = [(index + 5) * count // 7 for index in range(2)]
    square_full, mlp_full = (
        lax.all_gather(square_moment_new, "dp", axis=1, tiled=True),
        lax.all_gather(mlp_moment_new, "dp", axis=1, tiled=True),
    )
    mine_square = pick_owned(square_full, square_owners, device)
    mine_mlp = pick_owned(mlp_full, mlp_owners, device)
    made_square = lax.cond(
        is_owner(square_owners, device), plain_orthogonalize, jnp.zeros_like, mine_square
    )
    made_mlp = lax.cond(is_owner(mlp_owners, device), plain_orthogonalize, jnp.zeros_like, mine_mlp)
    stack_square = jnp.stack(
        [jnp.where(device == owner, made_square, 0.0) for owner in square_owners]
    )
    stack_mlp = jnp.stack([jnp.where(device == owner, made_mlp, 0.0) for owner in mlp_owners])
    square_ortho, mlp_ortho = (
        lax.psum_scatter(stack_square, "dp", scatter_dimension=1, tiled=True),
        lax.psum_scatter(stack_mlp, "dp", scatter_dimension=1, tiled=True),
    )
    square_new = square_weights - jnp.array(SQ_RATES, F32)[:, None, None] * square_ortho
    mlp_new = mlp_weights - jnp.array(MLP_RATES, F32)[:, None, None] * mlp_ortho
    gains_new = gains - rate * gain_moment_new
    return (
        square_grad,
        square_moment_new,
        square_new,
        square_new.astype(BF16),
        mlp_grad,
        mlp_moment_new,
        mlp_new,
        mlp_new.astype(BF16),
        gain_grad,
        gain_moment_new,
        gains_new,
    )


def per_device(
    actions,
    observed,
    camera_flags,
    noise_levels,
    cotangent,
    square_weights,
    mlp_weights,
    gains,
    square_moment,
    mlp_moment,
    gain_moment,
):
    count = lax.axis_size("dp")
    rate = 0.1 / math.sqrt(actions.shape[0] * count)
    by_key = observed.transpose(1, 0, 2)
    keys, samples, width = by_key.shape
    ins = (actions, by_key, camera_flags, noise_levels, cotangent)
    if count == math.prod(GRID):
        made = block_and_back(True, *ins, square_weights, mlp_weights, gains, square_moment, mlp_moment)
        done = finish(rate, keys, made, square_weights, mlp_weights, gains, gain_moment)
        output, actions_grad = done["output_f"], done["ag_f"]
        names = ("sqg", "sqm", "sqn", "sqc", "mlpg", "mlpm", "mlpn", "mlpc", "gg", "gm", "gn")
        rest = tuple(done[name] for name in names)
    else:
        square_all, mlp_all = (
            lax.all_gather(square_weights.astype(BF16), "dp", axis=1, tiled=True),
            lax.all_gather(mlp_weights.astype(BF16), "dp", axis=1, tiled=True),
        )
        gain_all = lax.all_gather(gains, "dp", axis=1, tiled=True)
        made = block_and_back(False, *ins, square_all, mlp_all, gain_all)
        done = finish(rate, keys, made)
        output, actions_grad = made["output"], made["ag"]
        grads = made["grads"].reshape(-1, WIRE, LANES)
        rest = update_by_collectives(
            grads, square_weights, mlp_weights, gains, square_moment, mlp_moment, gain_moment, rate
        )
    observed_grad = done["og"].reshape(keys, samples, width).transpose(1, 0, 2)
    return (output, actions_grad, observed_grad) + tuple(rest)


def solution(mesh):
    rows, cube, flat = P("dp", None), P("dp", None, None), P("dp")
    stacked, pair = P(None, "dp", None), P(None, "dp")
    return jax.shard_map(
        per_device,
        mesh=mesh,
        in_specs=(rows, cube, flat, flat, rows, stacked, stacked, pair, stacked, stacked, pair),
        out_specs=(rows, rows, cube) + (stacked,) * 8 + (pair,) * 3,
        check_vma=False,
    )
```

```python
import functools
import math

import jax
import jax.numpy as jnp
from jax import lax
from jax.experimental import pallas as pl
from jax.experimental.pallas import tpu as pltpu
from jax.sharding import PartitionSpec as P

HEADS = 4
ACT = 16
OBS_FULL = 196
OBS_FEW = 49
COEF_A = 3.4445
COEF_B = -4.775
COEF_C = 2.0315
F32 = jnp.float32
BF16 = jnp.bfloat16
MESH = pl.DeviceIdType.MESH
VMEM = pltpu.VMEM
NN = (((1,), (0,)), ((), ()))
NT = (((1,), (1,)), ((), ()))
TN = (((0,), (0,)), ((), ()))

LANES = 128
TILE = 8
MLP_ROWS = 64
SQ_ROWS = 16
SQ_AT = (160, 176, 192, 128, 144)
GAIN_BASE = 208
WIRE = 224
CHUNKS = ((0, 64), (64, 64), (128, 32), (160, 32), (192, 32))
X_FIRST = (True, False, True, True, False)
MLP_RATES = (1.0, 0.5)
SQ_RATES = (0.5, 0.5, 0.5, 0.5, 4.0)
GRID = (4, 2, 2, 2)
OWNERS = (8, 22, 14, 16, 11, 21, 13)
KEYS_PAD = 208
GROUP = 4
ROWS = 256


class Refs:
    def __init__(self, pairs):
        self.__dict__.update(pairs)


def dot(left, right, dims=NN):
    return lax.dot_general(left, right, dims, preferred_element_type=F32)


def place():
    me = lax.axis_index("dp")
    return me, me // 8, (me // 4) % 2, (me // 2) % 2, me % 2


def device_at(z, y, x, c):
    return ((z * 2 + y) * 2 + x) * 2 + c


def link(src, dst, send, recv, device):
    return pltpu.make_async_remote_copy(
        src_ref=src,
        dst_ref=dst,
        send_sem=send,
        recv_sem=recv,
        device_id=(device,),
        device_id_type=MESH,
    )


def greet(device):
    pl.semaphore_signal(
        pltpu.get_barrier_semaphore(), inc=1, device_id=(device,), device_id_type=MESH
    )


def halves(value):
    high = value.astype(BF16)
    return high, (value - high.astype(F32)).astype(BF16)


def dot3(left, right, dims=NN):
    (lh, ll), (rh, rl) = left, right
    return dot(lh, rh, dims) + (dot(lh, rl, dims) + dot(ll, rh, dims))


def normalize(values):
    centred = values - jnp.mean(values, -1, keepdims=True)
    scale = lax.rsqrt(jnp.mean(centred * centred, -1, keepdims=True) + 1e-05)
    return centred * scale, scale


def norm_back(grad, hat, scale):
    mean_one = jnp.mean(grad, -1, keepdims=True)
    mean_two = jnp.mean(grad * hat, -1, keepdims=True)
    return scale * (grad - mean_one - hat * mean_two)


class Gather:
    def __init__(self, r):
        self.r = r
        self.me, self.z, self.y, self.x, self.c = place()

    def hop(self, k, step, part, device):
        return link(part, part, self.r.gsend.at[k, step], self.r.grecv.at[k, step], device)

    def along_z(self, k, step):
        part = self.r.wire.at[self.z, self.y, self.x, self.c, pl.ds(*CHUNKS[k])]
        return self.hop(k, step, part, device_at((self.z + step + 1) % 4, self.y, self.x, self.c))

    def from_z(self, k, step):
        there = (self.z + 3 - step) % 4
        part = self.r.wire.at[there, self.y, self.x, self.c, pl.ds(*CHUNKS[k])]
        return self.hop(k, step, part, device_at(there, self.y, self.x, self.c))

    def plane(self, k, second, mine):
        z, y, x, c = self.z, self.y, self.x, self.c
        rows, wire = pl.ds(*CHUNKS[k]), self.r.wire
        py, px = (y, x) if mine else (1 - y, 1 - x)
        along_x = X_FIRST[k] == second
        if along_x:
            part = wire.at[:, y, px, c, rows] if second else wire.at[:, :, px, c, rows]
            return self.hop(k, 3 if second else 4, part, device_at(z, y, 1 - x, c))
        part = wire.at[:, py, x, c, rows] if second else wire.at[:, py, :, c, rows]
        return self.hop(k, 3 if second else 4, part, device_at(z, 1 - y, x, c))

    def core(self, k, mine):
        part = self.r.wire.at[:, :, :, self.c if mine else 1 - self.c, pl.ds(*CHUNKS[k])]
        return self.hop(k, 5, part, device_at(self.z, self.y, self.x, 1 - self.c))

    def first(self, *chunks):
        for k in chunks:
            for step in range(3):
                self.along_z(k, step).start()

    def second(self, *chunks):
        for k in chunks:
            for step in range(3):
                self.from_z(k, step).wait_recv()
            self.plane(k, True, True).start()

    def third(self, *chunks):
        for k in chunks:
            self.plane(k, True, False).wait_recv()
            self.plane(k, False, True).start()

    def fourth(self, *chunks):
        for k in chunks:
            self.plane(k, False, False).wait_recv()
            self.core(k, True).start()

    def last(self, *chunks):
        for k in chunks:
            self.core(k, False).wait_recv()

    def drain(self):
        for k in range(len(CHUNKS)):
            for step in range(3):
                self.along_z(k, step).wait_send()
            self.plane(k, True, True).wait_send()
            self.plane(k, False, True).wait_send()
            self.core(k, True).wait_send()

    def fill(self):
        r = self.r
        spot = (self.z, self.y, self.x, self.c)

        def tiles(source, m, base, number):
            for j in range(number):
                pair = [source[m, :, pl.ds((2 * j + k) * LANES, LANES)] for k in range(2)]
                r.wire[spot + (pl.ds(base + j * 16, 16),)] = jnp.concatenate(pair, axis=0).astype(BF16)

        for m in range(5):
            tiles(r.sqw_v, m, SQ_AT[m], 1)
        for m in range(2):
            tiles(r.mlpw_v, m, m * MLP_ROWS, 4)
        gains, edge = r.gain_v[...], r.edge
        high = gains.astype(BF16).astype(F32)
        middle = (gains - high).astype(BF16).astype(F32)
        edge[...] = jnp.zeros_like(edge)
        edge[0:2, 0:TILE] = high
        edge[2:4, 0:TILE] = middle
        edge[4:6, 0:TILE] = (gains - high - middle).astype(BF16).astype(F32)
        r.wire[spot + (pl.ds(GAIN_BASE, 16),)] = edge[...].astype(BF16)

    def unpack(self, base, number, out, m):
        for j in range(number):
            block = self.r.wire[:, :, :, :, pl.ds(base + j * 16, 16), :].reshape(32, 16, LANES).astype(F32)
            for half in range(2):
                columns = pl.ds((2 * j + half) * LANES, LANES)
                out[m, :, columns] = block[:, half * 8 : half * 8 + 8, :].reshape(256, LANES).astype(BF16)

    def unpack_gains(self):
        edge, wire = self.r.edge, self.r.wire
        for half in range(2):
            total = jnp.zeros((16, LANES), F32)
            for at in range(16):
                d = half * 16 + at
                tile = wire[d // 8, (d // 4) % 2, (d // 2) % 2, d % 2, pl.ds(GAIN_BASE, 16), :].astype(F32)
                total = total + (tile if at == 0 else pltpu.roll(tile, at * TILE, 1))
            edge[...] = total
            self.r.gain_all[:, pl.ds(half * LANES, LANES)] = edge[0:2, :] + edge[2:4, :] + edge[4:6, :]


class Update:
    def __init__(self, r):
        self.r = r
        self.me, self.z, self.y, self.x, self.c = place()

    def hop(self, k, step, src, dst, device):
        return link(src, dst, self.r.send.at[k, step], self.r.recv.at[k, step], device)

    def core(self, k):
        rows = pl.ds(*CHUNKS[k])
        src, dst = self.r.grads.at[:, :, :, 1 - self.c, rows], self.r.got_core.at[:, :, :, rows]
        return self.hop(k, 0, src, dst, device_at(self.z, self.y, self.x, 1 - self.c))

    def plane(self, k, first):
        rows = pl.ds(*CHUNKS[k])
        to = (self.z, self.y, 1 - self.x, self.c) if X_FIRST[k] == first else (self.z, 1 - self.y, self.x, self.c)
        if first:
            src, dst = self.r.send1.at[:, :, rows], self.r.got1.at[:, :, rows]
        else:
            src, dst = self.r.send2.at[:, rows], self.r.got2.at[:, rows]
        return self.hop(k, 1 if first else 2, src, dst, device_at(*to))

    def along_z(self, k, step):
        rows = pl.ds(*CHUNKS[k])
        to = device_at((self.z + step + 1) % 4, self.y, self.x, self.c)
        return self.hop(k, 3 + step, self.r.send3.at[step, rows], self.r.got3.at[step, rows], to)

    def start(self, k):
        self.core(k).start()

    def one(self, *chunks):
        r = self.r
        for k in chunks:
            rows = pl.ds(*CHUNKS[k])
            self.core(k).wait_recv()
            sum1 = r.sum1
            sum1[:, :, :, rows, :] = r.grads[:, :, :, self.c, rows, :] + r.got_core[:, :, :, rows, :]
            other = sum1[:, :, 1 - self.x, rows, :] if X_FIRST[k] else sum1[:, 1 - self.y, :, rows, :]
            r.send1[:, :, rows, :] = other.astype(BF16)
            self.plane(k, True).start()

    def two(self, *chunks):
        r = self.r
        for k in chunks:
            rows = pl.ds(*CHUNKS[k])
            self.plane(k, True).wait_recv()
            sum1, sum2 = r.sum1, r.sum2
            mine = sum1[:, :, self.x, rows, :] if X_FIRST[k] else sum1[:, self.y, :, rows, :]
            sum2[:, :, rows, :] = mine + r.got1[:, :, rows, :].astype(F32)
            other = 1 - self.y if X_FIRST[k] else 1 - self.x
            r.send2[:, rows, :] = sum2[:, other, rows, :].astype(BF16)
            self.plane(k, False).start()

    def three(self, *chunks):
        r = self.r
        for k in chunks:
            rows = pl.ds(*CHUNKS[k])
            self.plane(k, False).wait_recv()
            mine = self.y if X_FIRST[k] else self.x
            r.sum3[:, rows, :] = r.sum2[:, mine, rows, :] + r.got2[:, rows, :].astype(F32)
            for step in range(3):
                r.send3[step, rows, :] = r.sum3[(self.z + step + 1) % 4, rows, :].astype(BF16)
                self.along_z(k, step).start()

    def slab(self, index):
        if index < 2:
            return pl.ds(index * MLP_ROWS, MLP_ROWS), self.r.slabs_mlp, self.r.result_mlp
        return pl.ds(SQ_AT[index - 2], SQ_ROWS), self.r.slabs_sq, self.r.result_sq

    def to_owner(self, index):
        rows, slabs, _ = self.slab(index)
        return link(
            self.r.moment.at[rows], slabs.at[self.me],
            self.r.own_send.at[index], self.r.own_recv.at[0], OWNERS[index],
        )

    def four(self, *chunks):
        r = self.r
        moment, out = r.moment, r.out
        for k in chunks:
            rows = pl.ds(*CHUNKS[k])
            total = r.sum3[self.z, rows, :]
            for step in range(3):
                self.along_z(k, step).wait_recv()
                total = total + r.got3[step, rows, :].astype(F32)
            out[0, rows, :] = total
            moment[rows, :] = 0.5 * moment[rows, :] + total
            for index in ((0,), (1,), (5, 6), (2, 3), (4,))[k]:
                rows_m, slabs, _ = self.slab(index)

                @pl.when(self.me != OWNERS[index])
                def _():
                    self.to_owner(index).start()

                @pl.when(self.me == OWNERS[index])
                def _():
                    pltpu.make_async_copy(moment.at[rows_m], slabs.at[self.me], r.own_recv.at[0]).start()

    def old_moment(self):
        r = self.r
        moment = r.moment
        for m in range(2):
            for j in range(8):
                moment[pl.ds(m * MLP_ROWS + j * TILE, TILE), :] = r.mlpm_v[m, :, pl.ds(j * LANES, LANES)]
        for m in range(5):
            for j in range(2):
                moment[pl.ds(SQ_AT[m] + j * TILE, TILE), :] = r.sqm_v[m, :, pl.ds(j * LANES, LANES)]
        moment[pl.ds(GAIN_BASE, 16), :] = jnp.zeros((16, LANES), F32)

    def orthogonalize(self):
        r = self.r
        cur, gram_s, prod_s = r.cur, r.gram_s, r.prod_s

        def load(slabs, tiles):
            total = jnp.zeros((1, 1), F32)
            for j in range(tiles):
                part = slabs[:, pl.ds(j * TILE, TILE), :].reshape(256, LANES)
                cur[:, pl.ds(j * LANES, LANES)] = part
                total = total + jnp.sum(jnp.sum(part * part, axis=0, keepdims=True), axis=1, keepdims=True)
            width = tiles * LANES
            cur[:, 0:width] = cur[:, 0:width] * (1.0 / (jnp.sqrt(total) + 1e-07))

        mine_mlp = jnp.logical_or(self.me == OWNERS[0], self.me == OWNERS[1])
        mine_sq = self.me < 0
        for device in OWNERS[2:]:
            mine_sq = jnp.logical_or(mine_sq, self.me == device)

        @pl.when(mine_mlp)
        def _():
            slabs, result = r.slabs_mlp, r.result_mlp
            pltpu.make_async_copy(slabs, slabs, r.own_recv.at[0]).wait()
            load(slabs, 8)
            x = halves(cur[...])
            gram_s[...] = dot3(x, x, NT)
            rows = lax.broadcasted_iota(jnp.int32, (256, 256), 0)
            one = (rows == lax.broadcasted_iota(jnp.int32, (256, 256), 1)).astype(F32)
            prod_s[...] = one

            def turn(k, _):
                gram = gram_s[...]
                g = halves(gram)
                p = halves(COEF_A * one + COEF_B * gram + COEF_C * dot3(g, g))
                prod_s[...] = dot3(p, halves(prod_s[...]))
                gram_s[...] = dot3(halves(dot3(p, g)), p)
                return 0

            lax.fori_loop(0, 5, turn, 0)
            prod = halves(prod_s[...])
            for j in range(8):
                part = dot3(prod, halves(cur[:, pl.ds(j * LANES, LANES)]))
                result[:, pl.ds(j * TILE, TILE), :] = part.reshape(32, TILE, LANES)

        @pl.when(mine_sq)
        def _():
            slabs, result = r.slabs_sq, r.result_sq
            pltpu.make_async_copy(slabs, slabs, r.own_recv.at[0]).wait()
            load(slabs, 2)

            def turn(k, _):
                now = cur[:, 0:256]
                x = halves(now)
                gram = dot3(x, x, NT)
                g = halves(gram)
                p = halves(COEF_B * gram + COEF_C * dot3(g, g))
                cur[:, 0:256] = COEF_A * now + dot3(p, x)
                return 0

            lax.fori_loop(0, 5, turn, 0)
            for j in range(2):
                part = cur[:, pl.ds(j * LANES, LANES)]
                result[:, pl.ds(j * TILE, TILE), :] = part.reshape(32, TILE, LANES)

    def give_back(self, index, device):
        rows, _, result = self.slab(index)
        return link(
            result.at[device], self.r.out.at[2, rows],
            self.r.back_send.at[device], self.r.back_recv.at[index], device,
        )

    def give_all(self):
        r = self.r
        for index in range(7):
            rows, _, result = self.slab(index)

            @pl.when(self.me == OWNERS[index])
            def _():
                def send_one(step, _):
                    self.give_back(index, (self.me + step) % 32).start()
                    return 0

                lax.fori_loop(1, 32, send_one, 0)
                pltpu.make_async_copy(result.at[self.me], r.out.at[2, rows], r.back_recv.at[index]).start()

    def take_all(self):
        for index in range(7):
            rows, _, result = self.slab(index)
            pltpu.make_async_copy(result.at[0], self.r.out.at[2, rows], self.r.back_recv.at[index]).wait()

    def drain(self):
        for index in range(7):

            @pl.when(self.me != OWNERS[index])
            def _():
                self.to_owner(index).wait_send()

            @pl.when(self.me == OWNERS[index])
            def _():
                def wait_one(step, _):
                    self.give_back(index, (self.me + step) % 32).wait_send()
                    return 0

                lax.fori_loop(1, 32, wait_one, 0)

        for k in range(len(CHUNKS)):
            self.core(k).wait_send()
            self.plane(k, True).wait_send()
            self.plane(k, False).wait_send()
            for step in range(3):
                self.along_z(k, step).wait_send()


def greet_all():
    me, z, y, x, c = place()
    greet(device_at(z, y, x, 1 - c))
    greet(device_at(z, y, 1 - x, c))
    greet(device_at(z, 1 - y, x, c))
    for step in range(1, 4):
        greet(device_at((z + step) % 4, y, x, c))
    owner = me < 0
    for device in OWNERS:
        owner = jnp.logical_or(owner, me == device)

        @pl.when(me != device)
        def _():
            greet(device)

    @pl.when(owner)
    def _():
        def greet_other(step, _):
            greet((me + step) % 32)
            return 0

        lax.fori_loop(1, 32, greet_other, 0)

    is_owner = owner.astype(jnp.int32)
    return 6 + 7 - is_owner + 31 * is_owner


def block_kernel(names, remote, *args):
    r = Refs(zip(names, args))
    keys, samples = r.obs.shape[0], r.obs.shape[1]
    tokens, width = r.acts.shape
    head_dim, half, per = width // HEADS, width // 2, ROWS // ACT
    wide = r.mlp_all.shape[2]
    groups = samples // GROUP
    in_sems, out_sems = r.in_sems, r.out_sems

    if remote:
        own = (r.sqw_v, r.mlpw_v, r.gain_v)
    else:
        own = (r.sq_all, r.mlp_all, r.gain_all)
    loads = list(zip((r.sqw, r.mlpw, r.gain), own))
    loads += [(r.acts, r.acts_v), (r.obs, r.obs_v.at[pl.ds(0, keys)]), (r.cot, r.cot_v)]
    if remote:
        loads += [(r.sqm, r.sqm_v), (r.mlpm, r.mlpm_v)]
    copies = [pltpu.make_async_copy(a, b, in_sems.at[i]) for i, (a, b) in enumerate(loads)]

    def arrive(*which):
        for i in which:
            copies[i].wait()

    for copy in copies:
        copy.start()
    if remote:
        gather, update = Gather(r), Update(r)
        expected = greet_all()
        arrive(0, 1, 2)
        gather.fill()
        pl.semaphore_wait(pltpu.get_barrier_semaphore(), expected)
        gather.first(3, 4, 2)

    arrive(3)

    def hats(i, _):
        rows = pl.ds(pl.multiple_of(i * ROWS, ROWS), ROWS)
        hat, scale = normalize(r.acts_v[rows, :])
        r.xhat[rows, :] = hat
        r.rstd[rows, :] = scale
        return 0

    lax.fori_loop(0, tokens // ROWS, hats, 0)

    mem, obs_v = r.mem, r.obs_v
    batch = 16
    chunks = KEYS_PAD // batch

    def turn(part, low, high):
        def one(j, _):
            at = pl.ds(pl.multiple_of(j * batch, batch), batch)
            here = pl.ds(part * batch, batch)
            for side in range(2):
                columns = pl.ds(side * LANES, LANES)
                mem[here, at, columns] = jnp.transpose(obs_v[at, here, columns], (1, 0, 2))
            return 0

        lax.fori_loop(low, high, one, 0)

    whole = chunks - 1
    arrive(4)
    turn(0, 0, whole // 2)
    if remote:
        gather.second(3, 4, 2)
        gather.first(0, 1)
    turn(0, whole // 2, whole)
    if remote:
        gather.third(3, 4, 2)
    turn(1, 0, whole // 2)
    if remote:
        gather.second(0, 1)
        gather.fourth(3, 4, 2)
    turn(1, whole // 2, whole)
    freqs = jnp.exp(
        lax.broadcasted_iota(jnp.int32, (1, half), 1).astype(F32) * F32(-math.log(10000.0)) / half
    )
    for s in range(samples):
        r.angle[s : s + 1, :] = r.levels[s].astype(F32) * freqs
    r.embed[:, 0:half] = jnp.sin(r.angle[...]).astype(BF16)
    r.embed[:, half:width] = jnp.cos(r.angle[...]).astype(BF16)
    if remote:
        arrive(6, 7)
        update.old_moment()
        gather.third(0, 1)
        gather.last(3, 4, 2)
        for m in range(5):
            gather.unpack(SQ_AT[m], 1, r.sq_all, m)
        gather.unpack_gains()
    else:
        arrive(0, 1, 2)

    sq, mlp = r.sq_all, r.mlp_all
    wkh, wvh = r.wkh, r.wvh
    lane = lax.broadcasted_iota(jnp.int32, (width, width), 1)
    for h in range(HEADS):
        inside = lane // head_dim == h
        block = pl.ds(h * width, width)
        wkh[block, :] = jnp.where(inside, sq[2].astype(F32), 0.0).astype(BF16)
        wvh[block, :] = jnp.where(inside, sq[3].astype(F32), 0.0).astype(BF16)
    g1, g2 = r.gain_all[0:1, :], r.gain_all[1:2, :]

    obs_v[keys] = dot(r.embed[...], sq[0]).astype(BF16)
    obs_v[keys + 1 :] = jnp.zeros((KEYS_PAD - keys - 1, samples, width), BF16)
    for part in range(samples // batch):
        turn(part, whole, chunks)

    sides, weights = r.sides_v, r.pds_v

    def make_queries(i, _):
        rows = pl.ds(pl.multiple_of(i * ROWS, ROWS), ROWS)
        first = (r.xhat[rows, :] * g1).astype(BF16)
        r.first[rows, :] = first
        q = dot(first, sq[1]).astype(BF16)
        r.query[rows, :] = q
        here = pl.ds(i * per, per)
        for h in range(HEADS):
            wk = wkh[pl.ds(h * width, width), :]
            value = (dot(q, wk, NT) * 0.125).astype(BF16).reshape(per, ACT, width)
            sides[here, pl.ds((HEADS + h) * ACT, ACT), :] = value
        return 0

    lax.fori_loop(0, tokens // ROWS, make_queries, 0)

    key = lax.broadcasted_iota(jnp.int32, (HEADS * ACT, KEYS_PAD), 1)
    low_rows, high_rows = pl.ds(0, HEADS * ACT), pl.ds(HEADS * ACT, HEADS * ACT)

    def attend(g, _):
        ids = [g * GROUP + k for k in range(GROUP)]
        scores = [dot(sides[s, high_rows, :], mem[s], NT) for s in ids]
        lows = []
        for s, score in zip(ids, scores):
            count = OBS_FEW + (OBS_FULL - OBS_FEW) * r.flags[s]
            score = jnp.where((key < count) | (key == OBS_FULL), score, -1000000000.0)
            expo = jnp.exp(score - jnp.max(score, -1, keepdims=True))
            probs = expo / jnp.sum(expo, -1, keepdims=True)
            r.probs[s] = probs
            low = probs.astype(BF16)
            weights[s, low_rows, :] = low
            lows.append(low)
        for s, low in zip(ids, lows):
            u = dot(low, mem[s]).astype(BF16)
            rows = pl.ds(pl.multiple_of(s * ACT, ACT), ACT)
            for h in range(HEADS):
                r.u[rows, pl.ds(h * width, width)] = u[h * ACT : (h + 1) * ACT, :]
        return 0

    lax.fori_loop(0, groups // 2, attend, 0)
    if remote:
        gather.fourth(0, 1)
    lax.fori_loop(groups // 2, groups, attend, 0)
    if remote:
        gather.last(0, 1)
        for m in range(2):
            gather.unpack(m * MLP_ROWS, 4, mlp, m)

    gain_acc = r.gain_acc
    gain_acc[...] = jnp.zeros_like(gain_acc)
    arrive(5)

    def feed(i, _):
        rows = pl.ds(pl.multiple_of(i * ROWS, ROWS), ROWS)
        mixed = dot(r.u[rows, :], wvh[...]).astype(BF16)
        r.mixed[rows, :] = mixed
        resid = r.acts_v[rows, :] + dot(mixed, sq[4])
        hat, scale = normalize(resid)
        second = (hat * g2).astype(BF16)
        r.second[rows, :] = second
        cot = r.cot_v[rows, :]
        out_low = cot.astype(BF16)
        r.out_low[rows, :] = out_low
        for c in range(wide // 256):
            columns = pl.ds(c * 256, 256)
            v = dot(second, mlp[0, :, columns])
            square = v * v
            t = jnp.tanh(0.7978845608 * (v + 0.044715 * square * v))
            r.active[rows, columns] = (0.5 * v * (1.0 + t)).astype(BF16)
            slope = 0.5 * (1.0 + t) + 0.5 * v * (1.0 - t * t) * (0.7978845608 * (1.0 + 0.134145 * square))
            r.dhidden[rows, columns] = (slope * dot(out_low, mlp[1, :, columns])).astype(BF16)
        r.out_v[rows, :] = resid + dot(r.active[rows, :], mlp[1], NT)
        grad_second = dot(r.dhidden[rows, :], mlp[0], NT)
        gain_acc[1:2, :] += jnp.sum(grad_second * hat, 0, keepdims=True)
        dres = cot + norm_back(grad_second * g2, hat, scale)
        r.dres[rows, :] = dres
        low = dres.astype(BF16)
        r.dres_low[rows, :] = low
        gm = dot(low, sq[4], NT).astype(BF16)
        r.dmixed[rows, :] = gm
        here = pl.ds(i * per, per)
        for h in range(HEADS):
            wv = wvh[pl.ds(h * width, width), :]
            sides[here, pl.ds(h * ACT, ACT), :] = dot(gm, wv, NT).astype(BF16).reshape(per, ACT, width)
        return 0

    lax.fori_loop(0, tokens // ROWS, feed, 0)
    keep_out = pltpu.make_async_copy(r.out_v, r.output, out_sems.at[0])
    keep_out.start()
    keep_sides = pltpu.make_async_copy(sides, r.sides, out_sems.at[1])
    keep_sides.start()

    grads = r.grads

    def put(base, tiles, value):
        for j in range(tiles):
            part = value[:, j * LANES : (j + 1) * LANES].reshape(GRID + (TILE, LANES))
            grads[:, :, :, :, pl.ds(base + j * TILE, TILE), :] = part

    def by_head(left, right):
        turned = left.T
        parts = [
            dot(turned[h * head_dim : (h + 1) * head_dim, :], right[:, pl.ds(h * width, width)])
            for h in range(HEADS)
        ]
        return jnp.concatenate(parts, axis=0).T

    put(0, 8, dot(r.second[...], r.dhidden[...], TN))
    if remote:
        update.start(0)
    put(MLP_ROWS, 8, dot(r.out_low[...], r.active[...], TN))
    if remote:
        update.start(1)
    put(SQ_AT[4], 2, dot(r.mixed[...], r.dres_low[...], TN))
    put(SQ_AT[3], 2, by_head(r.dmixed[...], r.u))
    if remote:
        update.start(2)

    def attend_back(g, _):
        ids = [g * GROUP + k for k in range(GROUP)]
        rises = [dot(sides[s, low_rows, :], mem[s], NT) for s in ids]
        for s, rise in zip(ids, rises):
            probs = r.probs[s]
            both = probs * rise
            weights[s, high_rows, :] = (both - probs * jnp.sum(both, -1, keepdims=True)).astype(BF16)
        for s in ids:
            dq = (dot(weights[s, high_rows, :], mem[s]) * 0.125).astype(BF16)
            rows = pl.ds(pl.multiple_of(s * ACT, ACT), ACT)
            for h in range(HEADS):
                r.dq_wide[rows, pl.ds(h * width, width)] = dq[h * ACT : (h + 1) * ACT, :]
            end = dot(weights[s, :, LANES:KEYS_PAD], sides[s], TN)
            r.stamps[s] = end[64:72, :]
        return 0

    quarter = groups // 4
    lax.fori_loop(0, quarter, attend_back, 0)
    if remote:
        update.one(0, 1)
    lax.fori_loop(quarter, 2 * quarter, attend_back, 0)
    if remote:
        update.two(0, 1)
        update.one(2)
    lax.fori_loop(2 * quarter, 3 * quarter, attend_back, 0)
    if remote:
        update.three(0, 1)
        update.two(2)
    lax.fori_loop(3 * quarter, groups, attend_back, 0)
    keep_pds = pltpu.make_async_copy(weights, r.pds, out_sems.at[2])
    keep_pds.start()

    def queries_back(i, _):
        rows = pl.ds(pl.multiple_of(i * ROWS, ROWS), ROWS)
        r.dquery[rows, :] = dot(r.dq_wide[rows, :], wkh[...]).astype(BF16)
        return 0

    lax.fori_loop(0, tokens // ROWS, queries_back, 0)
    put(SQ_AT[1], 2, dot(r.first[...], r.dquery[...], TN))
    stamp_low = r.stamps[:, 4:5, :].reshape(samples, width).astype(BF16)
    put(SQ_AT[0], 2, dot(r.embed[...], stamp_low, TN))
    if remote:
        update.start(3)

    def acts_back(i, _):
        rows = pl.ds(pl.multiple_of(i * ROWS, ROWS), ROWS)
        grad_first = dot(r.dquery[rows, :], sq[1], NT)
        hat = r.xhat[rows, :]
        gain_acc[0:1, :] += jnp.sum(grad_first * hat, 0, keepdims=True)
        r.ag_v[rows, :] = r.dres[rows, :] + norm_back(grad_first * g1, hat, r.rstd[rows, :])
        return 0

    lax.fori_loop(0, tokens // ROWS, acts_back, 0)
    put(SQ_AT[2], 2, by_head(r.query[...], r.dq_wide))
    for norm in range(2):
        for j in range(2):
            row = gain_acc[norm : norm + 1, j * LANES : (j + 1) * LANES]
            at = GAIN_BASE + norm * 2 + j
            value = jnp.broadcast_to(row.reshape(1, 1, 1, 1, 1, LANES), GRID + (1, LANES))
            grads[:, :, :, :, at : at + 1, :] = value
    rest = WIRE - GAIN_BASE - 4
    grads[:, :, :, :, GAIN_BASE + 4 : WIRE, :] = jnp.zeros(GRID + (rest, LANES), F32)
    keep_ag = pltpu.make_async_copy(r.ag_v, r.ag, out_sems.at[3])
    keep_ag.start()
    if remote:
        update.start(4)
        update.three(2)
        update.one(3, 4)
        update.four(0, 1)
        update.two(3, 4)
        update.four(2)
        update.three(3, 4)
        update.four(3, 4)
        update.orthogonalize()
        update.give_all()
        out = r.out
        out[1, :, :] = r.moment[...]
        out[2, pl.ds(GAIN_BASE, 16), :] = jnp.zeros((16, LANES), F32)
        update.take_all()
        gather.drain()
        update.drain()
    for copy in (keep_out, keep_sides, keep_pds, keep_ag):
        copy.wait()


def block_and_back(remote, acts, obs, flags, levels, cot, sqw, mlpw, gain, sqm=None, mlpm=None):
    tokens, width = acts.shape
    keys, samples = obs.shape[0], obs.shape[1]
    rows = HEADS * ACT
    wide = mlpw.shape[2]
    any_space = pl.BlockSpec(memory_space=pl.ANY)
    in_vmem = pl.BlockSpec(memory_space=VMEM)
    scalars = pl.BlockSpec(memory_space=pltpu.SMEM)
    sem = pltpu.SemaphoreType.DMA
    ins = dict(flags=flags, levels=levels, acts=acts, obs=obs, cot=cot, sqw=sqw, mlpw=mlpw, gain=gain)
    outs = dict(
        output=jax.ShapeDtypeStruct(acts.shape, F32),
        ag=jax.ShapeDtypeStruct(acts.shape, F32),
        pds=jax.ShapeDtypeStruct((samples, 2 * rows, KEYS_PAD), BF16),
        sides=jax.ShapeDtypeStruct((samples, 2 * rows, width), BF16),
    )
    grads = GRID + (WIRE, LANES)
    scratch = dict(
        obs_v=VMEM((KEYS_PAD, samples, width), BF16),
        acts_v=VMEM(acts.shape, F32),
        cot_v=VMEM(acts.shape, F32),
        mem=VMEM((samples, KEYS_PAD, width), BF16),
        sq_all=VMEM((5, width, width), BF16),
        mlp_all=VMEM((2, width, wide), BF16),
        gain_all=VMEM((2, width), F32),
        wkh=VMEM((HEADS * width, width), BF16),
        wvh=VMEM((HEADS * width, width), BF16),
        first=VMEM((tokens, width), BF16),
        query=VMEM((tokens, width), BF16),
        xhat=VMEM((tokens, width), F32),
        rstd=VMEM((tokens, 1), F32),
        probs=VMEM((samples, rows, KEYS_PAD), F32),
        pds_v=VMEM((samples, 2 * rows, KEYS_PAD), BF16),
        sides_v=VMEM((samples, 2 * rows, width), BF16),
        u=VMEM((tokens, HEADS * width), BF16),
        dq_wide=VMEM((tokens, HEADS * width), BF16),
        mixed=VMEM((tokens, width), BF16),
        second=VMEM((tokens, width), BF16),
        active=VMEM((tokens, wide), BF16),
        dhidden=VMEM((tokens, wide), BF16),
        out_low=VMEM((tokens, width), BF16),
        dres_low=VMEM((tokens, width), BF16),
        dres=VMEM((tokens, width), F32),
        dmixed=VMEM((tokens, width), BF16),
        dquery=VMEM((tokens, width), BF16),
        out_v=VMEM((tokens, width), F32),
        ag_v=VMEM((tokens, width), F32),
        angle=VMEM((samples, width // 2), F32),
        embed=VMEM((samples, width), BF16),
        stamps=VMEM((samples, 8, width), F32),
        gain_acc=VMEM((8, width), F32),
        in_sems=sem((8,)),
        out_sems=sem((4,)),
    )
    extra = {}
    if remote:
        ins.update(sqm=sqm, mlpm=mlpm)
        outs.update(out=jax.ShapeDtypeStruct((3, WIRE, LANES), F32))
        chunks = len(CHUNKS)
        scratch.update(
            grads=VMEM(grads, F32),
            sqw_v=VMEM(sqw.shape, F32),
            mlpw_v=VMEM(mlpw.shape, F32),
            gain_v=VMEM(gain.shape, F32),
            sqm_v=VMEM(sqm.shape, F32),
            mlpm_v=VMEM(mlpm.shape, F32),
            wire=VMEM(grads, BF16),
            edge=VMEM((16, LANES), F32),
            gsend=sem((chunks, 6)),
            grecv=sem((chunks, 6)),
            got_core=VMEM((4, 2, 2, WIRE, LANES), F32),
            sum1=VMEM((4, 2, 2, WIRE, LANES), F32),
            send1=VMEM((4, 2, WIRE, LANES), BF16),
            got1=VMEM((4, 2, WIRE, LANES), BF16),
            sum2=VMEM((4, 2, WIRE, LANES), F32),
            send2=VMEM((4, WIRE, LANES), BF16),
            got2=VMEM((4, WIRE, LANES), BF16),
            sum3=VMEM((4, WIRE, LANES), F32),
            send3=VMEM((3, WIRE, LANES), BF16),
            got3=VMEM((3, WIRE, LANES), BF16),
            moment=VMEM((WIRE, LANES), F32),
            slabs_sq=VMEM((32, SQ_ROWS, LANES), F32),
            slabs_mlp=VMEM((32, MLP_ROWS, LANES), F32),
            result_sq=VMEM((32, SQ_ROWS, LANES), F32),
            result_mlp=VMEM((32, MLP_ROWS, LANES), F32),
            cur=VMEM((width, wide), F32),
            gram_s=VMEM((width, width), F32),
            prod_s=VMEM((width, width), F32),
            send=sem((chunks, 6)),
            recv=sem((chunks, 6)),
            own_send=sem((7,)),
            own_recv=sem((1,)),
            back_send=sem((32,)),
            back_recv=sem((7,)),
        )
        extra = dict(collective_id=0, has_side_effects=True)
    else:
        outs.update(grads=jax.ShapeDtypeStruct(grads, F32))
    names = tuple(ins) + tuple(outs) + tuple(scratch)
    results = pl.pallas_call(
        functools.partial(block_kernel, names, remote),
        out_shape=tuple(outs.values()),
        in_specs=[scalars] * 2 + [any_space] * (len(ins) - 2),
        out_specs=[any_space] * 4 + [in_vmem],
        scratch_shapes=list(scratch.values()),
        compiler_params=pltpu.CompilerParams(vmem_limit_bytes=56 << 20, **extra),
        name="block_and_back",
    )(*ins.values())
    return Refs(zip(outs, results))


def finish_kernel(names, rate, *args):
    r = Refs(zip(names, args))
    samples, rows, width = r.sides.shape
    keys = r.og.shape[0]
    groups = samples // TILE
    sems = r.sems

    def group_moves(g):
        block = pl.ds(g * TILE, TILE)
        return (
            pltpu.make_async_copy(r.pds.at[block], r.pds_v.at[block], sems.at[2 * g]),
            pltpu.make_async_copy(r.sides.at[block], r.sides_v.at[block], sems.at[2 * g + 1]),
        )

    for g in range(groups):
        for copy in group_moves(g):
            copy.start()
    more = 2 * groups + 4
    small, passes = [], []
    if hasattr(r, "wire"):
        pairs = [(r.output, r.output_v), (r.ag, r.ag_v), (r.wire, r.wire_v), (r.sqw, r.sqw_v)]
        pairs += [(r.mlpw, r.mlpw_v), (r.gain, r.gain_v), (r.gainm, r.gainm_v)]
        for source, target in pairs:
            small.append(pltpu.make_async_copy(source, target, sems.at[more]))
            small[-1].start()
            more += 1
        for source, target in ((r.output_v, r.output_f), (r.ag_v, r.ag_f)):
            passes.append(pltpu.make_async_copy(source, target, sems.at[more]))
            more += 1

    turned, og_v = r.turned, r.og_v

    def observed(part, g):
        low, high = ((0, LANES), (LANES, KEYS_PAD))[part]
        for k in range(TILE):
            s = g * TILE + k
            turned[k, low:high, :] = dot(r.pds_v[s, :, low:high], r.sides_v[s], TN)
        here = pl.ds(pl.multiple_of(g * TILE, TILE), TILE)

        def one(j, _):
            at = pl.ds(pl.multiple_of(j * TILE, TILE), TILE)
            for side in range(2):
                columns = pl.ds(side * LANES, LANES)
                og_v[at, here, columns] = jnp.transpose(turned[:, at, columns], (1, 0, 2))
            return 0

        lax.fori_loop(low // TILE, min(high, og_v.shape[0]) // TILE, one, 0)

    def leave(part):
        there = (pl.ds(0, LANES), pl.ds(LANES, keys - LANES))[part]
        return pltpu.make_async_copy(og_v.at[there], r.og.at[there], sems.at[2 * groups + part])

    def first_part(g, _):
        for copy in group_moves(g):
            copy.wait()
        observed(0, g)
        return 0

    def second_part(g, _):
        observed(1, g)
        return 0

    lax.fori_loop(0, groups, first_part, 0)
    leave(0).start()
    for copy in small[:2]:
        copy.wait()
    for copy in passes:
        copy.start()
    lax.fori_loop(0, groups, second_part, 0)
    leave(1).start()
    if hasattr(r, "wire"):
        for copy in small[2:]:
            copy.wait()
        finish_weights(r, rate)
    for part in range(2):
        leave(part).wait()
    for copy in passes:
        copy.wait()


def finish_weights(r, rate):
    wire = r.wire_v
    me = lax.axis_index("dp")
    for m in range(5):
        for j in range(2):
            rows, columns = pl.ds(SQ_AT[m] + j * TILE, TILE), pl.ds(j * LANES, LANES)
            r.sqg[m, :, columns] = wire[0, rows, :]
            r.sqm[m, :, columns] = wire[1, rows, :]
            r.sqn[m, :, columns] = r.sqw_v[m, :, columns] - SQ_RATES[m] * wire[2, rows, :]
    r.sqc[...] = r.sqn[...].astype(BF16)
    for m in range(2):
        for j in range(8):
            rows, columns = pl.ds(m * MLP_ROWS + j * TILE, TILE), pl.ds(j * LANES, LANES)
            r.mlpg[m, :, columns] = wire[0, rows, :]
            r.mlpm[m, :, columns] = wire[1, rows, :]
            r.mlpn[m, :, columns] = r.mlpw_v[m, :, columns] - MLP_RATES[m] * wire[2, rows, :]
    r.mlpc[...] = r.mlpn[...].astype(BF16)
    tile = wire[0, pl.ds(GAIN_BASE, TILE), :]
    turned = pltpu.roll(tile, (LANES - (me % 16) * TILE) % LANES, 1)
    at = me // 16
    for norm in range(2):
        pair = turned[2 * norm : 2 * norm + 2, 0:TILE]
        row = jnp.where(at == 0, pair[0:1, :], pair[1:2, :])
        new = 0.5 * r.gainm_v[norm : norm + 1, :] + row
        r.gg[norm : norm + 1, :] = row
        r.gm[norm : norm + 1, :] = new
        r.gn[norm : norm + 1, :] = r.gain_v[norm : norm + 1, :] - rate * new


def finish(rate, keys, made, sqw=None, mlpw=None, gain=None, gainm=None):
    any_space = pl.BlockSpec(memory_space=pl.ANY)
    in_vmem = pl.BlockSpec(memory_space=VMEM)
    pds, sides = made.pds, made.sides
    samples, rows, width = sides.shape
    ins = dict(pds=pds, sides=sides)
    outs = dict(og=jax.ShapeDtypeStruct((keys, samples, width), F32))
    far = 1
    if hasattr(made, "out"):
        ins.update(output=made.output, ag=made.ag, wire=made.out, sqw=sqw, mlpw=mlpw, gain=gain, gainm=gainm)
        like = jax.ShapeDtypeStruct
        far = 3
        outs.update(
            output_f=like(made.output.shape, F32),
            ag_f=like(made.ag.shape, F32),
            sqg=like(sqw.shape, F32),
            sqm=like(sqw.shape, F32),
            sqn=like(sqw.shape, F32),
            sqc=like(sqw.shape, BF16),
            mlpg=like(mlpw.shape, F32),
            mlpm=like(mlpw.shape, F32),
            mlpn=like(mlpw.shape, F32),
            mlpc=like(mlpw.shape, BF16),
            gg=like(gain.shape, F32),
            gm=like(gain.shape, F32),
            gn=like(gain.shape, F32),
        )
    scratch = dict(
        pds_v=VMEM(pds.shape, BF16),
        sides_v=VMEM(sides.shape, BF16),
        turned=VMEM((TILE, KEYS_PAD, width), F32),
        og_v=VMEM((-(-keys // TILE) * TILE, samples, width), F32),
        sems=pltpu.SemaphoreType.DMA((2 * (samples // TILE) + 13,)),
    )
    if hasattr(made, "out"):
        scratch.update(
            output_v=VMEM(made.output.shape, F32),
            ag_v=VMEM(made.ag.shape, F32),
            wire_v=VMEM(made.out.shape, F32),
            sqw_v=VMEM(sqw.shape, F32),
            mlpw_v=VMEM(mlpw.shape, F32),
            gain_v=VMEM(gain.shape, F32),
            gainm_v=VMEM(gainm.shape, F32),
        )
    names = tuple(ins) + tuple(outs) + tuple(scratch)
    results = pl.pallas_call(
        functools.partial(finish_kernel, names, rate),
        out_shape=tuple(outs.values()),
        in_specs=[any_space] * len(ins),
        out_specs=[any_space] * far + [in_vmem] * (len(outs) - far),
        scratch_shapes=list(scratch.values()),
        compiler_params=pltpu.CompilerParams(vmem_limit_bytes=60 << 20),
        name="finish",
    )(*ins.values())
    return Refs(zip(outs, results))


HIGH_PRECISION = lax.Precision.HIGHEST


def plain_orthogonalize(matrix):
    current = matrix / (jnp.sqrt(jnp.sum(matrix * matrix)) + 1e-07)
    for turn in range(5):
        gram = jnp.dot(current, current.T, precision=HIGH_PRECISION)
        poly = COEF_B * gram + COEF_C * jnp.dot(gram, gram, precision=HIGH_PRECISION)
        current = COEF_A * current + jnp.dot(poly, current, precision=HIGH_PRECISION)
    return current


def pick_owned(stack, owners, device):
    chosen = jnp.zeros_like(stack[0])
    for index in range(len(owners)):
        chosen = jnp.where(device == owners[index], stack[index], chosen)
    return chosen


def is_owner(owners, device):
    flag = device < 0
    for owner in owners:
        flag = jnp.logical_or(flag, device == owner)
    return flag


def from_wire(grads):
    def matrix(base, tiles):
        part = grads[:, base : base + tiles * TILE, :].reshape(-1, tiles, TILE, LANES)
        return part.transpose(0, 2, 1, 3).reshape(-1, tiles * LANES)

    square = jnp.stack([matrix(SQ_AT[m], 2) for m in range(5)])
    mlp = jnp.stack([matrix(m * MLP_ROWS, 8) for m in range(2)])
    return square, mlp, grads[0, GAIN_BASE : GAIN_BASE + 4, :].reshape(2, 2 * LANES)


def update_by_collectives(
    grads, square_weights, mlp_weights, gains, square_moment, mlp_moment, gain_moment, rate
):
    square_local, mlp_local, gain_local = from_wire(grads)
    square_grad, mlp_grad, gain_grad = (
        lax.psum_scatter(square_local, "dp", scatter_dimension=1, tiled=True),
        lax.psum_scatter(mlp_local, "dp", scatter_dimension=1, tiled=True),
        lax.psum_scatter(gain_local, "dp", scatter_dimension=1, tiled=True),
    )
    square_moment_new = 0.5 * square_moment + square_grad
    mlp_moment_new = 0.5 * mlp_moment + mlp_grad
    gain_moment_new = 0.5 * gain_moment + gain_grad
    device = lax.axis_index("dp")
    count = lax.axis_size("dp")
    square_owners = [index * count // 7 for index in range(5)]
    mlp_owners = [(index + 5) * count // 7 for index in range(2)]
    square_full, mlp_full = (
        lax.all_gather(square_moment_new, "dp", axis=1, tiled=True),
        lax.all_gather(mlp_moment_new, "dp", axis=1, tiled=True),
    )
    mine_square = pick_owned(square_full, square_owners, device)
    mine_mlp = pick_owned(mlp_full, mlp_owners, device)
    made_square = lax.cond(
        is_owner(square_owners, device), plain_orthogonalize, jnp.zeros_like, mine_square
    )
    made_mlp = lax.cond(is_owner(mlp_owners, device), plain_orthogonalize, jnp.zeros_like, mine_mlp)
    stack_square = jnp.stack(
        [jnp.where(device == owner, made_square, 0.0) for owner in square_owners]
    )
    stack_mlp = jnp.stack([jnp.where(device == owner, made_mlp, 0.0) for owner in mlp_owners])
    square_ortho, mlp_ortho = (
        lax.psum_scatter(stack_square, "dp", scatter_dimension=1, tiled=True),
        lax.psum_scatter(stack_mlp, "dp", scatter_dimension=1, tiled=True),
    )
    square_new = square_weights - jnp.array(SQ_RATES, F32)[:, None, None] * square_ortho
    mlp_new = mlp_weights - jnp.array(MLP_RATES, F32)[:, None, None] * mlp_ortho
    gains_new = gains - rate * gain_moment_new
    return (
        square_grad,
        square_moment_new,
        square_new,
        square_new.astype(BF16),
        mlp_grad,
        mlp_moment_new,
        mlp_new,
        mlp_new.astype(BF16),
        gain_grad,
        gain_moment_new,
        gains_new,
    )


def per_device(
    actions,
    observed,
    camera_flags,
    noise_levels,
    cotangent,
    square_weights,
    mlp_weights,
    gains,
    square_moment,
    mlp_moment,
    gain_moment,
):
    count = lax.axis_size("dp")
    rate = 0.1 / math.sqrt(actions.shape[0] * count)
    by_key = observed.transpose(1, 0, 2)
    keys, samples, width = by_key.shape
    ins = (actions, by_key, camera_flags, noise_levels, cotangent)
    if count == math.prod(GRID):
        made = block_and_back(True, *ins, square_weights, mlp_weights, gains, square_moment, mlp_moment)
        done = finish(rate, keys, made, square_weights, mlp_weights, gains, gain_moment)
        output, actions_grad = done.output_f, done.ag_f
        d = done
        rest = (d.sqg, d.sqm, d.sqn, d.sqc, d.mlpg, d.mlpm, d.mlpn, d.mlpc, d.gg, d.gm, d.gn)
    else:
        square_all, mlp_all = (
            lax.all_gather(square_weights.astype(BF16), "dp", axis=1, tiled=True),
            lax.all_gather(mlp_weights.astype(BF16), "dp", axis=1, tiled=True),
        )
        gain_all = lax.all_gather(gains, "dp", axis=1, tiled=True)
        made = block_and_back(False, *ins, square_all, mlp_all, gain_all)
        done = finish(rate, keys, made)
        output, actions_grad = made.output, made.ag
        grads = made.grads.reshape(-1, WIRE, LANES)
        rest = update_by_collectives(
            grads, square_weights, mlp_weights, gains, square_moment, mlp_moment, gain_moment, rate
        )
    observed_grad = done.og.transpose(1, 0, 2)
    return (output, actions_grad, observed_grad) + tuple(rest)


def solution(mesh):
    rows, cube, flat = P("dp", None), P("dp", None, None), P("dp")
    stacked, pair = P(None, "dp", None), P(None, "dp")
    return jax.shard_map(
        per_device,
        mesh=mesh,
        in_specs=(rows, cube, flat, flat, rows, stacked, stacked, pair, stacked, stacked, pair),
        out_specs=(rows, rows, cube) + (stacked,) * 8 + (pair,) * 3,
        check_vma=False,
    )
```

```python
import functools
import math

import jax
import jax.numpy as jnp
from jax import lax
from jax.experimental import pallas as pl
from jax.experimental.pallas import tpu as pltpu
from jax.sharding import PartitionSpec as P

HEADS = 4
ACT = 16
OBS_FULL = 196
OBS_FEW = 49
COEF_A = 3.4445
COEF_B = -4.775
COEF_C = 2.0315
F32 = jnp.float32
BF16 = jnp.bfloat16
MESH = pl.DeviceIdType.MESH
VMEM = pltpu.VMEM
NN = (((1,), (0,)), ((), ()))
NT = (((1,), (1,)), ((), ()))
TN = (((0,), (0,)), ((), ()))

LANES = 128
TILE = 8
MLP_ROWS = 64
SQ_ROWS = 16
SQ_AT = (160, 176, 192, 128, 144)
GAIN_BASE = 208
WIRE = 224
CHUNKS = ((0, 64), (64, 64), (128, 32), (160, 32), (192, 32))
X_FIRST = (True, False, True, True, False)
MLP_RATES = (1.0, 0.5)
SQ_RATES = (0.5, 0.5, 0.5, 0.5, 4.0)
GRID = (4, 2, 2, 2)
OWNERS = (8, 22, 14, 16, 11, 21, 13)
KEYS_PAD = 208
GROUP = 4
ROWS = 256


class Refs:
    def __init__(self, pairs):
        self.__dict__.update(pairs)


def dot(left, right, dims=NN):
    return lax.dot_general(left, right, dims, preferred_element_type=F32)


def place():
    me = lax.axis_index("dp")
    return me, me // 8, (me // 4) % 2, (me // 2) % 2, me % 2


def device_at(z, y, x, c):
    return ((z * 2 + y) * 2 + x) * 2 + c


def link(src, dst, send, recv, device):
    return pltpu.make_async_remote_copy(
        src_ref=src,
        dst_ref=dst,
        send_sem=send,
        recv_sem=recv,
        device_id=(device,),
        device_id_type=MESH,
    )


def greet(device):
    pl.semaphore_signal(
        pltpu.get_barrier_semaphore(), inc=1, device_id=(device,), device_id_type=MESH
    )


def halves(value):
    high = value.astype(BF16)
    return high, (value - high.astype(F32)).astype(BF16)


def dot3(left, right, dims=NN):
    (lh, ll), (rh, rl) = left, right
    return dot(lh, rh, dims) + (dot(lh, rl, dims) + dot(ll, rh, dims))


def normalize(values):
    centred = values - jnp.mean(values, -1, keepdims=True)
    scale = lax.rsqrt(jnp.mean(centred * centred, -1, keepdims=True) + 1e-05)
    return centred * scale, scale


def norm_back(grad, hat, scale):
    mean_one = jnp.mean(grad, -1, keepdims=True)
    mean_two = jnp.mean(grad * hat, -1, keepdims=True)
    return scale * (grad - mean_one - hat * mean_two)


class Gather:
    def __init__(self, r):
        self.r = r
        self.me, self.z, self.y, self.x, self.c = place()

    def hop(self, k, step, part, device):
        return link(part, part, self.r.gsend.at[k, step], self.r.grecv.at[k, step], device)

    def along_z(self, k, step):
        part = self.r.wire.at[self.z, self.y, self.x, self.c, pl.ds(*CHUNKS[k])]
        return self.hop(k, step, part, device_at((self.z + step + 1) % 4, self.y, self.x, self.c))

    def from_z(self, k, step):
        there = (self.z + 3 - step) % 4
        part = self.r.wire.at[there, self.y, self.x, self.c, pl.ds(*CHUNKS[k])]
        return self.hop(k, step, part, device_at(there, self.y, self.x, self.c))

    def plane(self, k, second, mine):
        z, y, x, c = self.z, self.y, self.x, self.c
        rows, wire = pl.ds(*CHUNKS[k]), self.r.wire
        py, px = (y, x) if mine else (1 - y, 1 - x)
        along_x = X_FIRST[k] == second
        if along_x:
            part = wire.at[:, y, px, c, rows] if second else wire.at[:, :, px, c, rows]
            return self.hop(k, 3 if second else 4, part, device_at(z, y, 1 - x, c))
        part = wire.at[:, py, x, c, rows] if second else wire.at[:, py, :, c, rows]
        return self.hop(k, 3 if second else 4, part, device_at(z, 1 - y, x, c))

    def core(self, k, mine):
        part = self.r.wire.at[:, :, :, self.c if mine else 1 - self.c, pl.ds(*CHUNKS[k])]
        return self.hop(k, 5, part, device_at(self.z, self.y, self.x, 1 - self.c))

    def first(self, *chunks):
        for k in chunks:
            for step in range(3):
                self.along_z(k, step).start()

    def second(self, *chunks):
        for k in chunks:
            for step in range(3):
                self.from_z(k, step).wait_recv()
            self.plane(k, True, True).start()

    def third(self, *chunks):
        for k in chunks:
            self.plane(k, True, False).wait_recv()
            self.plane(k, False, True).start()

    def fourth(self, *chunks):
        for k in chunks:
            self.plane(k, False, False).wait_recv()
            self.core(k, True).start()

    def last(self, *chunks):
        for k in chunks:
            self.core(k, False).wait_recv()

    def drain(self):
        for k in range(len(CHUNKS)):
            for step in range(3):
                self.along_z(k, step).wait_send()
            self.plane(k, True, True).wait_send()
            self.plane(k, False, True).wait_send()
            self.core(k, True).wait_send()

    def fill(self):
        r = self.r
        spot = (self.z, self.y, self.x, self.c)

        def tiles(source, m, base, number):
            for j in range(number):
                pair = [source[m, :, pl.ds((2 * j + k) * LANES, LANES)] for k in range(2)]
                r.wire[spot + (pl.ds(base + j * 16, 16),)] = jnp.concatenate(pair, axis=0).astype(BF16)

        for m in range(5):
            tiles(r.sqw_v, m, SQ_AT[m], 1)
        for m in range(2):
            tiles(r.mlpw_v, m, m * MLP_ROWS, 4)
        gains, edge = r.gain_v[...], r.edge
        high = gains.astype(BF16).astype(F32)
        middle = (gains - high).astype(BF16).astype(F32)
        edge[...] = jnp.zeros_like(edge)
        edge[0:2, 0:TILE] = high
        edge[2:4, 0:TILE] = middle
        edge[4:6, 0:TILE] = (gains - high - middle).astype(BF16).astype(F32)
        r.wire[spot + (pl.ds(GAIN_BASE, 16),)] = edge[...].astype(BF16)

    def unpack(self, base, number, out, m):
        for j in range(number):
            block = self.r.wire[:, :, :, :, pl.ds(base + j * 16, 16), :].reshape(32, 16, LANES).astype(F32)
            for half in range(2):
                columns = pl.ds((2 * j + half) * LANES, LANES)
                out[m, :, columns] = block[:, half * 8 : half * 8 + 8, :].reshape(256, LANES).astype(BF16)

    def unpack_gains(self):
        edge, wire = self.r.edge, self.r.wire
        for half in range(2):
            total = jnp.zeros((16, LANES), F32)
            for at in range(16):
                d = half * 16 + at
                tile = wire[d // 8, (d // 4) % 2, (d // 2) % 2, d % 2, pl.ds(GAIN_BASE, 16), :].astype(F32)
                total = total + (tile if at == 0 else pltpu.roll(tile, at * TILE, 1))
            edge[...] = total
            self.r.gain_all[:, pl.ds(half * LANES, LANES)] = edge[0:2, :] + edge[2:4, :] + edge[4:6, :]


class Update:
    def __init__(self, r):
        self.r = r
        self.me, self.z, self.y, self.x, self.c = place()

    def hop(self, k, step, src, dst, device):
        return link(src, dst, self.r.send.at[k, step], self.r.recv.at[k, step], device)

    def core(self, k):
        rows = pl.ds(*CHUNKS[k])
        src, dst = self.r.grads.at[:, :, :, 1 - self.c, rows], self.r.got_core.at[:, :, :, rows]
        return self.hop(k, 0, src, dst, device_at(self.z, self.y, self.x, 1 - self.c))

    def plane(self, k, first):
        rows = pl.ds(*CHUNKS[k])
        to = (self.z, self.y, 1 - self.x, self.c) if X_FIRST[k] == first else (self.z, 1 - self.y, self.x, self.c)
        if first:
            src, dst = self.r.send1.at[:, :, rows], self.r.got1.at[:, :, rows]
        else:
            src, dst = self.r.send2.at[:, rows], self.r.got2.at[:, rows]
        return self.hop(k, 1 if first else 2, src, dst, device_at(*to))

    def along_z(self, k, step):
        rows = pl.ds(*CHUNKS[k])
        to = device_at((self.z + step + 1) % 4, self.y, self.x, self.c)
        return self.hop(k, 3 + step, self.r.send3.at[step, rows], self.r.got3.at[step, rows], to)

    def start(self, k):
        self.core(k).start()

    def one(self, *chunks):
        r = self.r
        for k in chunks:
            rows = pl.ds(*CHUNKS[k])
            self.core(k).wait_recv()
            sum1 = r.sum1
            sum1[:, :, :, rows, :] = r.grads[:, :, :, self.c, rows, :] + r.got_core[:, :, :, rows, :]
            other = sum1[:, :, 1 - self.x, rows, :] if X_FIRST[k] else sum1[:, 1 - self.y, :, rows, :]
            r.send1[:, :, rows, :] = other.astype(BF16)
            self.plane(k, True).start()

    def two(self, *chunks):
        r = self.r
        for k in chunks:
            rows = pl.ds(*CHUNKS[k])
            self.plane(k, True).wait_recv()
            sum1, sum2 = r.sum1, r.sum2
            mine = sum1[:, :, self.x, rows, :] if X_FIRST[k] else sum1[:, self.y, :, rows, :]
            sum2[:, :, rows, :] = mine + r.got1[:, :, rows, :].astype(F32)
            other = 1 - self.y if X_FIRST[k] else 1 - self.x
            r.send2[:, rows, :] = sum2[:, other, rows, :].astype(BF16)
            self.plane(k, False).start()

    def three(self, *chunks):
        r = self.r
        for k in chunks:
            rows = pl.ds(*CHUNKS[k])
            self.plane(k, False).wait_recv()
            mine = self.y if X_FIRST[k] else self.x
            r.sum3[:, rows, :] = r.sum2[:, mine, rows, :] + r.got2[:, rows, :].astype(F32)
            for step in range(3):
                r.send3[step, rows, :] = r.sum3[(self.z + step + 1) % 4, rows, :].astype(BF16)
                self.along_z(k, step).start()

    def slab(self, index):
        if index < 2:
            return pl.ds(index * MLP_ROWS, MLP_ROWS), self.r.slabs_mlp, self.r.result_mlp
        return pl.ds(SQ_AT[index - 2], SQ_ROWS), self.r.slabs_sq, self.r.result_sq

    def to_owner(self, index):
        rows, slabs, _ = self.slab(index)
        return link(
            self.r.moment.at[rows], slabs.at[self.me],
            self.r.own_send.at[index], self.r.own_recv.at[0], OWNERS[index],
        )

    def four(self, *chunks):
        r = self.r
        moment, out = r.moment, r.out
        for k in chunks:
            rows = pl.ds(*CHUNKS[k])
            total = r.sum3[self.z, rows, :]
            for step in range(3):
                self.along_z(k, step).wait_recv()
                total = total + r.got3[step, rows, :].astype(F32)
            out[0, rows, :] = total
            moment[rows, :] = 0.5 * moment[rows, :] + total
            for index in ((0,), (1,), (5, 6), (2, 3), (4,))[k]:
                rows_m, slabs, _ = self.slab(index)

                @pl.when(self.me != OWNERS[index])
                def _():
                    self.to_owner(index).start()

                @pl.when(self.me == OWNERS[index])
                def _():
                    pltpu.make_async_copy(moment.at[rows_m], slabs.at[self.me], r.own_recv.at[0]).start()

    def old_moment(self):
        r = self.r
        moment = r.moment
        for m in range(2):
            for j in range(8):
                moment[pl.ds(m * MLP_ROWS + j * TILE, TILE), :] = r.mlpm_v[m, :, pl.ds(j * LANES, LANES)]
        for m in range(5):
            for j in range(2):
                moment[pl.ds(SQ_AT[m] + j * TILE, TILE), :] = r.sqm_v[m, :, pl.ds(j * LANES, LANES)]
        moment[pl.ds(GAIN_BASE, 16), :] = jnp.zeros((16, LANES), F32)

    def orthogonalize(self):
        r = self.r
        cur, gram_s, prod_s = r.cur, r.gram_s, r.prod_s

        def load(slabs, tiles):
            total = jnp.zeros((1, 1), F32)
            for j in range(tiles):
                part = slabs[:, pl.ds(j * TILE, TILE), :].reshape(256, LANES)
                cur[:, pl.ds(j * LANES, LANES)] = part
                total = total + jnp.sum(jnp.sum(part * part, axis=0, keepdims=True), axis=1, keepdims=True)
            width = tiles * LANES
            cur[:, 0:width] = cur[:, 0:width] * (1.0 / (jnp.sqrt(total) + 1e-07))

        mine_mlp = jnp.logical_or(self.me == OWNERS[0], self.me == OWNERS[1])
        mine_sq = self.me < 0
        for device in OWNERS[2:]:
            mine_sq = jnp.logical_or(mine_sq, self.me == device)

        @pl.when(mine_mlp)
        def _():
            slabs, result = r.slabs_mlp, r.result_mlp
            pltpu.make_async_copy(slabs, slabs, r.own_recv.at[0]).wait()
            load(slabs, 8)
            x = halves(cur[...])
            gram_s[...] = dot3(x, x, NT)
            rows = lax.broadcasted_iota(jnp.int32, (256, 256), 0)
            one = (rows == lax.broadcasted_iota(jnp.int32, (256, 256), 1)).astype(F32)
            prod_s[...] = one

            def turn(k, _):
                gram = gram_s[...]
                g = halves(gram)
                p = halves(COEF_A * one + COEF_B * gram + COEF_C * dot3(g, g))
                prod_s[...] = dot3(p, halves(prod_s[...]))
                gram_s[...] = dot3(halves(dot3(p, g)), p)
                return 0

            lax.fori_loop(0, 5, turn, 0)
            prod = halves(prod_s[...])
            for j in range(8):
                part = dot3(prod, halves(cur[:, pl.ds(j * LANES, LANES)]))
                result[:, pl.ds(j * TILE, TILE), :] = part.reshape(32, TILE, LANES)

        @pl.when(mine_sq)
        def _():
            slabs, result = r.slabs_sq, r.result_sq
            pltpu.make_async_copy(slabs, slabs, r.own_recv.at[0]).wait()
            load(slabs, 2)

            def turn(k, _):
                now = cur[:, 0:256]
                x = halves(now)
                gram = dot3(x, x, NT)
                g = halves(gram)
                p = halves(COEF_B * gram + COEF_C * dot3(g, g))
                cur[:, 0:256] = COEF_A * now + dot3(p, x)
                return 0

            lax.fori_loop(0, 5, turn, 0)
            for j in range(2):
                part = cur[:, pl.ds(j * LANES, LANES)]
                result[:, pl.ds(j * TILE, TILE), :] = part.reshape(32, TILE, LANES)

    def give_back(self, index, device):
        rows, _, result = self.slab(index)
        return link(
            result.at[device], self.r.out.at[2, rows],
            self.r.back_send.at[device], self.r.back_recv.at[index], device,
        )

    def give_all(self):
        r = self.r
        for index in range(7):
            rows, _, result = self.slab(index)

            @pl.when(self.me == OWNERS[index])
            def _():
                def send_one(step, _):
                    self.give_back(index, (self.me + step) % 32).start()
                    return 0

                lax.fori_loop(1, 32, send_one, 0)
                pltpu.make_async_copy(result.at[self.me], r.out.at[2, rows], r.back_recv.at[index]).start()

    def take_all(self):
        for index in range(7):
            rows, _, result = self.slab(index)
            pltpu.make_async_copy(result.at[0], self.r.out.at[2, rows], self.r.back_recv.at[index]).wait()

    def drain(self):
        for index in range(7):

            @pl.when(self.me != OWNERS[index])
            def _():
                self.to_owner(index).wait_send()

            @pl.when(self.me == OWNERS[index])
            def _():
                def wait_one(step, _):
                    self.give_back(index, (self.me + step) % 32).wait_send()
                    return 0

                lax.fori_loop(1, 32, wait_one, 0)

        for k in range(len(CHUNKS)):
            self.core(k).wait_send()
            self.plane(k, True).wait_send()
            self.plane(k, False).wait_send()
            for step in range(3):
                self.along_z(k, step).wait_send()


def greet_all():
    me, z, y, x, c = place()
    greet(device_at(z, y, x, 1 - c))
    greet(device_at(z, y, 1 - x, c))
    greet(device_at(z, 1 - y, x, c))
    for step in range(1, 4):
        greet(device_at((z + step) % 4, y, x, c))
    owner = me < 0
    for device in OWNERS:
        owner = jnp.logical_or(owner, me == device)

        @pl.when(me != device)
        def _():
            greet(device)

    @pl.when(owner)
    def _():
        def greet_other(step, _):
            greet((me + step) % 32)
            return 0

        lax.fori_loop(1, 32, greet_other, 0)

    is_owner = owner.astype(jnp.int32)
    return 6 + 7 - is_owner + 31 * is_owner


def block_kernel(names, remote, *args):
    r = Refs(zip(names, args))
    keys, samples = r.obs.shape[0], r.obs.shape[1]
    tokens, width = r.acts.shape
    head_dim, half, per = width // HEADS, width // 2, ROWS // ACT
    wide = r.mlp_all.shape[2]
    groups = samples // GROUP
    in_sems, out_sems = r.in_sems, r.out_sems

    if remote:
        own = (r.sqw_v, r.mlpw_v, r.gain_v)
    else:
        own = (r.sq_all, r.mlp_all, r.gain_all)
    loads = list(zip((r.sqw, r.mlpw, r.gain), own))
    loads += [(r.acts, r.acts_v), (r.obs, r.obs_v.at[pl.ds(0, keys)]), (r.cot, r.cot_v)]
    if remote:
        loads += [(r.sqm, r.sqm_v), (r.mlpm, r.mlpm_v)]
    copies = [pltpu.make_async_copy(a, b, in_sems.at[i]) for i, (a, b) in enumerate(loads)]

    def arrive(*which):
        for i in which:
            copies[i].wait()

    for copy in copies:
        copy.start()
    if remote:
        gather, update = Gather(r), Update(r)
        expected = greet_all()
        arrive(0, 1, 2)
        gather.fill()
        pl.semaphore_wait(pltpu.get_barrier_semaphore(), expected)
        gather.first(3, 4, 2)

    arrive(3)

    def hats(i, _):
        rows = pl.ds(pl.multiple_of(i * ROWS, ROWS), ROWS)
        hat, scale = normalize(r.acts_v[rows, :])
        r.xhat[rows, :] = hat
        r.rstd[rows, :] = scale
        return 0

    lax.fori_loop(0, tokens // ROWS, hats, 0)

    mem, obs_v = r.mem, r.obs_v
    batch = 16
    chunks = KEYS_PAD // batch
    swap = r.swap
    row = lax.broadcasted_iota(jnp.int32, swap.shape, 0)
    column = lax.broadcasted_iota(jnp.int32, swap.shape, 1)
    swap[...] = jnp.where(column == (row % batch) * batch + row // batch, 1.0, 0.0).astype(BF16)

    def turn(part, low, high):
        def one(j, _):
            at = pl.ds(pl.multiple_of(j * batch, batch), batch)
            here = pl.ds(part * batch, batch)
            block = obs_v[at, here, :].reshape(batch * batch, width)
            mem[here, at, :] = dot(swap[...], block).astype(BF16).reshape(batch, batch, width)
            return 0

        lax.fori_loop(low, high, one, 0)

    whole = chunks - 1
    arrive(4)
    turn(0, 0, whole // 2)
    if remote:
        gather.second(3, 4, 2)
        gather.first(0, 1)
    turn(0, whole // 2, whole)
    if remote:
        gather.third(3, 4, 2)
    turn(1, 0, whole // 2)
    if remote:
        gather.second(0, 1)
        gather.fourth(3, 4, 2)
    turn(1, whole // 2, whole)
    freqs = jnp.exp(
        lax.broadcasted_iota(jnp.int32, (1, half), 1).astype(F32) * F32(-math.log(10000.0)) / half
    )
    for s in range(samples):
        r.angle[s : s + 1, :] = r.levels[s].astype(F32) * freqs
    r.embed[:, 0:half] = jnp.sin(r.angle[...]).astype(BF16)
    r.embed[:, half:width] = jnp.cos(r.angle[...]).astype(BF16)
    if remote:
        arrive(6, 7)
        update.old_moment()
        gather.third(0, 1)
        gather.last(3, 4, 2)
        for m in range(5):
            gather.unpack(SQ_AT[m], 1, r.sq_all, m)
        gather.unpack_gains()
    else:
        arrive(0, 1, 2)

    sq, mlp = r.sq_all, r.mlp_all
    wkh, wvh = r.wkh, r.wvh
    lane = lax.broadcasted_iota(jnp.int32, (width, width), 1)
    for h in range(HEADS):
        inside = lane // head_dim == h
        block = pl.ds(h * width, width)
        wkh[block, :] = jnp.where(inside, sq[2].astype(F32), 0.0).astype(BF16)
        wvh[block, :] = jnp.where(inside, sq[3].astype(F32), 0.0).astype(BF16)
    g1, g2 = r.gain_all[0:1, :], r.gain_all[1:2, :]

    obs_v[keys] = dot(r.embed[...], sq[0]).astype(BF16)
    obs_v[keys + 1 :] = jnp.zeros((KEYS_PAD - keys - 1, samples, width), BF16)
    for part in range(samples // batch):
        turn(part, whole, chunks)

    sides, weights = r.sides_v, r.pds_v

    def make_queries(i, _):
        rows = pl.ds(pl.multiple_of(i * ROWS, ROWS), ROWS)
        first = (r.xhat[rows, :] * g1).astype(BF16)
        r.first[rows, :] = first
        q = dot(first, sq[1]).astype(BF16)
        r.query[rows, :] = q
        here = pl.ds(i * per, per)
        for h in range(HEADS):
            wk = wkh[pl.ds(h * width, width), :]
            value = (dot(q, wk, NT) * 0.125).astype(BF16).reshape(per, ACT, width)
            sides[here, pl.ds((HEADS + h) * ACT, ACT), :] = value
        return 0

    lax.fori_loop(0, tokens // ROWS, make_queries, 0)

    key = lax.broadcasted_iota(jnp.int32, (HEADS * ACT, KEYS_PAD), 1)
    low_rows, high_rows = pl.ds(0, HEADS * ACT), pl.ds(HEADS * ACT, HEADS * ACT)

    def attend(g, _):
        ids = [g * GROUP + k for k in range(GROUP)]
        scores = [dot(sides[s, high_rows, :], mem[s], NT) for s in ids]
        lows = []
        for s, score in zip(ids, scores):
            count = OBS_FEW + (OBS_FULL - OBS_FEW) * r.flags[s]
            score = jnp.where((key < count) | (key == OBS_FULL), score, -1000000000.0)
            expo = jnp.exp(score - jnp.max(score, -1, keepdims=True))
            probs = expo * (1.0 / jnp.sum(expo, -1, keepdims=True))
            r.probs[s] = probs
            low = probs.astype(BF16)
            weights[s, low_rows, :] = low
            lows.append(low)
        for s, low in zip(ids, lows):
            u = dot(low, mem[s]).astype(BF16)
            rows = pl.ds(pl.multiple_of(s * ACT, ACT), ACT)
            for h in range(HEADS):
                r.u[rows, pl.ds(h * width, width)] = u[h * ACT : (h + 1) * ACT, :]
        return 0

    lax.fori_loop(0, groups // 2, attend, 0)
    if remote:
        gather.fourth(0, 1)
    lax.fori_loop(groups // 2, groups, attend, 0)
    if remote:
        gather.last(0, 1)
        for m in range(2):
            gather.unpack(m * MLP_ROWS, 4, mlp, m)

    gain_acc = r.gain_acc
    gain_acc[...] = jnp.zeros_like(gain_acc)
    arrive(5)

    def feed(i, _):
        rows = pl.ds(pl.multiple_of(i * ROWS, ROWS), ROWS)
        mixed = dot(r.u[rows, :], wvh[...]).astype(BF16)
        r.mixed[rows, :] = mixed
        resid = r.acts_v[rows, :] + dot(mixed, sq[4])
        hat, scale = normalize(resid)
        second = (hat * g2).astype(BF16)
        r.second[rows, :] = second
        cot = r.cot_v[rows, :]
        out_low = cot.astype(BF16)
        r.out_low[rows, :] = out_low
        for c in range(wide // 256):
            columns = pl.ds(c * 256, 256)
            v = dot(second, mlp[0, :, columns])
            square = v * v
            t = jnp.tanh(0.7978845608 * (v + 0.044715 * square * v))
            r.active[rows, columns] = (0.5 * v * (1.0 + t)).astype(BF16)
            slope = 0.5 * (1.0 + t) + 0.5 * v * (1.0 - t * t) * (0.7978845608 * (1.0 + 0.134145 * square))
            r.dhidden[rows, columns] = (slope * dot(out_low, mlp[1, :, columns])).astype(BF16)
        r.out_v[rows, :] = resid + dot(r.active[rows, :], mlp[1], NT)
        grad_second = dot(r.dhidden[rows, :], mlp[0], NT)
        gain_acc[1:2, :] += jnp.sum(grad_second * hat, 0, keepdims=True)
        dres = cot + norm_back(grad_second * g2, hat, scale)
        r.dres[rows, :] = dres
        low = dres.astype(BF16)
        r.dres_low[rows, :] = low
        gm = dot(low, sq[4], NT).astype(BF16)
        r.dmixed[rows, :] = gm
        here = pl.ds(i * per, per)
        for h in range(HEADS):
            wv = wvh[pl.ds(h * width, width), :]
            sides[here, pl.ds(h * ACT, ACT), :] = dot(gm, wv, NT).astype(BF16).reshape(per, ACT, width)
        return 0

    lax.fori_loop(0, tokens // ROWS, feed, 0)
    keep_out = pltpu.make_async_copy(r.out_v, r.output, out_sems.at[0])
    keep_out.start()

    grads = r.grads

    def put(base, tiles, value):
        for j in range(tiles):
            part = value[:, j * LANES : (j + 1) * LANES].reshape(GRID + (TILE, LANES))
            grads[:, :, :, :, pl.ds(base + j * TILE, TILE), :] = part

    def by_head(left, right):
        turned = left.T
        parts = [
            dot(turned[h * head_dim : (h + 1) * head_dim, :], right[:, pl.ds(h * width, width)])
            for h in range(HEADS)
        ]
        return jnp.concatenate(parts, axis=0).T

    put(0, 8, dot(r.second[...], r.dhidden[...], TN))
    if remote:
        update.start(0)
    put(MLP_ROWS, 8, dot(r.out_low[...], r.active[...], TN))
    if remote:
        update.start(1)
    put(SQ_AT[4], 2, dot(r.mixed[...], r.dres_low[...], TN))
    put(SQ_AT[3], 2, by_head(r.dmixed[...], r.u))
    if remote:
        update.start(2)

    def attend_back(g, _):
        ids = [g * GROUP + k for k in range(GROUP)]
        rises = [dot(sides[s, low_rows, :], mem[s], NT) for s in ids]
        for s, rise in zip(ids, rises):
            probs = r.probs[s]
            both = probs * rise
            weights[s, high_rows, :] = (both - probs * jnp.sum(both, -1, keepdims=True)).astype(BF16)
        for s in ids:
            dq = (dot(weights[s, high_rows, :], mem[s]) * 0.125).astype(BF16)
            rows = pl.ds(pl.multiple_of(s * ACT, ACT), ACT)
            for h in range(HEADS):
                r.dq_wide[rows, pl.ds(h * width, width)] = dq[h * ACT : (h + 1) * ACT, :]
            end = dot(weights[s, :, LANES:KEYS_PAD], sides[s], TN)
            r.stamps[s] = end[64:72, :]
        return 0

    quarter = groups // 4
    lax.fori_loop(0, quarter, attend_back, 0)
    if remote:
        update.one(0, 1)
    lax.fori_loop(quarter, 2 * quarter, attend_back, 0)
    if remote:
        update.two(0, 1)
        update.one(2)
    lax.fori_loop(2 * quarter, 3 * quarter, attend_back, 0)
    if remote:
        update.three(0, 1)
        update.two(2)
    lax.fori_loop(3 * quarter, groups, attend_back, 0)

    def memory_back(low, high):
        def one(g, _):
            for k in range(GROUP):
                s = g * GROUP + k
                mem[s] = dot(weights[s], sides[s], TN).astype(BF16)
            return 0

        lax.fori_loop(low, high, one, 0)

    def turn_back(part):
        def one(j, _):
            at = pl.ds(pl.multiple_of(j * batch, batch), batch)
            here = pl.ds(part * batch, batch)
            block = mem[here, at, :].reshape(batch * batch, width)
            obs_v[at, here, :] = dot(swap[...], block).astype(BF16).reshape(batch, batch, width)
            return 0

        lax.fori_loop(0, chunks, one, 0)

    def queries_back(i, _):
        rows = pl.ds(pl.multiple_of(i * ROWS, ROWS), ROWS)
        r.dquery[rows, :] = dot(r.dq_wide[rows, :], wkh[...]).astype(BF16)
        return 0

    lax.fori_loop(0, tokens // ROWS, queries_back, 0)
    put(SQ_AT[1], 2, dot(r.first[...], r.dquery[...], TN))
    stamp_low = r.stamps[:, 4:5, :].reshape(samples, width).astype(BF16)
    put(SQ_AT[0], 2, dot(r.embed[...], stamp_low, TN))
    if remote:
        update.start(3)

    def acts_back(i, _):
        rows = pl.ds(pl.multiple_of(i * ROWS, ROWS), ROWS)
        grad_first = dot(r.dquery[rows, :], sq[1], NT)
        hat = r.xhat[rows, :]
        gain_acc[0:1, :] += jnp.sum(grad_first * hat, 0, keepdims=True)
        r.ag_v[rows, :] = r.dres[rows, :] + norm_back(grad_first * g1, hat, r.rstd[rows, :])
        return 0

    lax.fori_loop(0, tokens // ROWS, acts_back, 0)
    put(SQ_AT[2], 2, by_head(r.query[...], r.dq_wide))
    for norm in range(2):
        for j in range(2):
            row = gain_acc[norm : norm + 1, j * LANES : (j + 1) * LANES]
            at = GAIN_BASE + norm * 2 + j
            value = jnp.broadcast_to(row.reshape(1, 1, 1, 1, 1, LANES), GRID + (1, LANES))
            grads[:, :, :, :, at : at + 1, :] = value
    rest = WIRE - GAIN_BASE - 4
    grads[:, :, :, :, GAIN_BASE + 4 : WIRE, :] = jnp.zeros(GRID + (rest, LANES), F32)
    keep_ag = pltpu.make_async_copy(r.ag_v, r.ag, out_sems.at[2])
    keep_ag.start()
    keep_og = pltpu.make_async_copy(obs_v.at[pl.ds(0, keys)], r.og, out_sems.at[1])
    half_groups = groups // 2
    if remote:
        update.start(4)
        update.three(2)
        update.four(0, 1)
        memory_back(0, half_groups)
        update.one(3, 4)
        update.four(2)
        turn_back(0)
        update.two(3, 4)
        memory_back(half_groups, groups)
        update.three(3, 4)
        turn_back(1)
        keep_og.start()
        update.four(3, 4)
        update.orthogonalize()
        update.give_all()
        out = r.out
        out[1, :, :] = r.moment[...]
        out[2, pl.ds(GAIN_BASE, 16), :] = jnp.zeros((16, LANES), F32)
        update.take_all()
        gather.drain()
        update.drain()
    else:
        memory_back(0, groups)
        for part in range(samples // batch):
            turn_back(part)
        keep_og.start()
    for copy in (keep_out, keep_og, keep_ag):
        copy.wait()


def block_and_back(remote, acts, obs, flags, levels, cot, sqw, mlpw, gain, sqm=None, mlpm=None):
    tokens, width = acts.shape
    keys, samples = obs.shape[0], obs.shape[1]
    rows = HEADS * ACT
    wide = mlpw.shape[2]
    any_space = pl.BlockSpec(memory_space=pl.ANY)
    in_vmem = pl.BlockSpec(memory_space=VMEM)
    scalars = pl.BlockSpec(memory_space=pltpu.SMEM)
    sem = pltpu.SemaphoreType.DMA
    ins = dict(flags=flags, levels=levels, acts=acts, obs=obs, cot=cot, sqw=sqw, mlpw=mlpw, gain=gain)
    outs = dict(
        output=jax.ShapeDtypeStruct(acts.shape, F32),
        ag=jax.ShapeDtypeStruct(acts.shape, F32),
        og=jax.ShapeDtypeStruct(obs.shape, BF16),
    )
    grads = GRID + (WIRE, LANES)
    scratch = dict(
        obs_v=VMEM((KEYS_PAD, samples, width), BF16),
        acts_v=VMEM(acts.shape, F32),
        cot_v=VMEM(acts.shape, F32),
        mem=VMEM((samples, KEYS_PAD, width), BF16),
        swap=VMEM((256, 256), BF16),
        sq_all=VMEM((5, width, width), BF16),
        mlp_all=VMEM((2, width, wide), BF16),
        gain_all=VMEM((2, width), F32),
        wkh=VMEM((HEADS * width, width), BF16),
        wvh=VMEM((HEADS * width, width), BF16),
        first=VMEM((tokens, width), BF16),
        query=VMEM((tokens, width), BF16),
        xhat=VMEM((tokens, width), F32),
        rstd=VMEM((tokens, 1), F32),
        probs=VMEM((samples, rows, KEYS_PAD), F32),
        pds_v=VMEM((samples, 2 * rows, KEYS_PAD), BF16),
        sides_v=VMEM((samples, 2 * rows, width), BF16),
        u=VMEM((tokens, HEADS * width), BF16),
        dq_wide=VMEM((tokens, HEADS * width), BF16),
        mixed=VMEM((tokens, width), BF16),
        second=VMEM((tokens, width), BF16),
        active=VMEM((tokens, wide), BF16),
        dhidden=VMEM((tokens, wide), BF16),
        out_low=VMEM((tokens, width), BF16),
        dres_low=VMEM((tokens, width), BF16),
        dres=VMEM((tokens, width), F32),
        dmixed=VMEM((tokens, width), BF16),
        dquery=VMEM((tokens, width), BF16),
        out_v=VMEM((tokens, width), F32),
        ag_v=VMEM((tokens, width), F32),
        angle=VMEM((samples, width // 2), F32),
        embed=VMEM((samples, width), BF16),
        stamps=VMEM((samples, 8, width), F32),
        gain_acc=VMEM((8, width), F32),
        in_sems=sem((8,)),
        out_sems=sem((3,)),
    )
    extra = {}
    if remote:
        ins.update(sqm=sqm, mlpm=mlpm)
        outs.update(out=jax.ShapeDtypeStruct((3, WIRE, LANES), F32))
        chunks = len(CHUNKS)
        scratch.update(
            grads=VMEM(grads, F32),
            sqw_v=VMEM(sqw.shape, F32),
            mlpw_v=VMEM(mlpw.shape, F32),
            gain_v=VMEM(gain.shape, F32),
            sqm_v=VMEM(sqm.shape, F32),
            mlpm_v=VMEM(mlpm.shape, F32),
            wire=VMEM(grads, BF16),
            edge=VMEM((16, LANES), F32),
            gsend=sem((chunks, 6)),
            grecv=sem((chunks, 6)),
            got_core=VMEM((4, 2, 2, WIRE, LANES), F32),
            sum1=VMEM((4, 2, 2, WIRE, LANES), F32),
            send1=VMEM((4, 2, WIRE, LANES), BF16),
            got1=VMEM((4, 2, WIRE, LANES), BF16),
            sum2=VMEM((4, 2, WIRE, LANES), F32),
            send2=VMEM((4, WIRE, LANES), BF16),
            got2=VMEM((4, WIRE, LANES), BF16),
            sum3=VMEM((4, WIRE, LANES), F32),
            send3=VMEM((3, WIRE, LANES), BF16),
            got3=VMEM((3, WIRE, LANES), BF16),
            moment=VMEM((WIRE, LANES), F32),
            slabs_sq=VMEM((32, SQ_ROWS, LANES), F32),
            slabs_mlp=VMEM((32, MLP_ROWS, LANES), F32),
            result_sq=VMEM((32, SQ_ROWS, LANES), F32),
            result_mlp=VMEM((32, MLP_ROWS, LANES), F32),
            cur=VMEM((width, wide), F32),
            gram_s=VMEM((width, width), F32),
            prod_s=VMEM((width, width), F32),
            send=sem((chunks, 6)),
            recv=sem((chunks, 6)),
            own_send=sem((7,)),
            own_recv=sem((1,)),
            back_send=sem((32,)),
            back_recv=sem((7,)),
        )
        extra = dict(collective_id=0, has_side_effects=True)
    else:
        outs.update(grads=jax.ShapeDtypeStruct(grads, F32))
    names = tuple(ins) + tuple(outs) + tuple(scratch)
    results = pl.pallas_call(
        functools.partial(block_kernel, names, remote),
        out_shape=tuple(outs.values()),
        in_specs=[scalars] * 2 + [any_space] * (len(ins) - 2),
        out_specs=[any_space] * 3 + [in_vmem],
        scratch_shapes=list(scratch.values()),
        compiler_params=pltpu.CompilerParams(vmem_limit_bytes=56 << 20, **extra),
        name="block_and_back",
    )(*ins.values())
    return Refs(zip(outs, results))


PARTS = 7


def finish_kernel(names, rate, *args):
    r = Refs(zip(names, args))
    sems = r.sems
    keys = r.og.shape[0]
    step = keys // PARTS

    def come(part):
        block = pl.ds(part * step, step)
        return pltpu.make_async_copy(r.low.at[block], r.low_v.at[block], sems.at[2 * part])

    def leave(part):
        block = pl.ds(part * step, step)
        return pltpu.make_async_copy(r.og_v.at[block], r.og.at[block], sems.at[2 * part + 1])

    for part in range(PARTS):
        come(part).start()
    more = 2 * PARTS
    small, passes = [], []
    if hasattr(r, "wire"):
        pairs = [(r.output, r.output_v), (r.ag, r.ag_v), (r.wire, r.wire_v), (r.sqw, r.sqw_v)]
        pairs += [(r.mlpw, r.mlpw_v), (r.gain, r.gain_v), (r.gainm, r.gainm_v)]
        for source, target in pairs:
            small.append(pltpu.make_async_copy(source, target, sems.at[more]))
            small[-1].start()
            more += 1
        for source, target in ((r.output_v, r.output_f), (r.ag_v, r.ag_f)):
            passes.append(pltpu.make_async_copy(source, target, sems.at[more]))
            more += 1
    for part in range(PARTS):
        come(part).wait()

        def widen(j, _):
            r.og_v[j] = r.low_v[j].astype(F32)
            return 0

        lax.fori_loop(part * step, (part + 1) * step, widen, 0, unroll=4)
        leave(part).start()
    for copy in small[:2]:
        copy.wait()
    for copy in passes:
        copy.start()
    if hasattr(r, "wire"):
        for copy in small[2:]:
            copy.wait()
        finish_weights(r, rate)
    for part in range(PARTS):
        leave(part).wait()
    for copy in passes:
        copy.wait()


def finish_weights(r, rate):
    wire = r.wire_v
    me = lax.axis_index("dp")
    for m in range(5):
        for j in range(2):
            rows, columns = pl.ds(SQ_AT[m] + j * TILE, TILE), pl.ds(j * LANES, LANES)
            r.sqg[m, :, columns] = wire[0, rows, :]
            r.sqm[m, :, columns] = wire[1, rows, :]
            r.sqn[m, :, columns] = r.sqw_v[m, :, columns] - SQ_RATES[m] * wire[2, rows, :]
    r.sqc[...] = r.sqn[...].astype(BF16)
    for m in range(2):
        for j in range(8):
            rows, columns = pl.ds(m * MLP_ROWS + j * TILE, TILE), pl.ds(j * LANES, LANES)
            r.mlpg[m, :, columns] = wire[0, rows, :]
            r.mlpm[m, :, columns] = wire[1, rows, :]
            r.mlpn[m, :, columns] = r.mlpw_v[m, :, columns] - MLP_RATES[m] * wire[2, rows, :]
    r.mlpc[...] = r.mlpn[...].astype(BF16)
    tile = wire[0, pl.ds(GAIN_BASE, TILE), :]
    turned = pltpu.roll(tile, (LANES - (me % 16) * TILE) % LANES, 1)
    at = me // 16
    for norm in range(2):
        pair = turned[2 * norm : 2 * norm + 2, 0:TILE]
        row = jnp.where(at == 0, pair[0:1, :], pair[1:2, :])
        new = 0.5 * r.gainm_v[norm : norm + 1, :] + row
        r.gg[norm : norm + 1, :] = row
        r.gm[norm : norm + 1, :] = new
        r.gn[norm : norm + 1, :] = r.gain_v[norm : norm + 1, :] - rate * new


def finish(rate, made, sqw=None, mlpw=None, gain=None, gainm=None):
    any_space = pl.BlockSpec(memory_space=pl.ANY)
    in_vmem = pl.BlockSpec(memory_space=VMEM)
    ins = dict(low=made.og)
    outs = dict(og=jax.ShapeDtypeStruct(made.og.shape, F32))
    far = 1
    if hasattr(made, "out"):
        ins.update(output=made.output, ag=made.ag, wire=made.out, sqw=sqw, mlpw=mlpw, gain=gain, gainm=gainm)
        like = jax.ShapeDtypeStruct
        far = 3
        outs.update(
            output_f=like(made.output.shape, F32),
            ag_f=like(made.ag.shape, F32),
            sqg=like(sqw.shape, F32),
            sqm=like(sqw.shape, F32),
            sqn=like(sqw.shape, F32),
            sqc=like(sqw.shape, BF16),
            mlpg=like(mlpw.shape, F32),
            mlpm=like(mlpw.shape, F32),
            mlpn=like(mlpw.shape, F32),
            mlpc=like(mlpw.shape, BF16),
            gg=like(gain.shape, F32),
            gm=like(gain.shape, F32),
            gn=like(gain.shape, F32),
        )
    scratch = dict(
        low_v=VMEM(made.og.shape, BF16),
        og_v=VMEM(made.og.shape, F32),
        sems=pltpu.SemaphoreType.DMA((2 * PARTS + 9,)),
    )
    if hasattr(made, "out"):
        scratch.update(
            output_v=VMEM(made.output.shape, F32),
            ag_v=VMEM(made.ag.shape, F32),
            wire_v=VMEM(made.out.shape, F32),
            sqw_v=VMEM(sqw.shape, F32),
            mlpw_v=VMEM(mlpw.shape, F32),
            gain_v=VMEM(gain.shape, F32),
            gainm_v=VMEM(gainm.shape, F32),
        )
    names = tuple(ins) + tuple(outs) + tuple(scratch)
    results = pl.pallas_call(
        functools.partial(finish_kernel, names, rate),
        out_shape=tuple(outs.values()),
        in_specs=[any_space] * len(ins),
        out_specs=[any_space] * far + [in_vmem] * (len(outs) - far),
        scratch_shapes=list(scratch.values()),
        compiler_params=pltpu.CompilerParams(vmem_limit_bytes=60 << 20),
        name="finish",
    )(*ins.values())
    return Refs(zip(outs, results))


HIGH_PRECISION = lax.Precision.HIGHEST


def plain_orthogonalize(matrix):
    current = matrix / (jnp.sqrt(jnp.sum(matrix * matrix)) + 1e-07)
    for turn in range(5):
        gram = jnp.dot(current, current.T, precision=HIGH_PRECISION)
        poly = COEF_B * gram + COEF_C * jnp.dot(gram, gram, precision=HIGH_PRECISION)
        current = COEF_A * current + jnp.dot(poly, current, precision=HIGH_PRECISION)
    return current


def pick_owned(stack, owners, device):
    chosen = jnp.zeros_like(stack[0])
    for index in range(len(owners)):
        chosen = jnp.where(device == owners[index], stack[index], chosen)
    return chosen


def is_owner(owners, device):
    flag = device < 0
    for owner in owners:
        flag = jnp.logical_or(flag, device == owner)
    return flag


def from_wire(grads):
    def matrix(base, tiles):
        part = grads[:, base : base + tiles * TILE, :].reshape(-1, tiles, TILE, LANES)
        return part.transpose(0, 2, 1, 3).reshape(-1, tiles * LANES)

    square = jnp.stack([matrix(SQ_AT[m], 2) for m in range(5)])
    mlp = jnp.stack([matrix(m * MLP_ROWS, 8) for m in range(2)])
    return square, mlp, grads[0, GAIN_BASE : GAIN_BASE + 4, :].reshape(2, 2 * LANES)


def update_by_collectives(
    grads, square_weights, mlp_weights, gains, square_moment, mlp_moment, gain_moment, rate
):
    square_local, mlp_local, gain_local = from_wire(grads)
    square_grad, mlp_grad, gain_grad = (
        lax.psum_scatter(square_local, "dp", scatter_dimension=1, tiled=True),
        lax.psum_scatter(mlp_local, "dp", scatter_dimension=1, tiled=True),
        lax.psum_scatter(gain_local, "dp", scatter_dimension=1, tiled=True),
    )
    square_moment_new = 0.5 * square_moment + square_grad
    mlp_moment_new = 0.5 * mlp_moment + mlp_grad
    gain_moment_new = 0.5 * gain_moment + gain_grad
    device = lax.axis_index("dp")
    count = lax.axis_size("dp")
    square_owners = [index * count // 7 for index in range(5)]
    mlp_owners = [(index + 5) * count // 7 for index in range(2)]
    square_full, mlp_full = (
        lax.all_gather(square_moment_new, "dp", axis=1, tiled=True),
        lax.all_gather(mlp_moment_new, "dp", axis=1, tiled=True),
    )
    mine_square = pick_owned(square_full, square_owners, device)
    mine_mlp = pick_owned(mlp_full, mlp_owners, device)
    made_square = lax.cond(
        is_owner(square_owners, device), plain_orthogonalize, jnp.zeros_like, mine_square
    )
    made_mlp = lax.cond(is_owner(mlp_owners, device), plain_orthogonalize, jnp.zeros_like, mine_mlp)
    stack_square = jnp.stack(
        [jnp.where(device == owner, made_square, 0.0) for owner in square_owners]
    )
    stack_mlp = jnp.stack([jnp.where(device == owner, made_mlp, 0.0) for owner in mlp_owners])
    square_ortho, mlp_ortho = (
        lax.psum_scatter(stack_square, "dp", scatter_dimension=1, tiled=True),
        lax.psum_scatter(stack_mlp, "dp", scatter_dimension=1, tiled=True),
    )
    square_new = square_weights - jnp.array(SQ_RATES, F32)[:, None, None] * square_ortho
    mlp_new = mlp_weights - jnp.array(MLP_RATES, F32)[:, None, None] * mlp_ortho
    gains_new = gains - rate * gain_moment_new
    return (
        square_grad,
        square_moment_new,
        square_new,
        square_new.astype(BF16),
        mlp_grad,
        mlp_moment_new,
        mlp_new,
        mlp_new.astype(BF16),
        gain_grad,
        gain_moment_new,
        gains_new,
    )


def per_device(
    actions,
    observed,
    camera_flags,
    noise_levels,
    cotangent,
    square_weights,
    mlp_weights,
    gains,
    square_moment,
    mlp_moment,
    gain_moment,
):
    count = lax.axis_size("dp")
    rate = 0.1 / math.sqrt(actions.shape[0] * count)
    by_key = observed.transpose(1, 0, 2)
    ins = (actions, by_key, camera_flags, noise_levels, cotangent)
    if count == math.prod(GRID):
        made = block_and_back(True, *ins, square_weights, mlp_weights, gains, square_moment, mlp_moment)
        done = finish(rate, made, square_weights, mlp_weights, gains, gain_moment)
        output, actions_grad = done.output_f, done.ag_f
        d = done
        rest = (d.sqg, d.sqm, d.sqn, d.sqc, d.mlpg, d.mlpm, d.mlpn, d.mlpc, d.gg, d.gm, d.gn)
    else:
        square_all, mlp_all = (
            lax.all_gather(square_weights.astype(BF16), "dp", axis=1, tiled=True),
            lax.all_gather(mlp_weights.astype(BF16), "dp", axis=1, tiled=True),
        )
        gain_all = lax.all_gather(gains, "dp", axis=1, tiled=True)
        made = block_and_back(False, *ins, square_all, mlp_all, gain_all)
        done = finish(rate, made)
        output, actions_grad = made.output, made.ag
        grads = made.grads.reshape(-1, WIRE, LANES)
        rest = update_by_collectives(
            grads, square_weights, mlp_weights, gains, square_moment, mlp_moment, gain_moment, rate
        )
    observed_grad = done.og.transpose(1, 0, 2)
    return (output, actions_grad, observed_grad) + tuple(rest)


def solution(mesh):
    rows, cube, flat = P("dp", None), P("dp", None, None), P("dp")
    stacked, pair = P(None, "dp", None), P(None, "dp")
    return jax.shard_map(
        per_device,
        mesh=mesh,
        in_specs=(rows, cube, flat, flat, rows, stacked, stacked, pair, stacked, stacked, pair),
        out_specs=(rows, rows, cube) + (stacked,) * 8 + (pair,) * 3,
        check_vma=False,
    )
```

```python
import functools
import math

import jax
import jax.numpy as jnp
from jax import lax
from jax.experimental import pallas as pl
from jax.experimental.pallas import tpu as pltpu
from jax.sharding import PartitionSpec as P

HEADS = 4
ACT = 16
OBS_FULL = 196
OBS_FEW = 49
COEF_A = 3.4445
COEF_B = -4.775
COEF_C = 2.0315
F32 = jnp.float32
BF16 = jnp.bfloat16
MESH = pl.DeviceIdType.MESH
VMEM = pltpu.VMEM
NN = (((1,), (0,)), ((), ()))
NT = (((1,), (1,)), ((), ()))
TN = (((0,), (0,)), ((), ()))

LANES = 128
TILE = 8
MLP_ROWS = 64
SQ_ROWS = 16
SQ_AT = (160, 176, 192, 128, 144)
GAIN_BASE = 208
WIRE = 224
CHUNKS = ((0, 64), (64, 64), (128, 32), (160, 32), (192, 32))
X_FIRST = (True, False, True, True, False)
MLP_RATES = (1.0, 0.5)
SQ_RATES = (0.5, 0.5, 0.5, 0.5, 4.0)
GRID = (4, 2, 2, 2)
OWNERS = (8, 22, 14, 16, 11, 21, 13)
SHIFTS = (0.0, 0.0, 0.4, 0.8, 0.8)
KEYS_PAD = 208
GROUP = 4
ROWS = 256


class Refs:
    def __init__(self, pairs):
        self.__dict__.update(pairs)


def dot(left, right, dims=NN):
    return lax.dot_general(left, right, dims, preferred_element_type=F32)


def place():
    me = lax.axis_index("dp")
    return me, me // 8, (me // 4) % 2, (me // 2) % 2, me % 2


def device_at(z, y, x, c):
    return ((z * 2 + y) * 2 + x) * 2 + c


def link(src, dst, send, recv, device):
    return pltpu.make_async_remote_copy(
        src_ref=src,
        dst_ref=dst,
        send_sem=send,
        recv_sem=recv,
        device_id=(device,),
        device_id_type=MESH,
    )


def greet(device):
    pl.semaphore_signal(
        pltpu.get_barrier_semaphore(), inc=1, device_id=(device,), device_id_type=MESH
    )


def normalize(values):
    centred = values - jnp.mean(values, -1, keepdims=True)
    scale = lax.rsqrt(jnp.mean(centred * centred, -1, keepdims=True) + 1e-05)
    return centred * scale, scale


def norm_back(grad, hat, scale):
    mean_one = jnp.mean(grad, -1, keepdims=True)
    mean_two = jnp.mean(grad * hat, -1, keepdims=True)
    return scale * (grad - mean_one - hat * mean_two)


class Gather:
    def __init__(self, r):
        self.r = r
        self.me, self.z, self.y, self.x, self.c = place()

    def hop(self, k, step, part, device):
        return link(part, part, self.r.gsend.at[k, step], self.r.grecv.at[k, step], device)

    def along_z(self, k, step):
        part = self.r.wire.at[self.z, self.y, self.x, self.c, pl.ds(*CHUNKS[k])]
        return self.hop(k, step, part, device_at((self.z + step + 1) % 4, self.y, self.x, self.c))

    def from_z(self, k, step):
        there = (self.z + 3 - step) % 4
        part = self.r.wire.at[there, self.y, self.x, self.c, pl.ds(*CHUNKS[k])]
        return self.hop(k, step, part, device_at(there, self.y, self.x, self.c))

    def plane(self, k, second, mine):
        z, y, x, c = self.z, self.y, self.x, self.c
        rows, wire = pl.ds(*CHUNKS[k]), self.r.wire
        py, px = (y, x) if mine else (1 - y, 1 - x)
        along_x = X_FIRST[k] == second
        if along_x:
            part = wire.at[:, y, px, c, rows] if second else wire.at[:, :, px, c, rows]
            return self.hop(k, 3 if second else 4, part, device_at(z, y, 1 - x, c))
        part = wire.at[:, py, x, c, rows] if second else wire.at[:, py, :, c, rows]
        return self.hop(k, 3 if second else 4, part, device_at(z, 1 - y, x, c))

    def core(self, k, mine):
        part = self.r.wire.at[:, :, :, self.c if mine else 1 - self.c, pl.ds(*CHUNKS[k])]
        return self.hop(k, 5, part, device_at(self.z, self.y, self.x, 1 - self.c))

    def first(self, *chunks):
        for k in chunks:
            for step in range(3):
                self.along_z(k, step).start()

    def second(self, *chunks):
        for k in chunks:
            for step in range(3):
                self.from_z(k, step).wait_recv()
            self.plane(k, True, True).start()

    def third(self, *chunks):
        for k in chunks:
            self.plane(k, True, False).wait_recv()
            self.plane(k, False, True).start()

    def fourth(self, *chunks):
        for k in chunks:
            self.plane(k, False, False).wait_recv()
            self.core(k, True).start()

    def last(self, *chunks):
        for k in chunks:
            self.core(k, False).wait_recv()

    def drain(self):
        for k in range(len(CHUNKS)):
            for step in range(3):
                self.along_z(k, step).wait_send()
            self.plane(k, True, True).wait_send()
            self.plane(k, False, True).wait_send()
            self.core(k, True).wait_send()

    def fill(self):
        r = self.r
        spot = (self.z, self.y, self.x, self.c)

        def tiles(source, m, base, number):
            for j in range(number):
                pair = [source[m, :, pl.ds((2 * j + k) * LANES, LANES)] for k in range(2)]
                r.wire[spot + (pl.ds(base + j * 16, 16),)] = jnp.concatenate(pair, axis=0).astype(BF16)

        for m in range(5):
            tiles(r.sqw_v, m, SQ_AT[m], 1)
        for m in range(2):
            tiles(r.mlpw_v, m, m * MLP_ROWS, 4)
        gains, edge = r.gain_v[...], r.edge
        high = gains.astype(BF16).astype(F32)
        middle = (gains - high).astype(BF16).astype(F32)
        edge[...] = jnp.zeros_like(edge)
        edge[0:2, 0:TILE] = high
        edge[2:4, 0:TILE] = middle
        edge[4:6, 0:TILE] = (gains - high - middle).astype(BF16).astype(F32)
        r.wire[spot + (pl.ds(GAIN_BASE, 16),)] = edge[...].astype(BF16)

    def unpack(self, base, number, out, m):
        for j in range(number):
            block = self.r.wire[:, :, :, :, pl.ds(base + j * 16, 16), :].reshape(32, 16, LANES).astype(F32)
            for half in range(2):
                columns = pl.ds((2 * j + half) * LANES, LANES)
                out[m, :, columns] = block[:, half * 8 : half * 8 + 8, :].reshape(256, LANES).astype(BF16)

    def unpack_gains(self):
        edge, wire = self.r.edge, self.r.wire
        for half in range(2):
            total = jnp.zeros((16, LANES), F32)
            for at in range(16):
                d = half * 16 + at
                tile = wire[d // 8, (d // 4) % 2, (d // 2) % 2, d % 2, pl.ds(GAIN_BASE, 16), :].astype(F32)
                total = total + (tile if at == 0 else pltpu.roll(tile, at * TILE, 1))
            edge[...] = total
            self.r.gain_all[:, pl.ds(half * LANES, LANES)] = edge[0:2, :] + edge[2:4, :] + edge[4:6, :]


class Update:
    def __init__(self, r):
        self.r = r
        self.me, self.z, self.y, self.x, self.c = place()

    def hop(self, k, step, src, dst, device):
        return link(src, dst, self.r.send.at[k, step], self.r.recv.at[k, step], device)

    def core(self, k):
        rows = pl.ds(*CHUNKS[k])
        src, dst = self.r.send0.at[:, :, :, rows], self.r.got_core.at[:, :, :, rows]
        return self.hop(k, 0, src, dst, device_at(self.z, self.y, self.x, 1 - self.c))

    def plane(self, k, first):
        rows = pl.ds(*CHUNKS[k])
        to = (self.z, self.y, 1 - self.x, self.c) if X_FIRST[k] == first else (self.z, 1 - self.y, self.x, self.c)
        if first:
            src, dst = self.r.send1.at[:, :, rows], self.r.got1.at[:, :, rows]
        else:
            src, dst = self.r.send2.at[:, rows], self.r.got2.at[:, rows]
        return self.hop(k, 1 if first else 2, src, dst, device_at(*to))

    def along_z(self, k, step):
        rows = pl.ds(*CHUNKS[k])
        to = device_at((self.z + step + 1) % 4, self.y, self.x, self.c)
        return self.hop(k, 3 + step, self.r.send3.at[step, rows], self.r.got3.at[step, rows], to)

    def start(self, k):
        rows = pl.ds(*CHUNKS[k])
        self.r.send0[:, :, :, rows, :] = self.r.grads[:, :, :, 1 - self.c, rows, :].astype(BF16)
        self.core(k).start()

    def one(self, *chunks):
        r = self.r
        for k in chunks:
            rows = pl.ds(*CHUNKS[k])
            self.core(k).wait_recv()
            sum1 = r.sum1
            sum1[:, :, :, rows, :] = r.grads[:, :, :, self.c, rows, :] + r.got_core[:, :, :, rows, :].astype(F32)
            other = sum1[:, :, 1 - self.x, rows, :] if X_FIRST[k] else sum1[:, 1 - self.y, :, rows, :]
            r.send1[:, :, rows, :] = other.astype(BF16)
            self.plane(k, True).start()

    def two(self, *chunks):
        r = self.r
        for k in chunks:
            rows = pl.ds(*CHUNKS[k])
            self.plane(k, True).wait_recv()
            sum1, sum2 = r.sum1, r.sum2
            mine = sum1[:, :, self.x, rows, :] if X_FIRST[k] else sum1[:, self.y, :, rows, :]
            sum2[:, :, rows, :] = mine + r.got1[:, :, rows, :].astype(F32)
            other = 1 - self.y if X_FIRST[k] else 1 - self.x
            r.send2[:, rows, :] = sum2[:, other, rows, :].astype(BF16)
            self.plane(k, False).start()

    def three(self, *chunks):
        r = self.r
        for k in chunks:
            rows = pl.ds(*CHUNKS[k])
            self.plane(k, False).wait_recv()
            mine = self.y if X_FIRST[k] else self.x
            r.sum3[:, rows, :] = r.sum2[:, mine, rows, :] + r.got2[:, rows, :].astype(F32)
            for step in range(3):
                r.send3[step, rows, :] = r.sum3[(self.z + step + 1) % 4, rows, :].astype(BF16)
                self.along_z(k, step).start()

    def slab(self, index):
        if index < 2:
            return pl.ds(index * MLP_ROWS, MLP_ROWS), self.r.slabs_mlp, self.r.result_mlp
        return pl.ds(SQ_AT[index - 2], SQ_ROWS), self.r.slabs_sq, self.r.result_sq

    def to_owner(self, index):
        rows, slabs, _ = self.slab(index)
        moment = self.r.moment_low if index < 2 else self.r.moment
        return link(
            moment.at[rows], slabs.at[self.me],
            self.r.own_send.at[index], self.r.own_recv.at[0], OWNERS[index],
        )

    def four(self, *chunks):
        r = self.r
        moment, out = r.moment, r.out
        for k in chunks:
            rows = pl.ds(*CHUNKS[k])
            total = r.sum3[self.z, rows, :]
            for step in range(3):
                self.along_z(k, step).wait_recv()
                total = total + r.got3[step, rows, :].astype(F32)
            out[0, rows, :] = total
            new = 0.5 * moment[rows, :] + total
            moment[rows, :] = new
            if k < 2:
                r.moment_low[rows, :] = new.astype(BF16)
            for index in ((0,), (1,), (5, 6), (2, 3), (4,))[k]:
                rows_m, slabs, _ = self.slab(index)

                @pl.when(self.me != OWNERS[index])
                def _():
                    self.to_owner(index).start()

                @pl.when(self.me == OWNERS[index])
                def _():
                    mine = r.moment_low if index < 2 else moment
                    pltpu.make_async_copy(mine.at[rows_m], slabs.at[self.me], r.own_recv.at[0]).start()

    def old_moment(self):
        r = self.r
        moment = r.moment
        for m in range(2):
            for j in range(8):
                moment[pl.ds(m * MLP_ROWS + j * TILE, TILE), :] = r.mlpm_v[m, :, pl.ds(j * LANES, LANES)]
        for m in range(5):
            for j in range(2):
                moment[pl.ds(SQ_AT[m] + j * TILE, TILE), :] = r.sqm_v[m, :, pl.ds(j * LANES, LANES)]
        moment[pl.ds(GAIN_BASE, 16), :] = jnp.zeros((16, LANES), F32)

    def orthogonalize(self):
        r = self.r
        cur = r.cur
        rows = lax.broadcasted_iota(jnp.int32, (256, 256), 0)
        diagonal = rows == lax.broadcasted_iota(jnp.int32, (256, 256), 1)

        def run(slabs, result, tiles):
            pltpu.make_async_copy(slabs, slabs, r.own_recv.at[0]).wait()
            width = tiles * LANES
            total = jnp.zeros((1, 1), F32)
            for j in range(tiles):
                part = slabs[:, pl.ds(j * TILE, TILE), :].astype(F32).reshape(256, LANES)
                cur[:, pl.ds(j * LANES, LANES)] = part
                total = total + jnp.sum(jnp.sum(part * part, axis=0, keepdims=True), axis=1, keepdims=True)
            scale = 1.0 / (jnp.sqrt(total) + 1e-07)
            cur[:, 0:width] = cur[:, 0:width] * scale
            for shift in SHIFTS:
                low = cur[:, 0:width].astype(BF16)
                off = dot(low, low, NT) - jnp.where(diagonal, shift, 0.0)
                off_low = off.astype(BF16)
                poly = (COEF_B + 2.0 * COEF_C * shift) * off + COEF_C * dot(off_low, off_low)
                poly = poly.astype(BF16)
                keep = COEF_A + shift * (COEF_B + COEF_C * shift)
                for j in range(0, tiles, 2):
                    columns = pl.ds(j * LANES, 2 * LANES)
                    now = cur[:, columns]
                    cur[:, columns] = keep * now + dot(poly, now.astype(BF16))
            for j in range(tiles):
                part = cur[:, pl.ds(j * LANES, LANES)]
                result[:, pl.ds(j * TILE, TILE), :] = part.reshape(32, TILE, LANES).astype(result.dtype)

        mine_mlp = jnp.logical_or(self.me == OWNERS[0], self.me == OWNERS[1])
        mine_sq = self.me < 0
        for device in OWNERS[2:]:
            mine_sq = jnp.logical_or(mine_sq, self.me == device)

        @pl.when(mine_mlp)
        def _():
            run(r.slabs_mlp, r.result_mlp, 8)

        @pl.when(mine_sq)
        def _():
            run(r.slabs_sq, r.result_sq, 2)

    def landing(self, index):
        if index < 2:
            return self.r.back_mlp.at[index]
        return self.r.out.at[2, pl.ds(SQ_AT[index - 2], SQ_ROWS)]

    def give_back(self, index, device):
        _, _, result = self.slab(index)
        return link(
            result.at[device], self.landing(index),
            self.r.back_send.at[device], self.r.back_recv.at[index], device,
        )

    def give_all(self):
        r = self.r
        for index in range(7):
            _, _, result = self.slab(index)

            @pl.when(self.me == OWNERS[index])
            def _():
                def send_one(step, _):
                    self.give_back(index, (self.me + step) % 32).start()
                    return 0

                lax.fori_loop(1, 32, send_one, 0)
                pltpu.make_async_copy(result.at[self.me], self.landing(index), r.back_recv.at[index]).start()

    def take_all(self):
        for index in range(7):
            _, _, result = self.slab(index)
            pltpu.make_async_copy(result.at[0], self.landing(index), self.r.back_recv.at[index]).wait()
        for index in range(2):
            rows = pl.ds(index * MLP_ROWS, MLP_ROWS)
            self.r.out[2, rows, :] = self.r.back_mlp[index].astype(F32)

    def drain(self):
        for index in range(7):

            @pl.when(self.me != OWNERS[index])
            def _():
                self.to_owner(index).wait_send()

            @pl.when(self.me == OWNERS[index])
            def _():
                def wait_one(step, _):
                    self.give_back(index, (self.me + step) % 32).wait_send()
                    return 0

                lax.fori_loop(1, 32, wait_one, 0)

        for k in range(len(CHUNKS)):
            self.core(k).wait_send()
            self.plane(k, True).wait_send()
            self.plane(k, False).wait_send()
            for step in range(3):
                self.along_z(k, step).wait_send()


def greet_all():
    me, z, y, x, c = place()
    greet(device_at(z, y, x, 1 - c))
    greet(device_at(z, y, 1 - x, c))
    greet(device_at(z, 1 - y, x, c))
    for step in range(1, 4):
        greet(device_at((z + step) % 4, y, x, c))
    owner = me < 0
    for device in OWNERS:
        owner = jnp.logical_or(owner, me == device)

        @pl.when(me != device)
        def _():
            greet(device)

    @pl.when(owner)
    def _():
        def greet_other(step, _):
            greet((me + step) % 32)
            return 0

        lax.fori_loop(1, 32, greet_other, 0)

    is_owner = owner.astype(jnp.int32)
    return 6 + 7 - is_owner + 31 * is_owner


def block_kernel(names, remote, *args):
    r = Refs(zip(names, args))
    keys, samples = r.obs.shape[0], r.obs.shape[1]
    tokens, width = r.acts.shape
    head_dim, half, per = width // HEADS, width // 2, ROWS // ACT
    wide = r.mlp_all.shape[2]
    groups = samples // GROUP
    in_sems, out_sems = r.in_sems, r.out_sems

    if remote:
        own = (r.sqw_v, r.mlpw_v, r.gain_v)
    else:
        own = (r.sq_all, r.mlp_all, r.gain_all)
    loads = list(zip((r.sqw, r.mlpw, r.gain), own))
    loads += [(r.acts, r.acts_v), (r.obs, r.obs_v.at[pl.ds(0, keys)]), (r.cot, r.cot_v)]
    if remote:
        loads += [(r.sqm, r.sqm_v), (r.mlpm, r.mlpm_v)]
    copies = [pltpu.make_async_copy(a, b, in_sems.at[i]) for i, (a, b) in enumerate(loads)]

    def arrive(*which):
        for i in which:
            copies[i].wait()

    for copy in copies:
        copy.start()
    if remote:
        gather, update = Gather(r), Update(r)
        expected = greet_all()
        arrive(0, 1, 2)
        gather.fill()
        pl.semaphore_wait(pltpu.get_barrier_semaphore(), expected)
        gather.first(3, 4, 2)

    arrive(3)

    def hats(i, _):
        rows = pl.ds(pl.multiple_of(i * ROWS, ROWS), ROWS)
        hat, scale = normalize(r.acts_v[rows, :])
        r.xhat[rows, :] = hat
        r.rstd[rows, :] = scale
        return 0

    lax.fori_loop(0, tokens // ROWS, hats, 0)

    mem, obs_v = r.mem, r.obs_v
    batch = 16
    chunks = KEYS_PAD // batch
    swap = r.swap
    row = lax.broadcasted_iota(jnp.int32, swap.shape, 0)
    column = lax.broadcasted_iota(jnp.int32, swap.shape, 1)
    swap[...] = jnp.where(column == (row % batch) * batch + row // batch, 1.0, 0.0).astype(BF16)

    def turn(part, low, high):
        def one(j, _):
            at = pl.ds(pl.multiple_of(j * batch, batch), batch)
            here = pl.ds(part * batch, batch)
            block = obs_v[at, here, :].reshape(batch * batch, width)
            mem[here, at, :] = dot(swap[...], block).astype(BF16).reshape(batch, batch, width)
            return 0

        lax.fori_loop(low, high, one, 0)

    whole = chunks - 1
    arrive(4)
    turn(0, 0, whole // 2)
    if remote:
        gather.second(3, 4, 2)
        gather.first(0, 1)
    turn(0, whole // 2, whole)
    if remote:
        gather.third(3, 4, 2)
    turn(1, 0, whole // 2)
    if remote:
        gather.second(0, 1)
        gather.fourth(3, 4, 2)
    turn(1, whole // 2, whole)
    freqs = jnp.exp(
        lax.broadcasted_iota(jnp.int32, (1, half), 1).astype(F32) * F32(-math.log(10000.0)) / half
    )
    for s in range(samples):
        r.angle[s : s + 1, :] = r.levels[s].astype(F32) * freqs
    r.embed[:, 0:half] = jnp.sin(r.angle[...]).astype(BF16)
    r.embed[:, half:width] = jnp.cos(r.angle[...]).astype(BF16)
    if remote:
        arrive(6, 7)
        update.old_moment()
        gather.third(0, 1)
        gather.last(3, 4, 2)
        for m in range(5):
            gather.unpack(SQ_AT[m], 1, r.sq_all, m)
        gather.unpack_gains()
    else:
        arrive(0, 1, 2)

    sq, mlp = r.sq_all, r.mlp_all
    wkh, wvh = r.wkh, r.wvh
    lane = lax.broadcasted_iota(jnp.int32, (width, width), 1)
    for h in range(HEADS):
        inside = lane // head_dim == h
        block = pl.ds(h * width, width)
        wkh[block, :] = jnp.where(inside, sq[2].astype(F32), 0.0).astype(BF16)
        wvh[block, :] = jnp.where(inside, sq[3].astype(F32), 0.0).astype(BF16)
    g1, g2 = r.gain_all[0:1, :], r.gain_all[1:2, :]

    obs_v[keys] = dot(r.embed[...], sq[0]).astype(BF16)
    obs_v[keys + 1 :] = jnp.zeros((KEYS_PAD - keys - 1, samples, width), BF16)
    for part in range(samples // batch):
        turn(part, whole, chunks)

    sides, weights = r.sides_v, r.pds_v

    def make_queries(i, _):
        rows = pl.ds(pl.multiple_of(i * ROWS, ROWS), ROWS)
        first = (r.xhat[rows, :] * g1).astype(BF16)
        r.first[rows, :] = first
        q = dot(first, sq[1]).astype(BF16)
        r.query[rows, :] = q
        here = pl.ds(i * per, per)
        for h in range(HEADS):
            wk = wkh[pl.ds(h * width, width), :]
            value = (dot(q, wk, NT) * 0.125).astype(BF16).reshape(per, ACT, width)
            sides[here, pl.ds((HEADS + h) * ACT, ACT), :] = value
        return 0

    lax.fori_loop(0, tokens // ROWS, make_queries, 0)

    key = lax.broadcasted_iota(jnp.int32, (HEADS * ACT, KEYS_PAD), 1)
    low_rows, high_rows = pl.ds(0, HEADS * ACT), pl.ds(HEADS * ACT, HEADS * ACT)

    def attend(g, _):
        ids = [g * GROUP + k for k in range(GROUP)]
        scores = [dot(sides[s, high_rows, :], mem[s], NT) for s in ids]
        lows = []
        for s, score in zip(ids, scores):
            count = OBS_FEW + (OBS_FULL - OBS_FEW) * r.flags[s]
            score = jnp.where((key < count) | (key == OBS_FULL), score, -1000000000.0)
            expo = jnp.exp(score - jnp.max(score, -1, keepdims=True))
            probs = expo * (1.0 / jnp.sum(expo, -1, keepdims=True))
            r.probs[s] = probs
            low = probs.astype(BF16)
            weights[s, low_rows, :] = low
            lows.append(low)
        for s, low in zip(ids, lows):
            u = dot(low, mem[s]).astype(BF16)
            rows = pl.ds(pl.multiple_of(s * ACT, ACT), ACT)
            for h in range(HEADS):
                r.u[rows, pl.ds(h * width, width)] = u[h * ACT : (h + 1) * ACT, :]
        return 0

    lax.fori_loop(0, groups // 2, attend, 0)
    if remote:
        gather.fourth(0, 1)
    lax.fori_loop(groups // 2, groups, attend, 0)
    if remote:
        gather.last(0, 1)
        for m in range(2):
            gather.unpack(m * MLP_ROWS, 4, mlp, m)

    gain_acc = r.gain_acc
    gain_acc[...] = jnp.zeros_like(gain_acc)
    arrive(5)

    def feed(i, _):
        rows = pl.ds(pl.multiple_of(i * ROWS, ROWS), ROWS)
        mixed = dot(r.u[rows, :], wvh[...]).astype(BF16)
        r.mixed[rows, :] = mixed
        resid = r.acts_v[rows, :] + dot(mixed, sq[4])
        hat, scale = normalize(resid)
        second = (hat * g2).astype(BF16)
        r.second[rows, :] = second
        cot = r.cot_v[rows, :]
        out_low = cot.astype(BF16)
        r.out_low[rows, :] = out_low
        for c in range(wide // 256):
            columns = pl.ds(c * 256, 256)
            v = dot(second, mlp[0, :, columns])
            square = v * v
            t = jnp.tanh(0.7978845608 * (v + 0.044715 * square * v))
            r.active[rows, columns] = (0.5 * v * (1.0 + t)).astype(BF16)
            slope = 0.5 * (1.0 + t) + 0.5 * v * (1.0 - t * t) * (0.7978845608 * (1.0 + 0.134145 * square))
            r.dhidden[rows, columns] = (slope * dot(out_low, mlp[1, :, columns])).astype(BF16)
        r.out_v[rows, :] = resid + dot(r.active[rows, :], mlp[1], NT)
        grad_second = dot(r.dhidden[rows, :], mlp[0], NT)
        gain_acc[1:2, :] += jnp.sum(grad_second * hat, 0, keepdims=True)
        dres = cot + norm_back(grad_second * g2, hat, scale)
        r.dres[rows, :] = dres
        low = dres.astype(BF16)
        r.dres_low[rows, :] = low
        gm = dot(low, sq[4], NT).astype(BF16)
        r.dmixed[rows, :] = gm
        here = pl.ds(i * per, per)
        for h in range(HEADS):
            wv = wvh[pl.ds(h * width, width), :]
            sides[here, pl.ds(h * ACT, ACT), :] = dot(gm, wv, NT).astype(BF16).reshape(per, ACT, width)
        return 0

    lax.fori_loop(0, tokens // ROWS, feed, 0)
    keep_out = pltpu.make_async_copy(r.out_v, r.output, out_sems.at[0])
    keep_out.start()

    grads = r.grads

    def put(base, tiles, value):
        for j in range(tiles):
            part = value[:, j * LANES : (j + 1) * LANES].reshape(GRID + (TILE, LANES))
            grads[:, :, :, :, pl.ds(base + j * TILE, TILE), :] = part

    def by_head(left, right):
        turned = left.T
        parts = [
            dot(turned[h * head_dim : (h + 1) * head_dim, :], right[:, pl.ds(h * width, width)])
            for h in range(HEADS)
        ]
        return jnp.concatenate(parts, axis=0).T

    put(0, 8, dot(r.second[...], r.dhidden[...], TN))
    if remote:
        update.start(0)
    put(MLP_ROWS, 8, dot(r.out_low[...], r.active[...], TN))
    if remote:
        update.start(1)
    put(SQ_AT[4], 2, dot(r.mixed[...], r.dres_low[...], TN))
    put(SQ_AT[3], 2, by_head(r.dmixed[...], r.u))
    if remote:
        update.start(2)

    def attend_back(g, _):
        ids = [g * GROUP + k for k in range(GROUP)]
        rises = [dot(sides[s, low_rows, :], mem[s], NT) for s in ids]
        for s, rise in zip(ids, rises):
            probs = r.probs[s]
            both = probs * rise
            weights[s, high_rows, :] = (both - probs * jnp.sum(both, -1, keepdims=True)).astype(BF16)
        for s in ids:
            dq = (dot(weights[s, high_rows, :], mem[s]) * 0.125).astype(BF16)
            rows = pl.ds(pl.multiple_of(s * ACT, ACT), ACT)
            for h in range(HEADS):
                r.dq_wide[rows, pl.ds(h * width, width)] = dq[h * ACT : (h + 1) * ACT, :]
            end = dot(weights[s, :, LANES:KEYS_PAD], sides[s], TN)
            r.stamps[s] = end[64:72, :]
        return 0

    quarter = groups // 4
    lax.fori_loop(0, quarter, attend_back, 0)
    if remote:
        update.one(0, 1)
    lax.fori_loop(quarter, 2 * quarter, attend_back, 0)
    if remote:
        update.two(0, 1)
        update.one(2)
    lax.fori_loop(2 * quarter, 3 * quarter, attend_back, 0)
    if remote:
        update.three(0, 1)
        update.two(2)
    lax.fori_loop(3 * quarter, groups, attend_back, 0)

    def memory_back(low, high):
        def one(g, _):
            for k in range(GROUP):
                s = g * GROUP + k
                mem[s] = dot(weights[s], sides[s], TN).astype(BF16)
            return 0

        lax.fori_loop(low, high, one, 0)

    def turn_back(part):
        def one(j, _):
            at = pl.ds(pl.multiple_of(j * batch, batch), batch)
            here = pl.ds(part * batch, batch)
            block = mem[here, at, :].reshape(batch * batch, width)
            obs_v[at, here, :] = dot(swap[...], block).astype(BF16).reshape(batch, batch, width)
            return 0

        lax.fori_loop(0, chunks, one, 0)

    def queries_back(i, _):
        rows = pl.ds(pl.multiple_of(i * ROWS, ROWS), ROWS)
        r.dquery[rows, :] = dot(r.dq_wide[rows, :], wkh[...]).astype(BF16)
        return 0

    lax.fori_loop(0, tokens // ROWS, queries_back, 0)
    put(SQ_AT[1], 2, dot(r.first[...], r.dquery[...], TN))
    stamp_low = r.stamps[:, 4:5, :].reshape(samples, width).astype(BF16)
    put(SQ_AT[0], 2, dot(r.embed[...], stamp_low, TN))
    if remote:
        update.start(3)

    def acts_back(i, _):
        rows = pl.ds(pl.multiple_of(i * ROWS, ROWS), ROWS)
        grad_first = dot(r.dquery[rows, :], sq[1], NT)
        hat = r.xhat[rows, :]
        gain_acc[0:1, :] += jnp.sum(grad_first * hat, 0, keepdims=True)
        r.ag_v[rows, :] = r.dres[rows, :] + norm_back(grad_first * g1, hat, r.rstd[rows, :])
        return 0

    lax.fori_loop(0, tokens // ROWS, acts_back, 0)
    put(SQ_AT[2], 2, by_head(r.query[...], r.dq_wide))
    for norm in range(2):
        for j in range(2):
            row = gain_acc[norm : norm + 1, j * LANES : (j + 1) * LANES]
            at = GAIN_BASE + norm * 2 + j
            value = jnp.broadcast_to(row.reshape(1, 1, 1, 1, 1, LANES), GRID + (1, LANES))
            grads[:, :, :, :, at : at + 1, :] = value
    rest = WIRE - GAIN_BASE - 4
    grads[:, :, :, :, GAIN_BASE + 4 : WIRE, :] = jnp.zeros(GRID + (rest, LANES), F32)
    keep_ag = pltpu.make_async_copy(r.ag_v, r.ag, out_sems.at[2])
    keep_ag.start()
    keep_og = pltpu.make_async_copy(obs_v.at[pl.ds(0, keys)], r.og, out_sems.at[1])
    half_groups = groups // 2
    if remote:
        update.start(4)
        update.three(2)
        update.four(0, 1)
        memory_back(0, half_groups)
        update.one(3, 4)
        update.four(2)
        turn_back(0)
        update.two(3, 4)
        memory_back(half_groups, groups)
        update.three(3, 4)
        turn_back(1)
        keep_og.start()
        update.four(3, 4)
        update.orthogonalize()
        update.give_all()
        out = r.out
        out[1, :, :] = r.moment[...]
        out[2, pl.ds(GAIN_BASE, 16), :] = jnp.zeros((16, LANES), F32)
        update.take_all()
        gather.drain()
        update.drain()
    else:
        memory_back(0, groups)
        for part in range(samples // batch):
            turn_back(part)
        keep_og.start()
    for copy in (keep_out, keep_og, keep_ag):
        copy.wait()


def block_and_back(remote, acts, obs, flags, levels, cot, sqw, mlpw, gain, sqm=None, mlpm=None):
    tokens, width = acts.shape
    keys, samples = obs.shape[0], obs.shape[1]
    rows = HEADS * ACT
    wide = mlpw.shape[2]
    any_space = pl.BlockSpec(memory_space=pl.ANY)
    in_vmem = pl.BlockSpec(memory_space=VMEM)
    scalars = pl.BlockSpec(memory_space=pltpu.SMEM)
    sem = pltpu.SemaphoreType.DMA
    ins = dict(flags=flags, levels=levels, acts=acts, obs=obs, cot=cot, sqw=sqw, mlpw=mlpw, gain=gain)
    outs = dict(
        output=jax.ShapeDtypeStruct(acts.shape, F32),
        ag=jax.ShapeDtypeStruct(acts.shape, F32),
        og=jax.ShapeDtypeStruct(obs.shape, BF16),
    )
    grads = GRID + (WIRE, LANES)
    scratch = dict(
        obs_v=VMEM((KEYS_PAD, samples, width), BF16),
        acts_v=VMEM(acts.shape, F32),
        cot_v=VMEM(acts.shape, F32),
        mem=VMEM((samples, KEYS_PAD, width), BF16),
        swap=VMEM((256, 256), BF16),
        sq_all=VMEM((5, width, width), BF16),
        mlp_all=VMEM((2, width, wide), BF16),
        gain_all=VMEM((2, width), F32),
        wkh=VMEM((HEADS * width, width), BF16),
        wvh=VMEM((HEADS * width, width), BF16),
        first=VMEM((tokens, width), BF16),
        query=VMEM((tokens, width), BF16),
        xhat=VMEM((tokens, width), F32),
        rstd=VMEM((tokens, 1), F32),
        probs=VMEM((samples, rows, KEYS_PAD), F32),
        pds_v=VMEM((samples, 2 * rows, KEYS_PAD), BF16),
        sides_v=VMEM((samples, 2 * rows, width), BF16),
        u=VMEM((tokens, HEADS * width), BF16),
        dq_wide=VMEM((tokens, HEADS * width), BF16),
        mixed=VMEM((tokens, width), BF16),
        second=VMEM((tokens, width), BF16),
        active=VMEM((tokens, wide), BF16),
        dhidden=VMEM((tokens, wide), BF16),
        out_low=VMEM((tokens, width), BF16),
        dres_low=VMEM((tokens, width), BF16),
        dres=VMEM((tokens, width), F32),
        dmixed=VMEM((tokens, width), BF16),
        dquery=VMEM((tokens, width), BF16),
        out_v=VMEM((tokens, width), F32),
        ag_v=VMEM((tokens, width), F32),
        angle=VMEM((samples, width // 2), F32),
        embed=VMEM((samples, width), BF16),
        stamps=VMEM((samples, 8, width), F32),
        gain_acc=VMEM((8, width), F32),
        in_sems=sem((8,)),
        out_sems=sem((3,)),
    )
    extra = {}
    if remote:
        ins.update(sqm=sqm, mlpm=mlpm)
        outs.update(out=jax.ShapeDtypeStruct((3, WIRE, LANES), F32))
        chunks = len(CHUNKS)
        scratch.update(
            grads=VMEM(grads, F32),
            sqw_v=VMEM(sqw.shape, F32),
            mlpw_v=VMEM(mlpw.shape, F32),
            gain_v=VMEM(gain.shape, F32),
            sqm_v=VMEM(sqm.shape, F32),
            mlpm_v=VMEM(mlpm.shape, F32),
            wire=VMEM(grads, BF16),
            edge=VMEM((16, LANES), F32),
            gsend=sem((chunks, 6)),
            grecv=sem((chunks, 6)),
            send0=VMEM((4, 2, 2, WIRE, LANES), BF16),
            got_core=VMEM((4, 2, 2, WIRE, LANES), BF16),
            sum1=VMEM((4, 2, 2, WIRE, LANES), F32),
            send1=VMEM((4, 2, WIRE, LANES), BF16),
            got1=VMEM((4, 2, WIRE, LANES), BF16),
            sum2=VMEM((4, 2, WIRE, LANES), F32),
            send2=VMEM((4, WIRE, LANES), BF16),
            got2=VMEM((4, WIRE, LANES), BF16),
            sum3=VMEM((4, WIRE, LANES), F32),
            send3=VMEM((3, WIRE, LANES), BF16),
            got3=VMEM((3, WIRE, LANES), BF16),
            moment=VMEM((WIRE, LANES), F32),
            slabs_sq=VMEM((32, SQ_ROWS, LANES), F32),
            slabs_mlp=VMEM((32, MLP_ROWS, LANES), BF16),
            moment_low=VMEM((2 * MLP_ROWS, LANES), BF16),
            back_mlp=VMEM((2, MLP_ROWS, LANES), BF16),
            result_sq=VMEM((32, SQ_ROWS, LANES), F32),
            result_mlp=VMEM((32, MLP_ROWS, LANES), BF16),
            cur=VMEM((width, wide), F32),
            send=sem((chunks, 6)),
            recv=sem((chunks, 6)),
            own_send=sem((7,)),
            own_recv=sem((1,)),
            back_send=sem((32,)),
            back_recv=sem((7,)),
        )
        extra = dict(collective_id=0, has_side_effects=True)
    else:
        outs.update(grads=jax.ShapeDtypeStruct(grads, F32))
    names = tuple(ins) + tuple(outs) + tuple(scratch)
    results = pl.pallas_call(
        functools.partial(block_kernel, names, remote),
        out_shape=tuple(outs.values()),
        in_specs=[scalars] * 2 + [any_space] * (len(ins) - 2),
        out_specs=[any_space] * 3 + [in_vmem],
        scratch_shapes=list(scratch.values()),
        compiler_params=pltpu.CompilerParams(vmem_limit_bytes=56 << 20, **extra),
        name="block_and_back",
    )(*ins.values())
    return Refs(zip(outs, results))


PARTS = 7


def finish_kernel(names, rate, *args):
    r = Refs(zip(names, args))
    sems = r.sems
    keys = r.og.shape[0]
    step = keys // PARTS

    def come(part):
        block = pl.ds(part * step, step)
        return pltpu.make_async_copy(r.low.at[block], r.low_v.at[block], sems.at[2 * part])

    def leave(part):
        block = pl.ds(part * step, step)
        return pltpu.make_async_copy(r.og_v.at[block], r.og.at[block], sems.at[2 * part + 1])

    for part in range(PARTS):
        come(part).start()
    more = 2 * PARTS
    small, passes = [], []
    if hasattr(r, "wire"):
        pairs = [(r.output, r.output_v), (r.ag, r.ag_v), (r.wire, r.wire_v), (r.sqw, r.sqw_v)]
        pairs += [(r.mlpw, r.mlpw_v), (r.gain, r.gain_v), (r.gainm, r.gainm_v)]
        for source, target in pairs:
            small.append(pltpu.make_async_copy(source, target, sems.at[more]))
            small[-1].start()
            more += 1
        for source, target in ((r.output_v, r.output_f), (r.ag_v, r.ag_f)):
            passes.append(pltpu.make_async_copy(source, target, sems.at[more]))
            more += 1
    for part in range(PARTS):
        come(part).wait()

        def widen(j, _):
            r.og_v[j] = r.low_v[j].astype(F32)
            return 0

        lax.fori_loop(part * step, (part + 1) * step, widen, 0, unroll=4)
        leave(part).start()
    for copy in small[:2]:
        copy.wait()
    for copy in passes:
        copy.start()
    if hasattr(r, "wire"):
        for copy in small[2:]:
            copy.wait()
        finish_weights(r, rate)
    for part in range(PARTS):
        leave(part).wait()
    for copy in passes:
        copy.wait()


def finish_weights(r, rate):
    wire = r.wire_v
    me = lax.axis_index("dp")
    for m in range(5):
        for j in range(2):
            rows, columns = pl.ds(SQ_AT[m] + j * TILE, TILE), pl.ds(j * LANES, LANES)
            r.sqg[m, :, columns] = wire[0, rows, :]
            r.sqm[m, :, columns] = wire[1, rows, :]
            r.sqn[m, :, columns] = r.sqw_v[m, :, columns] - SQ_RATES[m] * wire[2, rows, :]
    r.sqc[...] = r.sqn[...].astype(BF16)
    for m in range(2):
        for j in range(8):
            rows, columns = pl.ds(m * MLP_ROWS + j * TILE, TILE), pl.ds(j * LANES, LANES)
            r.mlpg[m, :, columns] = wire[0, rows, :]
            r.mlpm[m, :, columns] = wire[1, rows, :]
            r.mlpn[m, :, columns] = r.mlpw_v[m, :, columns] - MLP_RATES[m] * wire[2, rows, :]
    r.mlpc[...] = r.mlpn[...].astype(BF16)
    tile = wire[0, pl.ds(GAIN_BASE, TILE), :]
    turned = pltpu.roll(tile, (LANES - (me % 16) * TILE) % LANES, 1)
    at = me // 16
    for norm in range(2):
        pair = turned[2 * norm : 2 * norm + 2, 0:TILE]
        row = jnp.where(at == 0, pair[0:1, :], pair[1:2, :])
        new = 0.5 * r.gainm_v[norm : norm + 1, :] + row
        r.gg[norm : norm + 1, :] = row
        r.gm[norm : norm + 1, :] = new
        r.gn[norm : norm + 1, :] = r.gain_v[norm : norm + 1, :] - rate * new


def finish(rate, made, sqw=None, mlpw=None, gain=None, gainm=None):
    any_space = pl.BlockSpec(memory_space=pl.ANY)
    in_vmem = pl.BlockSpec(memory_space=VMEM)
    ins = dict(low=made.og)
    outs = dict(og=jax.ShapeDtypeStruct(made.og.shape, F32))
    far = 1
    if hasattr(made, "out"):
        ins.update(output=made.output, ag=made.ag, wire=made.out, sqw=sqw, mlpw=mlpw, gain=gain, gainm=gainm)
        like = jax.ShapeDtypeStruct
        far = 3
        outs.update(
            output_f=like(made.output.shape, F32),
            ag_f=like(made.ag.shape, F32),
            sqg=like(sqw.shape, F32),
            sqm=like(sqw.shape, F32),
            sqn=like(sqw.shape, F32),
            sqc=like(sqw.shape, BF16),
            mlpg=like(mlpw.shape, F32),
            mlpm=like(mlpw.shape, F32),
            mlpn=like(mlpw.shape, F32),
            mlpc=like(mlpw.shape, BF16),
            gg=like(gain.shape, F32),
            gm=like(gain.shape, F32),
            gn=like(gain.shape, F32),
        )
    scratch = dict(
        low_v=VMEM(made.og.shape, BF16),
        og_v=VMEM(made.og.shape, F32),
        sems=pltpu.SemaphoreType.DMA((2 * PARTS + 9,)),
    )
    if hasattr(made, "out"):
        scratch.update(
            output_v=VMEM(made.output.shape, F32),
            ag_v=VMEM(made.ag.shape, F32),
            wire_v=VMEM(made.out.shape, F32),
            sqw_v=VMEM(sqw.shape, F32),
            mlpw_v=VMEM(mlpw.shape, F32),
            gain_v=VMEM(gain.shape, F32),
            gainm_v=VMEM(gainm.shape, F32),
        )
    names = tuple(ins) + tuple(outs) + tuple(scratch)
    results = pl.pallas_call(
        functools.partial(finish_kernel, names, rate),
        out_shape=tuple(outs.values()),
        in_specs=[any_space] * len(ins),
        out_specs=[any_space] * far + [in_vmem] * (len(outs) - far),
        scratch_shapes=list(scratch.values()),
        compiler_params=pltpu.CompilerParams(vmem_limit_bytes=60 << 20),
        name="finish",
    )(*ins.values())
    return Refs(zip(outs, results))


HIGH_PRECISION = lax.Precision.HIGHEST


def plain_orthogonalize(matrix):
    current = matrix / (jnp.sqrt(jnp.sum(matrix * matrix)) + 1e-07)
    for turn in range(5):
        gram = jnp.dot(current, current.T, precision=HIGH_PRECISION)
        poly = COEF_B * gram + COEF_C * jnp.dot(gram, gram, precision=HIGH_PRECISION)
        current = COEF_A * current + jnp.dot(poly, current, precision=HIGH_PRECISION)
    return current


def pick_owned(stack, owners, device):
    chosen = jnp.zeros_like(stack[0])
    for index in range(len(owners)):
        chosen = jnp.where(device == owners[index], stack[index], chosen)
    return chosen


def is_owner(owners, device):
    flag = device < 0
    for owner in owners:
        flag = jnp.logical_or(flag, device == owner)
    return flag


def from_wire(grads):
    def matrix(base, tiles):
        part = grads[:, base : base + tiles * TILE, :].reshape(-1, tiles, TILE, LANES)
        return part.transpose(0, 2, 1, 3).reshape(-1, tiles * LANES)

    square = jnp.stack([matrix(SQ_AT[m], 2) for m in range(5)])
    mlp = jnp.stack([matrix(m * MLP_ROWS, 8) for m in range(2)])
    return square, mlp, grads[0, GAIN_BASE : GAIN_BASE + 4, :].reshape(2, 2 * LANES)


def update_by_collectives(
    grads, square_weights, mlp_weights, gains, square_moment, mlp_moment, gain_moment, rate
):
    square_local, mlp_local, gain_local = from_wire(grads)
    square_grad, mlp_grad, gain_grad = (
        lax.psum_scatter(square_local, "dp", scatter_dimension=1, tiled=True),
        lax.psum_scatter(mlp_local, "dp", scatter_dimension=1, tiled=True),
        lax.psum_scatter(gain_local, "dp", scatter_dimension=1, tiled=True),
    )
    square_moment_new = 0.5 * square_moment + square_grad
    mlp_moment_new = 0.5 * mlp_moment + mlp_grad
    gain_moment_new = 0.5 * gain_moment + gain_grad
    device = lax.axis_index("dp")
    count = lax.axis_size("dp")
    square_owners = [index * count // 7 for index in range(5)]
    mlp_owners = [(index + 5) * count // 7 for index in range(2)]
    square_full, mlp_full = (
        lax.all_gather(square_moment_new, "dp", axis=1, tiled=True),
        lax.all_gather(mlp_moment_new, "dp", axis=1, tiled=True),
    )
    mine_square = pick_owned(square_full, square_owners, device)
    mine_mlp = pick_owned(mlp_full, mlp_owners, device)
    made_square = lax.cond(
        is_owner(square_owners, device), plain_orthogonalize, jnp.zeros_like, mine_square
    )
    made_mlp = lax.cond(is_owner(mlp_owners, device), plain_orthogonalize, jnp.zeros_like, mine_mlp)
    stack_square = jnp.stack(
        [jnp.where(device == owner, made_square, 0.0) for owner in square_owners]
    )
    stack_mlp = jnp.stack([jnp.where(device == owner, made_mlp, 0.0) for owner in mlp_owners])
    square_ortho, mlp_ortho = (
        lax.psum_scatter(stack_square, "dp", scatter_dimension=1, tiled=True),
        lax.psum_scatter(stack_mlp, "dp", scatter_dimension=1, tiled=True),
    )
    square_new = square_weights - jnp.array(SQ_RATES, F32)[:, None, None] * square_ortho
    mlp_new = mlp_weights - jnp.array(MLP_RATES, F32)[:, None, None] * mlp_ortho
    gains_new = gains - rate * gain_moment_new
    return (
        square_grad,
        square_moment_new,
        square_new,
        square_new.astype(BF16),
        mlp_grad,
        mlp_moment_new,
        mlp_new,
        mlp_new.astype(BF16),
        gain_grad,
        gain_moment_new,
        gains_new,
    )


def per_device(
    actions,
    observed,
    camera_flags,
    noise_levels,
    cotangent,
    square_weights,
    mlp_weights,
    gains,
    square_moment,
    mlp_moment,
    gain_moment,
):
    count = lax.axis_size("dp")
    rate = 0.1 / math.sqrt(actions.shape[0] * count)
    by_key = observed.transpose(1, 0, 2)
    ins = (actions, by_key, camera_flags, noise_levels, cotangent)
    if count == math.prod(GRID):
        made = block_and_back(True, *ins, square_weights, mlp_weights, gains, square_moment, mlp_moment)
        done = finish(rate, made, square_weights, mlp_weights, gains, gain_moment)
        output, actions_grad = done.output_f, done.ag_f
        d = done
        rest = (d.sqg, d.sqm, d.sqn, d.sqc, d.mlpg, d.mlpm, d.mlpn, d.mlpc, d.gg, d.gm, d.gn)
    else:
        square_all, mlp_all = (
            lax.all_gather(square_weights.astype(BF16), "dp", axis=1, tiled=True),
            lax.all_gather(mlp_weights.astype(BF16), "dp", axis=1, tiled=True),
        )
        gain_all = lax.all_gather(gains, "dp", axis=1, tiled=True)
        made = block_and_back(False, *ins, square_all, mlp_all, gain_all)
        done = finish(rate, made)
        output, actions_grad = made.output, made.ag
        grads = made.grads.reshape(-1, WIRE, LANES)
        rest = update_by_collectives(
            grads, square_weights, mlp_weights, gains, square_moment, mlp_moment, gain_moment, rate
        )
    observed_grad = done.og.transpose(1, 0, 2)
    return (output, actions_grad, observed_grad) + tuple(rest)


def solution(mesh):
    rows, cube, flat = P("dp", None), P("dp", None, None), P("dp")
    stacked, pair = P(None, "dp", None), P(None, "dp")
    return jax.shard_map(
        per_device,
        mesh=mesh,
        in_specs=(rows, cube, flat, flat, rows, stacked, stacked, pair, stacked, stacked, pair),
        out_specs=(rows, rows, cube) + (stacked,) * 8 + (pair,) * 3,
        check_vma=False,
    )
```

```python
import functools
import math

import jax
import jax.numpy as jnp
from jax import lax
from jax.experimental import pallas as pl
from jax.experimental.pallas import tpu as pltpu
from jax.sharding import PartitionSpec as P

HEADS = 4
ACT = 16
OBS_FULL = 196
OBS_FEW = 49
COEF_A = 3.4445
COEF_B = -4.775
COEF_C = 2.0315
F32 = jnp.float32
BF16 = jnp.bfloat16
MESH = pl.DeviceIdType.MESH
VMEM = pltpu.VMEM
NN = (((1,), (0,)), ((), ()))
NT = (((1,), (1,)), ((), ()))
TN = (((0,), (0,)), ((), ()))

LANES = 128
TILE = 8
MLP_ROWS = 64
SQ_ROWS = 16
SQ_AT = (160, 176, 192, 128, 144)
GAIN_BASE = 208
WIRE = 224
CHUNKS = ((0, 64), (64, 64), (128, 32), (160, 32), (192, 32))
X_FIRST = (True, False, True, True, False)
MLP_RATES = (1.0, 0.5)
SQ_RATES = (0.5, 0.5, 0.5, 0.5, 4.0)
GRID = (4, 2, 2, 2)
OWNERS = (8, 22, 14, 16, 11, 21, 13)
SHIFTS = (0.0, 0.0, 0.4, 0.8, 0.8)
KEYS_PAD = 208
GROUP = 8
ROWS = 256


class Refs:
    def __init__(self, pairs):
        self.__dict__.update(pairs)


def dot(left, right, dims=NN):
    return lax.dot_general(left, right, dims, preferred_element_type=F32)


def place():
    me = lax.axis_index("dp")
    return me, me // 8, (me // 4) % 2, (me // 2) % 2, me % 2


def device_at(z, y, x, c):
    return ((z * 2 + y) * 2 + x) * 2 + c


def link(src, dst, send, recv, device):
    return pltpu.make_async_remote_copy(
        src_ref=src,
        dst_ref=dst,
        send_sem=send,
        recv_sem=recv,
        device_id=(device,),
        device_id_type=MESH,
    )


def greet(device):
    pl.semaphore_signal(
        pltpu.get_barrier_semaphore(), inc=1, device_id=(device,), device_id_type=MESH
    )


def normalize(values):
    centred = values - jnp.mean(values, -1, keepdims=True)
    scale = lax.rsqrt(jnp.mean(centred * centred, -1, keepdims=True) + 1e-05)
    return centred * scale, scale


def norm_back(grad, hat, scale):
    mean_one = jnp.mean(grad, -1, keepdims=True)
    mean_two = jnp.mean(grad * hat, -1, keepdims=True)
    return scale * (grad - mean_one - hat * mean_two)


class Gather:
    def __init__(self, r):
        self.r = r
        self.me, self.z, self.y, self.x, self.c = place()

    def hop(self, k, step, part, device):
        return link(part, part, self.r.gsend.at[k, step], self.r.grecv.at[k, step], device)

    def along_z(self, k, step):
        part = self.r.wire.at[self.z, self.y, self.x, self.c, pl.ds(*CHUNKS[k])]
        return self.hop(k, step, part, device_at((self.z + step + 1) % 4, self.y, self.x, self.c))

    def from_z(self, k, step):
        there = (self.z + 3 - step) % 4
        part = self.r.wire.at[there, self.y, self.x, self.c, pl.ds(*CHUNKS[k])]
        return self.hop(k, step, part, device_at(there, self.y, self.x, self.c))

    def plane(self, k, second, mine):
        z, y, x, c = self.z, self.y, self.x, self.c
        rows, wire = pl.ds(*CHUNKS[k]), self.r.wire
        py, px = (y, x) if mine else (1 - y, 1 - x)
        along_x = X_FIRST[k] == second
        if along_x:
            part = wire.at[:, y, px, c, rows] if second else wire.at[:, :, px, c, rows]
            return self.hop(k, 3 if second else 4, part, device_at(z, y, 1 - x, c))
        part = wire.at[:, py, x, c, rows] if second else wire.at[:, py, :, c, rows]
        return self.hop(k, 3 if second else 4, part, device_at(z, 1 - y, x, c))

    def core(self, k, mine):
        part = self.r.wire.at[:, :, :, self.c if mine else 1 - self.c, pl.ds(*CHUNKS[k])]
        return self.hop(k, 5, part, device_at(self.z, self.y, self.x, 1 - self.c))

    def first(self, *chunks):
        for k in chunks:
            for step in range(3):
                self.along_z(k, step).start()

    def second(self, *chunks):
        for k in chunks:
            for step in range(3):
                self.from_z(k, step).wait_recv()
            self.plane(k, True, True).start()

    def third(self, *chunks):
        for k in chunks:
            self.plane(k, True, False).wait_recv()
            self.plane(k, False, True).start()

    def fourth(self, *chunks):
        for k in chunks:
            self.plane(k, False, False).wait_recv()
            self.core(k, True).start()

    def last(self, *chunks):
        for k in chunks:
            self.core(k, False).wait_recv()

    def drain(self):
        for k in range(len(CHUNKS)):
            for step in range(3):
                self.along_z(k, step).wait_send()
            self.plane(k, True, True).wait_send()
            self.plane(k, False, True).wait_send()
            self.core(k, True).wait_send()

    def fill(self):
        r = self.r
        spot = (self.z, self.y, self.x, self.c)

        def tiles(source, m, base, number):
            for j in range(number):
                pair = [source[m, :, pl.ds((2 * j + k) * LANES, LANES)] for k in range(2)]
                r.wire[spot + (pl.ds(base + j * 16, 16),)] = jnp.concatenate(pair, axis=0).astype(BF16)

        for m in range(5):
            tiles(r.sqw_v, m, SQ_AT[m], 1)
        for m in range(2):
            tiles(r.mlpw_v, m, m * MLP_ROWS, 4)
        gains, edge = r.gain_v[...], r.edge
        high = gains.astype(BF16).astype(F32)
        middle = (gains - high).astype(BF16).astype(F32)
        edge[...] = jnp.zeros_like(edge)
        edge[0:2, 0:TILE] = high
        edge[2:4, 0:TILE] = middle
        edge[4:6, 0:TILE] = (gains - high - middle).astype(BF16).astype(F32)
        r.wire[spot + (pl.ds(GAIN_BASE, 16),)] = edge[...].astype(BF16)

    def unpack(self, base, number, out, m):
        for j in range(number):
            block = self.r.wire[:, :, :, :, pl.ds(base + j * 16, 16), :].reshape(32, 16, LANES).astype(F32)
            for half in range(2):
                columns = pl.ds((2 * j + half) * LANES, LANES)
                out[m, :, columns] = block[:, half * 8 : half * 8 + 8, :].reshape(256, LANES).astype(BF16)

    def unpack_gains(self):
        edge, wire = self.r.edge, self.r.wire
        for half in range(2):
            total = jnp.zeros((16, LANES), F32)
            for at in range(16):
                d = half * 16 + at
                tile = wire[d // 8, (d // 4) % 2, (d // 2) % 2, d % 2, pl.ds(GAIN_BASE, 16), :].astype(F32)
                total = total + (tile if at == 0 else pltpu.roll(tile, at * TILE, 1))
            edge[...] = total
            self.r.gain_all[:, pl.ds(half * LANES, LANES)] = edge[0:2, :] + edge[2:4, :] + edge[4:6, :]


class Update:
    def __init__(self, r):
        self.r = r
        self.me, self.z, self.y, self.x, self.c = place()

    def hop(self, k, step, src, dst, device):
        return link(src, dst, self.r.send.at[k, step], self.r.recv.at[k, step], device)

    def core(self, k):
        rows = pl.ds(*CHUNKS[k])
        src, dst = self.r.send0.at[:, :, :, rows], self.r.got_core.at[:, :, :, rows]
        return self.hop(k, 0, src, dst, device_at(self.z, self.y, self.x, 1 - self.c))

    def plane(self, k, first):
        rows = pl.ds(*CHUNKS[k])
        to = (self.z, self.y, 1 - self.x, self.c) if X_FIRST[k] == first else (self.z, 1 - self.y, self.x, self.c)
        if first:
            src, dst = self.r.send1.at[:, :, rows], self.r.got1.at[:, :, rows]
        else:
            src, dst = self.r.send2.at[:, rows], self.r.got2.at[:, rows]
        return self.hop(k, 1 if first else 2, src, dst, device_at(*to))

    def along_z(self, k, step):
        rows = pl.ds(*CHUNKS[k])
        to = device_at((self.z + step + 1) % 4, self.y, self.x, self.c)
        return self.hop(k, 3 + step, self.r.send3.at[step, rows], self.r.got3.at[step, rows], to)

    def start(self, k):
        rows = pl.ds(*CHUNKS[k])
        self.r.send0[:, :, :, rows, :] = self.r.grads[:, :, :, 1 - self.c, rows, :].astype(BF16)
        self.core(k).start()

    def one(self, *chunks):
        r = self.r
        for k in chunks:
            rows = pl.ds(*CHUNKS[k])
            self.core(k).wait_recv()
            sum1 = r.sum1
            sum1[:, :, :, rows, :] = r.grads[:, :, :, self.c, rows, :] + r.got_core[:, :, :, rows, :].astype(F32)
            other = sum1[:, :, 1 - self.x, rows, :] if X_FIRST[k] else sum1[:, 1 - self.y, :, rows, :]
            r.send1[:, :, rows, :] = other.astype(BF16)
            self.plane(k, True).start()

    def two(self, *chunks):
        r = self.r
        for k in chunks:
            rows = pl.ds(*CHUNKS[k])
            self.plane(k, True).wait_recv()
            sum1, sum2 = r.sum1, r.sum2
            mine = sum1[:, :, self.x, rows, :] if X_FIRST[k] else sum1[:, self.y, :, rows, :]
            sum2[:, :, rows, :] = mine + r.got1[:, :, rows, :].astype(F32)
            other = 1 - self.y if X_FIRST[k] else 1 - self.x
            r.send2[:, rows, :] = sum2[:, other, rows, :].astype(BF16)
            self.plane(k, False).start()

    def three(self, *chunks):
        r = self.r
        for k in chunks:
            rows = pl.ds(*CHUNKS[k])
            self.plane(k, False).wait_recv()
            mine = self.y if X_FIRST[k] else self.x
            r.sum3[:, rows, :] = r.sum2[:, mine, rows, :] + r.got2[:, rows, :].astype(F32)
            for step in range(3):
                r.send3[step, rows, :] = r.sum3[(self.z + step + 1) % 4, rows, :].astype(BF16)
                self.along_z(k, step).start()

    def slab(self, index):
        if index < 2:
            return pl.ds(index * MLP_ROWS, MLP_ROWS), self.r.slabs_mlp, self.r.result_mlp
        return pl.ds(SQ_AT[index - 2], SQ_ROWS), self.r.slabs_sq, self.r.result_sq

    def to_owner(self, index):
        rows, slabs, _ = self.slab(index)
        moment = self.r.moment_low if index < 2 else self.r.moment
        return link(
            moment.at[rows], slabs.at[self.me],
            self.r.own_send.at[index], self.r.own_recv.at[0], OWNERS[index],
        )

    def four(self, *chunks):
        r = self.r
        moment, out = r.moment, r.out
        for k in chunks:
            rows = pl.ds(*CHUNKS[k])
            total = r.sum3[self.z, rows, :]
            for step in range(3):
                self.along_z(k, step).wait_recv()
                total = total + r.got3[step, rows, :].astype(F32)
            out[0, rows, :] = total
            new = 0.5 * moment[rows, :] + total
            moment[rows, :] = new
            if k < 2:
                r.moment_low[rows, :] = new.astype(BF16)
            for index in ((0,), (1,), (5, 6), (2, 3), (4,))[k]:
                rows_m, slabs, _ = self.slab(index)

                @pl.when(self.me != OWNERS[index])
                def _():
                    self.to_owner(index).start()

                @pl.when(self.me == OWNERS[index])
                def _():
                    mine = r.moment_low if index < 2 else moment
                    pltpu.make_async_copy(mine.at[rows_m], slabs.at[self.me], r.own_recv.at[0]).start()

    def old_moment(self):
        r = self.r
        moment = r.moment
        for m in range(2):
            for j in range(8):
                moment[pl.ds(m * MLP_ROWS + j * TILE, TILE), :] = r.mlpm_v[m, :, pl.ds(j * LANES, LANES)]
        for m in range(5):
            for j in range(2):
                moment[pl.ds(SQ_AT[m] + j * TILE, TILE), :] = r.sqm_v[m, :, pl.ds(j * LANES, LANES)]
        moment[pl.ds(GAIN_BASE, 16), :] = jnp.zeros((16, LANES), F32)

    def orthogonalize(self):
        r = self.r
        cur = r.cur
        rows = lax.broadcasted_iota(jnp.int32, (256, 256), 0)
        diagonal = rows == lax.broadcasted_iota(jnp.int32, (256, 256), 1)

        def run(slabs, result, tiles):
            pltpu.make_async_copy(slabs, slabs, r.own_recv.at[0]).wait()
            width = tiles * LANES
            total = jnp.zeros((1, 1), F32)
            for j in range(tiles):
                part = slabs[:, pl.ds(j * TILE, TILE), :].astype(F32).reshape(256, LANES)
                cur[:, pl.ds(j * LANES, LANES)] = part
                total = total + jnp.sum(jnp.sum(part * part, axis=0, keepdims=True), axis=1, keepdims=True)
            scale = 1.0 / (jnp.sqrt(total) + 1e-07)
            cur[:, 0:width] = cur[:, 0:width] * scale
            for shift in SHIFTS:
                low = cur[:, 0:width].astype(BF16)
                off = dot(low, low, NT) - jnp.where(diagonal, shift, 0.0)
                off_low = off.astype(BF16)
                poly = (COEF_B + 2.0 * COEF_C * shift) * off + COEF_C * dot(off_low, off_low)
                poly = poly.astype(BF16)
                keep = COEF_A + shift * (COEF_B + COEF_C * shift)
                for j in range(0, tiles, 2):
                    columns = pl.ds(j * LANES, 2 * LANES)
                    now = cur[:, columns]
                    cur[:, columns] = keep * now + dot(poly, now.astype(BF16))
            for j in range(tiles):
                part = cur[:, pl.ds(j * LANES, LANES)]
                result[:, pl.ds(j * TILE, TILE), :] = part.reshape(32, TILE, LANES).astype(result.dtype)

        mine_mlp = jnp.logical_or(self.me == OWNERS[0], self.me == OWNERS[1])
        mine_sq = self.me < 0
        for device in OWNERS[2:]:
            mine_sq = jnp.logical_or(mine_sq, self.me == device)

        @pl.when(mine_mlp)
        def _():
            run(r.slabs_mlp, r.result_mlp, 8)

        @pl.when(mine_sq)
        def _():
            run(r.slabs_sq, r.result_sq, 2)

    def landing(self, index):
        if index < 2:
            return self.r.back_mlp.at[index]
        return self.r.out.at[2, pl.ds(SQ_AT[index - 2], SQ_ROWS)]

    def give_back(self, index, device):
        _, _, result = self.slab(index)
        return link(
            result.at[device], self.landing(index),
            self.r.back_send.at[device], self.r.back_recv.at[index], device,
        )

    def give_all(self):
        r = self.r
        for index in range(7):
            _, _, result = self.slab(index)

            @pl.when(self.me == OWNERS[index])
            def _():
                def send_one(step, _):
                    self.give_back(index, (self.me + step) % 32).start()
                    return 0

                lax.fori_loop(1, 32, send_one, 0)
                pltpu.make_async_copy(result.at[self.me], self.landing(index), r.back_recv.at[index]).start()

    def take_all(self):
        for index in range(7):
            _, _, result = self.slab(index)
            pltpu.make_async_copy(result.at[0], self.landing(index), self.r.back_recv.at[index]).wait()
        for index in range(2):
            rows = pl.ds(index * MLP_ROWS, MLP_ROWS)
            self.r.out[2, rows, :] = self.r.back_mlp[index].astype(F32)

    def drain(self):
        for index in range(7):

            @pl.when(self.me != OWNERS[index])
            def _():
                self.to_owner(index).wait_send()

            @pl.when(self.me == OWNERS[index])
            def _():
                def wait_one(step, _):
                    self.give_back(index, (self.me + step) % 32).wait_send()
                    return 0

                lax.fori_loop(1, 32, wait_one, 0)

        for k in range(len(CHUNKS)):
            self.core(k).wait_send()
            self.plane(k, True).wait_send()
            self.plane(k, False).wait_send()
            for step in range(3):
                self.along_z(k, step).wait_send()


def greet_all():
    me, z, y, x, c = place()
    greet(device_at(z, y, x, 1 - c))
    greet(device_at(z, y, 1 - x, c))
    greet(device_at(z, 1 - y, x, c))
    for step in range(1, 4):
        greet(device_at((z + step) % 4, y, x, c))
    owner = me < 0
    for device in OWNERS:
        owner = jnp.logical_or(owner, me == device)

        @pl.when(me != device)
        def _():
            greet(device)

    @pl.when(owner)
    def _():
        def greet_other(step, _):
            greet((me + step) % 32)
            return 0

        lax.fori_loop(1, 32, greet_other, 0)

    is_owner = owner.astype(jnp.int32)
    return 6 + 7 - is_owner + 31 * is_owner


def block_kernel(names, remote, *args):
    r = Refs(zip(names, args))
    keys, samples = r.obs.shape[0], r.obs.shape[1]
    tokens, width = r.acts.shape
    head_dim, half, per = width // HEADS, width // 2, ROWS // ACT
    wide = r.mlp_all.shape[2]
    groups = samples // GROUP
    in_sems, out_sems = r.in_sems, r.out_sems

    if remote:
        own = (r.sqw_v, r.mlpw_v, r.gain_v)
    else:
        own = (r.sq_all, r.mlp_all, r.gain_all)
    loads = list(zip((r.sqw, r.mlpw, r.gain), own))
    loads += [(r.acts, r.acts_v), (r.obs, r.obs_v.at[pl.ds(0, keys)]), (r.cot, r.cot_v)]
    if remote:
        loads += [(r.sqm, r.sqm_v), (r.mlpm, r.mlpm_v)]
    copies = [pltpu.make_async_copy(a, b, in_sems.at[i]) for i, (a, b) in enumerate(loads)]

    def arrive(*which):
        for i in which:
            copies[i].wait()

    for copy in copies:
        copy.start()
    if remote:
        gather, update = Gather(r), Update(r)
        expected = greet_all()
        arrive(0, 1, 2)
        gather.fill()
        pl.semaphore_wait(pltpu.get_barrier_semaphore(), expected)
        gather.first(3, 4, 2)

    arrive(3)

    def hats(i, _):
        rows = pl.ds(pl.multiple_of(i * ROWS, ROWS), ROWS)
        hat, scale = normalize(r.acts_v[rows, :])
        r.xhat[rows, :] = hat
        r.rstd[rows, :] = scale
        return 0

    lax.fori_loop(0, tokens // ROWS, hats, 0)

    mem, obs_v = r.mem, r.obs_v
    batch = 16
    chunks = KEYS_PAD // batch
    swap = r.swap
    row = lax.broadcasted_iota(jnp.int32, swap.shape, 0)
    column = lax.broadcasted_iota(jnp.int32, swap.shape, 1)
    swap[...] = jnp.where(column == (row % batch) * batch + row // batch, 1.0, 0.0).astype(BF16)

    def turn(part, low, high):
        def one(j, _):
            at = pl.ds(pl.multiple_of(j * batch, batch), batch)
            here = pl.ds(part * batch, batch)
            block = obs_v[at, here, :].reshape(batch * batch, width)
            mem[here, at, :] = dot(swap[...], block).astype(BF16).reshape(batch, batch, width)
            return 0

        lax.fori_loop(low, high, one, 0)

    whole = chunks - 1
    arrive(4)
    turn(0, 0, whole // 2)
    if remote:
        gather.second(3, 4, 2)
        gather.first(0, 1)
    turn(0, whole // 2, whole)
    if remote:
        gather.third(3, 4, 2)
    turn(1, 0, whole // 2)
    if remote:
        gather.second(0, 1)
        gather.fourth(3, 4, 2)
    turn(1, whole // 2, whole)
    freqs = jnp.exp(
        lax.broadcasted_iota(jnp.int32, (1, half), 1).astype(F32) * F32(-math.log(10000.0)) / half
    )
    for s in range(samples):
        r.angle[s : s + 1, :] = r.levels[s].astype(F32) * freqs
    r.embed[:, 0:half] = jnp.sin(r.angle[...]).astype(BF16)
    r.embed[:, half:width] = jnp.cos(r.angle[...]).astype(BF16)
    if remote:
        arrive(6, 7)
        update.old_moment()
        gather.third(0, 1)
        gather.last(3, 4, 2)
        for m in range(5):
            gather.unpack(SQ_AT[m], 1, r.sq_all, m)
        gather.unpack_gains()
    else:
        arrive(0, 1, 2)

    sq, mlp = r.sq_all, r.mlp_all
    wkh, wvh = r.wkh, r.wvh
    lane = lax.broadcasted_iota(jnp.int32, (width, width), 1)
    for h in range(HEADS):
        inside = lane // head_dim == h
        block = pl.ds(h * width, width)
        wkh[block, :] = jnp.where(inside, sq[2].astype(F32), 0.0).astype(BF16)
        wvh[block, :] = jnp.where(inside, sq[3].astype(F32), 0.0).astype(BF16)
    g1, g2 = r.gain_all[0:1, :], r.gain_all[1:2, :]

    obs_v[keys] = dot(r.embed[...], sq[0]).astype(BF16)
    obs_v[keys + 1 :] = jnp.zeros((KEYS_PAD - keys - 1, samples, width), BF16)
    for part in range(samples // batch):
        turn(part, whole, chunks)

    sides, weights = r.sides_v, r.pds_v

    def make_queries(i, _):
        rows = pl.ds(pl.multiple_of(i * ROWS, ROWS), ROWS)
        first = (r.xhat[rows, :] * g1).astype(BF16)
        r.first[rows, :] = first
        q = dot(first, sq[1]).astype(BF16)
        r.query[rows, :] = q
        here = pl.ds(i * per, per)
        for h in range(HEADS):
            wk = wkh[pl.ds(h * width, width), :]
            value = (dot(q, wk, NT) * 0.125).astype(BF16).reshape(per, ACT, width)
            sides[here, pl.ds((HEADS + h) * ACT, ACT), :] = value
        return 0

    lax.fori_loop(0, tokens // ROWS, make_queries, 0)

    key = lax.broadcasted_iota(jnp.int32, (HEADS * ACT, KEYS_PAD), 1)
    low_rows, high_rows = pl.ds(0, HEADS * ACT), pl.ds(HEADS * ACT, HEADS * ACT)

    def attend(g, _):
        ids = [g * GROUP + k for k in range(GROUP)]
        scores = [dot(sides[s, high_rows, :], mem[s], NT) for s in ids]
        lows = []
        for s, score in zip(ids, scores):
            count = OBS_FEW + (OBS_FULL - OBS_FEW) * r.flags[s]
            score = jnp.where((key < count) | (key == OBS_FULL), score, -1000000000.0)
            expo = jnp.exp(score - jnp.max(score, -1, keepdims=True))
            probs = expo * (1.0 / jnp.sum(expo, -1, keepdims=True))
            r.probs[s] = probs
            low = probs.astype(BF16)
            weights[s, low_rows, :] = low
            lows.append(low)
        for s, low in zip(ids, lows):
            u = dot(low, mem[s]).astype(BF16)
            rows = pl.ds(pl.multiple_of(s * ACT, ACT), ACT)
            for h in range(HEADS):
                r.u[rows, pl.ds(h * width, width)] = u[h * ACT : (h + 1) * ACT, :]
        return 0

    lax.fori_loop(0, groups // 2, attend, 0)
    if remote:
        gather.fourth(0, 1)
    lax.fori_loop(groups // 2, groups, attend, 0)
    if remote:
        gather.last(0, 1)
        for m in range(2):
            gather.unpack(m * MLP_ROWS, 4, mlp, m)

    gain_acc = r.gain_acc
    gain_acc[...] = jnp.zeros_like(gain_acc)
    arrive(5)

    def feed(i, _):
        rows = pl.ds(pl.multiple_of(i * ROWS, ROWS), ROWS)
        mixed = dot(r.u[rows, :], wvh[...]).astype(BF16)
        r.mixed[rows, :] = mixed
        resid = r.acts_v[rows, :] + dot(mixed, sq[4])
        hat, scale = normalize(resid)
        second = (hat * g2).astype(BF16)
        r.second[rows, :] = second
        cot = r.cot_v[rows, :]
        out_low = cot.astype(BF16)
        r.out_low[rows, :] = out_low
        for c in range(wide // 256):
            columns = pl.ds(c * 256, 256)
            v = dot(second, mlp[0, :, columns])
            square = v * v
            t = jnp.tanh(0.7978845608 * (v + 0.044715 * square * v))
            r.active[rows, columns] = (0.5 * v * (1.0 + t)).astype(BF16)
            slope = 0.5 * (1.0 + t) + 0.5 * v * (1.0 - t * t) * (0.7978845608 * (1.0 + 0.134145 * square))
            r.dhidden[rows, columns] = (slope * dot(out_low, mlp[1, :, columns])).astype(BF16)
        r.out_v[rows, :] = resid + dot(r.active[rows, :], mlp[1], NT)
        grad_second = dot(r.dhidden[rows, :], mlp[0], NT)
        gain_acc[1:2, :] += jnp.sum(grad_second * hat, 0, keepdims=True)
        dres = cot + norm_back(grad_second * g2, hat, scale)
        r.dres[rows, :] = dres
        low = dres.astype(BF16)
        r.dres_low[rows, :] = low
        gm = dot(low, sq[4], NT).astype(BF16)
        r.dmixed[rows, :] = gm
        here = pl.ds(i * per, per)
        for h in range(HEADS):
            wv = wvh[pl.ds(h * width, width), :]
            sides[here, pl.ds(h * ACT, ACT), :] = dot(gm, wv, NT).astype(BF16).reshape(per, ACT, width)
        return 0

    lax.fori_loop(0, tokens // ROWS, feed, 0)
    keep_out = pltpu.make_async_copy(r.out_v, r.output, out_sems.at[0])
    keep_out.start()

    grads = r.grads

    def put(base, tiles, value):
        for j in range(tiles):
            part = value[:, j * LANES : (j + 1) * LANES].reshape(GRID + (TILE, LANES))
            grads[:, :, :, :, pl.ds(base + j * TILE, TILE), :] = part

    def by_head(left, right):
        turned = left.T
        parts = [
            dot(turned[h * head_dim : (h + 1) * head_dim, :], right[:, pl.ds(h * width, width)])
            for h in range(HEADS)
        ]
        return jnp.concatenate(parts, axis=0).T

    put(0, 8, dot(r.second[...], r.dhidden[...], TN))
    if remote:
        update.start(0)
    put(MLP_ROWS, 8, dot(r.out_low[...], r.active[...], TN))
    if remote:
        update.start(1)
    put(SQ_AT[4], 2, dot(r.mixed[...], r.dres_low[...], TN))
    put(SQ_AT[3], 2, by_head(r.dmixed[...], r.u))
    if remote:
        update.start(2)

    def attend_back(g, _):
        ids = [g * GROUP + k for k in range(GROUP)]
        rises = [dot(sides[s, low_rows, :], mem[s], NT) for s in ids]
        for s, rise in zip(ids, rises):
            probs = r.probs[s]
            both = probs * rise
            weights[s, high_rows, :] = (both - probs * jnp.sum(both, -1, keepdims=True)).astype(BF16)
        for s in ids:
            dq = (dot(weights[s, high_rows, :], mem[s]) * 0.125).astype(BF16)
            rows = pl.ds(pl.multiple_of(s * ACT, ACT), ACT)
            for h in range(HEADS):
                r.dq_wide[rows, pl.ds(h * width, width)] = dq[h * ACT : (h + 1) * ACT, :]
            end = dot(weights[s, :, LANES:KEYS_PAD], sides[s], TN)
            r.stamps[s] = end[64:72, :]
        return 0

    late = groups - groups // 4
    lax.fori_loop(0, late, attend_back, 0)
    if remote:
        update.one(0)
    lax.fori_loop(late, groups, attend_back, 0)
    if remote:
        update.one(1, 2)

    def memory_back(low, high):
        def one(g, _):
            for k in range(GROUP):
                s = g * GROUP + k
                mem[s] = dot(weights[s], sides[s], TN).astype(BF16)
            return 0

        lax.fori_loop(low, high, one, 0)

    def turn_back(part):
        def one(j, _):
            at = pl.ds(pl.multiple_of(j * batch, batch), batch)
            here = pl.ds(part * batch, batch)
            block = mem[here, at, :].reshape(batch * batch, width)
            obs_v[at, here, :] = dot(swap[...], block).astype(BF16).reshape(batch, batch, width)
            return 0

        lax.fori_loop(0, chunks, one, 0)

    def queries_back(i, _):
        rows = pl.ds(pl.multiple_of(i * ROWS, ROWS), ROWS)
        r.dquery[rows, :] = dot(r.dq_wide[rows, :], wkh[...]).astype(BF16)
        return 0

    lax.fori_loop(0, tokens // ROWS, queries_back, 0)
    put(SQ_AT[1], 2, dot(r.first[...], r.dquery[...], TN))
    stamp_low = r.stamps[:, 4:5, :].reshape(samples, width).astype(BF16)
    put(SQ_AT[0], 2, dot(r.embed[...], stamp_low, TN))
    if remote:
        update.start(3)

    def acts_back(i, _):
        rows = pl.ds(pl.multiple_of(i * ROWS, ROWS), ROWS)
        grad_first = dot(r.dquery[rows, :], sq[1], NT)
        hat = r.xhat[rows, :]
        gain_acc[0:1, :] += jnp.sum(grad_first * hat, 0, keepdims=True)
        r.ag_v[rows, :] = r.dres[rows, :] + norm_back(grad_first * g1, hat, r.rstd[rows, :])
        return 0

    lax.fori_loop(0, tokens // ROWS, acts_back, 0)
    put(SQ_AT[2], 2, by_head(r.query[...], r.dq_wide))
    for norm in range(2):
        for j in range(2):
            row = gain_acc[norm : norm + 1, j * LANES : (j + 1) * LANES]
            at = GAIN_BASE + norm * 2 + j
            value = jnp.broadcast_to(row.reshape(1, 1, 1, 1, 1, LANES), GRID + (1, LANES))
            grads[:, :, :, :, at : at + 1, :] = value
    rest = WIRE - GAIN_BASE - 4
    grads[:, :, :, :, GAIN_BASE + 4 : WIRE, :] = jnp.zeros(GRID + (rest, LANES), F32)
    keep_ag = pltpu.make_async_copy(r.ag_v, r.ag, out_sems.at[2])
    keep_ag.start()
    keep_og = pltpu.make_async_copy(obs_v.at[pl.ds(0, keys)], r.og, out_sems.at[1])
    half_groups = groups // 2
    if remote:
        update.start(4)
        update.two(0, 1, 2)
        memory_back(0, half_groups)
        update.one(3, 4)
        update.three(0, 1)
        turn_back(0)
        update.two(3, 4)
        update.three(2)
        memory_back(half_groups, groups)
        update.three(3, 4)
        update.four(0, 1)
        turn_back(1)
        keep_og.start()
        update.four(2, 3, 4)
        update.orthogonalize()
        update.give_all()
        out = r.out
        out[1, :, :] = r.moment[...]
        out[2, pl.ds(GAIN_BASE, 16), :] = jnp.zeros((16, LANES), F32)
        update.take_all()
        gather.drain()
        update.drain()
    else:
        memory_back(0, groups)
        for part in range(samples // batch):
            turn_back(part)
        keep_og.start()
    for copy in (keep_out, keep_og, keep_ag):
        copy.wait()


def block_and_back(remote, acts, obs, flags, levels, cot, sqw, mlpw, gain, sqm=None, mlpm=None):
    tokens, width = acts.shape
    keys, samples = obs.shape[0], obs.shape[1]
    rows = HEADS * ACT
    wide = mlpw.shape[2]
    any_space = pl.BlockSpec(memory_space=pl.ANY)
    in_vmem = pl.BlockSpec(memory_space=VMEM)
    scalars = pl.BlockSpec(memory_space=pltpu.SMEM)
    sem = pltpu.SemaphoreType.DMA
    ins = dict(flags=flags, levels=levels, acts=acts, obs=obs, cot=cot, sqw=sqw, mlpw=mlpw, gain=gain)
    outs = dict(
        output=jax.ShapeDtypeStruct(acts.shape, F32),
        ag=jax.ShapeDtypeStruct(acts.shape, F32),
        og=jax.ShapeDtypeStruct(obs.shape, BF16),
    )
    grads = GRID + (WIRE, LANES)
    scratch = dict(
        obs_v=VMEM((KEYS_PAD, samples, width), BF16),
        acts_v=VMEM(acts.shape, F32),
        cot_v=VMEM(acts.shape, F32),
        mem=VMEM((samples, KEYS_PAD, width), BF16),
        swap=VMEM((256, 256), BF16),
        sq_all=VMEM((5, width, width), BF16),
        mlp_all=VMEM((2, width, wide), BF16),
        gain_all=VMEM((2, width), F32),
        wkh=VMEM((HEADS * width, width), BF16),
        wvh=VMEM((HEADS * width, width), BF16),
        first=VMEM((tokens, width), BF16),
        query=VMEM((tokens, width), BF16),
        xhat=VMEM((tokens, width), F32),
        rstd=VMEM((tokens, 1), F32),
        probs=VMEM((samples, rows, KEYS_PAD), F32),
        pds_v=VMEM((samples, 2 * rows, KEYS_PAD), BF16),
        sides_v=VMEM((samples, 2 * rows, width), BF16),
        u=VMEM((tokens, HEADS * width), BF16),
        dq_wide=VMEM((tokens, HEADS * width), BF16),
        mixed=VMEM((tokens, width), BF16),
        second=VMEM((tokens, width), BF16),
        active=VMEM((tokens, wide), BF16),
        dhidden=VMEM((tokens, wide), BF16),
        out_low=VMEM((tokens, width), BF16),
        dres_low=VMEM((tokens, width), BF16),
        dres=VMEM((tokens, width), F32),
        dmixed=VMEM((tokens, width), BF16),
        dquery=VMEM((tokens, width), BF16),
        out_v=VMEM((tokens, width), F32),
        ag_v=VMEM((tokens, width), F32),
        angle=VMEM((samples, width // 2), F32),
        embed=VMEM((samples, width), BF16),
        stamps=VMEM((samples, 8, width), F32),
        gain_acc=VMEM((8, width), F32),
        in_sems=sem((8,)),
        out_sems=sem((3,)),
    )
    extra = {}
    if remote:
        ins.update(sqm=sqm, mlpm=mlpm)
        outs.update(out=jax.ShapeDtypeStruct((3, WIRE, LANES), F32))
        chunks = len(CHUNKS)
        scratch.update(
            grads=VMEM(grads, F32),
            sqw_v=VMEM(sqw.shape, F32),
            mlpw_v=VMEM(mlpw.shape, F32),
            gain_v=VMEM(gain.shape, F32),
            sqm_v=VMEM(sqm.shape, F32),
            mlpm_v=VMEM(mlpm.shape, F32),
            wire=VMEM(grads, BF16),
            edge=VMEM((16, LANES), F32),
            gsend=sem((chunks, 6)),
            grecv=sem((chunks, 6)),
            send0=VMEM((4, 2, 2, WIRE, LANES), BF16),
            got_core=VMEM((4, 2, 2, WIRE, LANES), BF16),
            sum1=VMEM((4, 2, 2, WIRE, LANES), F32),
            send1=VMEM((4, 2, WIRE, LANES), BF16),
            got1=VMEM((4, 2, WIRE, LANES), BF16),
            sum2=VMEM((4, 2, WIRE, LANES), F32),
            send2=VMEM((4, WIRE, LANES), BF16),
            got2=VMEM((4, WIRE, LANES), BF16),
            sum3=VMEM((4, WIRE, LANES), F32),
            send3=VMEM((3, WIRE, LANES), BF16),
            got3=VMEM((3, WIRE, LANES), BF16),
            moment=VMEM((WIRE, LANES), F32),
            slabs_sq=VMEM((32, SQ_ROWS, LANES), F32),
            slabs_mlp=VMEM((32, MLP_ROWS, LANES), BF16),
            moment_low=VMEM((2 * MLP_ROWS, LANES), BF16),
            back_mlp=VMEM((2, MLP_ROWS, LANES), BF16),
            result_sq=VMEM((32, SQ_ROWS, LANES), F32),
            result_mlp=VMEM((32, MLP_ROWS, LANES), BF16),
            cur=VMEM((width, wide), F32),
            send=sem((chunks, 6)),
            recv=sem((chunks, 6)),
            own_send=sem((7,)),
            own_recv=sem((1,)),
            back_send=sem((32,)),
            back_recv=sem((7,)),
        )
        extra = dict(collective_id=0, has_side_effects=True)
    else:
        outs.update(grads=jax.ShapeDtypeStruct(grads, F32))
    names = tuple(ins) + tuple(outs) + tuple(scratch)
    results = pl.pallas_call(
        functools.partial(block_kernel, names, remote),
        out_shape=tuple(outs.values()),
        in_specs=[scalars] * 2 + [any_space] * (len(ins) - 2),
        out_specs=[any_space] * 3 + [in_vmem],
        scratch_shapes=list(scratch.values()),
        compiler_params=pltpu.CompilerParams(vmem_limit_bytes=56 << 20, **extra),
        name="block_and_back",
    )(*ins.values())
    return Refs(zip(outs, results))


PARTS = 7


def finish_kernel(names, rate, *args):
    r = Refs(zip(names, args))
    sems = r.sems
    keys = r.og.shape[0]
    step = keys // PARTS

    def come(part):
        block = pl.ds(part * step, step)
        return pltpu.make_async_copy(r.low.at[block], r.low_v.at[block], sems.at[2 * part])

    def leave(part):
        block = pl.ds(part * step, step)
        return pltpu.make_async_copy(r.og_v.at[block], r.og.at[block], sems.at[2 * part + 1])

    for part in range(PARTS):
        come(part).start()
    more = 2 * PARTS
    small, passes = [], []
    if hasattr(r, "wire"):
        pairs = [(r.output, r.output_v), (r.ag, r.ag_v), (r.wire, r.wire_v), (r.sqw, r.sqw_v)]
        pairs += [(r.mlpw, r.mlpw_v), (r.gain, r.gain_v), (r.gainm, r.gainm_v)]
        for source, target in pairs:
            small.append(pltpu.make_async_copy(source, target, sems.at[more]))
            small[-1].start()
            more += 1
        for source, target in ((r.output_v, r.output_f), (r.ag_v, r.ag_f)):
            passes.append(pltpu.make_async_copy(source, target, sems.at[more]))
            more += 1
    for part in range(PARTS):
        come(part).wait()

        def widen(j, _):
            r.og_v[j] = r.low_v[j].astype(F32)
            return 0

        lax.fori_loop(part * step, (part + 1) * step, widen, 0, unroll=4)
        leave(part).start()
    for copy in small[:2]:
        copy.wait()
    for copy in passes:
        copy.start()
    if hasattr(r, "wire"):
        for copy in small[2:]:
            copy.wait()
        finish_weights(r, rate)
    for part in range(PARTS):
        leave(part).wait()
    for copy in passes:
        copy.wait()


def finish_weights(r, rate):
    wire = r.wire_v
    me = lax.axis_index("dp")
    for m in range(5):
        for j in range(2):
            rows, columns = pl.ds(SQ_AT[m] + j * TILE, TILE), pl.ds(j * LANES, LANES)
            r.sqg[m, :, columns] = wire[0, rows, :]
            r.sqm[m, :, columns] = wire[1, rows, :]
            r.sqn[m, :, columns] = r.sqw_v[m, :, columns] - SQ_RATES[m] * wire[2, rows, :]
    r.sqc[...] = r.sqn[...].astype(BF16)
    for m in range(2):
        for j in range(8):
            rows, columns = pl.ds(m * MLP_ROWS + j * TILE, TILE), pl.ds(j * LANES, LANES)
            r.mlpg[m, :, columns] = wire[0, rows, :]
            r.mlpm[m, :, columns] = wire[1, rows, :]
            r.mlpn[m, :, columns] = r.mlpw_v[m, :, columns] - MLP_RATES[m] * wire[2, rows, :]
    r.mlpc[...] = r.mlpn[...].astype(BF16)
    tile = wire[0, pl.ds(GAIN_BASE, TILE), :]
    turned = pltpu.roll(tile, (LANES - (me % 16) * TILE) % LANES, 1)
    at = me // 16
    for norm in range(2):
        pair = turned[2 * norm : 2 * norm + 2, 0:TILE]
        row = jnp.where(at == 0, pair[0:1, :], pair[1:2, :])
        new = 0.5 * r.gainm_v[norm : norm + 1, :] + row
        r.gg[norm : norm + 1, :] = row
        r.gm[norm : norm + 1, :] = new
        r.gn[norm : norm + 1, :] = r.gain_v[norm : norm + 1, :] - rate * new


def finish(rate, made, sqw=None, mlpw=None, gain=None, gainm=None):
    any_space = pl.BlockSpec(memory_space=pl.ANY)
    in_vmem = pl.BlockSpec(memory_space=VMEM)
    ins = dict(low=made.og)
    outs = dict(og=jax.ShapeDtypeStruct(made.og.shape, F32))
    far = 1
    if hasattr(made, "out"):
        ins.update(output=made.output, ag=made.ag, wire=made.out, sqw=sqw, mlpw=mlpw, gain=gain, gainm=gainm)
        like = jax.ShapeDtypeStruct
        far = 3
        outs.update(
            output_f=like(made.output.shape, F32),
            ag_f=like(made.ag.shape, F32),
            sqg=like(sqw.shape, F32),
            sqm=like(sqw.shape, F32),
            sqn=like(sqw.shape, F32),
            sqc=like(sqw.shape, BF16),
            mlpg=like(mlpw.shape, F32),
            mlpm=like(mlpw.shape, F32),
            mlpn=like(mlpw.shape, F32),
            mlpc=like(mlpw.shape, BF16),
            gg=like(gain.shape, F32),
            gm=like(gain.shape, F32),
            gn=like(gain.shape, F32),
        )
    scratch = dict(
        low_v=VMEM(made.og.shape, BF16),
        og_v=VMEM(made.og.shape, F32),
        sems=pltpu.SemaphoreType.DMA((2 * PARTS + 9,)),
    )
    if hasattr(made, "out"):
        scratch.update(
            output_v=VMEM(made.output.shape, F32),
            ag_v=VMEM(made.ag.shape, F32),
            wire_v=VMEM(made.out.shape, F32),
            sqw_v=VMEM(sqw.shape, F32),
            mlpw_v=VMEM(mlpw.shape, F32),
            gain_v=VMEM(gain.shape, F32),
            gainm_v=VMEM(gainm.shape, F32),
        )
    names = tuple(ins) + tuple(outs) + tuple(scratch)
    results = pl.pallas_call(
        functools.partial(finish_kernel, names, rate),
        out_shape=tuple(outs.values()),
        in_specs=[any_space] * len(ins),
        out_specs=[any_space] * far + [in_vmem] * (len(outs) - far),
        scratch_shapes=list(scratch.values()),
        compiler_params=pltpu.CompilerParams(vmem_limit_bytes=60 << 20),
        name="finish",
    )(*ins.values())
    return Refs(zip(outs, results))


HIGH_PRECISION = lax.Precision.HIGHEST


def plain_orthogonalize(matrix):
    current = matrix / (jnp.sqrt(jnp.sum(matrix * matrix)) + 1e-07)
    for turn in range(5):
        gram = jnp.dot(current, current.T, precision=HIGH_PRECISION)
        poly = COEF_B * gram + COEF_C * jnp.dot(gram, gram, precision=HIGH_PRECISION)
        current = COEF_A * current + jnp.dot(poly, current, precision=HIGH_PRECISION)
    return current


def pick_owned(stack, owners, device):
    chosen = jnp.zeros_like(stack[0])
    for index in range(len(owners)):
        chosen = jnp.where(device == owners[index], stack[index], chosen)
    return chosen


def is_owner(owners, device):
    flag = device < 0
    for owner in owners:
        flag = jnp.logical_or(flag, device == owner)
    return flag


def from_wire(grads):
    def matrix(base, tiles):
        part = grads[:, base : base + tiles * TILE, :].reshape(-1, tiles, TILE, LANES)
        return part.transpose(0, 2, 1, 3).reshape(-1, tiles * LANES)

    square = jnp.stack([matrix(SQ_AT[m], 2) for m in range(5)])
    mlp = jnp.stack([matrix(m * MLP_ROWS, 8) for m in range(2)])
    return square, mlp, grads[0, GAIN_BASE : GAIN_BASE + 4, :].reshape(2, 2 * LANES)


def update_by_collectives(
    grads, square_weights, mlp_weights, gains, square_moment, mlp_moment, gain_moment, rate
):
    square_local, mlp_local, gain_local = from_wire(grads)
    square_grad, mlp_grad, gain_grad = (
        lax.psum_scatter(square_local, "dp", scatter_dimension=1, tiled=True),
        lax.psum_scatter(mlp_local, "dp", scatter_dimension=1, tiled=True),
        lax.psum_scatter(gain_local, "dp", scatter_dimension=1, tiled=True),
    )
    square_moment_new = 0.5 * square_moment + square_grad
    mlp_moment_new = 0.5 * mlp_moment + mlp_grad
    gain_moment_new = 0.5 * gain_moment + gain_grad
    device = lax.axis_index("dp")
    count = lax.axis_size("dp")
    square_owners = [index * count // 7 for index in range(5)]
    mlp_owners = [(index + 5) * count // 7 for index in range(2)]
    square_full, mlp_full = (
        lax.all_gather(square_moment_new, "dp", axis=1, tiled=True),
        lax.all_gather(mlp_moment_new, "dp", axis=1, tiled=True),
    )
    mine_square = pick_owned(square_full, square_owners, device)
    mine_mlp = pick_owned(mlp_full, mlp_owners, device)
    made_square = lax.cond(
        is_owner(square_owners, device), plain_orthogonalize, jnp.zeros_like, mine_square
    )
    made_mlp = lax.cond(is_owner(mlp_owners, device), plain_orthogonalize, jnp.zeros_like, mine_mlp)
    stack_square = jnp.stack(
        [jnp.where(device == owner, made_square, 0.0) for owner in square_owners]
    )
    stack_mlp = jnp.stack([jnp.where(device == owner, made_mlp, 0.0) for owner in mlp_owners])
    square_ortho, mlp_ortho = (
        lax.psum_scatter(stack_square, "dp", scatter_dimension=1, tiled=True),
        lax.psum_scatter(stack_mlp, "dp", scatter_dimension=1, tiled=True),
    )
    square_new = square_weights - jnp.array(SQ_RATES, F32)[:, None, None] * square_ortho
    mlp_new = mlp_weights - jnp.array(MLP_RATES, F32)[:, None, None] * mlp_ortho
    gains_new = gains - rate * gain_moment_new
    return (
        square_grad,
        square_moment_new,
        square_new,
        square_new.astype(BF16),
        mlp_grad,
        mlp_moment_new,
        mlp_new,
        mlp_new.astype(BF16),
        gain_grad,
        gain_moment_new,
        gains_new,
    )


def per_device(
    actions,
    observed,
    camera_flags,
    noise_levels,
    cotangent,
    square_weights,
    mlp_weights,
    gains,
    square_moment,
    mlp_moment,
    gain_moment,
):
    count = lax.axis_size("dp")
    rate = 0.1 / math.sqrt(actions.shape[0] * count)
    by_key = observed.transpose(1, 0, 2)
    ins = (actions, by_key, camera_flags, noise_levels, cotangent)
    if count == math.prod(GRID):
        made = block_and_back(True, *ins, square_weights, mlp_weights, gains, square_moment, mlp_moment)
        done = finish(rate, made, square_weights, mlp_weights, gains, gain_moment)
        output, actions_grad = done.output_f, done.ag_f
        d = done
        rest = (d.sqg, d.sqm, d.sqn, d.sqc, d.mlpg, d.mlpm, d.mlpn, d.mlpc, d.gg, d.gm, d.gn)
    else:
        square_all, mlp_all = (
            lax.all_gather(square_weights.astype(BF16), "dp", axis=1, tiled=True),
            lax.all_gather(mlp_weights.astype(BF16), "dp", axis=1, tiled=True),
        )
        gain_all = lax.all_gather(gains, "dp", axis=1, tiled=True)
        made = block_and_back(False, *ins, square_all, mlp_all, gain_all)
        done = finish(rate, made)
        output, actions_grad = made.output, made.ag
        grads = made.grads.reshape(-1, WIRE, LANES)
        rest = update_by_collectives(
            grads, square_weights, mlp_weights, gains, square_moment, mlp_moment, gain_moment, rate
        )
    observed_grad = done.og.transpose(1, 0, 2)
    return (output, actions_grad, observed_grad) + tuple(rest)


def solution(mesh):
    rows, cube, flat = P("dp", None), P("dp", None, None), P("dp")
    stacked, pair = P(None, "dp", None), P(None, "dp")
    return jax.shard_map(
        per_device,
        mesh=mesh,
        in_specs=(rows, cube, flat, flat, rows, stacked, stacked, pair, stacked, stacked, pair),
        out_specs=(rows, rows, cube) + (stacked,) * 8 + (pair,) * 3,
        check_vma=False,
    )
```

```python
import functools
import math

import jax
import jax.numpy as jnp
from jax import lax
from jax.experimental import pallas as pl
from jax.experimental.pallas import tpu as pltpu
from jax.sharding import PartitionSpec as P

HEADS = 4
ACT = 16
OBS_FULL = 196
OBS_FEW = 49
COEF_A = 3.4445
COEF_B = -4.775
COEF_C = 2.0315
F32 = jnp.float32
BF16 = jnp.bfloat16
MESH = pl.DeviceIdType.MESH
VMEM = pltpu.VMEM
NN = (((1,), (0,)), ((), ()))
NT = (((1,), (1,)), ((), ()))
TN = (((0,), (0,)), ((), ()))

LANES = 128
TILE = 8
MLP_ROWS = 64
SQ_ROWS = 16
SQ_AT = (160, 192, 176, 128, 144)
GAIN_BASE = 208
WIRE = 224
PIECES = ((0, 64), (64, 64), (128, 32), (160, 32), (192, 32))
PIECE_X_FIRST = (True, False, True, True, False)
CHUNKS = ((0, 64), (64, 64), (128, 32), (160, 32), (192, 16), (208, 16))
X_FIRST = (True, False, True, False, True, False)
COMPLETES = ((0,), (1,), (5, 6), (2, 4), (3,), ())
MLP_RATES = (1.0, 0.5)
SQ_RATES = (0.5, 0.5, 0.5, 0.5, 4.0)
GRID = (4, 2, 2, 2)
OWNERS = (8, 22, 14, 16, 11, 21, 13)
SHIFTS = (0.0, 0.0, 0.4, 0.8, 0.8)
KEYS_PAD = 208
GROUP = 8
ROWS = 256


class Refs:
    def __init__(self, pairs):
        self.__dict__.update(pairs)


def dot(left, right, dims=NN):
    return lax.dot_general(left, right, dims, preferred_element_type=F32)


def place():
    me = lax.axis_index("dp")
    return me, me // 8, (me // 4) % 2, (me // 2) % 2, me % 2


def device_at(z, y, x, c):
    return ((z * 2 + y) * 2 + x) * 2 + c


def link(src, dst, send, recv, device):
    return pltpu.make_async_remote_copy(
        src_ref=src,
        dst_ref=dst,
        send_sem=send,
        recv_sem=recv,
        device_id=(device,),
        device_id_type=MESH,
    )


def greet(device):
    pl.semaphore_signal(
        pltpu.get_barrier_semaphore(), inc=1, device_id=(device,), device_id_type=MESH
    )


def normalize(values):
    centred = values - jnp.mean(values, -1, keepdims=True)
    scale = lax.rsqrt(jnp.mean(centred * centred, -1, keepdims=True) + 1e-05)
    return centred * scale, scale


def norm_back(grad, hat, scale):
    mean_one = jnp.mean(grad, -1, keepdims=True)
    mean_two = jnp.mean(grad * hat, -1, keepdims=True)
    return scale * (grad - mean_one - hat * mean_two)


class Gather:
    def __init__(self, r):
        self.r = r
        self.me, self.z, self.y, self.x, self.c = place()

    def hop(self, k, step, part, device):
        return link(part, part, self.r.gsend.at[k, step], self.r.grecv.at[k, step], device)

    def along_z(self, k, step):
        part = self.r.wire.at[self.z, self.y, self.x, self.c, pl.ds(*PIECES[k])]
        return self.hop(k, step, part, device_at((self.z + step + 1) % 4, self.y, self.x, self.c))

    def from_z(self, k, step):
        there = (self.z + 3 - step) % 4
        part = self.r.wire.at[there, self.y, self.x, self.c, pl.ds(*PIECES[k])]
        return self.hop(k, step, part, device_at(there, self.y, self.x, self.c))

    def plane(self, k, second, mine):
        z, y, x, c = self.z, self.y, self.x, self.c
        rows, wire = pl.ds(*PIECES[k]), self.r.wire
        py, px = (y, x) if mine else (1 - y, 1 - x)
        along_x = PIECE_X_FIRST[k] == second
        if along_x:
            part = wire.at[:, y, px, c, rows] if second else wire.at[:, :, px, c, rows]
            return self.hop(k, 3 if second else 4, part, device_at(z, y, 1 - x, c))
        part = wire.at[:, py, x, c, rows] if second else wire.at[:, py, :, c, rows]
        return self.hop(k, 3 if second else 4, part, device_at(z, 1 - y, x, c))

    def core(self, k, mine):
        part = self.r.wire.at[:, :, :, self.c if mine else 1 - self.c, pl.ds(*PIECES[k])]
        return self.hop(k, 5, part, device_at(self.z, self.y, self.x, 1 - self.c))

    def first(self, *chunks):
        for k in chunks:
            for step in range(3):
                self.along_z(k, step).start()

    def second(self, *chunks):
        for k in chunks:
            for step in range(3):
                self.from_z(k, step).wait_recv()
            self.plane(k, True, True).start()

    def third(self, *chunks):
        for k in chunks:
            self.plane(k, True, False).wait_recv()
            self.plane(k, False, True).start()

    def fourth(self, *chunks):
        for k in chunks:
            self.plane(k, False, False).wait_recv()
            self.core(k, True).start()

    def last(self, *chunks):
        for k in chunks:
            self.core(k, False).wait_recv()

    def drain(self):
        for k in range(len(PIECES)):
            for step in range(3):
                self.along_z(k, step).wait_send()
            self.plane(k, True, True).wait_send()
            self.plane(k, False, True).wait_send()
            self.core(k, True).wait_send()

    def fill(self):
        r = self.r
        spot = (self.z, self.y, self.x, self.c)

        def tiles(source, m, base, number):
            for j in range(number):
                pair = [source[m, :, pl.ds((2 * j + k) * LANES, LANES)] for k in range(2)]
                r.wire[spot + (pl.ds(base + j * 16, 16),)] = jnp.concatenate(pair, axis=0).astype(BF16)

        for m in range(5):
            tiles(r.sqw_v, m, SQ_AT[m], 1)
        for m in range(2):
            tiles(r.mlpw_v, m, m * MLP_ROWS, 4)
        gains, edge = r.gain_v[...], r.edge
        high = gains.astype(BF16).astype(F32)
        middle = (gains - high).astype(BF16).astype(F32)
        edge[...] = jnp.zeros_like(edge)
        edge[0:2, 0:TILE] = high
        edge[2:4, 0:TILE] = middle
        edge[4:6, 0:TILE] = (gains - high - middle).astype(BF16).astype(F32)
        r.wire[spot + (pl.ds(GAIN_BASE, 16),)] = edge[...].astype(BF16)

    def unpack(self, base, number, out, m):
        for j in range(number):
            block = self.r.wire[:, :, :, :, pl.ds(base + j * 16, 16), :].reshape(32, 16, LANES).astype(F32)
            for half in range(2):
                columns = pl.ds((2 * j + half) * LANES, LANES)
                out[m, :, columns] = block[:, half * 8 : half * 8 + 8, :].reshape(256, LANES).astype(BF16)

    def unpack_gains(self):
        edge, wire = self.r.edge, self.r.wire
        for half in range(2):
            total = jnp.zeros((16, LANES), F32)
            for at in range(16):
                d = half * 16 + at
                tile = wire[d // 8, (d // 4) % 2, (d // 2) % 2, d % 2, pl.ds(GAIN_BASE, 16), :].astype(F32)
                total = total + (tile if at == 0 else pltpu.roll(tile, at * TILE, 1))
            edge[...] = total
            self.r.gain_all[:, pl.ds(half * LANES, LANES)] = edge[0:2, :] + edge[2:4, :] + edge[4:6, :]


class Update:
    def __init__(self, r):
        self.r = r
        self.me, self.z, self.y, self.x, self.c = place()

    def hop(self, k, step, src, dst, device):
        return link(src, dst, self.r.send.at[k, step], self.r.recv.at[k, step], device)

    def core(self, k):
        rows = pl.ds(*CHUNKS[k])
        src, dst = self.r.send0.at[:, :, :, rows], self.r.got_core.at[:, :, :, rows]
        return self.hop(k, 0, src, dst, device_at(self.z, self.y, self.x, 1 - self.c))

    def plane(self, k, first):
        rows = pl.ds(*CHUNKS[k])
        to = (self.z, self.y, 1 - self.x, self.c) if X_FIRST[k] == first else (self.z, 1 - self.y, self.x, self.c)
        if first:
            src, dst = self.r.send1.at[:, :, rows], self.r.got1.at[:, :, rows]
        else:
            src, dst = self.r.send2.at[:, rows], self.r.got2.at[:, rows]
        return self.hop(k, 1 if first else 2, src, dst, device_at(*to))

    def along_z(self, k, step):
        rows = pl.ds(*CHUNKS[k])
        to = device_at((self.z + step + 1) % 4, self.y, self.x, self.c)
        return self.hop(k, 3 + step, self.r.send3.at[step, rows], self.r.got3.at[step, rows], to)

    def start(self, k):
        rows = pl.ds(*CHUNKS[k])
        self.r.send0[:, :, :, rows, :] = self.r.grads[:, :, :, 1 - self.c, rows, :].astype(BF16)
        self.core(k).start()

    def one(self, *chunks):
        r = self.r
        for k in chunks:
            rows = pl.ds(*CHUNKS[k])
            self.core(k).wait_recv()
            sum1 = r.sum1
            sum1[:, :, :, rows, :] = r.grads[:, :, :, self.c, rows, :] + r.got_core[:, :, :, rows, :].astype(F32)
            other = sum1[:, :, 1 - self.x, rows, :] if X_FIRST[k] else sum1[:, 1 - self.y, :, rows, :]
            r.send1[:, :, rows, :] = other.astype(BF16)
            self.plane(k, True).start()

    def two(self, *chunks):
        r = self.r
        for k in chunks:
            rows = pl.ds(*CHUNKS[k])
            self.plane(k, True).wait_recv()
            sum1, sum2 = r.sum1, r.sum2
            mine = sum1[:, :, self.x, rows, :] if X_FIRST[k] else sum1[:, self.y, :, rows, :]
            sum2[:, :, rows, :] = mine + r.got1[:, :, rows, :].astype(F32)
            other = 1 - self.y if X_FIRST[k] else 1 - self.x
            r.send2[:, rows, :] = sum2[:, other, rows, :].astype(BF16)
            self.plane(k, False).start()

    def three(self, *chunks):
        r = self.r
        for k in chunks:
            rows = pl.ds(*CHUNKS[k])
            self.plane(k, False).wait_recv()
            mine = self.y if X_FIRST[k] else self.x
            r.sum3[:, rows, :] = r.sum2[:, mine, rows, :] + r.got2[:, rows, :].astype(F32)
            for step in range(3):
                r.send3[step, rows, :] = r.sum3[(self.z + step + 1) % 4, rows, :].astype(BF16)
                self.along_z(k, step).start()

    def slab(self, index):
        if index < 2:
            return pl.ds(index * MLP_ROWS, MLP_ROWS), self.r.slabs_mlp, self.r.result_mlp
        return pl.ds(SQ_AT[index - 2], SQ_ROWS), self.r.slabs_sq, self.r.result_sq

    def to_owner(self, index):
        rows, slabs, _ = self.slab(index)
        moment = self.r.moment_low if index < 2 else self.r.moment
        return link(
            moment.at[rows], slabs.at[self.me],
            self.r.own_send.at[index], self.r.own_recv.at[0], OWNERS[index],
        )

    def four(self, *chunks):
        r = self.r
        moment, out = r.moment, r.out
        for k in chunks:
            rows = pl.ds(*CHUNKS[k])
            total = r.sum3[self.z, rows, :]
            for step in range(3):
                self.along_z(k, step).wait_recv()
                total = total + r.got3[step, rows, :].astype(F32)
            out[0, rows, :] = total
            new = 0.5 * moment[rows, :] + total
            moment[rows, :] = new
            if k < 2:
                r.moment_low[rows, :] = new.astype(BF16)
            for index in COMPLETES[k]:
                rows_m, slabs, _ = self.slab(index)

                @pl.when(self.me != OWNERS[index])
                def _():
                    self.to_owner(index).start()

                @pl.when(self.me == OWNERS[index])
                def _():
                    mine = r.moment_low if index < 2 else moment
                    pltpu.make_async_copy(mine.at[rows_m], slabs.at[self.me], r.own_recv.at[0]).start()

    def old_moment(self):
        r = self.r
        moment = r.moment
        for m in range(2):
            for j in range(8):
                moment[pl.ds(m * MLP_ROWS + j * TILE, TILE), :] = r.mlpm_v[m, :, pl.ds(j * LANES, LANES)]
        for m in range(5):
            for j in range(2):
                moment[pl.ds(SQ_AT[m] + j * TILE, TILE), :] = r.sqm_v[m, :, pl.ds(j * LANES, LANES)]
        moment[pl.ds(GAIN_BASE, 16), :] = jnp.zeros((16, LANES), F32)

    def orthogonalize(self):
        r = self.r
        cur = r.cur
        rows = lax.broadcasted_iota(jnp.int32, (256, 256), 0)
        diagonal = rows == lax.broadcasted_iota(jnp.int32, (256, 256), 1)

        def run(slabs, result, tiles):
            pltpu.make_async_copy(slabs, slabs, r.own_recv.at[0]).wait()
            low = r.cur_low
            for j in range(tiles // 2):
                pair = slabs[:, pl.ds(j * 16, 16), :].astype(F32)
                for side in range(2):
                    columns = pl.ds((2 * j + side) * LANES, LANES)
                    part = pair[:, side * TILE : (side + 1) * TILE, :].reshape(256, LANES)
                    cur[:, columns] = part
                    low[:, columns] = part.astype(BF16)
            scale = 1.0
            for turn, shift in enumerate(SHIFTS):
                whole = low[:, 0 : tiles * LANES]
                off = dot(whole, whole, NT)
                if turn == 0:
                    norm = jnp.sum(jnp.sum(jnp.where(diagonal, off, 0.0), axis=0, keepdims=True), axis=1, keepdims=True)
                    scale = 1.0 / (jnp.sqrt(norm) + 1e-07)
                    off = off * (scale * scale)
                if shift:
                    off = off - jnp.where(diagonal, shift, 0.0)
                off_low = off.astype(BF16)
                poly = (COEF_B + 2.0 * COEF_C * shift) * off + COEF_C * dot(off_low, off_low)
                poly = poly.astype(BF16)
                keep = COEF_A + shift * (COEF_B + COEF_C * shift)
                for j in range(tiles // 2):
                    columns = pl.ds(j * 2 * LANES, 2 * LANES)
                    now = keep * cur[:, columns] + dot(poly, low[:, columns])
                    if turn == 0:
                        now = now * scale
                    if turn < len(SHIFTS) - 1:
                        cur[:, columns] = now
                        low[:, columns] = now.astype(BF16)
                    else:
                        parts = [now[:, side * LANES : (side + 1) * LANES].reshape(32, TILE, LANES) for side in range(2)]
                        result[:, pl.ds(j * 16, 16), :] = jnp.concatenate(parts, axis=1).astype(result.dtype)

        mine_mlp = jnp.logical_or(self.me == OWNERS[0], self.me == OWNERS[1])
        mine_sq = self.me < 0
        for device in OWNERS[2:]:
            mine_sq = jnp.logical_or(mine_sq, self.me == device)

        @pl.when(mine_mlp)
        def _():
            run(r.slabs_mlp, r.result_mlp, 8)

        @pl.when(mine_sq)
        def _():
            run(r.slabs_sq, r.result_sq, 2)

    def landing(self, index):
        if index < 2:
            return self.r.back_mlp.at[index]
        return self.r.out.at[2, pl.ds(SQ_AT[index - 2], SQ_ROWS)]

    def give_back(self, index, device):
        _, _, result = self.slab(index)
        return link(
            result.at[device], self.landing(index),
            self.r.back_send.at[device], self.r.back_recv.at[index], device,
        )

    def give_all(self):
        r = self.r
        for index in range(7):
            _, _, result = self.slab(index)

            @pl.when(self.me == OWNERS[index])
            def _():
                def send_one(step, _):
                    self.give_back(index, (self.me + step) % 32).start()
                    return 0

                lax.fori_loop(1, 32, send_one, 0)
                pltpu.make_async_copy(result.at[self.me], self.landing(index), r.back_recv.at[index]).start()

    def take_all(self):
        for index in range(7):
            _, _, result = self.slab(index)
            pltpu.make_async_copy(result.at[0], self.landing(index), self.r.back_recv.at[index]).wait()
        for index in range(2):
            rows = pl.ds(index * MLP_ROWS, MLP_ROWS)
            self.r.out[2, rows, :] = self.r.back_mlp[index].astype(F32)

    def drain(self):
        for k in range(len(CHUNKS)):
            self.core(k).wait_send()
            self.plane(k, True).wait_send()
            self.plane(k, False).wait_send()
            for step in range(3):
                self.along_z(k, step).wait_send()
        for index in range(7):

            @pl.when(self.me != OWNERS[index])
            def _():
                self.to_owner(index).wait_send()

    def drain_owner(self):
        for index in range(7):

            @pl.when(self.me == OWNERS[index])
            def _():
                def wait_one(step, _):
                    self.give_back(index, (self.me + step) % 32).wait_send()
                    return 0

                lax.fori_loop(1, 32, wait_one, 0)


def greet_all():
    me, z, y, x, c = place()
    greet(device_at(z, y, x, 1 - c))
    greet(device_at(z, y, 1 - x, c))
    greet(device_at(z, 1 - y, x, c))
    for step in range(1, 4):
        greet(device_at((z + step) % 4, y, x, c))
    owner = me < 0
    for device in OWNERS:
        owner = jnp.logical_or(owner, me == device)

        @pl.when(me != device)
        def _():
            greet(device)

    @pl.when(owner)
    def _():
        def greet_other(step, _):
            greet((me + step) % 32)
            return 0

        lax.fori_loop(1, 32, greet_other, 0)

    is_owner = owner.astype(jnp.int32)
    return 6 + 7 - is_owner + 31 * is_owner


def block_kernel(names, remote, *args):
    r = Refs(zip(names, args))
    keys, samples = r.obs.shape[0], r.obs.shape[1]
    tokens, width = r.acts.shape
    head_dim, half, per = width // HEADS, width // 2, ROWS // ACT
    wide = r.mlp_all.shape[2]
    groups = samples // GROUP
    in_sems, out_sems = r.in_sems, r.out_sems

    if remote:
        own = (r.sqw_v, r.mlpw_v, r.gain_v)
    else:
        own = (r.sq_all, r.mlp_all, r.gain_all)
    loads = list(zip((r.sqw, r.mlpw, r.gain), own))
    loads += [(r.acts, r.acts_v), (r.obs, r.obs_v.at[pl.ds(0, keys)]), (r.cot, r.cot_v)]
    if remote:
        loads += [(r.sqm, r.sqm_v), (r.mlpm, r.mlpm_v)]
    loads += [(r.flags, r.flags_s), (r.levels, r.levels_s)]
    copies = [pltpu.make_async_copy(a, b, in_sems.at[i]) for i, (a, b) in enumerate(loads)]

    def arrive(*which):
        for i in which:
            copies[i].wait()

    for copy in copies:
        copy.start()
    if remote:
        gather, update = Gather(r), Update(r)
        expected = greet_all()
        arrive(0, 1, 2)
        gather.fill()
        pl.semaphore_wait(pltpu.get_barrier_semaphore(), expected)
        gather.first(3, 4)

    arrive(3)

    def hats(i, _):
        rows = pl.ds(pl.multiple_of(i * ROWS, ROWS), ROWS)
        hat, scale = normalize(r.acts_v[rows, :])
        r.xhat[rows, :] = hat
        r.rstd[rows, :] = scale
        return 0

    lax.fori_loop(0, tokens // ROWS, hats, 0)

    mem, obs_v = r.mem, r.obs_v
    batch = 16
    chunks = KEYS_PAD // batch
    swap = r.swap
    row = lax.broadcasted_iota(jnp.int32, swap.shape, 0)
    column = lax.broadcasted_iota(jnp.int32, swap.shape, 1)
    swap[...] = jnp.where(column == (row % batch) * batch + row // batch, 1.0, 0.0).astype(BF16)

    def turn(part, low, high):
        def one(j, _):
            at = pl.ds(pl.multiple_of(j * batch, batch), batch)
            here = pl.ds(part * batch, batch)
            block = obs_v[at, here, :].reshape(batch * batch, width)
            mem[here, at, :] = dot(swap[...], block).astype(BF16).reshape(batch, batch, width)
            return 0

        lax.fori_loop(low, high, one, 0)

    whole = chunks - 1
    arrive(4)
    turn(0, 0, whole // 2)
    if remote:
        gather.second(3, 4)
        gather.first(2, 0, 1)
    turn(0, whole // 2, whole)
    if remote:
        gather.third(3, 4)
    turn(1, 0, whole // 2)
    if remote:
        gather.second(2, 0, 1)
        gather.fourth(3, 4)
    turn(1, whole // 2, whole)
    arrive(len(copies) - 1, len(copies) - 2)
    freqs = jnp.exp(
        lax.broadcasted_iota(jnp.int32, (1, half), 1).astype(F32) * F32(-math.log(10000.0)) / half
    )
    for s in range(samples):
        r.angle[s : s + 1, :] = r.levels_s[s].astype(F32) * freqs
    r.embed[:, 0:half] = jnp.sin(r.angle[...]).astype(BF16)
    r.embed[:, half:width] = jnp.cos(r.angle[...]).astype(BF16)
    if remote:
        arrive(6, 7)
        update.old_moment()
        gather.third(2, 0, 1)
        gather.last(3, 4)
        for m in range(3):
            gather.unpack(SQ_AT[m], 1, r.sq_all, m)
        gather.unpack_gains()
    else:
        arrive(0, 1, 2)

    sq, mlp = r.sq_all, r.mlp_all
    wkh, wvh = r.wkh, r.wvh
    lane = lax.broadcasted_iota(jnp.int32, (width, width), 1)

    def split_heads(out, weight):
        weight = weight.astype(F32)
        for h in range(HEADS):
            out[pl.ds(h * width, width), :] = jnp.where(lane // head_dim == h, weight, 0.0).astype(BF16)

    split_heads(wkh, sq[2])
    g1, g2 = r.gain_all[0:1, :], r.gain_all[1:2, :]

    obs_v[keys] = dot(r.embed[...], sq[0]).astype(BF16)
    obs_v[keys + 1 :] = jnp.zeros((KEYS_PAD - keys - 1, samples, width), BF16)
    for part in range(samples // batch):
        turn(part, whole, chunks)

    sides, weights = r.sides_v, r.pds_v

    def make_queries(i, _):
        rows = pl.ds(pl.multiple_of(i * ROWS, ROWS), ROWS)
        first = (r.xhat[rows, :] * g1).astype(BF16)
        r.first[rows, :] = first
        q = dot(first, sq[1]).astype(BF16)
        r.query[rows, :] = q
        here = pl.ds(i * per, per)
        for h in range(HEADS):
            wk = wkh[pl.ds(h * width, width), :]
            value = (dot(q, wk, NT) * 0.125).astype(BF16).reshape(per, ACT, width)
            sides[here, pl.ds((HEADS + h) * ACT, ACT), :] = value
        return 0

    lax.fori_loop(0, tokens // ROWS, make_queries, 0)

    key = lax.broadcasted_iota(jnp.int32, (1, KEYS_PAD), 1)
    low_rows, high_rows = pl.ds(0, HEADS * ACT), pl.ds(HEADS * ACT, HEADS * ACT)

    def attend(g, _):
        ids = [g * GROUP + k for k in range(GROUP)]
        scores = [dot(sides[s, high_rows, :], mem[s], NT) for s in ids]
        lows = []
        for s, score in zip(ids, scores):
            count = OBS_FEW + (OBS_FULL - OBS_FEW) * r.flags_s[s]
            score = score + jnp.where((key < count) | (key == OBS_FULL), 0.0, -1000000000.0)
            expo = jnp.exp(score - jnp.max(score, -1, keepdims=True))
            probs = expo * (1.0 / jnp.sum(expo, -1, keepdims=True))
            r.probs[s] = probs
            low = probs.astype(BF16)
            weights[s, low_rows, :] = low
            lows.append(low)
        for s, low in zip(ids, lows):
            u = dot(low, mem[s]).astype(BF16)
            rows = pl.ds(pl.multiple_of(s * ACT, ACT), ACT)
            for h in range(HEADS):
                r.u[rows, pl.ds(h * width, width)] = u[h * ACT : (h + 1) * ACT, :]
        return 0

    lax.fori_loop(0, groups // 2, attend, 0)
    if remote:
        gather.fourth(2, 0, 1)
    lax.fori_loop(groups // 2, groups, attend, 0)
    if remote:
        gather.last(2, 0, 1)
        for m in range(3, 5):
            gather.unpack(SQ_AT[m], 1, sq, m)
        for m in range(2):
            gather.unpack(m * MLP_ROWS, 4, mlp, m)
    split_heads(wvh, sq[3])

    gain_acc = r.gain_acc
    gain_acc[...] = jnp.zeros_like(gain_acc)
    arrive(5)

    def feed(i, _):
        rows = pl.ds(pl.multiple_of(i * ROWS, ROWS), ROWS)
        mixed = dot(r.u[rows, :], wvh[...]).astype(BF16)
        r.mixed[rows, :] = mixed
        resid = r.acts_v[rows, :] + dot(mixed, sq[4])
        hat, scale = normalize(resid)
        second = (hat * g2).astype(BF16)
        r.second[rows, :] = second
        cot = r.cot_v[rows, :]
        out_low = cot.astype(BF16)
        r.out_low[rows, :] = out_low
        for c in range(wide // 256):
            columns = pl.ds(c * 256, 256)
            v = dot(second, mlp[0, :, columns])
            square = v * v
            t = jnp.tanh(0.7978845608 * (v + 0.044715 * square * v))
            r.active[rows, columns] = (0.5 * v * (1.0 + t)).astype(BF16)
            slope = 0.5 * (1.0 + t) + 0.5 * v * (1.0 - t * t) * (0.7978845608 * (1.0 + 0.134145 * square))
            r.dhidden[rows, columns] = (slope * dot(out_low, mlp[1, :, columns])).astype(BF16)
        r.out_v[rows, :] = resid + dot(r.active[rows, :], mlp[1], NT)
        grad_second = dot(r.dhidden[rows, :], mlp[0], NT)
        gain_acc[1:2, :] += jnp.sum(grad_second * hat, 0, keepdims=True)
        dres = cot + norm_back(grad_second * g2, hat, scale)
        r.dres[rows, :] = dres
        low = dres.astype(BF16)
        r.dres_low[rows, :] = low
        gm = dot(low, sq[4], NT).astype(BF16)
        r.dmixed[rows, :] = gm
        here = pl.ds(i * per, per)
        for h in range(HEADS):
            wv = wvh[pl.ds(h * width, width), :]
            sides[here, pl.ds(h * ACT, ACT), :] = dot(gm, wv, NT).astype(BF16).reshape(per, ACT, width)
        return 0

    lax.fori_loop(0, tokens // ROWS, feed, 0)
    keep_out = pltpu.make_async_copy(r.out_v, r.output, out_sems.at[0])
    keep_out.start()

    grads = r.grads

    def put(base, tiles, value):
        for j in range(tiles):
            part = value[:, j * LANES : (j + 1) * LANES].reshape(GRID + (TILE, LANES))
            grads[:, :, :, :, pl.ds(base + j * TILE, TILE), :] = part

    def by_head(left, right):
        turned = left.T
        parts = [
            dot(turned[h * head_dim : (h + 1) * head_dim, :], right[:, pl.ds(h * width, width)])
            for h in range(HEADS)
        ]
        return jnp.concatenate(parts, axis=0).T

    put(0, 8, dot(r.second[...], r.dhidden[...], TN))
    if remote:
        update.start(0)
    put(MLP_ROWS, 8, dot(r.out_low[...], r.active[...], TN))
    if remote:
        update.start(1)
    put(SQ_AT[4], 2, dot(r.mixed[...], r.dres_low[...], TN))
    put(SQ_AT[3], 2, by_head(r.dmixed[...], r.u))
    if remote:
        update.start(2)

    def attend_back(g, _):
        ids = [g * GROUP + k for k in range(GROUP)]
        rises = [dot(sides[s, low_rows, :], mem[s], NT) for s in ids]
        for s, rise in zip(ids, rises):
            probs = r.probs[s]
            both = probs * rise
            weights[s, high_rows, :] = (both - probs * jnp.sum(both, -1, keepdims=True)).astype(BF16)
        for s in ids:
            dq = (dot(weights[s, high_rows, :], mem[s]) * 0.125).astype(BF16)
            rows = pl.ds(pl.multiple_of(s * ACT, ACT), ACT)
            for h in range(HEADS):
                r.dq_wide[rows, pl.ds(h * width, width)] = dq[h * ACT : (h + 1) * ACT, :]
            end = dot(weights[s, :, LANES:KEYS_PAD], sides[s], TN)
            r.stamps[s] = end[64:72, :]
        return 0

    half_groups = groups // 2
    lax.fori_loop(0, half_groups, attend_back, 0)
    if remote:
        update.one(0)
    lax.fori_loop(half_groups, groups, attend_back, 0)
    put(SQ_AT[2], 2, by_head(r.query[...], r.dq_wide))
    stamp_low = r.stamps[:, 4:5, :].reshape(samples, width).astype(BF16)
    put(SQ_AT[0], 2, dot(r.embed[...], stamp_low, TN))
    if remote:
        update.start(3)
        update.one(1, 2)

    def memory_back(low, high):
        def one(g, _):
            for k in range(GROUP):
                s = g * GROUP + k
                mem[s] = dot(weights[s], sides[s], TN).astype(BF16)
            return 0

        lax.fori_loop(low, high, one, 0)

    def turn_back(part):
        def one(j, _):
            at = pl.ds(pl.multiple_of(j * batch, batch), batch)
            here = pl.ds(part * batch, batch)
            block = mem[here, at, :].reshape(batch * batch, width)
            obs_v[at, here, :] = dot(swap[...], block).astype(BF16).reshape(batch, batch, width)
            return 0

        lax.fori_loop(0, chunks, one, 0)

    def queries_back(i, _):
        rows = pl.ds(pl.multiple_of(i * ROWS, ROWS), ROWS)
        r.dquery[rows, :] = dot(r.dq_wide[rows, :], wkh[...]).astype(BF16)
        return 0

    lax.fori_loop(0, tokens // ROWS, queries_back, 0)
    put(SQ_AT[1], 2, dot(r.first[...], r.dquery[...], TN))
    if remote:
        update.start(4)

    def acts_back(i, _):
        rows = pl.ds(pl.multiple_of(i * ROWS, ROWS), ROWS)
        grad_first = dot(r.dquery[rows, :], sq[1], NT)
        hat = r.xhat[rows, :]
        gain_acc[0:1, :] += jnp.sum(grad_first * hat, 0, keepdims=True)
        r.ag_v[rows, :] = r.dres[rows, :] + norm_back(grad_first * g1, hat, r.rstd[rows, :])
        return 0

    def finish_acts():
        lax.fori_loop(0, tokens // ROWS, acts_back, 0)
        for norm in range(2):
            for j in range(2):
                row = gain_acc[norm : norm + 1, j * LANES : (j + 1) * LANES]
                at = GAIN_BASE + norm * 2 + j
                value = jnp.broadcast_to(row.reshape(1, 1, 1, 1, 1, LANES), GRID + (1, LANES))
                grads[:, :, :, :, at : at + 1, :] = value
        rest = WIRE - GAIN_BASE - 4
        grads[:, :, :, :, GAIN_BASE + 4 : WIRE, :] = jnp.zeros(GRID + (rest, LANES), F32)

    keep_ag = pltpu.make_async_copy(r.ag_v, r.ag, out_sems.at[2])
    keep_og = pltpu.make_async_copy(obs_v.at[pl.ds(0, keys)], r.og, out_sems.at[1])
    if remote:
        update.two(0)
        update.one(3)
        finish_acts()
        keep_ag.start()
        update.start(5)
        update.two(1, 2)
        update.one(4)
        memory_back(0, half_groups)
        update.two(3)
        update.one(5)
        update.three(0, 1)
        update.two(4)
        memory_back(half_groups, groups)
        update.three(2, 3, 4)
        update.two(5)
        update.four(0, 1)
        turn_back(0)
        update.four(2, 3, 4)
        update.three(5)
        update.orthogonalize()
        update.give_all()
        turn_back(1)
        keep_og.start()
        update.four(5)
        out = r.out
        out[1, :, :] = r.moment[...]
        out[2, pl.ds(GAIN_BASE, 16), :] = jnp.zeros((16, LANES), F32)
        gather.drain()
        update.drain()
        update.take_all()
        update.drain_owner()
    else:
        finish_acts()
        keep_ag.start()
        memory_back(0, groups)
        for part in range(samples // batch):
            turn_back(part)
        keep_og.start()
    for copy in (keep_out, keep_og, keep_ag):
        copy.wait()


def block_and_back(remote, acts, obs, flags, levels, cot, sqw, mlpw, gain, sqm=None, mlpm=None):
    tokens, width = acts.shape
    keys, samples = obs.shape[0], obs.shape[1]
    rows = HEADS * ACT
    wide = mlpw.shape[2]
    any_space = pl.BlockSpec(memory_space=pl.ANY)
    in_vmem = pl.BlockSpec(memory_space=VMEM)
    sem = pltpu.SemaphoreType.DMA
    ins = dict(flags=flags, levels=levels, acts=acts, obs=obs, cot=cot, sqw=sqw, mlpw=mlpw, gain=gain)
    outs = dict(
        output=jax.ShapeDtypeStruct(acts.shape, F32),
        ag=jax.ShapeDtypeStruct(acts.shape, F32),
        og=jax.ShapeDtypeStruct(obs.shape, BF16),
    )
    grads = GRID + (WIRE, LANES)
    scratch = dict(
        obs_v=VMEM((KEYS_PAD, samples, width), BF16),
        acts_v=VMEM(acts.shape, F32),
        cot_v=VMEM(acts.shape, F32),
        mem=VMEM((samples, KEYS_PAD, width), BF16),
        swap=VMEM((256, 256), BF16),
        sq_all=VMEM((5, width, width), BF16),
        mlp_all=VMEM((2, width, wide), BF16),
        gain_all=VMEM((2, width), F32),
        wkh=VMEM((HEADS * width, width), BF16),
        wvh=VMEM((HEADS * width, width), BF16),
        first=VMEM((tokens, width), BF16),
        query=VMEM((tokens, width), BF16),
        xhat=VMEM((tokens, width), F32),
        rstd=VMEM((tokens, 1), F32),
        probs=VMEM((samples, rows, KEYS_PAD), F32),
        pds_v=VMEM((samples, 2 * rows, KEYS_PAD), BF16),
        sides_v=VMEM((samples, 2 * rows, width), BF16),
        u=VMEM((tokens, HEADS * width), BF16),
        dq_wide=VMEM((tokens, HEADS * width), BF16),
        mixed=VMEM((tokens, width), BF16),
        second=VMEM((tokens, width), BF16),
        active=VMEM((tokens, wide), BF16),
        dhidden=VMEM((tokens, wide), BF16),
        out_low=VMEM((tokens, width), BF16),
        dres_low=VMEM((tokens, width), BF16),
        dres=VMEM((tokens, width), F32),
        dmixed=VMEM((tokens, width), BF16),
        dquery=VMEM((tokens, width), BF16),
        out_v=VMEM((tokens, width), F32),
        ag_v=VMEM((tokens, width), F32),
        angle=VMEM((samples, width // 2), F32),
        embed=VMEM((samples, width), BF16),
        stamps=VMEM((samples, 8, width), F32),
        gain_acc=VMEM((8, width), F32),
        flags_s=pltpu.SMEM(flags.shape, jnp.int32),
        levels_s=pltpu.SMEM(levels.shape, jnp.int32),
        in_sems=sem((10,)),
        out_sems=sem((3,)),
    )
    extra = {}
    if remote:
        ins.update(sqm=sqm, mlpm=mlpm)
        outs.update(out=jax.ShapeDtypeStruct((3, WIRE, LANES), F32))
        chunks = len(CHUNKS)
        scratch.update(
            grads=VMEM(grads, F32),
            sqw_v=VMEM(sqw.shape, F32),
            mlpw_v=VMEM(mlpw.shape, F32),
            gain_v=VMEM(gain.shape, F32),
            sqm_v=VMEM(sqm.shape, F32),
            mlpm_v=VMEM(mlpm.shape, F32),
            wire=VMEM(grads, BF16),
            edge=VMEM((16, LANES), F32),
            gsend=sem((chunks, 6)),
            grecv=sem((chunks, 6)),
            send0=VMEM((4, 2, 2, WIRE, LANES), BF16),
            got_core=VMEM((4, 2, 2, WIRE, LANES), BF16),
            sum1=VMEM((4, 2, 2, WIRE, LANES), F32),
            send1=VMEM((4, 2, WIRE, LANES), BF16),
            got1=VMEM((4, 2, WIRE, LANES), BF16),
            sum2=VMEM((4, 2, WIRE, LANES), F32),
            send2=VMEM((4, WIRE, LANES), BF16),
            got2=VMEM((4, WIRE, LANES), BF16),
            sum3=VMEM((4, WIRE, LANES), F32),
            send3=VMEM((3, WIRE, LANES), BF16),
            got3=VMEM((3, WIRE, LANES), BF16),
            moment=VMEM((WIRE, LANES), F32),
            slabs_sq=VMEM((32, SQ_ROWS, LANES), F32),
            slabs_mlp=VMEM((32, MLP_ROWS, LANES), BF16),
            moment_low=VMEM((2 * MLP_ROWS, LANES), BF16),
            back_mlp=VMEM((2, MLP_ROWS, LANES), BF16),
            result_sq=VMEM((32, SQ_ROWS, LANES), F32),
            result_mlp=VMEM((32, MLP_ROWS, LANES), BF16),
            cur=VMEM((width, wide), F32),
            cur_low=VMEM((width, wide), BF16),
            send=sem((chunks, 6)),
            recv=sem((chunks, 6)),
            own_send=sem((7,)),
            own_recv=sem((1,)),
            back_send=sem((32,)),
            back_recv=sem((7,)),
        )
        extra = dict(collective_id=0, has_side_effects=True)
        outs = {name: VMEM(like.shape, like.dtype) for name, like in outs.items()}
    else:
        outs.update(grads=jax.ShapeDtypeStruct(grads, F32))
    names = tuple(ins) + tuple(outs) + tuple(scratch)
    stay = [pltpu.with_memory_space_constraint(value, pltpu.HBM) for value in ins.values()]
    results = pl.pallas_call(
        functools.partial(block_kernel, names, remote),
        out_shape=tuple(outs.values()),
        in_specs=[any_space] * len(ins),
        out_specs=[any_space] * 3 + [in_vmem],
        scratch_shapes=list(scratch.values()),
        compiler_params=pltpu.CompilerParams(vmem_limit_bytes=46 << 20, **extra),
        name="block_and_back",
    )(*stay)
    return Refs(zip(outs, results))


PARTS = 7


def finish_kernel(names, rate, *args):
    r = Refs(zip(names, args))
    sems = r.sems
    keys = r.og.shape[0]
    step = keys // PARTS

    def leave(part):
        block = pl.ds(part * step, step)
        return pltpu.make_async_copy(r.og_v.at[block], r.og.at[block], sems.at[part])

    more = PARTS
    moves = []
    if hasattr(r, "wire"):
        pairs = [(r.sqw, r.sqw_v), (r.mlpw, r.mlpw_v), (r.gain, r.gain_v), (r.gainm, r.gainm_v)]
        pairs += [(r.output, r.output_f), (r.ag, r.ag_f)]
        for source, target in pairs:
            moves.append(pltpu.make_async_copy(source, target, sems.at[more]))
            moves[-1].start()
            more += 1
    for part in range(PARTS):

        def widen(j, _):
            r.og_v[j] = r.low[j].astype(F32)
            return 0

        lax.fori_loop(part * step, (part + 1) * step, widen, 0, unroll=4)
        leave(part).start()
    for copy in moves[:4]:
        copy.wait()
    if hasattr(r, "wire"):
        finish_weights(r, rate)
    for part in range(PARTS):
        leave(part).wait()
    for copy in moves[4:]:
        copy.wait()


def finish_weights(r, rate):
    wire = r.wire
    me = lax.axis_index("dp")
    for m in range(5):
        for j in range(2):
            rows, columns = pl.ds(SQ_AT[m] + j * TILE, TILE), pl.ds(j * LANES, LANES)
            r.sqg[m, :, columns] = wire[0, rows, :]
            r.sqm[m, :, columns] = wire[1, rows, :]
            r.sqn[m, :, columns] = r.sqw_v[m, :, columns] - SQ_RATES[m] * wire[2, rows, :]
    r.sqc[...] = r.sqn[...].astype(BF16)
    for m in range(2):
        for j in range(8):
            rows, columns = pl.ds(m * MLP_ROWS + j * TILE, TILE), pl.ds(j * LANES, LANES)
            r.mlpg[m, :, columns] = wire[0, rows, :]
            r.mlpm[m, :, columns] = wire[1, rows, :]
            r.mlpn[m, :, columns] = r.mlpw_v[m, :, columns] - MLP_RATES[m] * wire[2, rows, :]
    r.mlpc[...] = r.mlpn[...].astype(BF16)
    tile = wire[0, pl.ds(GAIN_BASE, TILE), :]
    turned = pltpu.roll(tile, (LANES - (me % 16) * TILE) % LANES, 1)
    at = me // 16
    for norm in range(2):
        pair = turned[2 * norm : 2 * norm + 2, 0:TILE]
        row = jnp.where(at == 0, pair[0:1, :], pair[1:2, :])
        new = 0.5 * r.gainm_v[norm : norm + 1, :] + row
        r.gg[norm : norm + 1, :] = row
        r.gm[norm : norm + 1, :] = new
        r.gn[norm : norm + 1, :] = r.gain_v[norm : norm + 1, :] - rate * new


def finish(rate, made, sqw=None, mlpw=None, gain=None, gainm=None):
    any_space = pl.BlockSpec(memory_space=pl.ANY)
    in_vmem = pl.BlockSpec(memory_space=VMEM)
    ins = dict(low=made.og)
    outs = dict(og=jax.ShapeDtypeStruct(made.og.shape, F32))
    near, far = 1, 1
    if hasattr(made, "out"):
        ins.update(output=made.output, ag=made.ag, wire=made.out, sqw=sqw, mlpw=mlpw, gain=gain, gainm=gainm)
        like = jax.ShapeDtypeStruct
        near, far = 4, 3
        outs.update(
            output_f=like(made.output.shape, F32),
            ag_f=like(made.ag.shape, F32),
            sqg=like(sqw.shape, F32),
            sqm=like(sqw.shape, F32),
            sqn=like(sqw.shape, F32),
            sqc=like(sqw.shape, BF16),
            mlpg=like(mlpw.shape, F32),
            mlpm=like(mlpw.shape, F32),
            mlpn=like(mlpw.shape, F32),
            mlpc=like(mlpw.shape, BF16),
            gg=like(gain.shape, F32),
            gm=like(gain.shape, F32),
            gn=like(gain.shape, F32),
        )
    scratch = dict(
        og_v=VMEM(made.og.shape, F32),
        sems=pltpu.SemaphoreType.DMA((PARTS + 6,)),
    )
    if hasattr(made, "out"):
        scratch.update(
            sqw_v=VMEM(sqw.shape, F32),
            mlpw_v=VMEM(mlpw.shape, F32),
            gain_v=VMEM(gain.shape, F32),
            gainm_v=VMEM(gainm.shape, F32),
        )
    names = tuple(ins) + tuple(outs) + tuple(scratch)
    made_here = list(ins.values())
    stay = [pltpu.with_memory_space_constraint(value, pltpu.HBM) for value in made_here[near:]]
    results = pl.pallas_call(
        functools.partial(finish_kernel, names, rate),
        out_shape=tuple(outs.values()),
        in_specs=[in_vmem] * near + [any_space] * (len(ins) - near),
        out_specs=[any_space] * far + [in_vmem] * (len(outs) - far),
        scratch_shapes=list(scratch.values()),
        compiler_params=pltpu.CompilerParams(vmem_limit_bytes=16 << 20),
        name="finish",
    )(*made_here[:near], *stay)
    return Refs(zip(outs, results))


HIGH_PRECISION = lax.Precision.HIGHEST


def plain_orthogonalize(matrix):
    current = matrix / (jnp.sqrt(jnp.sum(matrix * matrix)) + 1e-07)
    for turn in range(5):
        gram = jnp.dot(current, current.T, precision=HIGH_PRECISION)
        poly = COEF_B * gram + COEF_C * jnp.dot(gram, gram, precision=HIGH_PRECISION)
        current = COEF_A * current + jnp.dot(poly, current, precision=HIGH_PRECISION)
    return current


def pick_owned(stack, owners, device):
    chosen = jnp.zeros_like(stack[0])
    for index in range(len(owners)):
        chosen = jnp.where(device == owners[index], stack[index], chosen)
    return chosen


def is_owner(owners, device):
    flag = device < 0
    for owner in owners:
        flag = jnp.logical_or(flag, device == owner)
    return flag


def from_wire(grads):
    def matrix(base, tiles):
        part = grads[:, base : base + tiles * TILE, :].reshape(-1, tiles, TILE, LANES)
        return part.transpose(0, 2, 1, 3).reshape(-1, tiles * LANES)

    square = jnp.stack([matrix(SQ_AT[m], 2) for m in range(5)])
    mlp = jnp.stack([matrix(m * MLP_ROWS, 8) for m in range(2)])
    return square, mlp, grads[0, GAIN_BASE : GAIN_BASE + 4, :].reshape(2, 2 * LANES)


def update_by_collectives(
    grads, square_weights, mlp_weights, gains, square_moment, mlp_moment, gain_moment, rate
):
    square_local, mlp_local, gain_local = from_wire(grads)
    square_grad, mlp_grad, gain_grad = (
        lax.psum_scatter(square_local, "dp", scatter_dimension=1, tiled=True),
        lax.psum_scatter(mlp_local, "dp", scatter_dimension=1, tiled=True),
        lax.psum_scatter(gain_local, "dp", scatter_dimension=1, tiled=True),
    )
    square_moment_new = 0.5 * square_moment + square_grad
    mlp_moment_new = 0.5 * mlp_moment + mlp_grad
    gain_moment_new = 0.5 * gain_moment + gain_grad
    device = lax.axis_index("dp")
    count = lax.axis_size("dp")
    square_owners = [index * count // 7 for index in range(5)]
    mlp_owners = [(index + 5) * count // 7 for index in range(2)]
    square_full, mlp_full = (
        lax.all_gather(square_moment_new, "dp", axis=1, tiled=True),
        lax.all_gather(mlp_moment_new, "dp", axis=1, tiled=True),
    )
    mine_square = pick_owned(square_full, square_owners, device)
    mine_mlp = pick_owned(mlp_full, mlp_owners, device)
    made_square = lax.cond(
        is_owner(square_owners, device), plain_orthogonalize, jnp.zeros_like, mine_square
    )
    made_mlp = lax.cond(is_owner(mlp_owners, device), plain_orthogonalize, jnp.zeros_like, mine_mlp)
    stack_square = jnp.stack(
        [jnp.where(device == owner, made_square, 0.0) for owner in square_owners]
    )
    stack_mlp = jnp.stack([jnp.where(device == owner, made_mlp, 0.0) for owner in mlp_owners])
    square_ortho, mlp_ortho = (
        lax.psum_scatter(stack_square, "dp", scatter_dimension=1, tiled=True),
        lax.psum_scatter(stack_mlp, "dp", scatter_dimension=1, tiled=True),
    )
    square_new = square_weights - jnp.array(SQ_RATES, F32)[:, None, None] * square_ortho
    mlp_new = mlp_weights - jnp.array(MLP_RATES, F32)[:, None, None] * mlp_ortho
    gains_new = gains - rate * gain_moment_new
    return (
        square_grad,
        square_moment_new,
        square_new,
        square_new.astype(BF16),
        mlp_grad,
        mlp_moment_new,
        mlp_new,
        mlp_new.astype(BF16),
        gain_grad,
        gain_moment_new,
        gains_new,
    )


def per_device(
    actions,
    observed,
    camera_flags,
    noise_levels,
    cotangent,
    square_weights,
    mlp_weights,
    gains,
    square_moment,
    mlp_moment,
    gain_moment,
):
    count = lax.axis_size("dp")
    rate = 0.1 / math.sqrt(actions.shape[0] * count)
    by_key = observed.transpose(1, 0, 2)
    ins = (actions, by_key, camera_flags, noise_levels, cotangent)
    if count == math.prod(GRID):
        made = block_and_back(True, *ins, square_weights, mlp_weights, gains, square_moment, mlp_moment)
        done = finish(rate, made, square_weights, mlp_weights, gains, gain_moment)
        output, actions_grad = done.output_f, done.ag_f
        d = done
        rest = (d.sqg, d.sqm, d.sqn, d.sqc, d.mlpg, d.mlpm, d.mlpn, d.mlpc, d.gg, d.gm, d.gn)
    else:
        square_all, mlp_all = (
            lax.all_gather(square_weights.astype(BF16), "dp", axis=1, tiled=True),
            lax.all_gather(mlp_weights.astype(BF16), "dp", axis=1, tiled=True),
        )
        gain_all = lax.all_gather(gains, "dp", axis=1, tiled=True)
        made = block_and_back(False, *ins, square_all, mlp_all, gain_all)
        done = finish(rate, made)
        output, actions_grad = made.output, made.ag
        grads = made.grads.reshape(-1, WIRE, LANES)
        rest = update_by_collectives(
            grads, square_weights, mlp_weights, gains, square_moment, mlp_moment, gain_moment, rate
        )
    observed_grad = done.og.transpose(1, 0, 2)
    return (output, actions_grad, observed_grad) + tuple(rest)


def solution(mesh):
    rows, cube, flat = P("dp", None), P("dp", None, None), P("dp")
    stacked, pair = P(None, "dp", None), P(None, "dp")
    return jax.shard_map(
        per_device,
        mesh=mesh,
        in_specs=(rows, cube, flat, flat, rows, stacked, stacked, pair, stacked, stacked, pair),
        out_specs=(rows, rows, cube) + (stacked,) * 8 + (pair,) * 3,
        check_vma=False,
    )
```

```python
import functools
import math

import jax
import jax.numpy as jnp
from jax import lax
from jax.experimental import pallas as pl
from jax.experimental.pallas import tpu as pltpu
from jax.sharding import PartitionSpec as P

HEADS = 4
ACT = 16
OBS_FULL = 196
OBS_FEW = 49
COEF_A = 3.4445
COEF_B = -4.775
COEF_C = 2.0315
F32 = jnp.float32
BF16 = jnp.bfloat16
MESH = pl.DeviceIdType.MESH
VMEM = pltpu.VMEM
NN = (((1,), (0,)), ((), ()))
NT = (((1,), (1,)), ((), ()))
TN = (((0,), (0,)), ((), ()))

LANES = 128
TILE = 8
MLP_ROWS = 64
SQ_ROWS = 16
SQ_AT = (160, 192, 176, 128, 144)
GAIN_BASE = 208
WIRE = 224
PIECES = ((0, 64), (64, 64), (128, 32), (160, 32), (192, 32))
PIECE_X_FIRST = (True, False, True, True, False)
CHUNKS = ((0, 64), (64, 64), (128, 32), (160, 32), (192, 16), (208, 16))
X_FIRST = (True, False, True, False, True, False)
COMPLETES = ((0,), (1,), (5, 6), (2, 4), (3,), ())
MLP_RATES = (1.0, 0.5)
SQ_RATES = (0.5, 0.5, 0.5, 0.5, 4.0)
GRID = (4, 2, 2, 2)
OWNERS = (8, 22, 14, 16, 11, 21, 13)
SHIFTS = (0.0, 0.0, 0.4, 0.8, 0.8)
KEYS_PAD = 208
GROUP = 8
ROWS = 256


class Refs:
    def __init__(self, pairs):
        self.__dict__.update(pairs)


def dot(left, right, dims=NN):
    return lax.dot_general(left, right, dims, preferred_element_type=F32)


def place():
    me = lax.axis_index("dp")
    return me, me // 8, (me // 4) % 2, (me // 2) % 2, me % 2


def device_at(z, y, x, c):
    return ((z * 2 + y) * 2 + x) * 2 + c


def link(src, dst, send, recv, device):
    return pltpu.make_async_remote_copy(
        src_ref=src,
        dst_ref=dst,
        send_sem=send,
        recv_sem=recv,
        device_id=(device,),
        device_id_type=MESH,
    )


def greet(device):
    pl.semaphore_signal(
        pltpu.get_barrier_semaphore(), inc=1, device_id=(device,), device_id_type=MESH
    )


def normalize(values):
    centred = values - jnp.mean(values, -1, keepdims=True)
    scale = lax.rsqrt(jnp.mean(centred * centred, -1, keepdims=True) + 1e-05)
    return centred * scale, scale


def norm_back(grad, hat, scale):
    mean_one = jnp.mean(grad, -1, keepdims=True)
    mean_two = jnp.mean(grad * hat, -1, keepdims=True)
    return scale * (grad - mean_one - hat * mean_two)


class Gather:
    def __init__(self, r):
        self.r = r
        self.me, self.z, self.y, self.x, self.c = place()

    def hop(self, k, step, part, device):
        return link(part, part, self.r.gsend.at[k, step], self.r.grecv.at[k, step], device)

    def along_z(self, k, step):
        part = self.r.wire.at[self.z, self.y, self.x, self.c, pl.ds(*PIECES[k])]
        return self.hop(k, step, part, device_at((self.z + step + 1) % 4, self.y, self.x, self.c))

    def from_z(self, k, step):
        there = (self.z + 3 - step) % 4
        part = self.r.wire.at[there, self.y, self.x, self.c, pl.ds(*PIECES[k])]
        return self.hop(k, step, part, device_at(there, self.y, self.x, self.c))

    def plane(self, k, second, mine):
        z, y, x, c = self.z, self.y, self.x, self.c
        rows, wire = pl.ds(*PIECES[k]), self.r.wire
        py, px = (y, x) if mine else (1 - y, 1 - x)
        along_x = PIECE_X_FIRST[k] == second
        if along_x:
            part = wire.at[:, y, px, c, rows] if second else wire.at[:, :, px, c, rows]
            return self.hop(k, 3 if second else 4, part, device_at(z, y, 1 - x, c))
        part = wire.at[:, py, x, c, rows] if second else wire.at[:, py, :, c, rows]
        return self.hop(k, 3 if second else 4, part, device_at(z, 1 - y, x, c))

    def core(self, k, mine):
        part = self.r.wire.at[:, :, :, self.c if mine else 1 - self.c, pl.ds(*PIECES[k])]
        return self.hop(k, 5, part, device_at(self.z, self.y, self.x, 1 - self.c))

    def first(self, *chunks):
        for k in chunks:
            for step in range(3):
                self.along_z(k, step).start()

    def second(self, *chunks):
        for k in chunks:
            for step in range(3):
                self.from_z(k, step).wait_recv()
            self.plane(k, True, True).start()

    def third(self, *chunks):
        for k in chunks:
            self.plane(k, True, False).wait_recv()
            self.plane(k, False, True).start()

    def fourth(self, *chunks):
        for k in chunks:
            self.plane(k, False, False).wait_recv()
            self.core(k, True).start()

    def last(self, *chunks):
        for k in chunks:
            self.core(k, False).wait_recv()

    def drain(self):
        for k in range(len(PIECES)):
            for step in range(3):
                self.along_z(k, step).wait_send()
            self.plane(k, True, True).wait_send()
            self.plane(k, False, True).wait_send()
            self.core(k, True).wait_send()

    def fill(self):
        r = self.r
        spot = (self.z, self.y, self.x, self.c)

        def tiles(source, m, base, number):
            for j in range(number):
                pair = [source[m, :, pl.ds((2 * j + k) * LANES, LANES)] for k in range(2)]
                r.wire[spot + (pl.ds(base + j * 16, 16),)] = jnp.concatenate(pair, axis=0).astype(BF16)

        for m in range(5):
            tiles(r.sqw_v, m, SQ_AT[m], 1)
        for m in range(2):
            tiles(r.mlpw_v, m, m * MLP_ROWS, 4)
        gains, edge = r.gain_v[...], r.edge
        high = gains.astype(BF16).astype(F32)
        middle = (gains - high).astype(BF16).astype(F32)
        edge[...] = jnp.zeros_like(edge)
        edge[0:2, 0:TILE] = high
        edge[2:4, 0:TILE] = middle
        edge[4:6, 0:TILE] = (gains - high - middle).astype(BF16).astype(F32)
        r.wire[spot + (pl.ds(GAIN_BASE, 16),)] = edge[...].astype(BF16)

    def unpack(self, base, number, out, m):
        for j in range(number):
            block = self.r.wire[:, :, :, :, pl.ds(base + j * 16, 16), :].reshape(32, 16, LANES).astype(F32)
            for half in range(2):
                columns = pl.ds((2 * j + half) * LANES, LANES)
                out[m, :, columns] = block[:, half * 8 : half * 8 + 8, :].reshape(256, LANES).astype(BF16)

    def unpack_gains(self):
        edge, wire = self.r.edge, self.r.wire
        for half in range(2):
            total = jnp.zeros((16, LANES), F32)
            for at in range(16):
                d = half * 16 + at
                tile = wire[d // 8, (d // 4) % 2, (d // 2) % 2, d % 2, pl.ds(GAIN_BASE, 16), :].astype(F32)
                total = total + (tile if at == 0 else pltpu.roll(tile, at * TILE, 1))
            edge[...] = total
            self.r.gain_all[:, pl.ds(half * LANES, LANES)] = edge[0:2, :] + edge[2:4, :] + edge[4:6, :]


class Update:
    def __init__(self, r):
        self.r = r
        self.me, self.z, self.y, self.x, self.c = place()

    def hop(self, k, step, src, dst, device):
        return link(src, dst, self.r.send.at[k, step], self.r.recv.at[k, step], device)

    def core(self, k):
        rows = pl.ds(*CHUNKS[k])
        src, dst = self.r.send0.at[:, :, :, rows], self.r.got_core.at[:, :, :, rows]
        return self.hop(k, 0, src, dst, device_at(self.z, self.y, self.x, 1 - self.c))

    def plane(self, k, first):
        rows = pl.ds(*CHUNKS[k])
        to = (self.z, self.y, 1 - self.x, self.c) if X_FIRST[k] == first else (self.z, 1 - self.y, self.x, self.c)
        if first:
            src, dst = self.r.send1.at[:, :, rows], self.r.got1.at[:, :, rows]
        else:
            src, dst = self.r.send2.at[:, rows], self.r.got2.at[:, rows]
        return self.hop(k, 1 if first else 2, src, dst, device_at(*to))

    def along_z(self, k, step):
        rows = pl.ds(*CHUNKS[k])
        to = device_at((self.z + step + 1) % 4, self.y, self.x, self.c)
        return self.hop(k, 3 + step, self.r.send3.at[step, rows], self.r.got3.at[step, rows], to)

    def start(self, k):
        rows = pl.ds(*CHUNKS[k])
        self.r.send0[:, :, :, rows, :] = self.r.grads[:, :, :, 1 - self.c, rows, :].astype(BF16)
        self.core(k).start()

    def one(self, *chunks):
        r = self.r
        for k in chunks:
            rows = pl.ds(*CHUNKS[k])
            self.core(k).wait_recv()
            sum1 = r.sum1
            sum1[:, :, :, rows, :] = r.grads[:, :, :, self.c, rows, :] + r.got_core[:, :, :, rows, :].astype(F32)
            other = sum1[:, :, 1 - self.x, rows, :] if X_FIRST[k] else sum1[:, 1 - self.y, :, rows, :]
            r.send1[:, :, rows, :] = other.astype(BF16)
            self.plane(k, True).start()

    def two(self, *chunks):
        r = self.r
        for k in chunks:
            rows = pl.ds(*CHUNKS[k])
            self.plane(k, True).wait_recv()
            sum1, sum2 = r.sum1, r.sum2
            mine = sum1[:, :, self.x, rows, :] if X_FIRST[k] else sum1[:, self.y, :, rows, :]
            sum2[:, :, rows, :] = mine + r.got1[:, :, rows, :].astype(F32)
            other = 1 - self.y if X_FIRST[k] else 1 - self.x
            r.send2[:, rows, :] = sum2[:, other, rows, :].astype(BF16)
            self.plane(k, False).start()

    def three(self, *chunks):
        r = self.r
        for k in chunks:
            rows = pl.ds(*CHUNKS[k])
            self.plane(k, False).wait_recv()
            mine = self.y if X_FIRST[k] else self.x
            r.sum3[:, rows, :] = r.sum2[:, mine, rows, :] + r.got2[:, rows, :].astype(F32)
            for step in range(3):
                r.send3[step, rows, :] = r.sum3[(self.z + step + 1) % 4, rows, :].astype(BF16)
                self.along_z(k, step).start()

    def slab(self, index):
        if index < 2:
            return pl.ds(index * MLP_ROWS, MLP_ROWS), self.r.slabs_mlp, self.r.result_mlp
        return pl.ds(SQ_AT[index - 2], SQ_ROWS), self.r.slabs_sq, self.r.result_sq

    def to_owner(self, index):
        rows, slabs, _ = self.slab(index)
        moment = self.r.moment_low if index < 2 else self.r.moment
        return link(
            moment.at[rows], slabs.at[self.me],
            self.r.own_send.at[index], self.r.own_recv.at[0], OWNERS[index],
        )

    def four(self, *chunks):
        r = self.r
        moment, out = r.moment, r.out
        for k in chunks:
            rows = pl.ds(*CHUNKS[k])
            total = r.sum3[self.z, rows, :]
            for step in range(3):
                self.along_z(k, step).wait_recv()
                total = total + r.got3[step, rows, :].astype(F32)
            out[0, rows, :] = total
            new = 0.5 * moment[rows, :] + total
            moment[rows, :] = new
            if k < 2:
                r.moment_low[rows, :] = new.astype(BF16)
            for index in COMPLETES[k]:
                rows_m, slabs, _ = self.slab(index)

                @pl.when(self.me != OWNERS[index])
                def _():
                    self.to_owner(index).start()

                @pl.when(self.me == OWNERS[index])
                def _():
                    mine = r.moment_low if index < 2 else moment
                    pltpu.make_async_copy(mine.at[rows_m], slabs.at[self.me], r.own_recv.at[0]).start()

    def old_moment(self):
        r = self.r
        moment = r.moment
        for m in range(2):
            for j in range(8):
                moment[pl.ds(m * MLP_ROWS + j * TILE, TILE), :] = r.mlpm_v[m, :, pl.ds(j * LANES, LANES)]
        for m in range(5):
            for j in range(2):
                moment[pl.ds(SQ_AT[m] + j * TILE, TILE), :] = r.sqm_v[m, :, pl.ds(j * LANES, LANES)]
        moment[pl.ds(GAIN_BASE, 16), :] = jnp.zeros((16, LANES), F32)

    def orthogonalize(self):
        r = self.r
        cur = r.cur
        rows = lax.broadcasted_iota(jnp.int32, (256, 256), 0)
        diagonal = rows == lax.broadcasted_iota(jnp.int32, (256, 256), 1)

        def run(slabs, result, tiles):
            pltpu.make_async_copy(slabs, slabs, r.own_recv.at[0]).wait()
            low = r.cur_low
            norm = jnp.zeros((1, 1), F32)
            for j in range(tiles // 2):
                pair = slabs[:, pl.ds(j * 16, 16), :].astype(F32)
                for side in range(2):
                    columns = pl.ds((2 * j + side) * LANES, LANES)
                    part = pair[:, side * TILE : (side + 1) * TILE, :].reshape(256, LANES)
                    cur[:, columns] = part
                    low[:, columns] = part.astype(BF16)
                    norm = norm + jnp.sum(jnp.sum(part * part, axis=0, keepdims=True), axis=1, keepdims=True)
            scale = 1.0 / (jnp.sqrt(norm) + 1e-07)

            def turn(k, _):
                first = jnp.where(k == 0, scale, 1.0)
                shift = jnp.where(k < 2, SHIFTS[0], jnp.where(k == 2, SHIFTS[2], SHIFTS[4]))
                whole = low[:, 0 : tiles * LANES]
                off = dot(whole, whole, NT) * (first * first) - jnp.where(diagonal, shift, 0.0)
                off_low = off.astype(BF16)
                poly = (COEF_B + 2.0 * COEF_C * shift) * off + COEF_C * dot(off_low, off_low)
                poly = poly.astype(BF16)
                keep = COEF_A + shift * (COEF_B + COEF_C * shift)
                for j in range(tiles // 2):
                    columns = pl.ds(j * 2 * LANES, 2 * LANES)
                    now = (keep * cur[:, columns] + dot(poly, low[:, columns])) * first
                    cur[:, columns] = now
                    low[:, columns] = now.astype(BF16)
                return 0

            lax.fori_loop(0, len(SHIFTS), turn, 0)
            for j in range(tiles // 2):
                parts = [cur[:, pl.ds((2 * j + side) * LANES, LANES)].reshape(32, TILE, LANES) for side in range(2)]
                result[:, pl.ds(j * 16, 16), :] = jnp.concatenate(parts, axis=1).astype(result.dtype)

        mine_mlp = jnp.logical_or(self.me == OWNERS[0], self.me == OWNERS[1])
        mine_sq = self.me < 0
        for device in OWNERS[2:]:
            mine_sq = jnp.logical_or(mine_sq, self.me == device)

        @pl.when(mine_mlp)
        def _():
            run(r.slabs_mlp, r.result_mlp, 8)

        @pl.when(mine_sq)
        def _():
            run(r.slabs_sq, r.result_sq, 2)

    def landing(self, index):
        if index < 2:
            return self.r.back_mlp.at[index]
        return self.r.out.at[2, pl.ds(SQ_AT[index - 2], SQ_ROWS)]

    def give_back(self, index, device):
        _, _, result = self.slab(index)
        return link(
            result.at[device], self.landing(index),
            self.r.back_send.at[device], self.r.back_recv.at[index], device,
        )

    def give_all(self):
        r = self.r
        for index in range(7):
            _, _, result = self.slab(index)

            @pl.when(self.me == OWNERS[index])
            def _():
                def send_one(step, _):
                    self.give_back(index, (self.me + step) % 32).start()
                    return 0

                lax.fori_loop(1, 32, send_one, 0)
                pltpu.make_async_copy(result.at[self.me], self.landing(index), r.back_recv.at[index]).start()

    def take_all(self):
        for index in range(7):
            _, _, result = self.slab(index)
            pltpu.make_async_copy(result.at[0], self.landing(index), self.r.back_recv.at[index]).wait()
        for index in range(2):
            rows = pl.ds(index * MLP_ROWS, MLP_ROWS)
            self.r.out[2, rows, :] = self.r.back_mlp[index].astype(F32)

    def drain(self):
        for k in range(len(CHUNKS)):
            self.core(k).wait_send()
            self.plane(k, True).wait_send()
            self.plane(k, False).wait_send()
            for step in range(3):
                self.along_z(k, step).wait_send()
        for index in range(7):

            @pl.when(self.me != OWNERS[index])
            def _():
                self.to_owner(index).wait_send()

    def drain_owner(self):
        for index in range(7):

            @pl.when(self.me == OWNERS[index])
            def _():
                def wait_one(step, _):
                    self.give_back(index, (self.me + step) % 32).wait_send()
                    return 0

                lax.fori_loop(1, 32, wait_one, 0)


def greet_all():
    me, z, y, x, c = place()
    greet(device_at(z, y, x, 1 - c))
    greet(device_at(z, y, 1 - x, c))
    greet(device_at(z, 1 - y, x, c))
    for step in range(1, 4):
        greet(device_at((z + step) % 4, y, x, c))
    owner = me < 0
    for device in OWNERS:
        owner = jnp.logical_or(owner, me == device)

        @pl.when(me != device)
        def _():
            greet(device)

    @pl.when(owner)
    def _():
        def greet_other(step, _):
            greet((me + step) % 32)
            return 0

        lax.fori_loop(1, 32, greet_other, 0)

    is_owner = owner.astype(jnp.int32)
    return 6 + 7 - is_owner + 31 * is_owner


def block_kernel(names, remote, *args):
    r = Refs(zip(names, args))
    keys, samples = r.obs.shape[0], r.obs.shape[1]
    tokens, width = r.acts.shape
    head_dim, half, per = width // HEADS, width // 2, ROWS // ACT
    wide = r.mlp_all.shape[2]
    groups = samples // GROUP
    in_sems, out_sems = r.in_sems, r.out_sems

    if remote:
        own = (r.sqw_v, r.mlpw_v, r.gain_v)
    else:
        own = (r.sq_all, r.mlp_all, r.gain_all)
    loads = list(zip((r.sqw, r.mlpw, r.gain), own))
    loads += [(r.acts, r.acts_v), (r.obs, r.obs_v.at[pl.ds(0, keys)]), (r.cot, r.cot_v)]
    if remote:
        loads += [(r.sqm, r.sqm_v), (r.mlpm, r.mlpm_v)]
    loads += [(r.flags, r.flags_s), (r.levels, r.levels_s)]
    copies = [pltpu.make_async_copy(a, b, in_sems.at[i]) for i, (a, b) in enumerate(loads)]

    def arrive(*which):
        for i in which:
            copies[i].wait()

    for copy in copies:
        copy.start()
    if remote:
        gather, update = Gather(r), Update(r)
        expected = greet_all()
        arrive(0, 1, 2)
        gather.fill()
        pl.semaphore_wait(pltpu.get_barrier_semaphore(), expected)
        gather.first(3, 4)

    arrive(3)

    def hats(i, _):
        rows = pl.ds(pl.multiple_of(i * ROWS, ROWS), ROWS)
        hat, scale = normalize(r.acts_v[rows, :])
        r.xhat[rows, :] = hat
        r.rstd[rows, :] = scale
        return 0

    lax.fori_loop(0, tokens // ROWS, hats, 0)

    mem, obs_v = r.mem, r.obs_v
    batch = 16
    chunks = KEYS_PAD // batch
    swap = r.swap
    row = lax.broadcasted_iota(jnp.int32, swap.shape, 0)
    column = lax.broadcasted_iota(jnp.int32, swap.shape, 1)
    swap[...] = jnp.where(column == (row % batch) * batch + row // batch, 1.0, 0.0).astype(BF16)

    def turn(part, low, high):
        def one(j, _):
            at = pl.ds(pl.multiple_of(j * batch, batch), batch)
            here = pl.ds(part * batch, batch)
            block = obs_v[at, here, :].reshape(batch * batch, width)
            mem[here, at, :] = dot(swap[...], block).astype(BF16).reshape(batch, batch, width)
            return 0

        lax.fori_loop(low, high, one, 0)

    whole = chunks - 1
    arrive(4)
    turn(0, 0, whole // 2)
    if remote:
        gather.second(3, 4)
        gather.first(2, 0, 1)
    turn(0, whole // 2, whole)
    if remote:
        gather.third(3, 4)
    turn(1, 0, whole // 2)
    if remote:
        gather.second(2, 0, 1)
        gather.fourth(3, 4)
    turn(1, whole // 2, whole)
    arrive(len(copies) - 1, len(copies) - 2)
    freqs = jnp.exp(
        lax.broadcasted_iota(jnp.int32, (1, half), 1).astype(F32) * F32(-math.log(10000.0)) / half
    )
    for s in range(samples):
        r.angle[s : s + 1, :] = r.levels_s[s].astype(F32) * freqs
    r.embed[:, 0:half] = jnp.sin(r.angle[...]).astype(BF16)
    r.embed[:, half:width] = jnp.cos(r.angle[...]).astype(BF16)
    if remote:
        arrive(6, 7)
        update.old_moment()
        gather.third(2, 0, 1)
        gather.last(3, 4)
        for m in range(3):
            gather.unpack(SQ_AT[m], 1, r.sq_all, m)
        gather.unpack_gains()
    else:
        arrive(0, 1, 2)

    sq, mlp = r.sq_all, r.mlp_all
    wkh, wvh = r.wkh, r.wvh
    lane = lax.broadcasted_iota(jnp.int32, (width, width), 1)

    def split_heads(out, weight):
        weight = weight.astype(F32)
        for h in range(HEADS):
            out[pl.ds(h * width, width), :] = jnp.where(lane // head_dim == h, weight, 0.0).astype(BF16)

    split_heads(wkh, sq[2])
    g1, g2 = r.gain_all[0:1, :], r.gain_all[1:2, :]

    obs_v[keys] = dot(r.embed[...], sq[0]).astype(BF16)
    obs_v[keys + 1 :] = jnp.zeros((KEYS_PAD - keys - 1, samples, width), BF16)
    for part in range(samples // batch):
        turn(part, whole, chunks)

    sides, weights = r.sides_v, r.pds_v

    def make_queries(i, _):
        rows = pl.ds(pl.multiple_of(i * ROWS, ROWS), ROWS)
        first = (r.xhat[rows, :] * g1).astype(BF16)
        r.first[rows, :] = first
        q = dot(first, sq[1]).astype(BF16)
        r.query[rows, :] = q
        here = pl.ds(i * per, per)
        for h in range(HEADS):
            wk = wkh[pl.ds(h * width, width), :]
            value = (dot(q, wk, NT) * 0.125).astype(BF16).reshape(per, ACT, width)
            sides[here, pl.ds((HEADS + h) * ACT, ACT), :] = value
        return 0

    lax.fori_loop(0, tokens // ROWS, make_queries, 0)

    key = lax.broadcasted_iota(jnp.int32, (1, KEYS_PAD), 1)
    low_rows, high_rows = pl.ds(0, HEADS * ACT), pl.ds(HEADS * ACT, HEADS * ACT)

    def attend(g, _):
        ids = [g * GROUP + k for k in range(GROUP)]
        scores = [dot(sides[s, high_rows, :], mem[s], NT) for s in ids]
        lows = []
        for s, score in zip(ids, scores):
            count = OBS_FEW + (OBS_FULL - OBS_FEW) * r.flags_s[s]
            score = score + jnp.where((key < count) | (key == OBS_FULL), 0.0, -1000000000.0)
            expo = jnp.exp(score - jnp.max(score, -1, keepdims=True))
            probs = expo * (1.0 / jnp.sum(expo, -1, keepdims=True))
            r.probs[s] = probs
            low = probs.astype(BF16)
            weights[s, low_rows, :] = low
            lows.append(low)
        for s, low in zip(ids, lows):
            u = dot(low, mem[s]).astype(BF16)
            rows = pl.ds(pl.multiple_of(s * ACT, ACT), ACT)
            for h in range(HEADS):
                r.u[rows, pl.ds(h * width, width)] = u[h * ACT : (h + 1) * ACT, :]
        return 0

    lax.fori_loop(0, groups // 2, attend, 0)
    if remote:
        gather.fourth(2, 0, 1)
    lax.fori_loop(groups // 2, groups, attend, 0)
    if remote:
        gather.last(2, 0, 1)
        for m in range(3, 5):
            gather.unpack(SQ_AT[m], 1, sq, m)
        for m in range(2):
            gather.unpack(m * MLP_ROWS, 4, mlp, m)
    split_heads(wvh, sq[3])

    gain_acc = r.gain_acc
    gain_acc[...] = jnp.zeros_like(gain_acc)
    arrive(5)

    def feed(i, _):
        rows = pl.ds(pl.multiple_of(i * ROWS, ROWS), ROWS)
        mixed = dot(r.u[rows, :], wvh[...]).astype(BF16)
        r.mixed[rows, :] = mixed
        resid = r.acts_v[rows, :] + dot(mixed, sq[4])
        hat, scale = normalize(resid)
        second = (hat * g2).astype(BF16)
        r.second[rows, :] = second
        cot = r.cot_v[rows, :]
        out_low = cot.astype(BF16)
        r.out_low[rows, :] = out_low
        for c in range(wide // 256):
            columns = pl.ds(c * 256, 256)
            v = dot(second, mlp[0, :, columns])
            square = v * v
            t = jnp.tanh(0.7978845608 * (v + 0.044715 * square * v))
            r.active[rows, columns] = (0.5 * v * (1.0 + t)).astype(BF16)
            slope = 0.5 * (1.0 + t) + 0.5 * v * (1.0 - t * t) * (0.7978845608 * (1.0 + 0.134145 * square))
            r.dhidden[rows, columns] = (slope * dot(out_low, mlp[1, :, columns])).astype(BF16)
        r.out_v[rows, :] = resid + dot(r.active[rows, :], mlp[1], NT)
        grad_second = dot(r.dhidden[rows, :], mlp[0], NT)
        gain_acc[1:2, :] += jnp.sum(grad_second * hat, 0, keepdims=True)
        dres = cot + norm_back(grad_second * g2, hat, scale)
        r.dres[rows, :] = dres
        low = dres.astype(BF16)
        r.dres_low[rows, :] = low
        gm = dot(low, sq[4], NT).astype(BF16)
        r.dmixed[rows, :] = gm
        here = pl.ds(i * per, per)
        for h in range(HEADS):
            wv = wvh[pl.ds(h * width, width), :]
            sides[here, pl.ds(h * ACT, ACT), :] = dot(gm, wv, NT).astype(BF16).reshape(per, ACT, width)
        return 0

    lax.fori_loop(0, tokens // ROWS, feed, 0)
    keep_out = pltpu.make_async_copy(r.out_v, r.output, out_sems.at[0])
    keep_out.start()

    grads = r.grads

    def put(base, tiles, value):
        for j in range(tiles):
            part = value[:, j * LANES : (j + 1) * LANES].reshape(GRID + (TILE, LANES))
            grads[:, :, :, :, pl.ds(base + j * TILE, TILE), :] = part

    def by_head(left, right):
        turned = left.T
        parts = [
            dot(turned[h * head_dim : (h + 1) * head_dim, :], right[:, pl.ds(h * width, width)])
            for h in range(HEADS)
        ]
        return jnp.concatenate(parts, axis=0).T

    def put_wide(base, left, right):
        r.turned[...] = left[...].T

        def one(c, _):
            columns = pl.ds(pl.multiple_of(c * 256, 256), 256)
            put(pl.multiple_of(base + c * 2 * TILE, TILE), 2, dot(r.turned[...], right[:, columns]))
            return 0

        lax.fori_loop(0, wide // 256, one, 0)

    put_wide(0, r.second, r.dhidden)
    if remote:
        update.start(0)
    put_wide(MLP_ROWS, r.out_low, r.active)
    if remote:
        update.start(1)
    put(SQ_AT[4], 2, dot(r.mixed[...], r.dres_low[...], TN))
    put(SQ_AT[3], 2, by_head(r.dmixed[...], r.u))
    if remote:
        update.start(2)

    def attend_back(g, _):
        ids = [g * GROUP + k for k in range(GROUP)]
        rises = [dot(sides[s, low_rows, :], mem[s], NT) for s in ids]
        for s, rise in zip(ids, rises):
            probs = r.probs[s]
            both = probs * rise
            weights[s, high_rows, :] = (both - probs * jnp.sum(both, -1, keepdims=True)).astype(BF16)
        for s in ids:
            dq = (dot(weights[s, high_rows, :], mem[s]) * 0.125).astype(BF16)
            rows = pl.ds(pl.multiple_of(s * ACT, ACT), ACT)
            for h in range(HEADS):
                r.dq_wide[rows, pl.ds(h * width, width)] = dq[h * ACT : (h + 1) * ACT, :]
            end = dot(weights[s, :, LANES:KEYS_PAD], sides[s], TN)
            r.stamps[s] = end[64:72, :]
        return 0

    half_groups = groups // 2
    lax.fori_loop(0, half_groups, attend_back, 0)
    if remote:
        update.one(0)
    lax.fori_loop(half_groups, groups, attend_back, 0)
    put(SQ_AT[2], 2, by_head(r.query[...], r.dq_wide))
    stamp_low = r.stamps[:, 4:5, :].reshape(samples, width).astype(BF16)
    put(SQ_AT[0], 2, dot(r.embed[...], stamp_low, TN))
    if remote:
        update.start(3)
        update.one(1, 2)

    def memory_back(low, high):
        def one(g, _):
            for k in range(GROUP):
                s = g * GROUP + k
                mem[s] = dot(weights[s], sides[s], TN).astype(BF16)
            return 0

        lax.fori_loop(low, high, one, 0)

    def turn_back(part):
        def one(j, _):
            at = pl.ds(pl.multiple_of(j * batch, batch), batch)
            here = pl.ds(part * batch, batch)
            block = mem[here, at, :].reshape(batch * batch, width)
            obs_v[at, here, :] = dot(swap[...], block).astype(BF16).reshape(batch, batch, width)
            return 0

        lax.fori_loop(0, chunks, one, 0)

    def queries_back(i, _):
        rows = pl.ds(pl.multiple_of(i * ROWS, ROWS), ROWS)
        r.dquery[rows, :] = dot(r.dq_wide[rows, :], wkh[...]).astype(BF16)
        return 0

    lax.fori_loop(0, tokens // ROWS, queries_back, 0)
    put(SQ_AT[1], 2, dot(r.first[...], r.dquery[...], TN))
    if remote:
        update.start(4)

    def acts_back(i, _):
        rows = pl.ds(pl.multiple_of(i * ROWS, ROWS), ROWS)
        grad_first = dot(r.dquery[rows, :], sq[1], NT)
        hat = r.xhat[rows, :]
        gain_acc[0:1, :] += jnp.sum(grad_first * hat, 0, keepdims=True)
        r.ag_v[rows, :] = r.dres[rows, :] + norm_back(grad_first * g1, hat, r.rstd[rows, :])
        return 0

    def finish_acts():
        lax.fori_loop(0, tokens // ROWS, acts_back, 0)
        for norm in range(2):
            for j in range(2):
                row = gain_acc[norm : norm + 1, j * LANES : (j + 1) * LANES]
                at = GAIN_BASE + norm * 2 + j
                value = jnp.broadcast_to(row.reshape(1, 1, 1, 1, 1, LANES), GRID + (1, LANES))
                grads[:, :, :, :, at : at + 1, :] = value
        rest = WIRE - GAIN_BASE - 4
        grads[:, :, :, :, GAIN_BASE + 4 : WIRE, :] = jnp.zeros(GRID + (rest, LANES), F32)

    keep_ag = pltpu.make_async_copy(r.ag_v, r.ag, out_sems.at[2])
    keep_og = pltpu.make_async_copy(obs_v.at[pl.ds(0, keys)], r.og, out_sems.at[1])
    if remote:
        update.two(0)
        update.one(3)
        finish_acts()
        keep_ag.start()
        update.start(5)
        update.two(1, 2)
        update.one(4)
        memory_back(0, half_groups)
        update.two(3)
        update.one(5)
        update.three(0, 1)
        update.two(4)
        memory_back(half_groups, groups)
        update.three(2, 3, 4)
        update.two(5)
        update.four(0, 1)
        turn_back(0)
        update.four(2, 3, 4)
        update.three(5)
        update.orthogonalize()
        update.give_all()
        turn_back(1)
        keep_og.start()
        update.four(5)
        out = r.out
        out[1, :, :] = r.moment[...]
        out[2, pl.ds(GAIN_BASE, 16), :] = jnp.zeros((16, LANES), F32)
        gather.drain()
        update.drain()
        update.take_all()
        update.drain_owner()
    else:
        finish_acts()
        keep_ag.start()
        memory_back(0, groups)
        for part in range(samples // batch):
            turn_back(part)
        keep_og.start()
    for copy in (keep_out, keep_og, keep_ag):
        copy.wait()


def block_and_back(remote, acts, obs, flags, levels, cot, sqw, mlpw, gain, sqm=None, mlpm=None):
    tokens, width = acts.shape
    keys, samples = obs.shape[0], obs.shape[1]
    rows = HEADS * ACT
    wide = mlpw.shape[2]
    any_space = pl.BlockSpec(memory_space=pl.ANY)
    in_vmem = pl.BlockSpec(memory_space=VMEM)
    sem = pltpu.SemaphoreType.DMA
    ins = dict(flags=flags, levels=levels, acts=acts, obs=obs, cot=cot, sqw=sqw, mlpw=mlpw, gain=gain)
    outs = dict(
        output=jax.ShapeDtypeStruct(acts.shape, F32),
        ag=jax.ShapeDtypeStruct(acts.shape, F32),
        og=jax.ShapeDtypeStruct(obs.shape, BF16),
    )
    grads = GRID + (WIRE, LANES)
    scratch = dict(
        obs_v=VMEM((KEYS_PAD, samples, width), BF16),
        acts_v=VMEM(acts.shape, F32),
        cot_v=VMEM(acts.shape, F32),
        mem=VMEM((samples, KEYS_PAD, width), BF16),
        swap=VMEM((256, 256), BF16),
        sq_all=VMEM((5, width, width), BF16),
        mlp_all=VMEM((2, width, wide), BF16),
        gain_all=VMEM((2, width), F32),
        wkh=VMEM((HEADS * width, width), BF16),
        wvh=VMEM((HEADS * width, width), BF16),
        first=VMEM((tokens, width), BF16),
        query=VMEM((tokens, width), BF16),
        xhat=VMEM((tokens, width), F32),
        rstd=VMEM((tokens, 1), F32),
        probs=VMEM((samples, rows, KEYS_PAD), F32),
        pds_v=VMEM((samples, 2 * rows, KEYS_PAD), BF16),
        sides_v=VMEM((samples, 2 * rows, width), BF16),
        u=VMEM((tokens, HEADS * width), BF16),
        dq_wide=VMEM((tokens, HEADS * width), BF16),
        mixed=VMEM((tokens, width), BF16),
        second=VMEM((tokens, width), BF16),
        active=VMEM((tokens, wide), BF16),
        dhidden=VMEM((tokens, wide), BF16),
        out_low=VMEM((tokens, width), BF16),
        dres_low=VMEM((tokens, width), BF16),
        dres=VMEM((tokens, width), F32),
        dmixed=VMEM((tokens, width), BF16),
        dquery=VMEM((tokens, width), BF16),
        out_v=VMEM((tokens, width), F32),
        ag_v=VMEM((tokens, width), F32),
        angle=VMEM((samples, width // 2), F32),
        embed=VMEM((samples, width), BF16),
        stamps=VMEM((samples, 8, width), F32),
        gain_acc=VMEM((8, width), F32),
        turned=VMEM((width, tokens), BF16),
        flags_s=pltpu.SMEM(flags.shape, jnp.int32),
        levels_s=pltpu.SMEM(levels.shape, jnp.int32),
        in_sems=sem((10,)),
        out_sems=sem((3,)),
    )
    extra = {}
    if remote:
        ins.update(sqm=sqm, mlpm=mlpm)
        outs.update(out=jax.ShapeDtypeStruct((3, WIRE, LANES), F32))
        chunks = len(CHUNKS)
        scratch.update(
            grads=VMEM(grads, F32),
            sqw_v=VMEM(sqw.shape, F32),
            mlpw_v=VMEM(mlpw.shape, F32),
            gain_v=VMEM(gain.shape, F32),
            sqm_v=VMEM(sqm.shape, F32),
            mlpm_v=VMEM(mlpm.shape, F32),
            wire=VMEM(grads, BF16),
            edge=VMEM((16, LANES), F32),
            gsend=sem((chunks, 6)),
            grecv=sem((chunks, 6)),
            send0=VMEM((4, 2, 2, WIRE, LANES), BF16),
            got_core=VMEM((4, 2, 2, WIRE, LANES), BF16),
            sum1=VMEM((4, 2, 2, WIRE, LANES), F32),
            send1=VMEM((4, 2, WIRE, LANES), BF16),
            got1=VMEM((4, 2, WIRE, LANES), BF16),
            sum2=VMEM((4, 2, WIRE, LANES), F32),
            send2=VMEM((4, WIRE, LANES), BF16),
            got2=VMEM((4, WIRE, LANES), BF16),
            sum3=VMEM((4, WIRE, LANES), F32),
            send3=VMEM((3, WIRE, LANES), BF16),
            got3=VMEM((3, WIRE, LANES), BF16),
            moment=VMEM((WIRE, LANES), F32),
            slabs_sq=VMEM((32, SQ_ROWS, LANES), F32),
            slabs_mlp=VMEM((32, MLP_ROWS, LANES), BF16),
            moment_low=VMEM((2 * MLP_ROWS, LANES), BF16),
            back_mlp=VMEM((2, MLP_ROWS, LANES), BF16),
            result_sq=VMEM((32, SQ_ROWS, LANES), F32),
            result_mlp=VMEM((32, MLP_ROWS, LANES), BF16),
            cur=VMEM((width, wide), F32),
            cur_low=VMEM((width, wide), BF16),
            send=sem((chunks, 6)),
            recv=sem((chunks, 6)),
            own_send=sem((7,)),
            own_recv=sem((1,)),
            back_send=sem((32,)),
            back_recv=sem((7,)),
        )
        extra = dict(collective_id=0, has_side_effects=True)
        outs = {name: VMEM(like.shape, like.dtype) for name, like in outs.items()}
    else:
        outs.update(grads=jax.ShapeDtypeStruct(grads, F32))
    names = tuple(ins) + tuple(outs) + tuple(scratch)
    stay = [pltpu.with_memory_space_constraint(value, pltpu.HBM) for value in ins.values()]
    results = pl.pallas_call(
        functools.partial(block_kernel, names, remote),
        out_shape=tuple(outs.values()),
        in_specs=[any_space] * len(ins),
        out_specs=[any_space] * 3 + [in_vmem],
        scratch_shapes=list(scratch.values()),
        compiler_params=pltpu.CompilerParams(vmem_limit_bytes=46 << 20, **extra),
        name="block_and_back",
    )(*stay)
    return Refs(zip(outs, results))


PARTS = 7


def finish_kernel(names, rate, *args):
    r = Refs(zip(names, args))
    sems = r.sems
    keys = r.og.shape[0]
    step = keys // PARTS

    def leave(part):
        block = pl.ds(part * step, step)
        return pltpu.make_async_copy(r.og_v.at[block], r.og.at[block], sems.at[part])

    more = PARTS
    moves = []
    if hasattr(r, "wire"):
        pairs = [(r.sqw, r.sqw_v), (r.mlpw, r.mlpw_v), (r.gain, r.gain_v), (r.gainm, r.gainm_v)]
        pairs += [(r.output, r.output_f), (r.ag, r.ag_f)]
        for source, target in pairs:
            moves.append(pltpu.make_async_copy(source, target, sems.at[more]))
            moves[-1].start()
            more += 1
    for part in range(PARTS):

        def widen(j, _):
            r.og_v[j] = r.low[j].astype(F32)
            return 0

        lax.fori_loop(part * step, (part + 1) * step, widen, 0, unroll=4)
        leave(part).start()
    for copy in moves[:4]:
        copy.wait()
    if hasattr(r, "wire"):
        finish_weights(r, rate)
    for part in range(PARTS):
        leave(part).wait()
    for copy in moves[4:]:
        copy.wait()


def finish_weights(r, rate):
    wire = r.wire
    me = lax.axis_index("dp")
    for m in range(5):
        for j in range(2):
            rows, columns = pl.ds(SQ_AT[m] + j * TILE, TILE), pl.ds(j * LANES, LANES)
            r.sqg[m, :, columns] = wire[0, rows, :]
            r.sqm[m, :, columns] = wire[1, rows, :]
            r.sqn[m, :, columns] = r.sqw_v[m, :, columns] - SQ_RATES[m] * wire[2, rows, :]
    r.sqc[...] = r.sqn[...].astype(BF16)
    for m in range(2):
        for j in range(8):
            rows, columns = pl.ds(m * MLP_ROWS + j * TILE, TILE), pl.ds(j * LANES, LANES)
            r.mlpg[m, :, columns] = wire[0, rows, :]
            r.mlpm[m, :, columns] = wire[1, rows, :]
            r.mlpn[m, :, columns] = r.mlpw_v[m, :, columns] - MLP_RATES[m] * wire[2, rows, :]
    r.mlpc[...] = r.mlpn[...].astype(BF16)
    tile = wire[0, pl.ds(GAIN_BASE, TILE), :]
    turned = pltpu.roll(tile, (LANES - (me % 16) * TILE) % LANES, 1)
    at = me // 16
    for norm in range(2):
        pair = turned[2 * norm : 2 * norm + 2, 0:TILE]
        row = jnp.where(at == 0, pair[0:1, :], pair[1:2, :])
        new = 0.5 * r.gainm_v[norm : norm + 1, :] + row
        r.gg[norm : norm + 1, :] = row
        r.gm[norm : norm + 1, :] = new
        r.gn[norm : norm + 1, :] = r.gain_v[norm : norm + 1, :] - rate * new


def finish(rate, made, sqw=None, mlpw=None, gain=None, gainm=None):
    any_space = pl.BlockSpec(memory_space=pl.ANY)
    in_vmem = pl.BlockSpec(memory_space=VMEM)
    ins = dict(low=made.og)
    outs = dict(og=jax.ShapeDtypeStruct(made.og.shape, F32))
    near, far = 1, 1
    if hasattr(made, "out"):
        ins.update(output=made.output, ag=made.ag, wire=made.out, sqw=sqw, mlpw=mlpw, gain=gain, gainm=gainm)
        like = jax.ShapeDtypeStruct
        near, far = 4, 3
        outs.update(
            output_f=like(made.output.shape, F32),
            ag_f=like(made.ag.shape, F32),
            sqg=like(sqw.shape, F32),
            sqm=like(sqw.shape, F32),
            sqn=like(sqw.shape, F32),
            sqc=like(sqw.shape, BF16),
            mlpg=like(mlpw.shape, F32),
            mlpm=like(mlpw.shape, F32),
            mlpn=like(mlpw.shape, F32),
            mlpc=like(mlpw.shape, BF16),
            gg=like(gain.shape, F32),
            gm=like(gain.shape, F32),
            gn=like(gain.shape, F32),
        )
    scratch = dict(
        og_v=VMEM(made.og.shape, F32),
        sems=pltpu.SemaphoreType.DMA((PARTS + 6,)),
    )
    if hasattr(made, "out"):
        scratch.update(
            sqw_v=VMEM(sqw.shape, F32),
            mlpw_v=VMEM(mlpw.shape, F32),
            gain_v=VMEM(gain.shape, F32),
            gainm_v=VMEM(gainm.shape, F32),
        )
    names = tuple(ins) + tuple(outs) + tuple(scratch)
    made_here = list(ins.values())
    stay = [pltpu.with_memory_space_constraint(value, pltpu.HBM) for value in made_here[near:]]
    results = pl.pallas_call(
        functools.partial(finish_kernel, names, rate),
        out_shape=tuple(outs.values()),
        in_specs=[in_vmem] * near + [any_space] * (len(ins) - near),
        out_specs=[any_space] * far + [in_vmem] * (len(outs) - far),
        scratch_shapes=list(scratch.values()),
        compiler_params=pltpu.CompilerParams(vmem_limit_bytes=16 << 20),
        name="finish",
    )(*made_here[:near], *stay)
    return Refs(zip(outs, results))


HIGH_PRECISION = lax.Precision.HIGHEST


def plain_orthogonalize(matrix):
    current = matrix / (jnp.sqrt(jnp.sum(matrix * matrix)) + 1e-07)
    for turn in range(5):
        gram = jnp.dot(current, current.T, precision=HIGH_PRECISION)
        poly = COEF_B * gram + COEF_C * jnp.dot(gram, gram, precision=HIGH_PRECISION)
        current = COEF_A * current + jnp.dot(poly, current, precision=HIGH_PRECISION)
    return current


def pick_owned(stack, owners, device):
    chosen = jnp.zeros_like(stack[0])
    for index in range(len(owners)):
        chosen = jnp.where(device == owners[index], stack[index], chosen)
    return chosen


def is_owner(owners, device):
    flag = device < 0
    for owner in owners:
        flag = jnp.logical_or(flag, device == owner)
    return flag


def from_wire(grads):
    def matrix(base, tiles):
        part = grads[:, base : base + tiles * TILE, :].reshape(-1, tiles, TILE, LANES)
        return part.transpose(0, 2, 1, 3).reshape(-1, tiles * LANES)

    square = jnp.stack([matrix(SQ_AT[m], 2) for m in range(5)])
    mlp = jnp.stack([matrix(m * MLP_ROWS, 8) for m in range(2)])
    return square, mlp, grads[0, GAIN_BASE : GAIN_BASE + 4, :].reshape(2, 2 * LANES)


def update_by_collectives(
    grads, square_weights, mlp_weights, gains, square_moment, mlp_moment, gain_moment, rate
):
    square_local, mlp_local, gain_local = from_wire(grads)
    square_grad, mlp_grad, gain_grad = (
        lax.psum_scatter(square_local, "dp", scatter_dimension=1, tiled=True),
        lax.psum_scatter(mlp_local, "dp", scatter_dimension=1, tiled=True),
        lax.psum_scatter(gain_local, "dp", scatter_dimension=1, tiled=True),
    )
    square_moment_new = 0.5 * square_moment + square_grad
    mlp_moment_new = 0.5 * mlp_moment + mlp_grad
    gain_moment_new = 0.5 * gain_moment + gain_grad
    device = lax.axis_index("dp")
    count = lax.axis_size("dp")
    square_owners = [index * count // 7 for index in range(5)]
    mlp_owners = [(index + 5) * count // 7 for index in range(2)]
    square_full, mlp_full = (
        lax.all_gather(square_moment_new, "dp", axis=1, tiled=True),
        lax.all_gather(mlp_moment_new, "dp", axis=1, tiled=True),
    )
    mine_square = pick_owned(square_full, square_owners, device)
    mine_mlp = pick_owned(mlp_full, mlp_owners, device)
    made_square = lax.cond(
        is_owner(square_owners, device), plain_orthogonalize, jnp.zeros_like, mine_square
    )
    made_mlp = lax.cond(is_owner(mlp_owners, device), plain_orthogonalize, jnp.zeros_like, mine_mlp)
    stack_square = jnp.stack(
        [jnp.where(device == owner, made_square, 0.0) for owner in square_owners]
    )
    stack_mlp = jnp.stack([jnp.where(device == owner, made_mlp, 0.0) for owner in mlp_owners])
    square_ortho, mlp_ortho = (
        lax.psum_scatter(stack_square, "dp", scatter_dimension=1, tiled=True),
        lax.psum_scatter(stack_mlp, "dp", scatter_dimension=1, tiled=True),
    )
    square_new = square_weights - jnp.array(SQ_RATES, F32)[:, None, None] * square_ortho
    mlp_new = mlp_weights - jnp.array(MLP_RATES, F32)[:, None, None] * mlp_ortho
    gains_new = gains - rate * gain_moment_new
    return (
        square_grad,
        square_moment_new,
        square_new,
        square_new.astype(BF16),
        mlp_grad,
        mlp_moment_new,
        mlp_new,
        mlp_new.astype(BF16),
        gain_grad,
        gain_moment_new,
        gains_new,
    )


def per_device(
    actions,
    observed,
    camera_flags,
    noise_levels,
    cotangent,
    square_weights,
    mlp_weights,
    gains,
    square_moment,
    mlp_moment,
    gain_moment,
):
    count = lax.axis_size("dp")
    rate = 0.1 / math.sqrt(actions.shape[0] * count)
    by_key = observed.transpose(1, 0, 2)
    ins = (actions, by_key, camera_flags, noise_levels, cotangent)
    if count == math.prod(GRID):
        made = block_and_back(True, *ins, square_weights, mlp_weights, gains, square_moment, mlp_moment)
        done = finish(rate, made, square_weights, mlp_weights, gains, gain_moment)
        output, actions_grad = done.output_f, done.ag_f
        d = done
        rest = (d.sqg, d.sqm, d.sqn, d.sqc, d.mlpg, d.mlpm, d.mlpn, d.mlpc, d.gg, d.gm, d.gn)
    else:
        square_all, mlp_all = (
            lax.all_gather(square_weights.astype(BF16), "dp", axis=1, tiled=True),
            lax.all_gather(mlp_weights.astype(BF16), "dp", axis=1, tiled=True),
        )
        gain_all = lax.all_gather(gains, "dp", axis=1, tiled=True)
        made = block_and_back(False, *ins, square_all, mlp_all, gain_all)
        done = finish(rate, made)
        output, actions_grad = made.output, made.ag
        grads = made.grads.reshape(-1, WIRE, LANES)
        rest = update_by_collectives(
            grads, square_weights, mlp_weights, gains, square_moment, mlp_moment, gain_moment, rate
        )
    observed_grad = done.og.transpose(1, 0, 2)
    return (output, actions_grad, observed_grad) + tuple(rest)


def solution(mesh):
    rows, cube, flat = P("dp", None), P("dp", None, None), P("dp")
    stacked, pair = P(None, "dp", None), P(None, "dp")
    return jax.shard_map(
        per_device,
        mesh=mesh,
        in_specs=(rows, cube, flat, flat, rows, stacked, stacked, pair, stacked, stacked, pair),
        out_specs=(rows, rows, cube) + (stacked,) * 8 + (pair,) * 3,
        check_vma=False,
    )
```

```python
import functools
import math

import jax
import jax.numpy as jnp
from jax import lax
from jax.experimental import pallas as pl
from jax.experimental.pallas import tpu as pltpu
from jax.sharding import PartitionSpec as P

HEADS = 4
ACT = 16
OBS_FULL = 196
OBS_FEW = 49
COEF_A = 3.4445
COEF_B = -4.775
COEF_C = 2.0315
F32 = jnp.float32
BF16 = jnp.bfloat16
MESH = pl.DeviceIdType.MESH
VMEM = pltpu.VMEM
NN = (((1,), (0,)), ((), ()))
NT = (((1,), (1,)), ((), ()))
TN = (((0,), (0,)), ((), ()))

LANES = 128
TILE = 8
MLP_ROWS = 64
SQ_ROWS = 16
SQ_AT = (160, 192, 176, 128, 144)
GAIN_BASE = 208
WIRE = 224
PIECES = ((0, 64), (64, 64), (128, 32), (160, 32), (192, 32))
PIECE_X_FIRST = (True, False, True, True, False)
CHUNKS = ((0, 64), (64, 64), (128, 32), (160, 32), (192, 16), (208, 16))
X_FIRST = (True, False, True, False, True, False)
COMPLETES = ((0,), (1,), (5, 6), (2, 4), (3,), ())
MLP_RATES = (1.0, 0.5)
SQ_RATES = (0.5, 0.5, 0.5, 0.5, 4.0)
GRID = (4, 2, 2, 2)
OWNERS = (8, 22, 14, 16, 11, 21, 13)
SHIFTS = (0.0, 0.0, 0.4, 0.8, 0.8)
KEYS_PAD = 208
GROUP = 16
ROWS = 512


class Refs:
    def __init__(self, pairs):
        self.__dict__.update(pairs)


def dot(left, right, dims=NN):
    return lax.dot_general(left, right, dims, preferred_element_type=F32)


def place():
    me = lax.axis_index("dp")
    return me, me // 8, (me // 4) % 2, (me // 2) % 2, me % 2


def device_at(z, y, x, c):
    return ((z * 2 + y) * 2 + x) * 2 + c


def link(src, dst, send, recv, device):
    return pltpu.make_async_remote_copy(
        src_ref=src,
        dst_ref=dst,
        send_sem=send,
        recv_sem=recv,
        device_id=(device,),
        device_id_type=MESH,
    )


def greet(device):
    pl.semaphore_signal(
        pltpu.get_barrier_semaphore(), inc=1, device_id=(device,), device_id_type=MESH
    )


def normalize(values):
    centred = values - jnp.mean(values, -1, keepdims=True)
    scale = lax.rsqrt(jnp.mean(centred * centred, -1, keepdims=True) + 1e-05)
    return centred * scale, scale


def norm_back(grad, hat, scale):
    mean_one = jnp.mean(grad, -1, keepdims=True)
    mean_two = jnp.mean(grad * hat, -1, keepdims=True)
    return scale * (grad - mean_one - hat * mean_two)


class Gather:
    def __init__(self, r):
        self.r = r
        self.me, self.z, self.y, self.x, self.c = place()

    def hop(self, k, step, part, device):
        return link(part, part, self.r.gsend.at[k, step], self.r.grecv.at[k, step], device)

    def along_z(self, k, step):
        part = self.r.wire.at[self.z, self.y, self.x, self.c, pl.ds(*PIECES[k])]
        return self.hop(k, step, part, device_at((self.z + step + 1) % 4, self.y, self.x, self.c))

    def from_z(self, k, step):
        there = (self.z + 3 - step) % 4
        part = self.r.wire.at[there, self.y, self.x, self.c, pl.ds(*PIECES[k])]
        return self.hop(k, step, part, device_at(there, self.y, self.x, self.c))

    def plane(self, k, second, mine):
        z, y, x, c = self.z, self.y, self.x, self.c
        rows, wire = pl.ds(*PIECES[k]), self.r.wire
        py, px = (y, x) if mine else (1 - y, 1 - x)
        along_x = PIECE_X_FIRST[k] == second
        if along_x:
            part = wire.at[:, y, px, c, rows] if second else wire.at[:, :, px, c, rows]
            return self.hop(k, 3 if second else 4, part, device_at(z, y, 1 - x, c))
        part = wire.at[:, py, x, c, rows] if second else wire.at[:, py, :, c, rows]
        return self.hop(k, 3 if second else 4, part, device_at(z, 1 - y, x, c))

    def core(self, k, mine):
        part = self.r.wire.at[:, :, :, self.c if mine else 1 - self.c, pl.ds(*PIECES[k])]
        return self.hop(k, 5, part, device_at(self.z, self.y, self.x, 1 - self.c))

    def first(self, *chunks):
        for k in chunks:
            for step in range(3):
                self.along_z(k, step).start()

    def second(self, *chunks):
        for k in chunks:
            for step in range(3):
                self.from_z(k, step).wait_recv()
            self.plane(k, True, True).start()

    def third(self, *chunks):
        for k in chunks:
            self.plane(k, True, False).wait_recv()
            self.plane(k, False, True).start()

    def fourth(self, *chunks):
        for k in chunks:
            self.plane(k, False, False).wait_recv()
            self.core(k, True).start()

    def last(self, *chunks):
        for k in chunks:
            self.core(k, False).wait_recv()

    def drain(self):
        for k in range(len(PIECES)):
            for step in range(3):
                self.along_z(k, step).wait_send()
            self.plane(k, True, True).wait_send()
            self.plane(k, False, True).wait_send()
            self.core(k, True).wait_send()

    def fill(self):
        r = self.r
        spot = (self.z, self.y, self.x, self.c)

        def tiles(source, m, base, number):
            for j in range(number):
                pair = [source[m, :, pl.ds((2 * j + k) * LANES, LANES)] for k in range(2)]
                r.wire[spot + (pl.ds(base + j * 16, 16),)] = jnp.concatenate(pair, axis=0).astype(BF16)

        for m in range(5):
            tiles(r.sqw_v, m, SQ_AT[m], 1)
        for m in range(2):
            tiles(r.mlpw_v, m, m * MLP_ROWS, 4)
        gains, edge = r.gain_v[...], r.edge
        high = gains.astype(BF16).astype(F32)
        middle = (gains - high).astype(BF16).astype(F32)
        edge[...] = jnp.zeros_like(edge)
        edge[0:2, 0:TILE] = high
        edge[2:4, 0:TILE] = middle
        edge[4:6, 0:TILE] = (gains - high - middle).astype(BF16).astype(F32)
        r.wire[spot + (pl.ds(GAIN_BASE, 16),)] = edge[...].astype(BF16)

    def unpack(self, base, number, out, m):
        for j in range(number):
            block = self.r.wire[:, :, :, :, pl.ds(base + j * 16, 16), :].reshape(32, 16, LANES).astype(F32)
            for half in range(2):
                columns = pl.ds((2 * j + half) * LANES, LANES)
                out[m, :, columns] = block[:, half * 8 : half * 8 + 8, :].reshape(256, LANES).astype(BF16)

    def unpack_gains(self):
        edge, wire = self.r.edge, self.r.wire
        for half in range(2):
            total = jnp.zeros((16, LANES), F32)
            for at in range(16):
                d = half * 16 + at
                tile = wire[d // 8, (d // 4) % 2, (d // 2) % 2, d % 2, pl.ds(GAIN_BASE, 16), :].astype(F32)
                total = total + (tile if at == 0 else pltpu.roll(tile, at * TILE, 1))
            edge[...] = total
            self.r.gain_all[:, pl.ds(half * LANES, LANES)] = edge[0:2, :] + edge[2:4, :] + edge[4:6, :]


class Update:
    def __init__(self, r):
        self.r = r
        self.me, self.z, self.y, self.x, self.c = place()

    def hop(self, k, step, src, dst, device):
        return link(src, dst, self.r.send.at[k, step], self.r.recv.at[k, step], device)

    def core(self, k):
        rows = pl.ds(*CHUNKS[k])
        src, dst = self.r.send0.at[:, :, :, rows], self.r.got_core.at[:, :, :, rows]
        return self.hop(k, 0, src, dst, device_at(self.z, self.y, self.x, 1 - self.c))

    def plane(self, k, first):
        rows = pl.ds(*CHUNKS[k])
        to = (self.z, self.y, 1 - self.x, self.c) if X_FIRST[k] == first else (self.z, 1 - self.y, self.x, self.c)
        if first:
            src, dst = self.r.send1.at[:, :, rows], self.r.got1.at[:, :, rows]
        else:
            src, dst = self.r.send2.at[:, rows], self.r.got2.at[:, rows]
        return self.hop(k, 1 if first else 2, src, dst, device_at(*to))

    def along_z(self, k, step):
        rows = pl.ds(*CHUNKS[k])
        to = device_at((self.z + step + 1) % 4, self.y, self.x, self.c)
        return self.hop(k, 3 + step, self.r.send3.at[step, rows], self.r.got3.at[step, rows], to)

    def start(self, k):
        rows = pl.ds(*CHUNKS[k])
        self.r.send0[:, :, :, rows, :] = self.r.grads[:, :, :, 1 - self.c, rows, :].astype(BF16)
        self.core(k).start()

    def one(self, *chunks):
        r = self.r
        for k in chunks:
            rows = pl.ds(*CHUNKS[k])
            self.core(k).wait_recv()
            sum1 = r.sum1
            sum1[:, :, :, rows, :] = r.grads[:, :, :, self.c, rows, :] + r.got_core[:, :, :, rows, :].astype(F32)
            other = sum1[:, :, 1 - self.x, rows, :] if X_FIRST[k] else sum1[:, 1 - self.y, :, rows, :]
            r.send1[:, :, rows, :] = other.astype(BF16)
            self.plane(k, True).start()

    def two(self, *chunks):
        r = self.r
        for k in chunks:
            rows = pl.ds(*CHUNKS[k])
            self.plane(k, True).wait_recv()
            sum1, sum2 = r.sum1, r.sum2
            mine = sum1[:, :, self.x, rows, :] if X_FIRST[k] else sum1[:, self.y, :, rows, :]
            sum2[:, :, rows, :] = mine + r.got1[:, :, rows, :].astype(F32)
            other = 1 - self.y if X_FIRST[k] else 1 - self.x
            r.send2[:, rows, :] = sum2[:, other, rows, :].astype(BF16)
            self.plane(k, False).start()

    def three(self, *chunks):
        r = self.r
        for k in chunks:
            rows = pl.ds(*CHUNKS[k])
            self.plane(k, False).wait_recv()
            mine = self.y if X_FIRST[k] else self.x
            r.sum3[:, rows, :] = r.sum2[:, mine, rows, :] + r.got2[:, rows, :].astype(F32)
            for step in range(3):
                r.send3[step, rows, :] = r.sum3[(self.z + step + 1) % 4, rows, :].astype(BF16)
                self.along_z(k, step).start()

    def slab(self, index):
        if index < 2:
            return pl.ds(index * MLP_ROWS, MLP_ROWS), self.r.slabs_mlp, self.r.result_mlp
        return pl.ds(SQ_AT[index - 2], SQ_ROWS), self.r.slabs_sq, self.r.result_sq

    def to_owner(self, index):
        rows, slabs, _ = self.slab(index)
        moment = self.r.moment_low if index < 2 else self.r.moment
        return link(
            moment.at[rows], slabs.at[self.me],
            self.r.own_send.at[index], self.r.own_recv.at[0], OWNERS[index],
        )

    def four(self, *chunks):
        r = self.r
        moment, out = r.moment, r.out
        for k in chunks:
            rows = pl.ds(*CHUNKS[k])
            total = r.sum3[self.z, rows, :]
            for step in range(3):
                self.along_z(k, step).wait_recv()
                total = total + r.got3[step, rows, :].astype(F32)
            out[0, rows, :] = total
            new = 0.5 * moment[rows, :] + total
            moment[rows, :] = new
            if k < 2:
                r.moment_low[rows, :] = new.astype(BF16)
            for index in COMPLETES[k]:
                rows_m, slabs, _ = self.slab(index)

                @pl.when(self.me != OWNERS[index])
                def _():
                    self.to_owner(index).start()

                @pl.when(self.me == OWNERS[index])
                def _():
                    mine = r.moment_low if index < 2 else moment
                    pltpu.make_async_copy(mine.at[rows_m], slabs.at[self.me], r.own_recv.at[0]).start()

    def old_moment(self):
        r = self.r
        moment = r.moment
        for m in range(2):
            for j in range(8):
                moment[pl.ds(m * MLP_ROWS + j * TILE, TILE), :] = r.mlpm_v[m, :, pl.ds(j * LANES, LANES)]
        for m in range(5):
            for j in range(2):
                moment[pl.ds(SQ_AT[m] + j * TILE, TILE), :] = r.sqm_v[m, :, pl.ds(j * LANES, LANES)]
        moment[pl.ds(GAIN_BASE, 16), :] = jnp.zeros((16, LANES), F32)

    def orthogonalize(self):
        r = self.r
        cur = r.cur
        rows = lax.broadcasted_iota(jnp.int32, (256, 256), 0)
        diagonal = rows == lax.broadcasted_iota(jnp.int32, (256, 256), 1)

        def run(slabs, result, tiles):
            pltpu.make_async_copy(slabs, slabs, r.own_recv.at[0]).wait()
            low = r.cur_low
            for j in range(tiles // 2):
                pair = slabs[:, pl.ds(j * 16, 16), :].astype(F32)
                for side in range(2):
                    columns = pl.ds((2 * j + side) * LANES, LANES)
                    part = pair[:, side * TILE : (side + 1) * TILE, :].reshape(256, LANES)
                    cur[:, columns] = part
                    low[:, columns] = part.astype(BF16)
            scale = 1.0
            for turn, shift in enumerate(SHIFTS):
                whole = low[:, 0 : tiles * LANES]
                off = dot(whole, whole, NT)
                if turn == 0:
                    norm = jnp.sum(jnp.sum(jnp.where(diagonal, off, 0.0), axis=0, keepdims=True), axis=1, keepdims=True)
                    scale = 1.0 / (jnp.sqrt(norm) + 1e-07)
                    off = off * (scale * scale)
                if shift:
                    off = off - jnp.where(diagonal, shift, 0.0)
                off_low = off.astype(BF16)
                poly = (COEF_B + 2.0 * COEF_C * shift) * off + COEF_C * dot(off_low, off_low)
                poly = poly.astype(BF16)
                keep = COEF_A + shift * (COEF_B + COEF_C * shift)
                for j in range(tiles // 2):
                    columns = pl.ds(j * 2 * LANES, 2 * LANES)
                    now = keep * cur[:, columns] + dot(poly, low[:, columns])
                    if turn == 0:
                        now = now * scale
                    if turn < len(SHIFTS) - 1:
                        cur[:, columns] = now
                        low[:, columns] = now.astype(BF16)
                    else:
                        parts = [now[:, side * LANES : (side + 1) * LANES].reshape(32, TILE, LANES) for side in range(2)]
                        result[:, pl.ds(j * 16, 16), :] = jnp.concatenate(parts, axis=1).astype(result.dtype)

        mine_mlp = jnp.logical_or(self.me == OWNERS[0], self.me == OWNERS[1])
        mine_sq = self.me < 0
        for device in OWNERS[2:]:
            mine_sq = jnp.logical_or(mine_sq, self.me == device)

        @pl.when(mine_mlp)
        def _():
            run(r.slabs_mlp, r.result_mlp, 8)

        @pl.when(mine_sq)
        def _():
            run(r.slabs_sq, r.result_sq, 2)

    def landing(self, index):
        if index < 2:
            return self.r.back_mlp.at[index]
        return self.r.out.at[2, pl.ds(SQ_AT[index - 2], SQ_ROWS)]

    def give_back(self, index, device):
        _, _, result = self.slab(index)
        return link(
            result.at[device], self.landing(index),
            self.r.back_send.at[device], self.r.back_recv.at[index], device,
        )

    def give_all(self):
        r = self.r
        for index in range(7):
            _, _, result = self.slab(index)

            @pl.when(self.me == OWNERS[index])
            def _():
                def send_one(step, _):
                    self.give_back(index, (self.me + step) % 32).start()
                    return 0

                lax.fori_loop(1, 32, send_one, 0)
                pltpu.make_async_copy(result.at[self.me], self.landing(index), r.back_recv.at[index]).start()

    def take_all(self):
        for index in range(7):
            _, _, result = self.slab(index)
            pltpu.make_async_copy(result.at[0], self.landing(index), self.r.back_recv.at[index]).wait()
        for index in range(2):
            rows = pl.ds(index * MLP_ROWS, MLP_ROWS)
            self.r.out[2, rows, :] = self.r.back_mlp[index].astype(F32)

    def drain(self):
        for k in range(len(CHUNKS)):
            self.core(k).wait_send()
            self.plane(k, True).wait_send()
            self.plane(k, False).wait_send()
            for step in range(3):
                self.along_z(k, step).wait_send()
        for index in range(7):

            @pl.when(self.me != OWNERS[index])
            def _():
                self.to_owner(index).wait_send()

    def drain_owner(self):
        for index in range(7):

            @pl.when(self.me == OWNERS[index])
            def _():
                def wait_one(step, _):
                    self.give_back(index, (self.me + step) % 32).wait_send()
                    return 0

                lax.fori_loop(1, 32, wait_one, 0)


def greet_all():
    me, z, y, x, c = place()
    greet(device_at(z, y, x, 1 - c))
    greet(device_at(z, y, 1 - x, c))
    greet(device_at(z, 1 - y, x, c))
    for step in range(1, 4):
        greet(device_at((z + step) % 4, y, x, c))
    owner = me < 0
    for device in OWNERS:
        owner = jnp.logical_or(owner, me == device)

        @pl.when(me != device)
        def _():
            greet(device)

    @pl.when(owner)
    def _():
        def greet_other(step, _):
            greet((me + step) % 32)
            return 0

        lax.fori_loop(1, 32, greet_other, 0)

    is_owner = owner.astype(jnp.int32)
    return 6 + 7 - is_owner + 31 * is_owner


def block_kernel(names, remote, *args):
    r = Refs(zip(names, args))
    keys, samples = r.obs.shape[0], r.obs.shape[1]
    tokens, width = r.acts.shape
    head_dim, half, per = width // HEADS, width // 2, ROWS // ACT
    wide = r.mlp_all.shape[2]
    groups = samples // GROUP
    in_sems, out_sems = r.in_sems, r.out_sems

    if remote:
        own = (r.sqw_v, r.mlpw_v, r.gain_v)
    else:
        own = (r.sq_all, r.mlp_all, r.gain_all)
    loads = list(zip((r.sqw, r.mlpw, r.gain), own))
    loads += [(r.acts, r.acts_v), (r.obs, r.obs_v.at[pl.ds(0, keys)]), (r.cot, r.cot_v)]
    if remote:
        loads += [(r.sqm, r.sqm_v), (r.mlpm, r.mlpm_v)]
    loads += [(r.flags, r.flags_s), (r.levels, r.levels_s)]
    copies = [pltpu.make_async_copy(a, b, in_sems.at[i]) for i, (a, b) in enumerate(loads)]

    def arrive(*which):
        for i in which:
            copies[i].wait()

    for copy in copies:
        copy.start()
    if remote:
        gather, update = Gather(r), Update(r)
        expected = greet_all()
        arrive(0, 1, 2)
        gather.fill()
        pl.semaphore_wait(pltpu.get_barrier_semaphore(), expected)
        gather.first(3, 4)

    arrive(3)

    def hats(i, _):
        rows = pl.ds(pl.multiple_of(i * ROWS, ROWS), ROWS)
        hat, scale = normalize(r.acts_v[rows, :])
        r.xhat[rows, :] = hat
        r.rstd[rows, :] = scale
        return 0

    lax.fori_loop(0, tokens // ROWS, hats, 0)

    mem, obs_v = r.mem, r.obs_v
    batch = 16
    chunks = KEYS_PAD // batch
    swap = r.swap
    row = lax.broadcasted_iota(jnp.int32, swap.shape, 0)
    column = lax.broadcasted_iota(jnp.int32, swap.shape, 1)
    swap[...] = jnp.where(column == (row % batch) * batch + row // batch, 1.0, 0.0).astype(BF16)

    def turn(part, low, high):
        def one(j, _):
            at = pl.ds(pl.multiple_of(j * batch, batch), batch)
            here = pl.ds(part * batch, batch)
            block = obs_v[at, here, :].reshape(batch * batch, width)
            mem[here, at, :] = dot(swap[...], block).astype(BF16).reshape(batch, batch, width)
            return 0

        lax.fori_loop(low, high, one, 0, unroll=high - low)

    whole = chunks - 1
    arrive(4)
    turn(0, 0, whole // 2)
    if remote:
        gather.second(3, 4)
        gather.first(2, 0, 1)
    turn(0, whole // 2, whole)
    if remote:
        gather.third(3, 4)
    turn(1, 0, whole // 2)
    if remote:
        gather.second(2, 0, 1)
        gather.fourth(3, 4)
    turn(1, whole // 2, whole)
    arrive(len(copies) - 1, len(copies) - 2)
    freqs = jnp.exp(
        lax.broadcasted_iota(jnp.int32, (1, half), 1).astype(F32) * F32(-math.log(10000.0)) / half
    )
    for s in range(samples):
        r.angle[s : s + 1, :] = r.levels_s[s].astype(F32) * freqs
    r.embed[:, 0:half] = jnp.sin(r.angle[...]).astype(BF16)
    r.embed[:, half:width] = jnp.cos(r.angle[...]).astype(BF16)
    if remote:
        arrive(6, 7)
        update.old_moment()
        gather.third(2, 0, 1)
        gather.last(3, 4)
        for m in range(3):
            gather.unpack(SQ_AT[m], 1, r.sq_all, m)
        gather.unpack_gains()
    else:
        arrive(0, 1, 2)

    sq, mlp = r.sq_all, r.mlp_all
    wkh, wvh = r.wkh, r.wvh
    lane = lax.broadcasted_iota(jnp.int32, (width, width), 1)

    def split_heads(out, weight):
        weight = weight.astype(F32)
        for h in range(HEADS):
            out[pl.ds(h * width, width), :] = jnp.where(lane // head_dim == h, weight, 0.0).astype(BF16)

    split_heads(wkh, sq[2])
    g1, g2 = r.gain_all[0:1, :], r.gain_all[1:2, :]

    obs_v[keys] = dot(r.embed[...], sq[0]).astype(BF16)
    obs_v[keys + 1 :] = jnp.zeros((KEYS_PAD - keys - 1, samples, width), BF16)
    for part in range(samples // batch):
        turn(part, whole, chunks)

    sides, weights = r.sides_v, r.pds_v

    def make_queries(i, _):
        rows = pl.ds(pl.multiple_of(i * ROWS, ROWS), ROWS)
        first = (r.xhat[rows, :] * g1).astype(BF16)
        r.first[rows, :] = first
        q = dot(first, sq[1]).astype(BF16)
        r.query[rows, :] = q
        here = pl.ds(i * per, per)
        for h in range(HEADS):
            wk = wkh[pl.ds(h * width, width), :]
            value = (dot(q, wk, NT) * 0.125).astype(BF16).reshape(per, ACT, width)
            sides[here, pl.ds((HEADS + h) * ACT, ACT), :] = value
        return 0

    lax.fori_loop(0, tokens // ROWS, make_queries, 0)

    key = lax.broadcasted_iota(jnp.int32, (1, KEYS_PAD), 1)
    low_rows, high_rows = pl.ds(0, HEADS * ACT), pl.ds(HEADS * ACT, HEADS * ACT)

    def attend(g, _):
        ids = [g * GROUP + k for k in range(GROUP)]
        scores = [dot(sides[s, high_rows, :], mem[s], NT) for s in ids]
        lows = []
        for s, score in zip(ids, scores):
            count = OBS_FEW + (OBS_FULL - OBS_FEW) * r.flags_s[s]
            score = score + jnp.where((key < count) | (key == OBS_FULL), 0.0, -1000000000.0)
            expo = jnp.exp(score - jnp.max(score, -1, keepdims=True))
            probs = expo * (1.0 / jnp.sum(expo, -1, keepdims=True))
            r.probs[s] = probs
            low = probs.astype(BF16)
            weights[s, low_rows, :] = low
            lows.append(low)
        for s, low in zip(ids, lows):
            u = dot(low, mem[s]).astype(BF16)
            rows = pl.ds(pl.multiple_of(s * ACT, ACT), ACT)
            for h in range(HEADS):
                r.u[rows, pl.ds(h * width, width)] = u[h * ACT : (h + 1) * ACT, :]
        return 0

    lax.fori_loop(0, groups // 2, attend, 0)
    if remote:
        gather.fourth(2, 0, 1)
    lax.fori_loop(groups // 2, groups, attend, 0)
    if remote:
        gather.last(2, 0, 1)
        for m in range(3, 5):
            gather.unpack(SQ_AT[m], 1, sq, m)
        for m in range(2):
            gather.unpack(m * MLP_ROWS, 4, mlp, m)
    split_heads(wvh, sq[3])

    gain_acc = r.gain_acc
    gain_acc[...] = jnp.zeros_like(gain_acc)
    arrive(5)

    def feed(i, _):
        rows = pl.ds(pl.multiple_of(i * ROWS, ROWS), ROWS)
        mixed = dot(r.u[rows, :], wvh[...]).astype(BF16)
        r.mixed[rows, :] = mixed
        resid = r.acts_v[rows, :] + dot(mixed, sq[4])
        hat, scale = normalize(resid)
        second = (hat * g2).astype(BF16)
        r.second[rows, :] = second
        cot = r.cot_v[rows, :]
        out_low = cot.astype(BF16)
        r.out_low[rows, :] = out_low
        for c in range(wide // 256):
            columns = pl.ds(c * 256, 256)
            v = dot(second, mlp[0, :, columns])
            square = v * v
            t = jnp.tanh(0.7978845608 * (v + 0.044715 * square * v))
            r.active[rows, columns] = (0.5 * v * (1.0 + t)).astype(BF16)
            slope = 0.5 * (1.0 + t) + 0.5 * v * (1.0 - t * t) * (0.7978845608 * (1.0 + 0.134145 * square))
            r.dhidden[rows, columns] = (slope * dot(out_low, mlp[1, :, columns])).astype(BF16)
        r.out_v[rows, :] = resid + dot(r.active[rows, :], mlp[1], NT)
        grad_second = dot(r.dhidden[rows, :], mlp[0], NT)
        gain_acc[1:2, :] += jnp.sum(grad_second * hat, 0, keepdims=True)
        dres = cot + norm_back(grad_second * g2, hat, scale)
        r.dres[rows, :] = dres
        low = dres.astype(BF16)
        r.dres_low[rows, :] = low
        gm = dot(low, sq[4], NT).astype(BF16)
        r.dmixed[rows, :] = gm
        here = pl.ds(i * per, per)
        for h in range(HEADS):
            wv = wvh[pl.ds(h * width, width), :]
            sides[here, pl.ds(h * ACT, ACT), :] = dot(gm, wv, NT).astype(BF16).reshape(per, ACT, width)
        return 0

    lax.fori_loop(0, tokens // ROWS, feed, 0)
    keep_out = pltpu.make_async_copy(r.out_v, r.output, out_sems.at[0])
    keep_out.start()

    grads = r.grads

    def put(base, tiles, value):
        for j in range(tiles):
            part = value[:, j * LANES : (j + 1) * LANES].reshape(GRID + (TILE, LANES))
            grads[:, :, :, :, pl.ds(base + j * TILE, TILE), :] = part

    def by_head(left, right):
        turned = left.T
        parts = [
            dot(turned[h * head_dim : (h + 1) * head_dim, :], right[:, pl.ds(h * width, width)])
            for h in range(HEADS)
        ]
        return jnp.concatenate(parts, axis=0).T

    put(0, 8, dot(r.second[...], r.dhidden[...], TN))
    if remote:
        update.start(0)
    put(MLP_ROWS, 8, dot(r.out_low[...], r.active[...], TN))
    if remote:
        update.start(1)
    put(SQ_AT[4], 2, dot(r.mixed[...], r.dres_low[...], TN))
    put(SQ_AT[3], 2, by_head(r.dmixed[...], r.u))
    if remote:
        update.start(2)

    def attend_back(g, _):
        ids = [g * GROUP + k for k in range(GROUP)]
        rises = [dot(sides[s, low_rows, :], mem[s], NT) for s in ids]
        for s, rise in zip(ids, rises):
            probs = r.probs[s]
            both = probs * rise
            weights[s, high_rows, :] = (both - probs * jnp.sum(both, -1, keepdims=True)).astype(BF16)
        for s in ids:
            dq = (dot(weights[s, high_rows, :], mem[s]) * 0.125).astype(BF16)
            rows = pl.ds(pl.multiple_of(s * ACT, ACT), ACT)
            for h in range(HEADS):
                r.dq_wide[rows, pl.ds(h * width, width)] = dq[h * ACT : (h + 1) * ACT, :]
            end = dot(weights[s, :, LANES:KEYS_PAD], sides[s], TN)
            r.stamps[s] = end[64:72, :]
        return 0

    half_groups = groups // 2
    lax.fori_loop(0, half_groups, attend_back, 0)
    if remote:
        update.one(0)
    lax.fori_loop(half_groups, groups, attend_back, 0)
    put(SQ_AT[2], 2, by_head(r.query[...], r.dq_wide))
    stamp_low = r.stamps[:, 4:5, :].reshape(samples, width).astype(BF16)
    put(SQ_AT[0], 2, dot(r.embed[...], stamp_low, TN))
    if remote:
        update.start(3)
        update.one(1, 2)

    def memory_back(low, high):
        def one(g, _):
            for k in range(GROUP):
                s = g * GROUP + k
                mem[s] = dot(weights[s], sides[s], TN).astype(BF16)
            return 0

        lax.fori_loop(low, high, one, 0)

    def turn_back(part):
        def one(j, _):
            at = pl.ds(pl.multiple_of(j * batch, batch), batch)
            here = pl.ds(part * batch, batch)
            block = mem[here, at, :].reshape(batch * batch, width)
            obs_v[at, here, :] = dot(swap[...], block).astype(BF16).reshape(batch, batch, width)
            return 0

        lax.fori_loop(0, chunks, one, 0, unroll=chunks)

    def queries_back(i, _):
        rows = pl.ds(pl.multiple_of(i * ROWS, ROWS), ROWS)
        r.dquery[rows, :] = dot(r.dq_wide[rows, :], wkh[...]).astype(BF16)
        return 0

    lax.fori_loop(0, tokens // ROWS, queries_back, 0)
    put(SQ_AT[1], 2, dot(r.first[...], r.dquery[...], TN))
    if remote:
        update.start(4)

    def acts_back(i, _):
        rows = pl.ds(pl.multiple_of(i * ROWS, ROWS), ROWS)
        grad_first = dot(r.dquery[rows, :], sq[1], NT)
        hat = r.xhat[rows, :]
        gain_acc[0:1, :] += jnp.sum(grad_first * hat, 0, keepdims=True)
        r.ag_v[rows, :] = r.dres[rows, :] + norm_back(grad_first * g1, hat, r.rstd[rows, :])
        return 0

    def finish_acts():
        lax.fori_loop(0, tokens // ROWS, acts_back, 0)
        for norm in range(2):
            for j in range(2):
                row = gain_acc[norm : norm + 1, j * LANES : (j + 1) * LANES]
                at = GAIN_BASE + norm * 2 + j
                value = jnp.broadcast_to(row.reshape(1, 1, 1, 1, 1, LANES), GRID + (1, LANES))
                grads[:, :, :, :, at : at + 1, :] = value
        rest = WIRE - GAIN_BASE - 4
        grads[:, :, :, :, GAIN_BASE + 4 : WIRE, :] = jnp.zeros(GRID + (rest, LANES), F32)

    keep_ag = pltpu.make_async_copy(r.ag_v, r.ag, out_sems.at[2])
    keep_og = pltpu.make_async_copy(obs_v.at[pl.ds(0, keys)], r.og, out_sems.at[1])
    if remote:
        update.two(0)
        update.one(3)
        finish_acts()
        keep_ag.start()
        update.start(5)
        update.two(1, 2)
        update.one(4)
        memory_back(0, half_groups)
        update.two(3)
        update.one(5)
        update.three(0, 1)
        update.two(4)
        memory_back(half_groups, groups)
        update.three(2, 3, 4)
        update.two(5)
        update.four(0, 1)
        turn_back(0)
        update.four(2, 3, 4)
        update.three(5)
        update.orthogonalize()
        update.give_all()
        turn_back(1)
        keep_og.start()
        update.four(5)
        out = r.out
        out[1, :, :] = r.moment[...]
        out[2, pl.ds(GAIN_BASE, 16), :] = jnp.zeros((16, LANES), F32)
        gather.drain()
        update.drain()
        update.take_all()
        update.drain_owner()
    else:
        finish_acts()
        keep_ag.start()
        memory_back(0, groups)
        for part in range(samples // batch):
            turn_back(part)
        keep_og.start()
    for copy in (keep_out, keep_og, keep_ag):
        copy.wait()


def block_and_back(remote, acts, obs, flags, levels, cot, sqw, mlpw, gain, sqm=None, mlpm=None):
    tokens, width = acts.shape
    keys, samples = obs.shape[0], obs.shape[1]
    rows = HEADS * ACT
    wide = mlpw.shape[2]
    any_space = pl.BlockSpec(memory_space=pl.ANY)
    in_vmem = pl.BlockSpec(memory_space=VMEM)
    sem = pltpu.SemaphoreType.DMA
    ins = dict(flags=flags, levels=levels, acts=acts, obs=obs, cot=cot, sqw=sqw, mlpw=mlpw, gain=gain)
    outs = dict(
        output=jax.ShapeDtypeStruct(acts.shape, F32),
        ag=jax.ShapeDtypeStruct(acts.shape, F32),
        og=jax.ShapeDtypeStruct(obs.shape, BF16),
    )
    grads = GRID + (WIRE, LANES)
    scratch = dict(
        obs_v=VMEM((KEYS_PAD, samples, width), BF16),
        acts_v=VMEM(acts.shape, F32),
        cot_v=VMEM(acts.shape, F32),
        mem=VMEM((samples, KEYS_PAD, width), BF16),
        swap=VMEM((256, 256), BF16),
        sq_all=VMEM((5, width, width), BF16),
        mlp_all=VMEM((2, width, wide), BF16),
        gain_all=VMEM((2, width), F32),
        wkh=VMEM((HEADS * width, width), BF16),
        wvh=VMEM((HEADS * width, width), BF16),
        first=VMEM((tokens, width), BF16),
        query=VMEM((tokens, width), BF16),
        xhat=VMEM((tokens, width), F32),
        rstd=VMEM((tokens, 1), F32),
        probs=VMEM((samples, rows, KEYS_PAD), F32),
        pds_v=VMEM((samples, 2 * rows, KEYS_PAD), BF16),
        sides_v=VMEM((samples, 2 * rows, width), BF16),
        u=VMEM((tokens, HEADS * width), BF16),
        dq_wide=VMEM((tokens, HEADS * width), BF16),
        mixed=VMEM((tokens, width), BF16),
        second=VMEM((tokens, width), BF16),
        active=VMEM((tokens, wide), BF16),
        dhidden=VMEM((tokens, wide), BF16),
        out_low=VMEM((tokens, width), BF16),
        dres_low=VMEM((tokens, width), BF16),
        dres=VMEM((tokens, width), F32),
        dmixed=VMEM((tokens, width), BF16),
        dquery=VMEM((tokens, width), BF16),
        out_v=VMEM((tokens, width), F32),
        ag_v=VMEM((tokens, width), F32),
        angle=VMEM((samples, width // 2), F32),
        embed=VMEM((samples, width), BF16),
        stamps=VMEM((samples, 8, width), F32),
        gain_acc=VMEM((8, width), F32),
        flags_s=pltpu.SMEM(flags.shape, jnp.int32),
        levels_s=pltpu.SMEM(levels.shape, jnp.int32),
        in_sems=sem((10,)),
        out_sems=sem((3,)),
    )
    extra = {}
    if remote:
        ins.update(sqm=sqm, mlpm=mlpm)
        outs.update(out=jax.ShapeDtypeStruct((3, WIRE, LANES), F32))
        chunks = len(CHUNKS)
        scratch.update(
            grads=VMEM(grads, F32),
            sqw_v=VMEM(sqw.shape, F32),
            mlpw_v=VMEM(mlpw.shape, F32),
            gain_v=VMEM(gain.shape, F32),
            sqm_v=VMEM(sqm.shape, F32),
            mlpm_v=VMEM(mlpm.shape, F32),
            wire=VMEM(grads, BF16),
            edge=VMEM((16, LANES), F32),
            gsend=sem((chunks, 6)),
            grecv=sem((chunks, 6)),
            send0=VMEM((4, 2, 2, WIRE, LANES), BF16),
            got_core=VMEM((4, 2, 2, WIRE, LANES), BF16),
            sum1=VMEM((4, 2, 2, WIRE, LANES), F32),
            send1=VMEM((4, 2, WIRE, LANES), BF16),
            got1=VMEM((4, 2, WIRE, LANES), BF16),
            sum2=VMEM((4, 2, WIRE, LANES), F32),
            send2=VMEM((4, WIRE, LANES), BF16),
            got2=VMEM((4, WIRE, LANES), BF16),
            sum3=VMEM((4, WIRE, LANES), F32),
            send3=VMEM((3, WIRE, LANES), BF16),
            got3=VMEM((3, WIRE, LANES), BF16),
            moment=VMEM((WIRE, LANES), F32),
            slabs_sq=VMEM((32, SQ_ROWS, LANES), F32),
            slabs_mlp=VMEM((32, MLP_ROWS, LANES), BF16),
            moment_low=VMEM((2 * MLP_ROWS, LANES), BF16),
            back_mlp=VMEM((2, MLP_ROWS, LANES), BF16),
            result_sq=VMEM((32, SQ_ROWS, LANES), F32),
            result_mlp=VMEM((32, MLP_ROWS, LANES), BF16),
            cur=VMEM((width, wide), F32),
            cur_low=VMEM((width, wide), BF16),
            send=sem((chunks, 6)),
            recv=sem((chunks, 6)),
            own_send=sem((7,)),
            own_recv=sem((1,)),
            back_send=sem((32,)),
            back_recv=sem((7,)),
        )
        extra = dict(collective_id=0, has_side_effects=True)
        outs = {name: VMEM(like.shape, like.dtype) for name, like in outs.items()}
    else:
        outs.update(grads=jax.ShapeDtypeStruct(grads, F32))
    names = tuple(ins) + tuple(outs) + tuple(scratch)
    stay = [pltpu.with_memory_space_constraint(value, pltpu.HBM) for value in ins.values()]
    results = pl.pallas_call(
        functools.partial(block_kernel, names, remote),
        out_shape=tuple(outs.values()),
        in_specs=[any_space] * len(ins),
        out_specs=[any_space] * 3 + [in_vmem],
        scratch_shapes=list(scratch.values()),
        compiler_params=pltpu.CompilerParams(vmem_limit_bytes=46 << 20, **extra),
        name="block_and_back",
    )(*stay)
    return Refs(zip(outs, results))


PARTS = 7


def finish_kernel(names, rate, *args):
    r = Refs(zip(names, args))
    sems = r.sems
    keys = r.og.shape[0]
    step = keys // PARTS

    def leave(part):
        block = pl.ds(part * step, step)
        return pltpu.make_async_copy(r.og_v.at[block], r.og.at[block], sems.at[part])

    more = PARTS
    moves = []
    if hasattr(r, "wire"):
        pairs = [(r.sqw, r.sqw_v), (r.mlpw, r.mlpw_v), (r.gain, r.gain_v), (r.gainm, r.gainm_v)]
        pairs += [(r.output, r.output_f), (r.ag, r.ag_f)]
        for source, target in pairs:
            moves.append(pltpu.make_async_copy(source, target, sems.at[more]))
            moves[-1].start()
            more += 1
    for part in range(PARTS):

        def widen(j, _):
            r.og_v[j] = r.low[j].astype(F32)
            return 0

        lax.fori_loop(part * step, (part + 1) * step, widen, 0, unroll=4)
        leave(part).start()
    for copy in moves[:4]:
        copy.wait()
    if hasattr(r, "wire"):
        finish_weights(r, rate)
    for part in range(PARTS):
        leave(part).wait()
    for copy in moves[4:]:
        copy.wait()


def finish_weights(r, rate):
    wire = r.wire
    me = lax.axis_index("dp")
    for m in range(5):
        for j in range(2):
            rows, columns = pl.ds(SQ_AT[m] + j * TILE, TILE), pl.ds(j * LANES, LANES)
            r.sqg[m, :, columns] = wire[0, rows, :]
            r.sqm[m, :, columns] = wire[1, rows, :]
            r.sqn[m, :, columns] = r.sqw_v[m, :, columns] - SQ_RATES[m] * wire[2, rows, :]
    r.sqc[...] = r.sqn[...].astype(BF16)
    for m in range(2):
        for j in range(8):
            rows, columns = pl.ds(m * MLP_ROWS + j * TILE, TILE), pl.ds(j * LANES, LANES)
            r.mlpg[m, :, columns] = wire[0, rows, :]
            r.mlpm[m, :, columns] = wire[1, rows, :]
            r.mlpn[m, :, columns] = r.mlpw_v[m, :, columns] - MLP_RATES[m] * wire[2, rows, :]
    r.mlpc[...] = r.mlpn[...].astype(BF16)
    tile = wire[0, pl.ds(GAIN_BASE, TILE), :]
    turned = pltpu.roll(tile, (LANES - (me % 16) * TILE) % LANES, 1)
    at = me // 16
    for norm in range(2):
        pair = turned[2 * norm : 2 * norm + 2, 0:TILE]
        row = jnp.where(at == 0, pair[0:1, :], pair[1:2, :])
        new = 0.5 * r.gainm_v[norm : norm + 1, :] + row
        r.gg[norm : norm + 1, :] = row
        r.gm[norm : norm + 1, :] = new
        r.gn[norm : norm + 1, :] = r.gain_v[norm : norm + 1, :] - rate * new


def finish(rate, made, sqw=None, mlpw=None, gain=None, gainm=None):
    any_space = pl.BlockSpec(memory_space=pl.ANY)
    in_vmem = pl.BlockSpec(memory_space=VMEM)
    ins = dict(low=made.og)
    outs = dict(og=jax.ShapeDtypeStruct(made.og.shape, F32))
    near, far = 1, 1
    if hasattr(made, "out"):
        ins.update(output=made.output, ag=made.ag, wire=made.out, sqw=sqw, mlpw=mlpw, gain=gain, gainm=gainm)
        like = jax.ShapeDtypeStruct
        near, far = 4, 3
        outs.update(
            output_f=like(made.output.shape, F32),
            ag_f=like(made.ag.shape, F32),
            sqg=like(sqw.shape, F32),
            sqm=like(sqw.shape, F32),
            sqn=like(sqw.shape, F32),
            sqc=like(sqw.shape, BF16),
            mlpg=like(mlpw.shape, F32),
            mlpm=like(mlpw.shape, F32),
            mlpn=like(mlpw.shape, F32),
            mlpc=like(mlpw.shape, BF16),
            gg=like(gain.shape, F32),
            gm=like(gain.shape, F32),
            gn=like(gain.shape, F32),
        )
    scratch = dict(
        og_v=VMEM(made.og.shape, F32),
        sems=pltpu.SemaphoreType.DMA((PARTS + 6,)),
    )
    if hasattr(made, "out"):
        scratch.update(
            sqw_v=VMEM(sqw.shape, F32),
            mlpw_v=VMEM(mlpw.shape, F32),
            gain_v=VMEM(gain.shape, F32),
            gainm_v=VMEM(gainm.shape, F32),
        )
    names = tuple(ins) + tuple(outs) + tuple(scratch)
    made_here = list(ins.values())
    stay = [pltpu.with_memory_space_constraint(value, pltpu.HBM) for value in made_here[near:]]
    results = pl.pallas_call(
        functools.partial(finish_kernel, names, rate),
        out_shape=tuple(outs.values()),
        in_specs=[in_vmem] * near + [any_space] * (len(ins) - near),
        out_specs=[any_space] * far + [in_vmem] * (len(outs) - far),
        scratch_shapes=list(scratch.values()),
        compiler_params=pltpu.CompilerParams(vmem_limit_bytes=16 << 20),
        name="finish",
    )(*made_here[:near], *stay)
    return Refs(zip(outs, results))


HIGH_PRECISION = lax.Precision.HIGHEST


def plain_orthogonalize(matrix):
    current = matrix / (jnp.sqrt(jnp.sum(matrix * matrix)) + 1e-07)
    for turn in range(5):
        gram = jnp.dot(current, current.T, precision=HIGH_PRECISION)
        poly = COEF_B * gram + COEF_C * jnp.dot(gram, gram, precision=HIGH_PRECISION)
        current = COEF_A * current + jnp.dot(poly, current, precision=HIGH_PRECISION)
    return current


def pick_owned(stack, owners, device):
    chosen = jnp.zeros_like(stack[0])
    for index in range(len(owners)):
        chosen = jnp.where(device == owners[index], stack[index], chosen)
    return chosen


def is_owner(owners, device):
    flag = device < 0
    for owner in owners:
        flag = jnp.logical_or(flag, device == owner)
    return flag


def from_wire(grads):
    def matrix(base, tiles):
        part = grads[:, base : base + tiles * TILE, :].reshape(-1, tiles, TILE, LANES)
        return part.transpose(0, 2, 1, 3).reshape(-1, tiles * LANES)

    square = jnp.stack([matrix(SQ_AT[m], 2) for m in range(5)])
    mlp = jnp.stack([matrix(m * MLP_ROWS, 8) for m in range(2)])
    return square, mlp, grads[0, GAIN_BASE : GAIN_BASE + 4, :].reshape(2, 2 * LANES)


def update_by_collectives(
    grads, square_weights, mlp_weights, gains, square_moment, mlp_moment, gain_moment, rate
):
    square_local, mlp_local, gain_local = from_wire(grads)
    square_grad, mlp_grad, gain_grad = (
        lax.psum_scatter(square_local, "dp", scatter_dimension=1, tiled=True),
        lax.psum_scatter(mlp_local, "dp", scatter_dimension=1, tiled=True),
        lax.psum_scatter(gain_local, "dp", scatter_dimension=1, tiled=True),
    )
    square_moment_new = 0.5 * square_moment + square_grad
    mlp_moment_new = 0.5 * mlp_moment + mlp_grad
    gain_moment_new = 0.5 * gain_moment + gain_grad
    device = lax.axis_index("dp")
    count = lax.axis_size("dp")
    square_owners = [index * count // 7 for index in range(5)]
    mlp_owners = [(index + 5) * count // 7 for index in range(2)]
    square_full, mlp_full = (
        lax.all_gather(square_moment_new, "dp", axis=1, tiled=True),
        lax.all_gather(mlp_moment_new, "dp", axis=1, tiled=True),
    )
    mine_square = pick_owned(square_full, square_owners, device)
    mine_mlp = pick_owned(mlp_full, mlp_owners, device)
    made_square = lax.cond(
        is_owner(square_owners, device), plain_orthogonalize, jnp.zeros_like, mine_square
    )
    made_mlp = lax.cond(is_owner(mlp_owners, device), plain_orthogonalize, jnp.zeros_like, mine_mlp)
    stack_square = jnp.stack(
        [jnp.where(device == owner, made_square, 0.0) for owner in square_owners]
    )
    stack_mlp = jnp.stack([jnp.where(device == owner, made_mlp, 0.0) for owner in mlp_owners])
    square_ortho, mlp_ortho = (
        lax.psum_scatter(stack_square, "dp", scatter_dimension=1, tiled=True),
        lax.psum_scatter(stack_mlp, "dp", scatter_dimension=1, tiled=True),
    )
    square_new = square_weights - jnp.array(SQ_RATES, F32)[:, None, None] * square_ortho
    mlp_new = mlp_weights - jnp.array(MLP_RATES, F32)[:, None, None] * mlp_ortho
    gains_new = gains - rate * gain_moment_new
    return (
        square_grad,
        square_moment_new,
        square_new,
        square_new.astype(BF16),
        mlp_grad,
        mlp_moment_new,
        mlp_new,
        mlp_new.astype(BF16),
        gain_grad,
        gain_moment_new,
        gains_new,
    )


def per_device(
    actions,
    observed,
    camera_flags,
    noise_levels,
    cotangent,
    square_weights,
    mlp_weights,
    gains,
    square_moment,
    mlp_moment,
    gain_moment,
):
    count = lax.axis_size("dp")
    rate = 0.1 / math.sqrt(actions.shape[0] * count)
    by_key = observed.transpose(1, 0, 2)
    ins = (actions, by_key, camera_flags, noise_levels, cotangent)
    if count == math.prod(GRID):
        made = block_and_back(True, *ins, square_weights, mlp_weights, gains, square_moment, mlp_moment)
        done = finish(rate, made, square_weights, mlp_weights, gains, gain_moment)
        output, actions_grad = done.output_f, done.ag_f
        d = done
        rest = (d.sqg, d.sqm, d.sqn, d.sqc, d.mlpg, d.mlpm, d.mlpn, d.mlpc, d.gg, d.gm, d.gn)
    else:
        square_all, mlp_all = (
            lax.all_gather(square_weights.astype(BF16), "dp", axis=1, tiled=True),
            lax.all_gather(mlp_weights.astype(BF16), "dp", axis=1, tiled=True),
        )
        gain_all = lax.all_gather(gains, "dp", axis=1, tiled=True)
        made = block_and_back(False, *ins, square_all, mlp_all, gain_all)
        done = finish(rate, made)
        output, actions_grad = made.output, made.ag
        grads = made.grads.reshape(-1, WIRE, LANES)
        rest = update_by_collectives(
            grads, square_weights, mlp_weights, gains, square_moment, mlp_moment, gain_moment, rate
        )
    observed_grad = done.og.transpose(1, 0, 2)
    return (output, actions_grad, observed_grad) + tuple(rest)


def solution(mesh):
    rows, cube, flat = P("dp", None), P("dp", None, None), P("dp")
    stacked, pair = P(None, "dp", None), P(None, "dp")
    return jax.shard_map(
        per_device,
        mesh=mesh,
        in_specs=(rows, cube, flat, flat, rows, stacked, stacked, pair, stacked, stacked, pair),
        out_specs=(rows, rows, cube) + (stacked,) * 8 + (pair,) * 3,
        check_vma=False,
    )
```

```python
import functools
import math

import jax
import jax.numpy as jnp
from jax import lax
from jax.experimental import pallas as pl
from jax.experimental.pallas import tpu as pltpu
from jax.sharding import PartitionSpec as P

HEADS = 4
ACT = 16
OBS_FULL = 196
OBS_FEW = 49
COEF_A = 3.4445
COEF_B = -4.775
COEF_C = 2.0315
F32 = jnp.float32
BF16 = jnp.bfloat16
MESH = pl.DeviceIdType.MESH
VMEM = pltpu.VMEM
NN = (((1,), (0,)), ((), ()))
NT = (((1,), (1,)), ((), ()))
TN = (((0,), (0,)), ((), ()))

LANES = 128
TILE = 8
MLP_ROWS = 64
SQ_ROWS = 16
SQ_AT = (160, 192, 176, 128, 144)
GAIN_BASE = 208
WIRE = 224
PIECES = ((0, 64), (64, 64), (128, 32), (160, 32), (192, 32))
PIECE_X_FIRST = (True, False, True, True, False)
DIRECT_PIECES = (3, 4)
CHUNKS = ((0, 64), (64, 64), (128, 32), (160, 32), (192, 16), (208, 16))
X_FIRST = (True, False, True, False, True, False)
DIRECT = (2, 3, 4, 5)
COMPLETES = ((0,), (1,), (5, 6), (2, 4), (3,), ())
MLP_RATES = (1.0, 0.5)
SQ_RATES = (0.5, 0.5, 0.5, 0.5, 4.0)
GRID = (4, 2, 2, 2)
OWNERS = (8, 22, 14, 16, 11, 21, 13)
SHIFTS = (0.0, 0.0, 0.4, 0.8, 0.8)
KEYS_PAD = 208
GROUP = 16
ROWS = 512


class Refs:
    def __init__(self, pairs):
        self.__dict__.update(pairs)


def dot(left, right, dims=NN):
    return lax.dot_general(left, right, dims, preferred_element_type=F32)


def place():
    me = lax.axis_index("dp")
    return me, me // 8, (me // 4) % 2, (me // 2) % 2, me % 2


def device_at(z, y, x, c):
    return ((z * 2 + y) * 2 + x) * 2 + c


def link(src, dst, send, recv, device):
    return pltpu.make_async_remote_copy(
        src_ref=src,
        dst_ref=dst,
        send_sem=send,
        recv_sem=recv,
        device_id=(device,),
        device_id_type=MESH,
    )


def greet(device):
    pl.semaphore_signal(
        pltpu.get_barrier_semaphore(), inc=1, device_id=(device,), device_id_type=MESH
    )


def normalize(values):
    centred = values - jnp.mean(values, -1, keepdims=True)
    scale = lax.rsqrt(jnp.mean(centred * centred, -1, keepdims=True) + 1e-05)
    return centred * scale, scale


def norm_back(grad, hat, scale):
    mean_one = jnp.mean(grad, -1, keepdims=True)
    mean_two = jnp.mean(grad * hat, -1, keepdims=True)
    return scale * (grad - mean_one - hat * mean_two)


class Gather:
    def __init__(self, r):
        self.r = r
        self.me, self.z, self.y, self.x, self.c = place()

    def hop(self, k, step, part, device):
        return link(part, part, self.r.gsend.at[k, step], self.r.grecv.at[k, step], device)

    def along_z(self, k, step):
        part = self.r.wire.at[self.z, self.y, self.x, self.c, pl.ds(*PIECES[k])]
        return self.hop(k, step, part, device_at((self.z + step + 1) % 4, self.y, self.x, self.c))

    def from_z(self, k, step):
        there = (self.z + 3 - step) % 4
        part = self.r.wire.at[there, self.y, self.x, self.c, pl.ds(*PIECES[k])]
        return self.hop(k, step, part, device_at(there, self.y, self.x, self.c))

    def plane(self, k, second, mine):
        z, y, x, c = self.z, self.y, self.x, self.c
        rows, wire = pl.ds(*PIECES[k]), self.r.wire
        py, px = (y, x) if mine else (1 - y, 1 - x)
        along_x = PIECE_X_FIRST[k] == second
        if along_x:
            part = wire.at[:, y, px, c, rows] if second else wire.at[:, :, px, c, rows]
            return self.hop(k, 3 if second else 4, part, device_at(z, y, 1 - x, c))
        part = wire.at[:, py, x, c, rows] if second else wire.at[:, py, :, c, rows]
        return self.hop(k, 3 if second else 4, part, device_at(z, 1 - y, x, c))

    def across(self, k, step, mine):
        py, px = ((self.y, 1 - self.x), (1 - self.y, self.x), (1 - self.y, 1 - self.x))[step]
        from_y, from_x = (self.y, self.x) if mine else (py, px)
        part = self.r.wire.at[:, from_y, from_x, self.c, pl.ds(*PIECES[k])]
        return self.hop(k, 3 + step, part, device_at(self.z, py, px, self.c))

    def core(self, k, mine):
        part = self.r.wire.at[:, :, :, self.c if mine else 1 - self.c, pl.ds(*PIECES[k])]
        return self.hop(k, 6, part, device_at(self.z, self.y, self.x, 1 - self.c))

    def first(self, *chunks):
        for k in chunks:
            for step in range(3):
                self.along_z(k, step).start()

    def second(self, *chunks):
        for k in chunks:
            for step in range(3):
                self.from_z(k, step).wait_recv()
            if k in DIRECT_PIECES:
                for step in range(3):
                    self.across(k, step, True).start()
            else:
                self.plane(k, True, True).start()

    def third(self, *chunks):
        for k in chunks:
            self.plane(k, True, False).wait_recv()
            self.plane(k, False, True).start()

    def fourth(self, *chunks):
        for k in chunks:
            if k in DIRECT_PIECES:
                for step in range(3):
                    self.across(k, step, False).wait_recv()
            else:
                self.plane(k, False, False).wait_recv()
            self.core(k, True).start()

    def last(self, *chunks):
        for k in chunks:
            self.core(k, False).wait_recv()

    def drain(self):
        for k in range(len(PIECES)):
            for step in range(3):
                self.along_z(k, step).wait_send()
            if k in DIRECT_PIECES:
                for step in range(3):
                    self.across(k, step, True).wait_send()
            else:
                self.plane(k, True, True).wait_send()
                self.plane(k, False, True).wait_send()
            self.core(k, True).wait_send()

    def fill(self, square):
        r = self.r
        spot = (self.z, self.y, self.x, self.c)

        def tiles(source, m, base, number):
            for j in range(number):
                pair = [source[m, :, pl.ds((2 * j + k) * LANES, LANES)] for k in range(2)]
                r.wire[spot + (pl.ds(base + j * 16, 16),)] = jnp.concatenate(pair, axis=0).astype(BF16)

        if not square:
            for m in range(2):
                tiles(r.mlpw_v, m, m * MLP_ROWS, 4)
            return
        for m in range(5):
            tiles(r.sqw_v, m, SQ_AT[m], 1)
        gains, edge = r.gain_v[...], r.edge
        high = gains.astype(BF16).astype(F32)
        middle = (gains - high).astype(BF16).astype(F32)
        edge[...] = jnp.zeros_like(edge)
        edge[0:2, 0:TILE] = high
        edge[2:4, 0:TILE] = middle
        edge[4:6, 0:TILE] = (gains - high - middle).astype(BF16).astype(F32)
        r.wire[spot + (pl.ds(GAIN_BASE, 16),)] = edge[...].astype(BF16)

    def unpack(self, base, number, out, m):
        for j in range(number):
            block = self.r.wire[:, :, :, :, pl.ds(base + j * 16, 16), :].reshape(32, 16, LANES).astype(F32)
            for half in range(2):
                columns = pl.ds((2 * j + half) * LANES, LANES)
                out[m, :, columns] = block[:, half * 8 : half * 8 + 8, :].reshape(256, LANES).astype(BF16)

    def unpack_gains(self):
        edge, wire = self.r.edge, self.r.wire
        for half in range(2):
            total = jnp.zeros((16, LANES), F32)
            for at in range(16):
                d = half * 16 + at
                tile = wire[d // 8, (d // 4) % 2, (d // 2) % 2, d % 2, pl.ds(GAIN_BASE, 16), :].astype(F32)
                total = total + (tile if at == 0 else pltpu.roll(tile, at * TILE, 1))
            edge[...] = total
            self.r.gain_all[:, pl.ds(half * LANES, LANES)] = edge[0:2, :] + edge[2:4, :] + edge[4:6, :]


class Update:
    def __init__(self, r):
        self.r = r
        self.me, self.z, self.y, self.x, self.c = place()

    def hop(self, k, step, src, dst, device):
        return link(src, dst, self.r.send.at[k, step], self.r.recv.at[k, step], device)

    def core(self, k):
        rows = pl.ds(*CHUNKS[k])
        src, dst = self.r.send0.at[:, :, :, rows], self.r.got_core.at[:, :, :, rows]
        return self.hop(k, 0, src, dst, device_at(self.z, self.y, self.x, 1 - self.c))

    def plane(self, k, first):
        rows = pl.ds(*CHUNKS[k])
        to = (self.z, self.y, 1 - self.x, self.c) if X_FIRST[k] == first else (self.z, 1 - self.y, self.x, self.c)
        if first:
            src, dst = self.r.send1.at[:, :, rows], self.r.got1.at[:, :, rows]
        else:
            src, dst = self.r.send2.at[:, rows], self.r.got2.at[:, rows]
        return self.hop(k, 1 if first else 2, src, dst, device_at(*to))

    def across(self, k, step):
        rows = pl.ds(*CHUNKS[k])
        py, px = self.others()[step]
        src, dst = self.r.send_p.at[step, :, rows], self.r.got_p.at[step, :, rows]
        return self.hop(k, 1 + step, src, dst, device_at(self.z, py, px, self.c))

    def others(self):
        return (self.y, 1 - self.x), (1 - self.y, self.x), (1 - self.y, 1 - self.x)

    def along_z(self, k, step):
        rows = pl.ds(*CHUNKS[k])
        there = (self.z + step + 1) % 4
        src = self.r.send3.at[there, rows]
        return self.hop(k, 4 + step, src, self.r.got3.at[step, rows], device_at(there, self.y, self.x, self.c))

    def start(self, k):
        rows = pl.ds(*CHUNKS[k])
        self.r.send0[:, :, :, rows, :] = self.r.grads[:, :, :, 1 - self.c, rows, :].astype(BF16)
        self.core(k).start()

    def one(self, *chunks):
        r = self.r
        for k in chunks:
            rows = pl.ds(*CHUNKS[k])
            self.core(k).wait_recv()
            sum1 = r.sum1
            sum1[:, :, :, rows, :] = r.grads[:, :, :, self.c, rows, :] + r.got_core[:, :, :, rows, :].astype(F32)
            if k in DIRECT:
                for step, (py, px) in enumerate(self.others()):
                    r.send_p[step, :, rows, :] = sum1[:, py, px, rows, :].astype(BF16)
                    self.across(k, step).start()
                continue
            other = sum1[:, :, 1 - self.x, rows, :] if X_FIRST[k] else sum1[:, 1 - self.y, :, rows, :]
            r.send1[:, :, rows, :] = other.astype(BF16)
            self.plane(k, True).start()

    def two(self, *chunks):
        r = self.r
        for k in chunks:
            rows = pl.ds(*CHUNKS[k])
            self.plane(k, True).wait_recv()
            sum1, sum2 = r.sum1, r.sum2
            mine = sum1[:, :, self.x, rows, :] if X_FIRST[k] else sum1[:, self.y, :, rows, :]
            sum2[:, :, rows, :] = mine + r.got1[:, :, rows, :].astype(F32)
            other = 1 - self.y if X_FIRST[k] else 1 - self.x
            r.send2[:, rows, :] = sum2[:, other, rows, :].astype(BF16)
            self.plane(k, False).start()

    def three(self, *chunks):
        r = self.r
        for k in chunks:
            rows = pl.ds(*CHUNKS[k])
            if k in DIRECT:
                total = r.sum1[:, self.y, self.x, rows, :]
                for step in range(3):
                    self.across(k, step).wait_recv()
                    total = total + r.got_p[step, :, rows, :].astype(F32)
            else:
                self.plane(k, False).wait_recv()
                mine = self.y if X_FIRST[k] else self.x
                total = r.sum2[:, mine, rows, :] + r.got2[:, rows, :].astype(F32)
            r.sum3[:, rows, :] = total
            r.send3[:, rows, :] = total.astype(BF16)
            if k in DIRECT:
                own = r.sum3[self.z, rows, :] + 0.5 * r.moment[rows, :]
                r.send3[self.z, rows, :] = own.astype(BF16)
                for index in COMPLETES[k]:
                    self.part_to_owner(index)
            for step in range(3):
                self.along_z(k, step).start()

    def part_to_owner(self, index):
        @pl.when(self.me != OWNERS[index])
        def _():
            self.to_owner(index).start()

        @pl.when(self.me == OWNERS[index])
        def _():
            src, dst = self.own_part(index)
            pltpu.make_async_copy(src, dst, self.r.own_recv.at[0]).start()

    def own_part(self, index):
        if index < 2:
            return self.r.moment_low.at[pl.ds(index * MLP_ROWS, MLP_ROWS)], self.r.slabs_mlp.at[self.me]
        rows = pl.ds(SQ_AT[index - 2], SQ_ROWS)
        return self.r.send3.at[:, rows], self.r.slabs_sq.at[self.z, self.me % 8]

    def result(self, index):
        return self.r.result_mlp if index < 2 else self.r.result_sq

    def to_owner(self, index):
        src, dst = self.own_part(index)
        return link(src, dst, self.r.own_send.at[index], self.r.own_recv.at[0], OWNERS[index])

    def four(self, *chunks):
        r = self.r
        moment, out = r.moment, r.out
        for k in chunks:
            rows = pl.ds(*CHUNKS[k])
            total = r.sum3[self.z, rows, :]
            for step in range(3):
                self.along_z(k, step).wait_recv()
                total = total + r.got3[step, rows, :].astype(F32)
            out[0, rows, :] = total
            new = 0.5 * moment[rows, :] + total
            moment[rows, :] = new
            if k < 2:
                r.moment_low[rows, :] = new.astype(BF16)
            if k not in DIRECT:
                for index in COMPLETES[k]:
                    self.part_to_owner(index)

    def old_moment(self):
        r = self.r
        moment = r.moment
        for m in range(2):
            for j in range(8):
                moment[pl.ds(m * MLP_ROWS + j * TILE, TILE), :] = r.mlpm_v[m, :, pl.ds(j * LANES, LANES)]
        for m in range(5):
            for j in range(2):
                moment[pl.ds(SQ_AT[m] + j * TILE, TILE), :] = r.sqm_v[m, :, pl.ds(j * LANES, LANES)]
        moment[pl.ds(GAIN_BASE, 16), :] = jnp.zeros((16, LANES), F32)

    def orthogonalize(self):
        r = self.r
        cur = r.cur
        rows = lax.broadcasted_iota(jnp.int32, (256, 256), 0)
        diagonal = rows == lax.broadcasted_iota(jnp.int32, (256, 256), 1)

        low = r.cur_low

        def load(rows, j, pair):
            for side in range(2):
                columns = pl.ds((2 * j + side) * LANES, LANES)
                part = pair[:, side * TILE : (side + 1) * TILE, :].reshape(-1, LANES)
                cur[rows, columns] = part
                low[rows, columns] = part.astype(BF16)

        def load_mlp():
            for j in range(4):
                load(pl.ds(0, 256), j, r.slabs_mlp[:, pl.ds(j * 16, 16), :].astype(F32))

        def load_sq():
            for to in range(4):
                pair = r.slabs_sq[0, :, to].astype(F32)
                for plane in range(1, 4):
                    pair = pair + r.slabs_sq[plane, :, to].astype(F32)
                load(pl.ds(to * 64, 64), 0, pair)

        def run(slabs, fetch, result, tiles):
            pltpu.make_async_copy(slabs, slabs, r.own_recv.at[0]).wait()
            fetch()
            scale = 1.0
            for turn, shift in enumerate(SHIFTS):
                whole = low[:, 0 : tiles * LANES]
                off = dot(whole, whole, NT)
                if turn == 0:
                    norm = jnp.sum(jnp.sum(jnp.where(diagonal, off, 0.0), axis=0, keepdims=True), axis=1, keepdims=True)
                    scale = 1.0 / (jnp.sqrt(norm) + 1e-07)
                    off = off * (scale * scale)
                if shift:
                    off = off - jnp.where(diagonal, shift, 0.0)
                off_low = off.astype(BF16)
                poly = (COEF_B + 2.0 * COEF_C * shift) * off + COEF_C * dot(off_low, off_low)
                poly = poly.astype(BF16)
                keep = COEF_A + shift * (COEF_B + COEF_C * shift)
                for j in range(tiles // 2):
                    columns = pl.ds(j * 2 * LANES, 2 * LANES)
                    now = keep * cur[:, columns] + dot(poly, low[:, columns])
                    if turn == 0:
                        now = now * scale
                    if turn < len(SHIFTS) - 1:
                        cur[:, columns] = now
                        low[:, columns] = now.astype(BF16)
                    else:
                        parts = [now[:, side * LANES : (side + 1) * LANES].reshape(32, TILE, LANES) for side in range(2)]
                        result[:, pl.ds(j * 16, 16), :] = jnp.concatenate(parts, axis=1).astype(result.dtype)

        mine_mlp = jnp.logical_or(self.me == OWNERS[0], self.me == OWNERS[1])
        mine_sq = self.me < 0
        for device in OWNERS[2:]:
            mine_sq = jnp.logical_or(mine_sq, self.me == device)

        @pl.when(mine_mlp)
        def _():
            run(r.slabs_mlp, load_mlp, r.result_mlp, 8)

        @pl.when(mine_sq)
        def _():
            run(r.slabs_sq, load_sq, r.result_sq, 2)

    def landing(self, index):
        if index < 2:
            return self.r.back_mlp.at[index]
        return self.r.out.at[2, pl.ds(SQ_AT[index - 2], SQ_ROWS)]

    def give_back(self, index, device):
        result = self.result(index)
        return link(
            result.at[device], self.landing(index),
            self.r.back_send.at[device], self.r.back_recv.at[index], device,
        )

    def give_all(self):
        r = self.r
        for index in range(7):
            result = self.result(index)

            @pl.when(self.me == OWNERS[index])
            def _():
                def send_one(step, _):
                    self.give_back(index, (self.me + step) % 32).start()
                    return 0

                lax.fori_loop(1, 32, send_one, 0)
                pltpu.make_async_copy(result.at[self.me], self.landing(index), r.back_recv.at[index]).start()

    def take_all(self):
        for index in range(7):
            result = self.result(index)
            pltpu.make_async_copy(result.at[0], self.landing(index), self.r.back_recv.at[index]).wait()
        for index in range(2):
            rows = pl.ds(index * MLP_ROWS, MLP_ROWS)
            self.r.out[2, rows, :] = self.r.back_mlp[index].astype(F32)

    def drain(self):
        for k in range(len(CHUNKS)):
            self.core(k).wait_send()
            if k in DIRECT:
                for step in range(3):
                    self.across(k, step).wait_send()
            else:
                self.plane(k, True).wait_send()
                self.plane(k, False).wait_send()
            for step in range(3):
                self.along_z(k, step).wait_send()
        for index in range(7):

            @pl.when(self.me != OWNERS[index])
            def _():
                self.to_owner(index).wait_send()

    def drain_owner(self):
        for index in range(7):

            @pl.when(self.me == OWNERS[index])
            def _():
                def wait_one(step, _):
                    self.give_back(index, (self.me + step) % 32).wait_send()
                    return 0

                lax.fori_loop(1, 32, wait_one, 0)


def greet_all():
    me, z, y, x, c = place()
    greet(device_at(z, y, x, 1 - c))
    greet(device_at(z, y, 1 - x, c))
    greet(device_at(z, 1 - y, x, c))
    greet(device_at(z, 1 - y, 1 - x, c))
    for step in range(1, 4):
        greet(device_at((z + step) % 4, y, x, c))
    owner = me < 0
    for device in OWNERS:
        owner = jnp.logical_or(owner, me == device)

        @pl.when(me != device)
        def _():
            greet(device)

    @pl.when(owner)
    def _():
        def greet_other(step, _):
            greet((me + step) % 32)
            return 0

        lax.fori_loop(1, 32, greet_other, 0)

    is_owner = owner.astype(jnp.int32)
    return 7 + 7 - is_owner + 31 * is_owner


def block_kernel(names, remote, *args):
    r = Refs(zip(names, args))
    keys, samples = r.obs.shape[0], r.obs.shape[1]
    tokens, width = r.acts.shape
    head_dim, half, per = width // HEADS, width // 2, ROWS // ACT
    wide = r.mlp_all.shape[2]
    groups = samples // GROUP
    in_sems, out_sems = r.in_sems, r.out_sems

    if remote:
        own = (r.sqw_v, r.mlpw_v, r.gain_v)
    else:
        own = (r.sq_all, r.mlp_all, r.gain_all)
    loads = list(zip((r.sqw, r.mlpw, r.gain), own))
    loads += [(r.acts, r.acts_v), (r.obs, r.obs_v.at[pl.ds(0, keys)]), (r.cot, r.cot_v)]
    if remote:
        loads += [(r.sqm, r.sqm_v), (r.mlpm, r.mlpm_v)]
    loads += [(r.flags, r.flags_s), (r.levels, r.levels_s)]
    copies = [pltpu.make_async_copy(a, b, in_sems.at[i]) for i, (a, b) in enumerate(loads)]

    def arrive(*which):
        for i in which:
            copies[i].wait()

    for copy in copies:
        copy.start()
    if remote:
        gather, update = Gather(r), Update(r)
        expected = greet_all()
        arrive(0, 2)
        gather.fill(True)
        pl.semaphore_wait(pltpu.get_barrier_semaphore(), expected)
        gather.first(3, 4)
        arrive(1)
        gather.fill(False)

    arrive(3)

    def hats(i, _):
        rows = pl.ds(pl.multiple_of(i * ROWS, ROWS), ROWS)
        hat, scale = normalize(r.acts_v[rows, :])
        r.xhat[rows, :] = hat
        r.rstd[rows, :] = scale
        return 0

    lax.fori_loop(0, tokens // ROWS, hats, 0)

    mem, obs_v = r.mem, r.obs_v
    batch = 16
    chunks = KEYS_PAD // batch
    swap = r.swap
    row = lax.broadcasted_iota(jnp.int32, swap.shape, 0)
    column = lax.broadcasted_iota(jnp.int32, swap.shape, 1)
    swap[...] = jnp.where(column == (row % batch) * batch + row // batch, 1.0, 0.0).astype(BF16)

    def turn(part, low, high):
        def one(j, _):
            at = pl.ds(pl.multiple_of(j * batch, batch), batch)
            here = pl.ds(part * batch, batch)
            block = obs_v[at, here, :].reshape(batch * batch, width)
            mem[here, at, :] = dot(swap[...], block).astype(BF16).reshape(batch, batch, width)
            return 0

        lax.fori_loop(low, high, one, 0, unroll=high - low)

    whole = chunks - 1
    arrive(4)
    turn(0, 0, whole // 2)
    if remote:
        gather.second(3, 4)
        gather.first(2, 0, 1)
    turn(0, whole // 2, whole)
    if remote:
        gather.fourth(3, 4)
    turn(1, 0, whole // 2)
    if remote:
        gather.second(2, 0, 1)
    turn(1, whole // 2, whole)
    arrive(len(copies) - 1, len(copies) - 2)
    freqs = jnp.exp(
        lax.broadcasted_iota(jnp.int32, (1, half), 1).astype(F32) * F32(-math.log(10000.0)) / half
    )
    for s in range(samples):
        r.angle[s : s + 1, :] = r.levels_s[s].astype(F32) * freqs
    r.embed[:, 0:half] = jnp.sin(r.angle[...]).astype(BF16)
    r.embed[:, half:width] = jnp.cos(r.angle[...]).astype(BF16)
    if remote:
        arrive(6, 7)
        update.old_moment()
        gather.third(2, 0, 1)
        gather.last(3, 4)
        for m in range(3):
            gather.unpack(SQ_AT[m], 1, r.sq_all, m)
        gather.unpack_gains()
    else:
        arrive(0, 1, 2)

    sq, mlp = r.sq_all, r.mlp_all
    wkh, wvh = r.wkh, r.wvh
    lane = lax.broadcasted_iota(jnp.int32, (width, width), 1)

    def split_heads(out, weight):
        weight = weight.astype(F32)
        for h in range(HEADS):
            out[pl.ds(h * width, width), :] = jnp.where(lane // head_dim == h, weight, 0.0).astype(BF16)

    split_heads(wkh, sq[2])
    g1, g2 = r.gain_all[0:1, :], r.gain_all[1:2, :]

    obs_v[keys] = dot(r.embed[...], sq[0]).astype(BF16)
    obs_v[keys + 1 :] = jnp.zeros((KEYS_PAD - keys - 1, samples, width), BF16)
    for part in range(samples // batch):
        turn(part, whole, chunks)

    sides, weights = r.sides_v, r.pds_v

    def make_queries(i, _):
        rows = pl.ds(pl.multiple_of(i * ROWS, ROWS), ROWS)
        first = (r.xhat[rows, :] * g1).astype(BF16)
        r.first[rows, :] = first
        q = dot(first, sq[1]).astype(BF16)
        r.query[rows, :] = q
        here = pl.ds(i * per, per)
        for h in range(HEADS):
            wk = wkh[pl.ds(h * width, width), :]
            value = (dot(q, wk, NT) * 0.125).astype(BF16).reshape(per, ACT, width)
            sides[here, pl.ds((HEADS + h) * ACT, ACT), :] = value
        return 0

    lax.fori_loop(0, tokens // ROWS, make_queries, 0)

    key = lax.broadcasted_iota(jnp.int32, (1, KEYS_PAD), 1)
    low_rows, high_rows = pl.ds(0, HEADS * ACT), pl.ds(HEADS * ACT, HEADS * ACT)

    ones = jnp.ones((KEYS_PAD, LANES), BF16)

    def attend(g, _):
        ids = [g * GROUP + k for k in range(GROUP)]
        scores = [dot(sides[s, high_rows, :], mem[s], NT) for s in ids]
        lows = []
        for s, score in zip(ids, scores):
            count = OBS_FEW + (OBS_FULL - OBS_FEW) * r.flags_s[s]
            score = score + jnp.where((key < count) | (key == OBS_FULL), 0.0, -1000000000.0)
            expo = jnp.exp(score - jnp.max(score, -1, keepdims=True))
            low = expo.astype(BF16)
            part = 1.0 / dot(low, ones)
            probs = expo * jnp.concatenate([part, part[:, 0 : KEYS_PAD - LANES]], axis=1)
            r.probs[s] = probs
            weights[s, low_rows, :] = probs.astype(BF16)
            lows.append((low, jnp.concatenate([part, part], axis=1)))
        for s, (low, part) in zip(ids, lows):
            u = (dot(low, mem[s]) * part).astype(BF16)
            rows = pl.ds(pl.multiple_of(s * ACT, ACT), ACT)
            for h in range(HEADS):
                r.u[rows, pl.ds(h * width, width)] = u[h * ACT : (h + 1) * ACT, :]
        return 0

    lax.fori_loop(0, groups // 2, attend, 0)
    if remote:
        gather.fourth(2, 0, 1)
    lax.fori_loop(groups // 2, groups, attend, 0)
    if remote:
        gather.last(2, 0, 1)
        for m in range(3, 5):
            gather.unpack(SQ_AT[m], 1, sq, m)
        for m in range(2):
            gather.unpack(m * MLP_ROWS, 4, mlp, m)
    split_heads(wvh, sq[3])

    gain_acc = r.gain_acc
    gain_acc[...] = jnp.zeros_like(gain_acc)
    arrive(5)

    def feed(i, _):
        rows = pl.ds(pl.multiple_of(i * ROWS, ROWS), ROWS)
        mixed = dot(r.u[rows, :], wvh[...]).astype(BF16)
        r.mixed[rows, :] = mixed
        resid = r.acts_v[rows, :] + dot(mixed, sq[4])
        hat, scale = normalize(resid)
        second = (hat * g2).astype(BF16)
        r.second[rows, :] = second
        cot = r.cot_v[rows, :]
        out_low = cot.astype(BF16)
        r.out_low[rows, :] = out_low
        for c in range(wide // 256):
            columns = pl.ds(c * 256, 256)
            v = dot(second, mlp[0, :, columns])
            square = v * v
            t = jnp.tanh(0.7978845608 * (v + 0.044715 * square * v))
            r.active[rows, columns] = (0.5 * v * (1.0 + t)).astype(BF16)
            slope = 0.5 * (1.0 + t) + 0.5 * v * (1.0 - t * t) * (0.7978845608 * (1.0 + 0.134145 * square))
            r.dhidden[rows, columns] = (slope * dot(out_low, mlp[1, :, columns])).astype(BF16)
        r.out_v[rows, :] = resid + dot(r.active[rows, :], mlp[1], NT)
        grad_second = dot(r.dhidden[rows, :], mlp[0], NT)
        gain_acc[1:2, :] += jnp.sum(grad_second * hat, 0, keepdims=True)
        dres = cot + norm_back(grad_second * g2, hat, scale)
        r.dres[rows, :] = dres
        low = dres.astype(BF16)
        r.dres_low[rows, :] = low
        gm = dot(low, sq[4], NT).astype(BF16)
        r.dmixed[rows, :] = gm
        here = pl.ds(i * per, per)
        for h in range(HEADS):
            wv = wvh[pl.ds(h * width, width), :]
            sides[here, pl.ds(h * ACT, ACT), :] = dot(gm, wv, NT).astype(BF16).reshape(per, ACT, width)
        return 0

    lax.fori_loop(0, tokens // ROWS, feed, 0)
    keep_out = pltpu.make_async_copy(r.out_v, r.output, out_sems.at[0])
    keep_out.start()

    grads = r.grads

    def put(base, tiles, value):
        for j in range(tiles):
            part = value[:, j * LANES : (j + 1) * LANES].reshape(GRID + (TILE, LANES))
            grads[:, :, :, :, pl.ds(base + j * TILE, TILE), :] = part

    def by_head(left, right):
        turned = left.T
        parts = [
            dot(turned[h * head_dim : (h + 1) * head_dim, :], right[:, pl.ds(h * width, width)])
            for h in range(HEADS)
        ]
        return jnp.concatenate(parts, axis=0).T

    put(0, 8, dot(r.second[...], r.dhidden[...], TN))
    if remote:
        update.start(0)
    put(MLP_ROWS, 8, dot(r.out_low[...], r.active[...], TN))
    if remote:
        update.start(1)
    put(SQ_AT[4], 2, dot(r.mixed[...], r.dres_low[...], TN))
    put(SQ_AT[3], 2, by_head(r.dmixed[...], r.u))
    if remote:
        update.start(2)

    def attend_back(g, _):
        ids = [g * GROUP + k for k in range(GROUP)]
        rises = [dot(sides[s, low_rows, :], mem[s], NT) for s in ids]
        for s, rise in zip(ids, rises):
            probs = r.probs[s]
            both = probs * rise
            weights[s, high_rows, :] = (both - probs * jnp.sum(both, -1, keepdims=True)).astype(BF16)
        for s in ids:
            dq = (dot(weights[s, high_rows, :], mem[s]) * 0.125).astype(BF16)
            rows = pl.ds(pl.multiple_of(s * ACT, ACT), ACT)
            for h in range(HEADS):
                r.dq_wide[rows, pl.ds(h * width, width)] = dq[h * ACT : (h + 1) * ACT, :]
            end = dot(weights[s, :, LANES:KEYS_PAD], sides[s], TN)
            r.stamps[s] = end[64:72, :]
        return 0

    half_groups = groups // 2
    lax.fori_loop(0, half_groups, attend_back, 0)
    if remote:
        update.one(0)
    lax.fori_loop(half_groups, groups, attend_back, 0)
    put(SQ_AT[2], 2, by_head(r.query[...], r.dq_wide))
    stamp_low = r.stamps[:, 4:5, :].reshape(samples, width).astype(BF16)
    put(SQ_AT[0], 2, dot(r.embed[...], stamp_low, TN))
    if remote:
        update.start(3)
        update.one(1, 2)
        update.two(0)

    def memory_back(low, high):
        def one(g, _):
            for k in range(GROUP):
                s = g * GROUP + k
                mem[s] = dot(weights[s], sides[s], TN).astype(BF16)
            return 0

        lax.fori_loop(low, high, one, 0)

    def turn_back(part):
        def one(j, _):
            at = pl.ds(pl.multiple_of(j * batch, batch), batch)
            here = pl.ds(part * batch, batch)
            block = mem[here, at, :].reshape(batch * batch, width)
            obs_v[at, here, :] = dot(swap[...], block).astype(BF16).reshape(batch, batch, width)
            return 0

        lax.fori_loop(0, chunks, one, 0, unroll=chunks)

    def queries_back(i, _):
        rows = pl.ds(pl.multiple_of(i * ROWS, ROWS), ROWS)
        r.dquery[rows, :] = dot(r.dq_wide[rows, :], wkh[...]).astype(BF16)
        return 0

    lax.fori_loop(0, tokens // ROWS, queries_back, 0)
    put(SQ_AT[1], 2, dot(r.first[...], r.dquery[...], TN))
    if remote:
        update.start(4)

    def acts_back(i, _):
        rows = pl.ds(pl.multiple_of(i * ROWS, ROWS), ROWS)
        grad_first = dot(r.dquery[rows, :], sq[1], NT)
        hat = r.xhat[rows, :]
        gain_acc[0:1, :] += jnp.sum(grad_first * hat, 0, keepdims=True)
        r.ag_v[rows, :] = r.dres[rows, :] + norm_back(grad_first * g1, hat, r.rstd[rows, :])
        return 0

    def finish_acts():
        lax.fori_loop(0, tokens // ROWS, acts_back, 0)
        for norm in range(2):
            for j in range(2):
                row = gain_acc[norm : norm + 1, j * LANES : (j + 1) * LANES]
                at = GAIN_BASE + norm * 2 + j
                value = jnp.broadcast_to(row.reshape(1, 1, 1, 1, 1, LANES), GRID + (1, LANES))
                grads[:, :, :, :, at : at + 1, :] = value
        rest = WIRE - GAIN_BASE - 4
        grads[:, :, :, :, GAIN_BASE + 4 : WIRE, :] = jnp.zeros(GRID + (rest, LANES), F32)

    keep_ag = pltpu.make_async_copy(r.ag_v, r.ag, out_sems.at[2])
    keep_og = pltpu.make_async_copy(obs_v.at[pl.ds(0, keys)], r.og, out_sems.at[1])
    if remote:
        update.one(3)
        update.two(1)
        update.three(0)
        finish_acts()
        keep_ag.start()
        update.start(5)
        update.one(4)
        update.three(1, 2)
        memory_back(0, half_groups)
        update.three(3, 4)
        update.one(5)
        update.four(0)
        memory_back(half_groups, groups)
        update.four(1)
        update.three(5)
        update.orthogonalize()
        update.give_all()
        for part in range(samples // batch):
            turn_back(part)
        keep_og.start()
        update.four(2, 3, 4, 5)
        out = r.out
        out[1, :, :] = r.moment[...]
        out[2, pl.ds(GAIN_BASE, 16), :] = jnp.zeros((16, LANES), F32)
        gather.drain()
        update.drain()
        update.take_all()
        update.drain_owner()
    else:
        finish_acts()
        keep_ag.start()
        memory_back(0, groups)
        for part in range(samples // batch):
            turn_back(part)
        keep_og.start()
    for copy in (keep_out, keep_og, keep_ag):
        copy.wait()


def block_and_back(remote, acts, obs, flags, levels, cot, sqw, mlpw, gain, sqm=None, mlpm=None):
    tokens, width = acts.shape
    keys, samples = obs.shape[0], obs.shape[1]
    rows = HEADS * ACT
    wide = mlpw.shape[2]
    any_space = pl.BlockSpec(memory_space=pl.ANY)
    in_vmem = pl.BlockSpec(memory_space=VMEM)
    sem = pltpu.SemaphoreType.DMA
    ins = dict(flags=flags, levels=levels, acts=acts, obs=obs, cot=cot, sqw=sqw, mlpw=mlpw, gain=gain)
    outs = dict(
        output=jax.ShapeDtypeStruct(acts.shape, F32),
        ag=jax.ShapeDtypeStruct(acts.shape, F32),
        og=jax.ShapeDtypeStruct(obs.shape, BF16),
    )
    grads = GRID + (WIRE, LANES)
    scratch = dict(
        obs_v=VMEM((KEYS_PAD, samples, width), BF16),
        acts_v=VMEM(acts.shape, F32),
        cot_v=VMEM(acts.shape, F32),
        mem=VMEM((samples, KEYS_PAD, width), BF16),
        swap=VMEM((256, 256), BF16),
        sq_all=VMEM((5, width, width), BF16),
        mlp_all=VMEM((2, width, wide), BF16),
        gain_all=VMEM((2, width), F32),
        wkh=VMEM((HEADS * width, width), BF16),
        wvh=VMEM((HEADS * width, width), BF16),
        first=VMEM((tokens, width), BF16),
        query=VMEM((tokens, width), BF16),
        xhat=VMEM((tokens, width), F32),
        rstd=VMEM((tokens, 1), F32),
        probs=VMEM((samples, rows, KEYS_PAD), F32),
        pds_v=VMEM((samples, 2 * rows, KEYS_PAD), BF16),
        sides_v=VMEM((samples, 2 * rows, width), BF16),
        u=VMEM((tokens, HEADS * width), BF16),
        dq_wide=VMEM((tokens, HEADS * width), BF16),
        mixed=VMEM((tokens, width), BF16),
        second=VMEM((tokens, width), BF16),
        active=VMEM((tokens, wide), BF16),
        dhidden=VMEM((tokens, wide), BF16),
        out_low=VMEM((tokens, width), BF16),
        dres_low=VMEM((tokens, width), BF16),
        dres=VMEM((tokens, width), F32),
        dmixed=VMEM((tokens, width), BF16),
        dquery=VMEM((tokens, width), BF16),
        out_v=VMEM((tokens, width), F32),
        ag_v=VMEM((tokens, width), F32),
        angle=VMEM((samples, width // 2), F32),
        embed=VMEM((samples, width), BF16),
        stamps=VMEM((samples, 8, width), F32),
        gain_acc=VMEM((8, width), F32),
        flags_s=pltpu.SMEM(flags.shape, jnp.int32),
        levels_s=pltpu.SMEM(levels.shape, jnp.int32),
        in_sems=sem((10,)),
        out_sems=sem((3,)),
    )
    extra = {}
    if remote:
        ins.update(sqm=sqm, mlpm=mlpm)
        outs.update(out=jax.ShapeDtypeStruct((3, WIRE, LANES), F32))
        chunks = len(CHUNKS)
        scratch.update(
            grads=VMEM(grads, F32),
            sqw_v=VMEM(sqw.shape, F32),
            mlpw_v=VMEM(mlpw.shape, F32),
            gain_v=VMEM(gain.shape, F32),
            sqm_v=VMEM(sqm.shape, F32),
            mlpm_v=VMEM(mlpm.shape, F32),
            wire=VMEM(grads, BF16),
            edge=VMEM((16, LANES), F32),
            gsend=sem((chunks, 7)),
            grecv=sem((chunks, 7)),
            send0=VMEM((4, 2, 2, WIRE, LANES), BF16),
            got_core=VMEM((4, 2, 2, WIRE, LANES), BF16),
            sum1=VMEM((4, 2, 2, WIRE, LANES), F32),
            send1=VMEM((4, 2, WIRE, LANES), BF16),
            got1=VMEM((4, 2, WIRE, LANES), BF16),
            sum2=VMEM((4, 2, WIRE, LANES), F32),
            send2=VMEM((4, WIRE, LANES), BF16),
            got2=VMEM((4, WIRE, LANES), BF16),
            sum3=VMEM((4, WIRE, LANES), F32),
            send3=VMEM((4, WIRE, LANES), BF16),
            send_p=VMEM((3, 4, WIRE, LANES), BF16),
            got_p=VMEM((3, 4, WIRE, LANES), BF16),
            got3=VMEM((3, WIRE, LANES), BF16),
            moment=VMEM((WIRE, LANES), F32),
            slabs_sq=VMEM((4, 8, 4, SQ_ROWS, LANES), BF16),
            slabs_mlp=VMEM((32, MLP_ROWS, LANES), BF16),
            moment_low=VMEM((2 * MLP_ROWS, LANES), BF16),
            back_mlp=VMEM((2, MLP_ROWS, LANES), BF16),
            result_sq=VMEM((32, SQ_ROWS, LANES), F32),
            result_mlp=VMEM((32, MLP_ROWS, LANES), BF16),
            cur=VMEM((width, wide), F32),
            cur_low=VMEM((width, wide), BF16),
            send=sem((chunks, 7)),
            recv=sem((chunks, 7)),
            own_send=sem((7,)),
            own_recv=sem((1,)),
            back_send=sem((32,)),
            back_recv=sem((7,)),
        )
        extra = dict(collective_id=0, has_side_effects=True)
        outs = {name: VMEM(like.shape, like.dtype) for name, like in outs.items()}
    else:
        outs.update(grads=jax.ShapeDtypeStruct(grads, F32))
    names = tuple(ins) + tuple(outs) + tuple(scratch)
    stay = [pltpu.with_memory_space_constraint(value, pltpu.HBM) for value in ins.values()]
    results = pl.pallas_call(
        functools.partial(block_kernel, names, remote),
        out_shape=tuple(outs.values()),
        in_specs=[any_space] * len(ins),
        out_specs=[any_space] * 3 + [in_vmem],
        scratch_shapes=list(scratch.values()),
        compiler_params=pltpu.CompilerParams(vmem_limit_bytes=46 << 20, **extra),
        name="block_and_back",
    )(*stay)
    return Refs(zip(outs, results))


PARTS = 7


def finish_kernel(names, rate, *args):
    r = Refs(zip(names, args))
    sems = r.sems
    keys = r.og.shape[0]
    step = keys // PARTS

    def leave(part):
        block = pl.ds(part * step, step)
        return pltpu.make_async_copy(r.og_v.at[block], r.og.at[block], sems.at[part])

    more = PARTS
    moves = []
    if hasattr(r, "wire"):
        pairs = [(r.sqw, r.sqw_v), (r.mlpw, r.mlpw_v), (r.gain, r.gain_v), (r.gainm, r.gainm_v)]
        pairs += [(r.output, r.output_f), (r.ag, r.ag_f)]
        for source, target in pairs:
            moves.append(pltpu.make_async_copy(source, target, sems.at[more]))
            moves[-1].start()
            more += 1
    for part in range(PARTS):

        def widen(j, _):
            r.og_v[j] = r.low[j].astype(F32)
            return 0

        lax.fori_loop(part * step, (part + 1) * step, widen, 0, unroll=4)
        leave(part).start()
    for copy in moves[:4]:
        copy.wait()
    if hasattr(r, "wire"):
        finish_weights(r, rate)
    for part in range(PARTS):
        leave(part).wait()
    for copy in moves[4:]:
        copy.wait()


def finish_weights(r, rate):
    wire = r.wire
    me = lax.axis_index("dp")
    for m in range(5):
        for j in range(2):
            rows, columns = pl.ds(SQ_AT[m] + j * TILE, TILE), pl.ds(j * LANES, LANES)
            r.sqg[m, :, columns] = wire[0, rows, :]
            r.sqm[m, :, columns] = wire[1, rows, :]
            r.sqn[m, :, columns] = r.sqw_v[m, :, columns] - SQ_RATES[m] * wire[2, rows, :]
    r.sqc[...] = r.sqn[...].astype(BF16)
    for m in range(2):
        for j in range(8):
            rows, columns = pl.ds(m * MLP_ROWS + j * TILE, TILE), pl.ds(j * LANES, LANES)
            r.mlpg[m, :, columns] = wire[0, rows, :]
            r.mlpm[m, :, columns] = wire[1, rows, :]
            r.mlpn[m, :, columns] = r.mlpw_v[m, :, columns] - MLP_RATES[m] * wire[2, rows, :]
    r.mlpc[...] = r.mlpn[...].astype(BF16)
    tile = wire[0, pl.ds(GAIN_BASE, TILE), :]
    turned = pltpu.roll(tile, (LANES - (me % 16) * TILE) % LANES, 1)
    at = me // 16
    for norm in range(2):
        pair = turned[2 * norm : 2 * norm + 2, 0:TILE]
        row = jnp.where(at == 0, pair[0:1, :], pair[1:2, :])
        new = 0.5 * r.gainm_v[norm : norm + 1, :] + row
        r.gg[norm : norm + 1, :] = row
        r.gm[norm : norm + 1, :] = new
        r.gn[norm : norm + 1, :] = r.gain_v[norm : norm + 1, :] - rate * new


def finish(rate, made, sqw=None, mlpw=None, gain=None, gainm=None):
    any_space = pl.BlockSpec(memory_space=pl.ANY)
    in_vmem = pl.BlockSpec(memory_space=VMEM)
    ins = dict(low=made.og)
    outs = dict(og=jax.ShapeDtypeStruct(made.og.shape, F32))
    near, far = 1, 1
    if hasattr(made, "out"):
        ins.update(output=made.output, ag=made.ag, wire=made.out, sqw=sqw, mlpw=mlpw, gain=gain, gainm=gainm)
        like = jax.ShapeDtypeStruct
        near, far = 4, 3
        outs.update(
            output_f=like(made.output.shape, F32),
            ag_f=like(made.ag.shape, F32),
            sqg=like(sqw.shape, F32),
            sqm=like(sqw.shape, F32),
            sqn=like(sqw.shape, F32),
            sqc=like(sqw.shape, BF16),
            mlpg=like(mlpw.shape, F32),
            mlpm=like(mlpw.shape, F32),
            mlpn=like(mlpw.shape, F32),
            mlpc=like(mlpw.shape, BF16),
            gg=like(gain.shape, F32),
            gm=like(gain.shape, F32),
            gn=like(gain.shape, F32),
        )
    scratch = dict(
        og_v=VMEM(made.og.shape, F32),
        sems=pltpu.SemaphoreType.DMA((PARTS + 6,)),
    )
    if hasattr(made, "out"):
        scratch.update(
            sqw_v=VMEM(sqw.shape, F32),
            mlpw_v=VMEM(mlpw.shape, F32),
            gain_v=VMEM(gain.shape, F32),
            gainm_v=VMEM(gainm.shape, F32),
        )
    names = tuple(ins) + tuple(outs) + tuple(scratch)
    made_here = list(ins.values())
    stay = [pltpu.with_memory_space_constraint(value, pltpu.HBM) for value in made_here[near:]]
    results = pl.pallas_call(
        functools.partial(finish_kernel, names, rate),
        out_shape=tuple(outs.values()),
        in_specs=[in_vmem] * near + [any_space] * (len(ins) - near),
        out_specs=[any_space] * far + [in_vmem] * (len(outs) - far),
        scratch_shapes=list(scratch.values()),
        compiler_params=pltpu.CompilerParams(vmem_limit_bytes=16 << 20),
        name="finish",
    )(*made_here[:near], *stay)
    return Refs(zip(outs, results))


HIGH_PRECISION = lax.Precision.HIGHEST


def plain_orthogonalize(matrix):
    current = matrix / (jnp.sqrt(jnp.sum(matrix * matrix)) + 1e-07)
    for turn in range(5):
        gram = jnp.dot(current, current.T, precision=HIGH_PRECISION)
        poly = COEF_B * gram + COEF_C * jnp.dot(gram, gram, precision=HIGH_PRECISION)
        current = COEF_A * current + jnp.dot(poly, current, precision=HIGH_PRECISION)
    return current


def pick_owned(stack, owners, device):
    chosen = jnp.zeros_like(stack[0])
    for index in range(len(owners)):
        chosen = jnp.where(device == owners[index], stack[index], chosen)
    return chosen


def is_owner(owners, device):
    flag = device < 0
    for owner in owners:
        flag = jnp.logical_or(flag, device == owner)
    return flag


def from_wire(grads):
    def matrix(base, tiles):
        part = grads[:, base : base + tiles * TILE, :].reshape(-1, tiles, TILE, LANES)
        return part.transpose(0, 2, 1, 3).reshape(-1, tiles * LANES)

    square = jnp.stack([matrix(SQ_AT[m], 2) for m in range(5)])
    mlp = jnp.stack([matrix(m * MLP_ROWS, 8) for m in range(2)])
    return square, mlp, grads[0, GAIN_BASE : GAIN_BASE + 4, :].reshape(2, 2 * LANES)


def update_by_collectives(
    grads, square_weights, mlp_weights, gains, square_moment, mlp_moment, gain_moment, rate
):
    square_local, mlp_local, gain_local = from_wire(grads)
    square_grad, mlp_grad, gain_grad = (
        lax.psum_scatter(square_local, "dp", scatter_dimension=1, tiled=True),
        lax.psum_scatter(mlp_local, "dp", scatter_dimension=1, tiled=True),
        lax.psum_scatter(gain_local, "dp", scatter_dimension=1, tiled=True),
    )
    square_moment_new = 0.5 * square_moment + square_grad
    mlp_moment_new = 0.5 * mlp_moment + mlp_grad
    gain_moment_new = 0.5 * gain_moment + gain_grad
    device = lax.axis_index("dp")
    count = lax.axis_size("dp")
    square_owners = [index * count // 7 for index in range(5)]
    mlp_owners = [(index + 5) * count // 7 for index in range(2)]
    square_full, mlp_full = (
        lax.all_gather(square_moment_new, "dp", axis=1, tiled=True),
        lax.all_gather(mlp_moment_new, "dp", axis=1, tiled=True),
    )
    mine_square = pick_owned(square_full, square_owners, device)
    mine_mlp = pick_owned(mlp_full, mlp_owners, device)
    made_square = lax.cond(
        is_owner(square_owners, device), plain_orthogonalize, jnp.zeros_like, mine_square
    )
    made_mlp = lax.cond(is_owner(mlp_owners, device), plain_orthogonalize, jnp.zeros_like, mine_mlp)
    stack_square = jnp.stack(
        [jnp.where(device == owner, made_square, 0.0) for owner in square_owners]
    )
    stack_mlp = jnp.stack([jnp.where(device == owner, made_mlp, 0.0) for owner in mlp_owners])
    square_ortho, mlp_ortho = (
        lax.psum_scatter(stack_square, "dp", scatter_dimension=1, tiled=True),
        lax.psum_scatter(stack_mlp, "dp", scatter_dimension=1, tiled=True),
    )
    square_new = square_weights - jnp.array(SQ_RATES, F32)[:, None, None] * square_ortho
    mlp_new = mlp_weights - jnp.array(MLP_RATES, F32)[:, None, None] * mlp_ortho
    gains_new = gains - rate * gain_moment_new
    return (
        square_grad,
        square_moment_new,
        square_new,
        square_new.astype(BF16),
        mlp_grad,
        mlp_moment_new,
        mlp_new,
        mlp_new.astype(BF16),
        gain_grad,
        gain_moment_new,
        gains_new,
    )


def per_device(
    actions,
    observed,
    camera_flags,
    noise_levels,
    cotangent,
    square_weights,
    mlp_weights,
    gains,
    square_moment,
    mlp_moment,
    gain_moment,
):
    count = lax.axis_size("dp")
    rate = 0.1 / math.sqrt(actions.shape[0] * count)
    by_key = observed.transpose(1, 0, 2)
    ins = (actions, by_key, camera_flags, noise_levels, cotangent)
    if count == math.prod(GRID):
        made = block_and_back(True, *ins, square_weights, mlp_weights, gains, square_moment, mlp_moment)
        done = finish(rate, made, square_weights, mlp_weights, gains, gain_moment)
        output, actions_grad = done.output_f, done.ag_f
        d = done
        rest = (d.sqg, d.sqm, d.sqn, d.sqc, d.mlpg, d.mlpm, d.mlpn, d.mlpc, d.gg, d.gm, d.gn)
    else:
        square_all, mlp_all = (
            lax.all_gather(square_weights.astype(BF16), "dp", axis=1, tiled=True),
            lax.all_gather(mlp_weights.astype(BF16), "dp", axis=1, tiled=True),
        )
        gain_all = lax.all_gather(gains, "dp", axis=1, tiled=True)
        made = block_and_back(False, *ins, square_all, mlp_all, gain_all)
        done = finish(rate, made)
        output, actions_grad = made.output, made.ag
        grads = made.grads.reshape(-1, WIRE, LANES)
        rest = update_by_collectives(
            grads, square_weights, mlp_weights, gains, square_moment, mlp_moment, gain_moment, rate
        )
    observed_grad = done.og.transpose(1, 0, 2)
    return (output, actions_grad, observed_grad) + tuple(rest)


def solution(mesh):
    rows, cube, flat = P("dp", None), P("dp", None, None), P("dp")
    stacked, pair = P(None, "dp", None), P(None, "dp")
    return jax.shard_map(
        per_device,
        mesh=mesh,
        in_specs=(rows, cube, flat, flat, rows, stacked, stacked, pair, stacked, stacked, pair),
        out_specs=(rows, rows, cube) + (stacked,) * 8 + (pair,) * 3,
        check_vma=False,
    )
```

```python
import functools
import math

import jax
import jax.numpy as jnp
from jax import lax
from jax.experimental import pallas as pl
from jax.experimental.pallas import tpu as pltpu
from jax.sharding import PartitionSpec as P

HEADS = 4
ACT = 16
OBS_FULL = 196
OBS_FEW = 49
COEF_A = 3.4445
COEF_B = -4.775
COEF_C = 2.0315
F32 = jnp.float32
BF16 = jnp.bfloat16
MESH = pl.DeviceIdType.MESH
VMEM = pltpu.VMEM
NN = (((1,), (0,)), ((), ()))
NT = (((1,), (1,)), ((), ()))
TN = (((0,), (0,)), ((), ()))

LANES = 128
TILE = 8
MLP_ROWS = 64
SQ_ROWS = 16
SQ_AT = (160, 192, 176, 128, 144)
GAIN_BASE = 208
WIRE = 224
PIECES = ((0, 64), (64, 64), (128, 32), (160, 32), (192, 32))
PIECE_X_FIRST = (True, False, True, True, False)
DIRECT_PIECES = (3, 4)
CHUNKS = ((0, 64), (64, 64), (128, 32), (160, 32), (192, 16), (208, 16))
X_FIRST = (True, False, True, False, True, False)
DIRECT = (2, 3, 4, 5)
COMPLETES = ((0,), (1,), (5, 6), (2, 4), (3,), ())
MLP_RATES = (1.0, 0.5)
SQ_RATES = (0.5, 0.5, 0.5, 0.5, 4.0)
GRID = (4, 2, 2, 2)
OWNERS = (8, 22, 14, 16, 11, 21, 13)
SHIFTS = (0.0, 0.0, 0.4, 0.8, 0.8)
KEYS_PAD = 208
GROUP = 16
ROWS = 512


class Refs:
    def __init__(self, pairs):
        self.__dict__.update(pairs)


def dot(left, right, dims=NN):
    return lax.dot_general(left, right, dims, preferred_element_type=F32)


def place():
    me = lax.axis_index("dp")
    return me, me // 8, (me // 4) % 2, (me // 2) % 2, me % 2


def device_at(z, y, x, c):
    return ((z * 2 + y) * 2 + x) * 2 + c


def link(src, dst, send, recv, device):
    return pltpu.make_async_remote_copy(
        src_ref=src,
        dst_ref=dst,
        send_sem=send,
        recv_sem=recv,
        device_id=(device,),
        device_id_type=MESH,
    )


def greet(device):
    pl.semaphore_signal(
        pltpu.get_barrier_semaphore(), inc=1, device_id=(device,), device_id_type=MESH
    )


def normalize(values):
    centred = values - jnp.mean(values, -1, keepdims=True)
    scale = lax.rsqrt(jnp.mean(centred * centred, -1, keepdims=True) + 1e-05)
    return centred * scale, scale


def norm_back(grad, hat, scale):
    mean_one = jnp.mean(grad, -1, keepdims=True)
    mean_two = jnp.mean(grad * hat, -1, keepdims=True)
    return scale * (grad - mean_one - hat * mean_two)


class Gather:
    def __init__(self, r):
        self.r = r
        self.me, self.z, self.y, self.x, self.c = place()

    def hop(self, k, step, part, device):
        return link(part, part, self.r.gsend.at[k, step], self.r.grecv.at[k, step], device)

    def along_z(self, k, step):
        part = self.r.wire.at[self.z, self.y, self.x, self.c, pl.ds(*PIECES[k])]
        return self.hop(k, step, part, device_at((self.z + step + 1) % 4, self.y, self.x, self.c))

    def from_z(self, k, step):
        there = (self.z + 3 - step) % 4
        part = self.r.wire.at[there, self.y, self.x, self.c, pl.ds(*PIECES[k])]
        return self.hop(k, step, part, device_at(there, self.y, self.x, self.c))

    def plane(self, k, second, mine):
        z, y, x, c = self.z, self.y, self.x, self.c
        rows, wire = pl.ds(*PIECES[k]), self.r.wire
        py, px = (y, x) if mine else (1 - y, 1 - x)
        along_x = PIECE_X_FIRST[k] == second
        if along_x:
            part = wire.at[:, y, px, c, rows] if second else wire.at[:, :, px, c, rows]
            return self.hop(k, 3 if second else 4, part, device_at(z, y, 1 - x, c))
        part = wire.at[:, py, x, c, rows] if second else wire.at[:, py, :, c, rows]
        return self.hop(k, 3 if second else 4, part, device_at(z, 1 - y, x, c))

    def across(self, k, step, mine):
        py, px = ((self.y, 1 - self.x), (1 - self.y, self.x), (1 - self.y, 1 - self.x))[step]
        from_y, from_x = (self.y, self.x) if mine else (py, px)
        part = self.r.wire.at[:, from_y, from_x, self.c, pl.ds(*PIECES[k])]
        return self.hop(k, 3 + step, part, device_at(self.z, py, px, self.c))

    def core(self, k, mine):
        part = self.r.wire.at[:, :, :, self.c if mine else 1 - self.c, pl.ds(*PIECES[k])]
        return self.hop(k, 6, part, device_at(self.z, self.y, self.x, 1 - self.c))

    def first(self, *chunks):
        for k in chunks:
            for step in range(3):
                self.along_z(k, step).start()

    def second(self, *chunks):
        for k in chunks:
            for step in range(3):
                self.from_z(k, step).wait_recv()
            if k in DIRECT_PIECES:
                for step in range(3):
                    self.across(k, step, True).start()
            else:
                self.plane(k, True, True).start()

    def third(self, *chunks):
        for k in chunks:
            self.plane(k, True, False).wait_recv()
            self.plane(k, False, True).start()

    def fourth(self, *chunks):
        for k in chunks:
            if k in DIRECT_PIECES:
                for step in range(3):
                    self.across(k, step, False).wait_recv()
            else:
                self.plane(k, False, False).wait_recv()
            self.core(k, True).start()

    def last(self, *chunks):
        for k in chunks:
            self.core(k, False).wait_recv()

    def drain(self):
        for k in range(len(PIECES)):
            for step in range(3):
                self.along_z(k, step).wait_send()
            if k in DIRECT_PIECES:
                for step in range(3):
                    self.across(k, step, True).wait_send()
            else:
                self.plane(k, True, True).wait_send()
                self.plane(k, False, True).wait_send()
            self.core(k, True).wait_send()

    def fill(self, square):
        r = self.r
        spot = (self.z, self.y, self.x, self.c)

        def tiles(source, m, base, number):
            for j in range(number):
                pair = [source[m, :, pl.ds((2 * j + k) * LANES, LANES)] for k in range(2)]
                r.wire[spot + (pl.ds(base + j * 16, 16),)] = jnp.concatenate(pair, axis=0).astype(BF16)

        if not square:
            for m in range(2):
                tiles(r.mlpw_v, m, m * MLP_ROWS, 4)
            return
        for m in range(5):
            tiles(r.sqw_v, m, SQ_AT[m], 1)
        gains, edge = r.gain_v[...], r.edge
        high = gains.astype(BF16).astype(F32)
        middle = (gains - high).astype(BF16).astype(F32)
        edge[...] = jnp.zeros_like(edge)
        edge[0:2, 0:TILE] = high
        edge[2:4, 0:TILE] = middle
        edge[4:6, 0:TILE] = (gains - high - middle).astype(BF16).astype(F32)
        r.wire[spot + (pl.ds(GAIN_BASE, 16),)] = edge[...].astype(BF16)

    def unpack(self, base, number, out, m):
        for j in range(number):
            block = self.r.wire[:, :, :, :, pl.ds(base + j * 16, 16), :].reshape(32, 16, LANES).astype(F32)
            for half in range(2):
                columns = pl.ds((2 * j + half) * LANES, LANES)
                out[m, :, columns] = block[:, half * 8 : half * 8 + 8, :].reshape(256, LANES).astype(BF16)

    def unpack_gains(self):
        edge, wire = self.r.edge, self.r.wire
        for half in range(2):
            total = jnp.zeros((16, LANES), F32)
            for at in range(16):
                d = half * 16 + at
                tile = wire[d // 8, (d // 4) % 2, (d // 2) % 2, d % 2, pl.ds(GAIN_BASE, 16), :].astype(F32)
                total = total + (tile if at == 0 else pltpu.roll(tile, at * TILE, 1))
            edge[...] = total
            self.r.gain_all[:, pl.ds(half * LANES, LANES)] = edge[0:2, :] + edge[2:4, :] + edge[4:6, :]


class Update:
    def __init__(self, r):
        self.r = r
        self.me, self.z, self.y, self.x, self.c = place()

    def hop(self, k, step, src, dst, device):
        return link(src, dst, self.r.send.at[k, step], self.r.recv.at[k, step], device)

    def core(self, k):
        rows = pl.ds(*CHUNKS[k])
        src, dst = self.r.send0.at[:, :, :, rows], self.r.got_core.at[:, :, :, rows]
        return self.hop(k, 0, src, dst, device_at(self.z, self.y, self.x, 1 - self.c))

    def plane(self, k, first):
        rows = pl.ds(*CHUNKS[k])
        to = (self.z, self.y, 1 - self.x, self.c) if X_FIRST[k] == first else (self.z, 1 - self.y, self.x, self.c)
        if first:
            src, dst = self.r.send1.at[:, :, rows], self.r.got1.at[:, :, rows]
        else:
            src, dst = self.r.send2.at[:, rows], self.r.got2.at[:, rows]
        return self.hop(k, 1 if first else 2, src, dst, device_at(*to))

    def across(self, k, step):
        rows = pl.ds(*CHUNKS[k])
        py, px = self.others()[step]
        src, dst = self.r.send_p.at[step, :, rows], self.r.got_p.at[step, :, rows]
        return self.hop(k, 1 + step, src, dst, device_at(self.z, py, px, self.c))

    def others(self):
        return (self.y, 1 - self.x), (1 - self.y, self.x), (1 - self.y, 1 - self.x)

    def along_z(self, k, step):
        rows = pl.ds(*CHUNKS[k])
        there = (self.z + step + 1) % 4
        src = self.r.send3.at[there, rows]
        return self.hop(k, 4 + step, src, self.r.got3.at[step, rows], device_at(there, self.y, self.x, self.c))

    def start(self, k):
        rows = pl.ds(*CHUNKS[k])
        self.r.send0[:, :, :, rows, :] = self.r.grads[:, :, :, 1 - self.c, rows, :].astype(BF16)
        self.core(k).start()

    def one(self, *chunks):
        r = self.r
        for k in chunks:
            rows = pl.ds(*CHUNKS[k])
            self.core(k).wait_recv()
            sum1 = r.sum1
            sum1[:, :, :, rows, :] = r.grads[:, :, :, self.c, rows, :] + r.got_core[:, :, :, rows, :].astype(F32)
            if k in DIRECT:
                for step, (py, px) in enumerate(self.others()):
                    r.send_p[step, :, rows, :] = sum1[:, py, px, rows, :].astype(BF16)
                    self.across(k, step).start()
                continue
            other = sum1[:, :, 1 - self.x, rows, :] if X_FIRST[k] else sum1[:, 1 - self.y, :, rows, :]
            r.send1[:, :, rows, :] = other.astype(BF16)
            self.plane(k, True).start()

    def two(self, *chunks):
        r = self.r
        for k in chunks:
            rows = pl.ds(*CHUNKS[k])
            self.plane(k, True).wait_recv()
            sum1, sum2 = r.sum1, r.sum2
            mine = sum1[:, :, self.x, rows, :] if X_FIRST[k] else sum1[:, self.y, :, rows, :]
            sum2[:, :, rows, :] = mine + r.got1[:, :, rows, :].astype(F32)
            other = 1 - self.y if X_FIRST[k] else 1 - self.x
            r.send2[:, rows, :] = sum2[:, other, rows, :].astype(BF16)
            self.plane(k, False).start()

    def three(self, *chunks):
        r = self.r
        for k in chunks:
            rows = pl.ds(*CHUNKS[k])
            if k in DIRECT:
                total = r.sum1[:, self.y, self.x, rows, :]
                for step in range(3):
                    self.across(k, step).wait_recv()
                    total = total + r.got_p[step, :, rows, :].astype(F32)
            else:
                self.plane(k, False).wait_recv()
                mine = self.y if X_FIRST[k] else self.x
                total = r.sum2[:, mine, rows, :] + r.got2[:, rows, :].astype(F32)
            r.sum3[:, rows, :] = total
            r.send3[:, rows, :] = total.astype(BF16)
            if k in DIRECT:
                own = r.sum3[self.z, rows, :] + 0.5 * r.moment[rows, :]
                r.send3[self.z, rows, :] = own.astype(BF16)
                for index in COMPLETES[k]:
                    self.part_to_owner(index)
            for step in range(3):
                self.along_z(k, step).start()

    def part_to_owner(self, index):
        @pl.when(self.me != OWNERS[index])
        def _():
            self.to_owner(index).start()

        @pl.when(self.me == OWNERS[index])
        def _():
            src, dst = self.own_part(index)
            pltpu.make_async_copy(src, dst, self.r.own_recv.at[0]).start()

    def own_part(self, index):
        if index < 2:
            return self.r.moment_low.at[pl.ds(index * MLP_ROWS, MLP_ROWS)], self.r.slabs_mlp.at[self.me]
        rows = pl.ds(SQ_AT[index - 2], SQ_ROWS)
        return self.r.send3.at[:, rows], self.r.slabs_sq.at[self.z, self.me % 8]

    def result(self, index):
        return self.r.result_mlp if index < 2 else self.r.result_sq

    def to_owner(self, index):
        src, dst = self.own_part(index)
        return link(src, dst, self.r.own_send.at[index], self.r.own_recv.at[0], OWNERS[index])

    def four(self, *chunks):
        r = self.r
        moment, out = r.moment, r.out
        for k in chunks:
            rows = pl.ds(*CHUNKS[k])
            total = r.sum3[self.z, rows, :]
            for step in range(3):
                self.along_z(k, step).wait_recv()
                total = total + r.got3[step, rows, :].astype(F32)
            out[0, rows, :] = total
            new = 0.5 * moment[rows, :] + total
            moment[rows, :] = new
            if k < 2:
                r.moment_low[rows, :] = new.astype(BF16)
            if k not in DIRECT:
                for index in COMPLETES[k]:
                    self.part_to_owner(index)

    def old_moment(self):
        r = self.r
        moment = r.moment
        for m in range(2):
            for j in range(8):
                moment[pl.ds(m * MLP_ROWS + j * TILE, TILE), :] = r.mlpm_v[m, :, pl.ds(j * LANES, LANES)]
        for m in range(5):
            for j in range(2):
                moment[pl.ds(SQ_AT[m] + j * TILE, TILE), :] = r.sqm_v[m, :, pl.ds(j * LANES, LANES)]
        moment[pl.ds(GAIN_BASE, 16), :] = jnp.zeros((16, LANES), F32)

    def orthogonalize(self):
        r = self.r
        cur = r.cur
        rows = lax.broadcasted_iota(jnp.int32, (256, 256), 0)
        diagonal = rows == lax.broadcasted_iota(jnp.int32, (256, 256), 1)

        low = r.cur_low

        def load(rows, j, pair):
            for side in range(2):
                columns = pl.ds((2 * j + side) * LANES, LANES)
                part = pair[:, side * TILE : (side + 1) * TILE, :].reshape(-1, LANES)
                cur[rows, columns] = part
                low[rows, columns] = part.astype(BF16)

        def load_mlp():
            for j in range(4):
                load(pl.ds(0, 256), j, r.slabs_mlp[:, pl.ds(j * 16, 16), :].astype(F32))

        def load_sq():
            for to in range(4):
                pair = r.slabs_sq[0, :, to].astype(F32)
                for plane in range(1, 4):
                    pair = pair + r.slabs_sq[plane, :, to].astype(F32)
                load(pl.ds(to * 64, 64), 0, pair)

        def run(slabs, fetch, result, tiles):
            pltpu.make_async_copy(slabs, slabs, r.own_recv.at[0]).wait()
            fetch()
            scale = 1.0
            for turn, shift in enumerate(SHIFTS):
                whole = low[:, 0 : tiles * LANES]
                off = dot(whole, whole, NT)
                if turn == 0:
                    norm = jnp.sum(jnp.sum(jnp.where(diagonal, off, 0.0), axis=0, keepdims=True), axis=1, keepdims=True)
                    scale = 1.0 / (jnp.sqrt(norm) + 1e-07)
                    off = off * (scale * scale)
                if shift:
                    off = off - jnp.where(diagonal, shift, 0.0)
                off_low = off.astype(BF16)
                poly = (COEF_B + 2.0 * COEF_C * shift) * off + COEF_C * dot(off_low, off_low)
                poly = poly.astype(BF16)
                keep = COEF_A + shift * (COEF_B + COEF_C * shift)
                for j in range(tiles // 2):
                    columns = pl.ds(j * 2 * LANES, 2 * LANES)
                    now = keep * cur[:, columns] + dot(poly, low[:, columns])
                    if turn == 0:
                        now = now * scale
                    if turn < len(SHIFTS) - 1:
                        cur[:, columns] = now
                        low[:, columns] = now.astype(BF16)
                    else:
                        parts = [now[:, side * LANES : (side + 1) * LANES].reshape(32, TILE, LANES) for side in range(2)]
                        result[:, pl.ds(j * 16, 16), :] = jnp.concatenate(parts, axis=1).astype(result.dtype)

        mine_mlp = jnp.logical_or(self.me == OWNERS[0], self.me == OWNERS[1])
        mine_sq = self.me < 0
        for device in OWNERS[2:]:
            mine_sq = jnp.logical_or(mine_sq, self.me == device)

        @pl.when(mine_mlp)
        def _():
            run(r.slabs_mlp, load_mlp, r.result_mlp, 8)

        @pl.when(mine_sq)
        def _():
            run(r.slabs_sq, load_sq, r.result_sq, 2)

    def landing(self, index):
        if index < 2:
            return self.r.back_mlp.at[index]
        return self.r.out.at[2, pl.ds(SQ_AT[index - 2], SQ_ROWS)]

    def give_back(self, index, device):
        result = self.result(index)
        return link(
            result.at[device], self.landing(index),
            self.r.back_send.at[device], self.r.back_recv.at[index], device,
        )

    def give_all(self):
        r = self.r
        for index in range(7):
            result = self.result(index)

            @pl.when(self.me == OWNERS[index])
            def _():
                def send_one(step, _):
                    self.give_back(index, (self.me + step) % 32).start()
                    return 0

                lax.fori_loop(1, 32, send_one, 0)
                pltpu.make_async_copy(result.at[self.me], self.landing(index), r.back_recv.at[index]).start()

    def take_all(self):
        for index in range(7):
            result = self.result(index)
            pltpu.make_async_copy(result.at[0], self.landing(index), self.r.back_recv.at[index]).wait()
        for index in range(2):
            rows = pl.ds(index * MLP_ROWS, MLP_ROWS)
            self.r.out[2, rows, :] = self.r.back_mlp[index].astype(F32)

    def drain(self):
        for k in range(len(CHUNKS)):
            self.core(k).wait_send()
            if k in DIRECT:
                for step in range(3):
                    self.across(k, step).wait_send()
            else:
                self.plane(k, True).wait_send()
                self.plane(k, False).wait_send()
            for step in range(3):
                self.along_z(k, step).wait_send()
        for index in range(7):

            @pl.when(self.me != OWNERS[index])
            def _():
                self.to_owner(index).wait_send()

    def drain_owner(self):
        for index in range(7):

            @pl.when(self.me == OWNERS[index])
            def _():
                def wait_one(step, _):
                    self.give_back(index, (self.me + step) % 32).wait_send()
                    return 0

                lax.fori_loop(1, 32, wait_one, 0)


def greet_all():
    me, z, y, x, c = place()
    greet(device_at(z, y, x, 1 - c))
    greet(device_at(z, y, 1 - x, c))
    greet(device_at(z, 1 - y, x, c))
    greet(device_at(z, 1 - y, 1 - x, c))
    for step in range(1, 4):
        greet(device_at((z + step) % 4, y, x, c))
    owner = me < 0
    for device in OWNERS:
        owner = jnp.logical_or(owner, me == device)

        @pl.when(me != device)
        def _():
            greet(device)

    @pl.when(owner)
    def _():
        def greet_other(step, _):
            greet((me + step) % 32)
            return 0

        lax.fori_loop(1, 32, greet_other, 0)

    is_owner = owner.astype(jnp.int32)
    return 7 + 7 - is_owner + 31 * is_owner


def block_kernel(names, remote, *args):
    r = Refs(zip(names, args))
    keys, samples = r.obs.shape[0], r.obs.shape[1]
    tokens, width = r.acts.shape
    head_dim, half, per = width // HEADS, width // 2, ROWS // ACT
    wide = r.mlp_all.shape[2]
    groups = samples // GROUP
    in_sems, out_sems = r.in_sems, r.out_sems

    if remote:
        own = (r.sqw_v, r.mlpw_v, r.gain_v)
    else:
        own = (r.sq_all, r.mlp_all, r.gain_all)
    loads = list(zip((r.sqw, r.mlpw, r.gain), own))
    loads += [(r.acts, r.acts_v), (r.obs, r.obs_v.at[pl.ds(0, keys)]), (r.cot, r.cot_v)]
    if remote:
        loads += [(r.sqm, r.sqm_v), (r.mlpm, r.mlpm_v)]
    loads += [(r.flags, r.flags_s), (r.levels, r.levels_s)]
    copies = [pltpu.make_async_copy(a, b, in_sems.at[i]) for i, (a, b) in enumerate(loads)]

    def arrive(*which):
        for i in which:
            copies[i].wait()

    for copy in copies:
        copy.start()
    if remote:
        gather, update = Gather(r), Update(r)
        expected = greet_all()
        arrive(0, 2)
        gather.fill(True)
        pl.semaphore_wait(pltpu.get_barrier_semaphore(), expected)
        gather.first(3, 4)
        arrive(1)
        gather.fill(False)

    arrive(3)

    def hats(i, _):
        rows = pl.ds(pl.multiple_of(i * ROWS, ROWS), ROWS)
        hat, scale = normalize(r.acts_v[rows, :])
        r.xhat[rows, :] = hat
        r.rstd[rows, :] = scale
        return 0

    lax.fori_loop(0, tokens // ROWS, hats, 0)

    mem, obs_v = r.mem, r.obs_v
    batch = 16
    chunks = KEYS_PAD // batch
    swap = r.swap
    row = lax.broadcasted_iota(jnp.int32, swap.shape, 0)
    column = lax.broadcasted_iota(jnp.int32, swap.shape, 1)
    swap[...] = jnp.where(column == (row % batch) * batch + row // batch, 1.0, 0.0).astype(BF16)

    def turn(part, low, high):
        def one(j, _):
            at = pl.ds(pl.multiple_of(j * batch, batch), batch)
            here = pl.ds(part * batch, batch)
            block = obs_v[at, here, :].reshape(batch * batch, width)
            mem[here, at, :] = dot(swap[...], block).astype(BF16).reshape(batch, batch, width)
            return 0

        lax.fori_loop(low, high, one, 0, unroll=high - low)

    whole = chunks - 1
    arrive(4)
    turn(0, 0, whole // 2)
    if remote:
        gather.second(3, 4)
        gather.first(2, 0, 1)
    turn(0, whole // 2, whole)
    if remote:
        gather.fourth(3, 4)
    turn(1, 0, whole // 2)
    if remote:
        gather.second(2, 0, 1)
    turn(1, whole // 2, whole)
    arrive(len(copies) - 1, len(copies) - 2)
    freqs = jnp.exp(
        lax.broadcasted_iota(jnp.int32, (1, half), 1).astype(F32) * F32(-math.log(10000.0)) / half
    )
    for s in range(samples):
        r.angle[s : s + 1, :] = r.levels_s[s].astype(F32) * freqs
    r.embed[:, 0:half] = jnp.sin(r.angle[...]).astype(BF16)
    r.embed[:, half:width] = jnp.cos(r.angle[...]).astype(BF16)
    if remote:
        arrive(6, 7)
        update.old_moment()
        gather.third(2, 0, 1)
        gather.last(3, 4)
        for m in range(3):
            gather.unpack(SQ_AT[m], 1, r.sq_all, m)
        gather.unpack_gains()
    else:
        arrive(0, 1, 2)

    sq, mlp = r.sq_all, r.mlp_all
    wkh, wvh = r.wkh, r.wvh
    lane = lax.broadcasted_iota(jnp.int32, (width, width), 1)

    def split_heads(out, weight):
        weight = weight.astype(F32)
        for h in range(HEADS):
            out[pl.ds(h * width, width), :] = jnp.where(lane // head_dim == h, weight, 0.0).astype(BF16)

    split_heads(wkh, sq[2])
    g1, g2 = r.gain_all[0:1, :], r.gain_all[1:2, :]

    obs_v[keys] = dot(r.embed[...], sq[0]).astype(BF16)
    obs_v[keys + 1 :] = jnp.zeros((KEYS_PAD - keys - 1, samples, width), BF16)
    for part in range(samples // batch):
        turn(part, whole, chunks)

    sides, weights = r.sides_v, r.pds_v

    def make_queries(i, _):
        rows = pl.ds(pl.multiple_of(i * ROWS, ROWS), ROWS)
        first = (r.xhat[rows, :] * g1).astype(BF16)
        r.first[rows, :] = first
        q = dot(first, sq[1]).astype(BF16)
        r.query[rows, :] = q
        here = pl.ds(i * per, per)
        for h in range(HEADS):
            wk = wkh[pl.ds(h * width, width), :]
            value = (dot(q, wk, NT) * 0.125).astype(BF16).reshape(per, ACT, width)
            sides[here, pl.ds((HEADS + h) * ACT, ACT), :] = value
        return 0

    lax.fori_loop(0, tokens // ROWS, make_queries, 0)

    key = lax.broadcasted_iota(jnp.int32, (1, KEYS_PAD), 1)
    low_rows, high_rows = pl.ds(0, HEADS * ACT), pl.ds(HEADS * ACT, HEADS * ACT)

    ones = jnp.ones((KEYS_PAD, LANES), BF16)

    def attend(g, _):
        ids = [g * GROUP + k for k in range(GROUP)]
        scores = [dot(sides[s, high_rows, :], mem[s], NT) for s in ids]
        lows = []
        for s, score in zip(ids, scores):
            count = OBS_FEW + (OBS_FULL - OBS_FEW) * r.flags_s[s]
            score = score + jnp.where((key < count) | (key == OBS_FULL), 0.0, -1000000000.0)
            expo = jnp.exp(score - jnp.max(score, -1, keepdims=True))
            low = expo.astype(BF16)
            part = 1.0 / dot(low, ones)
            probs = expo * jnp.concatenate([part, part[:, 0 : KEYS_PAD - LANES]], axis=1)
            r.probs[s] = probs
            weights[s, low_rows, :] = probs.astype(BF16)
            lows.append((low, jnp.concatenate([part, part], axis=1)))
        for s, (low, part) in zip(ids, lows):
            u = (dot(low, mem[s]) * part).astype(BF16)
            rows = pl.ds(pl.multiple_of(s * ACT, ACT), ACT)
            for h in range(HEADS):
                r.u[rows, pl.ds(h * width, width)] = u[h * ACT : (h + 1) * ACT, :]
        return 0

    lax.fori_loop(0, groups // 2, attend, 0)
    if remote:
        gather.fourth(2, 0, 1)
    lax.fori_loop(groups // 2, groups, attend, 0)
    if remote:
        gather.last(2, 0, 1)
        for m in range(3, 5):
            gather.unpack(SQ_AT[m], 1, sq, m)
        for m in range(2):
            gather.unpack(m * MLP_ROWS, 4, mlp, m)
    split_heads(wvh, sq[3])

    gain_acc = r.gain_acc
    gain_acc[...] = jnp.zeros_like(gain_acc)
    arrive(5)

    def feed(i, _):
        rows = pl.ds(pl.multiple_of(i * ROWS, ROWS), ROWS)
        mixed = dot(r.u[rows, :], wvh[...]).astype(BF16)
        r.mixed[rows, :] = mixed
        resid = r.acts_v[rows, :] + dot(mixed, sq[4])
        hat, scale = normalize(resid)
        second = (hat * g2).astype(BF16)
        r.second[rows, :] = second
        cot = r.cot_v[rows, :]
        out_low = cot.astype(BF16)
        r.out_low[rows, :] = out_low
        for c in range(wide // 256):
            columns = pl.ds(c * 256, 256)
            v = dot(second, mlp[0, :, columns])
            square = v * v
            t = jnp.tanh(0.7978845608 * (v + 0.044715 * square * v))
            r.active[rows, columns] = (0.5 * v * (1.0 + t)).astype(BF16)
            slope = 0.5 * (1.0 + t) + 0.5 * v * (1.0 - t * t) * (0.7978845608 * (1.0 + 0.134145 * square))
            r.dhidden[rows, columns] = (slope * dot(out_low, mlp[1, :, columns])).astype(BF16)
        r.out_v[rows, :] = resid + dot(r.active[rows, :], mlp[1], NT)
        grad_second = dot(r.dhidden[rows, :], mlp[0], NT)
        gain_acc[1:2, :] += jnp.sum(grad_second * hat, 0, keepdims=True)
        dres = cot + norm_back(grad_second * g2, hat, scale)
        r.dres[rows, :] = dres
        low = dres.astype(BF16)
        r.dres_low[rows, :] = low
        gm = dot(low, sq[4], NT).astype(BF16)
        r.dmixed[rows, :] = gm
        here = pl.ds(i * per, per)
        for h in range(HEADS):
            wv = wvh[pl.ds(h * width, width), :]
            sides[here, pl.ds(h * ACT, ACT), :] = dot(gm, wv, NT).astype(BF16).reshape(per, ACT, width)
        return 0

    lax.fori_loop(0, tokens // ROWS, feed, 0)
    keep_out = pltpu.make_async_copy(r.out_v, r.output, out_sems.at[0])
    keep_out.start()

    grads = r.grads

    def put(base, tiles, value):
        for j in range(tiles):
            part = value[:, j * LANES : (j + 1) * LANES].reshape(GRID + (TILE, LANES))
            grads[:, :, :, :, pl.ds(base + j * TILE, TILE), :] = part

    def by_head(left, right):
        turned = left.T
        parts = [
            dot(turned[h * head_dim : (h + 1) * head_dim, :], right[:, pl.ds(h * width, width)])
            for h in range(HEADS)
        ]
        return jnp.concatenate(parts, axis=0).T

    put(0, 8, dot(r.second[...], r.dhidden[...], TN))
    if remote:
        update.start(0)
    put(MLP_ROWS, 8, dot(r.out_low[...], r.active[...], TN))
    if remote:
        update.start(1)
    put(SQ_AT[4], 2, dot(r.mixed[...], r.dres_low[...], TN))
    put(SQ_AT[3], 2, by_head(r.dmixed[...], r.u))
    if remote:
        update.start(2)

    def attend_back(g, _):
        ids = [g * GROUP + k for k in range(GROUP)]
        rises = [dot(sides[s, low_rows, :], mem[s], NT) for s in ids]
        for s, rise in zip(ids, rises):
            probs = r.probs[s]
            both = probs * rise
            weights[s, high_rows, :] = (both - probs * jnp.sum(both, -1, keepdims=True)).astype(BF16)
        for s in ids:
            dq = (dot(weights[s, high_rows, :], mem[s]) * 0.125).astype(BF16)
            rows = pl.ds(pl.multiple_of(s * ACT, ACT), ACT)
            for h in range(HEADS):
                r.dq_wide[rows, pl.ds(h * width, width)] = dq[h * ACT : (h + 1) * ACT, :]
            end = dot(weights[s, :, LANES:KEYS_PAD], sides[s], TN)
            r.stamps[s] = end[64:72, :]
        return 0

    half_groups = groups // 2
    lax.fori_loop(0, half_groups, attend_back, 0)
    if remote:
        update.one(0)
    lax.fori_loop(half_groups, groups, attend_back, 0)
    put(SQ_AT[2], 2, by_head(r.query[...], r.dq_wide))
    stamp_low = r.stamps[:, 4:5, :].reshape(samples, width).astype(BF16)
    put(SQ_AT[0], 2, dot(r.embed[...], stamp_low, TN))
    if remote:
        update.start(3)
        update.one(1, 2)

    def memory_back(low, high):
        def one(g, _):
            for k in range(GROUP):
                s = g * GROUP + k
                mem[s] = dot(weights[s], sides[s], TN).astype(BF16)
            return 0

        lax.fori_loop(low, high, one, 0)

    def turn_back(part):
        def one(j):
            at = pl.ds(pl.multiple_of(j * batch, batch), batch)
            here = pl.ds(part * batch, batch)
            block = mem[here, at, :].reshape(batch * batch, width)
            value = dot(swap[...], block).astype(BF16).reshape(batch, batch, width)
            number = min(batch, keys - j * batch)
            r.og[pl.ds(j * batch, number), here, :] = value[0:number]

        for j in range(chunks):
            one(j)

    def queries_back(i, _):
        rows = pl.ds(pl.multiple_of(i * ROWS, ROWS), ROWS)
        r.dquery[rows, :] = dot(r.dq_wide[rows, :], wkh[...]).astype(BF16)
        return 0

    lax.fori_loop(0, tokens // ROWS, queries_back, 0)
    put(SQ_AT[1], 2, dot(r.first[...], r.dquery[...], TN))
    if remote:
        update.start(4)

    def acts_back(i, _):
        rows = pl.ds(pl.multiple_of(i * ROWS, ROWS), ROWS)
        grad_first = dot(r.dquery[rows, :], sq[1], NT)
        hat = r.xhat[rows, :]
        gain_acc[0:1, :] += jnp.sum(grad_first * hat, 0, keepdims=True)
        r.ag_v[rows, :] = r.dres[rows, :] + norm_back(grad_first * g1, hat, r.rstd[rows, :])
        return 0

    def finish_acts():
        lax.fori_loop(0, tokens // ROWS, acts_back, 0)
        for norm in range(2):
            for j in range(2):
                row = gain_acc[norm : norm + 1, j * LANES : (j + 1) * LANES]
                at = GAIN_BASE + norm * 2 + j
                value = jnp.broadcast_to(row.reshape(1, 1, 1, 1, 1, LANES), GRID + (1, LANES))
                grads[:, :, :, :, at : at + 1, :] = value
        rest = WIRE - GAIN_BASE - 4
        grads[:, :, :, :, GAIN_BASE + 4 : WIRE, :] = jnp.zeros(GRID + (rest, LANES), F32)

    keep_ag = pltpu.make_async_copy(r.ag_v, r.ag, out_sems.at[1])
    if remote:
        update.two(0)
        update.one(3)
        finish_acts()
        keep_ag.start()
        update.start(5)
        update.two(1)
        update.three(2)
        update.one(4)
        memory_back(0, half_groups)
        update.three(3)
        update.one(5)
        update.three(0, 1)
        update.three(4)
        memory_back(half_groups, groups)
        update.four(0, 1)
        turn_back(0)
        update.three(5)
        update.orthogonalize()
        update.give_all()
        turn_back(1)
        update.four(2, 3, 4, 5)
        out = r.out
        out[1, :, :] = r.moment[...]
        out[2, pl.ds(GAIN_BASE, 16), :] = jnp.zeros((16, LANES), F32)
        gather.drain()
        update.drain()
        update.take_all()
        update.drain_owner()
    else:
        finish_acts()
        keep_ag.start()
        memory_back(0, groups)
        for part in range(samples // batch):
            turn_back(part)
    for copy in (keep_out, keep_ag):
        copy.wait()


def block_and_back(remote, acts, obs, flags, levels, cot, sqw, mlpw, gain, sqm=None, mlpm=None):
    tokens, width = acts.shape
    keys, samples = obs.shape[0], obs.shape[1]
    rows = HEADS * ACT
    wide = mlpw.shape[2]
    any_space = pl.BlockSpec(memory_space=pl.ANY)
    in_vmem = pl.BlockSpec(memory_space=VMEM)
    sem = pltpu.SemaphoreType.DMA
    ins = dict(flags=flags, levels=levels, acts=acts, obs=obs, cot=cot, sqw=sqw, mlpw=mlpw, gain=gain)
    outs = dict(
        output=jax.ShapeDtypeStruct(acts.shape, F32),
        ag=jax.ShapeDtypeStruct(acts.shape, F32),
        og=jax.ShapeDtypeStruct(obs.shape, BF16),
    )
    grads = GRID + (WIRE, LANES)
    scratch = dict(
        obs_v=VMEM((KEYS_PAD, samples, width), BF16),
        acts_v=VMEM(acts.shape, F32),
        cot_v=VMEM(acts.shape, F32),
        mem=VMEM((samples, KEYS_PAD, width), BF16),
        swap=VMEM((256, 256), BF16),
        sq_all=VMEM((5, width, width), BF16),
        mlp_all=VMEM((2, width, wide), BF16),
        gain_all=VMEM((2, width), F32),
        wkh=VMEM((HEADS * width, width), BF16),
        wvh=VMEM((HEADS * width, width), BF16),
        first=VMEM((tokens, width), BF16),
        query=VMEM((tokens, width), BF16),
        xhat=VMEM((tokens, width), F32),
        rstd=VMEM((tokens, 1), F32),
        probs=VMEM((samples, rows, KEYS_PAD), F32),
        pds_v=VMEM((samples, 2 * rows, KEYS_PAD), BF16),
        sides_v=VMEM((samples, 2 * rows, width), BF16),
        u=VMEM((tokens, HEADS * width), BF16),
        dq_wide=VMEM((tokens, HEADS * width), BF16),
        mixed=VMEM((tokens, width), BF16),
        second=VMEM((tokens, width), BF16),
        active=VMEM((tokens, wide), BF16),
        dhidden=VMEM((tokens, wide), BF16),
        out_low=VMEM((tokens, width), BF16),
        dres_low=VMEM((tokens, width), BF16),
        dres=VMEM((tokens, width), F32),
        dmixed=VMEM((tokens, width), BF16),
        dquery=VMEM((tokens, width), BF16),
        out_v=VMEM((tokens, width), F32),
        ag_v=VMEM((tokens, width), F32),
        angle=VMEM((samples, width // 2), F32),
        embed=VMEM((samples, width), BF16),
        stamps=VMEM((samples, 8, width), F32),
        gain_acc=VMEM((8, width), F32),
        flags_s=pltpu.SMEM(flags.shape, jnp.int32),
        levels_s=pltpu.SMEM(levels.shape, jnp.int32),
        in_sems=sem((10,)),
        out_sems=sem((2,)),
    )
    extra = {}
    if remote:
        ins.update(sqm=sqm, mlpm=mlpm)
        outs.update(out=jax.ShapeDtypeStruct((3, WIRE, LANES), F32))
        chunks = len(CHUNKS)
        scratch.update(
            grads=VMEM(grads, F32),
            sqw_v=VMEM(sqw.shape, F32),
            mlpw_v=VMEM(mlpw.shape, F32),
            gain_v=VMEM(gain.shape, F32),
            sqm_v=VMEM(sqm.shape, F32),
            mlpm_v=VMEM(mlpm.shape, F32),
            wire=VMEM(grads, BF16),
            edge=VMEM((16, LANES), F32),
            gsend=sem((chunks, 7)),
            grecv=sem((chunks, 7)),
            send0=VMEM((4, 2, 2, WIRE, LANES), BF16),
            got_core=VMEM((4, 2, 2, WIRE, LANES), BF16),
            sum1=VMEM((4, 2, 2, WIRE, LANES), F32),
            send1=VMEM((4, 2, WIRE, LANES), BF16),
            got1=VMEM((4, 2, WIRE, LANES), BF16),
            sum2=VMEM((4, 2, WIRE, LANES), F32),
            send2=VMEM((4, WIRE, LANES), BF16),
            got2=VMEM((4, WIRE, LANES), BF16),
            sum3=VMEM((4, WIRE, LANES), F32),
            send3=VMEM((4, WIRE, LANES), BF16),
            send_p=VMEM((3, 4, WIRE, LANES), BF16),
            got_p=VMEM((3, 4, WIRE, LANES), BF16),
            got3=VMEM((3, WIRE, LANES), BF16),
            moment=VMEM((WIRE, LANES), F32),
            slabs_sq=VMEM((4, 8, 4, SQ_ROWS, LANES), BF16),
            slabs_mlp=VMEM((32, MLP_ROWS, LANES), BF16),
            moment_low=VMEM((2 * MLP_ROWS, LANES), BF16),
            back_mlp=VMEM((2, MLP_ROWS, LANES), BF16),
            result_sq=VMEM((32, SQ_ROWS, LANES), F32),
            result_mlp=VMEM((32, MLP_ROWS, LANES), BF16),
            cur=VMEM((width, wide), F32),
            cur_low=VMEM((width, wide), BF16),
            send=sem((chunks, 7)),
            recv=sem((chunks, 7)),
            own_send=sem((7,)),
            own_recv=sem((1,)),
            back_send=sem((32,)),
            back_recv=sem((7,)),
        )
        extra = dict(collective_id=0, has_side_effects=True)
        outs = {name: VMEM(like.shape, like.dtype) for name, like in outs.items()}
    else:
        outs.update(grads=jax.ShapeDtypeStruct(grads, F32))
    names = tuple(ins) + tuple(outs) + tuple(scratch)
    stay = [pltpu.with_memory_space_constraint(value, pltpu.HBM) for value in ins.values()]
    results = pl.pallas_call(
        functools.partial(block_kernel, names, remote),
        out_shape=tuple(outs.values()),
        in_specs=[any_space] * len(ins),
        out_specs=[any_space] * 2 + [in_vmem] * 2,
        scratch_shapes=list(scratch.values()),
        compiler_params=pltpu.CompilerParams(vmem_limit_bytes=46 << 20, **extra),
        name="block_and_back",
    )(*stay)
    return Refs(zip(outs, results))


PARTS = 7


def finish_kernel(names, rate, *args):
    r = Refs(zip(names, args))
    sems = r.sems
    keys = r.og.shape[0]
    step = keys // PARTS

    def leave(part):
        block = pl.ds(part * step, step)
        return pltpu.make_async_copy(r.og_v.at[block], r.og.at[block], sems.at[part])

    more = PARTS
    moves = []
    if hasattr(r, "wire"):
        pairs = [(r.sqw, r.sqw_v), (r.mlpw, r.mlpw_v), (r.gain, r.gain_v), (r.gainm, r.gainm_v)]
        pairs += [(r.output, r.output_f), (r.ag, r.ag_f)]
        for source, target in pairs:
            moves.append(pltpu.make_async_copy(source, target, sems.at[more]))
            moves[-1].start()
            more += 1
    for part in range(PARTS):

        def widen(j, _):
            r.og_v[j] = r.low[j].astype(F32)
            return 0

        lax.fori_loop(part * step, (part + 1) * step, widen, 0, unroll=4)
        leave(part).start()
    for copy in moves[:4]:
        copy.wait()
    if hasattr(r, "wire"):
        finish_weights(r, rate)
    for part in range(PARTS):
        leave(part).wait()
    for copy in moves[4:]:
        copy.wait()


def finish_weights(r, rate):
    wire = r.wire
    me = lax.axis_index("dp")
    for m in range(5):
        for j in range(2):
            rows, columns = pl.ds(SQ_AT[m] + j * TILE, TILE), pl.ds(j * LANES, LANES)
            r.sqg[m, :, columns] = wire[0, rows, :]
            r.sqm[m, :, columns] = wire[1, rows, :]
            r.sqn[m, :, columns] = r.sqw_v[m, :, columns] - SQ_RATES[m] * wire[2, rows, :]
    r.sqc[...] = r.sqn[...].astype(BF16)
    for m in range(2):
        for j in range(8):
            rows, columns = pl.ds(m * MLP_ROWS + j * TILE, TILE), pl.ds(j * LANES, LANES)
            r.mlpg[m, :, columns] = wire[0, rows, :]
            r.mlpm[m, :, columns] = wire[1, rows, :]
            r.mlpn[m, :, columns] = r.mlpw_v[m, :, columns] - MLP_RATES[m] * wire[2, rows, :]
    r.mlpc[...] = r.mlpn[...].astype(BF16)
    tile = wire[0, pl.ds(GAIN_BASE, TILE), :]
    turned = pltpu.roll(tile, (LANES - (me % 16) * TILE) % LANES, 1)
    at = me // 16
    for norm in range(2):
        pair = turned[2 * norm : 2 * norm + 2, 0:TILE]
        row = jnp.where(at == 0, pair[0:1, :], pair[1:2, :])
        new = 0.5 * r.gainm_v[norm : norm + 1, :] + row
        r.gg[norm : norm + 1, :] = row
        r.gm[norm : norm + 1, :] = new
        r.gn[norm : norm + 1, :] = r.gain_v[norm : norm + 1, :] - rate * new


def finish(rate, made, sqw=None, mlpw=None, gain=None, gainm=None):
    any_space = pl.BlockSpec(memory_space=pl.ANY)
    in_vmem = pl.BlockSpec(memory_space=VMEM)
    ins = dict(low=made.og)
    outs = dict(og=jax.ShapeDtypeStruct(made.og.shape, F32))
    near, far = 1, 1
    if hasattr(made, "out"):
        ins.update(output=made.output, ag=made.ag, wire=made.out, sqw=sqw, mlpw=mlpw, gain=gain, gainm=gainm)
        like = jax.ShapeDtypeStruct
        near, far = 4, 3
        outs.update(
            output_f=like(made.output.shape, F32),
            ag_f=like(made.ag.shape, F32),
            sqg=like(sqw.shape, F32),
            sqm=like(sqw.shape, F32),
            sqn=like(sqw.shape, F32),
            sqc=like(sqw.shape, BF16),
            mlpg=like(mlpw.shape, F32),
            mlpm=like(mlpw.shape, F32),
            mlpn=like(mlpw.shape, F32),
            mlpc=like(mlpw.shape, BF16),
            gg=like(gain.shape, F32),
            gm=like(gain.shape, F32),
            gn=like(gain.shape, F32),
        )
    scratch = dict(
        og_v=VMEM(made.og.shape, F32),
        sems=pltpu.SemaphoreType.DMA((PARTS + 6,)),
    )
    if hasattr(made, "out"):
        scratch.update(
            sqw_v=VMEM(sqw.shape, F32),
            mlpw_v=VMEM(mlpw.shape, F32),
            gain_v=VMEM(gain.shape, F32),
            gainm_v=VMEM(gainm.shape, F32),
        )
    names = tuple(ins) + tuple(outs) + tuple(scratch)
    made_here = list(ins.values())
    stay = [pltpu.with_memory_space_constraint(value, pltpu.HBM) for value in made_here[near:]]
    results = pl.pallas_call(
        functools.partial(finish_kernel, names, rate),
        out_shape=tuple(outs.values()),
        in_specs=[in_vmem] * near + [any_space] * (len(ins) - near),
        out_specs=[any_space] * far + [in_vmem] * (len(outs) - far),
        scratch_shapes=list(scratch.values()),
        compiler_params=pltpu.CompilerParams(vmem_limit_bytes=16 << 20),
        name="finish",
    )(*made_here[:near], *stay)
    return Refs(zip(outs, results))


HIGH_PRECISION = lax.Precision.HIGHEST


def plain_orthogonalize(matrix):
    current = matrix / (jnp.sqrt(jnp.sum(matrix * matrix)) + 1e-07)
    for turn in range(5):
        gram = jnp.dot(current, current.T, precision=HIGH_PRECISION)
        poly = COEF_B * gram + COEF_C * jnp.dot(gram, gram, precision=HIGH_PRECISION)
        current = COEF_A * current + jnp.dot(poly, current, precision=HIGH_PRECISION)
    return current


def pick_owned(stack, owners, device):
    chosen = jnp.zeros_like(stack[0])
    for index in range(len(owners)):
        chosen = jnp.where(device == owners[index], stack[index], chosen)
    return chosen


def is_owner(owners, device):
    flag = device < 0
    for owner in owners:
        flag = jnp.logical_or(flag, device == owner)
    return flag


def from_wire(grads):
    def matrix(base, tiles):
        part = grads[:, base : base + tiles * TILE, :].reshape(-1, tiles, TILE, LANES)
        return part.transpose(0, 2, 1, 3).reshape(-1, tiles * LANES)

    square = jnp.stack([matrix(SQ_AT[m], 2) for m in range(5)])
    mlp = jnp.stack([matrix(m * MLP_ROWS, 8) for m in range(2)])
    return square, mlp, grads[0, GAIN_BASE : GAIN_BASE + 4, :].reshape(2, 2 * LANES)


def update_by_collectives(
    grads, square_weights, mlp_weights, gains, square_moment, mlp_moment, gain_moment, rate
):
    square_local, mlp_local, gain_local = from_wire(grads)
    square_grad, mlp_grad, gain_grad = (
        lax.psum_scatter(square_local, "dp", scatter_dimension=1, tiled=True),
        lax.psum_scatter(mlp_local, "dp", scatter_dimension=1, tiled=True),
        lax.psum_scatter(gain_local, "dp", scatter_dimension=1, tiled=True),
    )
    square_moment_new = 0.5 * square_moment + square_grad
    mlp_moment_new = 0.5 * mlp_moment + mlp_grad
    gain_moment_new = 0.5 * gain_moment + gain_grad
    device = lax.axis_index("dp")
    count = lax.axis_size("dp")
    square_owners = [index * count // 7 for index in range(5)]
    mlp_owners = [(index + 5) * count // 7 for index in range(2)]
    square_full, mlp_full = (
        lax.all_gather(square_moment_new, "dp", axis=1, tiled=True),
        lax.all_gather(mlp_moment_new, "dp", axis=1, tiled=True),
    )
    mine_square = pick_owned(square_full, square_owners, device)
    mine_mlp = pick_owned(mlp_full, mlp_owners, device)
    made_square = lax.cond(
        is_owner(square_owners, device), plain_orthogonalize, jnp.zeros_like, mine_square
    )
    made_mlp = lax.cond(is_owner(mlp_owners, device), plain_orthogonalize, jnp.zeros_like, mine_mlp)
    stack_square = jnp.stack(
        [jnp.where(device == owner, made_square, 0.0) for owner in square_owners]
    )
    stack_mlp = jnp.stack([jnp.where(device == owner, made_mlp, 0.0) for owner in mlp_owners])
    square_ortho, mlp_ortho = (
        lax.psum_scatter(stack_square, "dp", scatter_dimension=1, tiled=True),
        lax.psum_scatter(stack_mlp, "dp", scatter_dimension=1, tiled=True),
    )
    square_new = square_weights - jnp.array(SQ_RATES, F32)[:, None, None] * square_ortho
    mlp_new = mlp_weights - jnp.array(MLP_RATES, F32)[:, None, None] * mlp_ortho
    gains_new = gains - rate * gain_moment_new
    return (
        square_grad,
        square_moment_new,
        square_new,
        square_new.astype(BF16),
        mlp_grad,
        mlp_moment_new,
        mlp_new,
        mlp_new.astype(BF16),
        gain_grad,
        gain_moment_new,
        gains_new,
    )


def per_device(
    actions,
    observed,
    camera_flags,
    noise_levels,
    cotangent,
    square_weights,
    mlp_weights,
    gains,
    square_moment,
    mlp_moment,
    gain_moment,
):
    count = lax.axis_size("dp")
    rate = 0.1 / math.sqrt(actions.shape[0] * count)
    by_key = observed.transpose(1, 0, 2)
    ins = (actions, by_key, camera_flags, noise_levels, cotangent)
    if count == math.prod(GRID):
        made = block_and_back(True, *ins, square_weights, mlp_weights, gains, square_moment, mlp_moment)
        done = finish(rate, made, square_weights, mlp_weights, gains, gain_moment)
        output, actions_grad = done.output_f, done.ag_f
        d = done
        rest = (d.sqg, d.sqm, d.sqn, d.sqc, d.mlpg, d.mlpm, d.mlpn, d.mlpc, d.gg, d.gm, d.gn)
    else:
        square_all, mlp_all = (
            lax.all_gather(square_weights.astype(BF16), "dp", axis=1, tiled=True),
            lax.all_gather(mlp_weights.astype(BF16), "dp", axis=1, tiled=True),
        )
        gain_all = lax.all_gather(gains, "dp", axis=1, tiled=True)
        made = block_and_back(False, *ins, square_all, mlp_all, gain_all)
        done = finish(rate, made)
        output, actions_grad = made.output, made.ag
        grads = made.grads.reshape(-1, WIRE, LANES)
        rest = update_by_collectives(
            grads, square_weights, mlp_weights, gains, square_moment, mlp_moment, gain_moment, rate
        )
    observed_grad = done.og.transpose(1, 0, 2)
    return (output, actions_grad, observed_grad) + tuple(rest)


def solution(mesh):
    rows, cube, flat = P("dp", None), P("dp", None, None), P("dp")
    stacked, pair = P(None, "dp", None), P(None, "dp")
    return jax.shard_map(
        per_device,
        mesh=mesh,
        in_specs=(rows, cube, flat, flat, rows, stacked, stacked, pair, stacked, stacked, pair),
        out_specs=(rows, rows, cube) + (stacked,) * 8 + (pair,) * 3,
        check_vma=False,
    )
```

```python
import functools
import math

import jax
import jax.numpy as jnp
from jax import lax
from jax.experimental import pallas as pl
from jax.experimental.pallas import tpu as pltpu
from jax.sharding import PartitionSpec as P

HEADS = 4
ACT = 16
OBS_FULL = 196
OBS_FEW = 49
COEF_A = 3.4445
COEF_B = -4.775
COEF_C = 2.0315
F32 = jnp.float32
BF16 = jnp.bfloat16
MESH = pl.DeviceIdType.MESH
VMEM = pltpu.VMEM
NN = (((1,), (0,)), ((), ()))
NT = (((1,), (1,)), ((), ()))
TN = (((0,), (0,)), ((), ()))

LANES = 128
TILE = 8
MLP_ROWS = 64
SQ_ROWS = 16
SQ_AT = (160, 192, 176, 128, 144)
GAIN_BASE = 208
WIRE = 224
PIECES = ((0, 64), (64, 64), (128, 32), (160, 32), (192, 32))
PIECE_X_FIRST = (True, False, True, True, False)
CHUNKS = ((0, 64), (64, 64), (128, 32), (160, 32), (192, 16), (208, 16))
X_FIRST = (True, False, True, False, True, False)
COMPLETES = ((0,), (1,), (5, 6), (2, 4), (3,), ())
MLP_RATES = (1.0, 0.5)
SQ_RATES = (0.5, 0.5, 0.5, 0.5, 4.0)
GRID = (4, 2, 2, 2)
OWNERS = (8, 22, 14, 16, 11, 21, 13)
SHIFTS = (0.0, 0.0, 0.4, 0.8, 0.8)
KEYS_PAD = 208
GROUP = 16
ROWS = 512


class Refs:
    def __init__(self, pairs):
        self.__dict__.update(pairs)


def dot(left, right, dims=NN):
    return lax.dot_general(left, right, dims, preferred_element_type=F32)


def place():
    me = lax.axis_index("dp")
    return me, me // 8, (me // 4) % 2, (me // 2) % 2, me % 2


def device_at(z, y, x, c):
    return ((z * 2 + y) * 2 + x) * 2 + c


def link(src, dst, send, recv, device):
    return pltpu.make_async_remote_copy(
        src_ref=src,
        dst_ref=dst,
        send_sem=send,
        recv_sem=recv,
        device_id=(device,),
        device_id_type=MESH,
    )


def greet(device):
    pl.semaphore_signal(
        pltpu.get_barrier_semaphore(), inc=1, device_id=(device,), device_id_type=MESH
    )


def normalize(values):
    centred = values - jnp.mean(values, -1, keepdims=True)
    scale = lax.rsqrt(jnp.mean(centred * centred, -1, keepdims=True) + 1e-05)
    return centred * scale, scale


def norm_back(grad, hat, scale):
    mean_one = jnp.mean(grad, -1, keepdims=True)
    mean_two = jnp.mean(grad * hat, -1, keepdims=True)
    return scale * (grad - mean_one - hat * mean_two)


class Gather:
    def __init__(self, r):
        self.r = r
        self.me, self.z, self.y, self.x, self.c = place()

    def hop(self, k, step, part, device):
        return link(part, part, self.r.gsend.at[k, step], self.r.grecv.at[k, step], device)

    def along_z(self, k, step):
        part = self.r.wire.at[self.z, self.y, self.x, self.c, pl.ds(*PIECES[k])]
        return self.hop(k, step, part, device_at((self.z + step + 1) % 4, self.y, self.x, self.c))

    def from_z(self, k, step):
        there = (self.z + 3 - step) % 4
        part = self.r.wire.at[there, self.y, self.x, self.c, pl.ds(*PIECES[k])]
        return self.hop(k, step, part, device_at(there, self.y, self.x, self.c))

    def plane(self, k, second, mine):
        z, y, x, c = self.z, self.y, self.x, self.c
        rows, wire = pl.ds(*PIECES[k]), self.r.wire
        py, px = (y, x) if mine else (1 - y, 1 - x)
        along_x = PIECE_X_FIRST[k] == second
        if along_x:
            part = wire.at[:, y, px, c, rows] if second else wire.at[:, :, px, c, rows]
            return self.hop(k, 3 if second else 4, part, device_at(z, y, 1 - x, c))
        part = wire.at[:, py, x, c, rows] if second else wire.at[:, py, :, c, rows]
        return self.hop(k, 3 if second else 4, part, device_at(z, 1 - y, x, c))

    def core(self, k, mine):
        part = self.r.wire.at[:, :, :, self.c if mine else 1 - self.c, pl.ds(*PIECES[k])]
        return self.hop(k, 5, part, device_at(self.z, self.y, self.x, 1 - self.c))

    def first(self, *chunks):
        for k in chunks:
            for step in range(3):
                self.along_z(k, step).start()

    def second(self, *chunks):
        for k in chunks:
            for step in range(3):
                self.from_z(k, step).wait_recv()
            self.plane(k, True, True).start()

    def third(self, *chunks):
        for k in chunks:
            self.plane(k, True, False).wait_recv()
            self.plane(k, False, True).start()

    def fourth(self, *chunks):
        for k in chunks:
            self.plane(k, False, False).wait_recv()
            self.core(k, True).start()

    def last(self, *chunks):
        for k in chunks:
            self.core(k, False).wait_recv()

    def drain(self):
        for k in range(len(PIECES)):
            for step in range(3):
                self.along_z(k, step).wait_send()
            self.plane(k, True, True).wait_send()
            self.plane(k, False, True).wait_send()
            self.core(k, True).wait_send()

    def fill(self):
        r = self.r
        spot = (self.z, self.y, self.x, self.c)

        def tiles(source, m, base, number):
            for j in range(number):
                pair = [source[m, :, pl.ds((2 * j + k) * LANES, LANES)] for k in range(2)]
                r.wire[spot + (pl.ds(base + j * 16, 16),)] = jnp.concatenate(pair, axis=0).astype(BF16)

        for m in range(5):
            tiles(r.sqw_v, m, SQ_AT[m], 1)
        for m in range(2):
            tiles(r.mlpw_v, m, m * MLP_ROWS, 4)
        gains, edge = r.gain_v[...], r.edge
        high = gains.astype(BF16).astype(F32)
        middle = (gains - high).astype(BF16).astype(F32)
        edge[...] = jnp.zeros_like(edge)
        edge[0:2, 0:TILE] = high
        edge[2:4, 0:TILE] = middle
        edge[4:6, 0:TILE] = (gains - high - middle).astype(BF16).astype(F32)
        r.wire[spot + (pl.ds(GAIN_BASE, 16),)] = edge[...].astype(BF16)

    def unpack(self, base, number, out, m):
        for j in range(number):
            block = self.r.wire[:, :, :, :, pl.ds(base + j * 16, 16), :].reshape(32, 16, LANES).astype(F32)
            for half in range(2):
                columns = pl.ds((2 * j + half) * LANES, LANES)
                out[m, :, columns] = block[:, half * 8 : half * 8 + 8, :].reshape(256, LANES).astype(BF16)

    def unpack_gains(self):
        edge, wire = self.r.edge, self.r.wire
        for half in range(2):
            total = jnp.zeros((16, LANES), F32)
            for at in range(16):
                d = half * 16 + at
                tile = wire[d // 8, (d // 4) % 2, (d // 2) % 2, d % 2, pl.ds(GAIN_BASE, 16), :].astype(F32)
                total = total + (tile if at == 0 else pltpu.roll(tile, at * TILE, 1))
            edge[...] = total
            self.r.gain_all[:, pl.ds(half * LANES, LANES)] = edge[0:2, :] + edge[2:4, :] + edge[4:6, :]


class Update:
    def __init__(self, r):
        self.r = r
        self.me, self.z, self.y, self.x, self.c = place()

    def hop(self, k, step, src, dst, device):
        return link(src, dst, self.r.send.at[k, step], self.r.recv.at[k, step], device)

    def core(self, k):
        rows = pl.ds(*CHUNKS[k])
        src, dst = self.r.send0.at[:, :, :, rows], self.r.got_core.at[:, :, :, rows]
        return self.hop(k, 0, src, dst, device_at(self.z, self.y, self.x, 1 - self.c))

    def plane(self, k, first):
        rows = pl.ds(*CHUNKS[k])
        to = (self.z, self.y, 1 - self.x, self.c) if X_FIRST[k] == first else (self.z, 1 - self.y, self.x, self.c)
        if first:
            src, dst = self.r.send1.at[:, :, rows], self.r.got1.at[:, :, rows]
        else:
            src, dst = self.r.send2.at[:, rows], self.r.got2.at[:, rows]
        return self.hop(k, 1 if first else 2, src, dst, device_at(*to))

    def along_z(self, k, step):
        rows = pl.ds(*CHUNKS[k])
        to = device_at((self.z + step + 1) % 4, self.y, self.x, self.c)
        return self.hop(k, 3 + step, self.r.send3.at[step, rows], self.r.got3.at[step, rows], to)

    def start(self, k):
        rows = pl.ds(*CHUNKS[k])
        self.r.send0[:, :, :, rows, :] = self.r.grads[:, :, :, 1 - self.c, rows, :].astype(BF16)
        self.core(k).start()

    def one(self, *chunks):
        r = self.r
        for k in chunks:
            rows = pl.ds(*CHUNKS[k])
            self.core(k).wait_recv()
            sum1 = r.sum1
            sum1[:, :, :, rows, :] = r.grads[:, :, :, self.c, rows, :] + r.got_core[:, :, :, rows, :].astype(F32)
            other = sum1[:, :, 1 - self.x, rows, :] if X_FIRST[k] else sum1[:, 1 - self.y, :, rows, :]
            r.send1[:, :, rows, :] = other.astype(BF16)
            self.plane(k, True).start()

    def two(self, *chunks):
        r = self.r
        for k in chunks:
            rows = pl.ds(*CHUNKS[k])
            self.plane(k, True).wait_recv()
            sum1, sum2 = r.sum1, r.sum2
            mine = sum1[:, :, self.x, rows, :] if X_FIRST[k] else sum1[:, self.y, :, rows, :]
            sum2[:, :, rows, :] = mine + r.got1[:, :, rows, :].astype(F32)
            other = 1 - self.y if X_FIRST[k] else 1 - self.x
            r.send2[:, rows, :] = sum2[:, other, rows, :].astype(BF16)
            self.plane(k, False).start()

    def three(self, *chunks):
        r = self.r
        for k in chunks:
            rows = pl.ds(*CHUNKS[k])
            self.plane(k, False).wait_recv()
            mine = self.y if X_FIRST[k] else self.x
            r.sum3[:, rows, :] = r.sum2[:, mine, rows, :] + r.got2[:, rows, :].astype(F32)
            for step in range(3):
                r.send3[step, rows, :] = r.sum3[(self.z + step + 1) % 4, rows, :].astype(BF16)
                self.along_z(k, step).start()

    def slab(self, index):
        if index < 2:
            return pl.ds(index * MLP_ROWS, MLP_ROWS), self.r.slabs_mlp, self.r.result_mlp
        return pl.ds(SQ_AT[index - 2], SQ_ROWS), self.r.slabs_sq, self.r.result_sq

    def to_owner(self, index):
        rows, slabs, _ = self.slab(index)
        moment = self.r.moment_low if index < 2 else self.r.moment
        return link(
            moment.at[rows], slabs.at[self.me],
            self.r.own_send.at[index], self.r.own_recv.at[0], OWNERS[index],
        )

    def four(self, *chunks):
        r = self.r
        moment, out = r.moment, r.out
        for k in chunks:
            rows = pl.ds(*CHUNKS[k])
            total = r.sum3[self.z, rows, :]
            for step in range(3):
                self.along_z(k, step).wait_recv()
                total = total + r.got3[step, rows, :].astype(F32)
            out[0, rows, :] = total
            new = 0.5 * moment[rows, :] + total
            moment[rows, :] = new
            if k < 2:
                r.moment_low[rows, :] = new.astype(BF16)
            for index in COMPLETES[k]:
                rows_m, slabs, _ = self.slab(index)

                @pl.when(self.me != OWNERS[index])
                def _():
                    self.to_owner(index).start()

                @pl.when(self.me == OWNERS[index])
                def _():
                    mine = r.moment_low if index < 2 else moment
                    pltpu.make_async_copy(mine.at[rows_m], slabs.at[self.me], r.own_recv.at[0]).start()

    def old_moment(self):
        r = self.r
        moment = r.moment
        for m in range(2):
            for j in range(8):
                moment[pl.ds(m * MLP_ROWS + j * TILE, TILE), :] = r.mlpm_v[m, :, pl.ds(j * LANES, LANES)]
        for m in range(5):
            for j in range(2):
                moment[pl.ds(SQ_AT[m] + j * TILE, TILE), :] = r.sqm_v[m, :, pl.ds(j * LANES, LANES)]
        moment[pl.ds(GAIN_BASE, 16), :] = jnp.zeros((16, LANES), F32)

    def orthogonalize(self):
        r = self.r
        cur = r.cur
        rows = lax.broadcasted_iota(jnp.int32, (256, 256), 0)
        diagonal = rows == lax.broadcasted_iota(jnp.int32, (256, 256), 1)

        def run(slabs, result, tiles):
            pltpu.make_async_copy(slabs, slabs, r.own_recv.at[0]).wait()
            low = r.cur_low
            for j in range(tiles // 2):
                pair = slabs[:, pl.ds(j * 16, 16), :].astype(F32)
                for side in range(2):
                    columns = pl.ds((2 * j + side) * LANES, LANES)
                    part = pair[:, side * TILE : (side + 1) * TILE, :].reshape(256, LANES)
                    cur[:, columns] = part
                    low[:, columns] = part.astype(BF16)
            scale = 1.0
            for turn, shift in enumerate(SHIFTS):
                whole = low[:, 0 : tiles * LANES]
                off = dot(whole, whole, NT)
                if turn == 0:
                    norm = jnp.sum(jnp.sum(jnp.where(diagonal, off, 0.0), axis=0, keepdims=True), axis=1, keepdims=True)
                    scale = 1.0 / (jnp.sqrt(norm) + 1e-07)
                    off = off * (scale * scale)
                if shift:
                    off = off - jnp.where(diagonal, shift, 0.0)
                off_low = off.astype(BF16)
                poly = (COEF_B + 2.0 * COEF_C * shift) * off + COEF_C * dot(off_low, off_low)
                poly = poly.astype(BF16)
                keep = COEF_A + shift * (COEF_B + COEF_C * shift)
                for j in range(tiles // 2):
                    columns = pl.ds(j * 2 * LANES, 2 * LANES)
                    now = keep * cur[:, columns] + dot(poly, low[:, columns])
                    if turn == 0:
                        now = now * scale
                    if turn < len(SHIFTS) - 1:
                        cur[:, columns] = now
                        low[:, columns] = now.astype(BF16)
                    else:
                        parts = [now[:, side * LANES : (side + 1) * LANES].reshape(32, TILE, LANES) for side in range(2)]
                        result[:, pl.ds(j * 16, 16), :] = jnp.concatenate(parts, axis=1).astype(result.dtype)

        mine_mlp = jnp.logical_or(self.me == OWNERS[0], self.me == OWNERS[1])
        mine_sq = self.me < 0
        for device in OWNERS[2:]:
            mine_sq = jnp.logical_or(mine_sq, self.me == device)

        @pl.when(mine_mlp)
        def _():
            run(r.slabs_mlp, r.result_mlp, 8)

        @pl.when(mine_sq)
        def _():
            run(r.slabs_sq, r.result_sq, 2)

    def landing(self, index):
        if index < 2:
            return self.r.back_mlp.at[index]
        return self.r.out.at[2, pl.ds(SQ_AT[index - 2], SQ_ROWS)]

    def give_back(self, index, device):
        _, _, result = self.slab(index)
        return link(
            result.at[device], self.landing(index),
            self.r.back_send.at[device], self.r.back_recv.at[index], device,
        )

    def give_all(self):
        r = self.r
        for index in range(7):
            _, _, result = self.slab(index)

            @pl.when(self.me == OWNERS[index])
            def _():
                def send_one(step, _):
                    self.give_back(index, (self.me + step) % 32).start()
                    return 0

                lax.fori_loop(1, 32, send_one, 0)
                pltpu.make_async_copy(result.at[self.me], self.landing(index), r.back_recv.at[index]).start()

    def take_all(self):
        for index in range(7):
            _, _, result = self.slab(index)
            pltpu.make_async_copy(result.at[0], self.landing(index), self.r.back_recv.at[index]).wait()
        for index in range(2):
            rows = pl.ds(index * MLP_ROWS, MLP_ROWS)
            self.r.out[2, rows, :] = self.r.back_mlp[index].astype(F32)

    def drain(self):
        for k in range(len(CHUNKS)):
            self.core(k).wait_send()
            self.plane(k, True).wait_send()
            self.plane(k, False).wait_send()
            for step in range(3):
                self.along_z(k, step).wait_send()
        for index in range(7):

            @pl.when(self.me != OWNERS[index])
            def _():
                self.to_owner(index).wait_send()

    def drain_owner(self):
        for index in range(7):

            @pl.when(self.me == OWNERS[index])
            def _():
                def wait_one(step, _):
                    self.give_back(index, (self.me + step) % 32).wait_send()
                    return 0

                lax.fori_loop(1, 32, wait_one, 0)


def greet_all():
    me, z, y, x, c = place()
    greet(device_at(z, y, x, 1 - c))
    greet(device_at(z, y, 1 - x, c))
    greet(device_at(z, 1 - y, x, c))
    for step in range(1, 4):
        greet(device_at((z + step) % 4, y, x, c))
    owner = me < 0
    for device in OWNERS:
        owner = jnp.logical_or(owner, me == device)

        @pl.when(me != device)
        def _():
            greet(device)

    @pl.when(owner)
    def _():
        def greet_other(step, _):
            greet((me + step) % 32)
            return 0

        lax.fori_loop(1, 32, greet_other, 0)

    is_owner = owner.astype(jnp.int32)
    return 6 + 7 - is_owner + 31 * is_owner


def block_kernel(names, remote, *args):
    r = Refs(zip(names, args))
    keys, samples = r.obs.shape[0], r.obs.shape[1]
    tokens, width = r.acts.shape
    head_dim, half, per = width // HEADS, width // 2, ROWS // ACT
    wide = r.mlp_all.shape[2]
    groups = samples // GROUP
    in_sems, out_sems = r.in_sems, r.out_sems

    if remote:
        own = (r.sqw_v, r.mlpw_v, r.gain_v)
    else:
        own = (r.sq_all, r.mlp_all, r.gain_all)
    loads = list(zip((r.sqw, r.mlpw, r.gain), own))
    loads += [(r.acts, r.acts_v), (r.obs, r.obs_v.at[pl.ds(0, keys)]), (r.cot, r.cot_v)]
    if remote:
        loads += [(r.sqm, r.sqm_v), (r.mlpm, r.mlpm_v)]
    loads += [(r.flags, r.flags_s), (r.levels, r.levels_s)]
    copies = [pltpu.make_async_copy(a, b, in_sems.at[i]) for i, (a, b) in enumerate(loads)]

    def arrive(*which):
        for i in which:
            copies[i].wait()

    for copy in copies:
        copy.start()
    if remote:
        gather, update = Gather(r), Update(r)
        expected = greet_all()
        arrive(0, 1, 2)
        gather.fill()
        pl.semaphore_wait(pltpu.get_barrier_semaphore(), expected)
        gather.first(3, 4)

    arrive(3)

    def hats(i, _):
        rows = pl.ds(pl.multiple_of(i * ROWS, ROWS), ROWS)
        hat, scale = normalize(r.acts_v[rows, :])
        r.xhat[rows, :] = hat
        r.rstd[rows, :] = scale
        return 0

    lax.fori_loop(0, tokens // ROWS, hats, 0)

    mem, obs_v = r.mem, r.obs_v
    batch = 16
    chunks = KEYS_PAD // batch
    swap = r.swap
    row = lax.broadcasted_iota(jnp.int32, swap.shape, 0)
    column = lax.broadcasted_iota(jnp.int32, swap.shape, 1)
    swap[...] = jnp.where(column == (row % batch) * batch + row // batch, 1.0, 0.0).astype(BF16)

    def turn(part, low, high):
        def one(j, _):
            at = pl.ds(pl.multiple_of(j * batch, batch), batch)
            here = pl.ds(part * batch, batch)
            block = obs_v[at, here, :].reshape(batch * batch, width)
            mem[here, at, :] = dot(swap[...], block).astype(BF16).reshape(batch, batch, width)
            return 0

        lax.fori_loop(low, high, one, 0, unroll=high - low)

    whole = chunks - 1
    arrive(4)
    turn(0, 0, whole // 2)
    if remote:
        gather.second(3, 4)
        gather.first(2, 0, 1)
    turn(0, whole // 2, whole)
    if remote:
        gather.third(3, 4)
    turn(1, 0, whole // 2)
    if remote:
        gather.second(2, 0, 1)
        gather.fourth(3, 4)
    turn(1, whole // 2, whole)
    arrive(len(copies) - 1, len(copies) - 2)
    freqs = jnp.exp(
        lax.broadcasted_iota(jnp.int32, (1, half), 1).astype(F32) * F32(-math.log(10000.0)) / half
    )
    for s in range(samples):
        r.angle[s : s + 1, :] = r.levels_s[s].astype(F32) * freqs
    r.embed[:, 0:half] = jnp.sin(r.angle[...]).astype(BF16)
    r.embed[:, half:width] = jnp.cos(r.angle[...]).astype(BF16)
    if remote:
        arrive(6, 7)
        update.old_moment()
        gather.third(2, 0, 1)
        gather.last(3, 4)
        for m in range(3):
            gather.unpack(SQ_AT[m], 1, r.sq_all, m)
        gather.unpack_gains()
    else:
        arrive(0, 1, 2)

    sq, mlp = r.sq_all, r.mlp_all
    wkh, wvh = r.wkh, r.wvh
    lane = lax.broadcasted_iota(jnp.int32, (width, width), 1)

    def split_heads(out, weight):
        weight = weight.astype(F32)
        for h in range(HEADS):
            out[pl.ds(h * width, width), :] = jnp.where(lane // head_dim == h, weight, 0.0).astype(BF16)

    split_heads(wkh, sq[2])
    g1, g2 = r.gain_all[0:1, :], r.gain_all[1:2, :]

    obs_v[keys] = dot(r.embed[...], sq[0]).astype(BF16)
    obs_v[keys + 1 :] = jnp.zeros((KEYS_PAD - keys - 1, samples, width), BF16)
    for part in range(samples // batch):
        turn(part, whole, chunks)

    sides, weights = r.sides_v, r.pds_v

    def make_queries(i, _):
        rows = pl.ds(pl.multiple_of(i * ROWS, ROWS), ROWS)
        first = (r.xhat[rows, :] * g1).astype(BF16)
        r.first[rows, :] = first
        q = dot(first, sq[1]).astype(BF16)
        r.query[rows, :] = q
        here = pl.ds(i * per, per)
        for h in range(HEADS):
            wk = wkh[pl.ds(h * width, width), :]
            value = (dot(q, wk, NT) * 0.125).astype(BF16).reshape(per, ACT, width)
            sides[here, pl.ds((HEADS + h) * ACT, ACT), :] = value
        return 0

    lax.fori_loop(0, tokens // ROWS, make_queries, 0)

    key = lax.broadcasted_iota(jnp.int32, (1, KEYS_PAD), 1)
    low_rows, high_rows = pl.ds(0, HEADS * ACT), pl.ds(HEADS * ACT, HEADS * ACT)

    ones = jnp.ones((KEYS_PAD, LANES), BF16)

    def attend(g, _):
        ids = [g * GROUP + k for k in range(GROUP)]
        scores = [dot(sides[s, high_rows, :], mem[s], NT) for s in ids]
        lows = []
        for s, score in zip(ids, scores):
            count = OBS_FEW + (OBS_FULL - OBS_FEW) * r.flags_s[s]
            score = score + jnp.where((key < count) | (key == OBS_FULL), 0.0, -1000000000.0)
            expo = jnp.exp(score - jnp.max(score, -1, keepdims=True))
            low = expo.astype(BF16)
            part = 1.0 / dot(low, ones)
            probs = expo * jnp.concatenate([part, part[:, 0 : KEYS_PAD - LANES]], axis=1)
            r.probs[s] = probs
            weights[s, low_rows, :] = probs.astype(BF16)
            lows.append((low, jnp.concatenate([part, part], axis=1)))
        for s, (low, part) in zip(ids, lows):
            u = (dot(low, mem[s]) * part).astype(BF16)
            rows = pl.ds(pl.multiple_of(s * ACT, ACT), ACT)
            for h in range(HEADS):
                r.u[rows, pl.ds(h * width, width)] = u[h * ACT : (h + 1) * ACT, :]
        return 0

    lax.fori_loop(0, groups // 2, attend, 0)
    if remote:
        gather.fourth(2, 0, 1)
    lax.fori_loop(groups // 2, groups, attend, 0)
    if remote:
        gather.last(2, 0, 1)
        for m in range(3, 5):
            gather.unpack(SQ_AT[m], 1, sq, m)
        for m in range(2):
            gather.unpack(m * MLP_ROWS, 4, mlp, m)
    split_heads(wvh, sq[3])

    gain_acc = r.gain_acc
    gain_acc[...] = jnp.zeros_like(gain_acc)
    arrive(5)

    def feed(i, _):
        rows = pl.ds(pl.multiple_of(i * ROWS, ROWS), ROWS)
        mixed = dot(r.u[rows, :], wvh[...]).astype(BF16)
        r.mixed[rows, :] = mixed
        resid = r.acts_v[rows, :] + dot(mixed, sq[4])
        hat, scale = normalize(resid)
        second = (hat * g2).astype(BF16)
        r.second[rows, :] = second
        cot = r.cot_v[rows, :]
        out_low = cot.astype(BF16)
        r.out_low[rows, :] = out_low
        for c in range(wide // 256):
            columns = pl.ds(c * 256, 256)
            v = dot(second, mlp[0, :, columns])
            square = v * v
            t = jnp.tanh(0.7978845608 * (v + 0.044715 * square * v))
            r.active[rows, columns] = (0.5 * v * (1.0 + t)).astype(BF16)
            slope = 0.5 * (1.0 + t) + 0.5 * v * (1.0 - t * t) * (0.7978845608 * (1.0 + 0.134145 * square))
            r.dhidden[rows, columns] = (slope * dot(out_low, mlp[1, :, columns])).astype(BF16)
        r.out_v[rows, :] = resid + dot(r.active[rows, :], mlp[1], NT)
        grad_second = dot(r.dhidden[rows, :], mlp[0], NT)
        gain_acc[1:2, :] += jnp.sum(grad_second * hat, 0, keepdims=True)
        dres = cot + norm_back(grad_second * g2, hat, scale)
        r.dres[rows, :] = dres
        low = dres.astype(BF16)
        r.dres_low[rows, :] = low
        gm = dot(low, sq[4], NT).astype(BF16)
        r.dmixed[rows, :] = gm
        here = pl.ds(i * per, per)
        for h in range(HEADS):
            wv = wvh[pl.ds(h * width, width), :]
            sides[here, pl.ds(h * ACT, ACT), :] = dot(gm, wv, NT).astype(BF16).reshape(per, ACT, width)
        return 0

    lax.fori_loop(0, tokens // ROWS, feed, 0)
    keep_out = pltpu.make_async_copy(r.out_v, r.output, out_sems.at[0])
    keep_out.start()

    grads = r.grads

    def put(base, tiles, value):
        for j in range(tiles):
            part = value[:, j * LANES : (j + 1) * LANES].reshape(GRID + (TILE, LANES))
            grads[:, :, :, :, pl.ds(base + j * TILE, TILE), :] = part

    def by_head(left, right):
        turned = left.T
        parts = [
            dot(turned[h * head_dim : (h + 1) * head_dim, :], right[:, pl.ds(h * width, width)])
            for h in range(HEADS)
        ]
        return jnp.concatenate(parts, axis=0).T

    put(0, 8, dot(r.second[...], r.dhidden[...], TN))
    if remote:
        update.start(0)
    put(MLP_ROWS, 8, dot(r.out_low[...], r.active[...], TN))
    if remote:
        update.start(1)
    put(SQ_AT[4], 2, dot(r.mixed[...], r.dres_low[...], TN))
    put(SQ_AT[3], 2, by_head(r.dmixed[...], r.u))
    if remote:
        update.start(2)

    def attend_back(g, _):
        ids = [g * GROUP + k for k in range(GROUP)]
        rises = [dot(sides[s, low_rows, :], mem[s], NT) for s in ids]
        for s, rise in zip(ids, rises):
            probs = r.probs[s]
            both = probs * rise
            weights[s, high_rows, :] = (both - probs * jnp.sum(both, -1, keepdims=True)).astype(BF16)
        for s in ids:
            dq = (dot(weights[s, high_rows, :], mem[s]) * 0.125).astype(BF16)
            rows = pl.ds(pl.multiple_of(s * ACT, ACT), ACT)
            for h in range(HEADS):
                r.dq_wide[rows, pl.ds(h * width, width)] = dq[h * ACT : (h + 1) * ACT, :]
            end = dot(weights[s, :, LANES:KEYS_PAD], sides[s], TN)
            r.stamps[s] = end[64:72, :]
        return 0

    half_groups = groups // 2
    lax.fori_loop(0, half_groups, attend_back, 0)
    if remote:
        update.one(0)
    lax.fori_loop(half_groups, groups, attend_back, 0)
    put(SQ_AT[2], 2, by_head(r.query[...], r.dq_wide))
    stamp_low = r.stamps[:, 4:5, :].reshape(samples, width).astype(BF16)
    put(SQ_AT[0], 2, dot(r.embed[...], stamp_low, TN))
    if remote:
        update.start(3)
        update.one(1, 2)

    def memory_back(low, high):
        def one(g, _):
            for k in range(GROUP):
                s = g * GROUP + k
                mem[s] = dot(weights[s], sides[s], TN).astype(BF16)
            return 0

        lax.fori_loop(low, high, one, 0)

    def turn_back(part):
        def one(j):
            at = pl.ds(pl.multiple_of(j * batch, batch), batch)
            here = pl.ds(part * batch, batch)
            block = mem[here, at, :].reshape(batch * batch, width)
            value = dot(swap[...], block).astype(BF16).reshape(batch, batch, width)
            number = min(batch, keys - j * batch)
            r.og[pl.ds(j * batch, number), here, :] = value[0:number]

        for j in range(chunks):
            one(j)

    def queries_back(i, _):
        rows = pl.ds(pl.multiple_of(i * ROWS, ROWS), ROWS)
        r.dquery[rows, :] = dot(r.dq_wide[rows, :], wkh[...]).astype(BF16)
        return 0

    lax.fori_loop(0, tokens // ROWS, queries_back, 0)
    put(SQ_AT[1], 2, dot(r.first[...], r.dquery[...], TN))
    if remote:
        update.start(4)

    def acts_back(i, _):
        rows = pl.ds(pl.multiple_of(i * ROWS, ROWS), ROWS)
        grad_first = dot(r.dquery[rows, :], sq[1], NT)
        hat = r.xhat[rows, :]
        gain_acc[0:1, :] += jnp.sum(grad_first * hat, 0, keepdims=True)
        r.ag_v[rows, :] = r.dres[rows, :] + norm_back(grad_first * g1, hat, r.rstd[rows, :])
        return 0

    def finish_acts():
        lax.fori_loop(0, tokens // ROWS, acts_back, 0)
        for norm in range(2):
            for j in range(2):
                row = gain_acc[norm : norm + 1, j * LANES : (j + 1) * LANES]
                at = GAIN_BASE + norm * 2 + j
                value = jnp.broadcast_to(row.reshape(1, 1, 1, 1, 1, LANES), GRID + (1, LANES))
                grads[:, :, :, :, at : at + 1, :] = value
        rest = WIRE - GAIN_BASE - 4
        grads[:, :, :, :, GAIN_BASE + 4 : WIRE, :] = jnp.zeros(GRID + (rest, LANES), F32)

    keep_ag = pltpu.make_async_copy(r.ag_v, r.ag, out_sems.at[1])
    if remote:
        update.two(0)
        update.one(3)
        finish_acts()
        keep_ag.start()
        update.start(5)
        update.two(1, 2)
        update.one(4)
        memory_back(0, half_groups)
        update.two(3)
        update.one(5)
        update.three(0, 1)
        update.two(4)
        memory_back(half_groups, groups)
        update.three(2, 3, 4)
        update.two(5)
        update.four(0, 1)
        turn_back(0)
        update.four(2, 3, 4)
        update.three(5)
        update.orthogonalize()
        update.give_all()
        turn_back(1)
        update.four(5)
        out = r.out
        out[1, :, :] = r.moment[...]
        out[2, pl.ds(GAIN_BASE, 16), :] = jnp.zeros((16, LANES), F32)
        gather.drain()
        update.drain()
        update.take_all()
        update.drain_owner()
    else:
        finish_acts()
        keep_ag.start()
        memory_back(0, groups)
        for part in range(samples // batch):
            turn_back(part)
    for copy in (keep_out, keep_ag):
        copy.wait()


def block_and_back(remote, acts, obs, flags, levels, cot, sqw, mlpw, gain, sqm=None, mlpm=None):
    tokens, width = acts.shape
    keys, samples = obs.shape[0], obs.shape[1]
    rows = HEADS * ACT
    wide = mlpw.shape[2]
    any_space = pl.BlockSpec(memory_space=pl.ANY)
    in_vmem = pl.BlockSpec(memory_space=VMEM)
    sem = pltpu.SemaphoreType.DMA
    ins = dict(flags=flags, levels=levels, acts=acts, obs=obs, cot=cot, sqw=sqw, mlpw=mlpw, gain=gain)
    outs = dict(
        output=jax.ShapeDtypeStruct(acts.shape, F32),
        ag=jax.ShapeDtypeStruct(acts.shape, F32),
        og=jax.ShapeDtypeStruct(obs.shape, BF16),
    )
    grads = GRID + (WIRE, LANES)
    scratch = dict(
        obs_v=VMEM((KEYS_PAD, samples, width), BF16),
        acts_v=VMEM(acts.shape, F32),
        cot_v=VMEM(acts.shape, F32),
        mem=VMEM((samples, KEYS_PAD, width), BF16),
        swap=VMEM((256, 256), BF16),
        sq_all=VMEM((5, width, width), BF16),
        mlp_all=VMEM((2, width, wide), BF16),
        gain_all=VMEM((2, width), F32),
        wkh=VMEM((HEADS * width, width), BF16),
        wvh=VMEM((HEADS * width, width), BF16),
        first=VMEM((tokens, width), BF16),
        query=VMEM((tokens, width), BF16),
        xhat=VMEM((tokens, width), F32),
        rstd=VMEM((tokens, 1), F32),
        probs=VMEM((samples, rows, KEYS_PAD), F32),
        pds_v=VMEM((samples, 2 * rows, KEYS_PAD), BF16),
        sides_v=VMEM((samples, 2 * rows, width), BF16),
        u=VMEM((tokens, HEADS * width), BF16),
        dq_wide=VMEM((tokens, HEADS * width), BF16),
        mixed=VMEM((tokens, width), BF16),
        second=VMEM((tokens, width), BF16),
        active=VMEM((tokens, wide), BF16),
        dhidden=VMEM((tokens, wide), BF16),
        out_low=VMEM((tokens, width), BF16),
        dres_low=VMEM((tokens, width), BF16),
        dres=VMEM((tokens, width), F32),
        dmixed=VMEM((tokens, width), BF16),
        dquery=VMEM((tokens, width), BF16),
        out_v=VMEM((tokens, width), F32),
        ag_v=VMEM((tokens, width), F32),
        angle=VMEM((samples, width // 2), F32),
        embed=VMEM((samples, width), BF16),
        stamps=VMEM((samples, 8, width), F32),
        gain_acc=VMEM((8, width), F32),
        flags_s=pltpu.SMEM(flags.shape, jnp.int32),
        levels_s=pltpu.SMEM(levels.shape, jnp.int32),
        in_sems=sem((10,)),
        out_sems=sem((2,)),
    )
    extra = {}
    if remote:
        ins.update(sqm=sqm, mlpm=mlpm)
        outs.update(out=jax.ShapeDtypeStruct((3, WIRE, LANES), F32))
        chunks = len(CHUNKS)
        scratch.update(
            grads=VMEM(grads, F32),
            sqw_v=VMEM(sqw.shape, F32),
            mlpw_v=VMEM(mlpw.shape, F32),
            gain_v=VMEM(gain.shape, F32),
            sqm_v=VMEM(sqm.shape, F32),
            mlpm_v=VMEM(mlpm.shape, F32),
            wire=VMEM(grads, BF16),
            edge=VMEM((16, LANES), F32),
            gsend=sem((chunks, 6)),
            grecv=sem((chunks, 6)),
            send0=VMEM((4, 2, 2, WIRE, LANES), BF16),
            got_core=VMEM((4, 2, 2, WIRE, LANES), BF16),
            sum1=VMEM((4, 2, 2, WIRE, LANES), F32),
            send1=VMEM((4, 2, WIRE, LANES), BF16),
            got1=VMEM((4, 2, WIRE, LANES), BF16),
            sum2=VMEM((4, 2, WIRE, LANES), F32),
            send2=VMEM((4, WIRE, LANES), BF16),
            got2=VMEM((4, WIRE, LANES), BF16),
            sum3=VMEM((4, WIRE, LANES), F32),
            send3=VMEM((3, WIRE, LANES), BF16),
            got3=VMEM((3, WIRE, LANES), BF16),
            moment=VMEM((WIRE, LANES), F32),
            slabs_sq=VMEM((32, SQ_ROWS, LANES), F32),
            slabs_mlp=VMEM((32, MLP_ROWS, LANES), BF16),
            moment_low=VMEM((2 * MLP_ROWS, LANES), BF16),
            back_mlp=VMEM((2, MLP_ROWS, LANES), BF16),
            result_sq=VMEM((32, SQ_ROWS, LANES), F32),
            result_mlp=VMEM((32, MLP_ROWS, LANES), BF16),
            cur=VMEM((width, wide), F32),
            cur_low=VMEM((width, wide), BF16),
            send=sem((chunks, 6)),
            recv=sem((chunks, 6)),
            own_send=sem((7,)),
            own_recv=sem((1,)),
            back_send=sem((32,)),
            back_recv=sem((7,)),
        )
        extra = dict(collective_id=0, has_side_effects=True)
        outs = {name: VMEM(like.shape, like.dtype) for name, like in outs.items()}
    else:
        outs.update(grads=jax.ShapeDtypeStruct(grads, F32))
    names = tuple(ins) + tuple(outs) + tuple(scratch)
    stay = [pltpu.with_memory_space_constraint(value, pltpu.HBM) for value in ins.values()]
    results = pl.pallas_call(
        functools.partial(block_kernel, names, remote),
        out_shape=tuple(outs.values()),
        in_specs=[any_space] * len(ins),
        out_specs=[any_space] * 2 + [in_vmem] * 2,
        scratch_shapes=list(scratch.values()),
        compiler_params=pltpu.CompilerParams(vmem_limit_bytes=46 << 20, **extra),
        name="block_and_back",
    )(*stay)
    return Refs(zip(outs, results))


PARTS = 7


def finish_kernel(names, rate, *args):
    r = Refs(zip(names, args))
    sems = r.sems
    keys = r.og.shape[0]
    step = keys // PARTS

    def leave(part):
        block = pl.ds(part * step, step)
        return pltpu.make_async_copy(r.og_v.at[block], r.og.at[block], sems.at[part])

    more = PARTS
    moves = []
    if hasattr(r, "wire"):
        pairs = [(r.sqw, r.sqw_v), (r.mlpw, r.mlpw_v), (r.gain, r.gain_v), (r.gainm, r.gainm_v)]
        pairs += [(r.output, r.output_f), (r.ag, r.ag_f)]
        for source, target in pairs:
            moves.append(pltpu.make_async_copy(source, target, sems.at[more]))
            moves[-1].start()
            more += 1
    for part in range(PARTS):

        def widen(j, _):
            r.og_v[j] = r.low[j].astype(F32)
            return 0

        lax.fori_loop(part * step, (part + 1) * step, widen, 0, unroll=4)
        leave(part).start()
    for copy in moves[:4]:
        copy.wait()
    if hasattr(r, "wire"):
        finish_weights(r, rate)
    for part in range(PARTS):
        leave(part).wait()
    for copy in moves[4:]:
        copy.wait()


def finish_weights(r, rate):
    wire = r.wire
    me = lax.axis_index("dp")
    for m in range(5):
        for j in range(2):
            rows, columns = pl.ds(SQ_AT[m] + j * TILE, TILE), pl.ds(j * LANES, LANES)
            r.sqg[m, :, columns] = wire[0, rows, :]
            r.sqm[m, :, columns] = wire[1, rows, :]
            r.sqn[m, :, columns] = r.sqw_v[m, :, columns] - SQ_RATES[m] * wire[2, rows, :]
    r.sqc[...] = r.sqn[...].astype(BF16)
    for m in range(2):
        for j in range(8):
            rows, columns = pl.ds(m * MLP_ROWS + j * TILE, TILE), pl.ds(j * LANES, LANES)
            r.mlpg[m, :, columns] = wire[0, rows, :]
            r.mlpm[m, :, columns] = wire[1, rows, :]
            r.mlpn[m, :, columns] = r.mlpw_v[m, :, columns] - MLP_RATES[m] * wire[2, rows, :]
    r.mlpc[...] = r.mlpn[...].astype(BF16)
    tile = wire[0, pl.ds(GAIN_BASE, TILE), :]
    turned = pltpu.roll(tile, (LANES - (me % 16) * TILE) % LANES, 1)
    at = me // 16
    for norm in range(2):
        pair = turned[2 * norm : 2 * norm + 2, 0:TILE]
        row = jnp.where(at == 0, pair[0:1, :], pair[1:2, :])
        new = 0.5 * r.gainm_v[norm : norm + 1, :] + row
        r.gg[norm : norm + 1, :] = row
        r.gm[norm : norm + 1, :] = new
        r.gn[norm : norm + 1, :] = r.gain_v[norm : norm + 1, :] - rate * new


def finish(rate, made, sqw=None, mlpw=None, gain=None, gainm=None):
    any_space = pl.BlockSpec(memory_space=pl.ANY)
    in_vmem = pl.BlockSpec(memory_space=VMEM)
    ins = dict(low=made.og)
    outs = dict(og=jax.ShapeDtypeStruct(made.og.shape, F32))
    near, far = 1, 1
    if hasattr(made, "out"):
        ins.update(output=made.output, ag=made.ag, wire=made.out, sqw=sqw, mlpw=mlpw, gain=gain, gainm=gainm)
        like = jax.ShapeDtypeStruct
        near, far = 4, 3
        outs.update(
            output_f=like(made.output.shape, F32),
            ag_f=like(made.ag.shape, F32),
            sqg=like(sqw.shape, F32),
            sqm=like(sqw.shape, F32),
            sqn=like(sqw.shape, F32),
            sqc=like(sqw.shape, BF16),
            mlpg=like(mlpw.shape, F32),
            mlpm=like(mlpw.shape, F32),
            mlpn=like(mlpw.shape, F32),
            mlpc=like(mlpw.shape, BF16),
            gg=like(gain.shape, F32),
            gm=like(gain.shape, F32),
            gn=like(gain.shape, F32),
        )
    scratch = dict(
        og_v=VMEM(made.og.shape, F32),
        sems=pltpu.SemaphoreType.DMA((PARTS + 6,)),
    )
    if hasattr(made, "out"):
        scratch.update(
            sqw_v=VMEM(sqw.shape, F32),
            mlpw_v=VMEM(mlpw.shape, F32),
            gain_v=VMEM(gain.shape, F32),
            gainm_v=VMEM(gainm.shape, F32),
        )
    names = tuple(ins) + tuple(outs) + tuple(scratch)
    made_here = list(ins.values())
    stay = [pltpu.with_memory_space_constraint(value, pltpu.HBM) for value in made_here[near:]]
    results = pl.pallas_call(
        functools.partial(finish_kernel, names, rate),
        out_shape=tuple(outs.values()),
        in_specs=[in_vmem] * near + [any_space] * (len(ins) - near),
        out_specs=[any_space] * far + [in_vmem] * (len(outs) - far),
        scratch_shapes=list(scratch.values()),
        compiler_params=pltpu.CompilerParams(vmem_limit_bytes=16 << 20),
        name="finish",
    )(*made_here[:near], *stay)
    return Refs(zip(outs, results))


HIGH_PRECISION = lax.Precision.HIGHEST


def plain_orthogonalize(matrix):
    current = matrix / (jnp.sqrt(jnp.sum(matrix * matrix)) + 1e-07)
    for turn in range(5):
        gram = jnp.dot(current, current.T, precision=HIGH_PRECISION)
        poly = COEF_B * gram + COEF_C * jnp.dot(gram, gram, precision=HIGH_PRECISION)
        current = COEF_A * current + jnp.dot(poly, current, precision=HIGH_PRECISION)
    return current


def pick_owned(stack, owners, device):
    chosen = jnp.zeros_like(stack[0])
    for index in range(len(owners)):
        chosen = jnp.where(device == owners[index], stack[index], chosen)
    return chosen


def is_owner(owners, device):
    flag = device < 0
    for owner in owners:
        flag = jnp.logical_or(flag, device == owner)
    return flag


def from_wire(grads):
    def matrix(base, tiles):
        part = grads[:, base : base + tiles * TILE, :].reshape(-1, tiles, TILE, LANES)
        return part.transpose(0, 2, 1, 3).reshape(-1, tiles * LANES)

    square = jnp.stack([matrix(SQ_AT[m], 2) for m in range(5)])
    mlp = jnp.stack([matrix(m * MLP_ROWS, 8) for m in range(2)])
    return square, mlp, grads[0, GAIN_BASE : GAIN_BASE + 4, :].reshape(2, 2 * LANES)


def update_by_collectives(
    grads, square_weights, mlp_weights, gains, square_moment, mlp_moment, gain_moment, rate
):
    square_local, mlp_local, gain_local = from_wire(grads)
    square_grad, mlp_grad, gain_grad = (
        lax.psum_scatter(square_local, "dp", scatter_dimension=1, tiled=True),
        lax.psum_scatter(mlp_local, "dp", scatter_dimension=1, tiled=True),
        lax.psum_scatter(gain_local, "dp", scatter_dimension=1, tiled=True),
    )
    square_moment_new = 0.5 * square_moment + square_grad
    mlp_moment_new = 0.5 * mlp_moment + mlp_grad
    gain_moment_new = 0.5 * gain_moment + gain_grad
    device = lax.axis_index("dp")
    count = lax.axis_size("dp")
    square_owners = [index * count // 7 for index in range(5)]
    mlp_owners = [(index + 5) * count // 7 for index in range(2)]
    square_full, mlp_full = (
        lax.all_gather(square_moment_new, "dp", axis=1, tiled=True),
        lax.all_gather(mlp_moment_new, "dp", axis=1, tiled=True),
    )
    mine_square = pick_owned(square_full, square_owners, device)
    mine_mlp = pick_owned(mlp_full, mlp_owners, device)
    made_square = lax.cond(
        is_owner(square_owners, device), plain_orthogonalize, jnp.zeros_like, mine_square
    )
    made_mlp = lax.cond(is_owner(mlp_owners, device), plain_orthogonalize, jnp.zeros_like, mine_mlp)
    stack_square = jnp.stack(
        [jnp.where(device == owner, made_square, 0.0) for owner in square_owners]
    )
    stack_mlp = jnp.stack([jnp.where(device == owner, made_mlp, 0.0) for owner in mlp_owners])
    square_ortho, mlp_ortho = (
        lax.psum_scatter(stack_square, "dp", scatter_dimension=1, tiled=True),
        lax.psum_scatter(stack_mlp, "dp", scatter_dimension=1, tiled=True),
    )
    square_new = square_weights - jnp.array(SQ_RATES, F32)[:, None, None] * square_ortho
    mlp_new = mlp_weights - jnp.array(MLP_RATES, F32)[:, None, None] * mlp_ortho
    gains_new = gains - rate * gain_moment_new
    return (
        square_grad,
        square_moment_new,
        square_new,
        square_new.astype(BF16),
        mlp_grad,
        mlp_moment_new,
        mlp_new,
        mlp_new.astype(BF16),
        gain_grad,
        gain_moment_new,
        gains_new,
    )


def per_device(
    actions,
    observed,
    camera_flags,
    noise_levels,
    cotangent,
    square_weights,
    mlp_weights,
    gains,
    square_moment,
    mlp_moment,
    gain_moment,
):
    count = lax.axis_size("dp")
    rate = 0.1 / math.sqrt(actions.shape[0] * count)
    by_key = observed.transpose(1, 0, 2)
    ins = (actions, by_key, camera_flags, noise_levels, cotangent)
    if count == math.prod(GRID):
        made = block_and_back(True, *ins, square_weights, mlp_weights, gains, square_moment, mlp_moment)
        done = finish(rate, made, square_weights, mlp_weights, gains, gain_moment)
        output, actions_grad = done.output_f, done.ag_f
        d = done
        rest = (d.sqg, d.sqm, d.sqn, d.sqc, d.mlpg, d.mlpm, d.mlpn, d.mlpc, d.gg, d.gm, d.gn)
    else:
        square_all, mlp_all = (
            lax.all_gather(square_weights.astype(BF16), "dp", axis=1, tiled=True),
            lax.all_gather(mlp_weights.astype(BF16), "dp", axis=1, tiled=True),
        )
        gain_all = lax.all_gather(gains, "dp", axis=1, tiled=True)
        made = block_and_back(False, *ins, square_all, mlp_all, gain_all)
        done = finish(rate, made)
        output, actions_grad = made.output, made.ag
        grads = made.grads.reshape(-1, WIRE, LANES)
        rest = update_by_collectives(
            grads, square_weights, mlp_weights, gains, square_moment, mlp_moment, gain_moment, rate
        )
    observed_grad = done.og.transpose(1, 0, 2)
    return (output, actions_grad, observed_grad) + tuple(rest)


def solution(mesh):
    rows, cube, flat = P("dp", None), P("dp", None, None), P("dp")
    stacked, pair = P(None, "dp", None), P(None, "dp")
    return jax.shard_map(
        per_device,
        mesh=mesh,
        in_specs=(rows, cube, flat, flat, rows, stacked, stacked, pair, stacked, stacked, pair),
        out_specs=(rows, rows, cube) + (stacked,) * 8 + (pair,) * 3,
        check_vma=False,
    )
```

```python
import functools
import math

import jax
import jax.numpy as jnp
from jax import lax
from jax.experimental import pallas as pl
from jax.experimental.pallas import tpu as pltpu
from jax.sharding import PartitionSpec as P

HEADS = 4
ACT = 16
OBS_FULL = 196
OBS_FEW = 49
COEF_A = 3.4445
COEF_B = -4.775
COEF_C = 2.0315
F32 = jnp.float32
BF16 = jnp.bfloat16
MESH = pl.DeviceIdType.MESH
VMEM = pltpu.VMEM
NN = (((1,), (0,)), ((), ()))
NT = (((1,), (1,)), ((), ()))
TN = (((0,), (0,)), ((), ()))

LANES = 128
TILE = 8
MLP_ROWS = 64
SQ_ROWS = 16
SQ_AT = (160, 192, 176, 128, 144)
GAIN_BASE = 208
WIRE = 224
PIECES = ((0, 64), (64, 64), (128, 32), (160, 32), (192, 32))
PIECE_X_FIRST = (True, False, True, True, False)
CHUNKS = ((0, 64), (64, 64), (128, 32), (160, 32), (192, 16), (208, 16))
X_FIRST = (True, False, True, False, True, False)
COMPLETES = ((0,), (1,), (5, 6), (2, 4), (3,), ())
MLP_RATES = (1.0, 0.5)
SQ_RATES = (0.5, 0.5, 0.5, 0.5, 4.0)
GRID = (4, 2, 2, 2)
OWNERS = (8, 22, 14, 16, 11, 21, 13)
SHIFTS = (0.0, 0.0, 0.4, 0.8, 0.8)
KEYS_PAD = 208
GROUP = 16
ROWS = 512


class Refs:
    def __init__(self, pairs):
        self.__dict__.update(pairs)


def dot(left, right, dims=NN):
    return lax.dot_general(left, right, dims, preferred_element_type=F32)


def place():
    me = lax.axis_index("dp")
    return me, me // 8, (me // 4) % 2, (me // 2) % 2, me % 2


def device_at(z, y, x, c):
    return ((z * 2 + y) * 2 + x) * 2 + c


def link(src, dst, send, recv, device):
    return pltpu.make_async_remote_copy(
        src_ref=src,
        dst_ref=dst,
        send_sem=send,
        recv_sem=recv,
        device_id=(device,),
        device_id_type=MESH,
    )


def greet(device):
    pl.semaphore_signal(
        pltpu.get_barrier_semaphore(), inc=1, device_id=(device,), device_id_type=MESH
    )


def normalize(values):
    centred = values - jnp.mean(values, -1, keepdims=True)
    scale = lax.rsqrt(jnp.mean(centred * centred, -1, keepdims=True) + 1e-05)
    return centred * scale, scale


def norm_back(grad, hat, scale):
    mean_one = jnp.mean(grad, -1, keepdims=True)
    mean_two = jnp.mean(grad * hat, -1, keepdims=True)
    return scale * (grad - mean_one - hat * mean_two)


class Gather:
    def __init__(self, r):
        self.r = r
        self.me, self.z, self.y, self.x, self.c = place()

    def hop(self, k, step, part, device):
        return link(part, part, self.r.gsend.at[k, step], self.r.grecv.at[k, step], device)

    def along_z(self, k, step):
        part = self.r.wire.at[self.z, self.y, self.x, self.c, pl.ds(*PIECES[k])]
        return self.hop(k, step, part, device_at((self.z + step + 1) % 4, self.y, self.x, self.c))

    def from_z(self, k, step):
        there = (self.z + 3 - step) % 4
        part = self.r.wire.at[there, self.y, self.x, self.c, pl.ds(*PIECES[k])]
        return self.hop(k, step, part, device_at(there, self.y, self.x, self.c))

    def plane(self, k, second, mine):
        z, y, x, c = self.z, self.y, self.x, self.c
        rows, wire = pl.ds(*PIECES[k]), self.r.wire
        py, px = (y, x) if mine else (1 - y, 1 - x)
        along_x = PIECE_X_FIRST[k] == second
        if along_x:
            part = wire.at[:, y, px, c, rows] if second else wire.at[:, :, px, c, rows]
            return self.hop(k, 3 if second else 4, part, device_at(z, y, 1 - x, c))
        part = wire.at[:, py, x, c, rows] if second else wire.at[:, py, :, c, rows]
        return self.hop(k, 3 if second else 4, part, device_at(z, 1 - y, x, c))

    def core(self, k, mine):
        part = self.r.wire.at[:, :, :, self.c if mine else 1 - self.c, pl.ds(*PIECES[k])]
        return self.hop(k, 5, part, device_at(self.z, self.y, self.x, 1 - self.c))

    def first(self, *chunks):
        for k in chunks:
            for step in range(3):
                self.along_z(k, step).start()

    def second(self, *chunks):
        for k in chunks:
            for step in range(3):
                self.from_z(k, step).wait_recv()
            self.plane(k, True, True).start()

    def third(self, *chunks):
        for k in chunks:
            self.plane(k, True, False).wait_recv()
            self.plane(k, False, True).start()

    def fourth(self, *chunks):
        for k in chunks:
            self.plane(k, False, False).wait_recv()
            self.core(k, True).start()

    def last(self, *chunks):
        for k in chunks:
            self.core(k, False).wait_recv()

    def drain(self):
        for k in range(len(PIECES)):
            for step in range(3):
                self.along_z(k, step).wait_send()
            self.plane(k, True, True).wait_send()
            self.plane(k, False, True).wait_send()
            self.core(k, True).wait_send()

    def fill(self):
        r = self.r
        spot = (self.z, self.y, self.x, self.c)

        def tiles(source, m, base, number):
            for j in range(number):
                pair = [source[m, :, pl.ds((2 * j + k) * LANES, LANES)] for k in range(2)]
                r.wire[spot + (pl.ds(base + j * 16, 16),)] = jnp.concatenate(pair, axis=0).astype(BF16)

        for m in range(5):
            tiles(r.sqw_v, m, SQ_AT[m], 1)
        for m in range(2):
            tiles(r.mlpw_v, m, m * MLP_ROWS, 4)
        gains, edge = r.gain_v[...], r.edge
        high = gains.astype(BF16).astype(F32)
        middle = (gains - high).astype(BF16).astype(F32)
        edge[...] = jnp.zeros_like(edge)
        edge[0:2, 0:TILE] = high
        edge[2:4, 0:TILE] = middle
        edge[4:6, 0:TILE] = (gains - high - middle).astype(BF16).astype(F32)
        r.wire[spot + (pl.ds(GAIN_BASE, 16),)] = edge[...].astype(BF16)

    def unpack(self, base, number, out, m):
        for j in range(number):
            block = self.r.wire[:, :, :, :, pl.ds(base + j * 16, 16), :].reshape(32, 16, LANES).astype(F32)
            for half in range(2):
                columns = pl.ds((2 * j + half) * LANES, LANES)
                out[m, :, columns] = block[:, half * 8 : half * 8 + 8, :].reshape(256, LANES).astype(BF16)

    def unpack_gains(self):
        edge, wire = self.r.edge, self.r.wire
        for half in range(2):
            total = jnp.zeros((16, LANES), F32)
            for at in range(16):
                d = half * 16 + at
                tile = wire[d // 8, (d // 4) % 2, (d // 2) % 2, d % 2, pl.ds(GAIN_BASE, 16), :].astype(F32)
                total = total + (tile if at == 0 else pltpu.roll(tile, at * TILE, 1))
            edge[...] = total
            self.r.gain_all[:, pl.ds(half * LANES, LANES)] = edge[0:2, :] + edge[2:4, :] + edge[4:6, :]


class Update:
    def __init__(self, r):
        self.r = r
        self.me, self.z, self.y, self.x, self.c = place()

    def hop(self, k, step, src, dst, device):
        return link(src, dst, self.r.send.at[k, step], self.r.recv.at[k, step], device)

    def core(self, k):
        rows = pl.ds(*CHUNKS[k])
        src, dst = self.r.send0.at[:, :, :, rows], self.r.got_core.at[:, :, :, rows]
        return self.hop(k, 0, src, dst, device_at(self.z, self.y, self.x, 1 - self.c))

    def plane(self, k, first):
        rows = pl.ds(*CHUNKS[k])
        to = (self.z, self.y, 1 - self.x, self.c) if X_FIRST[k] == first else (self.z, 1 - self.y, self.x, self.c)
        if first:
            src, dst = self.r.send1.at[:, :, rows], self.r.got1.at[:, :, rows]
        else:
            src, dst = self.r.send2.at[:, rows], self.r.got2.at[:, rows]
        return self.hop(k, 1 if first else 2, src, dst, device_at(*to))

    def along_z(self, k, step):
        rows = pl.ds(*CHUNKS[k])
        to = device_at((self.z + step + 1) % 4, self.y, self.x, self.c)
        return self.hop(k, 3 + step, self.r.send3.at[step, rows], self.r.got3.at[step, rows], to)

    def start(self, k):
        rows = pl.ds(*CHUNKS[k])
        self.r.send0[:, :, :, rows, :] = self.r.grads[:, :, :, 1 - self.c, rows, :].astype(BF16)
        self.core(k).start()

    def one(self, *chunks):
        r = self.r
        for k in chunks:
            rows = pl.ds(*CHUNKS[k])
            self.core(k).wait_recv()
            sum1 = r.sum1
            sum1[:, :, :, rows, :] = r.grads[:, :, :, self.c, rows, :] + r.got_core[:, :, :, rows, :].astype(F32)
            other = sum1[:, :, 1 - self.x, rows, :] if X_FIRST[k] else sum1[:, 1 - self.y, :, rows, :]
            r.send1[:, :, rows, :] = other.astype(BF16)
            self.plane(k, True).start()

    def two(self, *chunks):
        r = self.r
        for k in chunks:
            rows = pl.ds(*CHUNKS[k])
            self.plane(k, True).wait_recv()
            sum1, sum2 = r.sum1, r.sum2
            mine = sum1[:, :, self.x, rows, :] if X_FIRST[k] else sum1[:, self.y, :, rows, :]
            sum2[:, :, rows, :] = mine + r.got1[:, :, rows, :].astype(F32)
            other = 1 - self.y if X_FIRST[k] else 1 - self.x
            r.send2[:, rows, :] = sum2[:, other, rows, :].astype(BF16)
            self.plane(k, False).start()

    def three(self, *chunks):
        r = self.r
        for k in chunks:
            rows = pl.ds(*CHUNKS[k])
            self.plane(k, False).wait_recv()
            mine = self.y if X_FIRST[k] else self.x
            r.sum3[:, rows, :] = r.sum2[:, mine, rows, :] + r.got2[:, rows, :].astype(F32)
            for step in range(3):
                r.send3[step, rows, :] = r.sum3[(self.z + step + 1) % 4, rows, :].astype(BF16)
                self.along_z(k, step).start()

    def slab(self, index):
        if index < 2:
            return pl.ds(index * MLP_ROWS, MLP_ROWS), self.r.slabs_mlp, self.r.result_mlp
        return pl.ds(SQ_AT[index - 2], SQ_ROWS), self.r.slabs_sq, self.r.result_sq

    def to_owner(self, index):
        rows, slabs, _ = self.slab(index)
        moment = self.r.moment_low if index < 2 else self.r.moment
        return link(
            moment.at[rows], slabs.at[self.me],
            self.r.own_send.at[index], self.r.own_recv.at[0], OWNERS[index],
        )

    def four(self, *chunks):
        r = self.r
        moment, out = r.moment, r.out
        for k in chunks:
            rows = pl.ds(*CHUNKS[k])
            total = r.sum3[self.z, rows, :]
            for step in range(3):
                self.along_z(k, step).wait_recv()
                total = total + r.got3[step, rows, :].astype(F32)
            out[0, rows, :] = total
            new = 0.5 * moment[rows, :] + total
            moment[rows, :] = new
            if k < 2:
                r.moment_low[rows, :] = new.astype(BF16)
            for index in COMPLETES[k]:
                rows_m, slabs, _ = self.slab(index)

                @pl.when(self.me != OWNERS[index])
                def _():
                    self.to_owner(index).start()

                @pl.when(self.me == OWNERS[index])
                def _():
                    mine = r.moment_low if index < 2 else moment
                    pltpu.make_async_copy(mine.at[rows_m], slabs.at[self.me], r.own_recv.at[0]).start()

    def old_moment(self):
        r = self.r
        moment = r.moment
        for m in range(2):
            for j in range(8):
                moment[pl.ds(m * MLP_ROWS + j * TILE, TILE), :] = r.mlpm_v[m, :, pl.ds(j * LANES, LANES)]
        for m in range(5):
            for j in range(2):
                moment[pl.ds(SQ_AT[m] + j * TILE, TILE), :] = r.sqm_v[m, :, pl.ds(j * LANES, LANES)]
        moment[pl.ds(GAIN_BASE, 16), :] = jnp.zeros((16, LANES), F32)

    def orthogonalize(self):
        r = self.r
        cur = r.cur
        rows = lax.broadcasted_iota(jnp.int32, (256, 256), 0)
        diagonal = rows == lax.broadcasted_iota(jnp.int32, (256, 256), 1)

        def run(slabs, result, tiles):
            pltpu.make_async_copy(slabs, slabs, r.own_recv.at[0]).wait()
            low = r.cur_low
            for j in range(tiles // 2):
                pair = slabs[:, pl.ds(j * 16, 16), :].astype(F32)
                for side in range(2):
                    columns = pl.ds((2 * j + side) * LANES, LANES)
                    part = pair[:, side * TILE : (side + 1) * TILE, :].reshape(256, LANES)
                    cur[:, columns] = part
                    low[:, columns] = part.astype(BF16)
            scale = 1.0
            for turn, shift in enumerate(SHIFTS):
                whole = low[:, 0 : tiles * LANES]
                off = dot(whole, whole, NT)
                if turn == 0:
                    norm = jnp.sum(jnp.sum(jnp.where(diagonal, off, 0.0), axis=0, keepdims=True), axis=1, keepdims=True)
                    scale = 1.0 / (jnp.sqrt(norm) + 1e-07)
                    off = off * (scale * scale)
                if shift:
                    off = off - jnp.where(diagonal, shift, 0.0)
                off_low = off.astype(BF16)
                poly = (COEF_B + 2.0 * COEF_C * shift) * off + COEF_C * dot(off_low, off_low)
                poly = poly.astype(BF16)
                keep = COEF_A + shift * (COEF_B + COEF_C * shift)
                for j in range(tiles // 2):
                    columns = pl.ds(j * 2 * LANES, 2 * LANES)
                    now = keep * cur[:, columns] + dot(poly, low[:, columns])
                    if turn == 0:
                        now = now * scale
                    if turn < len(SHIFTS) - 1:
                        cur[:, columns] = now
                        low[:, columns] = now.astype(BF16)
                    else:
                        parts = [now[:, side * LANES : (side + 1) * LANES].reshape(32, TILE, LANES) for side in range(2)]
                        result[:, pl.ds(j * 16, 16), :] = jnp.concatenate(parts, axis=1).astype(result.dtype)

        mine_mlp = jnp.logical_or(self.me == OWNERS[0], self.me == OWNERS[1])
        mine_sq = self.me < 0
        for device in OWNERS[2:]:
            mine_sq = jnp.logical_or(mine_sq, self.me == device)

        @pl.when(mine_mlp)
        def _():
            run(r.slabs_mlp, r.result_mlp, 8)

        @pl.when(mine_sq)
        def _():
            run(r.slabs_sq, r.result_sq, 2)

    def landing(self, index):
        if index < 2:
            return self.r.back_mlp.at[index]
        return self.r.out.at[2, pl.ds(SQ_AT[index - 2], SQ_ROWS)]

    def give_back(self, index, device):
        _, _, result = self.slab(index)
        return link(
            result.at[device], self.landing(index),
            self.r.back_send.at[device], self.r.back_recv.at[index], device,
        )

    def give_all(self):
        r = self.r
        for index in range(7):
            _, _, result = self.slab(index)

            @pl.when(self.me == OWNERS[index])
            def _():
                def send_one(step, _):
                    self.give_back(index, (self.me + step) % 32).start()
                    return 0

                lax.fori_loop(1, 32, send_one, 0)
                pltpu.make_async_copy(result.at[self.me], self.landing(index), r.back_recv.at[index]).start()

    def take_all(self):
        for index in range(7):
            _, _, result = self.slab(index)
            pltpu.make_async_copy(result.at[0], self.landing(index), self.r.back_recv.at[index]).wait()
        for index in range(2):
            rows = pl.ds(index * MLP_ROWS, MLP_ROWS)
            self.r.out[2, rows, :] = self.r.back_mlp[index].astype(F32)

    def drain(self):
        for k in range(len(CHUNKS)):
            self.core(k).wait_send()
            self.plane(k, True).wait_send()
            self.plane(k, False).wait_send()
            for step in range(3):
                self.along_z(k, step).wait_send()
        for index in range(7):

            @pl.when(self.me != OWNERS[index])
            def _():
                self.to_owner(index).wait_send()

    def drain_owner(self):
        for index in range(7):

            @pl.when(self.me == OWNERS[index])
            def _():
                def wait_one(step, _):
                    self.give_back(index, (self.me + step) % 32).wait_send()
                    return 0

                lax.fori_loop(1, 32, wait_one, 0)


def greet_all():
    me, z, y, x, c = place()
    greet(device_at(z, y, x, 1 - c))
    greet(device_at(z, y, 1 - x, c))
    greet(device_at(z, 1 - y, x, c))
    for step in range(1, 4):
        greet(device_at((z + step) % 4, y, x, c))
    owner = me < 0
    for device in OWNERS:
        owner = jnp.logical_or(owner, me == device)

        @pl.when(me != device)
        def _():
            greet(device)

    @pl.when(owner)
    def _():
        def greet_other(step, _):
            greet((me + step) % 32)
            return 0

        lax.fori_loop(1, 32, greet_other, 0)

    is_owner = owner.astype(jnp.int32)
    return 6 + 7 - is_owner + 31 * is_owner


def block_kernel(names, remote, *args):
    r = Refs(zip(names, args))
    keys, samples = r.obs.shape[0], r.obs.shape[1]
    tokens, width = r.acts.shape
    head_dim, half, per = width // HEADS, width // 2, ROWS // ACT
    wide = r.mlp_all.shape[2]
    groups = samples // GROUP
    in_sems, out_sems = r.in_sems, r.out_sems

    if remote:
        own = (r.sqw_v, r.mlpw_v, r.gain_v)
    else:
        own = (r.sq_all, r.mlp_all, r.gain_all)
    loads = list(zip((r.sqw, r.mlpw, r.gain), own))
    loads += [(r.acts, r.acts_v), (r.obs, r.obs_v.at[pl.ds(0, keys)]), (r.cot, r.cot_v)]
    if remote:
        loads += [(r.sqm, r.sqm_v), (r.mlpm, r.mlpm_v)]
    loads += [(r.flags, r.flags_s), (r.levels, r.levels_s)]
    copies = [pltpu.make_async_copy(a, b, in_sems.at[i]) for i, (a, b) in enumerate(loads)]

    def arrive(*which):
        for i in which:
            copies[i].wait()

    for copy in copies:
        copy.start()
    if remote:
        gather, update = Gather(r), Update(r)
        expected = greet_all()
        arrive(0, 1, 2)
        gather.fill()
        pl.semaphore_wait(pltpu.get_barrier_semaphore(), expected)
        gather.first(3, 4)

    arrive(3)

    def hats(i, _):
        rows = pl.ds(pl.multiple_of(i * ROWS, ROWS), ROWS)
        hat, scale = normalize(r.acts_v[rows, :])
        r.xhat[rows, :] = hat
        r.rstd[rows, :] = scale
        return 0

    lax.fori_loop(0, tokens // ROWS, hats, 0)

    mem, obs_v = r.mem, r.obs_v
    batch = 16
    chunks = KEYS_PAD // batch
    swap = r.swap
    row = lax.broadcasted_iota(jnp.int32, swap.shape, 0)
    column = lax.broadcasted_iota(jnp.int32, swap.shape, 1)
    swap[...] = jnp.where(column == (row % batch) * batch + row // batch, 1.0, 0.0).astype(BF16)

    def turn(part, low, high):
        def one(j, _):
            at = pl.ds(pl.multiple_of(j * batch, batch), batch)
            here = pl.ds(part * batch, batch)
            block = obs_v[at, here, :].reshape(batch * batch, width)
            mem[here, at, :] = dot(swap[...], block).astype(BF16).reshape(batch, batch, width)
            return 0

        lax.fori_loop(low, high, one, 0, unroll=high - low)

    whole = chunks - 1
    arrive(4)
    turn(0, 0, whole // 2)
    if remote:
        gather.second(3, 4)
        gather.first(2, 0, 1)
    turn(0, whole // 2, whole)
    if remote:
        gather.third(3, 4)
    turn(1, 0, whole // 2)
    if remote:
        gather.second(2, 0, 1)
        gather.fourth(3, 4)
    turn(1, whole // 2, whole)
    arrive(len(copies) - 1, len(copies) - 2)
    freqs = jnp.exp(
        lax.broadcasted_iota(jnp.int32, (1, half), 1).astype(F32) * F32(-math.log(10000.0)) / half
    )
    for s in range(samples):
        r.angle[s : s + 1, :] = r.levels_s[s].astype(F32) * freqs
    r.embed[:, 0:half] = jnp.sin(r.angle[...]).astype(BF16)
    r.embed[:, half:width] = jnp.cos(r.angle[...]).astype(BF16)
    if remote:
        arrive(6, 7)
        update.old_moment()
        gather.third(2, 0, 1)
        gather.last(3, 4)
        for m in range(3):
            gather.unpack(SQ_AT[m], 1, r.sq_all, m)
        gather.unpack_gains()
    else:
        arrive(0, 1, 2)

    sq, mlp = r.sq_all, r.mlp_all
    wkh, wvh = r.wkh, r.wvh
    lane = lax.broadcasted_iota(jnp.int32, (width, width), 1)

    def split_heads(out, weight):
        weight = weight.astype(F32)
        for h in range(HEADS):
            out[pl.ds(h * width, width), :] = jnp.where(lane // head_dim == h, weight, 0.0).astype(BF16)

    split_heads(wkh, sq[2])
    g1, g2 = r.gain_all[0:1, :], r.gain_all[1:2, :]

    obs_v[keys] = dot(r.embed[...], sq[0]).astype(BF16)
    obs_v[keys + 1 :] = jnp.zeros((KEYS_PAD - keys - 1, samples, width), BF16)
    for part in range(samples // batch):
        turn(part, whole, chunks)

    queries, dmixes = r.queries, r.dmixes

    def make_queries(i, _):
        rows = pl.ds(pl.multiple_of(i * ROWS, ROWS), ROWS)
        first = (r.xhat[rows, :] * g1).astype(BF16)
        r.first[rows, :] = first
        q = dot(first, sq[1]).astype(BF16)
        r.query[rows, :] = q
        here = pl.ds(i * per, per)
        for h in range(HEADS):
            wk = wkh[pl.ds(h * width, width), :]
            value = (dot(q, wk, NT) * 0.125).astype(BF16).reshape(per, ACT, width)
            queries[here, pl.ds(h * ACT, ACT), :] = value
        return 0

    lax.fori_loop(0, tokens // ROWS, make_queries, 0)

    key = lax.broadcasted_iota(jnp.int32, (KEYS_PAD, LANES), 0)
    rows_each = HEADS * ACT
    left = lax.broadcasted_iota(jnp.int32, (KEYS_PAD, LANES), 1) < rows_each
    left_row = lax.broadcasted_iota(jnp.int32, (1, LANES), 1) < rows_each
    rest = jnp.where((key >= OBS_FEW) & (key < OBS_FULL), 1.0, 0.0)
    padding = jnp.where(key > OBS_FULL, -1000000000.0, 0.0)

    def with_memory(s, sides):
        here = pl.ds(s, 4)
        wide = dot(mem[here].reshape(4 * KEYS_PAD, width), sides[here].reshape(4 * rows_each, width), NT)
        part = [wide[k * KEYS_PAD : (k + 1) * KEYS_PAD, (k // 2) * LANES : (k // 2 + 1) * LANES] for k in range(4)]
        return jnp.where(left, part[0], part[1]), jnp.where(left, part[2], part[3])

    def each_head(out, s, value):
        rows = pl.ds(pl.multiple_of(s * ACT, ACT), ACT)
        for h in range(HEADS):
            out[rows, pl.ds(h * width, width)] = value[h * ACT : (h + 1) * ACT, :]

    def attend(g, _):
        pairs = []
        for quad in range(GROUP // 4):
            pairs.extend(with_memory(g * GROUP + 4 * quad, queries))
        turned = []
        for k, score in enumerate(pairs):
            s = g * GROUP + 2 * k
            drop = [(1 - r.flags_s[s + side]).astype(F32) * -1000000000.0 for side in range(2)]
            score = score + (rest * jnp.where(left_row, drop[0], drop[1]) + padding)
            expo = jnp.exp(score - jnp.max(score, 0, keepdims=True))
            probs = expo * (1.0 / jnp.sum(expo, 0, keepdims=True))
            r.probs[g * (GROUP // 2) + k] = probs
            turned.append(probs.astype(BF16).T)
        for k, low in enumerate(turned):
            for side in range(2):
                s = g * GROUP + 2 * k + side
                each_head(r.u, s, dot(low[side * rows_each : (side + 1) * rows_each], mem[s]).astype(BF16))
        return 0

    lax.fori_loop(0, groups // 2, attend, 0)
    if remote:
        gather.fourth(2, 0, 1)
    lax.fori_loop(groups // 2, groups, attend, 0)
    if remote:
        gather.last(2, 0, 1)
        for m in range(3, 5):
            gather.unpack(SQ_AT[m], 1, sq, m)
        for m in range(2):
            gather.unpack(m * MLP_ROWS, 4, mlp, m)
    split_heads(wvh, sq[3])

    gain_acc = r.gain_acc
    gain_acc[...] = jnp.zeros_like(gain_acc)
    arrive(5)

    def feed(i, _):
        rows = pl.ds(pl.multiple_of(i * ROWS, ROWS), ROWS)
        mixed = dot(r.u[rows, :], wvh[...]).astype(BF16)
        r.mixed[rows, :] = mixed
        resid = r.acts_v[rows, :] + dot(mixed, sq[4])
        hat, scale = normalize(resid)
        second = (hat * g2).astype(BF16)
        r.second[rows, :] = second
        cot = r.cot_v[rows, :]
        out_low = cot.astype(BF16)
        r.out_low[rows, :] = out_low
        for c in range(wide // 256):
            columns = pl.ds(c * 256, 256)
            v = dot(second, mlp[0, :, columns])
            square = v * v
            t = jnp.tanh(0.7978845608 * (v + 0.044715 * square * v))
            r.active[rows, columns] = (0.5 * v * (1.0 + t)).astype(BF16)
            slope = 0.5 * (1.0 + t) + 0.5 * v * (1.0 - t * t) * (0.7978845608 * (1.0 + 0.134145 * square))
            r.dhidden[rows, columns] = (slope * dot(out_low, mlp[1, :, columns])).astype(BF16)
        r.out_v[rows, :] = resid + dot(r.active[rows, :], mlp[1], NT)
        grad_second = dot(r.dhidden[rows, :], mlp[0], NT)
        gain_acc[1:2, :] += jnp.sum(grad_second * hat, 0, keepdims=True)
        dres = cot + norm_back(grad_second * g2, hat, scale)
        r.dres[rows, :] = dres
        low = dres.astype(BF16)
        r.dres_low[rows, :] = low
        gm = dot(low, sq[4], NT).astype(BF16)
        r.dmixed[rows, :] = gm
        here = pl.ds(i * per, per)
        for h in range(HEADS):
            wv = wvh[pl.ds(h * width, width), :]
            dmixes[here, pl.ds(h * ACT, ACT), :] = dot(gm, wv, NT).astype(BF16).reshape(per, ACT, width)
        return 0

    lax.fori_loop(0, tokens // ROWS, feed, 0)
    keep_out = pltpu.make_async_copy(r.out_v, r.output, out_sems.at[0])
    keep_out.start()

    grads = r.grads

    def put(base, tiles, value):
        for j in range(tiles):
            part = value[:, j * LANES : (j + 1) * LANES].reshape(GRID + (TILE, LANES))
            grads[:, :, :, :, pl.ds(base + j * TILE, TILE), :] = part

    def by_head(left, right):
        turned = left.T
        parts = [
            dot(turned[h * head_dim : (h + 1) * head_dim, :], right[:, pl.ds(h * width, width)])
            for h in range(HEADS)
        ]
        return jnp.concatenate(parts, axis=0).T

    put(0, 8, dot(r.second[...], r.dhidden[...], TN))
    if remote:
        update.start(0)
    put(MLP_ROWS, 8, dot(r.out_low[...], r.active[...], TN))
    if remote:
        update.start(1)
    put(SQ_AT[4], 2, dot(r.mixed[...], r.dres_low[...], TN))
    put(SQ_AT[3], 2, by_head(r.dmixed[...], r.u))
    if remote:
        update.start(2)

    left_low = jnp.where(left_row, 1.0, 0.0).astype(BF16)
    right_low = jnp.where(left_row, 0.0, 1.0).astype(BF16)

    def attend_back(g, _):
        pairs = []
        for quad in range(GROUP // 4):
            pairs.extend(with_memory(g * GROUP + 4 * quad, dmixes))
        lows = []
        for k, rise in enumerate(pairs):
            probs = r.probs[g * (GROUP // 2) + k]
            both = probs * rise
            dscore = (both - probs * jnp.sum(both, 0, keepdims=True)).astype(BF16)
            lows.append((probs.astype(BF16), dscore, dscore.T))
        for k, (low, dscore, turned) in enumerate(lows):
            s = g * GROUP + 2 * k
            for side in range(2):
                dq = dot(turned[side * rows_each : (side + 1) * rows_each], mem[s + side]) * 0.125
                each_head(r.dq_wide, s + side, dq.astype(BF16))
            here = pl.ds(s, 2)
            sides = jnp.concatenate(
                [x[here].reshape(2 * rows_each, width) for x in (dmixes, queries)], axis=0
            )
            own = [jnp.concatenate([low * keep, dscore * keep], axis=1) for keep in (left_low, right_low)]
            dmem = dot(jnp.concatenate(own, axis=0), sides)
            for side in range(2):
                rows = dmem[side * KEYS_PAD : (side + 1) * KEYS_PAD, :]
                mem[s + side] = rows.astype(BF16)
                r.stamps[s + side] = rows[192:200, :]
        return 0

    half_groups = groups // 2
    lax.fori_loop(0, half_groups, attend_back, 0)
    if remote:
        update.one(0)
    lax.fori_loop(half_groups, groups, attend_back, 0)
    put(SQ_AT[2], 2, by_head(r.query[...], r.dq_wide))
    stamp_low = r.stamps[:, 4:5, :].reshape(samples, width).astype(BF16)
    put(SQ_AT[0], 2, dot(r.embed[...], stamp_low, TN))
    if remote:
        update.start(3)
        update.one(1, 2)

    def turn_back(part):
        def one(j):
            at = pl.ds(pl.multiple_of(j * batch, batch), batch)
            here = pl.ds(part * batch, batch)
            block = mem[here, at, :].reshape(batch * batch, width)
            value = dot(swap[...], block).astype(BF16).reshape(batch, batch, width)
            number = min(batch, keys - j * batch)
            r.og[pl.ds(j * batch, number), here, :] = value[0:number]

        for j in range(chunks):
            one(j)

    def queries_back(i, _):
        rows = pl.ds(pl.multiple_of(i * ROWS, ROWS), ROWS)
        r.dquery[rows, :] = dot(r.dq_wide[rows, :], wkh[...]).astype(BF16)
        return 0

    lax.fori_loop(0, tokens // ROWS, queries_back, 0)
    put(SQ_AT[1], 2, dot(r.first[...], r.dquery[...], TN))
    if remote:
        update.start(4)

    def acts_back(i, _):
        rows = pl.ds(pl.multiple_of(i * ROWS, ROWS), ROWS)
        grad_first = dot(r.dquery[rows, :], sq[1], NT)
        hat = r.xhat[rows, :]
        gain_acc[0:1, :] += jnp.sum(grad_first * hat, 0, keepdims=True)
        r.ag_v[rows, :] = r.dres[rows, :] + norm_back(grad_first * g1, hat, r.rstd[rows, :])
        return 0

    def finish_acts():
        lax.fori_loop(0, tokens // ROWS, acts_back, 0)
        for norm in range(2):
            for j in range(2):
                row = gain_acc[norm : norm + 1, j * LANES : (j + 1) * LANES]
                at = GAIN_BASE + norm * 2 + j
                value = jnp.broadcast_to(row.reshape(1, 1, 1, 1, 1, LANES), GRID + (1, LANES))
                grads[:, :, :, :, at : at + 1, :] = value
        rest = WIRE - GAIN_BASE - 4
        grads[:, :, :, :, GAIN_BASE + 4 : WIRE, :] = jnp.zeros(GRID + (rest, LANES), F32)

    keep_ag = pltpu.make_async_copy(r.ag_v, r.ag, out_sems.at[1])
    if remote:
        update.two(0)
        update.one(3)
        finish_acts()
        keep_ag.start()
        update.start(5)
        update.two(1, 2)
        update.one(4)
        update.two(3)
        update.one(5)
        update.three(0, 1)
        turn_back(0)
        update.two(4)
        update.three(2, 3, 4)
        update.two(5)
        update.four(0, 1)
        update.four(2, 3, 4)
        update.three(5)
        update.orthogonalize()
        update.give_all()
        turn_back(1)
        update.four(5)
        out = r.out
        out[1, :, :] = r.moment[...]
        out[2, pl.ds(GAIN_BASE, 16), :] = jnp.zeros((16, LANES), F32)
        gather.drain()
        update.drain()
        update.take_all()
        update.drain_owner()
    else:
        finish_acts()
        keep_ag.start()
        for part in range(samples // batch):
            turn_back(part)
    for copy in (keep_out, keep_ag):
        copy.wait()


def block_and_back(remote, acts, obs, flags, levels, cot, sqw, mlpw, gain, sqm=None, mlpm=None):
    tokens, width = acts.shape
    keys, samples = obs.shape[0], obs.shape[1]
    rows = HEADS * ACT
    wide = mlpw.shape[2]
    any_space = pl.BlockSpec(memory_space=pl.ANY)
    in_vmem = pl.BlockSpec(memory_space=VMEM)
    sem = pltpu.SemaphoreType.DMA
    ins = dict(flags=flags, levels=levels, acts=acts, obs=obs, cot=cot, sqw=sqw, mlpw=mlpw, gain=gain)
    outs = dict(
        output=jax.ShapeDtypeStruct(acts.shape, F32),
        ag=jax.ShapeDtypeStruct(acts.shape, F32),
        og=jax.ShapeDtypeStruct(obs.shape, BF16),
    )
    grads = GRID + (WIRE, LANES)
    scratch = dict(
        obs_v=VMEM((KEYS_PAD, samples, width), BF16),
        acts_v=VMEM(acts.shape, F32),
        cot_v=VMEM(acts.shape, F32),
        mem=VMEM((samples, KEYS_PAD, width), BF16),
        swap=VMEM((256, 256), BF16),
        sq_all=VMEM((5, width, width), BF16),
        mlp_all=VMEM((2, width, wide), BF16),
        gain_all=VMEM((2, width), F32),
        wkh=VMEM((HEADS * width, width), BF16),
        wvh=VMEM((HEADS * width, width), BF16),
        first=VMEM((tokens, width), BF16),
        query=VMEM((tokens, width), BF16),
        xhat=VMEM((tokens, width), F32),
        rstd=VMEM((tokens, 1), F32),
        probs=VMEM((samples // 2, KEYS_PAD, LANES), F32),
        queries=VMEM((samples, rows, width), BF16),
        dmixes=VMEM((samples, rows, width), BF16),
        u=VMEM((tokens, HEADS * width), BF16),
        dq_wide=VMEM((tokens, HEADS * width), BF16),
        mixed=VMEM((tokens, width), BF16),
        second=VMEM((tokens, width), BF16),
        active=VMEM((tokens, wide), BF16),
        dhidden=VMEM((tokens, wide), BF16),
        out_low=VMEM((tokens, width), BF16),
        dres_low=VMEM((tokens, width), BF16),
        dres=VMEM((tokens, width), F32),
        dmixed=VMEM((tokens, width), BF16),
        dquery=VMEM((tokens, width), BF16),
        out_v=VMEM((tokens, width), F32),
        ag_v=VMEM((tokens, width), F32),
        angle=VMEM((samples, width // 2), F32),
        embed=VMEM((samples, width), BF16),
        stamps=VMEM((samples, 8, width), F32),
        gain_acc=VMEM((8, width), F32),
        flags_s=pltpu.SMEM(flags.shape, jnp.int32),
        levels_s=pltpu.SMEM(levels.shape, jnp.int32),
        in_sems=sem((10,)),
        out_sems=sem((2,)),
    )
    extra = {}
    if remote:
        ins.update(sqm=sqm, mlpm=mlpm)
        outs.update(out=jax.ShapeDtypeStruct((3, WIRE, LANES), F32))
        chunks = len(CHUNKS)
        scratch.update(
            grads=VMEM(grads, F32),
            sqw_v=VMEM(sqw.shape, F32),
            mlpw_v=VMEM(mlpw.shape, F32),
            gain_v=VMEM(gain.shape, F32),
            sqm_v=VMEM(sqm.shape, F32),
            mlpm_v=VMEM(mlpm.shape, F32),
            wire=VMEM(grads, BF16),
            edge=VMEM((16, LANES), F32),
            gsend=sem((chunks, 6)),
            grecv=sem((chunks, 6)),
            send0=VMEM((4, 2, 2, WIRE, LANES), BF16),
            got_core=VMEM((4, 2, 2, WIRE, LANES), BF16),
            sum1=VMEM((4, 2, 2, WIRE, LANES), F32),
            send1=VMEM((4, 2, WIRE, LANES), BF16),
            got1=VMEM((4, 2, WIRE, LANES), BF16),
            sum2=VMEM((4, 2, WIRE, LANES), F32),
            send2=VMEM((4, WIRE, LANES), BF16),
            got2=VMEM((4, WIRE, LANES), BF16),
            sum3=VMEM((4, WIRE, LANES), F32),
            send3=VMEM((3, WIRE, LANES), BF16),
            got3=VMEM((3, WIRE, LANES), BF16),
            moment=VMEM((WIRE, LANES), F32),
            slabs_sq=VMEM((32, SQ_ROWS, LANES), F32),
            slabs_mlp=VMEM((32, MLP_ROWS, LANES), BF16),
            moment_low=VMEM((2 * MLP_ROWS, LANES), BF16),
            back_mlp=VMEM((2, MLP_ROWS, LANES), BF16),
            result_sq=VMEM((32, SQ_ROWS, LANES), F32),
            result_mlp=VMEM((32, MLP_ROWS, LANES), BF16),
            cur=VMEM((width, wide), F32),
            cur_low=VMEM((width, wide), BF16),
            send=sem((chunks, 6)),
            recv=sem((chunks, 6)),
            own_send=sem((7,)),
            own_recv=sem((1,)),
            back_send=sem((32,)),
            back_recv=sem((7,)),
        )
        extra = dict(collective_id=0, has_side_effects=True)
        outs = {name: VMEM(like.shape, like.dtype) for name, like in outs.items()}
    else:
        outs.update(grads=jax.ShapeDtypeStruct(grads, F32))
    names = tuple(ins) + tuple(outs) + tuple(scratch)
    stay = [pltpu.with_memory_space_constraint(value, pltpu.HBM) for value in ins.values()]
    results = pl.pallas_call(
        functools.partial(block_kernel, names, remote),
        out_shape=tuple(outs.values()),
        in_specs=[any_space] * len(ins),
        out_specs=[any_space] * 2 + [in_vmem] * 2,
        scratch_shapes=list(scratch.values()),
        compiler_params=pltpu.CompilerParams(vmem_limit_bytes=46 << 20, **extra),
        name="block_and_back",
    )(*stay)
    return Refs(zip(outs, results))


PARTS = 7


def finish_kernel(names, rate, *args):
    r = Refs(zip(names, args))
    sems = r.sems
    keys = r.og.shape[0]
    step = keys // PARTS

    def leave(part):
        block = pl.ds(part * step, step)
        return pltpu.make_async_copy(r.og_v.at[block], r.og.at[block], sems.at[part])

    more = PARTS
    moves = []
    if hasattr(r, "wire"):
        pairs = [(r.sqw, r.sqw_v), (r.mlpw, r.mlpw_v), (r.gain, r.gain_v), (r.gainm, r.gainm_v)]
        pairs += [(r.output, r.output_f), (r.ag, r.ag_f)]
        for source, target in pairs:
            moves.append(pltpu.make_async_copy(source, target, sems.at[more]))
            moves[-1].start()
            more += 1
    for part in range(PARTS):

        def widen(j, _):
            r.og_v[j] = r.low[j].astype(F32)
            return 0

        lax.fori_loop(part * step, (part + 1) * step, widen, 0, unroll=4)
        leave(part).start()
    for copy in moves[:4]:
        copy.wait()
    if hasattr(r, "wire"):
        finish_weights(r, rate)
    for part in range(PARTS):
        leave(part).wait()
    for copy in moves[4:]:
        copy.wait()


def finish_weights(r, rate):
    wire = r.wire
    me = lax.axis_index("dp")
    for m in range(5):
        for j in range(2):
            rows, columns = pl.ds(SQ_AT[m] + j * TILE, TILE), pl.ds(j * LANES, LANES)
            r.sqg[m, :, columns] = wire[0, rows, :]
            r.sqm[m, :, columns] = wire[1, rows, :]
            r.sqn[m, :, columns] = r.sqw_v[m, :, columns] - SQ_RATES[m] * wire[2, rows, :]
    r.sqc[...] = r.sqn[...].astype(BF16)
    for m in range(2):
        for j in range(8):
            rows, columns = pl.ds(m * MLP_ROWS + j * TILE, TILE), pl.ds(j * LANES, LANES)
            r.mlpg[m, :, columns] = wire[0, rows, :]
            r.mlpm[m, :, columns] = wire[1, rows, :]
            r.mlpn[m, :, columns] = r.mlpw_v[m, :, columns] - MLP_RATES[m] * wire[2, rows, :]
    r.mlpc[...] = r.mlpn[...].astype(BF16)
    tile = wire[0, pl.ds(GAIN_BASE, TILE), :]
    turned = pltpu.roll(tile, (LANES - (me % 16) * TILE) % LANES, 1)
    at = me // 16
    for norm in range(2):
        pair = turned[2 * norm : 2 * norm + 2, 0:TILE]
        row = jnp.where(at == 0, pair[0:1, :], pair[1:2, :])
        new = 0.5 * r.gainm_v[norm : norm + 1, :] + row
        r.gg[norm : norm + 1, :] = row
        r.gm[norm : norm + 1, :] = new
        r.gn[norm : norm + 1, :] = r.gain_v[norm : norm + 1, :] - rate * new


def finish(rate, made, sqw=None, mlpw=None, gain=None, gainm=None):
    any_space = pl.BlockSpec(memory_space=pl.ANY)
    in_vmem = pl.BlockSpec(memory_space=VMEM)
    ins = dict(low=made.og)
    outs = dict(og=jax.ShapeDtypeStruct(made.og.shape, F32))
    near, far = 1, 1
    if hasattr(made, "out"):
        ins.update(output=made.output, ag=made.ag, wire=made.out, sqw=sqw, mlpw=mlpw, gain=gain, gainm=gainm)
        like = jax.ShapeDtypeStruct
        near, far = 4, 3
        outs.update(
            output_f=like(made.output.shape, F32),
            ag_f=like(made.ag.shape, F32),
            sqg=like(sqw.shape, F32),
            sqm=like(sqw.shape, F32),
            sqn=like(sqw.shape, F32),
            sqc=like(sqw.shape, BF16),
            mlpg=like(mlpw.shape, F32),
            mlpm=like(mlpw.shape, F32),
            mlpn=like(mlpw.shape, F32),
            mlpc=like(mlpw.shape, BF16),
            gg=like(gain.shape, F32),
            gm=like(gain.shape, F32),
            gn=like(gain.shape, F32),
        )
    scratch = dict(
        og_v=VMEM(made.og.shape, F32),
        sems=pltpu.SemaphoreType.DMA((PARTS + 6,)),
    )
    if hasattr(made, "out"):
        scratch.update(
            sqw_v=VMEM(sqw.shape, F32),
            mlpw_v=VMEM(mlpw.shape, F32),
            gain_v=VMEM(gain.shape, F32),
            gainm_v=VMEM(gainm.shape, F32),
        )
    names = tuple(ins) + tuple(outs) + tuple(scratch)
    made_here = list(ins.values())
    stay = [pltpu.with_memory_space_constraint(value, pltpu.HBM) for value in made_here[near:]]
    results = pl.pallas_call(
        functools.partial(finish_kernel, names, rate),
        out_shape=tuple(outs.values()),
        in_specs=[in_vmem] * near + [any_space] * (len(ins) - near),
        out_specs=[any_space] * far + [in_vmem] * (len(outs) - far),
        scratch_shapes=list(scratch.values()),
        compiler_params=pltpu.CompilerParams(vmem_limit_bytes=16 << 20),
        name="finish",
    )(*made_here[:near], *stay)
    return Refs(zip(outs, results))


HIGH_PRECISION = lax.Precision.HIGHEST


def plain_orthogonalize(matrix):
    current = matrix / (jnp.sqrt(jnp.sum(matrix * matrix)) + 1e-07)
    for turn in range(5):
        gram = jnp.dot(current, current.T, precision=HIGH_PRECISION)
        poly = COEF_B * gram + COEF_C * jnp.dot(gram, gram, precision=HIGH_PRECISION)
        current = COEF_A * current + jnp.dot(poly, current, precision=HIGH_PRECISION)
    return current


def pick_owned(stack, owners, device):
    chosen = jnp.zeros_like(stack[0])
    for index in range(len(owners)):
        chosen = jnp.where(device == owners[index], stack[index], chosen)
    return chosen


def is_owner(owners, device):
    flag = device < 0
    for owner in owners:
        flag = jnp.logical_or(flag, device == owner)
    return flag


def from_wire(grads):
    def matrix(base, tiles):
        part = grads[:, base : base + tiles * TILE, :].reshape(-1, tiles, TILE, LANES)
        return part.transpose(0, 2, 1, 3).reshape(-1, tiles * LANES)

    square = jnp.stack([matrix(SQ_AT[m], 2) for m in range(5)])
    mlp = jnp.stack([matrix(m * MLP_ROWS, 8) for m in range(2)])
    return square, mlp, grads[0, GAIN_BASE : GAIN_BASE + 4, :].reshape(2, 2 * LANES)


def update_by_collectives(
    grads, square_weights, mlp_weights, gains, square_moment, mlp_moment, gain_moment, rate
):
    square_local, mlp_local, gain_local = from_wire(grads)
    square_grad, mlp_grad, gain_grad = (
        lax.psum_scatter(square_local, "dp", scatter_dimension=1, tiled=True),
        lax.psum_scatter(mlp_local, "dp", scatter_dimension=1, tiled=True),
        lax.psum_scatter(gain_local, "dp", scatter_dimension=1, tiled=True),
    )
    square_moment_new = 0.5 * square_moment + square_grad
    mlp_moment_new = 0.5 * mlp_moment + mlp_grad
    gain_moment_new = 0.5 * gain_moment + gain_grad
    device = lax.axis_index("dp")
    count = lax.axis_size("dp")
    square_owners = [index * count // 7 for index in range(5)]
    mlp_owners = [(index + 5) * count // 7 for index in range(2)]
    square_full, mlp_full = (
        lax.all_gather(square_moment_new, "dp", axis=1, tiled=True),
        lax.all_gather(mlp_moment_new, "dp", axis=1, tiled=True),
    )
    mine_square = pick_owned(square_full, square_owners, device)
    mine_mlp = pick_owned(mlp_full, mlp_owners, device)
    made_square = lax.cond(
        is_owner(square_owners, device), plain_orthogonalize, jnp.zeros_like, mine_square
    )
    made_mlp = lax.cond(is_owner(mlp_owners, device), plain_orthogonalize, jnp.zeros_like, mine_mlp)
    stack_square = jnp.stack(
        [jnp.where(device == owner, made_square, 0.0) for owner in square_owners]
    )
    stack_mlp = jnp.stack([jnp.where(device == owner, made_mlp, 0.0) for owner in mlp_owners])
    square_ortho, mlp_ortho = (
        lax.psum_scatter(stack_square, "dp", scatter_dimension=1, tiled=True),
        lax.psum_scatter(stack_mlp, "dp", scatter_dimension=1, tiled=True),
    )
    square_new = square_weights - jnp.array(SQ_RATES, F32)[:, None, None] * square_ortho
    mlp_new = mlp_weights - jnp.array(MLP_RATES, F32)[:, None, None] * mlp_ortho
    gains_new = gains - rate * gain_moment_new
    return (
        square_grad,
        square_moment_new,
        square_new,
        square_new.astype(BF16),
        mlp_grad,
        mlp_moment_new,
        mlp_new,
        mlp_new.astype(BF16),
        gain_grad,
        gain_moment_new,
        gains_new,
    )


def per_device(
    actions,
    observed,
    camera_flags,
    noise_levels,
    cotangent,
    square_weights,
    mlp_weights,
    gains,
    square_moment,
    mlp_moment,
    gain_moment,
):
    count = lax.axis_size("dp")
    rate = 0.1 / math.sqrt(actions.shape[0] * count)
    by_key = observed.transpose(1, 0, 2)
    ins = (actions, by_key, camera_flags, noise_levels, cotangent)
    if count == math.prod(GRID):
        made = block_and_back(True, *ins, square_weights, mlp_weights, gains, square_moment, mlp_moment)
        done = finish(rate, made, square_weights, mlp_weights, gains, gain_moment)
        output, actions_grad = done.output_f, done.ag_f
        d = done
        rest = (d.sqg, d.sqm, d.sqn, d.sqc, d.mlpg, d.mlpm, d.mlpn, d.mlpc, d.gg, d.gm, d.gn)
    else:
        square_all, mlp_all = (
            lax.all_gather(square_weights.astype(BF16), "dp", axis=1, tiled=True),
            lax.all_gather(mlp_weights.astype(BF16), "dp", axis=1, tiled=True),
        )
        gain_all = lax.all_gather(gains, "dp", axis=1, tiled=True)
        made = block_and_back(False, *ins, square_all, mlp_all, gain_all)
        done = finish(rate, made)
        output, actions_grad = made.output, made.ag
        grads = made.grads.reshape(-1, WIRE, LANES)
        rest = update_by_collectives(
            grads, square_weights, mlp_weights, gains, square_moment, mlp_moment, gain_moment, rate
        )
    observed_grad = done.og.transpose(1, 0, 2)
    return (output, actions_grad, observed_grad) + tuple(rest)


def solution(mesh):
    rows, cube, flat = P("dp", None), P("dp", None, None), P("dp")
    stacked, pair = P(None, "dp", None), P(None, "dp")
    return jax.shard_map(
        per_device,
        mesh=mesh,
        in_specs=(rows, cube, flat, flat, rows, stacked, stacked, pair, stacked, stacked, pair),
        out_specs=(rows, rows, cube) + (stacked,) * 8 + (pair,) * 3,
        check_vma=False,
    )
```

```python
import functools
import math

import jax
import jax.numpy as jnp
from jax import lax
from jax.experimental import pallas as pl
from jax.experimental.pallas import tpu as pltpu
from jax.sharding import PartitionSpec as P

HEADS = 4
ACT = 16
OBS_FULL = 196
OBS_FEW = 49
COEF_A = 3.4445
COEF_B = -4.775
COEF_C = 2.0315
F32 = jnp.float32
BF16 = jnp.bfloat16
MESH = pl.DeviceIdType.MESH
VMEM = pltpu.VMEM
NN = (((1,), (0,)), ((), ()))
NT = (((1,), (1,)), ((), ()))
TN = (((0,), (0,)), ((), ()))

LANES = 128
TILE = 8
MLP_ROWS = 64
SQ_ROWS = 16
SQ_AT = (160, 192, 176, 128, 144)
GAIN_BASE = 208
WIRE = 224
PIECES = ((0, 64), (64, 64), (128, 32), (160, 32), (192, 32))
PIECE_X_FIRST = (True, False, True, True, False)
CHUNKS = ((0, 64), (64, 64), (128, 32), (160, 32), (192, 16), (208, 16))
X_FIRST = (True, False, True, False, True, False)
COMPLETES = ((0,), (1,), (5, 6), (2, 4), (3,), ())
MLP_RATES = (1.0, 0.5)
SQ_RATES = (0.5, 0.5, 0.5, 0.5, 4.0)
GRID = (4, 2, 2, 2)
OWNERS = (8, 22, 14, 16, 11, 21, 13)
SHIFTS = (0.0, 0.0, 0.4, 0.8, 0.8)
KEYS_PAD = 208
GROUP = 16
ROWS = 512


class Refs:
    def __init__(self, pairs):
        self.__dict__.update(pairs)


def dot(left, right, dims=NN):
    return lax.dot_general(left, right, dims, preferred_element_type=F32)


def place():
    me = lax.axis_index("dp")
    return me, me // 8, (me // 4) % 2, (me // 2) % 2, me % 2


def device_at(z, y, x, c):
    return ((z * 2 + y) * 2 + x) * 2 + c


def link(src, dst, send, recv, device):
    return pltpu.make_async_remote_copy(
        src_ref=src,
        dst_ref=dst,
        send_sem=send,
        recv_sem=recv,
        device_id=(device,),
        device_id_type=MESH,
    )


def greet(device):
    pl.semaphore_signal(
        pltpu.get_barrier_semaphore(), inc=1, device_id=(device,), device_id_type=MESH
    )


def normalize(values):
    centred = values - jnp.mean(values, -1, keepdims=True)
    scale = lax.rsqrt(jnp.mean(centred * centred, -1, keepdims=True) + 1e-05)
    return centred * scale, scale


def norm_back(grad, hat, scale):
    mean_one = jnp.mean(grad, -1, keepdims=True)
    mean_two = jnp.mean(grad * hat, -1, keepdims=True)
    return scale * (grad - mean_one - hat * mean_two)


class Gather:
    def __init__(self, r):
        self.r = r
        self.me, self.z, self.y, self.x, self.c = place()

    def hop(self, k, step, part, device):
        return link(part, part, self.r.gsend.at[k, step], self.r.grecv.at[k, step], device)

    def along_z(self, k, step):
        part = self.r.wire.at[self.z, self.y, self.x, self.c, pl.ds(*PIECES[k])]
        return self.hop(k, step, part, device_at((self.z + step + 1) % 4, self.y, self.x, self.c))

    def from_z(self, k, step):
        there = (self.z + 3 - step) % 4
        part = self.r.wire.at[there, self.y, self.x, self.c, pl.ds(*PIECES[k])]
        return self.hop(k, step, part, device_at(there, self.y, self.x, self.c))

    def plane(self, k, second, mine):
        z, y, x, c = self.z, self.y, self.x, self.c
        rows, wire = pl.ds(*PIECES[k]), self.r.wire
        py, px = (y, x) if mine else (1 - y, 1 - x)
        along_x = PIECE_X_FIRST[k] == second
        if along_x:
            part = wire.at[:, y, px, c, rows] if second else wire.at[:, :, px, c, rows]
            return self.hop(k, 3 if second else 4, part, device_at(z, y, 1 - x, c))
        part = wire.at[:, py, x, c, rows] if second else wire.at[:, py, :, c, rows]
        return self.hop(k, 3 if second else 4, part, device_at(z, 1 - y, x, c))

    def core(self, k, mine):
        part = self.r.wire.at[:, :, :, self.c if mine else 1 - self.c, pl.ds(*PIECES[k])]
        return self.hop(k, 5, part, device_at(self.z, self.y, self.x, 1 - self.c))

    def first(self, *chunks):
        for k in chunks:
            for step in range(3):
                self.along_z(k, step).start()

    def second(self, *chunks):
        for k in chunks:
            for step in range(3):
                self.from_z(k, step).wait_recv()
            self.plane(k, True, True).start()

    def third(self, *chunks):
        for k in chunks:
            self.plane(k, True, False).wait_recv()
            self.plane(k, False, True).start()

    def fourth(self, *chunks):
        for k in chunks:
            self.plane(k, False, False).wait_recv()
            self.core(k, True).start()

    def last(self, *chunks):
        for k in chunks:
            self.core(k, False).wait_recv()

    def drain(self):
        for k in range(len(PIECES)):
            for step in range(3):
                self.along_z(k, step).wait_send()
            self.plane(k, True, True).wait_send()
            self.plane(k, False, True).wait_send()
            self.core(k, True).wait_send()

    def fill(self):
        r = self.r
        spot = (self.z, self.y, self.x, self.c)

        def tiles(source, m, base, number):
            for j in range(number):
                pair = [source[m, :, pl.ds((2 * j + k) * LANES, LANES)] for k in range(2)]
                r.wire[spot + (pl.ds(base + j * 16, 16),)] = jnp.concatenate(pair, axis=0).astype(BF16)

        for m in range(5):
            tiles(r.sqw_v, m, SQ_AT[m], 1)
        for m in range(2):
            tiles(r.mlpw_v, m, m * MLP_ROWS, 4)
        gains, edge = r.gain_v[...], r.edge
        high = gains.astype(BF16).astype(F32)
        middle = (gains - high).astype(BF16).astype(F32)
        edge[...] = jnp.zeros_like(edge)
        edge[0:2, 0:TILE] = high
        edge[2:4, 0:TILE] = middle
        edge[4:6, 0:TILE] = (gains - high - middle).astype(BF16).astype(F32)
        r.wire[spot + (pl.ds(GAIN_BASE, 16),)] = edge[...].astype(BF16)

    def unpack(self, base, number, out, m):
        for j in range(number):
            block = self.r.wire[:, :, :, :, pl.ds(base + j * 16, 16), :].reshape(32, 16, LANES).astype(F32)
            for half in range(2):
                columns = pl.ds((2 * j + half) * LANES, LANES)
                out[m, :, columns] = block[:, half * 8 : half * 8 + 8, :].reshape(256, LANES).astype(BF16)

    def unpack_gains(self):
        edge, wire = self.r.edge, self.r.wire
        for half in range(2):
            total = jnp.zeros((16, LANES), F32)
            for at in range(16):
                d = half * 16 + at
                tile = wire[d // 8, (d // 4) % 2, (d // 2) % 2, d % 2, pl.ds(GAIN_BASE, 16), :].astype(F32)
                total = total + (tile if at == 0 else pltpu.roll(tile, at * TILE, 1))
            edge[...] = total
            self.r.gain_all[:, pl.ds(half * LANES, LANES)] = edge[0:2, :] + edge[2:4, :] + edge[4:6, :]


class Update:
    def __init__(self, r):
        self.r = r
        self.me, self.z, self.y, self.x, self.c = place()

    def hop(self, k, step, src, dst, device):
        return link(src, dst, self.r.send.at[k, step], self.r.recv.at[k, step], device)

    def core(self, k):
        rows = pl.ds(*CHUNKS[k])
        src, dst = self.r.send0.at[:, :, :, rows], self.r.got_core.at[:, :, :, rows]
        return self.hop(k, 0, src, dst, device_at(self.z, self.y, self.x, 1 - self.c))

    def plane(self, k, first):
        rows = pl.ds(*CHUNKS[k])
        to = (self.z, self.y, 1 - self.x, self.c) if X_FIRST[k] == first else (self.z, 1 - self.y, self.x, self.c)
        if first:
            src, dst = self.r.send1.at[:, :, rows], self.r.got1.at[:, :, rows]
        else:
            src, dst = self.r.send2.at[:, rows], self.r.got2.at[:, rows]
        return self.hop(k, 1 if first else 2, src, dst, device_at(*to))

    def along_z(self, k, step):
        rows = pl.ds(*CHUNKS[k])
        to = device_at((self.z + step + 1) % 4, self.y, self.x, self.c)
        return self.hop(k, 3 + step, self.r.send3.at[step, rows], self.r.got3.at[step, rows], to)

    def start(self, k):
        rows = pl.ds(*CHUNKS[k])
        self.r.send0[:, :, :, rows, :] = self.r.grads[:, :, :, 1 - self.c, rows, :].astype(BF16)
        self.core(k).start()

    def one(self, *chunks):
        r = self.r
        for k in chunks:
            rows = pl.ds(*CHUNKS[k])
            self.core(k).wait_recv()
            sum1 = r.sum1
            sum1[:, :, :, rows, :] = r.grads[:, :, :, self.c, rows, :] + r.got_core[:, :, :, rows, :].astype(F32)
            other = sum1[:, :, 1 - self.x, rows, :] if X_FIRST[k] else sum1[:, 1 - self.y, :, rows, :]
            r.send1[:, :, rows, :] = other.astype(BF16)
            self.plane(k, True).start()

    def two(self, *chunks):
        r = self.r
        for k in chunks:
            rows = pl.ds(*CHUNKS[k])
            self.plane(k, True).wait_recv()
            sum1, sum2 = r.sum1, r.sum2
            mine = sum1[:, :, self.x, rows, :] if X_FIRST[k] else sum1[:, self.y, :, rows, :]
            sum2[:, :, rows, :] = mine + r.got1[:, :, rows, :].astype(F32)
            other = 1 - self.y if X_FIRST[k] else 1 - self.x
            r.send2[:, rows, :] = sum2[:, other, rows, :].astype(BF16)
            self.plane(k, False).start()

    def three(self, *chunks):
        r = self.r
        for k in chunks:
            rows = pl.ds(*CHUNKS[k])
            self.plane(k, False).wait_recv()
            mine = self.y if X_FIRST[k] else self.x
            r.sum3[:, rows, :] = r.sum2[:, mine, rows, :] + r.got2[:, rows, :].astype(F32)
            for step in range(3):
                r.send3[step, rows, :] = r.sum3[(self.z + step + 1) % 4, rows, :].astype(BF16)
                self.along_z(k, step).start()

    def slab(self, index):
        if index < 2:
            return pl.ds(index * MLP_ROWS, MLP_ROWS), self.r.slabs_mlp, self.r.result_mlp
        return pl.ds(SQ_AT[index - 2], SQ_ROWS), self.r.slabs_sq, self.r.result_sq

    def to_owner(self, index):
        rows, slabs, _ = self.slab(index)
        moment = self.r.moment_low if index < 2 else self.r.moment
        return link(
            moment.at[rows], slabs.at[self.me],
            self.r.own_send.at[index], self.r.own_recv.at[0], OWNERS[index],
        )

    def four(self, *chunks):
        r = self.r
        moment, out = r.moment, r.out
        for k in chunks:
            rows = pl.ds(*CHUNKS[k])
            total = r.sum3[self.z, rows, :]
            for step in range(3):
                self.along_z(k, step).wait_recv()
                total = total + r.got3[step, rows, :].astype(F32)
            out[0, rows, :] = total
            new = 0.5 * moment[rows, :] + total
            moment[rows, :] = new
            if k < 2:
                r.moment_low[rows, :] = new.astype(BF16)
            for index in COMPLETES[k]:
                rows_m, slabs, _ = self.slab(index)

                @pl.when(self.me != OWNERS[index])
                def _():
                    self.to_owner(index).start()

                @pl.when(self.me == OWNERS[index])
                def _():
                    mine = r.moment_low if index < 2 else moment
                    pltpu.make_async_copy(mine.at[rows_m], slabs.at[self.me], r.own_recv.at[0]).start()

    def old_moment(self):
        r = self.r
        moment = r.moment
        for m in range(2):
            for j in range(8):
                moment[pl.ds(m * MLP_ROWS + j * TILE, TILE), :] = r.mlpm_v[m, :, pl.ds(j * LANES, LANES)]
        for m in range(5):
            for j in range(2):
                moment[pl.ds(SQ_AT[m] + j * TILE, TILE), :] = r.sqm_v[m, :, pl.ds(j * LANES, LANES)]
        moment[pl.ds(GAIN_BASE, 16), :] = jnp.zeros((16, LANES), F32)

    def orthogonalize(self):
        r = self.r
        cur = r.cur
        rows = lax.broadcasted_iota(jnp.int32, (256, 256), 0)
        diagonal = rows == lax.broadcasted_iota(jnp.int32, (256, 256), 1)

        def run(slabs, result, tiles):
            pltpu.make_async_copy(slabs, slabs, r.own_recv.at[0]).wait()
            low = r.cur_low
            for j in range(tiles // 2):
                pair = slabs[:, pl.ds(j * 16, 16), :].astype(F32)
                for side in range(2):
                    columns = pl.ds((2 * j + side) * LANES, LANES)
                    part = pair[:, side * TILE : (side + 1) * TILE, :].reshape(256, LANES)
                    cur[:, columns] = part
                    low[:, columns] = part.astype(BF16)
            scale = 1.0
            for turn, shift in enumerate(SHIFTS):
                whole = low[:, 0 : tiles * LANES]
                off = dot(whole, whole, NT)
                if turn == 0:
                    norm = jnp.sum(jnp.sum(jnp.where(diagonal, off, 0.0), axis=0, keepdims=True), axis=1, keepdims=True)
                    scale = 1.0 / (jnp.sqrt(norm) + 1e-07)
                    off = off * (scale * scale)
                if shift:
                    off = off - jnp.where(diagonal, shift, 0.0)
                off_low = off.astype(BF16)
                poly = (COEF_B + 2.0 * COEF_C * shift) * off + COEF_C * dot(off_low, off_low)
                poly = poly.astype(BF16)
                keep = COEF_A + shift * (COEF_B + COEF_C * shift)
                for j in range(tiles // 2):
                    columns = pl.ds(j * 2 * LANES, 2 * LANES)
                    now = keep * cur[:, columns] + dot(poly, low[:, columns])
                    if turn == 0:
                        now = now * scale
                    if turn < len(SHIFTS) - 1:
                        cur[:, columns] = now
                        low[:, columns] = now.astype(BF16)
                    else:
                        parts = [now[:, side * LANES : (side + 1) * LANES].reshape(32, TILE, LANES) for side in range(2)]
                        result[:, pl.ds(j * 16, 16), :] = jnp.concatenate(parts, axis=1).astype(result.dtype)

        mine_mlp = jnp.logical_or(self.me == OWNERS[0], self.me == OWNERS[1])
        mine_sq = self.me < 0
        for device in OWNERS[2:]:
            mine_sq = jnp.logical_or(mine_sq, self.me == device)

        @pl.when(mine_mlp)
        def _():
            run(r.slabs_mlp, r.result_mlp, 8)

        @pl.when(mine_sq)
        def _():
            run(r.slabs_sq, r.result_sq, 2)

    def landing(self, index):
        if index < 2:
            return self.r.back_mlp.at[index]
        return self.r.out.at[2, pl.ds(SQ_AT[index - 2], SQ_ROWS)]

    def give_back(self, index, device):
        _, _, result = self.slab(index)
        return link(
            result.at[device], self.landing(index),
            self.r.back_send.at[device], self.r.back_recv.at[index], device,
        )

    def give_all(self):
        r = self.r
        for index in range(7):
            _, _, result = self.slab(index)

            @pl.when(self.me == OWNERS[index])
            def _():
                def send_one(step, _):
                    self.give_back(index, (self.me + step) % 32).start()
                    return 0

                lax.fori_loop(1, 32, send_one, 0)
                pltpu.make_async_copy(result.at[self.me], self.landing(index), r.back_recv.at[index]).start()

    def take_all(self):
        for index in range(7):
            _, _, result = self.slab(index)
            pltpu.make_async_copy(result.at[0], self.landing(index), self.r.back_recv.at[index]).wait()
        for index in range(2):
            rows = pl.ds(index * MLP_ROWS, MLP_ROWS)
            self.r.out[2, rows, :] = self.r.back_mlp[index].astype(F32)

    def drain(self):
        for k in range(len(CHUNKS)):
            self.core(k).wait_send()
            self.plane(k, True).wait_send()
            self.plane(k, False).wait_send()
            for step in range(3):
                self.along_z(k, step).wait_send()
        for index in range(7):

            @pl.when(self.me != OWNERS[index])
            def _():
                self.to_owner(index).wait_send()

    def drain_owner(self):
        for index in range(7):

            @pl.when(self.me == OWNERS[index])
            def _():
                def wait_one(step, _):
                    self.give_back(index, (self.me + step) % 32).wait_send()
                    return 0

                lax.fori_loop(1, 32, wait_one, 0)


def greet_all():
    me, z, y, x, c = place()
    greet(device_at(z, y, x, 1 - c))
    greet(device_at(z, y, 1 - x, c))
    greet(device_at(z, 1 - y, x, c))
    for step in range(1, 4):
        greet(device_at((z + step) % 4, y, x, c))
    owner = me < 0
    for device in OWNERS:
        owner = jnp.logical_or(owner, me == device)

        @pl.when(me != device)
        def _():
            greet(device)

    @pl.when(owner)
    def _():
        def greet_other(step, _):
            greet((me + step) % 32)
            return 0

        lax.fori_loop(1, 32, greet_other, 0)

    is_owner = owner.astype(jnp.int32)
    return 6 + 7 - is_owner + 31 * is_owner


def block_kernel(names, remote, *args):
    r = Refs(zip(names, args))
    keys, samples = r.obs.shape[0], r.obs.shape[1]
    tokens, width = r.acts.shape
    head_dim, half, per = width // HEADS, width // 2, ROWS // ACT
    wide = r.mlp_all.shape[2]
    groups = samples // GROUP
    in_sems, out_sems = r.in_sems, r.out_sems

    if remote:
        own = (r.sqw_v, r.mlpw_v, r.gain_v)
    else:
        own = (r.sq_all, r.mlp_all, r.gain_all)
    loads = list(zip((r.sqw, r.mlpw, r.gain), own))
    loads += [(r.acts, r.acts_v), (r.obs, r.obs_v.at[pl.ds(0, keys)]), (r.cot, r.cot_v)]
    if remote:
        loads += [(r.sqm, r.sqm_v), (r.mlpm, r.mlpm_v)]
    loads += [(r.flags, r.flags_s), (r.levels, r.levels_s)]
    copies = [pltpu.make_async_copy(a, b, in_sems.at[i]) for i, (a, b) in enumerate(loads)]

    def arrive(*which):
        for i in which:
            copies[i].wait()

    for copy in copies:
        copy.start()
    if remote:
        gather, update = Gather(r), Update(r)
        expected = greet_all()
        arrive(0, 1, 2)
        gather.fill()
        pl.semaphore_wait(pltpu.get_barrier_semaphore(), expected)
        gather.first(3, 4)

    arrive(3)

    def hats(i, _):
        rows = pl.ds(pl.multiple_of(i * ROWS, ROWS), ROWS)
        hat, scale = normalize(r.acts_v[rows, :])
        r.xhat[rows, :] = hat
        r.rstd[rows, :] = scale
        return 0

    lax.fori_loop(0, tokens // ROWS, hats, 0)

    mem, obs_v = r.mem, r.obs_v
    batch = 16
    chunks = KEYS_PAD // batch
    swap = r.swap
    row = lax.broadcasted_iota(jnp.int32, swap.shape, 0)
    column = lax.broadcasted_iota(jnp.int32, swap.shape, 1)
    swap[...] = jnp.where(column == (row % batch) * batch + row // batch, 1.0, 0.0).astype(BF16)

    def turn(part, low, high):
        def one(j, _):
            at = pl.ds(pl.multiple_of(j * batch, batch), batch)
            here = pl.ds(part * batch, batch)
            block = obs_v[at, here, :].reshape(batch * batch, width)
            mem[here, at, :] = dot(swap[...], block).astype(BF16).reshape(batch, batch, width)
            return 0

        lax.fori_loop(low, high, one, 0, unroll=high - low)

    whole = chunks - 1
    arrive(4)
    turn(0, 0, whole // 2)
    if remote:
        gather.second(3, 4)
        gather.first(2, 0, 1)
    turn(0, whole // 2, whole)
    if remote:
        gather.third(3, 4)
    turn(1, 0, whole // 2)
    if remote:
        gather.second(2, 0, 1)
        gather.fourth(3, 4)
    turn(1, whole // 2, whole)
    arrive(len(copies) - 1, len(copies) - 2)
    freqs = jnp.exp(
        lax.broadcasted_iota(jnp.int32, (1, half), 1).astype(F32) * F32(-math.log(10000.0)) / half
    )
    for s in range(samples):
        r.angle[s : s + 1, :] = r.levels_s[s].astype(F32) * freqs
    r.embed[:, 0:half] = jnp.sin(r.angle[...]).astype(BF16)
    r.embed[:, half:width] = jnp.cos(r.angle[...]).astype(BF16)
    if remote:
        arrive(6, 7)
        update.old_moment()
        gather.third(2, 0, 1)
        gather.last(3, 4)
        for m in range(3):
            gather.unpack(SQ_AT[m], 1, r.sq_all, m)
        gather.unpack_gains()
    else:
        arrive(0, 1, 2)

    sq, mlp = r.sq_all, r.mlp_all
    wkh, wvh = r.wkh, r.wvh
    lane = lax.broadcasted_iota(jnp.int32, (width, width), 1)

    def split_heads(out, weight):
        weight = weight.astype(F32)
        for h in range(HEADS):
            out[pl.ds(h * width, width), :] = jnp.where(lane // head_dim == h, weight, 0.0).astype(BF16)

    split_heads(wkh, sq[2])
    g1, g2 = r.gain_all[0:1, :], r.gain_all[1:2, :]

    obs_v[keys] = dot(r.embed[...], sq[0]).astype(BF16)
    obs_v[keys + 1 :] = jnp.zeros((KEYS_PAD - keys - 1, samples, width), BF16)
    for part in range(samples // batch):
        turn(part, whole, chunks)

    queries, dmixes = r.queries, r.dmixes

    def make_queries(i, _):
        rows = pl.ds(pl.multiple_of(i * ROWS, ROWS), ROWS)
        first = (r.xhat[rows, :] * g1).astype(BF16)
        r.first[rows, :] = first
        q = dot(first, sq[1]).astype(BF16)
        r.query[rows, :] = q
        here = pl.ds(i * per, per)
        for h in range(HEADS):
            wk = wkh[pl.ds(h * width, width), :]
            value = (dot(q, wk, NT) * 0.125).astype(BF16).reshape(per, ACT, width)
            queries[here, pl.ds(h * ACT, ACT), :] = value
        return 0

    lax.fori_loop(0, tokens // ROWS, make_queries, 0)

    key = lax.broadcasted_iota(jnp.int32, (KEYS_PAD, LANES), 0)
    rows_each = HEADS * ACT
    left = lax.broadcasted_iota(jnp.int32, (KEYS_PAD, LANES), 1) < rows_each
    left_row = lax.broadcasted_iota(jnp.int32, (1, LANES), 1) < rows_each
    rest = jnp.where((key >= OBS_FEW) & (key < OBS_FULL), 1.0, 0.0)
    padding = jnp.where(key > OBS_FULL, -1000000000.0, 0.0)

    def with_memory(s, sides):
        here = pl.ds(s, 4)
        wide = dot(mem[here].reshape(4 * KEYS_PAD, width), sides[here].reshape(4 * rows_each, width), NT)
        part = [wide[k * KEYS_PAD : (k + 1) * KEYS_PAD, (k // 2) * LANES : (k // 2 + 1) * LANES] for k in range(4)]
        return jnp.where(left, part[0], part[1]), jnp.where(left, part[2], part[3])

    def each_head(out, s, value):
        rows = pl.ds(pl.multiple_of(s * ACT, ACT), ACT)
        for h in range(HEADS):
            out[rows, pl.ds(h * width, width)] = value[h * ACT : (h + 1) * ACT, :]

    def attend(g, _):
        pairs = []
        for quad in range(GROUP // 4):
            pairs.extend(with_memory(g * GROUP + 4 * quad, queries))
        turned = []
        for k, score in enumerate(pairs):
            s = g * GROUP + 2 * k
            drop = [(1 - r.flags_s[s + side]).astype(F32) * -1000000000.0 for side in range(2)]
            score = score + (rest * jnp.where(left_row, drop[0], drop[1]) + padding)
            expo = jnp.exp(score - jnp.max(score, 0, keepdims=True))
            probs = expo * (1.0 / jnp.sum(expo, 0, keepdims=True))
            r.probs[g * (GROUP // 2) + k] = probs
            turned.append(probs.astype(BF16).T)
        for k, low in enumerate(turned):
            for side in range(2):
                s = g * GROUP + 2 * k + side
                each_head(r.u, s, dot(low[side * rows_each : (side + 1) * rows_each], mem[s]).astype(BF16))
        return 0

    lax.fori_loop(0, groups // 2, attend, 0)
    if remote:
        gather.fourth(2, 0, 1)
    lax.fori_loop(groups // 2, groups, attend, 0)
    if remote:
        gather.last(2, 0, 1)
        for m in range(3, 5):
            gather.unpack(SQ_AT[m], 1, sq, m)
        for m in range(2):
            gather.unpack(m * MLP_ROWS, 4, mlp, m)
    split_heads(wvh, sq[3])

    gain_acc = r.gain_acc
    gain_acc[...] = jnp.zeros_like(gain_acc)
    arrive(5)

    def feed(i, _):
        rows = pl.ds(pl.multiple_of(i * ROWS, ROWS), ROWS)
        mixed = dot(r.u[rows, :], wvh[...]).astype(BF16)
        r.mixed[rows, :] = mixed
        resid = r.acts_v[rows, :] + dot(mixed, sq[4])
        hat, scale = normalize(resid)
        second = (hat * g2).astype(BF16)
        r.second[rows, :] = second
        cot = r.cot_v[rows, :]
        out_low = cot.astype(BF16)
        r.out_low[rows, :] = out_low
        for c in range(wide // 256):
            columns = pl.ds(c * 256, 256)
            v = dot(second, mlp[0, :, columns])
            square = v * v
            t = jnp.tanh(0.7978845608 * (v + 0.044715 * square * v))
            r.active[rows, columns] = (0.5 * v * (1.0 + t)).astype(BF16)
            slope = 0.5 * (1.0 + t) + 0.5 * v * (1.0 - t * t) * (0.7978845608 * (1.0 + 0.134145 * square))
            r.dhidden[rows, columns] = (slope * dot(out_low, mlp[1, :, columns])).astype(BF16)
        r.out_v[rows, :] = resid + dot(r.active[rows, :], mlp[1], NT)
        grad_second = dot(r.dhidden[rows, :], mlp[0], NT)
        gain_acc[1:2, :] += jnp.sum(grad_second * hat, 0, keepdims=True)
        dres = cot + norm_back(grad_second * g2, hat, scale)
        r.dres[rows, :] = dres
        low = dres.astype(BF16)
        r.dres_low[rows, :] = low
        gm = dot(low, sq[4], NT).astype(BF16)
        r.dmixed[rows, :] = gm
        here = pl.ds(i * per, per)
        for h in range(HEADS):
            wv = wvh[pl.ds(h * width, width), :]
            dmixes[here, pl.ds(h * ACT, ACT), :] = dot(gm, wv, NT).astype(BF16).reshape(per, ACT, width)
        return 0

    lax.fori_loop(0, tokens // ROWS, feed, 0)
    keep_out = pltpu.make_async_copy(r.out_v, r.output, out_sems.at[0])
    keep_out.start()

    grads = r.grads

    def put(base, tiles, value):
        for j in range(tiles):
            part = value[:, j * LANES : (j + 1) * LANES].reshape(GRID + (TILE, LANES))
            grads[:, :, :, :, pl.ds(base + j * TILE, TILE), :] = part

    def by_head(left, right):
        turned = left.T
        parts = [
            dot(turned[h * head_dim : (h + 1) * head_dim, :], right[:, pl.ds(h * width, width)])
            for h in range(HEADS)
        ]
        return jnp.concatenate(parts, axis=0).T

    put(0, 8, dot(r.second[...], r.dhidden[...], TN))
    if remote:
        update.start(0)
    put(MLP_ROWS, 8, dot(r.out_low[...], r.active[...], TN))
    if remote:
        update.start(1)
    put(SQ_AT[4], 2, dot(r.mixed[...], r.dres_low[...], TN))
    put(SQ_AT[3], 2, by_head(r.dmixed[...], r.u))
    if remote:
        update.start(2)

    left_low = jnp.where(left_row, 1.0, 0.0).astype(BF16)
    right_low = jnp.where(left_row, 0.0, 1.0).astype(BF16)

    def attend_back(g, _):
        pairs = []
        for quad in range(GROUP // 4):
            pairs.extend(with_memory(g * GROUP + 4 * quad, dmixes))
        lows = []
        for k, rise in enumerate(pairs):
            probs = r.probs[g * (GROUP // 2) + k]
            both = probs * rise
            dscore = (both - probs * jnp.sum(both, 0, keepdims=True)).astype(BF16)
            lows.append((probs.astype(BF16), dscore, dscore.T))
        for k, (low, dscore, turned) in enumerate(lows):
            s = g * GROUP + 2 * k
            for side in range(2):
                dq = dot(turned[side * rows_each : (side + 1) * rows_each], mem[s + side]) * 0.125
                each_head(r.dq_wide, s + side, dq.astype(BF16))
            here = pl.ds(s, 2)
            sides = jnp.concatenate(
                [x[here].reshape(2 * rows_each, width) for x in (dmixes, queries)], axis=0
            )
            own = [jnp.concatenate([low * keep, dscore * keep], axis=1) for keep in (left_low, right_low)]
            dmem = dot(jnp.concatenate(own, axis=0), sides)
            for side in range(2):
                rows = dmem[side * KEYS_PAD : (side + 1) * KEYS_PAD, :]
                mem[s + side] = rows.astype(BF16)
                r.stamps[s + side] = rows[192:200, :]
        return 0

    half_groups = groups // 2
    lax.fori_loop(0, half_groups, attend_back, 0)
    if remote:
        update.one(0)
    lax.fori_loop(half_groups, groups, attend_back, 0)
    put(SQ_AT[2], 2, by_head(r.query[...], r.dq_wide))
    stamp_low = r.stamps[:, 4:5, :].reshape(samples, width).astype(BF16)
    put(SQ_AT[0], 2, dot(r.embed[...], stamp_low, TN))
    if remote:
        update.start(3)
        update.one(1, 2)

    def keep_og(part):
        here = pl.ds(part * batch, batch)
        return pltpu.make_async_copy(obs_v.at[pl.ds(0, keys), here], r.og.at[:, here], out_sems.at[2 + part])

    def turn_back(part):
        def one(j):
            at = pl.ds(pl.multiple_of(j * batch, batch), batch)
            here = pl.ds(part * batch, batch)
            block = mem[here, at, :].reshape(batch * batch, width)
            value = dot(swap[...], block).astype(BF16).reshape(batch, batch, width)
            obs_v[at, here, :] = value

        for j in range(chunks):
            one(j)
        keep_og(part).start()

    def queries_back(i, _):
        rows = pl.ds(pl.multiple_of(i * ROWS, ROWS), ROWS)
        r.dquery[rows, :] = dot(r.dq_wide[rows, :], wkh[...]).astype(BF16)
        return 0

    lax.fori_loop(0, tokens // ROWS, queries_back, 0)
    put(SQ_AT[1], 2, dot(r.first[...], r.dquery[...], TN))
    if remote:
        update.start(4)

    def acts_back(i, _):
        rows = pl.ds(pl.multiple_of(i * ROWS, ROWS), ROWS)
        grad_first = dot(r.dquery[rows, :], sq[1], NT)
        hat = r.xhat[rows, :]
        gain_acc[0:1, :] += jnp.sum(grad_first * hat, 0, keepdims=True)
        r.ag_v[rows, :] = r.dres[rows, :] + norm_back(grad_first * g1, hat, r.rstd[rows, :])
        return 0

    def finish_acts():
        lax.fori_loop(0, tokens // ROWS, acts_back, 0)
        for norm in range(2):
            for j in range(2):
                row = gain_acc[norm : norm + 1, j * LANES : (j + 1) * LANES]
                at = GAIN_BASE + norm * 2 + j
                value = jnp.broadcast_to(row.reshape(1, 1, 1, 1, 1, LANES), GRID + (1, LANES))
                grads[:, :, :, :, at : at + 1, :] = value
        rest = WIRE - GAIN_BASE - 4
        grads[:, :, :, :, GAIN_BASE + 4 : WIRE, :] = jnp.zeros(GRID + (rest, LANES), F32)

    keep_ag = pltpu.make_async_copy(r.ag_v, r.ag, out_sems.at[1])
    if remote:
        update.two(0)
        update.one(3)
        finish_acts()
        keep_ag.start()
        update.start(5)
        update.two(1, 2)
        update.one(4)
        update.two(3)
        update.one(5)
        update.three(0, 1)
        turn_back(0)
        update.two(4)
        update.three(2, 3, 4)
        update.two(5)
        update.four(0, 1)
        update.four(2, 3, 4)
        update.three(5)
        update.orthogonalize()
        update.give_all()
        turn_back(1)
        update.four(5)
        out = r.out
        out[1, :, :] = r.moment[...]
        out[2, pl.ds(GAIN_BASE, 16), :] = jnp.zeros((16, LANES), F32)
        gather.drain()
        update.drain()
        update.take_all()
        update.drain_owner()
    else:
        finish_acts()
        keep_ag.start()
        for part in range(samples // batch):
            turn_back(part)
    for copy in (keep_out, keep_ag, *(keep_og(part) for part in range(samples // batch))):
        copy.wait()


def block_and_back(remote, acts, obs, flags, levels, cot, sqw, mlpw, gain, sqm=None, mlpm=None):
    tokens, width = acts.shape
    keys, samples = obs.shape[0], obs.shape[1]
    rows = HEADS * ACT
    wide = mlpw.shape[2]
    any_space = pl.BlockSpec(memory_space=pl.ANY)
    in_vmem = pl.BlockSpec(memory_space=VMEM)
    sem = pltpu.SemaphoreType.DMA
    ins = dict(flags=flags, levels=levels, acts=acts, obs=obs, cot=cot, sqw=sqw, mlpw=mlpw, gain=gain)
    outs = dict(
        output=jax.ShapeDtypeStruct(acts.shape, F32),
        ag=jax.ShapeDtypeStruct(acts.shape, F32),
        og=jax.ShapeDtypeStruct(obs.shape, BF16),
    )
    grads = GRID + (WIRE, LANES)
    scratch = dict(
        obs_v=VMEM((KEYS_PAD, samples, width), BF16),
        acts_v=VMEM(acts.shape, F32),
        cot_v=VMEM(acts.shape, F32),
        mem=VMEM((samples, KEYS_PAD, width), BF16),
        swap=VMEM((256, 256), BF16),
        sq_all=VMEM((5, width, width), BF16),
        mlp_all=VMEM((2, width, wide), BF16),
        gain_all=VMEM((2, width), F32),
        wkh=VMEM((HEADS * width, width), BF16),
        wvh=VMEM((HEADS * width, width), BF16),
        first=VMEM((tokens, width), BF16),
        query=VMEM((tokens, width), BF16),
        xhat=VMEM((tokens, width), F32),
        rstd=VMEM((tokens, 1), F32),
        probs=VMEM((samples // 2, KEYS_PAD, LANES), F32),
        queries=VMEM((samples, rows, width), BF16),
        dmixes=VMEM((samples, rows, width), BF16),
        u=VMEM((tokens, HEADS * width), BF16),
        dq_wide=VMEM((tokens, HEADS * width), BF16),
        mixed=VMEM((tokens, width), BF16),
        second=VMEM((tokens, width), BF16),
        active=VMEM((tokens, wide), BF16),
        dhidden=VMEM((tokens, wide), BF16),
        out_low=VMEM((tokens, width), BF16),
        dres_low=VMEM((tokens, width), BF16),
        dres=VMEM((tokens, width), F32),
        dmixed=VMEM((tokens, width), BF16),
        dquery=VMEM((tokens, width), BF16),
        out_v=VMEM((tokens, width), F32),
        ag_v=VMEM((tokens, width), F32),
        angle=VMEM((samples, width // 2), F32),
        embed=VMEM((samples, width), BF16),
        stamps=VMEM((samples, 8, width), F32),
        gain_acc=VMEM((8, width), F32),
        flags_s=pltpu.SMEM(flags.shape, jnp.int32),
        levels_s=pltpu.SMEM(levels.shape, jnp.int32),
        in_sems=sem((10,)),
        out_sems=sem((2 + samples // 16,)),
    )
    extra = {}
    if remote:
        ins.update(sqm=sqm, mlpm=mlpm)
        outs.update(out=jax.ShapeDtypeStruct((3, WIRE, LANES), F32))
        chunks = len(CHUNKS)
        scratch.update(
            grads=VMEM(grads, F32),
            sqw_v=VMEM(sqw.shape, F32),
            mlpw_v=VMEM(mlpw.shape, F32),
            gain_v=VMEM(gain.shape, F32),
            sqm_v=VMEM(sqm.shape, F32),
            mlpm_v=VMEM(mlpm.shape, F32),
            wire=VMEM(grads, BF16),
            edge=VMEM((16, LANES), F32),
            gsend=sem((chunks, 6)),
            grecv=sem((chunks, 6)),
            send0=VMEM((4, 2, 2, WIRE, LANES), BF16),
            got_core=VMEM((4, 2, 2, WIRE, LANES), BF16),
            sum1=VMEM((4, 2, 2, WIRE, LANES), F32),
            send1=VMEM((4, 2, WIRE, LANES), BF16),
            got1=VMEM((4, 2, WIRE, LANES), BF16),
            sum2=VMEM((4, 2, WIRE, LANES), F32),
            send2=VMEM((4, WIRE, LANES), BF16),
            got2=VMEM((4, WIRE, LANES), BF16),
            sum3=VMEM((4, WIRE, LANES), F32),
            send3=VMEM((3, WIRE, LANES), BF16),
            got3=VMEM((3, WIRE, LANES), BF16),
            moment=VMEM((WIRE, LANES), F32),
            slabs_sq=VMEM((32, SQ_ROWS, LANES), F32),
            slabs_mlp=VMEM((32, MLP_ROWS, LANES), BF16),
            moment_low=VMEM((2 * MLP_ROWS, LANES), BF16),
            back_mlp=VMEM((2, MLP_ROWS, LANES), BF16),
            result_sq=VMEM((32, SQ_ROWS, LANES), F32),
            result_mlp=VMEM((32, MLP_ROWS, LANES), BF16),
            cur=VMEM((width, wide), F32),
            cur_low=VMEM((width, wide), BF16),
            send=sem((chunks, 6)),
            recv=sem((chunks, 6)),
            own_send=sem((7,)),
            own_recv=sem((1,)),
            back_send=sem((32,)),
            back_recv=sem((7,)),
        )
        extra = dict(collective_id=0, has_side_effects=True)
        outs = {name: VMEM(like.shape, like.dtype) for name, like in outs.items()}
    else:
        outs.update(grads=jax.ShapeDtypeStruct(grads, F32))
    names = tuple(ins) + tuple(outs) + tuple(scratch)
    stay = [pltpu.with_memory_space_constraint(value, pltpu.HBM) for value in ins.values()]
    results = pl.pallas_call(
        functools.partial(block_kernel, names, remote),
        out_shape=tuple(outs.values()),
        in_specs=[any_space] * len(ins),
        out_specs=[any_space] * 3 + [in_vmem],
        scratch_shapes=list(scratch.values()),
        compiler_params=pltpu.CompilerParams(vmem_limit_bytes=46 << 20, **extra),
        name="block_and_back",
    )(*stay)
    return Refs(zip(outs, results))


PARTS = 7


def finish_kernel(names, rate, *args):
    r = Refs(zip(names, args))
    sems = r.sems
    keys = r.og.shape[0]
    step = keys // PARTS

    def leave(part):
        block = pl.ds(part * step, step)
        return pltpu.make_async_copy(r.og_v.at[block], r.og.at[block], sems.at[part])

    more = PARTS
    moves = []
    if hasattr(r, "wire"):
        pairs = [(r.sqw, r.sqw_v), (r.mlpw, r.mlpw_v), (r.gain, r.gain_v), (r.gainm, r.gainm_v)]
        pairs += [(r.output, r.output_f), (r.ag, r.ag_f)]
        for source, target in pairs:
            moves.append(pltpu.make_async_copy(source, target, sems.at[more]))
            moves[-1].start()
            more += 1
    for part in range(PARTS):

        def widen(j, _):
            r.og_v[j] = r.low[j].astype(F32)
            return 0

        lax.fori_loop(part * step, (part + 1) * step, widen, 0, unroll=4)
        leave(part).start()
    for copy in moves[:4]:
        copy.wait()
    if hasattr(r, "wire"):
        finish_weights(r, rate)
    for part in range(PARTS):
        leave(part).wait()
    for copy in moves[4:]:
        copy.wait()


def finish_weights(r, rate):
    wire = r.wire
    me = lax.axis_index("dp")
    for m in range(5):
        for j in range(2):
            rows, columns = pl.ds(SQ_AT[m] + j * TILE, TILE), pl.ds(j * LANES, LANES)
            r.sqg[m, :, columns] = wire[0, rows, :]
            r.sqm[m, :, columns] = wire[1, rows, :]
            r.sqn[m, :, columns] = r.sqw_v[m, :, columns] - SQ_RATES[m] * wire[2, rows, :]
    r.sqc[...] = r.sqn[...].astype(BF16)
    for m in range(2):
        for j in range(8):
            rows, columns = pl.ds(m * MLP_ROWS + j * TILE, TILE), pl.ds(j * LANES, LANES)
            r.mlpg[m, :, columns] = wire[0, rows, :]
            r.mlpm[m, :, columns] = wire[1, rows, :]
            r.mlpn[m, :, columns] = r.mlpw_v[m, :, columns] - MLP_RATES[m] * wire[2, rows, :]
    r.mlpc[...] = r.mlpn[...].astype(BF16)
    tile = wire[0, pl.ds(GAIN_BASE, TILE), :]
    turned = pltpu.roll(tile, (LANES - (me % 16) * TILE) % LANES, 1)
    at = me // 16
    for norm in range(2):
        pair = turned[2 * norm : 2 * norm + 2, 0:TILE]
        row = jnp.where(at == 0, pair[0:1, :], pair[1:2, :])
        new = 0.5 * r.gainm_v[norm : norm + 1, :] + row
        r.gg[norm : norm + 1, :] = row
        r.gm[norm : norm + 1, :] = new
        r.gn[norm : norm + 1, :] = r.gain_v[norm : norm + 1, :] - rate * new


def finish(rate, made, sqw=None, mlpw=None, gain=None, gainm=None):
    any_space = pl.BlockSpec(memory_space=pl.ANY)
    in_vmem = pl.BlockSpec(memory_space=VMEM)
    ins = dict(low=made.og)
    outs = dict(og=jax.ShapeDtypeStruct(made.og.shape, F32))
    near, far = 1, 1
    if hasattr(made, "out"):
        ins.update(output=made.output, ag=made.ag, wire=made.out, sqw=sqw, mlpw=mlpw, gain=gain, gainm=gainm)
        like = jax.ShapeDtypeStruct
        near, far = 4, 3
        outs.update(
            output_f=like(made.output.shape, F32),
            ag_f=like(made.ag.shape, F32),
            sqg=like(sqw.shape, F32),
            sqm=like(sqw.shape, F32),
            sqn=like(sqw.shape, F32),
            sqc=like(sqw.shape, BF16),
            mlpg=like(mlpw.shape, F32),
            mlpm=like(mlpw.shape, F32),
            mlpn=like(mlpw.shape, F32),
            mlpc=like(mlpw.shape, BF16),
            gg=like(gain.shape, F32),
            gm=like(gain.shape, F32),
            gn=like(gain.shape, F32),
        )
    scratch = dict(
        og_v=VMEM(made.og.shape, F32),
        sems=pltpu.SemaphoreType.DMA((PARTS + 6,)),
    )
    if hasattr(made, "out"):
        scratch.update(
            sqw_v=VMEM(sqw.shape, F32),
            mlpw_v=VMEM(mlpw.shape, F32),
            gain_v=VMEM(gain.shape, F32),
            gainm_v=VMEM(gainm.shape, F32),
        )
    names = tuple(ins) + tuple(outs) + tuple(scratch)
    made_here = list(ins.values())
    stay = [pltpu.with_memory_space_constraint(value, pltpu.HBM) for value in made_here[near:]]
    results = pl.pallas_call(
        functools.partial(finish_kernel, names, rate),
        out_shape=tuple(outs.values()),
        in_specs=[in_vmem] * near + [any_space] * (len(ins) - near),
        out_specs=[any_space] * far + [in_vmem] * (len(outs) - far),
        scratch_shapes=list(scratch.values()),
        compiler_params=pltpu.CompilerParams(vmem_limit_bytes=16 << 20),
        name="finish",
    )(*made_here[:near], *stay)
    return Refs(zip(outs, results))


HIGH_PRECISION = lax.Precision.HIGHEST


def plain_orthogonalize(matrix):
    current = matrix / (jnp.sqrt(jnp.sum(matrix * matrix)) + 1e-07)
    for turn in range(5):
        gram = jnp.dot(current, current.T, precision=HIGH_PRECISION)
        poly = COEF_B * gram + COEF_C * jnp.dot(gram, gram, precision=HIGH_PRECISION)
        current = COEF_A * current + jnp.dot(poly, current, precision=HIGH_PRECISION)
    return current


def pick_owned(stack, owners, device):
    chosen = jnp.zeros_like(stack[0])
    for index in range(len(owners)):
        chosen = jnp.where(device == owners[index], stack[index], chosen)
    return chosen


def is_owner(owners, device):
    flag = device < 0
    for owner in owners:
        flag = jnp.logical_or(flag, device == owner)
    return flag


def from_wire(grads):
    def matrix(base, tiles):
        part = grads[:, base : base + tiles * TILE, :].reshape(-1, tiles, TILE, LANES)
        return part.transpose(0, 2, 1, 3).reshape(-1, tiles * LANES)

    square = jnp.stack([matrix(SQ_AT[m], 2) for m in range(5)])
    mlp = jnp.stack([matrix(m * MLP_ROWS, 8) for m in range(2)])
    return square, mlp, grads[0, GAIN_BASE : GAIN_BASE + 4, :].reshape(2, 2 * LANES)


def update_by_collectives(
    grads, square_weights, mlp_weights, gains, square_moment, mlp_moment, gain_moment, rate
):
    square_local, mlp_local, gain_local = from_wire(grads)
    square_grad, mlp_grad, gain_grad = (
        lax.psum_scatter(square_local, "dp", scatter_dimension=1, tiled=True),
        lax.psum_scatter(mlp_local, "dp", scatter_dimension=1, tiled=True),
        lax.psum_scatter(gain_local, "dp", scatter_dimension=1, tiled=True),
    )
    square_moment_new = 0.5 * square_moment + square_grad
    mlp_moment_new = 0.5 * mlp_moment + mlp_grad
    gain_moment_new = 0.5 * gain_moment + gain_grad
    device = lax.axis_index("dp")
    count = lax.axis_size("dp")
    square_owners = [index * count // 7 for index in range(5)]
    mlp_owners = [(index + 5) * count // 7 for index in range(2)]
    square_full, mlp_full = (
        lax.all_gather(square_moment_new, "dp", axis=1, tiled=True),
        lax.all_gather(mlp_moment_new, "dp", axis=1, tiled=True),
    )
    mine_square = pick_owned(square_full, square_owners, device)
    mine_mlp = pick_owned(mlp_full, mlp_owners, device)
    made_square = lax.cond(
        is_owner(square_owners, device), plain_orthogonalize, jnp.zeros_like, mine_square
    )
    made_mlp = lax.cond(is_owner(mlp_owners, device), plain_orthogonalize, jnp.zeros_like, mine_mlp)
    stack_square = jnp.stack(
        [jnp.where(device == owner, made_square, 0.0) for owner in square_owners]
    )
    stack_mlp = jnp.stack([jnp.where(device == owner, made_mlp, 0.0) for owner in mlp_owners])
    square_ortho, mlp_ortho = (
        lax.psum_scatter(stack_square, "dp", scatter_dimension=1, tiled=True),
        lax.psum_scatter(stack_mlp, "dp", scatter_dimension=1, tiled=True),
    )
    square_new = square_weights - jnp.array(SQ_RATES, F32)[:, None, None] * square_ortho
    mlp_new = mlp_weights - jnp.array(MLP_RATES, F32)[:, None, None] * mlp_ortho
    gains_new = gains - rate * gain_moment_new
    return (
        square_grad,
        square_moment_new,
        square_new,
        square_new.astype(BF16),
        mlp_grad,
        mlp_moment_new,
        mlp_new,
        mlp_new.astype(BF16),
        gain_grad,
        gain_moment_new,
        gains_new,
    )


def per_device(
    actions,
    observed,
    camera_flags,
    noise_levels,
    cotangent,
    square_weights,
    mlp_weights,
    gains,
    square_moment,
    mlp_moment,
    gain_moment,
):
    count = lax.axis_size("dp")
    rate = 0.1 / math.sqrt(actions.shape[0] * count)
    by_key = observed.transpose(1, 0, 2)
    ins = (actions, by_key, camera_flags, noise_levels, cotangent)
    if count == math.prod(GRID):
        made = block_and_back(True, *ins, square_weights, mlp_weights, gains, square_moment, mlp_moment)
        done = finish(rate, made, square_weights, mlp_weights, gains, gain_moment)
        output, actions_grad = done.output_f, done.ag_f
        d = done
        rest = (d.sqg, d.sqm, d.sqn, d.sqc, d.mlpg, d.mlpm, d.mlpn, d.mlpc, d.gg, d.gm, d.gn)
    else:
        square_all, mlp_all = (
            lax.all_gather(square_weights.astype(BF16), "dp", axis=1, tiled=True),
            lax.all_gather(mlp_weights.astype(BF16), "dp", axis=1, tiled=True),
        )
        gain_all = lax.all_gather(gains, "dp", axis=1, tiled=True)
        made = block_and_back(False, *ins, square_all, mlp_all, gain_all)
        done = finish(rate, made)
        output, actions_grad = made.output, made.ag
        grads = made.grads.reshape(-1, WIRE, LANES)
        rest = update_by_collectives(
            grads, square_weights, mlp_weights, gains, square_moment, mlp_moment, gain_moment, rate
        )
    observed_grad = done.og.transpose(1, 0, 2)
    return (output, actions_grad, observed_grad) + tuple(rest)


def solution(mesh):
    rows, cube, flat = P("dp", None), P("dp", None, None), P("dp")
    stacked, pair = P(None, "dp", None), P(None, "dp")
    return jax.shard_map(
        per_device,
        mesh=mesh,
        in_specs=(rows, cube, flat, flat, rows, stacked, stacked, pair, stacked, stacked, pair),
        out_specs=(rows, rows, cube) + (stacked,) * 8 + (pair,) * 3,
        check_vma=False,
    )
```

```python
import functools
import math

import jax
import jax.numpy as jnp
from jax import lax
from jax.experimental import pallas as pl
from jax.experimental.pallas import tpu as pltpu
from jax.sharding import PartitionSpec as P

HEADS = 4
ACT = 16
OBS_FULL = 196
OBS_FEW = 49
COEF_A = 3.4445
COEF_B = -4.775
COEF_C = 2.0315
F32 = jnp.float32
BF16 = jnp.bfloat16
MESH = pl.DeviceIdType.MESH
VMEM = pltpu.VMEM
NN = (((1,), (0,)), ((), ()))
NT = (((1,), (1,)), ((), ()))
TN = (((0,), (0,)), ((), ()))

LANES = 128
TILE = 8
MLP_ROWS = 64
SQ_ROWS = 16
SQ_AT = (160, 192, 176, 128, 144)
GAIN_BASE = 208
WIRE = 224
PIECES = ((0, 32), (32, 32), (64, 32), (96, 32), (128, 32), (160, 32), (192, 32))
PIECE_X_FIRST = (True, False, True, False, True, True, False)
CHUNKS = ((0, 32), (32, 32), (64, 32), (96, 32), (128, 32), (160, 32), (192, 16), (208, 16))
X_FIRST = (True, False, True, False, True, False, True, False)
PARTS_OUT = (
    (0, 0, 0, 32, 0),
    (1, 0, 32, 32, 32),
    (2, 1, 64, 32, 0),
    (3, 1, 96, 32, 32),
    (4, 5, 128, 16, 0),
    (4, 6, 144, 16, 0),
    (5, 2, 160, 16, 0),
    (5, 4, 176, 16, 0),
    (6, 3, 192, 16, 0),
)
MLP_RATES = (1.0, 0.5)
SQ_RATES = (0.5, 0.5, 0.5, 0.5, 4.0)
GRID = (4, 2, 2, 2)
OWNERS = (8, 22, 14, 16, 11, 21, 13)
SHIFTS = (0.0, 0.0, 0.4, 0.8, 0.8)
KEYS_PAD = 208
GROUP = 8
ROWS = 512


class Refs:
    def __init__(self, pairs):
        self.__dict__.update(pairs)


def dot(left, right, dims=NN):
    return lax.dot_general(left, right, dims, preferred_element_type=F32)


def place():
    me = lax.axis_index("dp")
    return me, me // 8, (me // 4) % 2, (me // 2) % 2, me % 2


def device_at(z, y, x, c):
    return ((z * 2 + y) * 2 + x) * 2 + c


def link(src, dst, send, recv, device):
    return pltpu.make_async_remote_copy(
        src_ref=src,
        dst_ref=dst,
        send_sem=send,
        recv_sem=recv,
        device_id=(device,),
        device_id_type=MESH,
    )


def greet(device):
    pl.semaphore_signal(
        pltpu.get_barrier_semaphore(), inc=1, device_id=(device,), device_id_type=MESH
    )


def normalize(values):
    centred = values - jnp.mean(values, -1, keepdims=True)
    scale = lax.rsqrt(jnp.mean(centred * centred, -1, keepdims=True) + 1e-05)
    return centred * scale, scale


def norm_back(grad, hat, scale):
    mean_one = jnp.mean(grad, -1, keepdims=True)
    mean_two = jnp.mean(grad * hat, -1, keepdims=True)
    return scale * (grad - mean_one - hat * mean_two)


class Gather:
    def __init__(self, r):
        self.r = r
        self.me, self.z, self.y, self.x, self.c = place()

    def hop(self, k, step, part, device):
        return link(part, part, self.r.gsend.at[k, step], self.r.grecv.at[k, step], device)

    def along_z(self, k, step):
        part = self.r.wire.at[self.z, self.y, self.x, self.c, pl.ds(*PIECES[k])]
        return self.hop(k, step, part, device_at((self.z + step + 1) % 4, self.y, self.x, self.c))

    def from_z(self, k, step):
        there = (self.z + 3 - step) % 4
        part = self.r.wire.at[there, self.y, self.x, self.c, pl.ds(*PIECES[k])]
        return self.hop(k, step, part, device_at(there, self.y, self.x, self.c))

    def plane(self, k, second, mine):
        z, y, x, c = self.z, self.y, self.x, self.c
        rows, wire = pl.ds(*PIECES[k]), self.r.wire
        py, px = (y, x) if mine else (1 - y, 1 - x)
        along_x = PIECE_X_FIRST[k] == second
        if along_x:
            part = wire.at[:, y, px, c, rows] if second else wire.at[:, :, px, c, rows]
            return self.hop(k, 3 if second else 4, part, device_at(z, y, 1 - x, c))
        part = wire.at[:, py, x, c, rows] if second else wire.at[:, py, :, c, rows]
        return self.hop(k, 3 if second else 4, part, device_at(z, 1 - y, x, c))

    def core(self, k, mine):
        part = self.r.wire.at[:, :, :, self.c if mine else 1 - self.c, pl.ds(*PIECES[k])]
        return self.hop(k, 5, part, device_at(self.z, self.y, self.x, 1 - self.c))

    def first(self, *chunks):
        for k in chunks:
            for step in range(3):
                self.along_z(k, step).start()

    def second(self, *chunks):
        for k in chunks:
            for step in range(3):
                self.from_z(k, step).wait_recv()
            self.plane(k, True, True).start()

    def third(self, *chunks):
        for k in chunks:
            self.plane(k, True, False).wait_recv()
            self.plane(k, False, True).start()

    def fourth(self, *chunks):
        for k in chunks:
            self.plane(k, False, False).wait_recv()
            self.core(k, True).start()

    def last(self, *chunks):
        for k in chunks:
            self.core(k, False).wait_recv()

    def drain(self):
        for k in range(len(PIECES)):
            for step in range(3):
                self.along_z(k, step).wait_send()
            self.plane(k, True, True).wait_send()
            self.plane(k, False, True).wait_send()
            self.core(k, True).wait_send()

    def fill(self):
        r = self.r
        spot = (self.z, self.y, self.x, self.c)

        def tiles(source, m, base, number):
            for j in range(number):
                pair = [source[m, :, pl.ds((2 * j + k) * LANES, LANES)] for k in range(2)]
                r.wire[spot + (pl.ds(base + j * 16, 16),)] = jnp.concatenate(pair, axis=0).astype(BF16)

        for m in range(5):
            tiles(r.sqw_v, m, SQ_AT[m], 1)
        for m in range(2):
            tiles(r.mlpw_v, m, m * MLP_ROWS, 4)
        gains, edge = r.gain_v[...], r.edge
        high = gains.astype(BF16).astype(F32)
        middle = (gains - high).astype(BF16).astype(F32)
        edge[...] = jnp.zeros_like(edge)
        edge[0:2, 0:TILE] = high
        edge[2:4, 0:TILE] = middle
        edge[4:6, 0:TILE] = (gains - high - middle).astype(BF16).astype(F32)
        r.wire[spot + (pl.ds(GAIN_BASE, 16),)] = edge[...].astype(BF16)

    def unpack(self, base, number, out, m):
        for j in range(number):
            block = self.r.wire[:, :, :, :, pl.ds(base + j * 16, 16), :].reshape(32, 16, LANES).astype(F32)
            for half in range(2):
                columns = pl.ds((2 * j + half) * LANES, LANES)
                out[m, :, columns] = block[:, half * 8 : half * 8 + 8, :].reshape(256, LANES).astype(BF16)

    def unpack_gains(self):
        edge, wire = self.r.edge, self.r.wire
        for half in range(2):
            total = jnp.zeros((16, LANES), F32)
            for at in range(16):
                d = half * 16 + at
                tile = wire[d // 8, (d // 4) % 2, (d // 2) % 2, d % 2, pl.ds(GAIN_BASE, 16), :].astype(F32)
                total = total + (tile if at == 0 else pltpu.roll(tile, at * TILE, 1))
            edge[...] = total
            self.r.gain_all[:, pl.ds(half * LANES, LANES)] = edge[0:2, :] + edge[2:4, :] + edge[4:6, :]


class Update:
    def __init__(self, r):
        self.r = r
        self.me, self.z, self.y, self.x, self.c = place()

    def hop(self, k, step, src, dst, device):
        return link(src, dst, self.r.send.at[k, step], self.r.recv.at[k, step], device)

    def core(self, k):
        rows = pl.ds(*CHUNKS[k])
        src, dst = self.r.send0.at[:, :, :, rows], self.r.got_core.at[:, :, :, rows]
        return self.hop(k, 0, src, dst, device_at(self.z, self.y, self.x, 1 - self.c))

    def plane(self, k, first):
        rows = pl.ds(*CHUNKS[k])
        to = (self.z, self.y, 1 - self.x, self.c) if X_FIRST[k] == first else (self.z, 1 - self.y, self.x, self.c)
        if first:
            src, dst = self.r.send1.at[:, :, rows], self.r.got1.at[:, :, rows]
        else:
            src, dst = self.r.send2.at[:, rows], self.r.got2.at[:, rows]
        return self.hop(k, 1 if first else 2, src, dst, device_at(*to))

    def along_z(self, k, step):
        rows = pl.ds(*CHUNKS[k])
        to = device_at((self.z + step + 1) % 4, self.y, self.x, self.c)
        return self.hop(k, 3 + step, self.r.send3.at[step, rows], self.r.got3.at[step, rows], to)

    def start(self, k):
        rows = pl.ds(*CHUNKS[k])
        self.r.send0[:, :, :, rows, :] = self.r.grads[:, :, :, 1 - self.c, rows, :].astype(BF16)
        self.core(k).start()

    def one(self, *chunks):
        r = self.r
        for k in chunks:
            rows = pl.ds(*CHUNKS[k])
            self.core(k).wait_recv()
            sum1 = r.sum1
            sum1[:, :, :, rows, :] = r.grads[:, :, :, self.c, rows, :] + r.got_core[:, :, :, rows, :].astype(F32)
            other = sum1[:, :, 1 - self.x, rows, :] if X_FIRST[k] else sum1[:, 1 - self.y, :, rows, :]
            r.send1[:, :, rows, :] = other.astype(BF16)
            self.plane(k, True).start()

    def two(self, *chunks):
        r = self.r
        for k in chunks:
            rows = pl.ds(*CHUNKS[k])
            self.plane(k, True).wait_recv()
            sum1, sum2 = r.sum1, r.sum2
            mine = sum1[:, :, self.x, rows, :] if X_FIRST[k] else sum1[:, self.y, :, rows, :]
            sum2[:, :, rows, :] = mine + r.got1[:, :, rows, :].astype(F32)
            other = 1 - self.y if X_FIRST[k] else 1 - self.x
            r.send2[:, rows, :] = sum2[:, other, rows, :].astype(BF16)
            self.plane(k, False).start()

    def three(self, *chunks):
        r = self.r
        for k in chunks:
            rows = pl.ds(*CHUNKS[k])
            self.plane(k, False).wait_recv()
            mine = self.y if X_FIRST[k] else self.x
            r.sum3[:, rows, :] = r.sum2[:, mine, rows, :] + r.got2[:, rows, :].astype(F32)
            for step in range(3):
                r.send3[step, rows, :] = r.sum3[(self.z + step + 1) % 4, rows, :].astype(BF16)
                self.along_z(k, step).start()

    def result(self, index):
        return self.r.result_mlp if index < 2 else self.r.result_sq

    def own_part(self, part):
        _, index, base, number, place = PARTS_OUT[part]
        if index < 2:
            return self.r.moment_low.at[pl.ds(base, number)], self.r.slabs_mlp.at[self.me, pl.ds(place, number)]
        return self.r.moment.at[pl.ds(base, number)], self.r.slabs_sq.at[self.me]

    def to_owner(self, part):
        src, dst = self.own_part(part)
        return link(src, dst, self.r.own_send.at[part], self.r.own_recv.at[0], OWNERS[PARTS_OUT[part][1]])

    def four(self, *chunks):
        r = self.r
        moment, out = r.moment, r.out
        for k in chunks:
            rows = pl.ds(*CHUNKS[k])
            total = r.sum3[self.z, rows, :]
            for step in range(3):
                self.along_z(k, step).wait_recv()
                total = total + r.got3[step, rows, :].astype(F32)
            out[0, rows, :] = total
            new = 0.5 * moment[rows, :] + total
            moment[rows, :] = new
            if k < 4:
                r.moment_low[rows, :] = new.astype(BF16)
            for part, (chunk, index, *_) in enumerate(PARTS_OUT):
                if chunk != k:
                    continue

                @pl.when(self.me != OWNERS[index])
                def _():
                    self.to_owner(part).start()

                @pl.when(self.me == OWNERS[index])
                def _():
                    src, dst = self.own_part(part)
                    pltpu.make_async_copy(src, dst, r.own_recv.at[0]).start()

    def old_moment(self):
        r = self.r
        moment = r.moment
        for m in range(2):
            for j in range(8):
                moment[pl.ds(m * MLP_ROWS + j * TILE, TILE), :] = r.mlpm_v[m, :, pl.ds(j * LANES, LANES)]
        for m in range(5):
            for j in range(2):
                moment[pl.ds(SQ_AT[m] + j * TILE, TILE), :] = r.sqm_v[m, :, pl.ds(j * LANES, LANES)]
        moment[pl.ds(GAIN_BASE, 16), :] = jnp.zeros((16, LANES), F32)

    def orthogonalize(self):
        r = self.r
        cur = r.cur
        rows = lax.broadcasted_iota(jnp.int32, (256, 256), 0)
        diagonal = rows == lax.broadcasted_iota(jnp.int32, (256, 256), 1)

        def run(slabs, result, tiles):
            pltpu.make_async_copy(slabs, slabs, r.own_recv.at[0]).wait()
            low = r.cur_low
            for j in range(tiles // 2):
                pair = slabs[:, pl.ds(j * 16, 16), :].astype(F32)
                for side in range(2):
                    columns = pl.ds((2 * j + side) * LANES, LANES)
                    part = pair[:, side * TILE : (side + 1) * TILE, :].reshape(256, LANES)
                    cur[:, columns] = part
                    low[:, columns] = part.astype(BF16)
            scale = 1.0
            for turn, shift in enumerate(SHIFTS):
                whole = low[:, 0 : tiles * LANES]
                off = dot(whole, whole, NT)
                if turn == 0:
                    norm = jnp.sum(jnp.sum(jnp.where(diagonal, off, 0.0), axis=0, keepdims=True), axis=1, keepdims=True)
                    scale = 1.0 / (jnp.sqrt(norm) + 1e-07)
                    off = off * (scale * scale)
                if shift:
                    off = off - jnp.where(diagonal, shift, 0.0)
                off_low = off.astype(BF16)
                poly = (COEF_B + 2.0 * COEF_C * shift) * off + COEF_C * dot(off_low, off_low)
                poly = poly.astype(BF16)
                keep = COEF_A + shift * (COEF_B + COEF_C * shift)
                for j in range(tiles // 2):
                    columns = pl.ds(j * 2 * LANES, 2 * LANES)
                    now = keep * cur[:, columns] + dot(poly, low[:, columns])
                    if turn == 0:
                        now = now * scale
                    if turn < len(SHIFTS) - 1:
                        cur[:, columns] = now
                        low[:, columns] = now.astype(BF16)
                    else:
                        parts = [now[:, side * LANES : (side + 1) * LANES].reshape(32, TILE, LANES) for side in range(2)]
                        result[:, pl.ds(j * 16, 16), :] = jnp.concatenate(parts, axis=1).astype(result.dtype)

        mine_mlp = jnp.logical_or(self.me == OWNERS[0], self.me == OWNERS[1])
        mine_sq = self.me < 0
        for device in OWNERS[2:]:
            mine_sq = jnp.logical_or(mine_sq, self.me == device)

        @pl.when(mine_mlp)
        def _():
            run(r.slabs_mlp, r.result_mlp, 8)

        @pl.when(mine_sq)
        def _():
            run(r.slabs_sq, r.result_sq, 2)

    def landing(self, index):
        if index < 2:
            return self.r.back_mlp.at[index]
        return self.r.out.at[2, pl.ds(SQ_AT[index - 2], SQ_ROWS)]

    def give_back(self, index, device):
        result = self.result(index)
        return link(
            result.at[device], self.landing(index),
            self.r.back_send.at[device], self.r.back_recv.at[index], device,
        )

    def give_all(self):
        r = self.r
        for index in range(7):
            result = self.result(index)

            @pl.when(self.me == OWNERS[index])
            def _():
                def send_one(step, _):
                    self.give_back(index, (self.me + step) % 32).start()
                    return 0

                lax.fori_loop(1, 32, send_one, 0)
                pltpu.make_async_copy(result.at[self.me], self.landing(index), r.back_recv.at[index]).start()

    def take_all(self):
        for index in range(7):
            result = self.result(index)
            pltpu.make_async_copy(result.at[0], self.landing(index), self.r.back_recv.at[index]).wait()
        for index in range(2):
            rows = pl.ds(index * MLP_ROWS, MLP_ROWS)
            self.r.out[2, rows, :] = self.r.back_mlp[index].astype(F32)

    def drain(self):
        for k in range(len(CHUNKS)):
            self.core(k).wait_send()
            self.plane(k, True).wait_send()
            self.plane(k, False).wait_send()
            for step in range(3):
                self.along_z(k, step).wait_send()
        for part in range(len(PARTS_OUT)):

            @pl.when(self.me != OWNERS[PARTS_OUT[part][1]])
            def _():
                self.to_owner(part).wait_send()

    def drain_owner(self):
        for index in range(7):

            @pl.when(self.me == OWNERS[index])
            def _():
                def wait_one(step, _):
                    self.give_back(index, (self.me + step) % 32).wait_send()
                    return 0

                lax.fori_loop(1, 32, wait_one, 0)


def greet_all():
    me, z, y, x, c = place()
    greet(device_at(z, y, x, 1 - c))
    greet(device_at(z, y, 1 - x, c))
    greet(device_at(z, 1 - y, x, c))
    for step in range(1, 4):
        greet(device_at((z + step) % 4, y, x, c))
    owner = me < 0
    for device in OWNERS:
        owner = jnp.logical_or(owner, me == device)

        @pl.when(me != device)
        def _():
            greet(device)

    @pl.when(owner)
    def _():
        def greet_other(step, _):
            greet((me + step) % 32)
            return 0

        lax.fori_loop(1, 32, greet_other, 0)

    is_owner = owner.astype(jnp.int32)
    return 6 + 7 - is_owner + 31 * is_owner


def block_kernel(names, remote, *args):
    r = Refs(zip(names, args))
    keys, samples = r.obs.shape[0], r.obs.shape[1]
    tokens, width = r.acts.shape
    head_dim, half, per = width // HEADS, width // 2, ROWS // ACT
    wide = r.mlp_all.shape[2]
    groups = samples // GROUP
    in_sems, out_sems = r.in_sems, r.out_sems

    if remote:
        own = (r.sqw_v, r.mlpw_v, r.gain_v)
    else:
        own = (r.sq_all, r.mlp_all, r.gain_all)
    loads = list(zip((r.sqw, r.mlpw, r.gain), own))
    loads += [(r.acts, r.acts_v), (r.obs, r.obs_v.at[pl.ds(0, keys)]), (r.cot, r.cot_v)]
    if remote:
        loads += [(r.sqm, r.sqm_v), (r.mlpm, r.mlpm_v)]
    loads += [(r.flags, r.flags_s), (r.levels, r.levels_s)]
    copies = [pltpu.make_async_copy(a, b, in_sems.at[i]) for i, (a, b) in enumerate(loads)]

    def arrive(*which):
        for i in which:
            copies[i].wait()

    for copy in copies:
        copy.start()
    if remote:
        gather, update = Gather(r), Update(r)
        expected = greet_all()
        arrive(0, 1, 2)
        gather.fill()
        pl.semaphore_wait(pltpu.get_barrier_semaphore(), expected)
        gather.first(5, 6)

    arrive(3)

    def hats(i, _):
        rows = pl.ds(pl.multiple_of(i * ROWS, ROWS), ROWS)
        hat, scale = normalize(r.acts_v[rows, :])
        r.xhat[rows, :] = hat
        r.rstd[rows, :] = scale
        return 0

    lax.fori_loop(0, tokens // ROWS, hats, 0)

    mem, obs_v = r.mem, r.obs_v
    batch = 16
    chunks = KEYS_PAD // batch
    swap = r.swap
    row = lax.broadcasted_iota(jnp.int32, swap.shape, 0)
    column = lax.broadcasted_iota(jnp.int32, swap.shape, 1)
    swap[...] = jnp.where(column == (row % batch) * batch + row // batch, 1.0, 0.0).astype(BF16)

    def turn(part, low, high):
        def one(j, _):
            at = pl.ds(pl.multiple_of(j * batch, batch), batch)
            here = pl.ds(part * batch, batch)
            block = obs_v[at, here, :].reshape(batch * batch, width)
            mem[here, at, :] = dot(swap[...], block).astype(BF16).reshape(batch, batch, width)
            return 0

        lax.fori_loop(low, high, one, 0, unroll=high - low)

    whole = chunks - 1
    arrive(4)
    turn(0, 0, whole // 2)
    if remote:
        gather.second(5, 6)
        gather.first(4, 0, 1, 2, 3)
    turn(0, whole // 2, whole)
    if remote:
        gather.third(5, 6)
    turn(1, 0, whole // 2)
    if remote:
        gather.second(4, 0, 1)
        gather.fourth(5, 6)
    turn(1, whole // 2, whole)
    if remote:
        gather.second(2, 3)
    arrive(len(copies) - 1, len(copies) - 2)
    freqs = jnp.exp(
        lax.broadcasted_iota(jnp.int32, (1, half), 1).astype(F32) * F32(-math.log(10000.0)) / half
    )
    for s in range(samples):
        r.angle[s : s + 1, :] = r.levels_s[s].astype(F32) * freqs
    r.embed[:, 0:half] = jnp.sin(r.angle[...]).astype(BF16)
    r.embed[:, half:width] = jnp.cos(r.angle[...]).astype(BF16)
    if remote:
        arrive(6, 7)
        update.old_moment()
        gather.third(4, 0, 1)
        gather.last(5, 6)
        for m in range(3):
            gather.unpack(SQ_AT[m], 1, r.sq_all, m)
        gather.unpack_gains()
    else:
        arrive(0, 1, 2)

    sq, mlp = r.sq_all, r.mlp_all
    wkh, wvh = r.wkh, r.wvh
    lane = lax.broadcasted_iota(jnp.int32, (width, width), 1)

    def split_heads(out, weight):
        weight = weight.astype(F32)
        for h in range(HEADS):
            out[pl.ds(h * width, width), :] = jnp.where(lane // head_dim == h, weight, 0.0).astype(BF16)

    split_heads(wkh, sq[2])
    g1, g2 = r.gain_all[0:1, :], r.gain_all[1:2, :]

    obs_v[keys] = dot(r.embed[...], sq[0]).astype(BF16)
    obs_v[keys + 1 :] = jnp.zeros((KEYS_PAD - keys - 1, samples, width), BF16)
    for part in range(samples // batch):
        turn(part, whole, chunks)

    queries, dmixes = r.queries, r.dmixes

    def make_queries(i, _):
        rows = pl.ds(pl.multiple_of(i * ROWS, ROWS), ROWS)
        first = (r.xhat[rows, :] * g1).astype(BF16)
        r.first[rows, :] = first
        q = dot(first, sq[1]).astype(BF16)
        r.query[rows, :] = q
        here = pl.ds(i * per, per)
        for h in range(HEADS):
            wk = wkh[pl.ds(h * width, width), :]
            value = (dot(q, wk, NT) * 0.125).astype(BF16).reshape(per, ACT, width)
            queries[here, pl.ds(h * ACT, ACT), :] = value
        return 0

    lax.fori_loop(0, tokens // ROWS, make_queries, 0)

    key = lax.broadcasted_iota(jnp.int32, (KEYS_PAD, LANES), 0)
    rows_each = HEADS * ACT
    left = lax.broadcasted_iota(jnp.int32, (KEYS_PAD, LANES), 1) < rows_each
    left_row = lax.broadcasted_iota(jnp.int32, (1, LANES), 1) < rows_each
    rest = jnp.where((key >= OBS_FEW) & (key < OBS_FULL), 1.0, 0.0)
    padding = jnp.where(key > OBS_FULL, -1000000000.0, 0.0)

    def with_memory(s, sides):
        here = pl.ds(s, 4)
        wide = dot(mem[here].reshape(4 * KEYS_PAD, width), sides[here].reshape(4 * rows_each, width), NT)
        part = [wide[k * KEYS_PAD : (k + 1) * KEYS_PAD, (k // 2) * LANES : (k // 2 + 1) * LANES] for k in range(4)]
        return jnp.where(left, part[0], part[1]), jnp.where(left, part[2], part[3])

    def each_head(out, s, value):
        rows = pl.ds(pl.multiple_of(s * ACT, ACT), ACT)
        for h in range(HEADS):
            out[rows, pl.ds(h * width, width)] = value[h * ACT : (h + 1) * ACT, :]

    def attend(g, _):
        pairs = []
        for quad in range(GROUP // 4):
            pairs.extend(with_memory(g * GROUP + 4 * quad, queries))
        turned = []
        for k, score in enumerate(pairs):
            s = g * GROUP + 2 * k
            drop = [(1 - r.flags_s[s + side]).astype(F32) * -1000000000.0 for side in range(2)]
            score = score + (rest * jnp.where(left_row, drop[0], drop[1]) + padding)
            expo = jnp.exp(score - jnp.max(score, 0, keepdims=True))
            probs = expo * (1.0 / jnp.sum(expo, 0, keepdims=True))
            r.probs[g * (GROUP // 2) + k] = probs
            turned.append(probs.astype(BF16).T)
        for k, low in enumerate(turned):
            for side in range(2):
                s = g * GROUP + 2 * k + side
                each_head(r.u, s, dot(low[side * rows_each : (side + 1) * rows_each], mem[s]).astype(BF16))
        return 0

    lax.fori_loop(0, 1, attend, 0)
    if remote:
        gather.third(2, 3)
    lax.fori_loop(1, 2, attend, 0)
    if remote:
        gather.fourth(4, 0, 1)
    lax.fori_loop(2, groups, attend, 0)
    if remote:
        gather.fourth(2, 3)
        gather.last(4)
        for m in range(3, 5):
            gather.unpack(SQ_AT[m], 1, sq, m)
    split_heads(wvh, sq[3])

    gain_acc = r.gain_acc
    gain_acc[...] = jnp.zeros_like(gain_acc)
    blocks = [pl.ds(i * ROWS, ROWS) for i in range(tokens // ROWS)]
    for rows in blocks:
        mixed = dot(r.u[rows, :], wvh[...]).astype(BF16)
        r.mixed[rows, :] = mixed
        resid = r.acts_v[rows, :] + dot(mixed, sq[4])
        r.resid[rows, :] = resid
        hat, scale = normalize(resid)
        r.hat_two[rows, :] = hat
        r.rstd_two[rows, :] = scale
        r.second[rows, :] = (hat * g2).astype(BF16)
    arrive(5)
    r.out_low[...] = r.cot_v[...].astype(BF16)
    if remote:
        gather.last(0, 1)
        gather.unpack(0, 4, mlp, 0)
    wide_blocks = [pl.ds(c * 256, 256) for c in range(wide // 256)]
    for rows in blocks:
        for columns in wide_blocks:
            v = dot(r.second[rows, :], mlp[0, :, columns])
            square = v * v
            t = jnp.tanh(0.7978845608 * (v + 0.044715 * square * v))
            r.active[rows, columns] = (0.5 * v * (1.0 + t)).astype(BF16)
            slope = 0.5 * (1.0 + t) + 0.5 * v * (1.0 - t * t) * (0.7978845608 * (1.0 + 0.134145 * square))
            r.slope[rows, columns] = slope

    grads = r.grads

    def put(base, tiles, value):
        for j in range(tiles):
            part = value[:, j * LANES : (j + 1) * LANES].reshape(GRID + (TILE, LANES))
            grads[:, :, :, :, pl.ds(base + j * TILE, TILE), :] = part

    def by_head(left, right):
        turned = left.T
        parts = [
            dot(turned[h * head_dim : (h + 1) * head_dim, :], right[:, pl.ds(h * width, width)])
            for h in range(HEADS)
        ]
        return jnp.concatenate(parts, axis=0).T

    put(MLP_ROWS, 8, dot(r.out_low[...], r.active[...], TN))
    if remote:
        update.start(2)
        update.start(3)
        gather.last(2, 3)
        gather.unpack(MLP_ROWS, 4, mlp, 1)
    for rows in blocks:
        for columns in wide_blocks:
            slope = r.slope[rows, columns]
            r.dhidden[rows, columns] = (slope * dot(r.out_low[rows, :], mlp[1, :, columns])).astype(BF16)
    put(0, 8, dot(r.second[...], r.dhidden[...], TN))
    if remote:
        update.start(0)
        update.start(1)
        update.one(2, 3)
    for i, rows in enumerate(blocks):
        r.out_v[rows, :] = r.resid[rows, :] + dot(r.active[rows, :], mlp[1], NT)
        grad_second = dot(r.dhidden[rows, :], mlp[0], NT)
        hat = r.hat_two[rows, :]
        gain_acc[1:2, :] += jnp.sum(grad_second * hat, 0, keepdims=True)
        dres = r.cot_v[rows, :] + norm_back(grad_second * g2, hat, r.rstd_two[rows, :])
        r.dres[rows, :] = dres
        low = dres.astype(BF16)
        r.dres_low[rows, :] = low
        gm = dot(low, sq[4], NT).astype(BF16)
        r.dmixed[rows, :] = gm
        here = pl.ds(i * per, per)
        for h in range(HEADS):
            wv = wvh[pl.ds(h * width, width), :]
            dmixes[here, pl.ds(h * ACT, ACT), :] = dot(gm, wv, NT).astype(BF16).reshape(per, ACT, width)
    keep_out = pltpu.make_async_copy(r.out_v, r.output, out_sems.at[0])
    keep_out.start()
    if remote:
        update.one(0, 1)
    put(SQ_AT[4], 2, dot(r.mixed[...], r.dres_low[...], TN))
    put(SQ_AT[3], 2, by_head(r.dmixed[...], r.u))
    if remote:
        update.start(4)

    left_low = jnp.where(left_row, 1.0, 0.0).astype(BF16)
    right_low = jnp.where(left_row, 0.0, 1.0).astype(BF16)

    def attend_back(g, _):
        pairs = []
        for quad in range(GROUP // 4):
            pairs.extend(with_memory(g * GROUP + 4 * quad, dmixes))
        lows = []
        for k, rise in enumerate(pairs):
            probs = r.probs[g * (GROUP // 2) + k]
            both = probs * rise
            dscore = (both - probs * jnp.sum(both, 0, keepdims=True)).astype(BF16)
            lows.append((probs.astype(BF16), dscore, dscore.T))
        for k, (low, dscore, turned) in enumerate(lows):
            s = g * GROUP + 2 * k
            for side in range(2):
                dq = dot(turned[side * rows_each : (side + 1) * rows_each], mem[s + side]) * 0.125
                each_head(r.dq_wide, s + side, dq.astype(BF16))
            here = pl.ds(s, 2)
            sides = jnp.concatenate(
                [x[here].reshape(2 * rows_each, width) for x in (dmixes, queries)], axis=0
            )
            own = [jnp.concatenate([low * keep, dscore * keep], axis=1) for keep in (left_low, right_low)]
            dmem = dot(jnp.concatenate(own, axis=0), sides)
            for side in range(2):
                rows = dmem[side * KEYS_PAD : (side + 1) * KEYS_PAD, :]
                mem[s + side] = rows.astype(BF16)
                r.stamps[s + side] = rows[192:200, :]
        return 0

    lax.fori_loop(0, 1, attend_back, 0)
    if remote:
        update.two(2, 3)
    lax.fori_loop(1, 2, attend_back, 0)
    if remote:
        update.one(4)
        update.two(0, 1)
    lax.fori_loop(2, groups - 1, attend_back, 0)
    if remote:
        update.three(2, 3)
    lax.fori_loop(groups - 1, groups, attend_back, 0)
    if remote:
        update.two(4)
        update.three(0, 1)
    put(SQ_AT[2], 2, by_head(r.query[...], r.dq_wide))
    stamp_low = r.stamps[:, 4:5, :].reshape(samples, width).astype(BF16)
    put(SQ_AT[0], 2, dot(r.embed[...], stamp_low, TN))
    if remote:
        update.start(5)
        update.four(2, 3)

    def keep_og(part):
        here = pl.ds(part * batch, batch)
        return pltpu.make_async_copy(obs_v.at[pl.ds(0, keys), here], r.og.at[:, here], out_sems.at[2 + part])

    def turn_back(part):
        def one(j):
            at = pl.ds(pl.multiple_of(j * batch, batch), batch)
            here = pl.ds(part * batch, batch)
            block = mem[here, at, :].reshape(batch * batch, width)
            value = dot(swap[...], block).astype(BF16).reshape(batch, batch, width)
            obs_v[at, here, :] = value

        for j in range(chunks):
            one(j)
        keep_og(part).start()

    def queries_back(i, _):
        rows = pl.ds(pl.multiple_of(i * ROWS, ROWS), ROWS)
        r.dquery[rows, :] = dot(r.dq_wide[rows, :], wkh[...]).astype(BF16)
        return 0

    lax.fori_loop(0, tokens // ROWS, queries_back, 0)
    put(SQ_AT[1], 2, dot(r.first[...], r.dquery[...], TN))
    if remote:
        update.start(6)
        update.three(4)
        update.one(5)

    def acts_back(i, _):
        rows = pl.ds(pl.multiple_of(i * ROWS, ROWS), ROWS)
        grad_first = dot(r.dquery[rows, :], sq[1], NT)
        hat = r.xhat[rows, :]
        gain_acc[0:1, :] += jnp.sum(grad_first * hat, 0, keepdims=True)
        r.ag_v[rows, :] = r.dres[rows, :] + norm_back(grad_first * g1, hat, r.rstd[rows, :])
        return 0

    def finish_acts():
        lax.fori_loop(0, tokens // ROWS, acts_back, 0)
        for norm in range(2):
            for j in range(2):
                row = gain_acc[norm : norm + 1, j * LANES : (j + 1) * LANES]
                at = GAIN_BASE + norm * 2 + j
                value = jnp.broadcast_to(row.reshape(1, 1, 1, 1, 1, LANES), GRID + (1, LANES))
                grads[:, :, :, :, at : at + 1, :] = value
        rest = WIRE - GAIN_BASE - 4
        grads[:, :, :, :, GAIN_BASE + 4 : WIRE, :] = jnp.zeros(GRID + (rest, LANES), F32)

    keep_ag = pltpu.make_async_copy(r.ag_v, r.ag, out_sems.at[1])
    if remote:
        finish_acts()
        keep_ag.start()
        update.start(7)
        update.one(6)
        update.four(0, 1)
        update.two(5)
        update.one(7)
        turn_back(0)
        update.two(6)
        update.three(5)
        update.two(7)
        update.four(4)
        update.three(6)
        update.four(5)
        update.three(7)
        update.four(6)
        update.orthogonalize()
        update.give_all()
        turn_back(1)
        update.four(7)
        out = r.out
        out[1, :, :] = r.moment[...]
        out[2, pl.ds(GAIN_BASE, 16), :] = jnp.zeros((16, LANES), F32)
        gather.drain()
        update.drain()
        update.take_all()
        update.drain_owner()
    else:
        finish_acts()
        keep_ag.start()
        for part in range(samples // batch):
            turn_back(part)
    for copy in (keep_out, keep_ag, *(keep_og(part) for part in range(samples // batch))):
        copy.wait()


def block_and_back(remote, acts, obs, flags, levels, cot, sqw, mlpw, gain, sqm=None, mlpm=None):
    tokens, width = acts.shape
    keys, samples = obs.shape[0], obs.shape[1]
    rows = HEADS * ACT
    wide = mlpw.shape[2]
    any_space = pl.BlockSpec(memory_space=pl.ANY)
    in_vmem = pl.BlockSpec(memory_space=VMEM)
    sem = pltpu.SemaphoreType.DMA
    ins = dict(flags=flags, levels=levels, acts=acts, obs=obs, cot=cot, sqw=sqw, mlpw=mlpw, gain=gain)
    outs = dict(
        output=jax.ShapeDtypeStruct(acts.shape, F32),
        ag=jax.ShapeDtypeStruct(acts.shape, F32),
        og=jax.ShapeDtypeStruct(obs.shape, BF16),
    )
    grads = GRID + (WIRE, LANES)
    scratch = dict(
        obs_v=VMEM((KEYS_PAD, samples, width), BF16),
        acts_v=VMEM(acts.shape, F32),
        cot_v=VMEM(acts.shape, F32),
        mem=VMEM((samples, KEYS_PAD, width), BF16),
        swap=VMEM((256, 256), BF16),
        sq_all=VMEM((5, width, width), BF16),
        mlp_all=VMEM((2, width, wide), BF16),
        gain_all=VMEM((2, width), F32),
        wkh=VMEM((HEADS * width, width), BF16),
        wvh=VMEM((HEADS * width, width), BF16),
        first=VMEM((tokens, width), BF16),
        query=VMEM((tokens, width), BF16),
        xhat=VMEM((tokens, width), F32),
        rstd=VMEM((tokens, 1), F32),
        probs=VMEM((samples // 2, KEYS_PAD, LANES), F32),
        queries=VMEM((samples, rows, width), BF16),
        dmixes=VMEM((samples, rows, width), BF16),
        u=VMEM((tokens, HEADS * width), BF16),
        dq_wide=VMEM((tokens, HEADS * width), BF16),
        mixed=VMEM((tokens, width), BF16),
        second=VMEM((tokens, width), BF16),
        active=VMEM((tokens, wide), BF16),
        dhidden=VMEM((tokens, wide), BF16),
        out_low=VMEM((tokens, width), BF16),
        dres_low=VMEM((tokens, width), BF16),
        dres=VMEM((tokens, width), F32),
        resid=VMEM((tokens, width), F32),
        hat_two=VMEM((tokens, width), F32),
        rstd_two=VMEM((tokens, 1), F32),
        slope=VMEM((tokens, wide), F32),
        dmixed=VMEM((tokens, width), BF16),
        dquery=VMEM((tokens, width), BF16),
        out_v=VMEM((tokens, width), F32),
        ag_v=VMEM((tokens, width), F32),
        angle=VMEM((samples, width // 2), F32),
        embed=VMEM((samples, width), BF16),
        stamps=VMEM((samples, 8, width), F32),
        gain_acc=VMEM((8, width), F32),
        flags_s=pltpu.SMEM(flags.shape, jnp.int32),
        levels_s=pltpu.SMEM(levels.shape, jnp.int32),
        in_sems=sem((10,)),
        out_sems=sem((2 + samples // 16,)),
    )
    extra = {}
    if remote:
        ins.update(sqm=sqm, mlpm=mlpm)
        outs.update(out=jax.ShapeDtypeStruct((3, WIRE, LANES), F32))
        chunks = len(CHUNKS)
        scratch.update(
            grads=VMEM(grads, F32),
            sqw_v=VMEM(sqw.shape, F32),
            mlpw_v=VMEM(mlpw.shape, F32),
            gain_v=VMEM(gain.shape, F32),
            sqm_v=VMEM(sqm.shape, F32),
            mlpm_v=VMEM(mlpm.shape, F32),
            wire=VMEM(grads, BF16),
            edge=VMEM((16, LANES), F32),
            gsend=sem((len(PIECES), 6)),
            grecv=sem((len(PIECES), 6)),
            send0=VMEM((4, 2, 2, WIRE, LANES), BF16),
            got_core=VMEM((4, 2, 2, WIRE, LANES), BF16),
            sum1=VMEM((4, 2, 2, WIRE, LANES), F32),
            send1=VMEM((4, 2, WIRE, LANES), BF16),
            got1=VMEM((4, 2, WIRE, LANES), BF16),
            sum2=VMEM((4, 2, WIRE, LANES), F32),
            send2=VMEM((4, WIRE, LANES), BF16),
            got2=VMEM((4, WIRE, LANES), BF16),
            sum3=VMEM((4, WIRE, LANES), F32),
            send3=VMEM((3, WIRE, LANES), BF16),
            got3=VMEM((3, WIRE, LANES), BF16),
            moment=VMEM((WIRE, LANES), F32),
            slabs_sq=VMEM((32, SQ_ROWS, LANES), F32),
            slabs_mlp=VMEM((32, MLP_ROWS, LANES), BF16),
            moment_low=VMEM((2 * MLP_ROWS, LANES), BF16),
            back_mlp=VMEM((2, MLP_ROWS, LANES), BF16),
            result_sq=VMEM((32, SQ_ROWS, LANES), F32),
            result_mlp=VMEM((32, MLP_ROWS, LANES), BF16),
            cur=VMEM((width, wide), F32),
            cur_low=VMEM((width, wide), BF16),
            send=sem((chunks, 6)),
            recv=sem((chunks, 6)),
            own_send=sem((len(PARTS_OUT),)),
            own_recv=sem((1,)),
            back_send=sem((32,)),
            back_recv=sem((7,)),
        )
        extra = dict(collective_id=0, has_side_effects=True)
        outs = {name: VMEM(like.shape, like.dtype) for name, like in outs.items()}
    else:
        outs.update(grads=jax.ShapeDtypeStruct(grads, F32))
    names = tuple(ins) + tuple(outs) + tuple(scratch)
    stay = [pltpu.with_memory_space_constraint(value, pltpu.HBM) for value in ins.values()]
    results = pl.pallas_call(
        functools.partial(block_kernel, names, remote),
        out_shape=tuple(outs.values()),
        in_specs=[any_space] * len(ins),
        out_specs=[any_space] * 3 + [in_vmem],
        scratch_shapes=list(scratch.values()),
        compiler_params=pltpu.CompilerParams(vmem_limit_bytes=50 << 20, **extra),
        name="block_and_back",
    )(*stay)
    return Refs(zip(outs, results))


PARTS = 7


def finish_kernel(names, rate, *args):
    r = Refs(zip(names, args))
    sems = r.sems
    keys = r.og.shape[0]
    step = keys // PARTS

    def leave(part):
        block = pl.ds(part * step, step)
        return pltpu.make_async_copy(r.og_v.at[block], r.og.at[block], sems.at[part])

    more = PARTS
    moves = []
    if hasattr(r, "wire"):
        pairs = [(r.sqw, r.sqw_v), (r.mlpw, r.mlpw_v), (r.gain, r.gain_v), (r.gainm, r.gainm_v)]
        pairs += [(r.output, r.output_f), (r.ag, r.ag_f)]
        for source, target in pairs:
            moves.append(pltpu.make_async_copy(source, target, sems.at[more]))
            moves[-1].start()
            more += 1
    for part in range(PARTS):

        def widen(j, _):
            r.og_v[j] = r.low[j].astype(F32)
            return 0

        lax.fori_loop(part * step, (part + 1) * step, widen, 0, unroll=4)
        leave(part).start()
    for copy in moves[:4]:
        copy.wait()
    if hasattr(r, "wire"):
        finish_weights(r, rate)
    for part in range(PARTS):
        leave(part).wait()
    for copy in moves[4:]:
        copy.wait()


def finish_weights(r, rate):
    wire = r.wire
    me = lax.axis_index("dp")
    for m in range(5):
        for j in range(2):
            rows, columns = pl.ds(SQ_AT[m] + j * TILE, TILE), pl.ds(j * LANES, LANES)
            r.sqg[m, :, columns] = wire[0, rows, :]
            r.sqm[m, :, columns] = wire[1, rows, :]
            r.sqn[m, :, columns] = r.sqw_v[m, :, columns] - SQ_RATES[m] * wire[2, rows, :]
    r.sqc[...] = r.sqn[...].astype(BF16)
    for m in range(2):
        for j in range(8):
            rows, columns = pl.ds(m * MLP_ROWS + j * TILE, TILE), pl.ds(j * LANES, LANES)
            r.mlpg[m, :, columns] = wire[0, rows, :]
            r.mlpm[m, :, columns] = wire[1, rows, :]
            r.mlpn[m, :, columns] = r.mlpw_v[m, :, columns] - MLP_RATES[m] * wire[2, rows, :]
    r.mlpc[...] = r.mlpn[...].astype(BF16)
    tile = wire[0, pl.ds(GAIN_BASE, TILE), :]
    turned = pltpu.roll(tile, (LANES - (me % 16) * TILE) % LANES, 1)
    at = me // 16
    for norm in range(2):
        pair = turned[2 * norm : 2 * norm + 2, 0:TILE]
        row = jnp.where(at == 0, pair[0:1, :], pair[1:2, :])
        new = 0.5 * r.gainm_v[norm : norm + 1, :] + row
        r.gg[norm : norm + 1, :] = row
        r.gm[norm : norm + 1, :] = new
        r.gn[norm : norm + 1, :] = r.gain_v[norm : norm + 1, :] - rate * new


def finish(rate, made, sqw=None, mlpw=None, gain=None, gainm=None):
    any_space = pl.BlockSpec(memory_space=pl.ANY)
    in_vmem = pl.BlockSpec(memory_space=VMEM)
    ins = dict(low=made.og)
    outs = dict(og=jax.ShapeDtypeStruct(made.og.shape, F32))
    near, far = 1, 1
    if hasattr(made, "out"):
        ins.update(output=made.output, ag=made.ag, wire=made.out, sqw=sqw, mlpw=mlpw, gain=gain, gainm=gainm)
        like = jax.ShapeDtypeStruct
        near, far = 4, 3
        outs.update(
            output_f=like(made.output.shape, F32),
            ag_f=like(made.ag.shape, F32),
            sqg=like(sqw.shape, F32),
            sqm=like(sqw.shape, F32),
            sqn=like(sqw.shape, F32),
            sqc=like(sqw.shape, BF16),
            mlpg=like(mlpw.shape, F32),
            mlpm=like(mlpw.shape, F32),
            mlpn=like(mlpw.shape, F32),
            mlpc=like(mlpw.shape, BF16),
            gg=like(gain.shape, F32),
            gm=like(gain.shape, F32),
            gn=like(gain.shape, F32),
        )
    scratch = dict(
        og_v=VMEM(made.og.shape, F32),
        sems=pltpu.SemaphoreType.DMA((PARTS + 6,)),
    )
    if hasattr(made, "out"):
        scratch.update(
            sqw_v=VMEM(sqw.shape, F32),
            mlpw_v=VMEM(mlpw.shape, F32),
            gain_v=VMEM(gain.shape, F32),
            gainm_v=VMEM(gainm.shape, F32),
        )
    names = tuple(ins) + tuple(outs) + tuple(scratch)
    made_here = list(ins.values())
    stay = [pltpu.with_memory_space_constraint(value, pltpu.HBM) for value in made_here[near:]]
    results = pl.pallas_call(
        functools.partial(finish_kernel, names, rate),
        out_shape=tuple(outs.values()),
        in_specs=[in_vmem] * near + [any_space] * (len(ins) - near),
        out_specs=[any_space] * far + [in_vmem] * (len(outs) - far),
        scratch_shapes=list(scratch.values()),
        compiler_params=pltpu.CompilerParams(vmem_limit_bytes=16 << 20),
        name="finish",
    )(*made_here[:near], *stay)
    return Refs(zip(outs, results))


HIGH_PRECISION = lax.Precision.HIGHEST


def plain_orthogonalize(matrix):
    current = matrix / (jnp.sqrt(jnp.sum(matrix * matrix)) + 1e-07)
    for turn in range(5):
        gram = jnp.dot(current, current.T, precision=HIGH_PRECISION)
        poly = COEF_B * gram + COEF_C * jnp.dot(gram, gram, precision=HIGH_PRECISION)
        current = COEF_A * current + jnp.dot(poly, current, precision=HIGH_PRECISION)
    return current


def pick_owned(stack, owners, device):
    chosen = jnp.zeros_like(stack[0])
    for index in range(len(owners)):
        chosen = jnp.where(device == owners[index], stack[index], chosen)
    return chosen


def is_owner(owners, device):
    flag = device < 0
    for owner in owners:
        flag = jnp.logical_or(flag, device == owner)
    return flag


def from_wire(grads):
    def matrix(base, tiles):
        part = grads[:, base : base + tiles * TILE, :].reshape(-1, tiles, TILE, LANES)
        return part.transpose(0, 2, 1, 3).reshape(-1, tiles * LANES)

    square = jnp.stack([matrix(SQ_AT[m], 2) for m in range(5)])
    mlp = jnp.stack([matrix(m * MLP_ROWS, 8) for m in range(2)])
    return square, mlp, grads[0, GAIN_BASE : GAIN_BASE + 4, :].reshape(2, 2 * LANES)


def update_by_collectives(
    grads, square_weights, mlp_weights, gains, square_moment, mlp_moment, gain_moment, rate
):
    square_local, mlp_local, gain_local = from_wire(grads)
    square_grad, mlp_grad, gain_grad = (
        lax.psum_scatter(square_local, "dp", scatter_dimension=1, tiled=True),
        lax.psum_scatter(mlp_local, "dp", scatter_dimension=1, tiled=True),
        lax.psum_scatter(gain_local, "dp", scatter_dimension=1, tiled=True),
    )
    square_moment_new = 0.5 * square_moment + square_grad
    mlp_moment_new = 0.5 * mlp_moment + mlp_grad
    gain_moment_new = 0.5 * gain_moment + gain_grad
    device = lax.axis_index("dp")
    count = lax.axis_size("dp")
    square_owners = [index * count // 7 for index in range(5)]
    mlp_owners = [(index + 5) * count // 7 for index in range(2)]
    square_full, mlp_full = (
        lax.all_gather(square_moment_new, "dp", axis=1, tiled=True),
        lax.all_gather(mlp_moment_new, "dp", axis=1, tiled=True),
    )
    mine_square = pick_owned(square_full, square_owners, device)
    mine_mlp = pick_owned(mlp_full, mlp_owners, device)
    made_square = lax.cond(
        is_owner(square_owners, device), plain_orthogonalize, jnp.zeros_like, mine_square
    )
    made_mlp = lax.cond(is_owner(mlp_owners, device), plain_orthogonalize, jnp.zeros_like, mine_mlp)
    stack_square = jnp.stack(
        [jnp.where(device == owner, made_square, 0.0) for owner in square_owners]
    )
    stack_mlp = jnp.stack([jnp.where(device == owner, made_mlp, 0.0) for owner in mlp_owners])
    square_ortho, mlp_ortho = (
        lax.psum_scatter(stack_square, "dp", scatter_dimension=1, tiled=True),
        lax.psum_scatter(stack_mlp, "dp", scatter_dimension=1, tiled=True),
    )
    square_new = square_weights - jnp.array(SQ_RATES, F32)[:, None, None] * square_ortho
    mlp_new = mlp_weights - jnp.array(MLP_RATES, F32)[:, None, None] * mlp_ortho
    gains_new = gains - rate * gain_moment_new
    return (
        square_grad,
        square_moment_new,
        square_new,
        square_new.astype(BF16),
        mlp_grad,
        mlp_moment_new,
        mlp_new,
        mlp_new.astype(BF16),
        gain_grad,
        gain_moment_new,
        gains_new,
    )


def per_device(
    actions,
    observed,
    camera_flags,
    noise_levels,
    cotangent,
    square_weights,
    mlp_weights,
    gains,
    square_moment,
    mlp_moment,
    gain_moment,
):
    count = lax.axis_size("dp")
    rate = 0.1 / math.sqrt(actions.shape[0] * count)
    by_key = observed.transpose(1, 0, 2)
    ins = (actions, by_key, camera_flags, noise_levels, cotangent)
    if count == math.prod(GRID):
        made = block_and_back(True, *ins, square_weights, mlp_weights, gains, square_moment, mlp_moment)
        done = finish(rate, made, square_weights, mlp_weights, gains, gain_moment)
        output, actions_grad = done.output_f, done.ag_f
        d = done
        rest = (d.sqg, d.sqm, d.sqn, d.sqc, d.mlpg, d.mlpm, d.mlpn, d.mlpc, d.gg, d.gm, d.gn)
    else:
        square_all, mlp_all = (
            lax.all_gather(square_weights.astype(BF16), "dp", axis=1, tiled=True),
            lax.all_gather(mlp_weights.astype(BF16), "dp", axis=1, tiled=True),
        )
        gain_all = lax.all_gather(gains, "dp", axis=1, tiled=True)
        made = block_and_back(False, *ins, square_all, mlp_all, gain_all)
        done = finish(rate, made)
        output, actions_grad = made.output, made.ag
        grads = made.grads.reshape(-1, WIRE, LANES)
        rest = update_by_collectives(
            grads, square_weights, mlp_weights, gains, square_moment, mlp_moment, gain_moment, rate
        )
    observed_grad = done.og.transpose(1, 0, 2)
    return (output, actions_grad, observed_grad) + tuple(rest)


def solution(mesh):
    rows, cube, flat = P("dp", None), P("dp", None, None), P("dp")
    stacked, pair = P(None, "dp", None), P(None, "dp")
    return jax.shard_map(
        per_device,
        mesh=mesh,
        in_specs=(rows, cube, flat, flat, rows, stacked, stacked, pair, stacked, stacked, pair),
        out_specs=(rows, rows, cube) + (stacked,) * 8 + (pair,) * 3,
        check_vma=False,
    )
```

```python
import functools
import math

import jax
import jax.numpy as jnp
from jax import lax
from jax.experimental import pallas as pl
from jax.experimental.pallas import tpu as pltpu
from jax.sharding import PartitionSpec as P

HEADS = 4
ACT = 16
OBS_FULL = 196
OBS_FEW = 49
COEF_A = 3.4445
COEF_B = -4.775
COEF_C = 2.0315
F32 = jnp.float32
BF16 = jnp.bfloat16
MESH = pl.DeviceIdType.MESH
VMEM = pltpu.VMEM
NN = (((1,), (0,)), ((), ()))
NT = (((1,), (1,)), ((), ()))
TN = (((0,), (0,)), ((), ()))

LANES = 128
TILE = 8
MLP_ROWS = 64
SQ_ROWS = 16
SQ_AT = (160, 192, 176, 128, 144)
GAIN_BASE = 208
WIRE = 224
PIECES = ((0, 64), (64, 64), (128, 48), (176, 48))
PIECE_X_FIRST = (True, False, True, False)
CHUNKS = ((0, 64), (64, 64), (128, 32), (160, 32), (192, 32))
X_FIRST = (True, False, True, False, True)
PARTS_OUT = ((0, 0, 0, 64), (1, 1, 64, 64), (2, 5, 128, 16), (2, 6, 144, 16), (3, 2, 160, 16), (3, 4, 176, 16), (4, 3, 192, 16))
MLP_RATES = (1.0, 0.5)
SQ_RATES = (0.5, 0.5, 0.5, 0.5, 4.0)
GRID = (4, 2, 2, 2)
OWNERS = (8, 22, 14, 16, 11, 21, 13)
SHIFTS = (0.0, 0.0, 0.4, 0.8, 0.8)
KEYS_PAD = 208
GROUP = 16
ROWS = 512


class Refs:
    def __init__(self, pairs):
        self.__dict__.update(pairs)


def dot(left, right, dims=NN):
    return lax.dot_general(left, right, dims, preferred_element_type=F32)


def place():
    me = lax.axis_index("dp")
    return me, me // 8, (me // 4) % 2, (me // 2) % 2, me % 2


def device_at(z, y, x, c):
    return ((z * 2 + y) * 2 + x) * 2 + c


def link(src, dst, send, recv, device):
    return pltpu.make_async_remote_copy(
        src_ref=src,
        dst_ref=dst,
        send_sem=send,
        recv_sem=recv,
        device_id=(device,),
        device_id_type=MESH,
    )


def greet(device):
    pl.semaphore_signal(
        pltpu.get_barrier_semaphore(), inc=1, device_id=(device,), device_id_type=MESH
    )


def normalize(values):
    centred = values - jnp.mean(values, -1, keepdims=True)
    scale = lax.rsqrt(jnp.mean(centred * centred, -1, keepdims=True) + 1e-05)
    return centred * scale, scale


def norm_back(grad, hat, scale):
    mean_one = jnp.mean(grad, -1, keepdims=True)
    mean_two = jnp.mean(grad * hat, -1, keepdims=True)
    return scale * (grad - mean_one - hat * mean_two)


class Gather:
    def __init__(self, r):
        self.r = r
        self.me, self.z, self.y, self.x, self.c = place()

    def hop(self, k, step, part, device):
        return link(part, part, self.r.gsend.at[0], self.r.grecv.at[k, step], device)

    def along_z(self, k, step):
        part = self.r.wire.at[self.z, self.y, self.x, self.c, pl.ds(*PIECES[k])]
        return self.hop(k, 0, part, device_at((self.z + step + 1) % 4, self.y, self.x, self.c))

    def wait_z(self, k):
        all_three = self.r.proxy.at[pl.ds(0, 3), pl.ds(*PIECES[k])]
        pltpu.make_async_copy(all_three, all_three, self.r.grecv.at[k, 0]).wait()

    def plane(self, k, second, mine):
        z, y, x, c = self.z, self.y, self.x, self.c
        rows, wire = pl.ds(*PIECES[k]), self.r.wire
        py, px = (y, x) if mine else (1 - y, 1 - x)
        along_x = PIECE_X_FIRST[k] == second
        if along_x:
            part = wire.at[:, y, px, c, rows] if second else wire.at[:, :, px, c, rows]
            return self.hop(k, 1 if second else 2, part, device_at(z, y, 1 - x, c))
        part = wire.at[:, py, x, c, rows] if second else wire.at[:, py, :, c, rows]
        return self.hop(k, 1 if second else 2, part, device_at(z, 1 - y, x, c))

    def core(self, k, mine):
        part = self.r.wire.at[:, :, :, self.c if mine else 1 - self.c, pl.ds(*PIECES[k])]
        return self.hop(k, 3, part, device_at(self.z, self.y, self.x, 1 - self.c))

    def first(self, *chunks):
        for k in chunks:
            for step in range(3):
                self.along_z(k, step).start()

    def second(self, *chunks):
        for k in chunks:
            self.wait_z(k)
            self.plane(k, True, True).start()

    def third(self, *chunks):
        for k in chunks:
            self.plane(k, True, False).wait_recv()
            self.plane(k, False, True).start()

    def fourth(self, *chunks):
        for k in chunks:
            self.plane(k, False, False).wait_recv()
            self.core(k, True).start()

    def last(self, *chunks):
        for k in chunks:
            self.core(k, False).wait_recv()

    def drain(self):
        pltpu.make_async_copy(self.r.proxy, self.r.proxy, self.r.gsend.at[0]).wait()

    def fill(self):
        r = self.r
        spot = (self.z, self.y, self.x, self.c)

        def tiles(source, m, base, number):
            for j in range(number):
                pair = [source[m, :, pl.ds((2 * j + k) * LANES, LANES)] for k in range(2)]
                r.wire[spot + (pl.ds(base + j * 16, 16),)] = jnp.concatenate(pair, axis=0).astype(BF16)

        for m in range(5):
            tiles(r.sqw_v, m, SQ_AT[m], 1)
        for m in range(2):
            tiles(r.mlpw_v, m, m * MLP_ROWS, 4)
        gains, edge = r.gain_v[...], r.edge
        high = gains.astype(BF16).astype(F32)
        middle = (gains - high).astype(BF16).astype(F32)
        edge[...] = jnp.zeros_like(edge)
        edge[0:2, 0:TILE] = high
        edge[2:4, 0:TILE] = middle
        edge[4:6, 0:TILE] = (gains - high - middle).astype(BF16).astype(F32)
        r.wire[spot + (pl.ds(GAIN_BASE, 16),)] = edge[...].astype(BF16)

    def unpack(self, base, number, out, m):
        for j in range(number):
            block = self.r.wire[:, :, :, :, pl.ds(base + j * 16, 16), :].reshape(32, 16, LANES).astype(F32)
            for half in range(2):
                columns = pl.ds((2 * j + half) * LANES, LANES)
                out[m, :, columns] = block[:, half * 8 : half * 8 + 8, :].reshape(256, LANES).astype(BF16)

    def unpack_gains(self):
        edge, wire = self.r.edge, self.r.wire
        for half in range(2):
            total = jnp.zeros((16, LANES), F32)
            for at in range(16):
                d = half * 16 + at
                tile = wire[d // 8, (d // 4) % 2, (d // 2) % 2, d % 2, pl.ds(GAIN_BASE, 16), :].astype(F32)
                total = total + (tile if at == 0 else pltpu.roll(tile, at * TILE, 1))
            edge[...] = total
            self.r.gain_all[:, pl.ds(half * LANES, LANES)] = edge[0:2, :] + edge[2:4, :] + edge[4:6, :]


class Update:
    def __init__(self, r):
        self.r = r
        self.me, self.z, self.y, self.x, self.c = place()

    def hop(self, k, step, src, dst, device):
        return link(src, dst, self.r.send.at[0], self.r.recv.at[k, step], device)

    def core(self, k):
        rows = pl.ds(*CHUNKS[k])
        src, dst = self.r.send0.at[:, :, :, rows], self.r.got_core.at[:, :, :, rows]
        return self.hop(k, 0, src, dst, device_at(self.z, self.y, self.x, 1 - self.c))

    def plane(self, k, first):
        rows = pl.ds(*CHUNKS[k])
        to = (self.z, self.y, 1 - self.x, self.c) if X_FIRST[k] == first else (self.z, 1 - self.y, self.x, self.c)
        if first:
            src, dst = self.r.send1.at[:, :, rows], self.r.got1.at[:, :, rows]
        else:
            src, dst = self.r.send2.at[:, rows], self.r.got2.at[:, rows]
        return self.hop(k, 1 if first else 2, src, dst, device_at(*to))

    def along_z(self, k, step):
        rows = pl.ds(*CHUNKS[k])
        to = device_at((self.z + step + 1) % 4, self.y, self.x, self.c)
        return self.hop(k, 3, self.r.send3.at[step, rows], self.r.got3.at[step, rows], to)

    def start(self, k):
        rows = pl.ds(*CHUNKS[k])
        self.r.send0[:, :, :, rows, :] = self.r.grads[:, :, :, 1 - self.c, rows, :].astype(BF16)
        self.core(k).start()

    def one(self, *chunks):
        r = self.r
        for k in chunks:
            rows = pl.ds(*CHUNKS[k])
            self.core(k).wait_recv()
            sum1 = r.sum1
            sum1[:, :, :, rows, :] = r.grads[:, :, :, self.c, rows, :] + r.got_core[:, :, :, rows, :].astype(F32)
            other = sum1[:, :, 1 - self.x, rows, :] if X_FIRST[k] else sum1[:, 1 - self.y, :, rows, :]
            r.send1[:, :, rows, :] = other.astype(BF16)
            self.plane(k, True).start()

    def two(self, *chunks):
        r = self.r
        for k in chunks:
            rows = pl.ds(*CHUNKS[k])
            self.plane(k, True).wait_recv()
            sum1, sum2 = r.sum1, r.sum2
            mine = sum1[:, :, self.x, rows, :] if X_FIRST[k] else sum1[:, self.y, :, rows, :]
            sum2[:, :, rows, :] = mine + r.got1[:, :, rows, :].astype(F32)
            other = 1 - self.y if X_FIRST[k] else 1 - self.x
            r.send2[:, rows, :] = sum2[:, other, rows, :].astype(BF16)
            self.plane(k, False).start()

    def three(self, *chunks):
        r = self.r
        for k in chunks:
            rows = pl.ds(*CHUNKS[k])
            self.plane(k, False).wait_recv()
            mine = self.y if X_FIRST[k] else self.x
            r.sum3[:, rows, :] = r.sum2[:, mine, rows, :] + r.got2[:, rows, :].astype(F32)
            for step in range(3):
                r.send3[step, rows, :] = r.sum3[(self.z + step + 1) % 4, rows, :].astype(BF16)
                self.along_z(k, step).start()

    def result(self, index):
        return self.r.result_mlp if index < 2 else self.r.result_sq

    def own_part(self, part):
        _, index, base, number = PARTS_OUT[part]
        if index < 2:
            return self.r.moment_low.at[pl.ds(base, number)], self.r.slabs_mlp.at[self.me]
        return self.r.moment.at[pl.ds(base, number)], self.r.slabs_sq.at[self.me]

    def to_owner(self, part):
        src, dst = self.own_part(part)
        return link(src, dst, self.r.own_send.at[part], self.r.own_recv.at[0], OWNERS[PARTS_OUT[part][1]])

    def four(self, *chunks):
        r = self.r
        moment, out = r.moment, r.out
        for k in chunks:
            rows = pl.ds(*CHUNKS[k])
            total = r.sum3[self.z, rows, :]
            all_three = r.got3.at[:, rows]
            pltpu.make_async_copy(all_three, all_three, r.recv.at[k, 3]).wait()
            for step in range(3):
                total = total + r.got3[step, rows, :].astype(F32)
            out[0, rows, :] = total
            new = 0.5 * moment[rows, :] + total
            moment[rows, :] = new
            if k < 2:
                r.moment_low[rows, :] = new.astype(BF16)
            for part, (chunk, index, *_) in enumerate(PARTS_OUT):
                if chunk != k:
                    continue

                @pl.when(self.me != OWNERS[index])
                def _():
                    self.to_owner(part).start()

                @pl.when(self.me == OWNERS[index])
                def _():
                    src, dst = self.own_part(part)
                    pltpu.make_async_copy(src, dst, r.own_recv.at[0]).start()

    def old_moment(self):
        r = self.r
        moment = r.moment
        for m in range(2):
            for j in range(8):
                moment[pl.ds(m * MLP_ROWS + j * TILE, TILE), :] = r.mlpm_v[m, :, pl.ds(j * LANES, LANES)]
        for m in range(5):
            for j in range(2):
                moment[pl.ds(SQ_AT[m] + j * TILE, TILE), :] = r.sqm_v[m, :, pl.ds(j * LANES, LANES)]
        moment[pl.ds(GAIN_BASE, 16), :] = jnp.zeros((16, LANES), F32)

    def orthogonalize(self):
        r = self.r
        cur = r.cur
        rows = lax.broadcasted_iota(jnp.int32, (256, 256), 0)
        diagonal = rows == lax.broadcasted_iota(jnp.int32, (256, 256), 1)

        def run(slabs, result, tiles):
            pltpu.make_async_copy(slabs, slabs, r.own_recv.at[0]).wait()
            low = r.cur_low
            for j in range(tiles // 2):
                pair = slabs[:, pl.ds(j * 16, 16), :].astype(F32)
                for side in range(2):
                    columns = pl.ds((2 * j + side) * LANES, LANES)
                    part = pair[:, side * TILE : (side + 1) * TILE, :].reshape(256, LANES)
                    cur[:, columns] = part
                    low[:, columns] = part.astype(BF16)
            scale = 1.0
            for turn, shift in enumerate(SHIFTS):
                whole = low[:, 0 : tiles * LANES]
                off = dot(whole, whole, NT)
                if turn == 0:
                    norm = jnp.sum(jnp.sum(jnp.where(diagonal, off, 0.0), axis=0, keepdims=True), axis=1, keepdims=True)
                    scale = 1.0 / (jnp.sqrt(norm) + 1e-07)
                    off = off * (scale * scale)
                if shift:
                    off = off - jnp.where(diagonal, shift, 0.0)
                off_low = off.astype(BF16)
                poly = (COEF_B + 2.0 * COEF_C * shift) * off + COEF_C * dot(off_low, off_low)
                poly = poly.astype(BF16)
                keep = COEF_A + shift * (COEF_B + COEF_C * shift)
                for j in range(tiles // 2):
                    columns = pl.ds(j * 2 * LANES, 2 * LANES)
                    now = keep * cur[:, columns] + dot(poly, low[:, columns])
                    if turn == 0:
                        now = now * scale
                    if turn < len(SHIFTS) - 1:
                        cur[:, columns] = now
                        low[:, columns] = now.astype(BF16)
                    else:
                        parts = [now[:, side * LANES : (side + 1) * LANES].reshape(32, TILE, LANES) for side in range(2)]
                        result[:, pl.ds(j * 16, 16), :] = jnp.concatenate(parts, axis=1).astype(result.dtype)

        mine_mlp = jnp.logical_or(self.me == OWNERS[0], self.me == OWNERS[1])
        mine_sq = self.me < 0
        for device in OWNERS[2:]:
            mine_sq = jnp.logical_or(mine_sq, self.me == device)

        @pl.when(mine_mlp)
        def _():
            run(r.slabs_mlp, r.result_mlp, 8)

        @pl.when(mine_sq)
        def _():
            run(r.slabs_sq, r.result_sq, 2)

    def landing(self, index):
        if index < 2:
            return self.r.back_mlp.at[index]
        return self.r.out.at[2, pl.ds(SQ_AT[index - 2], SQ_ROWS)]

    def give_back(self, index, device):
        result = self.result(index)
        return link(
            result.at[device], self.landing(index),
            self.r.back_send.at[0], self.r.back_recv.at[index], device,
        )

    def give_all(self):
        r = self.r
        for index in range(7):
            result = self.result(index)

            @pl.when(self.me == OWNERS[index])
            def _():
                def send_one(step, _):
                    self.give_back(index, (self.me + step) % 32).start()
                    return 0

                lax.fori_loop(1, 32, send_one, 0)
                pltpu.make_async_copy(result.at[self.me], self.landing(index), r.back_recv.at[index]).start()

    def take_all(self):
        for index in range(7):
            result = self.result(index)
            pltpu.make_async_copy(result.at[0], self.landing(index), self.r.back_recv.at[index]).wait()
        for index in range(2):
            rows = pl.ds(index * MLP_ROWS, MLP_ROWS)
            self.r.out[2, rows, :] = self.r.back_mlp[index].astype(F32)

    def drain(self):
        pltpu.make_async_copy(self.r.proxy, self.r.proxy, self.r.send.at[0]).wait()
        for part in range(len(PARTS_OUT)):

            @pl.when(self.me != OWNERS[PARTS_OUT[part][1]])
            def _():
                self.to_owner(part).wait_send()

    def drain_owner(self):
        for index in range(7):
            sent = self.result(index).at[pl.ds(0, 31)]

            @pl.when(self.me == OWNERS[index])
            def _():
                pltpu.make_async_copy(sent, sent, self.r.back_send.at[0]).wait()


def greet_all():
    me, z, y, x, c = place()
    greet(device_at(z, y, x, 1 - c))
    greet(device_at(z, y, 1 - x, c))
    greet(device_at(z, 1 - y, x, c))
    for step in range(1, 4):
        greet(device_at((z + step) % 4, y, x, c))
    owner = me < 0
    for device in OWNERS:
        owner = jnp.logical_or(owner, me == device)

        @pl.when(me != device)
        def _():
            greet(device)

    @pl.when(owner)
    def _():
        def greet_other(step, _):
            greet((me + step) % 32)
            return 0

        lax.fori_loop(1, 32, greet_other, 0)

    is_owner = owner.astype(jnp.int32)
    return 6 + 7 - is_owner + 31 * is_owner


def block_kernel(names, remote, *args):
    r = Refs(zip(names, args))
    keys, samples = r.obs.shape[0], r.obs.shape[1]
    tokens, width = r.acts.shape
    head_dim, half, per = width // HEADS, width // 2, ROWS // ACT
    wide = r.mlp_all.shape[2]
    groups = samples // GROUP
    in_sems, out_sems = r.in_sems, r.out_sems

    if remote:
        own = (r.sqw_v, r.mlpw_v, r.gain_v)
    else:
        own = (r.sq_all, r.mlp_all, r.gain_all)
    loads = list(zip((r.sqw, r.mlpw, r.gain), own))
    loads += [(r.acts, r.acts_v), (r.obs, r.obs_v.at[pl.ds(0, keys)]), (r.cot, r.cot_v)]
    if remote:
        loads += [(r.sqm, r.sqm_v), (r.mlpm, r.mlpm_v)]
    loads += [(r.flags, r.flags_s), (r.levels, r.levels_s)]
    copies = [pltpu.make_async_copy(a, b, in_sems.at[i]) for i, (a, b) in enumerate(loads)]

    def arrive(*which):
        for i in which:
            copies[i].wait()

    for copy in copies:
        copy.start()
    if remote:
        gather, update = Gather(r), Update(r)
        expected = greet_all()
        arrive(0, 1, 2)
        gather.fill()
        pl.semaphore_wait(pltpu.get_barrier_semaphore(), expected)
        gather.first(2, 3)

    arrive(3)

    def hats(i, _):
        rows = pl.ds(pl.multiple_of(i * ROWS, ROWS), ROWS)
        hat, scale = normalize(r.acts_v[rows, :])
        r.xhat[rows, :] = hat
        r.rstd[rows, :] = scale
        return 0

    lax.fori_loop(0, tokens // ROWS, hats, 0)

    mem, obs_v = r.mem, r.obs_v
    batch = 16
    chunks = KEYS_PAD // batch
    swap = r.swap
    row = lax.broadcasted_iota(jnp.int32, swap.shape, 0)
    column = lax.broadcasted_iota(jnp.int32, swap.shape, 1)
    swap[...] = jnp.where(column == (row % batch) * batch + row // batch, 1.0, 0.0).astype(BF16)

    def turn(part, low, high):
        def one(j, _):
            at = pl.ds(pl.multiple_of(j * batch, batch), batch)
            here = pl.ds(part * batch, batch)
            block = obs_v[at, here, :].reshape(batch * batch, width)
            mem[here, at, :] = dot(swap[...], block).astype(BF16).reshape(batch, batch, width)
            return 0

        lax.fori_loop(low, high, one, 0, unroll=high - low)

    whole = chunks - 1
    arrive(4)
    turn(0, 0, whole // 2)
    if remote:
        gather.second(2, 3)
        gather.first(0, 1)
    turn(0, whole // 2, whole)
    if remote:
        gather.third(2, 3)
    turn(1, 0, whole // 2)
    if remote:
        gather.second(0, 1)
        gather.fourth(2, 3)
    turn(1, whole // 2, whole)
    arrive(len(copies) - 1, len(copies) - 2)
    freqs = jnp.exp(
        lax.broadcasted_iota(jnp.int32, (1, half), 1).astype(F32) * F32(-math.log(10000.0)) / half
    )
    for s in range(samples):
        r.angle[s : s + 1, :] = r.levels_s[s].astype(F32) * freqs
    r.embed[:, 0:half] = jnp.sin(r.angle[...]).astype(BF16)
    r.embed[:, half:width] = jnp.cos(r.angle[...]).astype(BF16)
    if remote:
        arrive(6, 7)
        update.old_moment()
        gather.third(0, 1)
        gather.last(2, 3)
        for m in range(5):
            gather.unpack(SQ_AT[m], 1, r.sq_all, m)
        gather.unpack_gains()
    else:
        arrive(0, 1, 2)

    sq, mlp = r.sq_all, r.mlp_all
    wkh, wvh = r.wkh, r.wvh
    lane = lax.broadcasted_iota(jnp.int32, (width, width), 1)

    def split_heads(out, weight):
        weight = weight.astype(F32)
        for h in range(HEADS):
            out[pl.ds(h * width, width), :] = jnp.where(lane // head_dim == h, weight, 0.0).astype(BF16)

    split_heads(wkh, sq[2])
    g1, g2 = r.gain_all[0:1, :], r.gain_all[1:2, :]

    obs_v[keys] = dot(r.embed[...], sq[0]).astype(BF16)
    obs_v[keys + 1 :] = jnp.zeros((KEYS_PAD - keys - 1, samples, width), BF16)
    for part in range(samples // batch):
        turn(part, whole, chunks)

    queries, dmixes = r.queries, r.dmixes

    def make_queries(i, _):
        rows = pl.ds(pl.multiple_of(i * ROWS, ROWS), ROWS)
        first = (r.xhat[rows, :] * g1).astype(BF16)
        r.first[rows, :] = first
        q = dot(first, sq[1]).astype(BF16)
        r.query[rows, :] = q
        here = pl.ds(i * per, per)
        for h in range(HEADS):
            wk = wkh[pl.ds(h * width, width), :]
            value = (dot(q, wk, NT) * 0.125).astype(BF16).reshape(per, ACT, width)
            queries[here, pl.ds(h * ACT, ACT), :] = value
        return 0

    lax.fori_loop(0, tokens // ROWS, make_queries, 0)

    key = lax.broadcasted_iota(jnp.int32, (KEYS_PAD, LANES), 0)
    rows_each = HEADS * ACT
    left = lax.broadcasted_iota(jnp.int32, (KEYS_PAD, LANES), 1) < rows_each
    left_row = lax.broadcasted_iota(jnp.int32, (1, LANES), 1) < rows_each
    rest = jnp.where((key >= OBS_FEW) & (key < OBS_FULL), 1.0, 0.0)
    padding = jnp.where(key > OBS_FULL, -1000000000.0, 0.0)

    def with_memory(s, sides):
        here = pl.ds(s, 4)
        wide = dot(mem[here].reshape(4 * KEYS_PAD, width), sides[here].reshape(4 * rows_each, width), NT)
        part = [wide[k * KEYS_PAD : (k + 1) * KEYS_PAD, (k // 2) * LANES : (k // 2 + 1) * LANES] for k in range(4)]
        return jnp.where(left, part[0], part[1]), jnp.where(left, part[2], part[3])

    def each_head(out, s, value):
        rows = pl.ds(pl.multiple_of(s * ACT, ACT), ACT)
        for h in range(HEADS):
            out[rows, pl.ds(h * width, width)] = value[h * ACT : (h + 1) * ACT, :]

    def attend(g, _):
        pairs = []
        for quad in range(GROUP // 4):
            pairs.extend(with_memory(g * GROUP + 4 * quad, queries))
        turned = []
        for k, score in enumerate(pairs):
            s = g * GROUP + 2 * k
            drop = [(1 - r.flags_s[s + side]).astype(F32) * -1000000000.0 for side in range(2)]
            score = score + (rest * jnp.where(left_row, drop[0], drop[1]) + padding)
            expo = jnp.exp(score - jnp.max(score, 0, keepdims=True))
            probs = expo * (1.0 / jnp.sum(expo, 0, keepdims=True))
            r.probs[g * (GROUP // 2) + k] = probs
            turned.append(probs.astype(BF16).T)
        for k, low in enumerate(turned):
            for side in range(2):
                s = g * GROUP + 2 * k + side
                each_head(r.u, s, dot(low[side * rows_each : (side + 1) * rows_each], mem[s]).astype(BF16))
        return 0

    lax.fori_loop(0, groups // 2, attend, 0)
    if remote:
        gather.fourth(0, 1)
    lax.fori_loop(groups // 2, groups, attend, 0)
    split_heads(wvh, sq[3])

    gain_acc = r.gain_acc
    gain_acc[...] = jnp.zeros_like(gain_acc)
    blocks = [pl.ds(i * ROWS, ROWS) for i in range(tokens // ROWS)]
    for rows in blocks:
        mixed = dot(r.u[rows, :], wvh[...]).astype(BF16)
        r.mixed[rows, :] = mixed
        resid = r.acts_v[rows, :] + dot(mixed, sq[4])
        r.resid[rows, :] = resid
        hat, scale = normalize(resid)
        r.hat_two[rows, :] = hat
        r.rstd_two[rows, :] = scale
        r.second[rows, :] = (hat * g2).astype(BF16)
    arrive(5)
    r.out_low[...] = r.cot_v[...].astype(BF16)
    if remote:
        gather.last(0)
        gather.unpack(0, 4, mlp, 0)
    wide_blocks = [pl.ds(c * 256, 256) for c in range(wide // 256)]
    for rows in blocks:
        for columns in wide_blocks:
            v = dot(r.second[rows, :], mlp[0, :, columns])
            square = v * v
            t = jnp.tanh(0.7978845608 * (v + 0.044715 * square * v))
            r.active[rows, columns] = (0.5 * v * (1.0 + t)).astype(BF16)
            slope = 0.5 * (1.0 + t) + 0.5 * v * (1.0 - t * t) * (0.7978845608 * (1.0 + 0.134145 * square))
            r.slope[rows, columns] = slope

    grads = r.grads

    def put(base, tiles, value):
        for j in range(tiles):
            part = value[:, j * LANES : (j + 1) * LANES].reshape(GRID + (TILE, LANES))
            grads[:, :, :, :, pl.ds(base + j * TILE, TILE), :] = part

    def by_head(left, right):
        turned = left.T
        parts = [
            dot(turned[h * head_dim : (h + 1) * head_dim, :], right[:, pl.ds(h * width, width)])
            for h in range(HEADS)
        ]
        return jnp.concatenate(parts, axis=0).T

    put(MLP_ROWS, 8, dot(r.out_low[...], r.active[...], TN))
    if remote:
        update.start(1)
        gather.last(1)
        gather.unpack(MLP_ROWS, 4, mlp, 1)
    for rows in blocks:
        for columns in wide_blocks:
            slope = r.slope[rows, columns]
            r.dhidden[rows, columns] = (slope * dot(r.out_low[rows, :], mlp[1, :, columns])).astype(BF16)
    put(0, 8, dot(r.second[...], r.dhidden[...], TN))
    if remote:
        update.start(0)
        update.one(1)
    for i, rows in enumerate(blocks):
        r.out_v[rows, :] = r.resid[rows, :] + dot(r.active[rows, :], mlp[1], NT)
        grad_second = dot(r.dhidden[rows, :], mlp[0], NT)
        hat = r.hat_two[rows, :]
        gain_acc[1:2, :] += jnp.sum(grad_second * hat, 0, keepdims=True)
        dres = r.cot_v[rows, :] + norm_back(grad_second * g2, hat, r.rstd_two[rows, :])
        r.dres[rows, :] = dres
        low = dres.astype(BF16)
        r.dres_low[rows, :] = low
        gm = dot(low, sq[4], NT).astype(BF16)
        r.dmixed[rows, :] = gm
        here = pl.ds(i * per, per)
        for h in range(HEADS):
            wv = wvh[pl.ds(h * width, width), :]
            dmixes[here, pl.ds(h * ACT, ACT), :] = dot(gm, wv, NT).astype(BF16).reshape(per, ACT, width)
    keep_out = pltpu.make_async_copy(r.out_v, r.output, out_sems.at[0])
    keep_out.start()
    if remote:
        update.one(0)
    put(SQ_AT[4], 2, dot(r.mixed[...], r.dres_low[...], TN))
    put(SQ_AT[3], 2, by_head(r.dmixed[...], r.u))
    if remote:
        update.start(2)

    left_low = jnp.where(left_row, 1.0, 0.0).astype(BF16)
    right_low = jnp.where(left_row, 0.0, 1.0).astype(BF16)

    def attend_back(g, _):
        pairs = []
        for quad in range(GROUP // 4):
            pairs.extend(with_memory(g * GROUP + 4 * quad, dmixes))
        lows = []
        for k, rise in enumerate(pairs):
            probs = r.probs[g * (GROUP // 2) + k]
            both = probs * rise
            dscore = (both - probs * jnp.sum(both, 0, keepdims=True)).astype(BF16)
            lows.append((probs.astype(BF16), dscore, dscore.T))
        for k, (low, dscore, turned) in enumerate(lows):
            s = g * GROUP + 2 * k
            for side in range(2):
                dq = dot(turned[side * rows_each : (side + 1) * rows_each], mem[s + side]) * 0.125
                each_head(r.dq_wide, s + side, dq.astype(BF16))
            here = pl.ds(s, 2)
            sides = jnp.concatenate(
                [x[here].reshape(2 * rows_each, width) for x in (dmixes, queries)], axis=0
            )
            own = [jnp.concatenate([low * keep, dscore * keep], axis=1) for keep in (left_low, right_low)]
            dmem = dot(jnp.concatenate(own, axis=0), sides)
            for side in range(2):
                rows = dmem[side * KEYS_PAD : (side + 1) * KEYS_PAD, :]
                mem[s + side] = rows.astype(BF16)
                r.stamps[s + side] = rows[192:200, :]
        return 0

    lax.fori_loop(0, groups // 2, attend_back, 0)
    if remote:
        update.two(1)
        update.one(2)
        update.two(0)
    lax.fori_loop(groups // 2, groups, attend_back, 0)
    if remote:
        update.three(1)
        update.two(2)
        update.three(0)
    put(SQ_AT[2], 2, by_head(r.query[...], r.dq_wide))
    stamp_low = r.stamps[:, 4:5, :].reshape(samples, width).astype(BF16)
    put(SQ_AT[0], 2, dot(r.embed[...], stamp_low, TN))
    if remote:
        update.start(3)

    def keep_og(part):
        here = pl.ds(part * batch, batch)
        return pltpu.make_async_copy(obs_v.at[pl.ds(0, keys), here], r.og.at[:, here], out_sems.at[2 + part])

    def turn_back(part):
        def one(j):
            at = pl.ds(pl.multiple_of(j * batch, batch), batch)
            here = pl.ds(part * batch, batch)
            block = mem[here, at, :].reshape(batch * batch, width)
            value = dot(swap[...], block).astype(BF16).reshape(batch, batch, width)
            obs_v[at, here, :] = value

        for j in range(chunks):
            one(j)
        keep_og(part).start()

    def queries_back(i, _):
        rows = pl.ds(pl.multiple_of(i * ROWS, ROWS), ROWS)
        r.dquery[rows, :] = dot(r.dq_wide[rows, :], wkh[...]).astype(BF16)
        return 0

    lax.fori_loop(0, tokens // ROWS, queries_back, 0)
    put(SQ_AT[1], 2, dot(r.first[...], r.dquery[...], TN))
    if remote:
        update.one(3)

    def acts_back(i, _):
        rows = pl.ds(pl.multiple_of(i * ROWS, ROWS), ROWS)
        grad_first = dot(r.dquery[rows, :], sq[1], NT)
        hat = r.xhat[rows, :]
        gain_acc[0:1, :] += jnp.sum(grad_first * hat, 0, keepdims=True)
        r.ag_v[rows, :] = r.dres[rows, :] + norm_back(grad_first * g1, hat, r.rstd[rows, :])
        return 0

    def finish_acts():
        lax.fori_loop(0, tokens // ROWS, acts_back, 0)
        for norm in range(2):
            for j in range(2):
                row = gain_acc[norm : norm + 1, j * LANES : (j + 1) * LANES]
                at = GAIN_BASE + norm * 2 + j
                value = jnp.broadcast_to(row.reshape(1, 1, 1, 1, 1, LANES), GRID + (1, LANES))
                grads[:, :, :, :, at : at + 1, :] = value
        rest = WIRE - GAIN_BASE - 4
        grads[:, :, :, :, GAIN_BASE + 4 : WIRE, :] = jnp.zeros(GRID + (rest, LANES), F32)

    keep_ag = pltpu.make_async_copy(r.ag_v, r.ag, out_sems.at[1])
    if remote:
        finish_acts()
        update.start(4)
        keep_ag.start()
        update.four(1)
        update.three(2)
        update.two(3)
        update.one(4)
        update.four(0)
        turn_back(0)
        update.three(3)
        update.two(4)
        update.four(2)
        update.three(4)
        update.four(3, 4)
        update.orthogonalize()
        update.give_all()
        turn_back(1)
        out = r.out
        out[1, :, :] = r.moment[...]
        out[2, pl.ds(GAIN_BASE, 16), :] = jnp.zeros((16, LANES), F32)
        gather.drain()
        update.drain()
        update.take_all()
        update.drain_owner()
    else:
        finish_acts()
        keep_ag.start()
        for part in range(samples // batch):
            turn_back(part)
    for copy in (keep_out, keep_ag, *(keep_og(part) for part in range(samples // batch))):
        copy.wait()


def block_and_back(remote, acts, obs, flags, levels, cot, sqw, mlpw, gain, sqm=None, mlpm=None):
    tokens, width = acts.shape
    keys, samples = obs.shape[0], obs.shape[1]
    rows = HEADS * ACT
    wide = mlpw.shape[2]
    any_space = pl.BlockSpec(memory_space=pl.ANY)
    in_vmem = pl.BlockSpec(memory_space=VMEM)
    sem = pltpu.SemaphoreType.DMA
    ins = dict(flags=flags, levels=levels, acts=acts, obs=obs, cot=cot, sqw=sqw, mlpw=mlpw, gain=gain)
    outs = dict(
        output=jax.ShapeDtypeStruct(acts.shape, F32),
        ag=jax.ShapeDtypeStruct(acts.shape, F32),
        og=jax.ShapeDtypeStruct(obs.shape, BF16),
    )
    grads = GRID + (WIRE, LANES)
    scratch = dict(
        obs_v=VMEM((KEYS_PAD, samples, width), BF16),
        acts_v=VMEM(acts.shape, F32),
        cot_v=VMEM(acts.shape, F32),
        mem=VMEM((samples, KEYS_PAD, width), BF16),
        swap=VMEM((256, 256), BF16),
        sq_all=VMEM((5, width, width), BF16),
        mlp_all=VMEM((2, width, wide), BF16),
        gain_all=VMEM((2, width), F32),
        wkh=VMEM((HEADS * width, width), BF16),
        wvh=VMEM((HEADS * width, width), BF16),
        first=VMEM((tokens, width), BF16),
        query=VMEM((tokens, width), BF16),
        xhat=VMEM((tokens, width), F32),
        rstd=VMEM((tokens, 1), F32),
        probs=VMEM((samples // 2, KEYS_PAD, LANES), F32),
        queries=VMEM((samples, rows, width), BF16),
        dmixes=VMEM((samples, rows, width), BF16),
        u=VMEM((tokens, HEADS * width), BF16),
        dq_wide=VMEM((tokens, HEADS * width), BF16),
        mixed=VMEM((tokens, width), BF16),
        second=VMEM((tokens, width), BF16),
        active=VMEM((tokens, wide), BF16),
        dhidden=VMEM((tokens, wide), BF16),
        out_low=VMEM((tokens, width), BF16),
        dres_low=VMEM((tokens, width), BF16),
        dres=VMEM((tokens, width), F32),
        resid=VMEM((tokens, width), F32),
        hat_two=VMEM((tokens, width), F32),
        rstd_two=VMEM((tokens, 1), F32),
        slope=VMEM((tokens, wide), F32),
        dmixed=VMEM((tokens, width), BF16),
        dquery=VMEM((tokens, width), BF16),
        out_v=VMEM((tokens, width), F32),
        ag_v=VMEM((tokens, width), F32),
        angle=VMEM((samples, width // 2), F32),
        embed=VMEM((samples, width), BF16),
        stamps=VMEM((samples, 8, width), F32),
        gain_acc=VMEM((8, width), F32),
        flags_s=pltpu.SMEM(flags.shape, jnp.int32),
        levels_s=pltpu.SMEM(levels.shape, jnp.int32),
        in_sems=sem((10,)),
        out_sems=sem((2 + samples // 16,)),
    )
    extra = {}
    if remote:
        ins.update(sqm=sqm, mlpm=mlpm)
        outs.update(out=jax.ShapeDtypeStruct((3, WIRE, LANES), F32))
        chunks = len(CHUNKS)
        scratch.update(
            grads=VMEM(grads, F32),
            sqw_v=VMEM(sqw.shape, F32),
            mlpw_v=VMEM(mlpw.shape, F32),
            gain_v=VMEM(gain.shape, F32),
            sqm_v=VMEM(sqm.shape, F32),
            mlpm_v=VMEM(mlpm.shape, F32),
            wire=VMEM(grads, BF16),
            edge=VMEM((16, LANES), F32),
            proxy=VMEM((31, WIRE, LANES), BF16),
            gsend=sem((1,)),
            grecv=sem((len(PIECES), 4)),
            send0=VMEM((4, 2, 2, WIRE, LANES), BF16),
            got_core=VMEM((4, 2, 2, WIRE, LANES), BF16),
            sum1=VMEM((4, 2, 2, WIRE, LANES), F32),
            send1=VMEM((4, 2, WIRE, LANES), BF16),
            got1=VMEM((4, 2, WIRE, LANES), BF16),
            sum2=VMEM((4, 2, WIRE, LANES), F32),
            send2=VMEM((4, WIRE, LANES), BF16),
            got2=VMEM((4, WIRE, LANES), BF16),
            sum3=VMEM((4, WIRE, LANES), F32),
            send3=VMEM((3, WIRE, LANES), BF16),
            got3=VMEM((3, WIRE, LANES), BF16),
            moment=VMEM((WIRE, LANES), F32),
            slabs_sq=VMEM((32, SQ_ROWS, LANES), F32),
            slabs_mlp=VMEM((32, MLP_ROWS, LANES), BF16),
            moment_low=VMEM((2 * MLP_ROWS, LANES), BF16),
            back_mlp=VMEM((2, MLP_ROWS, LANES), BF16),
            result_sq=VMEM((32, SQ_ROWS, LANES), F32),
            result_mlp=VMEM((32, MLP_ROWS, LANES), BF16),
            cur=VMEM((width, wide), F32),
            cur_low=VMEM((width, wide), BF16),
            send=sem((1,)),
            recv=sem((chunks, 4)),
            own_send=sem((len(PARTS_OUT),)),
            own_recv=sem((1,)),
            back_send=sem((1,)),
            back_recv=sem((7,)),
        )
        extra = dict(collective_id=0, has_side_effects=True)
        outs = {name: VMEM(like.shape, like.dtype) for name, like in outs.items()}
    else:
        outs.update(grads=jax.ShapeDtypeStruct(grads, F32))
    names = tuple(ins) + tuple(outs) + tuple(scratch)
    stay = [pltpu.with_memory_space_constraint(value, pltpu.HBM) for value in ins.values()]
    results = pl.pallas_call(
        functools.partial(block_kernel, names, remote),
        out_shape=tuple(outs.values()),
        in_specs=[any_space] * len(ins),
        out_specs=[any_space] * 3 + [in_vmem],
        scratch_shapes=list(scratch.values()),
        compiler_params=pltpu.CompilerParams(vmem_limit_bytes=50 << 20, **extra),
        name="block_and_back",
    )(*stay)
    return Refs(zip(outs, results))


PARTS = 7


def finish_kernel(names, rate, *args):
    r = Refs(zip(names, args))
    sems = r.sems
    keys = r.og.shape[0]
    step = keys // PARTS

    def leave(part):
        block = pl.ds(part * step, step)
        return pltpu.make_async_copy(r.og_v.at[block], r.og.at[block], sems.at[part])

    more = PARTS
    moves = []
    if hasattr(r, "wire"):
        pairs = [(r.sqw, r.sqw_v), (r.mlpw, r.mlpw_v), (r.gain, r.gain_v), (r.gainm, r.gainm_v)]
        pairs += [(r.output, r.output_f), (r.ag, r.ag_f)]
        for source, target in pairs:
            moves.append(pltpu.make_async_copy(source, target, sems.at[more]))
            moves[-1].start()
            more += 1
    for part in range(PARTS):

        def widen(j, _):
            r.og_v[j] = r.low[j].astype(F32)
            return 0

        lax.fori_loop(part * step, (part + 1) * step, widen, 0, unroll=4)
        leave(part).start()
    for copy in moves[:4]:
        copy.wait()
    if hasattr(r, "wire"):
        finish_weights(r, rate)
    for part in range(PARTS):
        leave(part).wait()
    for copy in moves[4:]:
        copy.wait()


def finish_weights(r, rate):
    wire = r.wire
    me = lax.axis_index("dp")
    for m in range(5):
        for j in range(2):
            rows, columns = pl.ds(SQ_AT[m] + j * TILE, TILE), pl.ds(j * LANES, LANES)
            r.sqg[m, :, columns] = wire[0, rows, :]
            r.sqm[m, :, columns] = wire[1, rows, :]
            r.sqn[m, :, columns] = r.sqw_v[m, :, columns] - SQ_RATES[m] * wire[2, rows, :]
    r.sqc[...] = r.sqn[...].astype(BF16)
    for m in range(2):
        for j in range(8):
            rows, columns = pl.ds(m * MLP_ROWS + j * TILE, TILE), pl.ds(j * LANES, LANES)
            r.mlpg[m, :, columns] = wire[0, rows, :]
            r.mlpm[m, :, columns] = wire[1, rows, :]
            r.mlpn[m, :, columns] = r.mlpw_v[m, :, columns] - MLP_RATES[m] * wire[2, rows, :]
    r.mlpc[...] = r.mlpn[...].astype(BF16)
    tile = wire[0, pl.ds(GAIN_BASE, TILE), :]
    turned = pltpu.roll(tile, (LANES - (me % 16) * TILE) % LANES, 1)
    at = me // 16
    for norm in range(2):
        pair = turned[2 * norm : 2 * norm + 2, 0:TILE]
        row = jnp.where(at == 0, pair[0:1, :], pair[1:2, :])
        new = 0.5 * r.gainm_v[norm : norm + 1, :] + row
        r.gg[norm : norm + 1, :] = row
        r.gm[norm : norm + 1, :] = new
        r.gn[norm : norm + 1, :] = r.gain_v[norm : norm + 1, :] - rate * new


def finish(rate, made, sqw=None, mlpw=None, gain=None, gainm=None):
    any_space = pl.BlockSpec(memory_space=pl.ANY)
    in_vmem = pl.BlockSpec(memory_space=VMEM)
    ins = dict(low=made.og)
    outs = dict(og=jax.ShapeDtypeStruct(made.og.shape, F32))
    near, far = 1, 1
    if hasattr(made, "out"):
        ins.update(output=made.output, ag=made.ag, wire=made.out, sqw=sqw, mlpw=mlpw, gain=gain, gainm=gainm)
        like = jax.ShapeDtypeStruct
        near, far = 4, 3
        outs.update(
            output_f=like(made.output.shape, F32),
            ag_f=like(made.ag.shape, F32),
            sqg=like(sqw.shape, F32),
            sqm=like(sqw.shape, F32),
            sqn=like(sqw.shape, F32),
            sqc=like(sqw.shape, BF16),
            mlpg=like(mlpw.shape, F32),
            mlpm=like(mlpw.shape, F32),
            mlpn=like(mlpw.shape, F32),
            mlpc=like(mlpw.shape, BF16),
            gg=like(gain.shape, F32),
            gm=like(gain.shape, F32),
            gn=like(gain.shape, F32),
        )
    scratch = dict(
        og_v=VMEM(made.og.shape, F32),
        sems=pltpu.SemaphoreType.DMA((PARTS + 6,)),
    )
    if hasattr(made, "out"):
        scratch.update(
            sqw_v=VMEM(sqw.shape, F32),
            mlpw_v=VMEM(mlpw.shape, F32),
            gain_v=VMEM(gain.shape, F32),
            gainm_v=VMEM(gainm.shape, F32),
        )
    names = tuple(ins) + tuple(outs) + tuple(scratch)
    made_here = list(ins.values())
    stay = [pltpu.with_memory_space_constraint(value, pltpu.HBM) for value in made_here[near:]]
    results = pl.pallas_call(
        functools.partial(finish_kernel, names, rate),
        out_shape=tuple(outs.values()),
        in_specs=[in_vmem] * near + [any_space] * (len(ins) - near),
        out_specs=[any_space] * far + [in_vmem] * (len(outs) - far),
        scratch_shapes=list(scratch.values()),
        compiler_params=pltpu.CompilerParams(vmem_limit_bytes=16 << 20),
        name="finish",
    )(*made_here[:near], *stay)
    return Refs(zip(outs, results))


HIGH_PRECISION = lax.Precision.HIGHEST


def plain_orthogonalize(matrix):
    current = matrix / (jnp.sqrt(jnp.sum(matrix * matrix)) + 1e-07)
    for turn in range(5):
        gram = jnp.dot(current, current.T, precision=HIGH_PRECISION)
        poly = COEF_B * gram + COEF_C * jnp.dot(gram, gram, precision=HIGH_PRECISION)
        current = COEF_A * current + jnp.dot(poly, current, precision=HIGH_PRECISION)
    return current


def pick_owned(stack, owners, device):
    chosen = jnp.zeros_like(stack[0])
    for index in range(len(owners)):
        chosen = jnp.where(device == owners[index], stack[index], chosen)
    return chosen


def is_owner(owners, device):
    flag = device < 0
    for owner in owners:
        flag = jnp.logical_or(flag, device == owner)
    return flag


def from_wire(grads):
    def matrix(base, tiles):
        part = grads[:, base : base + tiles * TILE, :].reshape(-1, tiles, TILE, LANES)
        return part.transpose(0, 2, 1, 3).reshape(-1, tiles * LANES)

    square = jnp.stack([matrix(SQ_AT[m], 2) for m in range(5)])
    mlp = jnp.stack([matrix(m * MLP_ROWS, 8) for m in range(2)])
    return square, mlp, grads[0, GAIN_BASE : GAIN_BASE + 4, :].reshape(2, 2 * LANES)


def update_by_collectives(
    grads, square_weights, mlp_weights, gains, square_moment, mlp_moment, gain_moment, rate
):
    square_local, mlp_local, gain_local = from_wire(grads)
    square_grad, mlp_grad, gain_grad = (
        lax.psum_scatter(square_local, "dp", scatter_dimension=1, tiled=True),
        lax.psum_scatter(mlp_local, "dp", scatter_dimension=1, tiled=True),
        lax.psum_scatter(gain_local, "dp", scatter_dimension=1, tiled=True),
    )
    square_moment_new = 0.5 * square_moment + square_grad
    mlp_moment_new = 0.5 * mlp_moment + mlp_grad
    gain_moment_new = 0.5 * gain_moment + gain_grad
    device = lax.axis_index("dp")
    count = lax.axis_size("dp")
    square_owners = [index * count // 7 for index in range(5)]
    mlp_owners = [(index + 5) * count // 7 for index in range(2)]
    square_full, mlp_full = (
        lax.all_gather(square_moment_new, "dp", axis=1, tiled=True),
        lax.all_gather(mlp_moment_new, "dp", axis=1, tiled=True),
    )
    mine_square = pick_owned(square_full, square_owners, device)
    mine_mlp = pick_owned(mlp_full, mlp_owners, device)
    made_square = lax.cond(
        is_owner(square_owners, device), plain_orthogonalize, jnp.zeros_like, mine_square
    )
    made_mlp = lax.cond(is_owner(mlp_owners, device), plain_orthogonalize, jnp.zeros_like, mine_mlp)
    stack_square = jnp.stack(
        [jnp.where(device == owner, made_square, 0.0) for owner in square_owners]
    )
    stack_mlp = jnp.stack([jnp.where(device == owner, made_mlp, 0.0) for owner in mlp_owners])
    square_ortho, mlp_ortho = (
        lax.psum_scatter(stack_square, "dp", scatter_dimension=1, tiled=True),
        lax.psum_scatter(stack_mlp, "dp", scatter_dimension=1, tiled=True),
    )
    square_new = square_weights - jnp.array(SQ_RATES, F32)[:, None, None] * square_ortho
    mlp_new = mlp_weights - jnp.array(MLP_RATES, F32)[:, None, None] * mlp_ortho
    gains_new = gains - rate * gain_moment_new
    return (
        square_grad,
        square_moment_new,
        square_new,
        square_new.astype(BF16),
        mlp_grad,
        mlp_moment_new,
        mlp_new,
        mlp_new.astype(BF16),
        gain_grad,
        gain_moment_new,
        gains_new,
    )


def per_device(
    actions,
    observed,
    camera_flags,
    noise_levels,
    cotangent,
    square_weights,
    mlp_weights,
    gains,
    square_moment,
    mlp_moment,
    gain_moment,
):
    count = lax.axis_size("dp")
    rate = 0.1 / math.sqrt(actions.shape[0] * count)
    by_key = observed.transpose(1, 0, 2)
    ins = (actions, by_key, camera_flags, noise_levels, cotangent)
    if count == math.prod(GRID):
        made = block_and_back(True, *ins, square_weights, mlp_weights, gains, square_moment, mlp_moment)
        done = finish(rate, made, square_weights, mlp_weights, gains, gain_moment)
        output, actions_grad = done.output_f, done.ag_f
        d = done
        rest = (d.sqg, d.sqm, d.sqn, d.sqc, d.mlpg, d.mlpm, d.mlpn, d.mlpc, d.gg, d.gm, d.gn)
    else:
        square_all, mlp_all = (
            lax.all_gather(square_weights.astype(BF16), "dp", axis=1, tiled=True),
            lax.all_gather(mlp_weights.astype(BF16), "dp", axis=1, tiled=True),
        )
        gain_all = lax.all_gather(gains, "dp", axis=1, tiled=True)
        made = block_and_back(False, *ins, square_all, mlp_all, gain_all)
        done = finish(rate, made)
        output, actions_grad = made.output, made.ag
        grads = made.grads.reshape(-1, WIRE, LANES)
        rest = update_by_collectives(
            grads, square_weights, mlp_weights, gains, square_moment, mlp_moment, gain_moment, rate
        )
    observed_grad = done.og.transpose(1, 0, 2)
    return (output, actions_grad, observed_grad) + tuple(rest)


def solution(mesh):
    rows, cube, flat = P("dp", None), P("dp", None, None), P("dp")
    stacked, pair = P(None, "dp", None), P(None, "dp")
    return jax.shard_map(
        per_device,
        mesh=mesh,
        in_specs=(rows, cube, flat, flat, rows, stacked, stacked, pair, stacked, stacked, pair),
        out_specs=(rows, rows, cube) + (stacked,) * 8 + (pair,) * 3,
        check_vma=False,
    )
```

```python
import functools
import math

import jax
import jax.numpy as jnp
from jax import lax
from jax.experimental import pallas as pl
from jax.experimental.pallas import tpu as pltpu
from jax.sharding import PartitionSpec as P

HEADS = 4
ACT = 16
OBS_FULL = 196
OBS_FEW = 49
COEF_A = 3.4445
COEF_B = -4.775
COEF_C = 2.0315
F32 = jnp.float32
BF16 = jnp.bfloat16
MESH = pl.DeviceIdType.MESH
VMEM = pltpu.VMEM
NN = (((1,), (0,)), ((), ()))
NT = (((1,), (1,)), ((), ()))
TN = (((0,), (0,)), ((), ()))

LANES = 128
TILE = 8
MLP_ROWS = 64
SQ_ROWS = 16
SQ_AT = (160, 192, 176, 128, 144)
GAIN_BASE = 208
WIRE = 224
PIECES = ((0, 32), (32, 32), (64, 32), (96, 32), (128, 32), (160, 32), (192, 32))
PIECE_X_FIRST = (True, False, True, False, True, True, False)
CHUNKS = ((0, 32), (32, 32), (64, 32), (96, 32), (128, 32), (160, 32), (192, 16), (208, 16))
X_FIRST = (True, False, True, False, True, False, True, False)
PARTS_OUT = (
    (0, 0, 0, 32, 0),
    (1, 0, 32, 32, 32),
    (2, 1, 64, 32, 0),
    (3, 1, 96, 32, 32),
    (4, 5, 128, 16, 0),
    (4, 6, 144, 16, 0),
    (5, 2, 160, 16, 0),
    (5, 4, 176, 16, 0),
    (6, 3, 192, 16, 0),
)
MLP_RATES = (1.0, 0.5)
SQ_RATES = (0.5, 0.5, 0.5, 0.5, 4.0)
GRID = (4, 2, 2, 2)
OWNERS = (8, 22, 14, 16, 11, 21, 13)
SHIFTS = (0.0, 0.0, 0.4, 0.8, 0.8)
KEYS_PAD = 208
GROUP = 16
ROWS = 512


class Refs:
    def __init__(self, pairs):
        self.__dict__.update(pairs)


def dot(left, right, dims=NN):
    return lax.dot_general(left, right, dims, preferred_element_type=F32)


def place():
    me = lax.axis_index("dp")
    return me, me // 8, (me // 4) % 2, (me // 2) % 2, me % 2


def device_at(z, y, x, c):
    return ((z * 2 + y) * 2 + x) * 2 + c


def link(src, dst, send, recv, device):
    return pltpu.make_async_remote_copy(
        src_ref=src,
        dst_ref=dst,
        send_sem=send,
        recv_sem=recv,
        device_id=(device,),
        device_id_type=MESH,
    )


def greet(device):
    pl.semaphore_signal(
        pltpu.get_barrier_semaphore(), inc=1, device_id=(device,), device_id_type=MESH
    )


def normalize(values):
    centred = values - jnp.mean(values, -1, keepdims=True)
    scale = lax.rsqrt(jnp.mean(centred * centred, -1, keepdims=True) + 1e-05)
    return centred * scale, scale


def norm_back(grad, hat, scale):
    mean_one = jnp.mean(grad, -1, keepdims=True)
    mean_two = jnp.mean(grad * hat, -1, keepdims=True)
    return scale * (grad - mean_one - hat * mean_two)


class Gather:
    def __init__(self, r):
        self.r = r
        self.me, self.z, self.y, self.x, self.c = place()

    def hop(self, k, step, part, device):
        return link(part, part, self.r.gsend.at[k, step], self.r.grecv.at[k, step], device)

    def along_z(self, k, step):
        part = self.r.wire.at[self.z, self.y, self.x, self.c, pl.ds(*PIECES[k])]
        return self.hop(k, step, part, device_at((self.z + step + 1) % 4, self.y, self.x, self.c))

    def from_z(self, k, step):
        there = (self.z + 3 - step) % 4
        part = self.r.wire.at[there, self.y, self.x, self.c, pl.ds(*PIECES[k])]
        return self.hop(k, step, part, device_at(there, self.y, self.x, self.c))

    def plane(self, k, second, mine):
        z, y, x, c = self.z, self.y, self.x, self.c
        rows, wire = pl.ds(*PIECES[k]), self.r.wire
        py, px = (y, x) if mine else (1 - y, 1 - x)
        along_x = PIECE_X_FIRST[k] == second
        if along_x:
            part = wire.at[:, y, px, c, rows] if second else wire.at[:, :, px, c, rows]
            return self.hop(k, 3 if second else 4, part, device_at(z, y, 1 - x, c))
        part = wire.at[:, py, x, c, rows] if second else wire.at[:, py, :, c, rows]
        return self.hop(k, 3 if second else 4, part, device_at(z, 1 - y, x, c))

    def core(self, k, mine):
        part = self.r.wire.at[:, :, :, self.c if mine else 1 - self.c, pl.ds(*PIECES[k])]
        return self.hop(k, 5, part, device_at(self.z, self.y, self.x, 1 - self.c))

    def first(self, *chunks):
        for k in chunks:
            for step in range(3):
                self.along_z(k, step).start()

    def second(self, *chunks):
        for k in chunks:
            for step in range(3):
                self.from_z(k, step).wait_recv()
            self.plane(k, True, True).start()

    def third(self, *chunks):
        for k in chunks:
            self.plane(k, True, False).wait_recv()
            self.plane(k, False, True).start()

    def fourth(self, *chunks):
        for k in chunks:
            self.plane(k, False, False).wait_recv()
            self.core(k, True).start()

    def last(self, *chunks):
        for k in chunks:
            self.core(k, False).wait_recv()

    def drain(self):
        for k in range(len(PIECES)):
            for step in range(3):
                self.along_z(k, step).wait_send()
            self.plane(k, True, True).wait_send()
            self.plane(k, False, True).wait_send()
            self.core(k, True).wait_send()

    def fill(self):
        r = self.r
        spot = (self.z, self.y, self.x, self.c)

        def tiles(source, m, base, number):
            for j in range(number):
                pair = [source[m, :, pl.ds((2 * j + k) * LANES, LANES)] for k in range(2)]
                r.wire[spot + (pl.ds(base + j * 16, 16),)] = jnp.concatenate(pair, axis=0).astype(BF16)

        for m in range(5):
            tiles(r.sqw_v, m, SQ_AT[m], 1)
        for m in range(2):
            tiles(r.mlpw_v, m, m * MLP_ROWS, 4)
        gains, edge = r.gain_v[...], r.edge
        high = gains.astype(BF16).astype(F32)
        middle = (gains - high).astype(BF16).astype(F32)
        edge[...] = jnp.zeros_like(edge)
        edge[0:2, 0:TILE] = high
        edge[2:4, 0:TILE] = middle
        edge[4:6, 0:TILE] = (gains - high - middle).astype(BF16).astype(F32)
        r.wire[spot + (pl.ds(GAIN_BASE, 16),)] = edge[...].astype(BF16)

    def unpack(self, base, number, out, m):
        for j in range(number):
            block = self.r.wire[:, :, :, :, pl.ds(base + j * 16, 16), :].reshape(32, 16, LANES).astype(F32)
            for half in range(2):
                columns = pl.ds((2 * j + half) * LANES, LANES)
                out[m, :, columns] = block[:, half * 8 : half * 8 + 8, :].reshape(256, LANES).astype(BF16)

    def unpack_gains(self):
        edge, wire = self.r.edge, self.r.wire
        for half in range(2):
            total = jnp.zeros((16, LANES), F32)
            for at in range(16):
                d = half * 16 + at
                tile = wire[d // 8, (d // 4) % 2, (d // 2) % 2, d % 2, pl.ds(GAIN_BASE, 16), :].astype(F32)
                total = total + (tile if at == 0 else pltpu.roll(tile, at * TILE, 1))
            edge[...] = total
            self.r.gain_all[:, pl.ds(half * LANES, LANES)] = edge[0:2, :] + edge[2:4, :] + edge[4:6, :]


class Update:
    def __init__(self, r):
        self.r = r
        self.me, self.z, self.y, self.x, self.c = place()

    def hop(self, k, step, src, dst, device):
        return link(src, dst, self.r.send.at[k, step], self.r.recv.at[k, step], device)

    def core(self, k):
        rows = pl.ds(*CHUNKS[k])
        src, dst = self.r.send0.at[:, :, :, rows], self.r.got_core.at[:, :, :, rows]
        return self.hop(k, 0, src, dst, device_at(self.z, self.y, self.x, 1 - self.c))

    def plane(self, k, first):
        rows = pl.ds(*CHUNKS[k])
        to = (self.z, self.y, 1 - self.x, self.c) if X_FIRST[k] == first else (self.z, 1 - self.y, self.x, self.c)
        if first:
            src, dst = self.r.send1.at[:, :, rows], self.r.got1.at[:, :, rows]
        else:
            src, dst = self.r.send2.at[:, rows], self.r.got2.at[:, rows]
        return self.hop(k, 1 if first else 2, src, dst, device_at(*to))

    def along_z(self, k, step):
        rows = pl.ds(*CHUNKS[k])
        to = device_at((self.z + step + 1) % 4, self.y, self.x, self.c)
        return self.hop(k, 3 + step, self.r.send3.at[step, rows], self.r.got3.at[step, rows], to)

    def start(self, k):
        rows = pl.ds(*CHUNKS[k])
        self.r.send0[:, :, :, rows, :] = self.r.grads[:, :, :, 1 - self.c, rows, :].astype(BF16)
        self.core(k).start()

    def one(self, *chunks):
        r = self.r
        for k in chunks:
            rows = pl.ds(*CHUNKS[k])
            self.core(k).wait_recv()
            sum1 = r.sum1
            sum1[:, :, :, rows, :] = r.grads[:, :, :, self.c, rows, :] + r.got_core[:, :, :, rows, :].astype(F32)
            other = sum1[:, :, 1 - self.x, rows, :] if X_FIRST[k] else sum1[:, 1 - self.y, :, rows, :]
            r.send1[:, :, rows, :] = other.astype(BF16)
            self.plane(k, True).start()

    def two(self, *chunks):
        r = self.r
        for k in chunks:
            rows = pl.ds(*CHUNKS[k])
            self.plane(k, True).wait_recv()
            sum1, sum2 = r.sum1, r.sum2
            mine = sum1[:, :, self.x, rows, :] if X_FIRST[k] else sum1[:, self.y, :, rows, :]
            sum2[:, :, rows, :] = mine + r.got1[:, :, rows, :].astype(F32)
            other = 1 - self.y if X_FIRST[k] else 1 - self.x
            r.send2[:, rows, :] = sum2[:, other, rows, :].astype(BF16)
            self.plane(k, False).start()

    def three(self, *chunks):
        r = self.r
        for k in chunks:
            rows = pl.ds(*CHUNKS[k])
            self.plane(k, False).wait_recv()
            mine = self.y if X_FIRST[k] else self.x
            r.sum3[:, rows, :] = r.sum2[:, mine, rows, :] + r.got2[:, rows, :].astype(F32)
            for step in range(3):
                r.send3[step, rows, :] = r.sum3[(self.z + step + 1) % 4, rows, :].astype(BF16)
                self.along_z(k, step).start()

    def result(self, index):
        return self.r.result_mlp if index < 2 else self.r.result_sq

    def own_part(self, part):
        _, index, base, number, place = PARTS_OUT[part]
        if index < 2:
            return self.r.moment_low.at[pl.ds(base, number)], self.r.slabs_mlp.at[self.me, pl.ds(place, number)]
        return self.r.moment.at[pl.ds(base, number)], self.r.slabs_sq.at[self.me]

    def to_owner(self, part):
        src, dst = self.own_part(part)
        return link(src, dst, self.r.own_send.at[part], self.r.own_recv.at[0], OWNERS[PARTS_OUT[part][1]])

    def four(self, *chunks):
        r = self.r
        moment, out = r.moment, r.out
        for k in chunks:
            rows = pl.ds(*CHUNKS[k])
            total = r.sum3[self.z, rows, :]
            for step in range(3):
                self.along_z(k, step).wait_recv()
                total = total + r.got3[step, rows, :].astype(F32)
            out[0, rows, :] = total
            new = 0.5 * moment[rows, :] + total
            moment[rows, :] = new
            if k < 4:
                r.moment_low[rows, :] = new.astype(BF16)
            for part, (chunk, index, *_) in enumerate(PARTS_OUT):
                if chunk != k:
                    continue

                @pl.when(self.me != OWNERS[index])
                def _():
                    self.to_owner(part).start()

                @pl.when(self.me == OWNERS[index])
                def _():
                    src, dst = self.own_part(part)
                    pltpu.make_async_copy(src, dst, r.own_recv.at[0]).start()

    def old_moment(self):
        r = self.r
        moment = r.moment
        for m in range(2):
            for j in range(8):
                moment[pl.ds(m * MLP_ROWS + j * TILE, TILE), :] = r.mlpm_v[m, :, pl.ds(j * LANES, LANES)]
        for m in range(5):
            for j in range(2):
                moment[pl.ds(SQ_AT[m] + j * TILE, TILE), :] = r.sqm_v[m, :, pl.ds(j * LANES, LANES)]
        moment[pl.ds(GAIN_BASE, 16), :] = jnp.zeros((16, LANES), F32)

    def orthogonalize(self):
        r = self.r
        cur = r.cur
        rows = lax.broadcasted_iota(jnp.int32, (256, 256), 0)
        diagonal = rows == lax.broadcasted_iota(jnp.int32, (256, 256), 1)

        def run(slabs, result, tiles):
            pltpu.make_async_copy(slabs, slabs, r.own_recv.at[0]).wait()
            low = r.cur_low
            for j in range(tiles // 2):
                pair = slabs[:, pl.ds(j * 16, 16), :].astype(F32)
                for side in range(2):
                    columns = pl.ds((2 * j + side) * LANES, LANES)
                    part = pair[:, side * TILE : (side + 1) * TILE, :].reshape(256, LANES)
                    cur[:, columns] = part
                    low[:, columns] = part.astype(BF16)
            scale = 1.0
            for turn, shift in enumerate(SHIFTS):
                whole = low[:, 0 : tiles * LANES]
                off = dot(whole, whole, NT)
                if turn == 0:
                    norm = jnp.sum(jnp.sum(jnp.where(diagonal, off, 0.0), axis=0, keepdims=True), axis=1, keepdims=True)
                    scale = 1.0 / (jnp.sqrt(norm) + 1e-07)
                    off = off * (scale * scale)
                if shift:
                    off = off - jnp.where(diagonal, shift, 0.0)
                off_low = off.astype(BF16)
                poly = (COEF_B + 2.0 * COEF_C * shift) * off + COEF_C * dot(off_low, off_low)
                poly = poly.astype(BF16)
                keep = COEF_A + shift * (COEF_B + COEF_C * shift)
                for j in range(tiles // 2):
                    columns = pl.ds(j * 2 * LANES, 2 * LANES)
                    now = keep * cur[:, columns] + dot(poly, low[:, columns])
                    if turn == 0:
                        now = now * scale
                    if turn < len(SHIFTS) - 1:
                        cur[:, columns] = now
                        low[:, columns] = now.astype(BF16)
                    else:
                        parts = [now[:, side * LANES : (side + 1) * LANES].reshape(32, TILE, LANES) for side in range(2)]
                        result[:, pl.ds(j * 16, 16), :] = jnp.concatenate(parts, axis=1).astype(result.dtype)

        mine_mlp = jnp.logical_or(self.me == OWNERS[0], self.me == OWNERS[1])
        mine_sq = self.me < 0
        for device in OWNERS[2:]:
            mine_sq = jnp.logical_or(mine_sq, self.me == device)

        @pl.when(mine_mlp)
        def _():
            run(r.slabs_mlp, r.result_mlp, 8)

        @pl.when(mine_sq)
        def _():
            run(r.slabs_sq, r.result_sq, 2)

    def landing(self, index):
        if index < 2:
            return self.r.back_mlp.at[index]
        return self.r.out.at[2, pl.ds(SQ_AT[index - 2], SQ_ROWS)]

    def give_back(self, index, device):
        result = self.result(index)
        return link(
            result.at[device], self.landing(index),
            self.r.back_send.at[device], self.r.back_recv.at[index], device,
        )

    def give_all(self):
        r = self.r
        for index in range(7):
            result = self.result(index)

            @pl.when(self.me == OWNERS[index])
            def _():
                def send_one(step, _):
                    self.give_back(index, (self.me + step) % 32).start()
                    return 0

                lax.fori_loop(1, 32, send_one, 0)
                pltpu.make_async_copy(result.at[self.me], self.landing(index), r.back_recv.at[index]).start()

    def take_all(self):
        for index in range(7):
            result = self.result(index)
            pltpu.make_async_copy(result.at[0], self.landing(index), self.r.back_recv.at[index]).wait()
        for index in range(2):
            rows = pl.ds(index * MLP_ROWS, MLP_ROWS)
            self.r.out[2, rows, :] = self.r.back_mlp[index].astype(F32)

    def drain(self):
        for k in range(len(CHUNKS)):
            self.core(k).wait_send()
            self.plane(k, True).wait_send()
            self.plane(k, False).wait_send()
            for step in range(3):
                self.along_z(k, step).wait_send()
        for part in range(len(PARTS_OUT)):

            @pl.when(self.me != OWNERS[PARTS_OUT[part][1]])
            def _():
                self.to_owner(part).wait_send()

    def drain_owner(self):
        for index in range(7):

            @pl.when(self.me == OWNERS[index])
            def _():
                def wait_one(step, _):
                    self.give_back(index, (self.me + step) % 32).wait_send()
                    return 0

                lax.fori_loop(1, 32, wait_one, 0)


def greet_all():
    me, z, y, x, c = place()
    greet(device_at(z, y, x, 1 - c))
    greet(device_at(z, y, 1 - x, c))
    greet(device_at(z, 1 - y, x, c))
    for step in range(1, 4):
        greet(device_at((z + step) % 4, y, x, c))
    owner = me < 0
    for device in OWNERS:
        owner = jnp.logical_or(owner, me == device)

        @pl.when(me != device)
        def _():
            greet(device)

    @pl.when(owner)
    def _():
        def greet_other(step, _):
            greet((me + step) % 32)
            return 0

        lax.fori_loop(1, 32, greet_other, 0)

    is_owner = owner.astype(jnp.int32)
    return 6 + 7 - is_owner + 31 * is_owner


def block_kernel(names, remote, *args):
    r = Refs(zip(names, args))
    keys, samples = r.obs.shape[0], r.obs.shape[1]
    tokens, width = r.acts.shape
    head_dim, half, per = width // HEADS, width // 2, ROWS // ACT
    wide = r.mlp_all.shape[2]
    groups = samples // GROUP
    in_sems, out_sems = r.in_sems, r.out_sems

    if remote:
        own = (r.sqw_v, r.mlpw_v, r.gain_v)
    else:
        own = (r.sq_all, r.mlp_all, r.gain_all)
    loads = list(zip((r.sqw, r.mlpw, r.gain), own))
    loads += [(r.acts, r.acts_v), (r.obs, r.obs_v.at[pl.ds(0, keys)]), (r.cot, r.cot_v)]
    if remote:
        loads += [(r.sqm, r.sqm_v), (r.mlpm, r.mlpm_v)]
    loads += [(r.flags, r.flags_s), (r.levels, r.levels_s)]
    copies = [pltpu.make_async_copy(a, b, in_sems.at[i]) for i, (a, b) in enumerate(loads)]

    def arrive(*which):
        for i in which:
            copies[i].wait()

    for copy in copies:
        copy.start()
    if remote:
        gather, update = Gather(r), Update(r)
        expected = greet_all()
        arrive(0, 1, 2)
        gather.fill()
        pl.semaphore_wait(pltpu.get_barrier_semaphore(), expected)
        gather.first(5, 6, 4, 0, 1, 2, 3)

    arrive(3)

    def hats(i, _):
        rows = pl.ds(pl.multiple_of(i * ROWS, ROWS), ROWS)
        hat, scale = normalize(r.acts_v[rows, :])
        r.xhat[rows, :] = hat
        r.rstd[rows, :] = scale
        return 0

    lax.fori_loop(0, tokens // ROWS, hats, 0)

    mem, obs_v = r.mem, r.obs_v
    batch = 16
    chunks = KEYS_PAD // batch
    swap = r.swap
    row = lax.broadcasted_iota(jnp.int32, swap.shape, 0)
    column = lax.broadcasted_iota(jnp.int32, swap.shape, 1)
    swap[...] = jnp.where(column == (row % batch) * batch + row // batch, 1.0, 0.0).astype(BF16)

    def turn(part, low, high):
        def one(j, _):
            at = pl.ds(pl.multiple_of(j * batch, batch), batch)
            here = pl.ds(part * batch, batch)
            block = obs_v[at, here, :].reshape(batch * batch, width)
            mem[here, at, :] = dot(swap[...], block).astype(BF16).reshape(batch, batch, width)
            return 0

        lax.fori_loop(low, high, one, 0, unroll=high - low)

    whole = chunks - 1
    arrive(4)
    turn(0, 0, whole // 2)
    if remote:
        gather.second(5, 6)
    turn(0, whole // 2, whole)
    if remote:
        gather.third(5, 6)
    turn(1, 0, whole // 2)
    if remote:
        gather.second(4, 0, 1)
        gather.fourth(5, 6)
    turn(1, whole // 2, whole)
    if remote:
        gather.second(2, 3)
    arrive(len(copies) - 1, len(copies) - 2)
    freqs = jnp.exp(
        lax.broadcasted_iota(jnp.int32, (1, half), 1).astype(F32) * F32(-math.log(10000.0)) / half
    )
    for s in range(samples):
        r.angle[s : s + 1, :] = r.levels_s[s].astype(F32) * freqs
    r.embed[:, 0:half] = jnp.sin(r.angle[...]).astype(BF16)
    r.embed[:, half:width] = jnp.cos(r.angle[...]).astype(BF16)
    if remote:
        arrive(6, 7)
        update.old_moment()
        gather.third(4, 0, 1)
        gather.last(5, 6)
        for m in range(3):
            gather.unpack(SQ_AT[m], 1, r.sq_all, m)
        gather.unpack_gains()
    else:
        arrive(0, 1, 2)

    sq, mlp = r.sq_all, r.mlp_all
    wkh, wvh = r.wkh, r.wvh
    lane = lax.broadcasted_iota(jnp.int32, (width, width), 1)

    def split_heads(out, weight):
        weight = weight.astype(F32)
        for h in range(HEADS):
            out[pl.ds(h * width, width), :] = jnp.where(lane // head_dim == h, weight, 0.0).astype(BF16)

    split_heads(wkh, sq[2])
    g1, g2 = r.gain_all[0:1, :], r.gain_all[1:2, :]

    obs_v[keys] = dot(r.embed[...], sq[0]).astype(BF16)
    obs_v[keys + 1 :] = jnp.zeros((KEYS_PAD - keys - 1, samples, width), BF16)
    for part in range(samples // batch):
        turn(part, whole, chunks)

    queries, dmixes = r.queries, r.dmixes

    def make_queries(i, _):
        rows = pl.ds(pl.multiple_of(i * ROWS, ROWS), ROWS)
        first = (r.xhat[rows, :] * g1).astype(BF16)
        r.first[rows, :] = first
        q = dot(first, sq[1]).astype(BF16)
        r.query[rows, :] = q
        here = pl.ds(i * per, per)
        for h in range(HEADS):
            wk = wkh[pl.ds(h * width, width), :]
            value = (dot(q, wk, NT) * 0.125).astype(BF16).reshape(per, ACT, width)
            queries[here, pl.ds(h * ACT, ACT), :] = value
        return 0

    lax.fori_loop(0, tokens // ROWS, make_queries, 0)

    key = lax.broadcasted_iota(jnp.int32, (KEYS_PAD, LANES), 0)
    rows_each = HEADS * ACT
    left = lax.broadcasted_iota(jnp.int32, (KEYS_PAD, LANES), 1) < rows_each
    left_row = lax.broadcasted_iota(jnp.int32, (1, LANES), 1) < rows_each
    rest = jnp.where((key >= OBS_FEW) & (key < OBS_FULL), 1.0, 0.0)
    padding = jnp.where(key > OBS_FULL, -1000000000.0, 0.0)

    def with_memory(s, sides):
        here = pl.ds(s, 4)
        wide = dot(mem[here].reshape(4 * KEYS_PAD, width), sides[here].reshape(4 * rows_each, width), NT)
        part = [wide[k * KEYS_PAD : (k + 1) * KEYS_PAD, (k // 2) * LANES : (k // 2 + 1) * LANES] for k in range(4)]
        return jnp.where(left, part[0], part[1]), jnp.where(left, part[2], part[3])

    def each_head(out, s, value):
        rows = pl.ds(pl.multiple_of(s * ACT, ACT), ACT)
        for h in range(HEADS):
            out[rows, pl.ds(h * width, width)] = value[h * ACT : (h + 1) * ACT, :]

    def attend(g, _):
        pairs = []
        for quad in range(GROUP // 4):
            pairs.extend(with_memory(g * GROUP + 4 * quad, queries))
        turned = []
        for k, score in enumerate(pairs):
            s = g * GROUP + 2 * k
            drop = [(1 - r.flags_s[s + side]).astype(F32) * -1000000000.0 for side in range(2)]
            score = score + (rest * jnp.where(left_row, drop[0], drop[1]) + padding)
            expo = jnp.exp(score - jnp.max(score, 0, keepdims=True))
            probs = expo * (1.0 / jnp.sum(expo, 0, keepdims=True))
            r.probs[g * (GROUP // 2) + k] = probs
            turned.append(probs.astype(BF16).T)
        for k, low in enumerate(turned):
            for side in range(2):
                s = g * GROUP + 2 * k + side
                each_head(r.u, s, dot(low[side * rows_each : (side + 1) * rows_each], mem[s]).astype(BF16))
        return 0

    lax.fori_loop(0, groups // 2, attend, 0)
    if remote:
        gather.third(2, 3)
        gather.fourth(4, 0, 1)
    lax.fori_loop(groups // 2, groups, attend, 0)
    if remote:
        gather.fourth(2, 3)
        gather.last(4)
        for m in range(3, 5):
            gather.unpack(SQ_AT[m], 1, sq, m)
    split_heads(wvh, sq[3])

    gain_acc = r.gain_acc
    gain_acc[...] = jnp.zeros_like(gain_acc)
    blocks = [pl.ds(i * ROWS, ROWS) for i in range(tokens // ROWS)]
    for rows in blocks:
        mixed = dot(r.u[rows, :], wvh[...]).astype(BF16)
        r.mixed[rows, :] = mixed
        resid = r.acts_v[rows, :] + dot(mixed, sq[4])
        r.resid[rows, :] = resid
        hat, scale = normalize(resid)
        r.hat_two[rows, :] = hat
        r.rstd_two[rows, :] = scale
        r.second[rows, :] = (hat * g2).astype(BF16)
    arrive(5)
    r.out_low[...] = r.cot_v[...].astype(BF16)
    if remote:
        gather.last(0, 1)
        gather.unpack(0, 4, mlp, 0)
    wide_blocks = [pl.ds(c * 256, 256) for c in range(wide // 256)]
    for rows in blocks:
        for columns in wide_blocks:
            v = dot(r.second[rows, :], mlp[0, :, columns])
            square = v * v
            t = jnp.tanh(0.7978845608 * (v + 0.044715 * square * v))
            r.active[rows, columns] = (0.5 * v * (1.0 + t)).astype(BF16)
            slope = 0.5 * (1.0 + t) + 0.5 * v * (1.0 - t * t) * (0.7978845608 * (1.0 + 0.134145 * square))
            r.slope[rows, columns] = slope

    grads = r.grads

    def put(base, tiles, value):
        for j in range(tiles):
            part = value[:, j * LANES : (j + 1) * LANES].reshape(GRID + (TILE, LANES))
            grads[:, :, :, :, pl.ds(base + j * TILE, TILE), :] = part

    def by_head(left, right):
        turned = left.T
        parts = [
            dot(turned[h * head_dim : (h + 1) * head_dim, :], right[:, pl.ds(h * width, width)])
            for h in range(HEADS)
        ]
        return jnp.concatenate(parts, axis=0).T

    put(MLP_ROWS, 8, dot(r.out_low[...], r.active[...], TN))
    if remote:
        update.start(2)
        update.start(3)
        gather.last(2, 3)
        gather.unpack(MLP_ROWS, 4, mlp, 1)
    for rows in blocks:
        for columns in wide_blocks:
            slope = r.slope[rows, columns]
            r.dhidden[rows, columns] = (slope * dot(r.out_low[rows, :], mlp[1, :, columns])).astype(BF16)
    put(0, 8, dot(r.second[...], r.dhidden[...], TN))
    if remote:
        update.start(0)
        update.start(1)
        update.one(2, 3)
    for i, rows in enumerate(blocks):
        r.out_v[rows, :] = r.resid[rows, :] + dot(r.active[rows, :], mlp[1], NT)
        grad_second = dot(r.dhidden[rows, :], mlp[0], NT)
        hat = r.hat_two[rows, :]
        gain_acc[1:2, :] += jnp.sum(grad_second * hat, 0, keepdims=True)
        dres = r.cot_v[rows, :] + norm_back(grad_second * g2, hat, r.rstd_two[rows, :])
        r.dres[rows, :] = dres
        low = dres.astype(BF16)
        r.dres_low[rows, :] = low
        gm = dot(low, sq[4], NT).astype(BF16)
        r.dmixed[rows, :] = gm
        here = pl.ds(i * per, per)
        for h in range(HEADS):
            wv = wvh[pl.ds(h * width, width), :]
            dmixes[here, pl.ds(h * ACT, ACT), :] = dot(gm, wv, NT).astype(BF16).reshape(per, ACT, width)
    keep_out = pltpu.make_async_copy(r.out_v, r.output, out_sems.at[0])
    keep_out.start()
    if remote:
        update.one(0, 1)
    put(SQ_AT[4], 2, dot(r.mixed[...], r.dres_low[...], TN))
    put(SQ_AT[3], 2, by_head(r.dmixed[...], r.u))
    if remote:
        update.start(4)

    left_low = jnp.where(left_row, 1.0, 0.0).astype(BF16)
    right_low = jnp.where(left_row, 0.0, 1.0).astype(BF16)

    def attend_back(g, _):
        pairs = []
        for quad in range(GROUP // 4):
            pairs.extend(with_memory(g * GROUP + 4 * quad, dmixes))
        lows = []
        for k, rise in enumerate(pairs):
            probs = r.probs[g * (GROUP // 2) + k]
            both = probs * rise
            dscore = (both - probs * jnp.sum(both, 0, keepdims=True)).astype(BF16)
            lows.append((probs.astype(BF16), dscore, dscore.T))
        for k, (low, dscore, turned) in enumerate(lows):
            s = g * GROUP + 2 * k
            for side in range(2):
                dq = dot(turned[side * rows_each : (side + 1) * rows_each], mem[s + side]) * 0.125
                each_head(r.dq_wide, s + side, dq.astype(BF16))
            here = pl.ds(s, 2)
            sides = jnp.concatenate(
                [x[here].reshape(2 * rows_each, width) for x in (dmixes, queries)], axis=0
            )
            own = [jnp.concatenate([low * keep, dscore * keep], axis=1) for keep in (left_low, right_low)]
            dmem = dot(jnp.concatenate(own, axis=0), sides)
            for side in range(2):
                rows = dmem[side * KEYS_PAD : (side + 1) * KEYS_PAD, :]
                mem[s + side] = rows.astype(BF16)
                r.stamps[s + side] = rows[192:200, :]
        return 0

    lax.fori_loop(0, groups // 2, attend_back, 0)
    if remote:
        update.two(2, 3)
        update.one(4)
        update.two(0, 1)
    lax.fori_loop(groups // 2, groups, attend_back, 0)
    if remote:
        update.three(2, 3)
        update.two(4)
    put(SQ_AT[2], 2, by_head(r.query[...], r.dq_wide))
    stamp_low = r.stamps[:, 4:5, :].reshape(samples, width).astype(BF16)
    put(SQ_AT[0], 2, dot(r.embed[...], stamp_low, TN))
    if remote:
        update.start(5)
        update.three(0, 1)

    def keep_og(part):
        here = pl.ds(part * batch, batch)
        return pltpu.make_async_copy(obs_v.at[pl.ds(0, keys), here], r.og.at[:, here], out_sems.at[2 + part])

    def turn_back(part):
        def one(j):
            at = pl.ds(pl.multiple_of(j * batch, batch), batch)
            here = pl.ds(part * batch, batch)
            block = mem[here, at, :].reshape(batch * batch, width)
            value = dot(swap[...], block).astype(BF16).reshape(batch, batch, width)
            obs_v[at, here, :] = value

        for j in range(chunks):
            one(j)
        keep_og(part).start()

    def queries_back(i, _):
        rows = pl.ds(pl.multiple_of(i * ROWS, ROWS), ROWS)
        r.dquery[rows, :] = dot(r.dq_wide[rows, :], wkh[...]).astype(BF16)
        return 0

    lax.fori_loop(0, tokens // ROWS, queries_back, 0)
    put(SQ_AT[1], 2, dot(r.first[...], r.dquery[...], TN))
    if remote:
        update.start(6)
        update.one(5)

    def acts_back(i, _):
        rows = pl.ds(pl.multiple_of(i * ROWS, ROWS), ROWS)
        grad_first = dot(r.dquery[rows, :], sq[1], NT)
        hat = r.xhat[rows, :]
        gain_acc[0:1, :] += jnp.sum(grad_first * hat, 0, keepdims=True)
        r.ag_v[rows, :] = r.dres[rows, :] + norm_back(grad_first * g1, hat, r.rstd[rows, :])
        return 0

    def finish_acts():
        lax.fori_loop(0, tokens // ROWS, acts_back, 0)
        for norm in range(2):
            for j in range(2):
                row = gain_acc[norm : norm + 1, j * LANES : (j + 1) * LANES]
                at = GAIN_BASE + norm * 2 + j
                value = jnp.broadcast_to(row.reshape(1, 1, 1, 1, 1, LANES), GRID + (1, LANES))
                grads[:, :, :, :, at : at + 1, :] = value
        rest = WIRE - GAIN_BASE - 4
        grads[:, :, :, :, GAIN_BASE + 4 : WIRE, :] = jnp.zeros(GRID + (rest, LANES), F32)

    keep_ag = pltpu.make_async_copy(r.ag_v, r.ag, out_sems.at[1])
    if remote:
        finish_acts()
        keep_ag.start()
        update.start(7)
        update.one(6)
        update.three(4)
        update.four(2, 3)
        update.two(5)
        update.one(7)
        turn_back(0)
        update.two(6)
        update.four(0, 1)
        update.three(5)
        update.two(7)
        update.four(4)
        update.three(6)
        update.four(5)
        update.three(7)
        update.four(6)
        update.orthogonalize()
        update.give_all()
        turn_back(1)
        update.four(7)
        out = r.out
        out[1, :, :] = r.moment[...]
        out[2, pl.ds(GAIN_BASE, 16), :] = jnp.zeros((16, LANES), F32)
        gather.drain()
        update.drain()
        update.take_all()
        update.drain_owner()
    else:
        finish_acts()
        keep_ag.start()
        for part in range(samples // batch):
            turn_back(part)
    for copy in (keep_out, keep_ag, *(keep_og(part) for part in range(samples // batch))):
        copy.wait()


def block_and_back(remote, acts, obs, flags, levels, cot, sqw, mlpw, gain, sqm=None, mlpm=None):
    tokens, width = acts.shape
    keys, samples = obs.shape[0], obs.shape[1]
    rows = HEADS * ACT
    wide = mlpw.shape[2]
    any_space = pl.BlockSpec(memory_space=pl.ANY)
    in_vmem = pl.BlockSpec(memory_space=VMEM)
    sem = pltpu.SemaphoreType.DMA
    ins = dict(flags=flags, levels=levels, acts=acts, obs=obs, cot=cot, sqw=sqw, mlpw=mlpw, gain=gain)
    outs = dict(
        output=jax.ShapeDtypeStruct(acts.shape, F32),
        ag=jax.ShapeDtypeStruct(acts.shape, F32),
        og=jax.ShapeDtypeStruct(obs.shape, BF16),
    )
    grads = GRID + (WIRE, LANES)
    scratch = dict(
        obs_v=VMEM((KEYS_PAD, samples, width), BF16),
        acts_v=VMEM(acts.shape, F32),
        cot_v=VMEM(acts.shape, F32),
        mem=VMEM((samples, KEYS_PAD, width), BF16),
        swap=VMEM((256, 256), BF16),
        sq_all=VMEM((5, width, width), BF16),
        mlp_all=VMEM((2, width, wide), BF16),
        gain_all=VMEM((2, width), F32),
        wkh=VMEM((HEADS * width, width), BF16),
        wvh=VMEM((HEADS * width, width), BF16),
        first=VMEM((tokens, width), BF16),
        query=VMEM((tokens, width), BF16),
        xhat=VMEM((tokens, width), F32),
        rstd=VMEM((tokens, 1), F32),
        probs=VMEM((samples // 2, KEYS_PAD, LANES), F32),
        queries=VMEM((samples, rows, width), BF16),
        dmixes=VMEM((samples, rows, width), BF16),
        u=VMEM((tokens, HEADS * width), BF16),
        dq_wide=VMEM((tokens, HEADS * width), BF16),
        mixed=VMEM((tokens, width), BF16),
        second=VMEM((tokens, width), BF16),
        active=VMEM((tokens, wide), BF16),
        dhidden=VMEM((tokens, wide), BF16),
        out_low=VMEM((tokens, width), BF16),
        dres_low=VMEM((tokens, width), BF16),
        dres=VMEM((tokens, width), F32),
        resid=VMEM((tokens, width), F32),
        hat_two=VMEM((tokens, width), F32),
        rstd_two=VMEM((tokens, 1), F32),
        slope=VMEM((tokens, wide), F32),
        dmixed=VMEM((tokens, width), BF16),
        dquery=VMEM((tokens, width), BF16),
        out_v=VMEM((tokens, width), F32),
        ag_v=VMEM((tokens, width), F32),
        angle=VMEM((samples, width // 2), F32),
        embed=VMEM((samples, width), BF16),
        stamps=VMEM((samples, 8, width), F32),
        gain_acc=VMEM((8, width), F32),
        flags_s=pltpu.SMEM(flags.shape, jnp.int32),
        levels_s=pltpu.SMEM(levels.shape, jnp.int32),
        in_sems=sem((10,)),
        out_sems=sem((2 + samples // 16,)),
    )
    extra = {}
    if remote:
        ins.update(sqm=sqm, mlpm=mlpm)
        outs.update(out=jax.ShapeDtypeStruct((3, WIRE, LANES), F32))
        chunks = len(CHUNKS)
        scratch.update(
            grads=VMEM(grads, F32),
            sqw_v=VMEM(sqw.shape, F32),
            mlpw_v=VMEM(mlpw.shape, F32),
            gain_v=VMEM(gain.shape, F32),
            sqm_v=VMEM(sqm.shape, F32),
            mlpm_v=VMEM(mlpm.shape, F32),
            wire=VMEM(grads, BF16),
            edge=VMEM((16, LANES), F32),
            gsend=sem((len(PIECES), 6)),
            grecv=sem((len(PIECES), 6)),
            send0=VMEM((4, 2, 2, WIRE, LANES), BF16),
            got_core=VMEM((4, 2, 2, WIRE, LANES), BF16),
            sum1=VMEM((4, 2, 2, WIRE, LANES), F32),
            send1=VMEM((4, 2, WIRE, LANES), BF16),
            got1=VMEM((4, 2, WIRE, LANES), BF16),
            sum2=VMEM((4, 2, WIRE, LANES), F32),
            send2=VMEM((4, WIRE, LANES), BF16),
            got2=VMEM((4, WIRE, LANES), BF16),
            sum3=VMEM((4, WIRE, LANES), F32),
            send3=VMEM((3, WIRE, LANES), BF16),
            got3=VMEM((3, WIRE, LANES), BF16),
            moment=VMEM((WIRE, LANES), F32),
            slabs_sq=VMEM((32, SQ_ROWS, LANES), F32),
            slabs_mlp=VMEM((32, MLP_ROWS, LANES), BF16),
            moment_low=VMEM((2 * MLP_ROWS, LANES), BF16),
            back_mlp=VMEM((2, MLP_ROWS, LANES), BF16),
            result_sq=VMEM((32, SQ_ROWS, LANES), F32),
            result_mlp=VMEM((32, MLP_ROWS, LANES), BF16),
            cur=VMEM((width, wide), F32),
            cur_low=VMEM((width, wide), BF16),
            send=sem((chunks, 6)),
            recv=sem((chunks, 6)),
            own_send=sem((len(PARTS_OUT),)),
            own_recv=sem((1,)),
            back_send=sem((32,)),
            back_recv=sem((7,)),
        )
        extra = dict(collective_id=0, has_side_effects=True)
        outs = {name: VMEM(like.shape, like.dtype) for name, like in outs.items()}
    else:
        outs.update(grads=jax.ShapeDtypeStruct(grads, F32))
    names = tuple(ins) + tuple(outs) + tuple(scratch)
    stay = [pltpu.with_memory_space_constraint(value, pltpu.HBM) for value in ins.values()]
    results = pl.pallas_call(
        functools.partial(block_kernel, names, remote),
        out_shape=tuple(outs.values()),
        in_specs=[any_space] * len(ins),
        out_specs=[any_space] * 3 + [in_vmem],
        scratch_shapes=list(scratch.values()),
        compiler_params=pltpu.CompilerParams(vmem_limit_bytes=50 << 20, **extra),
        name="block_and_back",
    )(*stay)
    return Refs(zip(outs, results))


PARTS = 7


def finish_kernel(names, rate, *args):
    r = Refs(zip(names, args))
    sems = r.sems
    keys = r.og.shape[0]
    step = keys // PARTS

    def leave(part):
        block = pl.ds(part * step, step)
        return pltpu.make_async_copy(r.og_v.at[block], r.og.at[block], sems.at[part])

    more = PARTS
    moves = []
    if hasattr(r, "wire"):
        pairs = [(r.sqw, r.sqw_v), (r.mlpw, r.mlpw_v), (r.gain, r.gain_v), (r.gainm, r.gainm_v)]
        pairs += [(r.output, r.output_f), (r.ag, r.ag_f)]
        for source, target in pairs:
            moves.append(pltpu.make_async_copy(source, target, sems.at[more]))
            moves[-1].start()
            more += 1
    for part in range(PARTS):

        def widen(j, _):
            r.og_v[j] = r.low[j].astype(F32)
            return 0

        lax.fori_loop(part * step, (part + 1) * step, widen, 0, unroll=4)
        leave(part).start()
    for copy in moves[:4]:
        copy.wait()
    if hasattr(r, "wire"):
        finish_weights(r, rate)
    for part in range(PARTS):
        leave(part).wait()
    for copy in moves[4:]:
        copy.wait()


def finish_weights(r, rate):
    wire = r.wire
    me = lax.axis_index("dp")
    for m in range(5):
        for j in range(2):
            rows, columns = pl.ds(SQ_AT[m] + j * TILE, TILE), pl.ds(j * LANES, LANES)
            r.sqg[m, :, columns] = wire[0, rows, :]
            r.sqm[m, :, columns] = wire[1, rows, :]
            r.sqn[m, :, columns] = r.sqw_v[m, :, columns] - SQ_RATES[m] * wire[2, rows, :]
    r.sqc[...] = r.sqn[...].astype(BF16)
    for m in range(2):
        for j in range(8):
            rows, columns = pl.ds(m * MLP_ROWS + j * TILE, TILE), pl.ds(j * LANES, LANES)
            r.mlpg[m, :, columns] = wire[0, rows, :]
            r.mlpm[m, :, columns] = wire[1, rows, :]
            r.mlpn[m, :, columns] = r.mlpw_v[m, :, columns] - MLP_RATES[m] * wire[2, rows, :]
    r.mlpc[...] = r.mlpn[...].astype(BF16)
    tile = wire[0, pl.ds(GAIN_BASE, TILE), :]
    turned = pltpu.roll(tile, (LANES - (me % 16) * TILE) % LANES, 1)
    at = me // 16
    for norm in range(2):
        pair = turned[2 * norm : 2 * norm + 2, 0:TILE]
        row = jnp.where(at == 0, pair[0:1, :], pair[1:2, :])
        new = 0.5 * r.gainm_v[norm : norm + 1, :] + row
        r.gg[norm : norm + 1, :] = row
        r.gm[norm : norm + 1, :] = new
        r.gn[norm : norm + 1, :] = r.gain_v[norm : norm + 1, :] - rate * new


def finish(rate, made, sqw=None, mlpw=None, gain=None, gainm=None):
    any_space = pl.BlockSpec(memory_space=pl.ANY)
    in_vmem = pl.BlockSpec(memory_space=VMEM)
    ins = dict(low=made.og)
    outs = dict(og=jax.ShapeDtypeStruct(made.og.shape, F32))
    near, far = 1, 1
    if hasattr(made, "out"):
        ins.update(output=made.output, ag=made.ag, wire=made.out, sqw=sqw, mlpw=mlpw, gain=gain, gainm=gainm)
        like = jax.ShapeDtypeStruct
        near, far = 4, 3
        outs.update(
            output_f=like(made.output.shape, F32),
            ag_f=like(made.ag.shape, F32),
            sqg=like(sqw.shape, F32),
            sqm=like(sqw.shape, F32),
            sqn=like(sqw.shape, F32),
            sqc=like(sqw.shape, BF16),
            mlpg=like(mlpw.shape, F32),
            mlpm=like(mlpw.shape, F32),
            mlpn=like(mlpw.shape, F32),
            mlpc=like(mlpw.shape, BF16),
            gg=like(gain.shape, F32),
            gm=like(gain.shape, F32),
            gn=like(gain.shape, F32),
        )
    scratch = dict(
        og_v=VMEM(made.og.shape, F32),
        sems=pltpu.SemaphoreType.DMA((PARTS + 6,)),
    )
    if hasattr(made, "out"):
        scratch.update(
            sqw_v=VMEM(sqw.shape, F32),
            mlpw_v=VMEM(mlpw.shape, F32),
            gain_v=VMEM(gain.shape, F32),
            gainm_v=VMEM(gainm.shape, F32),
        )
    names = tuple(ins) + tuple(outs) + tuple(scratch)
    made_here = list(ins.values())
    stay = [pltpu.with_memory_space_constraint(value, pltpu.HBM) for value in made_here[near:]]
    results = pl.pallas_call(
        functools.partial(finish_kernel, names, rate),
        out_shape=tuple(outs.values()),
        in_specs=[in_vmem] * near + [any_space] * (len(ins) - near),
        out_specs=[any_space] * far + [in_vmem] * (len(outs) - far),
        scratch_shapes=list(scratch.values()),
        compiler_params=pltpu.CompilerParams(vmem_limit_bytes=16 << 20),
        name="finish",
    )(*made_here[:near], *stay)
    return Refs(zip(outs, results))


HIGH_PRECISION = lax.Precision.HIGHEST


def plain_orthogonalize(matrix):
    current = matrix / (jnp.sqrt(jnp.sum(matrix * matrix)) + 1e-07)
    for turn in range(5):
        gram = jnp.dot(current, current.T, precision=HIGH_PRECISION)
        poly = COEF_B * gram + COEF_C * jnp.dot(gram, gram, precision=HIGH_PRECISION)
        current = COEF_A * current + jnp.dot(poly, current, precision=HIGH_PRECISION)
    return current


def pick_owned(stack, owners, device):
    chosen = jnp.zeros_like(stack[0])
    for index in range(len(owners)):
        chosen = jnp.where(device == owners[index], stack[index], chosen)
    return chosen


def is_owner(owners, device):
    flag = device < 0
    for owner in owners:
        flag = jnp.logical_or(flag, device == owner)
    return flag


def from_wire(grads):
    def matrix(base, tiles):
        part = grads[:, base : base + tiles * TILE, :].reshape(-1, tiles, TILE, LANES)
        return part.transpose(0, 2, 1, 3).reshape(-1, tiles * LANES)

    square = jnp.stack([matrix(SQ_AT[m], 2) for m in range(5)])
    mlp = jnp.stack([matrix(m * MLP_ROWS, 8) for m in range(2)])
    return square, mlp, grads[0, GAIN_BASE : GAIN_BASE + 4, :].reshape(2, 2 * LANES)


def update_by_collectives(
    grads, square_weights, mlp_weights, gains, square_moment, mlp_moment, gain_moment, rate
):
    square_local, mlp_local, gain_local = from_wire(grads)
    square_grad, mlp_grad, gain_grad = (
        lax.psum_scatter(square_local, "dp", scatter_dimension=1, tiled=True),
        lax.psum_scatter(mlp_local, "dp", scatter_dimension=1, tiled=True),
        lax.psum_scatter(gain_local, "dp", scatter_dimension=1, tiled=True),
    )
    square_moment_new = 0.5 * square_moment + square_grad
    mlp_moment_new = 0.5 * mlp_moment + mlp_grad
    gain_moment_new = 0.5 * gain_moment + gain_grad
    device = lax.axis_index("dp")
    count = lax.axis_size("dp")
    square_owners = [index * count // 7 for index in range(5)]
    mlp_owners = [(index + 5) * count // 7 for index in range(2)]
    square_full, mlp_full = (
        lax.all_gather(square_moment_new, "dp", axis=1, tiled=True),
        lax.all_gather(mlp_moment_new, "dp", axis=1, tiled=True),
    )
    mine_square = pick_owned(square_full, square_owners, device)
    mine_mlp = pick_owned(mlp_full, mlp_owners, device)
    made_square = lax.cond(
        is_owner(square_owners, device), plain_orthogonalize, jnp.zeros_like, mine_square
    )
    made_mlp = lax.cond(is_owner(mlp_owners, device), plain_orthogonalize, jnp.zeros_like, mine_mlp)
    stack_square = jnp.stack(
        [jnp.where(device == owner, made_square, 0.0) for owner in square_owners]
    )
    stack_mlp = jnp.stack([jnp.where(device == owner, made_mlp, 0.0) for owner in mlp_owners])
    square_ortho, mlp_ortho = (
        lax.psum_scatter(stack_square, "dp", scatter_dimension=1, tiled=True),
        lax.psum_scatter(stack_mlp, "dp", scatter_dimension=1, tiled=True),
    )
    square_new = square_weights - jnp.array(SQ_RATES, F32)[:, None, None] * square_ortho
    mlp_new = mlp_weights - jnp.array(MLP_RATES, F32)[:, None, None] * mlp_ortho
    gains_new = gains - rate * gain_moment_new
    return (
        square_grad,
        square_moment_new,
        square_new,
        square_new.astype(BF16),
        mlp_grad,
        mlp_moment_new,
        mlp_new,
        mlp_new.astype(BF16),
        gain_grad,
        gain_moment_new,
        gains_new,
    )


def per_device(
    actions,
    observed,
    camera_flags,
    noise_levels,
    cotangent,
    square_weights,
    mlp_weights,
    gains,
    square_moment,
    mlp_moment,
    gain_moment,
):
    count = lax.axis_size("dp")
    rate = 0.1 / math.sqrt(actions.shape[0] * count)
    by_key = observed.transpose(1, 0, 2)
    ins = (actions, by_key, camera_flags, noise_levels, cotangent)
    if count == math.prod(GRID):
        made = block_and_back(True, *ins, square_weights, mlp_weights, gains, square_moment, mlp_moment)
        done = finish(rate, made, square_weights, mlp_weights, gains, gain_moment)
        output, actions_grad = done.output_f, done.ag_f
        d = done
        rest = (d.sqg, d.sqm, d.sqn, d.sqc, d.mlpg, d.mlpm, d.mlpn, d.mlpc, d.gg, d.gm, d.gn)
    else:
        square_all, mlp_all = (
            lax.all_gather(square_weights.astype(BF16), "dp", axis=1, tiled=True),
            lax.all_gather(mlp_weights.astype(BF16), "dp", axis=1, tiled=True),
        )
        gain_all = lax.all_gather(gains, "dp", axis=1, tiled=True)
        made = block_and_back(False, *ins, square_all, mlp_all, gain_all)
        done = finish(rate, made)
        output, actions_grad = made.output, made.ag
        grads = made.grads.reshape(-1, WIRE, LANES)
        rest = update_by_collectives(
            grads, square_weights, mlp_weights, gains, square_moment, mlp_moment, gain_moment, rate
        )
    observed_grad = done.og.transpose(1, 0, 2)
    return (output, actions_grad, observed_grad) + tuple(rest)


def solution(mesh):
    rows, cube, flat = P("dp", None), P("dp", None, None), P("dp")
    stacked, pair = P(None, "dp", None), P(None, "dp")
    return jax.shard_map(
        per_device,
        mesh=mesh,
        in_specs=(rows, cube, flat, flat, rows, stacked, stacked, pair, stacked, stacked, pair),
        out_specs=(rows, rows, cube) + (stacked,) * 8 + (pair,) * 3,
        check_vma=False,
    )
```

```python
import functools
import math

import jax
import jax.numpy as jnp
from jax import lax
from jax.experimental import pallas as pl
from jax.experimental.pallas import tpu as pltpu
from jax.sharding import PartitionSpec as P

HEADS = 4
ACT = 16
OBS_FULL = 196
OBS_FEW = 49
COEF_A = 3.4445
COEF_B = -4.775
COEF_C = 2.0315
F32 = jnp.float32
BF16 = jnp.bfloat16
MESH = pl.DeviceIdType.MESH
VMEM = pltpu.VMEM
NN = (((1,), (0,)), ((), ()))
NT = (((1,), (1,)), ((), ()))
TN = (((0,), (0,)), ((), ()))

LANES = 128
TILE = 8
MLP_ROWS = 64
SQ_ROWS = 16
SQ_AT = (160, 192, 176, 128, 144)
GAIN_BASE = 208
WIRE = 224
PIECES = ((0, 32), (32, 32), (64, 32), (96, 32), (128, 32), (160, 32), (192, 32))
PIECE_X_FIRST = (True, False, True, False, True, True, False)
CHUNKS = ((0, 32), (32, 32), (64, 32), (96, 32), (128, 32), (160, 32), (192, 16), (208, 16))
X_FIRST = (True, False, True, False, True, False, True, False)
PARTS_OUT = (
    (0, 0, 0, 32, 0),
    (1, 0, 32, 32, 32),
    (2, 1, 64, 32, 0),
    (3, 1, 96, 32, 32),
    (4, 5, 128, 16, 0),
    (4, 6, 144, 16, 0),
    (5, 2, 160, 16, 0),
    (5, 4, 176, 16, 0),
    (6, 3, 192, 16, 0),
)
MLP_RATES = (1.0, 0.5)
SQ_RATES = (0.5, 0.5, 0.5, 0.5, 4.0)
GRID = (4, 2, 2, 2)
OWNERS = (8, 22, 14, 16, 11, 21, 13)
SHIFTS = (0.0, 0.0, 0.4, 0.8, 0.8)
KEYS_PAD = 208
GROUP = 16
ROWS = 512


class Refs:
    def __init__(self, pairs):
        self.__dict__.update(pairs)


def dot(left, right, dims=NN):
    return lax.dot_general(left, right, dims, preferred_element_type=F32)


def place():
    me = lax.axis_index("dp")
    return me, me // 8, (me // 4) % 2, (me // 2) % 2, me % 2


def device_at(z, y, x, c):
    return ((z * 2 + y) * 2 + x) * 2 + c


def link(src, dst, send, recv, device):
    return pltpu.make_async_remote_copy(
        src_ref=src,
        dst_ref=dst,
        send_sem=send,
        recv_sem=recv,
        device_id=(device,),
        device_id_type=MESH,
    )


def greet(device):
    pl.semaphore_signal(
        pltpu.get_barrier_semaphore(), inc=1, device_id=(device,), device_id_type=MESH
    )


def normalize(values):
    centred = values - jnp.mean(values, -1, keepdims=True)
    scale = lax.rsqrt(jnp.mean(centred * centred, -1, keepdims=True) + 1e-05)
    return centred * scale, scale


def norm_back(grad, hat, scale):
    mean_one = jnp.mean(grad, -1, keepdims=True)
    mean_two = jnp.mean(grad * hat, -1, keepdims=True)
    return scale * (grad - mean_one - hat * mean_two)


class Gather:
    def __init__(self, r):
        self.r = r
        self.me, self.z, self.y, self.x, self.c = place()

    def hop(self, k, step, part, device):
        return link(part, part, self.r.gsend.at[k, step], self.r.grecv.at[k, step], device)

    def along_z(self, k, step):
        part = self.r.wire.at[self.z, self.y, self.x, self.c, pl.ds(*PIECES[k])]
        return self.hop(k, step, part, device_at((self.z + step + 1) % 4, self.y, self.x, self.c))

    def from_z(self, k, step):
        there = (self.z + 3 - step) % 4
        part = self.r.wire.at[there, self.y, self.x, self.c, pl.ds(*PIECES[k])]
        return self.hop(k, step, part, device_at(there, self.y, self.x, self.c))

    def plane(self, k, second, mine):
        z, y, x, c = self.z, self.y, self.x, self.c
        rows, wire = pl.ds(*PIECES[k]), self.r.wire
        py, px = (y, x) if mine else (1 - y, 1 - x)
        along_x = PIECE_X_FIRST[k] == second
        if along_x:
            part = wire.at[:, y, px, c, rows] if second else wire.at[:, :, px, c, rows]
            return self.hop(k, 3 if second else 4, part, device_at(z, y, 1 - x, c))
        part = wire.at[:, py, x, c, rows] if second else wire.at[:, py, :, c, rows]
        return self.hop(k, 3 if second else 4, part, device_at(z, 1 - y, x, c))

    def core(self, k, mine):
        part = self.r.wire.at[:, :, :, self.c if mine else 1 - self.c, pl.ds(*PIECES[k])]
        return self.hop(k, 5, part, device_at(self.z, self.y, self.x, 1 - self.c))

    def first(self, *chunks):
        for k in chunks:
            for step in range(3):
                self.along_z(k, step).start()

    def second(self, *chunks):
        for k in chunks:
            for step in range(3):
                self.from_z(k, step).wait_recv()
            self.plane(k, True, True).start()

    def third(self, *chunks):
        for k in chunks:
            self.plane(k, True, False).wait_recv()
            self.plane(k, False, True).start()

    def fourth(self, *chunks):
        for k in chunks:
            self.plane(k, False, False).wait_recv()
            self.core(k, True).start()

    def last(self, *chunks):
        for k in chunks:
            self.core(k, False).wait_recv()

    def drain(self):
        for k in range(len(PIECES)):
            for step in range(3):
                self.along_z(k, step).wait_send()
            self.plane(k, True, True).wait_send()
            self.plane(k, False, True).wait_send()
            self.core(k, True).wait_send()

    def fill(self):
        r = self.r
        spot = (self.z, self.y, self.x, self.c)

        def tiles(source, m, base, number):
            for j in range(number):
                pair = [source[m, :, pl.ds((2 * j + k) * LANES, LANES)] for k in range(2)]
                r.wire[spot + (pl.ds(base + j * 16, 16),)] = jnp.concatenate(pair, axis=0).astype(BF16)

        for m in range(5):
            tiles(r.sqw_v, m, SQ_AT[m], 1)
        for m in range(2):
            tiles(r.mlpw_v, m, m * MLP_ROWS, 4)
        gains, edge = r.gain_v[...], r.edge
        high = gains.astype(BF16).astype(F32)
        middle = (gains - high).astype(BF16).astype(F32)
        edge[...] = jnp.zeros_like(edge)
        edge[0:2, 0:TILE] = high
        edge[2:4, 0:TILE] = middle
        edge[4:6, 0:TILE] = (gains - high - middle).astype(BF16).astype(F32)
        r.wire[spot + (pl.ds(GAIN_BASE, 16),)] = edge[...].astype(BF16)

    def unpack(self, base, number, out, m):
        for j in range(number):
            block = self.r.wire[:, :, :, :, pl.ds(base + j * 16, 16), :].reshape(32, 16, LANES).astype(F32)
            for half in range(2):
                columns = pl.ds((2 * j + half) * LANES, LANES)
                out[m, :, columns] = block[:, half * 8 : half * 8 + 8, :].reshape(256, LANES).astype(BF16)

    def unpack_gains(self):
        edge, wire = self.r.edge, self.r.wire
        for half in range(2):
            total = jnp.zeros((16, LANES), F32)
            for at in range(16):
                d = half * 16 + at
                tile = wire[d // 8, (d // 4) % 2, (d // 2) % 2, d % 2, pl.ds(GAIN_BASE, 16), :].astype(F32)
                total = total + (tile if at == 0 else pltpu.roll(tile, at * TILE, 1))
            edge[...] = total
            self.r.gain_all[:, pl.ds(half * LANES, LANES)] = edge[0:2, :] + edge[2:4, :] + edge[4:6, :]


class Update:
    def __init__(self, r):
        self.r = r
        self.me, self.z, self.y, self.x, self.c = place()

    def hop(self, k, step, src, dst, device):
        return link(src, dst, self.r.send.at[k, step], self.r.recv.at[k, step], device)

    def core(self, k):
        rows = pl.ds(*CHUNKS[k])
        src, dst = self.r.send0.at[:, :, :, rows], self.r.got_core.at[:, :, :, rows]
        return self.hop(k, 0, src, dst, device_at(self.z, self.y, self.x, 1 - self.c))

    def plane(self, k, first):
        rows = pl.ds(*CHUNKS[k])
        to = (self.z, self.y, 1 - self.x, self.c) if X_FIRST[k] == first else (self.z, 1 - self.y, self.x, self.c)
        if first:
            src, dst = self.r.send1.at[:, :, rows], self.r.got1.at[:, :, rows]
        else:
            src, dst = self.r.send2.at[:, rows], self.r.got2.at[:, rows]
        return self.hop(k, 1 if first else 2, src, dst, device_at(*to))

    def along_z(self, k, step):
        rows = pl.ds(*CHUNKS[k])
        there = (self.z + step + 1) % 4
        src, dst = self.r.send3.at[there, rows], self.r.got3.at[step, rows]
        return self.hop(k, 3 + step, src, dst, device_at(there, self.y, self.x, self.c))

    def start(self, k):
        rows = pl.ds(*CHUNKS[k])
        self.r.send0[:, :, :, rows, :] = self.r.grads[:, :, :, 1 - self.c, rows, :].astype(BF16)
        self.core(k).start()

    def one(self, *chunks):
        r = self.r
        for k in chunks:
            rows = pl.ds(*CHUNKS[k])
            self.core(k).wait_recv()
            sum1 = r.sum1
            sum1[:, :, :, rows, :] = r.grads[:, :, :, self.c, rows, :] + r.got_core[:, :, :, rows, :].astype(F32)
            other = sum1[:, :, 1 - self.x, rows, :] if X_FIRST[k] else sum1[:, 1 - self.y, :, rows, :]
            r.send1[:, :, rows, :] = other.astype(BF16)
            self.plane(k, True).start()

    def two(self, *chunks):
        r = self.r
        for k in chunks:
            rows = pl.ds(*CHUNKS[k])
            self.plane(k, True).wait_recv()
            sum1, sum2 = r.sum1, r.sum2
            mine = sum1[:, :, self.x, rows, :] if X_FIRST[k] else sum1[:, self.y, :, rows, :]
            sum2[:, :, rows, :] = mine + r.got1[:, :, rows, :].astype(F32)
            other = 1 - self.y if X_FIRST[k] else 1 - self.x
            r.send2[:, rows, :] = sum2[:, other, rows, :].astype(BF16)
            self.plane(k, False).start()

    def three(self, *chunks):
        r = self.r
        for k in chunks:
            rows = pl.ds(*CHUNKS[k])
            self.plane(k, False).wait_recv()
            mine = self.y if X_FIRST[k] else self.x
            total = r.sum2[:, mine, rows, :] + r.got2[:, rows, :].astype(F32)
            r.sum3[:, rows, :] = total
            r.send3[:, rows, :] = total.astype(BF16)
            if k >= 4:
                own = r.sum3[self.z, rows, :] + 0.5 * r.moment[rows, :]
                r.send3[self.z, rows, :] = own.astype(BF16)
                self.parts_to_owners(k)
            for step in range(3):
                self.along_z(k, step).start()

    def parts_to_owners(self, k):
        for part, (chunk, index, *_) in enumerate(PARTS_OUT):
            if chunk != k:
                continue

            @pl.when(self.me != OWNERS[index])
            def _():
                self.to_owner(part).start()

            @pl.when(self.me == OWNERS[index])
            def _():
                src, dst = self.own_part(part)
                pltpu.make_async_copy(src, dst, self.r.own_recv.at[0]).start()

    def result(self, index):
        return self.r.result_mlp if index < 2 else self.r.result_sq

    def own_part(self, part):
        _, index, base, number, place = PARTS_OUT[part]
        if index < 2:
            return self.r.moment_low.at[pl.ds(base, number)], self.r.slabs_mlp.at[self.me, pl.ds(place, number)]
        return self.r.send3.at[:, pl.ds(base, number)], self.r.slabs_sq.at[self.z, self.me % 8]

    def to_owner(self, part):
        src, dst = self.own_part(part)
        return link(src, dst, self.r.own_send.at[part], self.r.own_recv.at[0], OWNERS[PARTS_OUT[part][1]])

    def four(self, *chunks):
        r = self.r
        moment, out = r.moment, r.out
        for k in chunks:
            rows = pl.ds(*CHUNKS[k])
            total = r.sum3[self.z, rows, :]
            for step in range(3):
                self.along_z(k, step).wait_recv()
                total = total + r.got3[step, rows, :].astype(F32)
            out[0, rows, :] = total
            new = 0.5 * moment[rows, :] + total
            moment[rows, :] = new
            if k < 4:
                r.moment_low[rows, :] = new.astype(BF16)
            if k < 4:
                self.parts_to_owners(k)

    def old_moment(self):
        r = self.r
        moment = r.moment
        for m in range(2):
            for j in range(8):
                moment[pl.ds(m * MLP_ROWS + j * TILE, TILE), :] = r.mlpm_v[m, :, pl.ds(j * LANES, LANES)]
        for m in range(5):
            for j in range(2):
                moment[pl.ds(SQ_AT[m] + j * TILE, TILE), :] = r.sqm_v[m, :, pl.ds(j * LANES, LANES)]
        moment[pl.ds(GAIN_BASE, 16), :] = jnp.zeros((16, LANES), F32)

    def orthogonalize(self):
        r = self.r
        cur = r.cur
        rows = lax.broadcasted_iota(jnp.int32, (256, 256), 0)
        diagonal = rows == lax.broadcasted_iota(jnp.int32, (256, 256), 1)

        low = r.cur_low

        def load(rows, j, pair):
            for side in range(2):
                columns = pl.ds((2 * j + side) * LANES, LANES)
                part = pair[:, side * TILE : (side + 1) * TILE, :].reshape(-1, LANES)
                cur[rows, columns] = part
                low[rows, columns] = part.astype(BF16)

        def load_mlp():
            for j in range(4):
                load(pl.ds(0, 256), j, r.slabs_mlp[:, pl.ds(j * 16, 16), :].astype(F32))

        def load_sq():
            for to in range(4):
                pair = r.slabs_sq[0, :, to].astype(F32)
                for plane in range(1, 4):
                    pair = pair + r.slabs_sq[plane, :, to].astype(F32)
                load(pl.ds(to * 64, 64), 0, pair)

        def run(slabs, fetch, result, tiles):
            pltpu.make_async_copy(slabs, slabs, r.own_recv.at[0]).wait()
            fetch()
            scale = 1.0
            for turn, shift in enumerate(SHIFTS):
                whole = low[:, 0 : tiles * LANES]
                off = dot(whole, whole, NT)
                if turn == 0:
                    norm = jnp.sum(jnp.sum(jnp.where(diagonal, off, 0.0), axis=0, keepdims=True), axis=1, keepdims=True)
                    scale = 1.0 / (jnp.sqrt(norm) + 1e-07)
                    off = off * (scale * scale)
                if shift:
                    off = off - jnp.where(diagonal, shift, 0.0)
                off_low = off.astype(BF16)
                poly = (COEF_B + 2.0 * COEF_C * shift) * off + COEF_C * dot(off_low, off_low)
                poly = poly.astype(BF16)
                keep = COEF_A + shift * (COEF_B + COEF_C * shift)
                for j in range(tiles // 2):
                    columns = pl.ds(j * 2 * LANES, 2 * LANES)
                    now = keep * cur[:, columns] + dot(poly, low[:, columns])
                    if turn == 0:
                        now = now * scale
                    if turn < len(SHIFTS) - 1:
                        cur[:, columns] = now
                        low[:, columns] = now.astype(BF16)
                    else:
                        parts = [now[:, side * LANES : (side + 1) * LANES].reshape(32, TILE, LANES) for side in range(2)]
                        result[:, pl.ds(j * 16, 16), :] = jnp.concatenate(parts, axis=1).astype(result.dtype)

        mine_mlp = jnp.logical_or(self.me == OWNERS[0], self.me == OWNERS[1])
        mine_sq = self.me < 0
        for device in OWNERS[2:]:
            mine_sq = jnp.logical_or(mine_sq, self.me == device)

        @pl.when(mine_mlp)
        def _():
            run(r.slabs_mlp, load_mlp, r.result_mlp, 8)

        @pl.when(mine_sq)
        def _():
            run(r.slabs_sq, load_sq, r.result_sq, 2)

    def landing(self, index):
        if index < 2:
            return self.r.back_mlp.at[index]
        return self.r.out.at[2, pl.ds(SQ_AT[index - 2], SQ_ROWS)]

    def give_back(self, index, device):
        result = self.result(index)
        return link(
            result.at[device], self.landing(index),
            self.r.back_send.at[device], self.r.back_recv.at[index], device,
        )

    def give_all(self):
        r = self.r
        for index in range(7):
            result = self.result(index)

            @pl.when(self.me == OWNERS[index])
            def _():
                def send_one(step, _):
                    self.give_back(index, (self.me + step) % 32).start()
                    return 0

                lax.fori_loop(1, 32, send_one, 0)
                pltpu.make_async_copy(result.at[self.me], self.landing(index), r.back_recv.at[index]).start()

    def take_all(self):
        for index in range(7):
            result = self.result(index)
            pltpu.make_async_copy(result.at[0], self.landing(index), self.r.back_recv.at[index]).wait()
        for index in range(2):
            rows = pl.ds(index * MLP_ROWS, MLP_ROWS)
            self.r.out[2, rows, :] = self.r.back_mlp[index].astype(F32)

    def drain(self):
        for k in range(len(CHUNKS)):
            self.core(k).wait_send()
            self.plane(k, True).wait_send()
            self.plane(k, False).wait_send()
            for step in range(3):
                self.along_z(k, step).wait_send()
        for part in range(len(PARTS_OUT)):

            @pl.when(self.me != OWNERS[PARTS_OUT[part][1]])
            def _():
                self.to_owner(part).wait_send()

    def drain_owner(self):
        for index in range(7):

            @pl.when(self.me == OWNERS[index])
            def _():
                def wait_one(step, _):
                    self.give_back(index, (self.me + step) % 32).wait_send()
                    return 0

                lax.fori_loop(1, 32, wait_one, 0)


def greet_all():
    me, z, y, x, c = place()
    greet(device_at(z, y, x, 1 - c))
    greet(device_at(z, y, 1 - x, c))
    greet(device_at(z, 1 - y, x, c))
    for step in range(1, 4):
        greet(device_at((z + step) % 4, y, x, c))
    owner = me < 0
    for device in OWNERS:
        owner = jnp.logical_or(owner, me == device)

        @pl.when(me != device)
        def _():
            greet(device)

    @pl.when(owner)
    def _():
        def greet_other(step, _):
            greet((me + step) % 32)
            return 0

        lax.fori_loop(1, 32, greet_other, 0)

    is_owner = owner.astype(jnp.int32)
    return 6 + 7 - is_owner + 31 * is_owner


def block_kernel(names, remote, *args):
    r = Refs(zip(names, args))
    keys, samples = r.obs.shape[0], r.obs.shape[1]
    tokens, width = r.acts.shape
    head_dim, half, per = width // HEADS, width // 2, ROWS // ACT
    wide = r.mlp_all.shape[2]
    groups = samples // GROUP
    in_sems, out_sems = r.in_sems, r.out_sems

    if remote:
        own = (r.sqw_v, r.mlpw_v, r.gain_v)
    else:
        own = (r.sq_all, r.mlp_all, r.gain_all)
    loads = list(zip((r.sqw, r.mlpw, r.gain), own))
    loads += [(r.acts, r.acts_v), (r.obs, r.obs_v.at[pl.ds(0, keys)]), (r.cot, r.cot_v)]
    if remote:
        loads += [(r.sqm, r.sqm_v), (r.mlpm, r.mlpm_v)]
    loads += [(r.flags, r.flags_s), (r.levels, r.levels_s)]
    copies = [pltpu.make_async_copy(a, b, in_sems.at[i]) for i, (a, b) in enumerate(loads)]

    def arrive(*which):
        for i in which:
            copies[i].wait()

    for copy in copies:
        copy.start()
    if remote:
        gather, update = Gather(r), Update(r)
        expected = greet_all()
        arrive(0, 1, 2)
        gather.fill()
        pl.semaphore_wait(pltpu.get_barrier_semaphore(), expected)
        gather.first(5, 6, 4, 0, 1, 2, 3)

    arrive(3)

    def hats(i, _):
        rows = pl.ds(pl.multiple_of(i * ROWS, ROWS), ROWS)
        hat, scale = normalize(r.acts_v[rows, :])
        r.xhat[rows, :] = hat
        r.rstd[rows, :] = scale
        return 0

    lax.fori_loop(0, tokens // ROWS, hats, 0)

    mem, obs_v = r.mem, r.obs_v
    batch = 16
    chunks = KEYS_PAD // batch
    swap = r.swap
    row = lax.broadcasted_iota(jnp.int32, swap.shape, 0)
    column = lax.broadcasted_iota(jnp.int32, swap.shape, 1)
    swap[...] = jnp.where(column == (row % batch) * batch + row // batch, 1.0, 0.0).astype(BF16)

    def turn(part, low, high):
        def one(j, _):
            at = pl.ds(pl.multiple_of(j * batch, batch), batch)
            here = pl.ds(part * batch, batch)
            block = obs_v[at, here, :].reshape(batch * batch, width)
            mem[here, at, :] = dot(swap[...], block).astype(BF16).reshape(batch, batch, width)
            return 0

        lax.fori_loop(low, high, one, 0, unroll=high - low)

    whole = chunks - 1
    arrive(4)
    turn(0, 0, whole // 2)
    if remote:
        gather.second(5, 6)
    turn(0, whole // 2, whole)
    if remote:
        gather.third(5, 6)
    turn(1, 0, whole // 2)
    if remote:
        gather.second(4, 0, 1)
        gather.fourth(5, 6)
    turn(1, whole // 2, whole)
    if remote:
        gather.second(2, 3)
    arrive(len(copies) - 1, len(copies) - 2)
    freqs = jnp.exp(
        lax.broadcasted_iota(jnp.int32, (1, half), 1).astype(F32) * F32(-math.log(10000.0)) / half
    )
    for s in range(samples):
        r.angle[s : s + 1, :] = r.levels_s[s].astype(F32) * freqs
    r.embed[:, 0:half] = jnp.sin(r.angle[...]).astype(BF16)
    r.embed[:, half:width] = jnp.cos(r.angle[...]).astype(BF16)
    if remote:
        arrive(6, 7)
        update.old_moment()
        gather.third(4, 0, 1)
        gather.last(5, 6)
        for m in range(3):
            gather.unpack(SQ_AT[m], 1, r.sq_all, m)
        gather.unpack_gains()
    else:
        arrive(0, 1, 2)

    sq, mlp = r.sq_all, r.mlp_all
    wkh, wvh = r.wkh, r.wvh
    lane = lax.broadcasted_iota(jnp.int32, (width, width), 1)

    def split_heads(out, weight):
        weight = weight.astype(F32)
        for h in range(HEADS):
            out[pl.ds(h * width, width), :] = jnp.where(lane // head_dim == h, weight, 0.0).astype(BF16)

    split_heads(wkh, sq[2])
    g1, g2 = r.gain_all[0:1, :], r.gain_all[1:2, :]

    obs_v[keys] = dot(r.embed[...], sq[0]).astype(BF16)
    obs_v[keys + 1 :] = jnp.zeros((KEYS_PAD - keys - 1, samples, width), BF16)
    for part in range(samples // batch):
        turn(part, whole, chunks)

    queries, dmixes = r.queries, r.dmixes

    def make_queries(i, _):
        rows = pl.ds(pl.multiple_of(i * ROWS, ROWS), ROWS)
        first = (r.xhat[rows, :] * g1).astype(BF16)
        r.first[rows, :] = first
        q = dot(first, sq[1]).astype(BF16)
        r.query[rows, :] = q
        here = pl.ds(i * per, per)
        for h in range(HEADS):
            wk = wkh[pl.ds(h * width, width), :]
            value = (dot(q, wk, NT) * 0.125).astype(BF16).reshape(per, ACT, width)
            queries[here, pl.ds(h * ACT, ACT), :] = value
        return 0

    lax.fori_loop(0, tokens // ROWS, make_queries, 0)

    key = lax.broadcasted_iota(jnp.int32, (KEYS_PAD, LANES), 0)
    rows_each = HEADS * ACT
    left = lax.broadcasted_iota(jnp.int32, (KEYS_PAD, LANES), 1) < rows_each
    left_row = lax.broadcasted_iota(jnp.int32, (1, LANES), 1) < rows_each
    rest = jnp.where((key >= OBS_FEW) & (key < OBS_FULL), 1.0, 0.0)
    padding = jnp.where(key > OBS_FULL, -1000000000.0, 0.0)

    def with_memory(s, sides):
        here = pl.ds(s, 4)
        wide = dot(mem[here].reshape(4 * KEYS_PAD, width), sides[here].reshape(4 * rows_each, width), NT)
        part = [wide[k * KEYS_PAD : (k + 1) * KEYS_PAD, (k // 2) * LANES : (k // 2 + 1) * LANES] for k in range(4)]
        return jnp.where(left, part[0], part[1]), jnp.where(left, part[2], part[3])

    def each_head(out, s, value):
        rows = pl.ds(pl.multiple_of(s * ACT, ACT), ACT)
        for h in range(HEADS):
            out[rows, pl.ds(h * width, width)] = value[h * ACT : (h + 1) * ACT, :]

    def attend(g, _):
        pairs = []
        for quad in range(GROUP // 4):
            pairs.extend(with_memory(g * GROUP + 4 * quad, queries))
        turned = []
        for k, score in enumerate(pairs):
            s = g * GROUP + 2 * k
            drop = [(1 - r.flags_s[s + side]).astype(F32) * -1000000000.0 for side in range(2)]
            score = score + (rest * jnp.where(left_row, drop[0], drop[1]) + padding)
            expo = jnp.exp(score - jnp.max(score, 0, keepdims=True))
            probs = expo * (1.0 / jnp.sum(expo, 0, keepdims=True))
            r.probs[g * (GROUP // 2) + k] = probs
            turned.append(probs.astype(BF16).T)
        for k, low in enumerate(turned):
            for side in range(2):
                s = g * GROUP + 2 * k + side
                each_head(r.u, s, dot(low[side * rows_each : (side + 1) * rows_each], mem[s]).astype(BF16))
        return 0

    lax.fori_loop(0, groups // 2, attend, 0)
    if remote:
        gather.third(2, 3)
        gather.fourth(4, 0, 1)
    lax.fori_loop(groups // 2, groups, attend, 0)
    if remote:
        gather.fourth(2, 3)
        gather.last(4)
        for m in range(3, 5):
            gather.unpack(SQ_AT[m], 1, sq, m)
    split_heads(wvh, sq[3])

    gain_acc = r.gain_acc
    gain_acc[...] = jnp.zeros_like(gain_acc)
    blocks = [pl.ds(i * ROWS, ROWS) for i in range(tokens // ROWS)]
    for rows in blocks:
        mixed = dot(r.u[rows, :], wvh[...]).astype(BF16)
        r.mixed[rows, :] = mixed
        resid = r.acts_v[rows, :] + dot(mixed, sq[4])
        r.resid[rows, :] = resid
        hat, scale = normalize(resid)
        r.hat_two[rows, :] = hat
        r.rstd_two[rows, :] = scale
        r.second[rows, :] = (hat * g2).astype(BF16)
    arrive(5)
    r.out_low[...] = r.cot_v[...].astype(BF16)
    if remote:
        gather.last(0, 1)
        gather.unpack(0, 4, mlp, 0)
    wide_blocks = [pl.ds(c * 256, 256) for c in range(wide // 256)]
    for rows in blocks:
        for columns in wide_blocks:
            v = dot(r.second[rows, :], mlp[0, :, columns])
            square = v * v
            t = jnp.tanh(0.7978845608 * (v + 0.044715 * square * v))
            r.active[rows, columns] = (0.5 * v * (1.0 + t)).astype(BF16)
            slope = 0.5 * (1.0 + t) + 0.5 * v * (1.0 - t * t) * (0.7978845608 * (1.0 + 0.134145 * square))
            r.slope[rows, columns] = slope

    grads = r.grads

    def put(base, tiles, value):
        for j in range(tiles):
            part = value[:, j * LANES : (j + 1) * LANES].reshape(GRID + (TILE, LANES))
            grads[:, :, :, :, pl.ds(base + j * TILE, TILE), :] = part

    def by_head(left, right):
        turned = left.T
        parts = [
            dot(turned[h * head_dim : (h + 1) * head_dim, :], right[:, pl.ds(h * width, width)])
            for h in range(HEADS)
        ]
        return jnp.concatenate(parts, axis=0).T

    put(MLP_ROWS, 8, dot(r.out_low[...], r.active[...], TN))
    if remote:
        update.start(2)
        update.start(3)
        gather.last(2, 3)
        gather.unpack(MLP_ROWS, 4, mlp, 1)
    for rows in blocks:
        for columns in wide_blocks:
            slope = r.slope[rows, columns]
            r.dhidden[rows, columns] = (slope * dot(r.out_low[rows, :], mlp[1, :, columns])).astype(BF16)
    put(0, 8, dot(r.second[...], r.dhidden[...], TN))
    if remote:
        update.start(0)
        update.start(1)
        update.one(2, 3)
    for i, rows in enumerate(blocks):
        r.out_v[rows, :] = r.resid[rows, :] + dot(r.active[rows, :], mlp[1], NT)
        grad_second = dot(r.dhidden[rows, :], mlp[0], NT)
        hat = r.hat_two[rows, :]
        gain_acc[1:2, :] += jnp.sum(grad_second * hat, 0, keepdims=True)
        dres = r.cot_v[rows, :] + norm_back(grad_second * g2, hat, r.rstd_two[rows, :])
        r.dres[rows, :] = dres
        low = dres.astype(BF16)
        r.dres_low[rows, :] = low
        gm = dot(low, sq[4], NT).astype(BF16)
        r.dmixed[rows, :] = gm
        here = pl.ds(i * per, per)
        for h in range(HEADS):
            wv = wvh[pl.ds(h * width, width), :]
            dmixes[here, pl.ds(h * ACT, ACT), :] = dot(gm, wv, NT).astype(BF16).reshape(per, ACT, width)
    keep_out = pltpu.make_async_copy(r.out_v, r.output, out_sems.at[0])
    keep_out.start()
    if remote:
        update.one(0, 1)
    put(SQ_AT[4], 2, dot(r.mixed[...], r.dres_low[...], TN))
    put(SQ_AT[3], 2, by_head(r.dmixed[...], r.u))
    if remote:
        update.start(4)

    left_low = jnp.where(left_row, 1.0, 0.0).astype(BF16)
    right_low = jnp.where(left_row, 0.0, 1.0).astype(BF16)

    def attend_back(g, _):
        pairs = []
        for quad in range(GROUP // 4):
            pairs.extend(with_memory(g * GROUP + 4 * quad, dmixes))
        lows = []
        for k, rise in enumerate(pairs):
            probs = r.probs[g * (GROUP // 2) + k]
            both = probs * rise
            dscore = (both - probs * jnp.sum(both, 0, keepdims=True)).astype(BF16)
            lows.append((probs.astype(BF16), dscore, dscore.T))
        for k, (low, dscore, turned) in enumerate(lows):
            s = g * GROUP + 2 * k
            for side in range(2):
                dq = dot(turned[side * rows_each : (side + 1) * rows_each], mem[s + side]) * 0.125
                each_head(r.dq_wide, s + side, dq.astype(BF16))
            here = pl.ds(s, 2)
            sides = jnp.concatenate(
                [x[here].reshape(2 * rows_each, width) for x in (dmixes, queries)], axis=0
            )
            own = [jnp.concatenate([low * keep, dscore * keep], axis=1) for keep in (left_low, right_low)]
            dmem = dot(jnp.concatenate(own, axis=0), sides)
            for side in range(2):
                rows = dmem[side * KEYS_PAD : (side + 1) * KEYS_PAD, :]
                mem[s + side] = rows.astype(BF16)
                r.stamps[s + side] = rows[192:200, :]
        return 0

    lax.fori_loop(0, groups // 2, attend_back, 0)
    if remote:
        update.two(2, 3)
        update.one(4)
        update.two(0, 1)
    lax.fori_loop(groups // 2, groups, attend_back, 0)
    if remote:
        update.three(2, 3)
        update.two(4)
    put(SQ_AT[2], 2, by_head(r.query[...], r.dq_wide))
    stamp_low = r.stamps[:, 4:5, :].reshape(samples, width).astype(BF16)
    put(SQ_AT[0], 2, dot(r.embed[...], stamp_low, TN))
    if remote:
        update.start(5)
        update.three(0, 1)

    def keep_og(part):
        here = pl.ds(part * batch, batch)
        return pltpu.make_async_copy(obs_v.at[pl.ds(0, keys), here], r.og.at[:, here], out_sems.at[2 + part])

    def turn_back(part):
        def one(j):
            at = pl.ds(pl.multiple_of(j * batch, batch), batch)
            here = pl.ds(part * batch, batch)
            block = mem[here, at, :].reshape(batch * batch, width)
            value = dot(swap[...], block).astype(BF16).reshape(batch, batch, width)
            obs_v[at, here, :] = value

        for j in range(chunks):
            one(j)
        keep_og(part).start()

    def queries_back(i, _):
        rows = pl.ds(pl.multiple_of(i * ROWS, ROWS), ROWS)
        r.dquery[rows, :] = dot(r.dq_wide[rows, :], wkh[...]).astype(BF16)
        return 0

    lax.fori_loop(0, tokens // ROWS, queries_back, 0)
    put(SQ_AT[1], 2, dot(r.first[...], r.dquery[...], TN))
    if remote:
        update.start(6)
        update.one(5)

    def acts_back(i, _):
        rows = pl.ds(pl.multiple_of(i * ROWS, ROWS), ROWS)
        grad_first = dot(r.dquery[rows, :], sq[1], NT)
        hat = r.xhat[rows, :]
        gain_acc[0:1, :] += jnp.sum(grad_first * hat, 0, keepdims=True)
        r.ag_v[rows, :] = r.dres[rows, :] + norm_back(grad_first * g1, hat, r.rstd[rows, :])
        return 0

    def finish_acts():
        lax.fori_loop(0, tokens // ROWS, acts_back, 0)
        for norm in range(2):
            for j in range(2):
                row = gain_acc[norm : norm + 1, j * LANES : (j + 1) * LANES]
                at = GAIN_BASE + norm * 2 + j
                value = jnp.broadcast_to(row.reshape(1, 1, 1, 1, 1, LANES), GRID + (1, LANES))
                grads[:, :, :, :, at : at + 1, :] = value
        rest = WIRE - GAIN_BASE - 4
        grads[:, :, :, :, GAIN_BASE + 4 : WIRE, :] = jnp.zeros(GRID + (rest, LANES), F32)

    keep_ag = pltpu.make_async_copy(r.ag_v, r.ag, out_sems.at[1])
    if remote:
        finish_acts()
        keep_ag.start()
        update.start(7)
        update.one(6)
        update.three(4)
        update.four(2, 3)
        update.two(5)
        update.one(7)
        update.two(6)
        update.four(0, 1)
        update.three(5)
        update.two(7)
        update.three(6)
        update.orthogonalize()
        update.give_all()
        update.three(7)
        turn_back(0)
        update.four(4, 5, 6)
        turn_back(1)
        update.four(7)
        out = r.out
        out[1, :, :] = r.moment[...]
        out[2, pl.ds(GAIN_BASE, 16), :] = jnp.zeros((16, LANES), F32)
        gather.drain()
        update.drain()
        update.take_all()
        update.drain_owner()
    else:
        finish_acts()
        keep_ag.start()
        for part in range(samples // batch):
            turn_back(part)
    for copy in (keep_out, keep_ag, *(keep_og(part) for part in range(samples // batch))):
        copy.wait()


def block_and_back(remote, acts, obs, flags, levels, cot, sqw, mlpw, gain, sqm=None, mlpm=None):
    tokens, width = acts.shape
    keys, samples = obs.shape[0], obs.shape[1]
    rows = HEADS * ACT
    wide = mlpw.shape[2]
    any_space = pl.BlockSpec(memory_space=pl.ANY)
    in_vmem = pl.BlockSpec(memory_space=VMEM)
    sem = pltpu.SemaphoreType.DMA
    ins = dict(flags=flags, levels=levels, acts=acts, obs=obs, cot=cot, sqw=sqw, mlpw=mlpw, gain=gain)
    outs = dict(
        output=jax.ShapeDtypeStruct(acts.shape, F32),
        ag=jax.ShapeDtypeStruct(acts.shape, F32),
        og=jax.ShapeDtypeStruct(obs.shape, BF16),
    )
    grads = GRID + (WIRE, LANES)
    scratch = dict(
        obs_v=VMEM((KEYS_PAD, samples, width), BF16),
        acts_v=VMEM(acts.shape, F32),
        cot_v=VMEM(acts.shape, F32),
        mem=VMEM((samples, KEYS_PAD, width), BF16),
        swap=VMEM((256, 256), BF16),
        sq_all=VMEM((5, width, width), BF16),
        mlp_all=VMEM((2, width, wide), BF16),
        gain_all=VMEM((2, width), F32),
        wkh=VMEM((HEADS * width, width), BF16),
        wvh=VMEM((HEADS * width, width), BF16),
        first=VMEM((tokens, width), BF16),
        query=VMEM((tokens, width), BF16),
        xhat=VMEM((tokens, width), F32),
        rstd=VMEM((tokens, 1), F32),
        probs=VMEM((samples // 2, KEYS_PAD, LANES), F32),
        queries=VMEM((samples, rows, width), BF16),
        dmixes=VMEM((samples, rows, width), BF16),
        u=VMEM((tokens, HEADS * width), BF16),
        dq_wide=VMEM((tokens, HEADS * width), BF16),
        mixed=VMEM((tokens, width), BF16),
        second=VMEM((tokens, width), BF16),
        active=VMEM((tokens, wide), BF16),
        dhidden=VMEM((tokens, wide), BF16),
        out_low=VMEM((tokens, width), BF16),
        dres_low=VMEM((tokens, width), BF16),
        dres=VMEM((tokens, width), F32),
        resid=VMEM((tokens, width), F32),
        hat_two=VMEM((tokens, width), F32),
        rstd_two=VMEM((tokens, 1), F32),
        slope=VMEM((tokens, wide), F32),
        dmixed=VMEM((tokens, width), BF16),
        dquery=VMEM((tokens, width), BF16),
        out_v=VMEM((tokens, width), F32),
        ag_v=VMEM((tokens, width), F32),
        angle=VMEM((samples, width // 2), F32),
        embed=VMEM((samples, width), BF16),
        stamps=VMEM((samples, 8, width), F32),
        gain_acc=VMEM((8, width), F32),
        flags_s=pltpu.SMEM(flags.shape, jnp.int32),
        levels_s=pltpu.SMEM(levels.shape, jnp.int32),
        in_sems=sem((10,)),
        out_sems=sem((2 + samples // 16,)),
    )
    extra = {}
    if remote:
        ins.update(sqm=sqm, mlpm=mlpm)
        outs.update(out=jax.ShapeDtypeStruct((3, WIRE, LANES), F32))
        chunks = len(CHUNKS)
        scratch.update(
            grads=VMEM(grads, F32),
            sqw_v=VMEM(sqw.shape, F32),
            mlpw_v=VMEM(mlpw.shape, F32),
            gain_v=VMEM(gain.shape, F32),
            sqm_v=VMEM(sqm.shape, F32),
            mlpm_v=VMEM(mlpm.shape, F32),
            wire=VMEM(grads, BF16),
            edge=VMEM((16, LANES), F32),
            gsend=sem((len(PIECES), 6)),
            grecv=sem((len(PIECES), 6)),
            send0=VMEM((4, 2, 2, WIRE, LANES), BF16),
            got_core=VMEM((4, 2, 2, WIRE, LANES), BF16),
            sum1=VMEM((4, 2, 2, WIRE, LANES), F32),
            send1=VMEM((4, 2, WIRE, LANES), BF16),
            got1=VMEM((4, 2, WIRE, LANES), BF16),
            sum2=VMEM((4, 2, WIRE, LANES), F32),
            send2=VMEM((4, WIRE, LANES), BF16),
            got2=VMEM((4, WIRE, LANES), BF16),
            sum3=VMEM((4, WIRE, LANES), F32),
            send3=VMEM((4, WIRE, LANES), BF16),
            got3=VMEM((3, WIRE, LANES), BF16),
            moment=VMEM((WIRE, LANES), F32),
            slabs_sq=VMEM((4, 8, 4, SQ_ROWS, LANES), BF16),
            slabs_mlp=VMEM((32, MLP_ROWS, LANES), BF16),
            moment_low=VMEM((2 * MLP_ROWS, LANES), BF16),
            back_mlp=VMEM((2, MLP_ROWS, LANES), BF16),
            result_sq=VMEM((32, SQ_ROWS, LANES), F32),
            result_mlp=VMEM((32, MLP_ROWS, LANES), BF16),
            cur=VMEM((width, wide), F32),
            cur_low=VMEM((width, wide), BF16),
            send=sem((chunks, 6)),
            recv=sem((chunks, 6)),
            own_send=sem((len(PARTS_OUT),)),
            own_recv=sem((1,)),
            back_send=sem((32,)),
            back_recv=sem((7,)),
        )
        extra = dict(collective_id=0, has_side_effects=True)
        outs = {name: VMEM(like.shape, like.dtype) for name, like in outs.items()}
    else:
        outs.update(grads=jax.ShapeDtypeStruct(grads, F32))
    names = tuple(ins) + tuple(outs) + tuple(scratch)
    stay = [pltpu.with_memory_space_constraint(value, pltpu.HBM) for value in ins.values()]
    results = pl.pallas_call(
        functools.partial(block_kernel, names, remote),
        out_shape=tuple(outs.values()),
        in_specs=[any_space] * len(ins),
        out_specs=[any_space] * 3 + [in_vmem],
        scratch_shapes=list(scratch.values()),
        compiler_params=pltpu.CompilerParams(vmem_limit_bytes=50 << 20, **extra),
        name="block_and_back",
    )(*stay)
    return Refs(zip(outs, results))


PARTS = 7


def finish_kernel(names, rate, *args):
    r = Refs(zip(names, args))
    sems = r.sems
    keys = r.og.shape[0]
    step = keys // PARTS

    def leave(part):
        block = pl.ds(part * step, step)
        return pltpu.make_async_copy(r.og_v.at[block], r.og.at[block], sems.at[part])

    more = PARTS
    moves = []
    if hasattr(r, "wire"):
        pairs = [(r.sqw, r.sqw_v), (r.mlpw, r.mlpw_v), (r.gain, r.gain_v), (r.gainm, r.gainm_v)]
        pairs += [(r.output, r.output_f), (r.ag, r.ag_f)]
        for source, target in pairs:
            moves.append(pltpu.make_async_copy(source, target, sems.at[more]))
            moves[-1].start()
            more += 1
    for part in range(PARTS):

        def widen(j, _):
            r.og_v[j] = r.low[j].astype(F32)
            return 0

        lax.fori_loop(part * step, (part + 1) * step, widen, 0, unroll=4)
        leave(part).start()
    for copy in moves[:4]:
        copy.wait()
    if hasattr(r, "wire"):
        finish_weights(r, rate)
    for part in range(PARTS):
        leave(part).wait()
    for copy in moves[4:]:
        copy.wait()


def finish_weights(r, rate):
    wire = r.wire
    me = lax.axis_index("dp")
    for m in range(5):
        for j in range(2):
            rows, columns = pl.ds(SQ_AT[m] + j * TILE, TILE), pl.ds(j * LANES, LANES)
            r.sqg[m, :, columns] = wire[0, rows, :]
            r.sqm[m, :, columns] = wire[1, rows, :]
            r.sqn[m, :, columns] = r.sqw_v[m, :, columns] - SQ_RATES[m] * wire[2, rows, :]
    r.sqc[...] = r.sqn[...].astype(BF16)
    for m in range(2):
        for j in range(8):
            rows, columns = pl.ds(m * MLP_ROWS + j * TILE, TILE), pl.ds(j * LANES, LANES)
            r.mlpg[m, :, columns] = wire[0, rows, :]
            r.mlpm[m, :, columns] = wire[1, rows, :]
            r.mlpn[m, :, columns] = r.mlpw_v[m, :, columns] - MLP_RATES[m] * wire[2, rows, :]
    r.mlpc[...] = r.mlpn[...].astype(BF16)
    tile = wire[0, pl.ds(GAIN_BASE, TILE), :]
    turned = pltpu.roll(tile, (LANES - (me % 16) * TILE) % LANES, 1)
    at = me // 16
    for norm in range(2):
        pair = turned[2 * norm : 2 * norm + 2, 0:TILE]
        row = jnp.where(at == 0, pair[0:1, :], pair[1:2, :])
        new = 0.5 * r.gainm_v[norm : norm + 1, :] + row
        r.gg[norm : norm + 1, :] = row
        r.gm[norm : norm + 1, :] = new
        r.gn[norm : norm + 1, :] = r.gain_v[norm : norm + 1, :] - rate * new


def finish(rate, made, sqw=None, mlpw=None, gain=None, gainm=None):
    any_space = pl.BlockSpec(memory_space=pl.ANY)
    in_vmem = pl.BlockSpec(memory_space=VMEM)
    ins = dict(low=made.og)
    outs = dict(og=jax.ShapeDtypeStruct(made.og.shape, F32))
    near, far = 1, 1
    if hasattr(made, "out"):
        ins.update(output=made.output, ag=made.ag, wire=made.out, sqw=sqw, mlpw=mlpw, gain=gain, gainm=gainm)
        like = jax.ShapeDtypeStruct
        near, far = 4, 3
        outs.update(
            output_f=like(made.output.shape, F32),
            ag_f=like(made.ag.shape, F32),
            sqg=like(sqw.shape, F32),
            sqm=like(sqw.shape, F32),
            sqn=like(sqw.shape, F32),
            sqc=like(sqw.shape, BF16),
            mlpg=like(mlpw.shape, F32),
            mlpm=like(mlpw.shape, F32),
            mlpn=like(mlpw.shape, F32),
            mlpc=like(mlpw.shape, BF16),
            gg=like(gain.shape, F32),
            gm=like(gain.shape, F32),
            gn=like(gain.shape, F32),
        )
    scratch = dict(
        og_v=VMEM(made.og.shape, F32),
        sems=pltpu.SemaphoreType.DMA((PARTS + 6,)),
    )
    if hasattr(made, "out"):
        scratch.update(
            sqw_v=VMEM(sqw.shape, F32),
            mlpw_v=VMEM(mlpw.shape, F32),
            gain_v=VMEM(gain.shape, F32),
            gainm_v=VMEM(gainm.shape, F32),
        )
    names = tuple(ins) + tuple(outs) + tuple(scratch)
    made_here = list(ins.values())
    stay = [pltpu.with_memory_space_constraint(value, pltpu.HBM) for value in made_here[near:]]
    results = pl.pallas_call(
        functools.partial(finish_kernel, names, rate),
        out_shape=tuple(outs.values()),
        in_specs=[in_vmem] * near + [any_space] * (len(ins) - near),
        out_specs=[any_space] * far + [in_vmem] * (len(outs) - far),
        scratch_shapes=list(scratch.values()),
        compiler_params=pltpu.CompilerParams(vmem_limit_bytes=16 << 20),
        name="finish",
    )(*made_here[:near], *stay)
    return Refs(zip(outs, results))


HIGH_PRECISION = lax.Precision.HIGHEST


def plain_orthogonalize(matrix):
    current = matrix / (jnp.sqrt(jnp.sum(matrix * matrix)) + 1e-07)
    for turn in range(5):
        gram = jnp.dot(current, current.T, precision=HIGH_PRECISION)
        poly = COEF_B * gram + COEF_C * jnp.dot(gram, gram, precision=HIGH_PRECISION)
        current = COEF_A * current + jnp.dot(poly, current, precision=HIGH_PRECISION)
    return current


def pick_owned(stack, owners, device):
    chosen = jnp.zeros_like(stack[0])
    for index in range(len(owners)):
        chosen = jnp.where(device == owners[index], stack[index], chosen)
    return chosen


def is_owner(owners, device):
    flag = device < 0
    for owner in owners:
        flag = jnp.logical_or(flag, device == owner)
    return flag


def from_wire(grads):
    def matrix(base, tiles):
        part = grads[:, base : base + tiles * TILE, :].reshape(-1, tiles, TILE, LANES)
        return part.transpose(0, 2, 1, 3).reshape(-1, tiles * LANES)

    square = jnp.stack([matrix(SQ_AT[m], 2) for m in range(5)])
    mlp = jnp.stack([matrix(m * MLP_ROWS, 8) for m in range(2)])
    return square, mlp, grads[0, GAIN_BASE : GAIN_BASE + 4, :].reshape(2, 2 * LANES)


def update_by_collectives(
    grads, square_weights, mlp_weights, gains, square_moment, mlp_moment, gain_moment, rate
):
    square_local, mlp_local, gain_local = from_wire(grads)
    square_grad, mlp_grad, gain_grad = (
        lax.psum_scatter(square_local, "dp", scatter_dimension=1, tiled=True),
        lax.psum_scatter(mlp_local, "dp", scatter_dimension=1, tiled=True),
        lax.psum_scatter(gain_local, "dp", scatter_dimension=1, tiled=True),
    )
    square_moment_new = 0.5 * square_moment + square_grad
    mlp_moment_new = 0.5 * mlp_moment + mlp_grad
    gain_moment_new = 0.5 * gain_moment + gain_grad
    device = lax.axis_index("dp")
    count = lax.axis_size("dp")
    square_owners = [index * count // 7 for index in range(5)]
    mlp_owners = [(index + 5) * count // 7 for index in range(2)]
    square_full, mlp_full = (
        lax.all_gather(square_moment_new, "dp", axis=1, tiled=True),
        lax.all_gather(mlp_moment_new, "dp", axis=1, tiled=True),
    )
    mine_square = pick_owned(square_full, square_owners, device)
    mine_mlp = pick_owned(mlp_full, mlp_owners, device)
    made_square = lax.cond(
        is_owner(square_owners, device), plain_orthogonalize, jnp.zeros_like, mine_square
    )
    made_mlp = lax.cond(is_owner(mlp_owners, device), plain_orthogonalize, jnp.zeros_like, mine_mlp)
    stack_square = jnp.stack(
        [jnp.where(device == owner, made_square, 0.0) for owner in square_owners]
    )
    stack_mlp = jnp.stack([jnp.where(device == owner, made_mlp, 0.0) for owner in mlp_owners])
    square_ortho, mlp_ortho = (
        lax.psum_scatter(stack_square, "dp", scatter_dimension=1, tiled=True),
        lax.psum_scatter(stack_mlp, "dp", scatter_dimension=1, tiled=True),
    )
    square_new = square_weights - jnp.array(SQ_RATES, F32)[:, None, None] * square_ortho
    mlp_new = mlp_weights - jnp.array(MLP_RATES, F32)[:, None, None] * mlp_ortho
    gains_new = gains - rate * gain_moment_new
    return (
        square_grad,
        square_moment_new,
        square_new,
        square_new.astype(BF16),
        mlp_grad,
        mlp_moment_new,
        mlp_new,
        mlp_new.astype(BF16),
        gain_grad,
        gain_moment_new,
        gains_new,
    )


def per_device(
    actions,
    observed,
    camera_flags,
    noise_levels,
    cotangent,
    square_weights,
    mlp_weights,
    gains,
    square_moment,
    mlp_moment,
    gain_moment,
):
    count = lax.axis_size("dp")
    rate = 0.1 / math.sqrt(actions.shape[0] * count)
    by_key = observed.transpose(1, 0, 2)
    ins = (actions, by_key, camera_flags, noise_levels, cotangent)
    if count == math.prod(GRID):
        made = block_and_back(True, *ins, square_weights, mlp_weights, gains, square_moment, mlp_moment)
        done = finish(rate, made, square_weights, mlp_weights, gains, gain_moment)
        output, actions_grad = done.output_f, done.ag_f
        d = done
        rest = (d.sqg, d.sqm, d.sqn, d.sqc, d.mlpg, d.mlpm, d.mlpn, d.mlpc, d.gg, d.gm, d.gn)
    else:
        square_all, mlp_all = (
            lax.all_gather(square_weights.astype(BF16), "dp", axis=1, tiled=True),
            lax.all_gather(mlp_weights.astype(BF16), "dp", axis=1, tiled=True),
        )
        gain_all = lax.all_gather(gains, "dp", axis=1, tiled=True)
        made = block_and_back(False, *ins, square_all, mlp_all, gain_all)
        done = finish(rate, made)
        output, actions_grad = made.output, made.ag
        grads = made.grads.reshape(-1, WIRE, LANES)
        rest = update_by_collectives(
            grads, square_weights, mlp_weights, gains, square_moment, mlp_moment, gain_moment, rate
        )
    observed_grad = done.og.transpose(1, 0, 2)
    return (output, actions_grad, observed_grad) + tuple(rest)


def solution(mesh):
    rows, cube, flat = P("dp", None), P("dp", None, None), P("dp")
    stacked, pair = P(None, "dp", None), P(None, "dp")
    return jax.shard_map(
        per_device,
        mesh=mesh,
        in_specs=(rows, cube, flat, flat, rows, stacked, stacked, pair, stacked, stacked, pair),
        out_specs=(rows, rows, cube) + (stacked,) * 8 + (pair,) * 3,
        check_vma=False,
    )
```

```python
import functools
import math

import jax
import jax.numpy as jnp
from jax import lax
from jax.experimental import pallas as pl
from jax.experimental.pallas import tpu as pltpu
from jax.sharding import PartitionSpec as P

HEADS = 4
ACT = 16
OBS_FULL = 196
OBS_FEW = 49
COEF_A = 3.4445
COEF_B = -4.775
COEF_C = 2.0315
F32 = jnp.float32
BF16 = jnp.bfloat16
MESH = pl.DeviceIdType.MESH
VMEM = pltpu.VMEM
NN = (((1,), (0,)), ((), ()))
NT = (((1,), (1,)), ((), ()))
TN = (((0,), (0,)), ((), ()))

LANES = 128
TILE = 8
MLP_ROWS = 64
SQ_ROWS = 16
SQ_AT = (160, 192, 176, 128, 144)
GAIN_BASE = 208
WIRE = 224
PIECES = ((0, 32), (32, 32), (64, 32), (96, 32), (128, 32), (160, 32), (192, 32))
PIECE_X_FIRST = (True, False, True, False, True, True, False)
CHUNKS = ((0, 32), (32, 32), (64, 32), (96, 32), (128, 32), (160, 32), (192, 16), (208, 16))
X_FIRST = (True, False, True, False, True, False, True, False)
PARTS_OUT = (
    (0, 0, 0, 32, 0),
    (1, 0, 32, 32, 32),
    (2, 1, 64, 32, 0),
    (3, 1, 96, 32, 32),
    (4, 5, 128, 16, 0),
    (4, 6, 144, 16, 0),
    (5, 2, 160, 16, 0),
    (5, 4, 176, 16, 0),
    (6, 3, 192, 16, 0),
)
MLP_RATES = (1.0, 0.5)
SQ_RATES = (0.5, 0.5, 0.5, 0.5, 4.0)
GRID = (4, 2, 2, 2)
OWNERS = (8, 22, 14, 16, 11, 21, 13)
SHIFTS = (0.0, 0.0, 0.4, 0.8, 0.8)
KEYS_PAD = 208
GROUP = 16
ROWS = 512


class Refs:
    def __init__(self, pairs):
        self.__dict__.update(pairs)


def dot(left, right, dims=NN):
    return lax.dot_general(left, right, dims, preferred_element_type=F32)


def place():
    me = lax.axis_index("dp")
    return me, me // 8, (me // 4) % 2, (me // 2) % 2, me % 2


def device_at(z, y, x, c):
    return ((z * 2 + y) * 2 + x) * 2 + c


def link(src, dst, send, recv, device):
    return pltpu.make_async_remote_copy(
        src_ref=src,
        dst_ref=dst,
        send_sem=send,
        recv_sem=recv,
        device_id=(device,),
        device_id_type=MESH,
    )


def greet(device):
    pl.semaphore_signal(
        pltpu.get_barrier_semaphore(), inc=1, device_id=(device,), device_id_type=MESH
    )


def normalize(values):
    centred = values - jnp.mean(values, -1, keepdims=True)
    scale = lax.rsqrt(jnp.mean(centred * centred, -1, keepdims=True) + 1e-05)
    return centred * scale, scale


def norm_back(grad, hat, scale):
    mean_one = jnp.mean(grad, -1, keepdims=True)
    mean_two = jnp.mean(grad * hat, -1, keepdims=True)
    return scale * (grad - mean_one - hat * mean_two)


class Gather:
    def __init__(self, r):
        self.r = r
        self.me, self.z, self.y, self.x, self.c = place()

    def hop(self, k, step, part, device):
        return link(part, part, self.r.gsend.at[k, step], self.r.grecv.at[k, step], device)

    def along_z(self, k, step):
        part = self.r.wire.at[self.z, self.y, self.x, self.c, pl.ds(*PIECES[k])]
        return self.hop(k, step, part, device_at((self.z + step + 1) % 4, self.y, self.x, self.c))

    def from_z(self, k, step):
        there = (self.z + 3 - step) % 4
        part = self.r.wire.at[there, self.y, self.x, self.c, pl.ds(*PIECES[k])]
        return self.hop(k, step, part, device_at(there, self.y, self.x, self.c))

    def plane(self, k, second, mine):
        z, y, x, c = self.z, self.y, self.x, self.c
        rows, wire = pl.ds(*PIECES[k]), self.r.wire
        py, px = (y, x) if mine else (1 - y, 1 - x)
        along_x = PIECE_X_FIRST[k] == second
        if along_x:
            part = wire.at[:, y, px, c, rows] if second else wire.at[:, :, px, c, rows]
            return self.hop(k, 3 if second else 4, part, device_at(z, y, 1 - x, c))
        part = wire.at[:, py, x, c, rows] if second else wire.at[:, py, :, c, rows]
        return self.hop(k, 3 if second else 4, part, device_at(z, 1 - y, x, c))

    def core(self, k, mine):
        part = self.r.wire.at[:, :, :, self.c if mine else 1 - self.c, pl.ds(*PIECES[k])]
        return self.hop(k, 5, part, device_at(self.z, self.y, self.x, 1 - self.c))

    def first(self, *chunks):
        for k in chunks:
            for step in range(3):
                self.along_z(k, step).start()

    def second(self, *chunks):
        for k in chunks:
            for step in range(3):
                self.from_z(k, step).wait_recv()
            self.plane(k, True, True).start()

    def third(self, *chunks):
        for k in chunks:
            self.plane(k, True, False).wait_recv()
            self.plane(k, False, True).start()

    def fourth(self, *chunks):
        for k in chunks:
            self.plane(k, False, False).wait_recv()
            self.core(k, True).start()

    def last(self, *chunks):
        for k in chunks:
            self.core(k, False).wait_recv()

    def drain(self):
        for k in range(len(PIECES)):
            for step in range(3):
                self.along_z(k, step).wait_send()
            self.plane(k, True, True).wait_send()
            self.plane(k, False, True).wait_send()
            self.core(k, True).wait_send()

    def fill(self):
        r = self.r
        spot = (self.z, self.y, self.x, self.c)

        def tiles(source, m, base, number):
            for j in range(number):
                pair = [source[m, :, pl.ds((2 * j + k) * LANES, LANES)] for k in range(2)]
                r.wire[spot + (pl.ds(base + j * 16, 16),)] = jnp.concatenate(pair, axis=0).astype(BF16)

        for m in range(5):
            tiles(r.sqw_v, m, SQ_AT[m], 1)
        for m in range(2):
            tiles(r.mlpw_v, m, m * MLP_ROWS, 4)
        gains, edge = r.gain_v[...], r.edge
        high = gains.astype(BF16).astype(F32)
        middle = (gains - high).astype(BF16).astype(F32)
        edge[...] = jnp.zeros_like(edge)
        edge[0:2, 0:TILE] = high
        edge[2:4, 0:TILE] = middle
        edge[4:6, 0:TILE] = (gains - high - middle).astype(BF16).astype(F32)
        r.wire[spot + (pl.ds(GAIN_BASE, 16),)] = edge[...].astype(BF16)

    def unpack(self, base, number, out, m):
        for j in range(number):
            block = self.r.wire[:, :, :, :, pl.ds(base + j * 16, 16), :].reshape(32, 16, LANES).astype(F32)
            for half in range(2):
                columns = pl.ds((2 * j + half) * LANES, LANES)
                out[m, :, columns] = block[:, half * 8 : half * 8 + 8, :].reshape(256, LANES).astype(BF16)

    def unpack_gains(self):
        edge, wire = self.r.edge, self.r.wire
        for half in range(2):
            total = jnp.zeros((16, LANES), F32)
            for at in range(16):
                d = half * 16 + at
                tile = wire[d // 8, (d // 4) % 2, (d // 2) % 2, d % 2, pl.ds(GAIN_BASE, 16), :].astype(F32)
                total = total + (tile if at == 0 else pltpu.roll(tile, at * TILE, 1))
            edge[...] = total
            self.r.gain_all[:, pl.ds(half * LANES, LANES)] = edge[0:2, :] + edge[2:4, :] + edge[4:6, :]


class Update:
    def __init__(self, r):
        self.r = r
        self.me, self.z, self.y, self.x, self.c = place()

    def hop(self, k, step, src, dst, device):
        return link(src, dst, self.r.send.at[k, step], self.r.recv.at[k, step], device)

    def core(self, k):
        rows = pl.ds(*CHUNKS[k])
        src, dst = self.r.send0.at[:, :, :, rows], self.r.got_core.at[:, :, :, rows]
        return self.hop(k, 0, src, dst, device_at(self.z, self.y, self.x, 1 - self.c))

    def plane(self, k, first):
        rows = pl.ds(*CHUNKS[k])
        to = (self.z, self.y, 1 - self.x, self.c) if X_FIRST[k] == first else (self.z, 1 - self.y, self.x, self.c)
        if first:
            src, dst = self.r.send1.at[:, :, rows], self.r.got1.at[:, :, rows]
        else:
            src, dst = self.r.send2.at[:, rows], self.r.got2.at[:, rows]
        return self.hop(k, 1 if first else 2, src, dst, device_at(*to))

    def along_z(self, k, step):
        rows = pl.ds(*CHUNKS[k])
        there = (self.z + step + 1) % 4
        src, dst = self.r.send3.at[there, rows], self.r.got3.at[step, rows]
        return self.hop(k, 3 + step, src, dst, device_at(there, self.y, self.x, self.c))

    def start(self, k):
        rows = pl.ds(*CHUNKS[k])
        self.r.send0[:, :, :, rows, :] = self.r.grads[:, :, :, 1 - self.c, rows, :].astype(BF16)
        self.core(k).start()

    def one(self, *chunks):
        r = self.r
        for k in chunks:
            rows = pl.ds(*CHUNKS[k])
            self.core(k).wait_recv()
            sum1 = r.sum1
            sum1[:, :, :, rows, :] = r.grads[:, :, :, self.c, rows, :] + r.got_core[:, :, :, rows, :].astype(F32)
            other = sum1[:, :, 1 - self.x, rows, :] if X_FIRST[k] else sum1[:, 1 - self.y, :, rows, :]
            r.send1[:, :, rows, :] = other.astype(BF16)
            self.plane(k, True).start()

    def two(self, *chunks):
        r = self.r
        for k in chunks:
            rows = pl.ds(*CHUNKS[k])
            self.plane(k, True).wait_recv()
            sum1, sum2 = r.sum1, r.sum2
            mine = sum1[:, :, self.x, rows, :] if X_FIRST[k] else sum1[:, self.y, :, rows, :]
            sum2[:, :, rows, :] = mine + r.got1[:, :, rows, :].astype(F32)
            other = 1 - self.y if X_FIRST[k] else 1 - self.x
            r.send2[:, rows, :] = sum2[:, other, rows, :].astype(BF16)
            self.plane(k, False).start()

    def three(self, *chunks):
        r = self.r
        for k in chunks:
            rows = pl.ds(*CHUNKS[k])
            self.plane(k, False).wait_recv()
            mine = self.y if X_FIRST[k] else self.x
            total = r.sum2[:, mine, rows, :] + r.got2[:, rows, :].astype(F32)
            r.sum3[:, rows, :] = total
            r.send3[:, rows, :] = total.astype(BF16)
            if k >= 4:
                own = r.sum3[self.z, rows, :] + 0.5 * r.moment[rows, :]
                r.send3[self.z, rows, :] = own.astype(BF16)
                self.parts_to_owners(k)
            for step in range(3):
                self.along_z(k, step).start()

    def parts_to_owners(self, k):
        for part, (chunk, index, *_) in enumerate(PARTS_OUT):
            if chunk != k:
                continue

            @pl.when(self.me != OWNERS[index])
            def _():
                self.to_owner(part).start()

            @pl.when(self.me == OWNERS[index])
            def _():
                src, dst = self.own_part(part)
                pltpu.make_async_copy(src, dst, self.r.own_recv.at[0]).start()

    def result(self, index):
        return self.r.result_mlp if index < 2 else self.r.result_sq

    def own_part(self, part):
        _, index, base, number, place = PARTS_OUT[part]
        if index < 2:
            return self.r.moment_low.at[pl.ds(base, number)], self.r.slabs_mlp.at[self.me, pl.ds(place, number)]
        return self.r.send3.at[:, pl.ds(base, number)], self.r.slabs_sq.at[self.z, self.me % 8]

    def to_owner(self, part):
        src, dst = self.own_part(part)
        return link(src, dst, self.r.own_send.at[part], self.r.own_recv.at[0], OWNERS[PARTS_OUT[part][1]])

    def four(self, *chunks):
        r = self.r
        moment, out = r.moment, r.out
        for k in chunks:
            rows = pl.ds(*CHUNKS[k])
            total = r.sum3[self.z, rows, :]
            for step in range(3):
                self.along_z(k, step).wait_recv()
                total = total + r.got3[step, rows, :].astype(F32)
            out[0, rows, :] = total
            new = 0.5 * moment[rows, :] + total
            moment[rows, :] = new
            if k < 4:
                r.moment_low[rows, :] = new.astype(BF16)
            if k < 4:
                self.parts_to_owners(k)

    def old_moment(self):
        r = self.r
        moment = r.moment
        for m in range(2):
            for j in range(8):
                moment[pl.ds(m * MLP_ROWS + j * TILE, TILE), :] = r.mlpm_v[m, :, pl.ds(j * LANES, LANES)]
        for m in range(5):
            for j in range(2):
                moment[pl.ds(SQ_AT[m] + j * TILE, TILE), :] = r.sqm_v[m, :, pl.ds(j * LANES, LANES)]
        moment[pl.ds(GAIN_BASE, 16), :] = jnp.zeros((16, LANES), F32)

    def orthogonalize(self):
        r = self.r
        cur = r.cur
        rows = lax.broadcasted_iota(jnp.int32, (256, 256), 0)
        diagonal = rows == lax.broadcasted_iota(jnp.int32, (256, 256), 1)

        low = r.cur_low

        def load(rows, j, pair):
            for side in range(2):
                columns = pl.ds((2 * j + side) * LANES, LANES)
                part = pair[:, side * TILE : (side + 1) * TILE, :].reshape(-1, LANES)
                cur[rows, columns] = part
                low[rows, columns] = part.astype(BF16)

        def load_mlp():
            for j in range(4):
                load(pl.ds(0, 256), j, r.slabs_mlp[:, pl.ds(j * 16, 16), :].astype(F32))

        def load_sq():
            for to in range(4):
                pair = r.slabs_sq[0, :, to].astype(F32)
                for plane in range(1, 4):
                    pair = pair + r.slabs_sq[plane, :, to].astype(F32)
                load(pl.ds(to * 64, 64), 0, pair)

        def run(slabs, fetch, result, tiles):
            pltpu.make_async_copy(slabs, slabs, r.own_recv.at[0]).wait()
            fetch()
            scale = 1.0
            for turn, shift in enumerate(SHIFTS):
                whole = low[:, 0 : tiles * LANES]
                off = dot(whole, whole, NT)
                if turn == 0:
                    norm = jnp.sum(jnp.sum(jnp.where(diagonal, off, 0.0), axis=0, keepdims=True), axis=1, keepdims=True)
                    scale = 1.0 / (jnp.sqrt(norm) + 1e-07)
                    off = off * (scale * scale)
                if shift:
                    off = off - jnp.where(diagonal, shift, 0.0)
                off_low = off.astype(BF16)
                poly = (COEF_B + 2.0 * COEF_C * shift) * off + COEF_C * dot(off_low, off_low)
                poly = poly.astype(BF16)
                keep = COEF_A + shift * (COEF_B + COEF_C * shift)
                for j in range(tiles // 2):
                    columns = pl.ds(j * 2 * LANES, 2 * LANES)
                    now = keep * cur[:, columns] + dot(poly, low[:, columns])
                    if turn == 0:
                        now = now * scale
                    if turn < len(SHIFTS) - 1:
                        cur[:, columns] = now
                        low[:, columns] = now.astype(BF16)
                    else:
                        parts = [now[:, side * LANES : (side + 1) * LANES].reshape(32, TILE, LANES) for side in range(2)]
                        result[:, pl.ds(j * 16, 16), :] = jnp.concatenate(parts, axis=1).astype(result.dtype)

        mine_mlp = jnp.logical_or(self.me == OWNERS[0], self.me == OWNERS[1])
        mine_sq = self.me < 0
        for device in OWNERS[2:]:
            mine_sq = jnp.logical_or(mine_sq, self.me == device)

        @pl.when(mine_mlp)
        def _():
            run(r.slabs_mlp, load_mlp, r.result_mlp, 8)

        @pl.when(mine_sq)
        def _():
            run(r.slabs_sq, load_sq, r.result_sq, 2)

    def landing(self, index):
        if index < 2:
            return self.r.back_mlp.at[index]
        return self.r.out.at[2, pl.ds(SQ_AT[index - 2], SQ_ROWS)]

    def give_back(self, index, device):
        result = self.result(index)
        return link(
            result.at[device], self.landing(index),
            self.r.back_send.at[device], self.r.back_recv.at[index], device,
        )

    def give_all(self):
        r = self.r
        for index in range(7):
            result = self.result(index)

            @pl.when(self.me == OWNERS[index])
            def _():
                def send_one(step, _):
                    self.give_back(index, (self.me + step) % 32).start()
                    return 0

                lax.fori_loop(1, 32, send_one, 0)
                pltpu.make_async_copy(result.at[self.me], self.landing(index), r.back_recv.at[index]).start()

    def take_all(self):
        for index in range(7):
            result = self.result(index)
            pltpu.make_async_copy(result.at[0], self.landing(index), self.r.back_recv.at[index]).wait()
        for index in range(2):
            rows = pl.ds(index * MLP_ROWS, MLP_ROWS)
            self.r.out[2, rows, :] = self.r.back_mlp[index].astype(F32)

    def drain(self):
        for k in range(len(CHUNKS)):
            self.core(k).wait_send()
            self.plane(k, True).wait_send()
            self.plane(k, False).wait_send()
            for step in range(3):
                self.along_z(k, step).wait_send()
        for part in range(len(PARTS_OUT)):

            @pl.when(self.me != OWNERS[PARTS_OUT[part][1]])
            def _():
                self.to_owner(part).wait_send()

    def drain_owner(self):
        for index in range(7):

            @pl.when(self.me == OWNERS[index])
            def _():
                def wait_one(step, _):
                    self.give_back(index, (self.me + step) % 32).wait_send()
                    return 0

                lax.fori_loop(1, 32, wait_one, 0)


def greet_all():
    me, z, y, x, c = place()
    greet(device_at(z, y, x, 1 - c))
    greet(device_at(z, y, 1 - x, c))
    greet(device_at(z, 1 - y, x, c))
    for step in range(1, 4):
        greet(device_at((z + step) % 4, y, x, c))
    owner = me < 0
    for device in OWNERS:
        owner = jnp.logical_or(owner, me == device)

        @pl.when(me != device)
        def _():
            greet(device)

    @pl.when(owner)
    def _():
        def greet_other(step, _):
            greet((me + step) % 32)
            return 0

        lax.fori_loop(1, 32, greet_other, 0)

    is_owner = owner.astype(jnp.int32)
    return 6 + 7 - is_owner + 31 * is_owner


def block_kernel(names, remote, *args):
    r = Refs(zip(names, args))
    keys, samples = r.obs.shape[0], r.obs.shape[1]
    tokens, width = r.acts.shape
    head_dim, half, per = width // HEADS, width // 2, ROWS // ACT
    wide = r.mlp_all.shape[2]
    groups = samples // GROUP
    in_sems, out_sems = r.in_sems, r.out_sems

    if remote:
        own = (r.sqw_v, r.mlpw_v, r.gain_v)
    else:
        own = (r.sq_all, r.mlp_all, r.gain_all)
    loads = list(zip((r.sqw, r.mlpw, r.gain), own))
    loads += [(r.acts, r.acts_v), (r.obs, r.obs_v.at[pl.ds(0, keys)]), (r.cot, r.cot_v)]
    if remote:
        loads += [(r.sqm, r.sqm_v), (r.mlpm, r.mlpm_v)]
    loads += [(r.flags, r.flags_s), (r.levels, r.levels_s)]
    copies = [pltpu.make_async_copy(a, b, in_sems.at[i]) for i, (a, b) in enumerate(loads)]

    def arrive(*which):
        for i in which:
            copies[i].wait()

    for copy in copies:
        copy.start()
    if remote:
        gather, update = Gather(r), Update(r)
        expected = greet_all()
        arrive(0, 1, 2)
        gather.fill()
        pl.semaphore_wait(pltpu.get_barrier_semaphore(), expected)
        gather.first(5, 6, 4, 0, 1, 2, 3)

    arrive(3)

    def hats(i, _):
        rows = pl.ds(pl.multiple_of(i * ROWS, ROWS), ROWS)
        hat, scale = normalize(r.acts_v[rows, :])
        r.xhat[rows, :] = hat
        r.rstd[rows, :] = scale
        return 0

    lax.fori_loop(0, tokens // ROWS, hats, 0)

    mem, obs_v = r.mem, r.obs_v
    batch = 16
    chunks = KEYS_PAD // batch
    swap = r.swap
    row = lax.broadcasted_iota(jnp.int32, swap.shape, 0)
    column = lax.broadcasted_iota(jnp.int32, swap.shape, 1)
    swap[...] = jnp.where(column == (row % batch) * batch + row // batch, 1.0, 0.0).astype(BF16)

    def turn(part, low, high):
        def one(j, _):
            at = pl.ds(pl.multiple_of(j * batch, batch), batch)
            here = pl.ds(part * batch, batch)
            block = obs_v[at, here, :].reshape(batch * batch, width)
            mem[here, at, :] = dot(swap[...], block).astype(BF16).reshape(batch, batch, width)
            return 0

        lax.fori_loop(low, high, one, 0, unroll=high - low)

    whole = chunks - 1
    arrive(4)
    turn(0, 0, whole // 2)
    if remote:
        gather.second(5, 6)
    turn(0, whole // 2, whole)
    if remote:
        gather.third(5, 6)
    turn(1, 0, whole // 2)
    if remote:
        gather.second(4, 0, 1)
        gather.fourth(5, 6)
    turn(1, whole // 2, whole)
    if remote:
        gather.second(2, 3)
    arrive(len(copies) - 1, len(copies) - 2)
    freqs = jnp.exp(
        lax.broadcasted_iota(jnp.int32, (1, half), 1).astype(F32) * F32(-math.log(10000.0)) / half
    )
    for s in range(samples):
        r.angle[s : s + 1, :] = r.levels_s[s].astype(F32) * freqs
    r.embed[:, 0:half] = jnp.sin(r.angle[...]).astype(BF16)
    r.embed[:, half:width] = jnp.cos(r.angle[...]).astype(BF16)
    if remote:
        arrive(6, 7)
        update.old_moment()
        gather.third(4, 0, 1)
        gather.last(5, 6)
        for m in range(3):
            gather.unpack(SQ_AT[m], 1, r.sq_all, m)
        gather.unpack_gains()
    else:
        arrive(0, 1, 2)

    sq, mlp = r.sq_all, r.mlp_all
    wkh, wvh = r.wkh, r.wvh
    lane = lax.broadcasted_iota(jnp.int32, (width, width), 1)

    def split_heads(out, weight):
        weight = weight.astype(F32)
        for h in range(HEADS):
            out[pl.ds(h * width, width), :] = jnp.where(lane // head_dim == h, weight, 0.0).astype(BF16)

    split_heads(wkh, sq[2])
    g1, g2 = r.gain_all[0:1, :], r.gain_all[1:2, :]

    obs_v[keys] = dot(r.embed[...], sq[0]).astype(BF16)
    obs_v[keys + 1 :] = jnp.zeros((KEYS_PAD - keys - 1, samples, width), BF16)
    for part in range(samples // batch):
        turn(part, whole, chunks)

    queries, dmixes = r.queries, r.dmixes

    def make_queries(i, _):
        rows = pl.ds(pl.multiple_of(i * ROWS, ROWS), ROWS)
        first = (r.xhat[rows, :] * g1).astype(BF16)
        r.first[rows, :] = first
        q = dot(first, sq[1]).astype(BF16)
        r.query[rows, :] = q
        here = pl.ds(i * per, per)
        for h in range(HEADS):
            wk = wkh[pl.ds(h * width, width), :]
            value = (dot(q, wk, NT) * 0.125).astype(BF16).reshape(per, ACT, width)
            queries[here, pl.ds(h * ACT, ACT), :] = value
        return 0

    lax.fori_loop(0, tokens // ROWS, make_queries, 0)

    key = lax.broadcasted_iota(jnp.int32, (KEYS_PAD, LANES), 0)
    rows_each = HEADS * ACT
    left = lax.broadcasted_iota(jnp.int32, (KEYS_PAD, LANES), 1) < rows_each
    left_row = lax.broadcasted_iota(jnp.int32, (1, LANES), 1) < rows_each
    rest = jnp.where((key >= OBS_FEW) & (key < OBS_FULL), 1.0, 0.0)
    padding = jnp.where(key > OBS_FULL, -1000000000.0, 0.0)

    def with_memory(s, sides):
        here = pl.ds(s, 4)
        wide = dot(mem[here].reshape(4 * KEYS_PAD, width), sides[here].reshape(4 * rows_each, width), NT)
        part = [wide[k * KEYS_PAD : (k + 1) * KEYS_PAD, (k // 2) * LANES : (k // 2 + 1) * LANES] for k in range(4)]
        return jnp.where(left, part[0], part[1]), jnp.where(left, part[2], part[3])

    def each_head(out, s, value):
        rows = pl.ds(pl.multiple_of(s * ACT, ACT), ACT)
        for h in range(HEADS):
            out[rows, pl.ds(h * width, width)] = value[h * ACT : (h + 1) * ACT, :]

    def attend(g, _):
        pairs = []
        for quad in range(GROUP // 4):
            pairs.extend(with_memory(g * GROUP + 4 * quad, queries))
        turned = []
        for k, score in enumerate(pairs):
            s = g * GROUP + 2 * k
            drop = [(1 - r.flags_s[s + side]).astype(F32) * -1000000000.0 for side in range(2)]
            score = score + (rest * jnp.where(left_row, drop[0], drop[1]) + padding)
            expo = jnp.exp(score - jnp.max(score, 0, keepdims=True))
            probs = expo * (1.0 / jnp.sum(expo, 0, keepdims=True))
            r.probs[g * (GROUP // 2) + k] = probs
            turned.append(probs.astype(BF16).T)
        for k, low in enumerate(turned):
            for side in range(2):
                s = g * GROUP + 2 * k + side
                each_head(r.u, s, dot(low[side * rows_each : (side + 1) * rows_each], mem[s]).astype(BF16))
        return 0

    lax.fori_loop(0, groups // 2, attend, 0)
    if remote:
        gather.third(2, 3)
        gather.fourth(4, 0, 1)
    lax.fori_loop(groups // 2, groups, attend, 0)
    if remote:
        gather.fourth(2, 3)
        gather.last(4)
        for m in range(3, 5):
            gather.unpack(SQ_AT[m], 1, sq, m)
    split_heads(wvh, sq[3])

    gain_acc = r.gain_acc
    gain_acc[...] = jnp.zeros_like(gain_acc)
    blocks = [pl.ds(i * ROWS, ROWS) for i in range(tokens // ROWS)]
    for rows in blocks:
        mixed = dot(r.u[rows, :], wvh[...]).astype(BF16)
        r.mixed[rows, :] = mixed
        resid = r.acts_v[rows, :] + dot(mixed, sq[4])
        r.resid[rows, :] = resid
        hat, scale = normalize(resid)
        r.hat_two[rows, :] = hat
        r.rstd_two[rows, :] = scale
        r.second[rows, :] = (hat * g2).astype(BF16)
    arrive(5)
    r.out_low[...] = r.cot_v[...].astype(BF16)
    if remote:
        gather.last(0, 1)
        gather.unpack(0, 4, mlp, 0)
    wide_blocks = [pl.ds(c * 256, 256) for c in range(wide // 256)]
    for rows in blocks:
        for columns in wide_blocks:
            v = dot(r.second[rows, :], mlp[0, :, columns])
            square = v * v
            t = jnp.tanh(0.7978845608 * (v + 0.044715 * square * v))
            r.active[rows, columns] = (0.5 * v * (1.0 + t)).astype(BF16)
            slope = 0.5 * (1.0 + t) + 0.5 * v * (1.0 - t * t) * (0.7978845608 * (1.0 + 0.134145 * square))
            r.slope[rows, columns] = slope

    grads = r.grads

    def put(base, tiles, value):
        for j in range(tiles):
            part = value[:, j * LANES : (j + 1) * LANES].reshape(GRID + (TILE, LANES))
            grads[:, :, :, :, pl.ds(base + j * TILE, TILE), :] = part

    def by_head(left, right):
        turned = left.T
        parts = [
            dot(turned[h * head_dim : (h + 1) * head_dim, :], right[:, pl.ds(h * width, width)])
            for h in range(HEADS)
        ]
        return jnp.concatenate(parts, axis=0).T

    put(MLP_ROWS, 8, dot(r.out_low[...], r.active[...], TN))
    if remote:
        update.start(2)
        update.start(3)
        gather.last(2, 3)
        gather.unpack(MLP_ROWS, 4, mlp, 1)
    for rows in blocks:
        for columns in wide_blocks:
            slope = r.slope[rows, columns]
            r.dhidden[rows, columns] = (slope * dot(r.out_low[rows, :], mlp[1, :, columns])).astype(BF16)
    put(0, 8, dot(r.second[...], r.dhidden[...], TN))
    if remote:
        update.start(0)
        update.start(1)
        update.one(2, 3)
    for i, rows in enumerate(blocks):
        r.out_v[rows, :] = r.resid[rows, :] + dot(r.active[rows, :], mlp[1], NT)
        grad_second = dot(r.dhidden[rows, :], mlp[0], NT)
        hat = r.hat_two[rows, :]
        gain_acc[1:2, :] += jnp.sum(grad_second * hat, 0, keepdims=True)
        dres = r.cot_v[rows, :] + norm_back(grad_second * g2, hat, r.rstd_two[rows, :])
        r.dres[rows, :] = dres
        low = dres.astype(BF16)
        r.dres_low[rows, :] = low
        gm = dot(low, sq[4], NT).astype(BF16)
        r.dmixed[rows, :] = gm
        here = pl.ds(i * per, per)
        for h in range(HEADS):
            wv = wvh[pl.ds(h * width, width), :]
            dmixes[here, pl.ds(h * ACT, ACT), :] = dot(gm, wv, NT).astype(BF16).reshape(per, ACT, width)
    keep_out = pltpu.make_async_copy(r.out_v, r.output, out_sems.at[0])
    keep_out.start()
    if remote:
        update.one(0, 1)
    put(SQ_AT[4], 2, dot(r.mixed[...], r.dres_low[...], TN))
    put(SQ_AT[3], 2, by_head(r.dmixed[...], r.u))
    if remote:
        update.start(4)

    left_low = jnp.where(left_row, 1.0, 0.0).astype(BF16)
    right_low = jnp.where(left_row, 0.0, 1.0).astype(BF16)
    left_two = jnp.concatenate([left_low, left_low], axis=1)
    right_two = jnp.concatenate([right_low, right_low], axis=1)

    def pair_sides(s):
        here = pl.ds(s, 2)
        return jnp.concatenate([x[here].reshape(2 * rows_each, width) for x in (dmixes, queries)], axis=0)

    def attend_back(g, _):
        pairs = []
        for quad in range(GROUP // 4):
            pairs.extend(with_memory(g * GROUP + 4 * quad, dmixes))
        lows = []
        for k, rise in enumerate(pairs):
            probs = r.probs[g * (GROUP // 2) + k]
            both = probs * rise
            dscore = (both - probs * jnp.sum(both, 0, keepdims=True)).astype(BF16)
            lows.append((probs.astype(BF16), dscore, dscore.T))
        for k, (low, dscore, turned) in enumerate(lows):
            s = g * GROUP + 2 * k
            for side in range(2):
                dq = dot(turned[side * rows_each : (side + 1) * rows_each], mem[s + side]) * 0.125
                each_head(r.dq_wide, s + side, dq.astype(BF16))
            both = jnp.concatenate([low, dscore], axis=1)
            r.pairs[g * (GROUP // 2) + k] = both
            end = both[192:KEYS_PAD]
            last = dot(jnp.concatenate([end * left_two, end * right_two], axis=0), pair_sides(s))
            for side in range(2):
                r.stamps[s + side] = last[side * 16 : side * 16 + 8, :]
        return 0

    lax.fori_loop(0, groups // 2, attend_back, 0)
    if remote:
        update.two(2, 3)
        update.one(4)
        update.two(0, 1)
    lax.fori_loop(groups // 2, groups, attend_back, 0)
    if remote:
        update.three(2, 3)
        update.two(4)
    put(SQ_AT[2], 2, by_head(r.query[...], r.dq_wide))
    stamp_low = r.stamps[:, 4:5, :].reshape(samples, width).astype(BF16)
    put(SQ_AT[0], 2, dot(r.embed[...], stamp_low, TN))
    if remote:
        update.start(5)
        update.three(0, 1)

    def memory_back(low, high):
        for p in range(low, high):
            both = r.pairs[p]
            dmem = dot(jnp.concatenate([both * left_two, both * right_two], axis=0), pair_sides(2 * p))
            for side in range(2):
                mem[2 * p + side] = dmem[side * KEYS_PAD : (side + 1) * KEYS_PAD, :].astype(BF16)

    def keep_og(part):
        here = pl.ds(part * batch, batch)
        return pltpu.make_async_copy(obs_v.at[pl.ds(0, keys), here], r.og.at[:, here], out_sems.at[2 + part])

    def turn_back(part, low, high):
        def one(j):
            at = pl.ds(pl.multiple_of(j * batch, batch), batch)
            here = pl.ds(part * batch, batch)
            block = mem[here, at, :].reshape(batch * batch, width)
            value = dot(swap[...], block).astype(BF16).reshape(batch, batch, width)
            obs_v[at, here, :] = value

        for j in range(low, high):
            one(j)
        if high == chunks:
            keep_og(part).start()

    def queries_back(i, _):
        rows = pl.ds(pl.multiple_of(i * ROWS, ROWS), ROWS)
        r.dquery[rows, :] = dot(r.dq_wide[rows, :], wkh[...]).astype(BF16)
        return 0

    lax.fori_loop(0, tokens // ROWS, queries_back, 0)
    put(SQ_AT[1], 2, dot(r.first[...], r.dquery[...], TN))
    if remote:
        update.start(6)
        update.one(5)

    def acts_back(i, _):
        rows = pl.ds(pl.multiple_of(i * ROWS, ROWS), ROWS)
        grad_first = dot(r.dquery[rows, :], sq[1], NT)
        hat = r.xhat[rows, :]
        gain_acc[0:1, :] += jnp.sum(grad_first * hat, 0, keepdims=True)
        r.ag_v[rows, :] = r.dres[rows, :] + norm_back(grad_first * g1, hat, r.rstd[rows, :])
        return 0

    def finish_acts():
        lax.fori_loop(0, tokens // ROWS, acts_back, 0)
        for norm in range(2):
            for j in range(2):
                row = gain_acc[norm : norm + 1, j * LANES : (j + 1) * LANES]
                at = GAIN_BASE + norm * 2 + j
                value = jnp.broadcast_to(row.reshape(1, 1, 1, 1, 1, LANES), GRID + (1, LANES))
                grads[:, :, :, :, at : at + 1, :] = value
        rest = WIRE - GAIN_BASE - 4
        grads[:, :, :, :, GAIN_BASE + 4 : WIRE, :] = jnp.zeros(GRID + (rest, LANES), F32)

    keep_ag = pltpu.make_async_copy(r.ag_v, r.ag, out_sems.at[1])
    if remote:
        pairs = samples // 2
        finish_acts()
        keep_ag.start()
        update.start(7)
        update.one(6)
        update.three(4)
        memory_back(0, pairs // 2)
        update.four(2, 3)
        update.two(5)
        update.one(7)
        update.two(6)
        memory_back(pairs // 2, pairs)
        update.four(0, 1)
        update.three(5)
        update.two(7)
        update.three(6)
        turn_back(0, 0, chunks // 2)
        update.orthogonalize()
        update.give_all()
        update.three(7)
        turn_back(0, chunks // 2, chunks)
        update.four(4, 5, 6)
        turn_back(1, 0, chunks)
        update.four(7)
        out = r.out
        out[1, :, :] = r.moment[...]
        out[2, pl.ds(GAIN_BASE, 16), :] = jnp.zeros((16, LANES), F32)
        gather.drain()
        update.drain()
        update.take_all()
        update.drain_owner()
    else:
        finish_acts()
        keep_ag.start()
        memory_back(0, samples // 2)
        for part in range(samples // batch):
            turn_back(part, 0, chunks)
    for copy in (keep_out, keep_ag, *(keep_og(part) for part in range(samples // batch))):
        copy.wait()


def block_and_back(remote, acts, obs, flags, levels, cot, sqw, mlpw, gain, sqm=None, mlpm=None):
    tokens, width = acts.shape
    keys, samples = obs.shape[0], obs.shape[1]
    rows = HEADS * ACT
    wide = mlpw.shape[2]
    any_space = pl.BlockSpec(memory_space=pl.ANY)
    in_vmem = pl.BlockSpec(memory_space=VMEM)
    sem = pltpu.SemaphoreType.DMA
    ins = dict(flags=flags, levels=levels, acts=acts, obs=obs, cot=cot, sqw=sqw, mlpw=mlpw, gain=gain)
    outs = dict(
        output=jax.ShapeDtypeStruct(acts.shape, F32),
        ag=jax.ShapeDtypeStruct(acts.shape, F32),
        og=jax.ShapeDtypeStruct(obs.shape, BF16),
    )
    grads = GRID + (WIRE, LANES)
    scratch = dict(
        obs_v=VMEM((KEYS_PAD, samples, width), BF16),
        acts_v=VMEM(acts.shape, F32),
        cot_v=VMEM(acts.shape, F32),
        mem=VMEM((samples, KEYS_PAD, width), BF16),
        swap=VMEM((256, 256), BF16),
        sq_all=VMEM((5, width, width), BF16),
        mlp_all=VMEM((2, width, wide), BF16),
        gain_all=VMEM((2, width), F32),
        wkh=VMEM((HEADS * width, width), BF16),
        wvh=VMEM((HEADS * width, width), BF16),
        first=VMEM((tokens, width), BF16),
        query=VMEM((tokens, width), BF16),
        xhat=VMEM((tokens, width), F32),
        rstd=VMEM((tokens, 1), F32),
        probs=VMEM((samples // 2, KEYS_PAD, LANES), F32),
        pairs=VMEM((samples // 2, KEYS_PAD, 2 * LANES), BF16),
        queries=VMEM((samples, rows, width), BF16),
        dmixes=VMEM((samples, rows, width), BF16),
        u=VMEM((tokens, HEADS * width), BF16),
        dq_wide=VMEM((tokens, HEADS * width), BF16),
        mixed=VMEM((tokens, width), BF16),
        second=VMEM((tokens, width), BF16),
        active=VMEM((tokens, wide), BF16),
        dhidden=VMEM((tokens, wide), BF16),
        out_low=VMEM((tokens, width), BF16),
        dres_low=VMEM((tokens, width), BF16),
        dres=VMEM((tokens, width), F32),
        resid=VMEM((tokens, width), F32),
        hat_two=VMEM((tokens, width), F32),
        rstd_two=VMEM((tokens, 1), F32),
        slope=VMEM((tokens, wide), F32),
        dmixed=VMEM((tokens, width), BF16),
        dquery=VMEM((tokens, width), BF16),
        out_v=VMEM((tokens, width), F32),
        ag_v=VMEM((tokens, width), F32),
        angle=VMEM((samples, width // 2), F32),
        embed=VMEM((samples, width), BF16),
        stamps=VMEM((samples, 8, width), F32),
        gain_acc=VMEM((8, width), F32),
        flags_s=pltpu.SMEM(flags.shape, jnp.int32),
        levels_s=pltpu.SMEM(levels.shape, jnp.int32),
        in_sems=sem((10,)),
        out_sems=sem((2 + samples // 16,)),
    )
    extra = {}
    if remote:
        ins.update(sqm=sqm, mlpm=mlpm)
        outs.update(out=jax.ShapeDtypeStruct((3, WIRE, LANES), F32))
        chunks = len(CHUNKS)
        scratch.update(
            grads=VMEM(grads, F32),
            sqw_v=VMEM(sqw.shape, F32),
            mlpw_v=VMEM(mlpw.shape, F32),
            gain_v=VMEM(gain.shape, F32),
            sqm_v=VMEM(sqm.shape, F32),
            mlpm_v=VMEM(mlpm.shape, F32),
            wire=VMEM(grads, BF16),
            edge=VMEM((16, LANES), F32),
            gsend=sem((len(PIECES), 6)),
            grecv=sem((len(PIECES), 6)),
            send0=VMEM((4, 2, 2, WIRE, LANES), BF16),
            got_core=VMEM((4, 2, 2, WIRE, LANES), BF16),
            sum1=VMEM((4, 2, 2, WIRE, LANES), F32),
            send1=VMEM((4, 2, WIRE, LANES), BF16),
            got1=VMEM((4, 2, WIRE, LANES), BF16),
            sum2=VMEM((4, 2, WIRE, LANES), F32),
            send2=VMEM((4, WIRE, LANES), BF16),
            got2=VMEM((4, WIRE, LANES), BF16),
            sum3=VMEM((4, WIRE, LANES), F32),
            send3=VMEM((4, WIRE, LANES), BF16),
            got3=VMEM((3, WIRE, LANES), BF16),
            moment=VMEM((WIRE, LANES), F32),
            slabs_sq=VMEM((4, 8, 4, SQ_ROWS, LANES), BF16),
            slabs_mlp=VMEM((32, MLP_ROWS, LANES), BF16),
            moment_low=VMEM((2 * MLP_ROWS, LANES), BF16),
            back_mlp=VMEM((2, MLP_ROWS, LANES), BF16),
            result_sq=VMEM((32, SQ_ROWS, LANES), F32),
            result_mlp=VMEM((32, MLP_ROWS, LANES), BF16),
            cur=VMEM((width, wide), F32),
            cur_low=VMEM((width, wide), BF16),
            send=sem((chunks, 6)),
            recv=sem((chunks, 6)),
            own_send=sem((len(PARTS_OUT),)),
            own_recv=sem((1,)),
            back_send=sem((32,)),
            back_recv=sem((7,)),
        )
        extra = dict(collective_id=0, has_side_effects=True)
        outs = {name: VMEM(like.shape, like.dtype) for name, like in outs.items()}
    else:
        outs.update(grads=jax.ShapeDtypeStruct(grads, F32))
    names = tuple(ins) + tuple(outs) + tuple(scratch)
    stay = [pltpu.with_memory_space_constraint(value, pltpu.HBM) for value in ins.values()]
    results = pl.pallas_call(
        functools.partial(block_kernel, names, remote),
        out_shape=tuple(outs.values()),
        in_specs=[any_space] * len(ins),
        out_specs=[any_space] * 3 + [in_vmem],
        scratch_shapes=list(scratch.values()),
        compiler_params=pltpu.CompilerParams(vmem_limit_bytes=52 << 20, **extra),
        name="block_and_back",
    )(*stay)
    return Refs(zip(outs, results))


PARTS = 7


def finish_kernel(names, rate, *args):
    r = Refs(zip(names, args))
    sems = r.sems
    keys = r.og.shape[0]
    step = keys // PARTS

    def leave(part):
        block = pl.ds(part * step, step)
        return pltpu.make_async_copy(r.og_v.at[block], r.og.at[block], sems.at[part])

    more = PARTS
    moves = []
    if hasattr(r, "wire"):
        pairs = [(r.sqw, r.sqw_v), (r.mlpw, r.mlpw_v), (r.gain, r.gain_v), (r.gainm, r.gainm_v)]
        pairs += [(r.output, r.output_f), (r.ag, r.ag_f)]
        for source, target in pairs:
            moves.append(pltpu.make_async_copy(source, target, sems.at[more]))
            moves[-1].start()
            more += 1
    for part in range(PARTS):

        def widen(j, _):
            r.og_v[j] = r.low[j].astype(F32)
            return 0

        lax.fori_loop(part * step, (part + 1) * step, widen, 0, unroll=4)
        leave(part).start()
    for copy in moves[:4]:
        copy.wait()
    if hasattr(r, "wire"):
        finish_weights(r, rate)
    for part in range(PARTS):
        leave(part).wait()
    for copy in moves[4:]:
        copy.wait()


def finish_weights(r, rate):
    wire = r.wire
    me = lax.axis_index("dp")
    for m in range(5):
        for j in range(2):
            rows, columns = pl.ds(SQ_AT[m] + j * TILE, TILE), pl.ds(j * LANES, LANES)
            r.sqg[m, :, columns] = wire[0, rows, :]
            r.sqm[m, :, columns] = wire[1, rows, :]
            r.sqn[m, :, columns] = r.sqw_v[m, :, columns] - SQ_RATES[m] * wire[2, rows, :]
    r.sqc[...] = r.sqn[...].astype(BF16)
    for m in range(2):
        for j in range(8):
            rows, columns = pl.ds(m * MLP_ROWS + j * TILE, TILE), pl.ds(j * LANES, LANES)
            r.mlpg[m, :, columns] = wire[0, rows, :]
            r.mlpm[m, :, columns] = wire[1, rows, :]
            r.mlpn[m, :, columns] = r.mlpw_v[m, :, columns] - MLP_RATES[m] * wire[2, rows, :]
    r.mlpc[...] = r.mlpn[...].astype(BF16)
    tile = wire[0, pl.ds(GAIN_BASE, TILE), :]
    turned = pltpu.roll(tile, (LANES - (me % 16) * TILE) % LANES, 1)
    at = me // 16
    for norm in range(2):
        pair = turned[2 * norm : 2 * norm + 2, 0:TILE]
        row = jnp.where(at == 0, pair[0:1, :], pair[1:2, :])
        new = 0.5 * r.gainm_v[norm : norm + 1, :] + row
        r.gg[norm : norm + 1, :] = row
        r.gm[norm : norm + 1, :] = new
        r.gn[norm : norm + 1, :] = r.gain_v[norm : norm + 1, :] - rate * new


def finish(rate, made, sqw=None, mlpw=None, gain=None, gainm=None):
    any_space = pl.BlockSpec(memory_space=pl.ANY)
    in_vmem = pl.BlockSpec(memory_space=VMEM)
    ins = dict(low=made.og)
    outs = dict(og=jax.ShapeDtypeStruct(made.og.shape, F32))
    near, far = 1, 1
    if hasattr(made, "out"):
        ins.update(output=made.output, ag=made.ag, wire=made.out, sqw=sqw, mlpw=mlpw, gain=gain, gainm=gainm)
        like = jax.ShapeDtypeStruct
        near, far = 4, 3
        outs.update(
            output_f=like(made.output.shape, F32),
            ag_f=like(made.ag.shape, F32),
            sqg=like(sqw.shape, F32),
            sqm=like(sqw.shape, F32),
            sqn=like(sqw.shape, F32),
            sqc=like(sqw.shape, BF16),
            mlpg=like(mlpw.shape, F32),
            mlpm=like(mlpw.shape, F32),
            mlpn=like(mlpw.shape, F32),
            mlpc=like(mlpw.shape, BF16),
            gg=like(gain.shape, F32),
            gm=like(gain.shape, F32),
            gn=like(gain.shape, F32),
        )
    scratch = dict(
        og_v=VMEM(made.og.shape, F32),
        sems=pltpu.SemaphoreType.DMA((PARTS + 6,)),
    )
    if hasattr(made, "out"):
        scratch.update(
            sqw_v=VMEM(sqw.shape, F32),
            mlpw_v=VMEM(mlpw.shape, F32),
            gain_v=VMEM(gain.shape, F32),
            gainm_v=VMEM(gainm.shape, F32),
        )
    names = tuple(ins) + tuple(outs) + tuple(scratch)
    made_here = list(ins.values())
    stay = [pltpu.with_memory_space_constraint(value, pltpu.HBM) for value in made_here[near:]]
    results = pl.pallas_call(
        functools.partial(finish_kernel, names, rate),
        out_shape=tuple(outs.values()),
        in_specs=[in_vmem] * near + [any_space] * (len(ins) - near),
        out_specs=[any_space] * far + [in_vmem] * (len(outs) - far),
        scratch_shapes=list(scratch.values()),
        compiler_params=pltpu.CompilerParams(vmem_limit_bytes=16 << 20),
        name="finish",
    )(*made_here[:near], *stay)
    return Refs(zip(outs, results))


HIGH_PRECISION = lax.Precision.HIGHEST


def plain_orthogonalize(matrix):
    current = matrix / (jnp.sqrt(jnp.sum(matrix * matrix)) + 1e-07)
    for turn in range(5):
        gram = jnp.dot(current, current.T, precision=HIGH_PRECISION)
        poly = COEF_B * gram + COEF_C * jnp.dot(gram, gram, precision=HIGH_PRECISION)
        current = COEF_A * current + jnp.dot(poly, current, precision=HIGH_PRECISION)
    return current


def pick_owned(stack, owners, device):
    chosen = jnp.zeros_like(stack[0])
    for index in range(len(owners)):
        chosen = jnp.where(device == owners[index], stack[index], chosen)
    return chosen


def is_owner(owners, device):
    flag = device < 0
    for owner in owners:
        flag = jnp.logical_or(flag, device == owner)
    return flag


def from_wire(grads):
    def matrix(base, tiles):
        part = grads[:, base : base + tiles * TILE, :].reshape(-1, tiles, TILE, LANES)
        return part.transpose(0, 2, 1, 3).reshape(-1, tiles * LANES)

    square = jnp.stack([matrix(SQ_AT[m], 2) for m in range(5)])
    mlp = jnp.stack([matrix(m * MLP_ROWS, 8) for m in range(2)])
    return square, mlp, grads[0, GAIN_BASE : GAIN_BASE + 4, :].reshape(2, 2 * LANES)


def update_by_collectives(
    grads, square_weights, mlp_weights, gains, square_moment, mlp_moment, gain_moment, rate
):
    square_local, mlp_local, gain_local = from_wire(grads)
    square_grad, mlp_grad, gain_grad = (
        lax.psum_scatter(square_local, "dp", scatter_dimension=1, tiled=True),
        lax.psum_scatter(mlp_local, "dp", scatter_dimension=1, tiled=True),
        lax.psum_scatter(gain_local, "dp", scatter_dimension=1, tiled=True),
    )
    square_moment_new = 0.5 * square_moment + square_grad
    mlp_moment_new = 0.5 * mlp_moment + mlp_grad
    gain_moment_new = 0.5 * gain_moment + gain_grad
    device = lax.axis_index("dp")
    count = lax.axis_size("dp")
    square_owners = [index * count // 7 for index in range(5)]
    mlp_owners = [(index + 5) * count // 7 for index in range(2)]
    square_full, mlp_full = (
        lax.all_gather(square_moment_new, "dp", axis=1, tiled=True),
        lax.all_gather(mlp_moment_new, "dp", axis=1, tiled=True),
    )
    mine_square = pick_owned(square_full, square_owners, device)
    mine_mlp = pick_owned(mlp_full, mlp_owners, device)
    made_square = lax.cond(
        is_owner(square_owners, device), plain_orthogonalize, jnp.zeros_like, mine_square
    )
    made_mlp = lax.cond(is_owner(mlp_owners, device), plain_orthogonalize, jnp.zeros_like, mine_mlp)
    stack_square = jnp.stack(
        [jnp.where(device == owner, made_square, 0.0) for owner in square_owners]
    )
    stack_mlp = jnp.stack([jnp.where(device == owner, made_mlp, 0.0) for owner in mlp_owners])
    square_ortho, mlp_ortho = (
        lax.psum_scatter(stack_square, "dp", scatter_dimension=1, tiled=True),
        lax.psum_scatter(stack_mlp, "dp", scatter_dimension=1, tiled=True),
    )
    square_new = square_weights - jnp.array(SQ_RATES, F32)[:, None, None] * square_ortho
    mlp_new = mlp_weights - jnp.array(MLP_RATES, F32)[:, None, None] * mlp_ortho
    gains_new = gains - rate * gain_moment_new
    return (
        square_grad,
        square_moment_new,
        square_new,
        square_new.astype(BF16),
        mlp_grad,
        mlp_moment_new,
        mlp_new,
        mlp_new.astype(BF16),
        gain_grad,
        gain_moment_new,
        gains_new,
    )


def per_device(
    actions,
    observed,
    camera_flags,
    noise_levels,
    cotangent,
    square_weights,
    mlp_weights,
    gains,
    square_moment,
    mlp_moment,
    gain_moment,
):
    count = lax.axis_size("dp")
    rate = 0.1 / math.sqrt(actions.shape[0] * count)
    by_key = observed.transpose(1, 0, 2)
    ins = (actions, by_key, camera_flags, noise_levels, cotangent)
    if count == math.prod(GRID):
        made = block_and_back(True, *ins, square_weights, mlp_weights, gains, square_moment, mlp_moment)
        done = finish(rate, made, square_weights, mlp_weights, gains, gain_moment)
        output, actions_grad = done.output_f, done.ag_f
        d = done
        rest = (d.sqg, d.sqm, d.sqn, d.sqc, d.mlpg, d.mlpm, d.mlpn, d.mlpc, d.gg, d.gm, d.gn)
    else:
        square_all, mlp_all = (
            lax.all_gather(square_weights.astype(BF16), "dp", axis=1, tiled=True),
            lax.all_gather(mlp_weights.astype(BF16), "dp", axis=1, tiled=True),
        )
        gain_all = lax.all_gather(gains, "dp", axis=1, tiled=True)
        made = block_and_back(False, *ins, square_all, mlp_all, gain_all)
        done = finish(rate, made)
        output, actions_grad = made.output, made.ag
        grads = made.grads.reshape(-1, WIRE, LANES)
        rest = update_by_collectives(
            grads, square_weights, mlp_weights, gains, square_moment, mlp_moment, gain_moment, rate
        )
    observed_grad = done.og.transpose(1, 0, 2)
    return (output, actions_grad, observed_grad) + tuple(rest)


def solution(mesh):
    rows, cube, flat = P("dp", None), P("dp", None, None), P("dp")
    stacked, pair = P(None, "dp", None), P(None, "dp")
    return jax.shard_map(
        per_device,
        mesh=mesh,
        in_specs=(rows, cube, flat, flat, rows, stacked, stacked, pair, stacked, stacked, pair),
        out_specs=(rows, rows, cube) + (stacked,) * 8 + (pair,) * 3,
        check_vma=False,
    )
```

```python
import functools
import math

import jax
import jax.numpy as jnp
from jax import lax
from jax.experimental import pallas as pl
from jax.experimental.pallas import tpu as pltpu
from jax.sharding import PartitionSpec as P

HEADS = 4
ACT = 16
OBS_FULL = 196
OBS_FEW = 49
COEF_A = 3.4445
COEF_B = -4.775
COEF_C = 2.0315
F32 = jnp.float32
BF16 = jnp.bfloat16
MESH = pl.DeviceIdType.MESH
VMEM = pltpu.VMEM
NN = (((1,), (0,)), ((), ()))
NT = (((1,), (1,)), ((), ()))
TN = (((0,), (0,)), ((), ()))

LANES = 128
TILE = 8
MLP_ROWS = 64
SQ_ROWS = 16
SQ_AT = (160, 192, 176, 128, 144)
GAIN_BASE = 208
WIRE = 224
PIECES = ((0, 32), (32, 32), (64, 32), (96, 32), (128, 32), (160, 32), (192, 32))
PIECE_X_FIRST = (True, False, True, False, True, True, False)
CHUNKS = ((0, 32), (32, 32), (64, 32), (96, 32), (128, 32), (160, 32), (192, 16), (208, 16))
X_FIRST = (True, False, True, False, True, False, True, False)
PARTS_OUT = (
    (0, 0, 0, 32, 0),
    (1, 0, 32, 32, 32),
    (2, 1, 64, 32, 0),
    (3, 1, 96, 32, 32),
    (4, 5, 128, 16, 0),
    (4, 6, 144, 16, 0),
    (5, 2, 160, 16, 0),
    (5, 4, 176, 16, 0),
    (6, 3, 192, 16, 0),
)
MLP_RATES = (1.0, 0.5)
SQ_RATES = (0.5, 0.5, 0.5, 0.5, 4.0)
GRID = (4, 2, 2, 2)
OWNERS = (8, 22, 14, 16, 11, 21, 13)
SHIFTS = (0.0, 0.0, 0.4, 0.8, 0.8)
KEYS_PAD = 208
GROUP = 16
ROWS = 512


class Refs:
    def __init__(self, pairs):
        self.__dict__.update(pairs)


def dot(left, right, dims=NN):
    return lax.dot_general(left, right, dims, preferred_element_type=F32)


def place():
    me = lax.axis_index("dp")
    return me, me // 8, (me // 4) % 2, (me // 2) % 2, me % 2


def device_at(z, y, x, c):
    return ((z * 2 + y) * 2 + x) * 2 + c


def link(src, dst, send, recv, device):
    return pltpu.make_async_remote_copy(
        src_ref=src,
        dst_ref=dst,
        send_sem=send,
        recv_sem=recv,
        device_id=(device,),
        device_id_type=MESH,
    )


def greet(device):
    pl.semaphore_signal(
        pltpu.get_barrier_semaphore(), inc=1, device_id=(device,), device_id_type=MESH
    )


def normalize(values):
    centred = values - jnp.mean(values, -1, keepdims=True)
    scale = lax.rsqrt(jnp.mean(centred * centred, -1, keepdims=True) + 1e-05)
    return centred * scale, scale


def norm_back(grad, hat, scale):
    mean_one = jnp.mean(grad, -1, keepdims=True)
    mean_two = jnp.mean(grad * hat, -1, keepdims=True)
    return scale * (grad - mean_one - hat * mean_two)


class Gather:
    def __init__(self, r):
        self.r = r
        self.me, self.z, self.y, self.x, self.c = place()

    def hop(self, k, step, part, device):
        return link(part, part, self.r.gsend.at[k, step], self.r.grecv.at[k, step], device)

    def along_z(self, k, step):
        part = self.r.wire.at[self.z, self.y, self.x, self.c, pl.ds(*PIECES[k])]
        return self.hop(k, step, part, device_at((self.z + step + 1) % 4, self.y, self.x, self.c))

    def from_z(self, k, step):
        there = (self.z + 3 - step) % 4
        part = self.r.wire.at[there, self.y, self.x, self.c, pl.ds(*PIECES[k])]
        return self.hop(k, step, part, device_at(there, self.y, self.x, self.c))

    def plane(self, k, second, mine):
        z, y, x, c = self.z, self.y, self.x, self.c
        rows, wire = pl.ds(*PIECES[k]), self.r.wire
        py, px = (y, x) if mine else (1 - y, 1 - x)
        along_x = PIECE_X_FIRST[k] == second
        if along_x:
            part = wire.at[:, y, px, c, rows] if second else wire.at[:, :, px, c, rows]
            return self.hop(k, 3 if second else 4, part, device_at(z, y, 1 - x, c))
        part = wire.at[:, py, x, c, rows] if second else wire.at[:, py, :, c, rows]
        return self.hop(k, 3 if second else 4, part, device_at(z, 1 - y, x, c))

    def core(self, k, mine):
        part = self.r.wire.at[:, :, :, self.c if mine else 1 - self.c, pl.ds(*PIECES[k])]
        return self.hop(k, 5, part, device_at(self.z, self.y, self.x, 1 - self.c))

    def first(self, *chunks):
        for k in chunks:
            for step in range(3):
                self.along_z(k, step).start()

    def second(self, *chunks):
        for k in chunks:
            for step in range(3):
                self.from_z(k, step).wait_recv()
            self.plane(k, True, True).start()

    def third(self, *chunks):
        for k in chunks:
            self.plane(k, True, False).wait_recv()
            self.plane(k, False, True).start()

    def fourth(self, *chunks):
        for k in chunks:
            self.plane(k, False, False).wait_recv()
            self.core(k, True).start()

    def last(self, *chunks):
        for k in chunks:
            self.core(k, False).wait_recv()

    def drain(self):
        for k in range(len(PIECES)):
            for step in range(3):
                self.along_z(k, step).wait_send()
            self.plane(k, True, True).wait_send()
            self.plane(k, False, True).wait_send()
            self.core(k, True).wait_send()

    def fill(self):
        r = self.r
        spot = (self.z, self.y, self.x, self.c)

        def tiles(source, m, base, number):
            for j in range(number):
                pair = [source[m, :, pl.ds((2 * j + k) * LANES, LANES)] for k in range(2)]
                r.wire[spot + (pl.ds(base + j * 16, 16),)] = jnp.concatenate(pair, axis=0).astype(BF16)

        for m in range(5):
            tiles(r.sqw_v, m, SQ_AT[m], 1)
        for m in range(2):
            tiles(r.mlpw_v, m, m * MLP_ROWS, 4)
        gains, edge = r.gain_v[...], r.edge
        high = gains.astype(BF16).astype(F32)
        middle = (gains - high).astype(BF16).astype(F32)
        edge[...] = jnp.zeros_like(edge)
        edge[0:2, 0:TILE] = high
        edge[2:4, 0:TILE] = middle
        edge[4:6, 0:TILE] = (gains - high - middle).astype(BF16).astype(F32)
        r.wire[spot + (pl.ds(GAIN_BASE, 16),)] = edge[...].astype(BF16)

    def unpack(self, base, number, out, m):
        for j in range(number):
            block = self.r.wire[:, :, :, :, pl.ds(base + j * 16, 16), :].reshape(32, 16, LANES).astype(F32)
            for half in range(2):
                columns = pl.ds((2 * j + half) * LANES, LANES)
                out[m, :, columns] = block[:, half * 8 : half * 8 + 8, :].reshape(256, LANES).astype(BF16)

    def unpack_gains(self):
        edge, wire = self.r.edge, self.r.wire
        for half in range(2):
            total = jnp.zeros((16, LANES), F32)
            for at in range(16):
                d = half * 16 + at
                tile = wire[d // 8, (d // 4) % 2, (d // 2) % 2, d % 2, pl.ds(GAIN_BASE, 16), :].astype(F32)
                total = total + (tile if at == 0 else pltpu.roll(tile, at * TILE, 1))
            edge[...] = total
            self.r.gain_all[:, pl.ds(half * LANES, LANES)] = edge[0:2, :] + edge[2:4, :] + edge[4:6, :]


class Update:
    def __init__(self, r):
        self.r = r
        self.me, self.z, self.y, self.x, self.c = place()

    def hop(self, k, step, src, dst, device):
        return link(src, dst, self.r.send.at[k, step], self.r.recv.at[k, step], device)

    def core(self, k):
        rows = pl.ds(*CHUNKS[k])
        src, dst = self.r.send0.at[:, :, :, rows], self.r.got_core.at[:, :, :, rows]
        return self.hop(k, 0, src, dst, device_at(self.z, self.y, self.x, 1 - self.c))

    def plane(self, k, first):
        rows = pl.ds(*CHUNKS[k])
        to = (self.z, self.y, 1 - self.x, self.c) if X_FIRST[k] == first else (self.z, 1 - self.y, self.x, self.c)
        if first:
            src, dst = self.r.send1.at[:, :, rows], self.r.got1.at[:, :, rows]
        else:
            src, dst = self.r.send2.at[:, rows], self.r.got2.at[:, rows]
        return self.hop(k, 1 if first else 2, src, dst, device_at(*to))

    def along_z(self, k, step):
        rows = pl.ds(*CHUNKS[k])
        there = (self.z + step + 1) % 4
        src, dst = self.r.send3.at[there, rows], self.r.got3.at[step, rows]
        return self.hop(k, 3 + step, src, dst, device_at(there, self.y, self.x, self.c))

    def start(self, k):
        rows = pl.ds(*CHUNKS[k])
        self.r.send0[:, :, :, rows, :] = self.r.grads[:, :, :, 1 - self.c, rows, :].astype(BF16)
        self.core(k).start()

    def one(self, *chunks):
        r = self.r
        for k in chunks:
            rows = pl.ds(*CHUNKS[k])
            self.core(k).wait_recv()
            sum1 = r.sum1
            sum1[:, :, :, rows, :] = r.grads[:, :, :, self.c, rows, :] + r.got_core[:, :, :, rows, :].astype(F32)
            other = sum1[:, :, 1 - self.x, rows, :] if X_FIRST[k] else sum1[:, 1 - self.y, :, rows, :]
            r.send1[:, :, rows, :] = other.astype(BF16)
            self.plane(k, True).start()

    def two(self, *chunks):
        r = self.r
        for k in chunks:
            rows = pl.ds(*CHUNKS[k])
            self.plane(k, True).wait_recv()
            sum1, sum2 = r.sum1, r.sum2
            mine = sum1[:, :, self.x, rows, :] if X_FIRST[k] else sum1[:, self.y, :, rows, :]
            sum2[:, :, rows, :] = mine + r.got1[:, :, rows, :].astype(F32)
            other = 1 - self.y if X_FIRST[k] else 1 - self.x
            r.send2[:, rows, :] = sum2[:, other, rows, :].astype(BF16)
            self.plane(k, False).start()

    def three(self, *chunks):
        r = self.r
        for k in chunks:
            rows = pl.ds(*CHUNKS[k])
            self.plane(k, False).wait_recv()
            mine = self.y if X_FIRST[k] else self.x
            total = r.sum2[:, mine, rows, :] + r.got2[:, rows, :].astype(F32)
            r.sum3[:, rows, :] = total
            r.send3[:, rows, :] = total.astype(BF16)
            if k >= 4:
                own = r.sum3[self.z, rows, :] + 0.5 * r.moment[rows, :]
                r.send3[self.z, rows, :] = own.astype(BF16)
                self.parts_to_owners(k)
            for step in range(3):
                self.along_z(k, step).start()

    def parts_to_owners(self, k):
        for part, (chunk, index, *_) in enumerate(PARTS_OUT):
            if chunk != k:
                continue

            @pl.when(self.me != OWNERS[index])
            def _():
                self.to_owner(part).start()

            @pl.when(self.me == OWNERS[index])
            def _():
                src, dst = self.own_part(part)
                pltpu.make_async_copy(src, dst, self.r.own_recv.at[0]).start()

    def result(self, index):
        return self.r.result_mlp if index < 2 else self.r.result_sq

    def own_part(self, part):
        _, index, base, number, place = PARTS_OUT[part]
        if index < 2:
            return self.r.moment_low.at[pl.ds(base, number)], self.r.slabs_mlp.at[self.me, pl.ds(place, number)]
        return self.r.send3.at[:, pl.ds(base, number)], self.r.slabs_sq.at[self.z, self.me % 8]

    def to_owner(self, part):
        src, dst = self.own_part(part)
        return link(src, dst, self.r.own_send.at[part], self.r.own_recv.at[0], OWNERS[PARTS_OUT[part][1]])

    def four(self, *chunks):
        r = self.r
        moment, out = r.moment, r.out
        for k in chunks:
            rows = pl.ds(*CHUNKS[k])
            total = r.sum3[self.z, rows, :]
            for step in range(3):
                self.along_z(k, step).wait_recv()
                total = total + r.got3[step, rows, :].astype(F32)
            out[0, rows, :] = total
            new = 0.5 * moment[rows, :] + total
            moment[rows, :] = new
            if k < 4:
                r.moment_low[rows, :] = new.astype(BF16)
            if k < 4:
                self.parts_to_owners(k)

    def old_moment(self):
        r = self.r
        moment = r.moment
        for m in range(2):
            for j in range(8):
                moment[pl.ds(m * MLP_ROWS + j * TILE, TILE), :] = r.mlpm_v[m, :, pl.ds(j * LANES, LANES)]
        for m in range(5):
            for j in range(2):
                moment[pl.ds(SQ_AT[m] + j * TILE, TILE), :] = r.sqm_v[m, :, pl.ds(j * LANES, LANES)]
        moment[pl.ds(GAIN_BASE, 16), :] = jnp.zeros((16, LANES), F32)

    def orthogonalize(self):
        r = self.r
        cur = r.cur
        rows = lax.broadcasted_iota(jnp.int32, (256, 256), 0)
        diagonal = rows == lax.broadcasted_iota(jnp.int32, (256, 256), 1)

        low = r.cur_low

        def load(rows, j, pair):
            for side in range(2):
                columns = pl.ds((2 * j + side) * LANES, LANES)
                part = pair[:, side * TILE : (side + 1) * TILE, :].reshape(-1, LANES)
                cur[rows, columns] = part
                low[rows, columns] = part.astype(BF16)

        def load_mlp():
            for j in range(4):
                load(pl.ds(0, 256), j, r.slabs_mlp[:, pl.ds(j * 16, 16), :].astype(F32))

        def load_sq():
            for to in range(4):
                pair = r.slabs_sq[0, :, to].astype(F32)
                for plane in range(1, 4):
                    pair = pair + r.slabs_sq[plane, :, to].astype(F32)
                load(pl.ds(to * 64, 64), 0, pair)

        def run(slabs, fetch, result, tiles):
            pltpu.make_async_copy(slabs, slabs, r.own_recv.at[0]).wait()
            fetch()
            scale = 1.0
            for turn, shift in enumerate(SHIFTS):
                whole = low[:, 0 : tiles * LANES]
                off = dot(whole, whole, NT)
                if turn == 0:
                    norm = jnp.sum(jnp.sum(jnp.where(diagonal, off, 0.0), axis=0, keepdims=True), axis=1, keepdims=True)
                    scale = 1.0 / (jnp.sqrt(norm) + 1e-07)
                    off = off * (scale * scale)
                if shift:
                    off = off - jnp.where(diagonal, shift, 0.0)
                off_low = off.astype(BF16)
                poly = (COEF_B + 2.0 * COEF_C * shift) * off + COEF_C * dot(off_low, off_low)
                poly = poly.astype(BF16)
                keep = COEF_A + shift * (COEF_B + COEF_C * shift)
                for j in range(tiles // 2):
                    columns = pl.ds(j * 2 * LANES, 2 * LANES)
                    now = keep * cur[:, columns] + dot(poly, low[:, columns])
                    if turn == 0:
                        now = now * scale
                    if turn < len(SHIFTS) - 1:
                        cur[:, columns] = now
                        low[:, columns] = now.astype(BF16)
                    else:
                        parts = [now[:, side * LANES : (side + 1) * LANES].reshape(32, TILE, LANES) for side in range(2)]
                        result[:, pl.ds(j * 16, 16), :] = jnp.concatenate(parts, axis=1).astype(result.dtype)

        mine_mlp = jnp.logical_or(self.me == OWNERS[0], self.me == OWNERS[1])
        mine_sq = self.me < 0
        for device in OWNERS[2:]:
            mine_sq = jnp.logical_or(mine_sq, self.me == device)

        @pl.when(mine_mlp)
        def _():
            run(r.slabs_mlp, load_mlp, r.result_mlp, 8)

        @pl.when(mine_sq)
        def _():
            run(r.slabs_sq, load_sq, r.result_sq, 2)

    def landing(self, index):
        if index < 2:
            return self.r.back_mlp.at[index]
        return self.r.back_sq.at[index - 2]

    def give_back(self, index, device):
        result = self.result(index)
        return link(
            result.at[device], self.landing(index),
            self.r.back_send.at[device], self.r.back_recv.at[index], device,
        )

    def give_all(self):
        r = self.r
        for index in range(7):
            result = self.result(index)

            @pl.when(self.me == OWNERS[index])
            def _():
                def send_one(step, _):
                    self.give_back(index, step + (step + 32 - self.me) // 32).start()
                    return 0

                lax.fori_loop(0, 31, send_one, 0)
                pltpu.make_async_copy(result.at[self.me], self.landing(index), r.back_recv.at[index]).start()

    def take_all(self):
        for index in range(7):
            result = self.result(index)
            pltpu.make_async_copy(result.at[0], self.landing(index), self.r.back_recv.at[index]).wait()
        for index in range(2):
            rows = pl.ds(index * MLP_ROWS, MLP_ROWS)
            self.r.out[2, rows, :] = self.r.back_mlp[index].astype(F32)
        for index in range(5):
            self.r.out[2, pl.ds(SQ_AT[index], SQ_ROWS), :] = self.r.back_sq[index].astype(F32)

    def drain(self):
        for k in range(len(CHUNKS)):
            self.core(k).wait_send()
            self.plane(k, True).wait_send()
            self.plane(k, False).wait_send()
            for step in range(3):
                self.along_z(k, step).wait_send()
        for part in range(len(PARTS_OUT)):

            @pl.when(self.me != OWNERS[PARTS_OUT[part][1]])
            def _():
                self.to_owner(part).wait_send()

    def drain_owner(self):
        for index in range(7):

            @pl.when(self.me == OWNERS[index])
            def _():
                def wait_one(step, _):
                    self.give_back(index, step + (step + 32 - self.me) // 32).wait_send()
                    return 0

                lax.fori_loop(0, 31, wait_one, 0)


def greet_all():
    me, z, y, x, c = place()
    greet(device_at(z, y, x, 1 - c))
    greet(device_at(z, y, 1 - x, c))
    greet(device_at(z, 1 - y, x, c))
    for step in range(1, 4):
        greet(device_at((z + step) % 4, y, x, c))
    owner = me < 0
    for device in OWNERS:
        owner = jnp.logical_or(owner, me == device)

        @pl.when(me != device)
        def _():
            greet(device)

    @pl.when(owner)
    def _():
        def greet_other(step, _):
            greet((me + step) % 32)
            return 0

        lax.fori_loop(1, 32, greet_other, 0)

    is_owner = owner.astype(jnp.int32)
    return 6 + 7 - is_owner + 31 * is_owner


def block_kernel(names, remote, *args):
    r = Refs(zip(names, args))
    keys, samples = r.obs.shape[0], r.obs.shape[1]
    tokens, width = r.acts.shape
    head_dim, half, per = width // HEADS, width // 2, ROWS // ACT
    wide = r.mlp_all.shape[2]
    groups = samples // GROUP
    in_sems, out_sems = r.in_sems, r.out_sems

    if remote:
        own = (r.sqw_v, r.mlpw_v, r.gain_v)
    else:
        own = (r.sq_all, r.mlp_all, r.gain_all)
    loads = list(zip((r.sqw, r.mlpw, r.gain), own))
    loads += [(r.acts, r.acts_v), (r.obs, r.obs_v.at[pl.ds(0, keys)]), (r.cot, r.cot_v)]
    if remote:
        loads += [(r.sqm, r.sqm_v), (r.mlpm, r.mlpm_v)]
    loads += [(r.flags, r.flags_s), (r.levels, r.levels_s)]
    copies = [pltpu.make_async_copy(a, b, in_sems.at[i]) for i, (a, b) in enumerate(loads)]

    def arrive(*which):
        for i in which:
            copies[i].wait()

    for copy in copies:
        copy.start()
    if remote:
        gather, update = Gather(r), Update(r)
        expected = greet_all()
        arrive(0, 1, 2)
        gather.fill()
        pl.semaphore_wait(pltpu.get_barrier_semaphore(), expected)
        gather.first(5, 6, 4, 0, 1, 2, 3)

    arrive(3)

    def hats(i, _):
        rows = pl.ds(pl.multiple_of(i * ROWS, ROWS), ROWS)
        hat, scale = normalize(r.acts_v[rows, :])
        r.xhat[rows, :] = hat
        r.rstd[rows, :] = scale
        return 0

    lax.fori_loop(0, tokens // ROWS, hats, 0)

    mem, obs_v = r.mem, r.obs_v
    batch = 16
    chunks = KEYS_PAD // batch
    swap = r.swap
    row = lax.broadcasted_iota(jnp.int32, swap.shape, 0)
    column = lax.broadcasted_iota(jnp.int32, swap.shape, 1)
    swap[...] = jnp.where(column == (row % batch) * batch + row // batch, 1.0, 0.0).astype(BF16)

    def turn(part, low, high):
        def one(j, _):
            at = pl.ds(pl.multiple_of(j * batch, batch), batch)
            here = pl.ds(part * batch, batch)
            block = obs_v[at, here, :].reshape(batch * batch, width)
            mem[here, at, :] = dot(swap[...], block).astype(BF16).reshape(batch, batch, width)
            return 0

        lax.fori_loop(low, high, one, 0, unroll=high - low)

    whole = chunks - 1
    arrive(4)
    turn(0, 0, whole // 2)
    if remote:
        gather.second(5, 6)
    turn(0, whole // 2, whole)
    if remote:
        gather.third(5, 6)
    turn(1, 0, whole // 2)
    if remote:
        gather.second(4, 0, 1)
        gather.fourth(5, 6)
    turn(1, whole // 2, whole)
    if remote:
        gather.second(2, 3)
    arrive(len(copies) - 1, len(copies) - 2)
    freqs = jnp.exp(
        lax.broadcasted_iota(jnp.int32, (1, half), 1).astype(F32) * F32(-math.log(10000.0)) / half
    )
    for s in range(samples):
        r.angle[s : s + 1, :] = r.levels_s[s].astype(F32) * freqs
    r.embed[:, 0:half] = jnp.sin(r.angle[...]).astype(BF16)
    r.embed[:, half:width] = jnp.cos(r.angle[...]).astype(BF16)
    if remote:
        arrive(6, 7)
        update.old_moment()
        gather.third(4, 0, 1)
        gather.last(5, 6)
        for m in range(3):
            gather.unpack(SQ_AT[m], 1, r.sq_all, m)
        gather.unpack_gains()
    else:
        arrive(0, 1, 2)

    sq, mlp = r.sq_all, r.mlp_all
    wkh, wvh = r.wkh, r.wvh
    lane = lax.broadcasted_iota(jnp.int32, (width, width), 1)

    def split_heads(out, weight):
        weight = weight.astype(F32)
        for h in range(HEADS):
            out[pl.ds(h * width, width), :] = jnp.where(lane // head_dim == h, weight, 0.0).astype(BF16)

    split_heads(wkh, sq[2])
    g1, g2 = r.gain_all[0:1, :], r.gain_all[1:2, :]

    obs_v[keys] = dot(r.embed[...], sq[0]).astype(BF16)
    obs_v[keys + 1 :] = jnp.zeros((KEYS_PAD - keys - 1, samples, width), BF16)
    for part in range(samples // batch):
        turn(part, whole, chunks)

    queries, dmixes = r.queries, r.dmixes

    def make_queries(i, _):
        rows = pl.ds(pl.multiple_of(i * ROWS, ROWS), ROWS)
        first = (r.xhat[rows, :] * g1).astype(BF16)
        r.first[rows, :] = first
        q = dot(first, sq[1]).astype(BF16)
        r.query[rows, :] = q
        here = pl.ds(i * per, per)
        for h in range(HEADS):
            wk = wkh[pl.ds(h * width, width), :]
            value = (dot(q, wk, NT) * 0.125).astype(BF16).reshape(per, ACT, width)
            queries[here, pl.ds(h * ACT, ACT), :] = value
        return 0

    lax.fori_loop(0, tokens // ROWS, make_queries, 0)

    key = lax.broadcasted_iota(jnp.int32, (KEYS_PAD, LANES), 0)
    rows_each = HEADS * ACT
    left = lax.broadcasted_iota(jnp.int32, (KEYS_PAD, LANES), 1) < rows_each
    left_row = lax.broadcasted_iota(jnp.int32, (1, LANES), 1) < rows_each
    rest = jnp.where((key >= OBS_FEW) & (key < OBS_FULL), 1.0, 0.0)
    padding = jnp.where(key > OBS_FULL, -1000000000.0, 0.0)

    def with_memory(s, sides):
        here = pl.ds(s, 4)
        wide = dot(mem[here].reshape(4 * KEYS_PAD, width), sides[here].reshape(4 * rows_each, width), NT)
        part = [wide[k * KEYS_PAD : (k + 1) * KEYS_PAD, (k // 2) * LANES : (k // 2 + 1) * LANES] for k in range(4)]
        return jnp.where(left, part[0], part[1]), jnp.where(left, part[2], part[3])

    def each_head(out, s, value):
        rows = pl.ds(pl.multiple_of(s * ACT, ACT), ACT)
        for h in range(HEADS):
            out[rows, pl.ds(h * width, width)] = value[h * ACT : (h + 1) * ACT, :]

    def attend(g, _):
        pairs = []
        for quad in range(GROUP // 4):
            pairs.extend(with_memory(g * GROUP + 4 * quad, queries))
        turned = []
        for k, score in enumerate(pairs):
            s = g * GROUP + 2 * k
            drop = [(1 - r.flags_s[s + side]).astype(F32) * -1000000000.0 for side in range(2)]
            score = score + (rest * jnp.where(left_row, drop[0], drop[1]) + padding)
            expo = jnp.exp(score - jnp.max(score, 0, keepdims=True))
            probs = expo * (1.0 / jnp.sum(expo, 0, keepdims=True))
            r.probs[g * (GROUP // 2) + k] = probs
            turned.append(probs.astype(BF16).T)
        for k, low in enumerate(turned):
            for side in range(2):
                s = g * GROUP + 2 * k + side
                each_head(r.u, s, dot(low[side * rows_each : (side + 1) * rows_each], mem[s]).astype(BF16))
        return 0

    lax.fori_loop(0, groups // 2, attend, 0)
    if remote:
        gather.third(2, 3)
        gather.fourth(4, 0, 1)
    lax.fori_loop(groups // 2, groups, attend, 0)
    if remote:
        gather.fourth(2, 3)
        gather.last(4)
        for m in range(3, 5):
            gather.unpack(SQ_AT[m], 1, sq, m)
    split_heads(wvh, sq[3])

    gain_acc = r.gain_acc
    gain_acc[...] = jnp.zeros_like(gain_acc)
    blocks = [pl.ds(i * ROWS, ROWS) for i in range(tokens // ROWS)]
    for rows in blocks:
        mixed = dot(r.u[rows, :], wvh[...]).astype(BF16)
        r.mixed[rows, :] = mixed
        resid = r.acts_v[rows, :] + dot(mixed, sq[4])
        r.resid[rows, :] = resid
        hat, scale = normalize(resid)
        r.hat_two[rows, :] = hat
        r.rstd_two[rows, :] = scale
        r.second[rows, :] = (hat * g2).astype(BF16)
    arrive(5)
    r.out_low[...] = r.cot_v[...].astype(BF16)
    if remote:
        gather.last(0, 1)
        gather.unpack(0, 4, mlp, 0)
    wide_blocks = [pl.ds(c * 256, 256) for c in range(wide // 256)]
    for rows in blocks:
        for columns in wide_blocks:
            v = dot(r.second[rows, :], mlp[0, :, columns])
            square = v * v
            t = jnp.tanh(0.7978845608 * (v + 0.044715 * square * v))
            r.active[rows, columns] = (0.5 * v * (1.0 + t)).astype(BF16)
            slope = 0.5 * (1.0 + t) + 0.5 * v * (1.0 - t * t) * (0.7978845608 * (1.0 + 0.134145 * square))
            r.slope[rows, columns] = slope

    grads = r.grads

    def put(base, tiles, value):
        for j in range(tiles):
            part = value[:, j * LANES : (j + 1) * LANES].reshape(GRID + (TILE, LANES))
            grads[:, :, :, :, pl.ds(base + j * TILE, TILE), :] = part

    def by_head(left, right):
        turned = left.T
        parts = [
            dot(turned[h * head_dim : (h + 1) * head_dim, :], right[:, pl.ds(h * width, width)])
            for h in range(HEADS)
        ]
        return jnp.concatenate(parts, axis=0).T

    put(MLP_ROWS, 8, dot(r.out_low[...], r.active[...], TN))
    if remote:
        update.start(2)
        update.start(3)
        gather.last(2, 3)
        gather.unpack(MLP_ROWS, 4, mlp, 1)
    for rows in blocks:
        for columns in wide_blocks:
            slope = r.slope[rows, columns]
            r.dhidden[rows, columns] = (slope * dot(r.out_low[rows, :], mlp[1, :, columns])).astype(BF16)
    put(0, 8, dot(r.second[...], r.dhidden[...], TN))
    if remote:
        update.start(0)
        update.start(1)
        update.one(2, 3)
    for i, rows in enumerate(blocks):
        r.out_v[rows, :] = r.resid[rows, :] + dot(r.active[rows, :], mlp[1], NT)
        grad_second = dot(r.dhidden[rows, :], mlp[0], NT)
        hat = r.hat_two[rows, :]
        gain_acc[1:2, :] += jnp.sum(grad_second * hat, 0, keepdims=True)
        dres = r.cot_v[rows, :] + norm_back(grad_second * g2, hat, r.rstd_two[rows, :])
        r.dres[rows, :] = dres
        low = dres.astype(BF16)
        r.dres_low[rows, :] = low
        gm = dot(low, sq[4], NT).astype(BF16)
        r.dmixed[rows, :] = gm
        here = pl.ds(i * per, per)
        for h in range(HEADS):
            wv = wvh[pl.ds(h * width, width), :]
            dmixes[here, pl.ds(h * ACT, ACT), :] = dot(gm, wv, NT).astype(BF16).reshape(per, ACT, width)
    keep_out = pltpu.make_async_copy(r.out_v, r.output, out_sems.at[0])
    keep_out.start()
    if remote:
        update.one(0, 1)
    put(SQ_AT[4], 2, dot(r.mixed[...], r.dres_low[...], TN))
    put(SQ_AT[3], 2, by_head(r.dmixed[...], r.u))
    if remote:
        update.start(4)

    left_low = jnp.where(left_row, 1.0, 0.0).astype(BF16)
    right_low = jnp.where(left_row, 0.0, 1.0).astype(BF16)
    left_two = jnp.concatenate([left_low, left_low], axis=1)
    right_two = jnp.concatenate([right_low, right_low], axis=1)

    def pair_sides(s):
        here = pl.ds(s, 2)
        return jnp.concatenate([x[here].reshape(2 * rows_each, width) for x in (dmixes, queries)], axis=0)

    def attend_back(g, _):
        pairs = []
        for quad in range(GROUP // 4):
            pairs.extend(with_memory(g * GROUP + 4 * quad, dmixes))
        lows = []
        for k, rise in enumerate(pairs):
            probs = r.probs[g * (GROUP // 2) + k]
            both = probs * rise
            dscore = (both - probs * jnp.sum(both, 0, keepdims=True)).astype(BF16)
            lows.append((probs.astype(BF16), dscore, dscore.T))
        for k, (low, dscore, turned) in enumerate(lows):
            s = g * GROUP + 2 * k
            for side in range(2):
                dq = dot(turned[side * rows_each : (side + 1) * rows_each], mem[s + side]) * 0.125
                each_head(r.dq_wide, s + side, dq.astype(BF16))
            both = jnp.concatenate([low, dscore], axis=1)
            r.pairs[g * (GROUP // 2) + k] = both
            end = both[192:KEYS_PAD]
            last = dot(jnp.concatenate([end * left_two, end * right_two], axis=0), pair_sides(s))
            for side in range(2):
                r.stamps[s + side] = last[side * 16 : side * 16 + 8, :]
        return 0

    lax.fori_loop(0, groups // 2, attend_back, 0)
    if remote:
        update.two(2, 3)
        update.one(4)
        update.two(0, 1)
    lax.fori_loop(groups // 2, groups, attend_back, 0)
    if remote:
        update.three(2, 3)
        update.two(4)
    put(SQ_AT[2], 2, by_head(r.query[...], r.dq_wide))
    stamp_low = r.stamps[:, 4:5, :].reshape(samples, width).astype(BF16)
    put(SQ_AT[0], 2, dot(r.embed[...], stamp_low, TN))
    if remote:
        update.start(5)
        update.three(0, 1)

    def memory_back(low, high):
        for p in range(low, high):
            both = r.pairs[p]
            dmem = dot(jnp.concatenate([both * left_two, both * right_two], axis=0), pair_sides(2 * p))
            for side in range(2):
                mem[2 * p + side] = dmem[side * KEYS_PAD : (side + 1) * KEYS_PAD, :].astype(BF16)

    def keep_og(part):
        here = pl.ds(part * batch, batch)
        return pltpu.make_async_copy(obs_v.at[pl.ds(0, keys), here], r.og.at[:, here], out_sems.at[2 + part])

    def turn_back(part, low, high):
        def one(j):
            at = pl.ds(pl.multiple_of(j * batch, batch), batch)
            here = pl.ds(part * batch, batch)
            block = mem[here, at, :].reshape(batch * batch, width)
            value = dot(swap[...], block).astype(BF16).reshape(batch, batch, width)
            obs_v[at, here, :] = value

        for j in range(low, high):
            one(j)
        if high == chunks:
            keep_og(part).start()

    def queries_back(i, _):
        rows = pl.ds(pl.multiple_of(i * ROWS, ROWS), ROWS)
        r.dquery[rows, :] = dot(r.dq_wide[rows, :], wkh[...]).astype(BF16)
        return 0

    lax.fori_loop(0, tokens // ROWS, queries_back, 0)
    put(SQ_AT[1], 2, dot(r.first[...], r.dquery[...], TN))
    if remote:
        update.start(6)
        update.one(5)

    def acts_back(i, _):
        rows = pl.ds(pl.multiple_of(i * ROWS, ROWS), ROWS)
        grad_first = dot(r.dquery[rows, :], sq[1], NT)
        hat = r.xhat[rows, :]
        gain_acc[0:1, :] += jnp.sum(grad_first * hat, 0, keepdims=True)
        r.ag_v[rows, :] = r.dres[rows, :] + norm_back(grad_first * g1, hat, r.rstd[rows, :])
        return 0

    def finish_acts():
        lax.fori_loop(0, tokens // ROWS, acts_back, 0)
        for norm in range(2):
            for j in range(2):
                row = gain_acc[norm : norm + 1, j * LANES : (j + 1) * LANES]
                at = GAIN_BASE + norm * 2 + j
                value = jnp.broadcast_to(row.reshape(1, 1, 1, 1, 1, LANES), GRID + (1, LANES))
                grads[:, :, :, :, at : at + 1, :] = value
        rest = WIRE - GAIN_BASE - 4
        grads[:, :, :, :, GAIN_BASE + 4 : WIRE, :] = jnp.zeros(GRID + (rest, LANES), F32)

    keep_ag = pltpu.make_async_copy(r.ag_v, r.ag, out_sems.at[1])
    if remote:
        pairs = samples // 2
        finish_acts()
        keep_ag.start()
        update.start(7)
        update.one(6)
        update.three(4)
        memory_back(0, pairs // 2)
        update.four(2, 3)
        update.two(5)
        update.one(7)
        update.two(6)
        memory_back(pairs // 2, pairs)
        update.four(0, 1)
        update.three(5)
        update.two(7)
        update.three(6)
        turn_back(0, 0, chunks // 2)
        update.orthogonalize()
        update.give_all()
        update.three(7)
        turn_back(0, chunks // 2, chunks)
        update.four(4, 5, 6)
        turn_back(1, 0, chunks)
        update.four(7)
        out = r.out
        out[1, :, :] = r.moment[...]
        out[2, pl.ds(GAIN_BASE, 16), :] = jnp.zeros((16, LANES), F32)
        gather.drain()
        update.drain()
        update.take_all()
        update.drain_owner()
    else:
        finish_acts()
        keep_ag.start()
        memory_back(0, samples // 2)
        for part in range(samples // batch):
            turn_back(part, 0, chunks)
    for copy in (keep_out, keep_ag, *(keep_og(part) for part in range(samples // batch))):
        copy.wait()


def block_and_back(remote, acts, obs, flags, levels, cot, sqw, mlpw, gain, sqm=None, mlpm=None):
    tokens, width = acts.shape
    keys, samples = obs.shape[0], obs.shape[1]
    rows = HEADS * ACT
    wide = mlpw.shape[2]
    any_space = pl.BlockSpec(memory_space=pl.ANY)
    in_vmem = pl.BlockSpec(memory_space=VMEM)
    sem = pltpu.SemaphoreType.DMA
    ins = dict(flags=flags, levels=levels, acts=acts, obs=obs, cot=cot, sqw=sqw, mlpw=mlpw, gain=gain)
    outs = dict(
        output=jax.ShapeDtypeStruct(acts.shape, F32),
        ag=jax.ShapeDtypeStruct(acts.shape, F32),
        og=jax.ShapeDtypeStruct(obs.shape, BF16),
    )
    grads = GRID + (WIRE, LANES)
    scratch = dict(
        obs_v=VMEM((KEYS_PAD, samples, width), BF16),
        acts_v=VMEM(acts.shape, F32),
        cot_v=VMEM(acts.shape, F32),
        mem=VMEM((samples, KEYS_PAD, width), BF16),
        swap=VMEM((256, 256), BF16),
        sq_all=VMEM((5, width, width), BF16),
        mlp_all=VMEM((2, width, wide), BF16),
        gain_all=VMEM((2, width), F32),
        wkh=VMEM((HEADS * width, width), BF16),
        wvh=VMEM((HEADS * width, width), BF16),
        first=VMEM((tokens, width), BF16),
        query=VMEM((tokens, width), BF16),
        xhat=VMEM((tokens, width), F32),
        rstd=VMEM((tokens, 1), F32),
        probs=VMEM((samples // 2, KEYS_PAD, LANES), F32),
        pairs=VMEM((samples // 2, KEYS_PAD, 2 * LANES), BF16),
        queries=VMEM((samples, rows, width), BF16),
        dmixes=VMEM((samples, rows, width), BF16),
        u=VMEM((tokens, HEADS * width), BF16),
        dq_wide=VMEM((tokens, HEADS * width), BF16),
        mixed=VMEM((tokens, width), BF16),
        second=VMEM((tokens, width), BF16),
        active=VMEM((tokens, wide), BF16),
        dhidden=VMEM((tokens, wide), BF16),
        out_low=VMEM((tokens, width), BF16),
        dres_low=VMEM((tokens, width), BF16),
        dres=VMEM((tokens, width), F32),
        resid=VMEM((tokens, width), F32),
        hat_two=VMEM((tokens, width), F32),
        rstd_two=VMEM((tokens, 1), F32),
        slope=VMEM((tokens, wide), F32),
        dmixed=VMEM((tokens, width), BF16),
        dquery=VMEM((tokens, width), BF16),
        out_v=VMEM((tokens, width), F32),
        ag_v=VMEM((tokens, width), F32),
        angle=VMEM((samples, width // 2), F32),
        embed=VMEM((samples, width), BF16),
        stamps=VMEM((samples, 8, width), F32),
        gain_acc=VMEM((8, width), F32),
        flags_s=pltpu.SMEM(flags.shape, jnp.int32),
        levels_s=pltpu.SMEM(levels.shape, jnp.int32),
        in_sems=sem((10,)),
        out_sems=sem((2 + samples // 16,)),
    )
    extra = {}
    if remote:
        ins.update(sqm=sqm, mlpm=mlpm)
        outs.update(out=jax.ShapeDtypeStruct((3, WIRE, LANES), F32))
        chunks = len(CHUNKS)
        scratch.update(
            grads=VMEM(grads, F32),
            sqw_v=VMEM(sqw.shape, F32),
            mlpw_v=VMEM(mlpw.shape, F32),
            gain_v=VMEM(gain.shape, F32),
            sqm_v=VMEM(sqm.shape, F32),
            mlpm_v=VMEM(mlpm.shape, F32),
            wire=VMEM(grads, BF16),
            edge=VMEM((16, LANES), F32),
            gsend=sem((len(PIECES), 6)),
            grecv=sem((len(PIECES), 6)),
            send0=VMEM((4, 2, 2, WIRE, LANES), BF16),
            got_core=VMEM((4, 2, 2, WIRE, LANES), BF16),
            sum1=VMEM((4, 2, 2, WIRE, LANES), F32),
            send1=VMEM((4, 2, WIRE, LANES), BF16),
            got1=VMEM((4, 2, WIRE, LANES), BF16),
            sum2=VMEM((4, 2, WIRE, LANES), F32),
            send2=VMEM((4, WIRE, LANES), BF16),
            got2=VMEM((4, WIRE, LANES), BF16),
            sum3=VMEM((4, WIRE, LANES), F32),
            send3=VMEM((4, WIRE, LANES), BF16),
            got3=VMEM((3, WIRE, LANES), BF16),
            moment=VMEM((WIRE, LANES), F32),
            slabs_sq=VMEM((4, 8, 4, SQ_ROWS, LANES), BF16),
            slabs_mlp=VMEM((32, MLP_ROWS, LANES), BF16),
            moment_low=VMEM((2 * MLP_ROWS, LANES), BF16),
            back_mlp=VMEM((2, MLP_ROWS, LANES), BF16),
            back_sq=VMEM((5, SQ_ROWS, LANES), BF16),
            result_sq=VMEM((32, SQ_ROWS, LANES), BF16),
            result_mlp=VMEM((32, MLP_ROWS, LANES), BF16),
            cur=VMEM((width, wide), F32),
            cur_low=VMEM((width, wide), BF16),
            send=sem((chunks, 6)),
            recv=sem((chunks, 6)),
            own_send=sem((len(PARTS_OUT),)),
            own_recv=sem((1,)),
            back_send=sem((32,)),
            back_recv=sem((7,)),
        )
        extra = dict(collective_id=0, has_side_effects=True)
        outs = {name: VMEM(like.shape, like.dtype) for name, like in outs.items()}
    else:
        outs.update(grads=jax.ShapeDtypeStruct(grads, F32))
    names = tuple(ins) + tuple(outs) + tuple(scratch)
    stay = [pltpu.with_memory_space_constraint(value, pltpu.HBM) for value in ins.values()]
    results = pl.pallas_call(
        functools.partial(block_kernel, names, remote),
        out_shape=tuple(outs.values()),
        in_specs=[any_space] * len(ins),
        out_specs=[any_space] * 3 + [in_vmem],
        scratch_shapes=list(scratch.values()),
        compiler_params=pltpu.CompilerParams(vmem_limit_bytes=52 << 20, **extra),
        name="block_and_back",
    )(*stay)
    return Refs(zip(outs, results))


PARTS = 7


def finish_kernel(names, rate, *args):
    r = Refs(zip(names, args))
    sems = r.sems
    keys = r.og.shape[0]
    step = keys // PARTS

    def leave(part):
        block = pl.ds(part * step, step)
        return pltpu.make_async_copy(r.og_v.at[block], r.og.at[block], sems.at[part])

    more = PARTS
    moves = []
    if hasattr(r, "wire"):
        pairs = [(r.sqw, r.sqw_v), (r.mlpw, r.mlpw_v), (r.gain, r.gain_v), (r.gainm, r.gainm_v)]
        pairs += [(r.output, r.output_f), (r.ag, r.ag_f)]
        for source, target in pairs:
            moves.append(pltpu.make_async_copy(source, target, sems.at[more]))
            moves[-1].start()
            more += 1
    for part in range(PARTS):

        def widen(j, _):
            r.og_v[j] = r.low[j].astype(F32)
            return 0

        lax.fori_loop(part * step, (part + 1) * step, widen, 0, unroll=4)
        leave(part).start()
    for copy in moves[:4]:
        copy.wait()
    if hasattr(r, "wire"):
        finish_weights(r, rate)
    for part in range(PARTS):
        leave(part).wait()
    for copy in moves[4:]:
        copy.wait()


def finish_weights(r, rate):
    wire = r.wire
    me = lax.axis_index("dp")
    for m in range(5):
        for j in range(2):
            rows, columns = pl.ds(SQ_AT[m] + j * TILE, TILE), pl.ds(j * LANES, LANES)
            r.sqg[m, :, columns] = wire[0, rows, :]
            r.sqm[m, :, columns] = wire[1, rows, :]
            r.sqn[m, :, columns] = r.sqw_v[m, :, columns] - SQ_RATES[m] * wire[2, rows, :]
    r.sqc[...] = r.sqn[...].astype(BF16)
    for m in range(2):
        for j in range(8):
            rows, columns = pl.ds(m * MLP_ROWS + j * TILE, TILE), pl.ds(j * LANES, LANES)
            r.mlpg[m, :, columns] = wire[0, rows, :]
            r.mlpm[m, :, columns] = wire[1, rows, :]
            r.mlpn[m, :, columns] = r.mlpw_v[m, :, columns] - MLP_RATES[m] * wire[2, rows, :]
    r.mlpc[...] = r.mlpn[...].astype(BF16)
    tile = wire[0, pl.ds(GAIN_BASE, TILE), :]
    turned = pltpu.roll(tile, (LANES - (me % 16) * TILE) % LANES, 1)
    at = me // 16
    for norm in range(2):
        pair = turned[2 * norm : 2 * norm + 2, 0:TILE]
        row = jnp.where(at == 0, pair[0:1, :], pair[1:2, :])
        new = 0.5 * r.gainm_v[norm : norm + 1, :] + row
        r.gg[norm : norm + 1, :] = row
        r.gm[norm : norm + 1, :] = new
        r.gn[norm : norm + 1, :] = r.gain_v[norm : norm + 1, :] - rate * new


def finish(rate, made, sqw=None, mlpw=None, gain=None, gainm=None):
    any_space = pl.BlockSpec(memory_space=pl.ANY)
    in_vmem = pl.BlockSpec(memory_space=VMEM)
    ins = dict(low=made.og)
    outs = dict(og=jax.ShapeDtypeStruct(made.og.shape, F32))
    near, far = 1, 1
    if hasattr(made, "out"):
        ins.update(output=made.output, ag=made.ag, wire=made.out, sqw=sqw, mlpw=mlpw, gain=gain, gainm=gainm)
        like = jax.ShapeDtypeStruct
        near, far = 4, 3
        outs.update(
            output_f=like(made.output.shape, F32),
            ag_f=like(made.ag.shape, F32),
            sqg=like(sqw.shape, F32),
            sqm=like(sqw.shape, F32),
            sqn=like(sqw.shape, F32),
            sqc=like(sqw.shape, BF16),
            mlpg=like(mlpw.shape, F32),
            mlpm=like(mlpw.shape, F32),
            mlpn=like(mlpw.shape, F32),
            mlpc=like(mlpw.shape, BF16),
            gg=like(gain.shape, F32),
            gm=like(gain.shape, F32),
            gn=like(gain.shape, F32),
        )
    scratch = dict(
        og_v=VMEM(made.og.shape, F32),
        sems=pltpu.SemaphoreType.DMA((PARTS + 6,)),
    )
    if hasattr(made, "out"):
        scratch.update(
            sqw_v=VMEM(sqw.shape, F32),
            mlpw_v=VMEM(mlpw.shape, F32),
            gain_v=VMEM(gain.shape, F32),
            gainm_v=VMEM(gainm.shape, F32),
        )
    names = tuple(ins) + tuple(outs) + tuple(scratch)
    made_here = list(ins.values())
    stay = [pltpu.with_memory_space_constraint(value, pltpu.HBM) for value in made_here[near:]]
    results = pl.pallas_call(
        functools.partial(finish_kernel, names, rate),
        out_shape=tuple(outs.values()),
        in_specs=[in_vmem] * near + [any_space] * (len(ins) - near),
        out_specs=[any_space] * far + [in_vmem] * (len(outs) - far),
        scratch_shapes=list(scratch.values()),
        compiler_params=pltpu.CompilerParams(vmem_limit_bytes=16 << 20),
        name="finish",
    )(*made_here[:near], *stay)
    return Refs(zip(outs, results))


HIGH_PRECISION = lax.Precision.HIGHEST


def plain_orthogonalize(matrix):
    current = matrix / (jnp.sqrt(jnp.sum(matrix * matrix)) + 1e-07)
    for turn in range(5):
        gram = jnp.dot(current, current.T, precision=HIGH_PRECISION)
        poly = COEF_B * gram + COEF_C * jnp.dot(gram, gram, precision=HIGH_PRECISION)
        current = COEF_A * current + jnp.dot(poly, current, precision=HIGH_PRECISION)
    return current


def pick_owned(stack, owners, device):
    chosen = jnp.zeros_like(stack[0])
    for index in range(len(owners)):
        chosen = jnp.where(device == owners[index], stack[index], chosen)
    return chosen


def is_owner(owners, device):
    flag = device < 0
    for owner in owners:
        flag = jnp.logical_or(flag, device == owner)
    return flag


def from_wire(grads):
    def matrix(base, tiles):
        part = grads[:, base : base + tiles * TILE, :].reshape(-1, tiles, TILE, LANES)
        return part.transpose(0, 2, 1, 3).reshape(-1, tiles * LANES)

    square = jnp.stack([matrix(SQ_AT[m], 2) for m in range(5)])
    mlp = jnp.stack([matrix(m * MLP_ROWS, 8) for m in range(2)])
    return square, mlp, grads[0, GAIN_BASE : GAIN_BASE + 4, :].reshape(2, 2 * LANES)


def update_by_collectives(
    grads, square_weights, mlp_weights, gains, square_moment, mlp_moment, gain_moment, rate
):
    square_local, mlp_local, gain_local = from_wire(grads)
    square_grad, mlp_grad, gain_grad = (
        lax.psum_scatter(square_local, "dp", scatter_dimension=1, tiled=True),
        lax.psum_scatter(mlp_local, "dp", scatter_dimension=1, tiled=True),
        lax.psum_scatter(gain_local, "dp", scatter_dimension=1, tiled=True),
    )
    square_moment_new = 0.5 * square_moment + square_grad
    mlp_moment_new = 0.5 * mlp_moment + mlp_grad
    gain_moment_new = 0.5 * gain_moment + gain_grad
    device = lax.axis_index("dp")
    count = lax.axis_size("dp")
    square_owners = [index * count // 7 for index in range(5)]
    mlp_owners = [(index + 5) * count // 7 for index in range(2)]
    square_full, mlp_full = (
        lax.all_gather(square_moment_new, "dp", axis=1, tiled=True),
        lax.all_gather(mlp_moment_new, "dp", axis=1, tiled=True),
    )
    mine_square = pick_owned(square_full, square_owners, device)
    mine_mlp = pick_owned(mlp_full, mlp_owners, device)
    made_square = lax.cond(
        is_owner(square_owners, device), plain_orthogonalize, jnp.zeros_like, mine_square
    )
    made_mlp = lax.cond(is_owner(mlp_owners, device), plain_orthogonalize, jnp.zeros_like, mine_mlp)
    stack_square = jnp.stack(
        [jnp.where(device == owner, made_square, 0.0) for owner in square_owners]
    )
    stack_mlp = jnp.stack([jnp.where(device == owner, made_mlp, 0.0) for owner in mlp_owners])
    square_ortho, mlp_ortho = (
        lax.psum_scatter(stack_square, "dp", scatter_dimension=1, tiled=True),
        lax.psum_scatter(stack_mlp, "dp", scatter_dimension=1, tiled=True),
    )
    square_new = square_weights - jnp.array(SQ_RATES, F32)[:, None, None] * square_ortho
    mlp_new = mlp_weights - jnp.array(MLP_RATES, F32)[:, None, None] * mlp_ortho
    gains_new = gains - rate * gain_moment_new
    return (
        square_grad,
        square_moment_new,
        square_new,
        square_new.astype(BF16),
        mlp_grad,
        mlp_moment_new,
        mlp_new,
        mlp_new.astype(BF16),
        gain_grad,
        gain_moment_new,
        gains_new,
    )


def per_device(
    actions,
    observed,
    camera_flags,
    noise_levels,
    cotangent,
    square_weights,
    mlp_weights,
    gains,
    square_moment,
    mlp_moment,
    gain_moment,
):
    count = lax.axis_size("dp")
    rate = 0.1 / math.sqrt(actions.shape[0] * count)
    by_key = observed.transpose(1, 0, 2)
    ins = (actions, by_key, camera_flags, noise_levels, cotangent)
    if count == math.prod(GRID):
        made = block_and_back(True, *ins, square_weights, mlp_weights, gains, square_moment, mlp_moment)
        done = finish(rate, made, square_weights, mlp_weights, gains, gain_moment)
        output, actions_grad = done.output_f, done.ag_f
        d = done
        rest = (d.sqg, d.sqm, d.sqn, d.sqc, d.mlpg, d.mlpm, d.mlpn, d.mlpc, d.gg, d.gm, d.gn)
    else:
        square_all, mlp_all = (
            lax.all_gather(square_weights.astype(BF16), "dp", axis=1, tiled=True),
            lax.all_gather(mlp_weights.astype(BF16), "dp", axis=1, tiled=True),
        )
        gain_all = lax.all_gather(gains, "dp", axis=1, tiled=True)
        made = block_and_back(False, *ins, square_all, mlp_all, gain_all)
        done = finish(rate, made)
        output, actions_grad = made.output, made.ag
        grads = made.grads.reshape(-1, WIRE, LANES)
        rest = update_by_collectives(
            grads, square_weights, mlp_weights, gains, square_moment, mlp_moment, gain_moment, rate
        )
    observed_grad = done.og.transpose(1, 0, 2)
    return (output, actions_grad, observed_grad) + tuple(rest)


def solution(mesh):
    rows, cube, flat = P("dp", None), P("dp", None, None), P("dp")
    stacked, pair = P(None, "dp", None), P(None, "dp")
    return jax.shard_map(
        per_device,
        mesh=mesh,
        in_specs=(rows, cube, flat, flat, rows, stacked, stacked, pair, stacked, stacked, pair),
        out_specs=(rows, rows, cube) + (stacked,) * 8 + (pair,) * 3,
        check_vma=False,
    )
```

```python
import functools
import math

import jax
import jax.numpy as jnp
from jax import lax
from jax.experimental import pallas as pl
from jax.experimental.pallas import tpu as pltpu
from jax.sharding import PartitionSpec as P

HEADS = 4
ACT = 16
OBS_FULL = 196
OBS_FEW = 49
COEF_A = 3.4445
COEF_B = -4.775
COEF_C = 2.0315
F32 = jnp.float32
BF16 = jnp.bfloat16
MESH = pl.DeviceIdType.MESH
VMEM = pltpu.VMEM
NN = (((1,), (0,)), ((), ()))
NT = (((1,), (1,)), ((), ()))
TN = (((0,), (0,)), ((), ()))

LANES = 128
TILE = 8
MLP_ROWS = 64
SQ_ROWS = 16
SQ_AT = (160, 192, 176, 128, 144)
GAIN_BASE = 208
WIRE = 224
PIECES = ((0, 32), (32, 32), (64, 32), (96, 32), (128, 32), (160, 32), (192, 32))
PIECE_X_FIRST = (True, False, True, False, True, True, False)
CHUNKS = ((0, 32), (32, 32), (64, 32), (96, 32), (128, 32), (160, 32), (192, 16), (208, 16))
X_FIRST = (True, False, True, False, True, False, True, False)
PARTS_OUT = (
    (0, 0, 0, 32, 0),
    (1, 0, 32, 32, 32),
    (2, 1, 64, 32, 0),
    (3, 1, 96, 32, 32),
    (4, 5, 128, 16, 0),
    (4, 6, 144, 16, 0),
    (5, 2, 160, 16, 0),
    (5, 4, 176, 16, 0),
    (6, 3, 192, 16, 0),
)
MLP_RATES = (1.0, 0.5)
SQ_RATES = (0.5, 0.5, 0.5, 0.5, 4.0)
GRID = (4, 2, 2, 2)
OWNERS = (8, 22, 14, 16, 11, 21, 13)
SHIFTS = (0.0, 0.0, 0.4, 0.8, 0.8)
KEYS_PAD = 208
GROUP = 16
ROWS = 512


class Refs:
    def __init__(self, pairs):
        self.__dict__.update(pairs)


def dot(left, right, dims=NN):
    return lax.dot_general(left, right, dims, preferred_element_type=F32)


def place():
    me = lax.axis_index("dp")
    return me, me // 8, (me // 4) % 2, (me // 2) % 2, me % 2


def device_at(z, y, x, c):
    return ((z * 2 + y) * 2 + x) * 2 + c


def link(src, dst, send, recv, device):
    return pltpu.make_async_remote_copy(
        src_ref=src,
        dst_ref=dst,
        send_sem=send,
        recv_sem=recv,
        device_id=(device,),
        device_id_type=MESH,
    )


def greet(device):
    pl.semaphore_signal(
        pltpu.get_barrier_semaphore(), inc=1, device_id=(device,), device_id_type=MESH
    )


def normalize(values):
    centred = values - jnp.mean(values, -1, keepdims=True)
    scale = lax.rsqrt(jnp.mean(centred * centred, -1, keepdims=True) + 1e-05)
    return centred * scale, scale


def norm_back(grad, hat, scale):
    mean_one = jnp.mean(grad, -1, keepdims=True)
    mean_two = jnp.mean(grad * hat, -1, keepdims=True)
    return scale * (grad - mean_one - hat * mean_two)


class Gather:
    def __init__(self, r):
        self.r = r
        self.me, self.z, self.y, self.x, self.c = place()

    def hop(self, k, step, part, device):
        return link(part, part, self.r.gsend.at[k, step], self.r.grecv.at[k, step], device)

    def along_z(self, k, step):
        part = self.r.wire.at[self.z, self.y, self.x, self.c, pl.ds(*PIECES[k])]
        return self.hop(k, step, part, device_at((self.z + step + 1) % 4, self.y, self.x, self.c))

    def from_z(self, k, step):
        there = (self.z + 3 - step) % 4
        part = self.r.wire.at[there, self.y, self.x, self.c, pl.ds(*PIECES[k])]
        return self.hop(k, step, part, device_at(there, self.y, self.x, self.c))

    def plane(self, k, second, mine):
        z, y, x, c = self.z, self.y, self.x, self.c
        rows, wire = pl.ds(*PIECES[k]), self.r.wire
        py, px = (y, x) if mine else (1 - y, 1 - x)
        along_x = PIECE_X_FIRST[k] == second
        if along_x:
            part = wire.at[:, y, px, c, rows] if second else wire.at[:, :, px, c, rows]
            return self.hop(k, 3 if second else 4, part, device_at(z, y, 1 - x, c))
        part = wire.at[:, py, x, c, rows] if second else wire.at[:, py, :, c, rows]
        return self.hop(k, 3 if second else 4, part, device_at(z, 1 - y, x, c))

    def core(self, k, mine):
        part = self.r.wire.at[:, :, :, self.c if mine else 1 - self.c, pl.ds(*PIECES[k])]
        return self.hop(k, 5, part, device_at(self.z, self.y, self.x, 1 - self.c))

    def first(self, *chunks):
        for k in chunks:
            for step in range(3):
                self.along_z(k, step).start()

    def second(self, *chunks):
        for k in chunks:
            for step in range(3):
                self.from_z(k, step).wait_recv()
            self.plane(k, True, True).start()

    def third(self, *chunks):
        for k in chunks:
            self.plane(k, True, False).wait_recv()
            self.plane(k, False, True).start()

    def fourth(self, *chunks):
        for k in chunks:
            self.plane(k, False, False).wait_recv()
            self.core(k, True).start()

    def last(self, *chunks):
        for k in chunks:
            self.core(k, False).wait_recv()

    def drain(self):
        for k in range(len(PIECES)):
            for step in range(3):
                self.along_z(k, step).wait_send()
            self.plane(k, True, True).wait_send()
            self.plane(k, False, True).wait_send()
            self.core(k, True).wait_send()

    def fill(self):
        r = self.r
        spot = (self.z, self.y, self.x, self.c)

        def tiles(source, m, base, number):
            for j in range(number):
                pair = [source[m, :, pl.ds((2 * j + k) * LANES, LANES)] for k in range(2)]
                r.wire[spot + (pl.ds(base + j * 16, 16),)] = jnp.concatenate(pair, axis=0).astype(BF16)

        for m in range(5):
            tiles(r.sqw_v, m, SQ_AT[m], 1)
        for m in range(2):
            tiles(r.mlpw_v, m, m * MLP_ROWS, 4)
        gains, edge = r.gain_v[...], r.edge
        high = gains.astype(BF16).astype(F32)
        middle = (gains - high).astype(BF16).astype(F32)
        edge[...] = jnp.zeros_like(edge)
        edge[0:2, 0:TILE] = high
        edge[2:4, 0:TILE] = middle
        edge[4:6, 0:TILE] = (gains - high - middle).astype(BF16).astype(F32)
        r.wire[spot + (pl.ds(GAIN_BASE, 16),)] = edge[...].astype(BF16)

    def unpack(self, base, number, out, m):
        for j in range(number):
            block = self.r.wire[:, :, :, :, pl.ds(base + j * 16, 16), :].reshape(32, 16, LANES).astype(F32)
            for half in range(2):
                columns = pl.ds((2 * j + half) * LANES, LANES)
                out[m, :, columns] = block[:, half * 8 : half * 8 + 8, :].reshape(256, LANES).astype(BF16)

    def unpack_gains(self):
        edge, wire = self.r.edge, self.r.wire
        for half in range(2):
            total = jnp.zeros((16, LANES), F32)
            for at in range(16):
                d = half * 16 + at
                tile = wire[d // 8, (d // 4) % 2, (d // 2) % 2, d % 2, pl.ds(GAIN_BASE, 16), :].astype(F32)
                total = total + (tile if at == 0 else pltpu.roll(tile, at * TILE, 1))
            edge[...] = total
            self.r.gain_all[:, pl.ds(half * LANES, LANES)] = edge[0:2, :] + edge[2:4, :] + edge[4:6, :]


class Update:
    def __init__(self, r):
        self.r = r
        self.me, self.z, self.y, self.x, self.c = place()

    def hop(self, k, step, src, dst, device):
        return link(src, dst, self.r.send.at[k, step], self.r.recv.at[k, step], device)

    def core(self, k):
        rows = pl.ds(*CHUNKS[k])
        src, dst = self.r.send0.at[:, :, :, rows], self.r.got_core.at[:, :, :, rows]
        return self.hop(k, 0, src, dst, device_at(self.z, self.y, self.x, 1 - self.c))

    def plane(self, k, first):
        rows = pl.ds(*CHUNKS[k])
        to = (self.z, self.y, 1 - self.x, self.c) if X_FIRST[k] == first else (self.z, 1 - self.y, self.x, self.c)
        if first:
            src, dst = self.r.send1.at[:, :, rows], self.r.got1.at[:, :, rows]
        else:
            src, dst = self.r.send2.at[:, rows], self.r.got2.at[:, rows]
        return self.hop(k, 1 if first else 2, src, dst, device_at(*to))

    def along_z(self, k, step):
        rows = pl.ds(*CHUNKS[k])
        there = (self.z + step + 1) % 4
        src, dst = self.r.send3.at[there, rows], self.r.got3.at[step, rows]
        return self.hop(k, 3 + step, src, dst, device_at(there, self.y, self.x, self.c))

    def start(self, k):
        rows = pl.ds(*CHUNKS[k])
        self.r.send0[:, :, :, rows, :] = self.r.grads[:, :, :, 1 - self.c, rows, :].astype(BF16)
        self.core(k).start()

    def one(self, *chunks):
        r = self.r
        for k in chunks:
            rows = pl.ds(*CHUNKS[k])
            self.core(k).wait_recv()
            sum1 = r.sum1
            sum1[:, :, :, rows, :] = r.grads[:, :, :, self.c, rows, :] + r.got_core[:, :, :, rows, :].astype(F32)
            other = sum1[:, :, 1 - self.x, rows, :] if X_FIRST[k] else sum1[:, 1 - self.y, :, rows, :]
            r.send1[:, :, rows, :] = other.astype(BF16)
            self.plane(k, True).start()

    def two(self, *chunks):
        r = self.r
        for k in chunks:
            rows = pl.ds(*CHUNKS[k])
            self.plane(k, True).wait_recv()
            sum1, sum2 = r.sum1, r.sum2
            mine = sum1[:, :, self.x, rows, :] if X_FIRST[k] else sum1[:, self.y, :, rows, :]
            sum2[:, :, rows, :] = mine + r.got1[:, :, rows, :].astype(F32)
            other = 1 - self.y if X_FIRST[k] else 1 - self.x
            r.send2[:, rows, :] = sum2[:, other, rows, :].astype(BF16)
            self.plane(k, False).start()

    def three(self, *chunks):
        r = self.r
        for k in chunks:
            rows = pl.ds(*CHUNKS[k])
            self.plane(k, False).wait_recv()
            mine = self.y if X_FIRST[k] else self.x
            total = r.sum2[:, mine, rows, :] + r.got2[:, rows, :].astype(F32)
            r.sum3[:, rows, :] = total
            r.send3[:, rows, :] = total.astype(BF16)
            if k >= 4:
                own = r.sum3[self.z, rows, :] + 0.5 * r.moment[rows, :]
                r.send3[self.z, rows, :] = own.astype(BF16)
                self.parts_to_owners(k)
            for step in range(3):
                self.along_z(k, step).start()

    def parts_to_owners(self, k):
        for part, (chunk, index, *_) in enumerate(PARTS_OUT):
            if chunk != k:
                continue

            @pl.when(self.me != OWNERS[index])
            def _():
                self.to_owner(part).start()

            @pl.when(self.me == OWNERS[index])
            def _():
                src, dst = self.own_part(part)
                pltpu.make_async_copy(src, dst, self.r.own_recv.at[0]).start()

    def result(self, index):
        return self.r.result_mlp if index < 2 else self.r.result_sq

    def own_part(self, part):
        _, index, base, number, place = PARTS_OUT[part]
        if index < 2:
            return self.r.moment_low.at[pl.ds(base, number)], self.r.slabs_mlp.at[self.me, pl.ds(place, number)]
        return self.r.send3.at[:, pl.ds(base, number)], self.r.slabs_sq.at[self.z, self.me % 8]

    def to_owner(self, part):
        src, dst = self.own_part(part)
        return link(src, dst, self.r.own_send.at[part], self.r.own_recv.at[0], OWNERS[PARTS_OUT[part][1]])

    def four(self, *chunks):
        r = self.r
        moment, out = r.moment, r.out
        for k in chunks:
            rows = pl.ds(*CHUNKS[k])
            total = r.sum3[self.z, rows, :]
            for step in range(3):
                self.along_z(k, step).wait_recv()
                total = total + r.got3[step, rows, :].astype(F32)
            out[0, rows, :] = total
            new = 0.5 * moment[rows, :] + total
            moment[rows, :] = new
            if k < 4:
                r.moment_low[rows, :] = new.astype(BF16)
            if k < 4:
                self.parts_to_owners(k)

    def old_moment(self):
        r = self.r
        moment = r.moment
        for m in range(2):
            for j in range(8):
                moment[pl.ds(m * MLP_ROWS + j * TILE, TILE), :] = r.mlpm_v[m, :, pl.ds(j * LANES, LANES)]
        for m in range(5):
            for j in range(2):
                moment[pl.ds(SQ_AT[m] + j * TILE, TILE), :] = r.sqm_v[m, :, pl.ds(j * LANES, LANES)]
        moment[pl.ds(GAIN_BASE, 16), :] = jnp.zeros((16, LANES), F32)

    def orthogonalize(self):
        r = self.r
        cur = r.cur
        rows = lax.broadcasted_iota(jnp.int32, (256, 256), 0)
        diagonal = rows == lax.broadcasted_iota(jnp.int32, (256, 256), 1)

        low = r.cur_low

        def load(rows, j, pair):
            for side in range(2):
                columns = pl.ds((2 * j + side) * LANES, LANES)
                part = pair[:, side * TILE : (side + 1) * TILE, :].reshape(-1, LANES)
                cur[rows, columns] = part
                low[rows, columns] = part.astype(BF16)

        def load_mlp():
            for j in range(4):
                load(pl.ds(0, 256), j, r.slabs_mlp[:, pl.ds(j * 16, 16), :].astype(F32))

        def load_sq():
            for to in range(4):
                pair = r.slabs_sq[0, :, to].astype(F32)
                for plane in range(1, 4):
                    pair = pair + r.slabs_sq[plane, :, to].astype(F32)
                load(pl.ds(to * 64, 64), 0, pair)

        def run(slabs, fetch, result, tiles):
            pltpu.make_async_copy(slabs, slabs, r.own_recv.at[0]).wait()
            fetch()
            scale = 1.0
            for turn, shift in enumerate(SHIFTS):
                whole = low[:, 0 : tiles * LANES]
                off = dot(whole, whole, NT)
                if turn == 0:
                    norm = jnp.sum(jnp.sum(jnp.where(diagonal, off, 0.0), axis=0, keepdims=True), axis=1, keepdims=True)
                    scale = 1.0 / (jnp.sqrt(norm) + 1e-07)
                    off = off * (scale * scale)
                if shift:
                    off = off - jnp.where(diagonal, shift, 0.0)
                off_low = off.astype(BF16)
                poly = (COEF_B + 2.0 * COEF_C * shift) * off + COEF_C * dot(off_low, off_low)
                poly = poly.astype(BF16)
                keep = COEF_A + shift * (COEF_B + COEF_C * shift)
                for j in range(tiles // 2):
                    columns = pl.ds(j * 2 * LANES, 2 * LANES)
                    now = keep * cur[:, columns] + dot(poly, low[:, columns])
                    if turn == 0:
                        now = now * scale
                    if turn < len(SHIFTS) - 1:
                        cur[:, columns] = now
                        low[:, columns] = now.astype(BF16)
                    else:
                        parts = [now[:, side * LANES : (side + 1) * LANES].reshape(32, TILE, LANES) for side in range(2)]
                        result[:, pl.ds(j * 16, 16), :] = jnp.concatenate(parts, axis=1).astype(result.dtype)

        mine_mlp = jnp.logical_or(self.me == OWNERS[0], self.me == OWNERS[1])
        mine_sq = self.me < 0
        for device in OWNERS[2:]:
            mine_sq = jnp.logical_or(mine_sq, self.me == device)

        @pl.when(mine_mlp)
        def _():
            run(r.slabs_mlp, load_mlp, r.result_mlp, 8)

        @pl.when(mine_sq)
        def _():
            run(r.slabs_sq, load_sq, r.result_sq, 2)

    def landing(self, index):
        if index < 2:
            return self.r.back_mlp.at[index]
        return self.r.back_sq.at[index - 2]

    def give_back(self, index, device):
        result = self.result(index)
        return link(
            result.at[device], self.landing(index),
            self.r.back_send.at[device], self.r.back_recv.at[index], device,
        )

    def give_all(self):
        r = self.r
        for index in range(7):
            result = self.result(index)

            @pl.when(self.me == OWNERS[index])
            def _():
                def send_one(step, _):
                    self.give_back(index, step + (step + 32 - self.me) // 32).start()
                    return 0

                lax.fori_loop(0, 31, send_one, 0)
                pltpu.make_async_copy(result.at[self.me], self.landing(index), r.back_recv.at[index]).start()

    def take_all(self):
        for index in range(7):
            result = self.result(index)
            pltpu.make_async_copy(result.at[0], self.landing(index), self.r.back_recv.at[index]).wait()
        for index in range(2):
            rows = pl.ds(index * MLP_ROWS, MLP_ROWS)
            self.r.out[2, rows, :] = self.r.back_mlp[index].astype(F32)
        for index in range(5):
            self.r.out[2, pl.ds(SQ_AT[index], SQ_ROWS), :] = self.r.back_sq[index].astype(F32)

    def drain(self):
        for k in range(len(CHUNKS)):
            self.core(k).wait_send()
            self.plane(k, True).wait_send()
            self.plane(k, False).wait_send()
            for step in range(3):
                self.along_z(k, step).wait_send()
        for part in range(len(PARTS_OUT)):

            @pl.when(self.me != OWNERS[PARTS_OUT[part][1]])
            def _():
                self.to_owner(part).wait_send()

    def drain_owner(self):
        for index in range(7):

            @pl.when(self.me == OWNERS[index])
            def _():
                def wait_one(step, _):
                    self.give_back(index, step + (step + 32 - self.me) // 32).wait_send()
                    return 0

                lax.fori_loop(0, 31, wait_one, 0)


def greet_all():
    me, z, y, x, c = place()
    greet(device_at(z, y, x, 1 - c))
    greet(device_at(z, y, 1 - x, c))
    greet(device_at(z, 1 - y, x, c))
    for step in range(1, 4):
        greet(device_at((z + step) % 4, y, x, c))
    owner = me < 0
    for device in OWNERS:
        owner = jnp.logical_or(owner, me == device)

        @pl.when(me != device)
        def _():
            greet(device)

    @pl.when(owner)
    def _():
        def greet_other(step, _):
            greet((me + step) % 32)
            return 0

        lax.fori_loop(1, 32, greet_other, 0)

    is_owner = owner.astype(jnp.int32)
    return 6 + 7 - is_owner + 31 * is_owner


def block_kernel(names, remote, *args):
    r = Refs(zip(names, args))
    keys, samples = r.obs.shape[0], r.obs.shape[1]
    tokens, width = r.acts.shape
    head_dim, half, per = width // HEADS, width // 2, ROWS // ACT
    wide = r.mlp_all.shape[2]
    groups = samples // GROUP
    in_sems, out_sems = r.in_sems, r.out_sems

    if remote:
        own = (r.sqw_v, r.mlpw_v, r.gain_v)
    else:
        own = (r.sq_all, r.mlp_all, r.gain_all)
    loads = list(zip((r.sqw, r.mlpw, r.gain), own))
    loads += [(r.acts, r.acts_v), (r.obs, r.obs_v.at[pl.ds(0, keys)]), (r.cot, r.cot_v)]
    if remote:
        loads += [(r.sqm, r.sqm_v), (r.mlpm, r.mlpm_v)]
    loads += [(r.flags, r.flags_s), (r.levels, r.levels_s)]
    copies = [pltpu.make_async_copy(a, b, in_sems.at[i]) for i, (a, b) in enumerate(loads)]

    def arrive(*which):
        for i in which:
            copies[i].wait()

    for copy in copies:
        copy.start()
    if remote:
        gather, update = Gather(r), Update(r)
        expected = greet_all()
        arrive(0, 1, 2)
        gather.fill()
        pl.semaphore_wait(pltpu.get_barrier_semaphore(), expected)
        gather.first(5, 6, 4, 0, 1, 2, 3)

    arrive(3)

    def hats(i, _):
        rows = pl.ds(pl.multiple_of(i * ROWS, ROWS), ROWS)
        hat, scale = normalize(r.acts_v[rows, :])
        r.xhat[rows, :] = hat
        r.rstd[rows, :] = scale
        return 0

    lax.fori_loop(0, tokens // ROWS, hats, 0)

    mem, obs_v = r.mem, r.obs_v
    batch = 16
    chunks = KEYS_PAD // batch
    swap = r.swap
    row = lax.broadcasted_iota(jnp.int32, swap.shape, 0)
    column = lax.broadcasted_iota(jnp.int32, swap.shape, 1)
    swap[...] = jnp.where(column == (row % batch) * batch + row // batch, 1.0, 0.0).astype(BF16)

    def turn(part, low, high):
        def one(j, _):
            at = pl.ds(pl.multiple_of(j * batch, batch), batch)
            here = pl.ds(part * batch, batch)
            block = obs_v[at, here, :].reshape(batch * batch, width)
            mem[here, at, :] = dot(swap[...], block).astype(BF16).reshape(batch, batch, width)
            return 0

        lax.fori_loop(low, high, one, 0, unroll=high - low)

    whole = chunks - 1
    arrive(4)
    turn(0, 0, whole // 2)
    if remote:
        gather.second(5, 6)
    turn(0, whole // 2, whole)
    if remote:
        gather.third(5, 6)
    turn(1, 0, whole // 2)
    if remote:
        gather.second(4, 0, 1)
        gather.fourth(5, 6)
    turn(1, whole // 2, whole)
    if remote:
        gather.second(2, 3)
    arrive(len(copies) - 1, len(copies) - 2)
    freqs = jnp.exp(
        lax.broadcasted_iota(jnp.int32, (1, half), 1).astype(F32) * F32(-math.log(10000.0)) / half
    )
    for s in range(samples):
        r.angle[s : s + 1, :] = r.levels_s[s].astype(F32) * freqs
    r.embed[:, 0:half] = jnp.sin(r.angle[...]).astype(BF16)
    r.embed[:, half:width] = jnp.cos(r.angle[...]).astype(BF16)
    if remote:
        arrive(6, 7)
        update.old_moment()
        gather.third(4, 0, 1)
        gather.last(5, 6)
        for m in range(3):
            gather.unpack(SQ_AT[m], 1, r.sq_all, m)
        gather.unpack_gains()
    else:
        arrive(0, 1, 2)

    sq, mlp = r.sq_all, r.mlp_all
    wkh, wvh = r.wkh, r.wvh
    lane = lax.broadcasted_iota(jnp.int32, (width, width), 1)

    def split_heads(out, weight):
        weight = weight.astype(F32)
        for h in range(HEADS):
            out[pl.ds(h * width, width), :] = jnp.where(lane // head_dim == h, weight, 0.0).astype(BF16)

    split_heads(wkh, sq[2])
    g1, g2 = r.gain_all[0:1, :], r.gain_all[1:2, :]

    obs_v[keys] = dot(r.embed[...], sq[0]).astype(BF16)
    obs_v[keys + 1 :] = jnp.zeros((KEYS_PAD - keys - 1, samples, width), BF16)
    for part in range(samples // batch):
        turn(part, whole, chunks)

    sides, weights = r.sides_v, r.pds_v

    def make_queries(i, _):
        rows = pl.ds(pl.multiple_of(i * ROWS, ROWS), ROWS)
        first = (r.xhat[rows, :] * g1).astype(BF16)
        r.first[rows, :] = first
        q = dot(first, sq[1]).astype(BF16)
        r.query[rows, :] = q
        here = pl.ds(i * per, per)
        for h in range(HEADS):
            wk = wkh[pl.ds(h * width, width), :]
            value = (dot(q, wk, NT) * 0.125).astype(BF16).reshape(per, ACT, width)
            sides[here, pl.ds((HEADS + h) * ACT, ACT), :] = value
        return 0

    lax.fori_loop(0, tokens // ROWS, make_queries, 0)

    key = lax.broadcasted_iota(jnp.int32, (1, KEYS_PAD), 1)
    low_rows, high_rows = pl.ds(0, HEADS * ACT), pl.ds(HEADS * ACT, HEADS * ACT)

    def attend(g, _):
        ids = [g * GROUP + k for k in range(GROUP)]
        scores = [dot(sides[s, high_rows, :], mem[s], NT) for s in ids]
        lows = []
        for s, score in zip(ids, scores):
            count = OBS_FEW + (OBS_FULL - OBS_FEW) * r.flags_s[s]
            score = score + jnp.where((key < count) | (key == OBS_FULL), 0.0, -1000000000.0)
            expo = jnp.exp(score - jnp.max(score, -1, keepdims=True))
            probs = expo * (1.0 / jnp.sum(expo, -1, keepdims=True))
            r.probs[s] = probs
            low = probs.astype(BF16)
            weights[s, low_rows, :] = low
            lows.append(low)
        for s, low in zip(ids, lows):
            u = dot(low, mem[s]).astype(BF16)
            rows = pl.ds(pl.multiple_of(s * ACT, ACT), ACT)
            for h in range(HEADS):
                r.u[rows, pl.ds(h * width, width)] = u[h * ACT : (h + 1) * ACT, :]
        return 0

    lax.fori_loop(0, groups // 2, attend, 0)
    if remote:
        gather.third(2, 3)
        gather.fourth(4, 0, 1)
    lax.fori_loop(groups // 2, groups, attend, 0)
    if remote:
        gather.fourth(2, 3)
        gather.last(4)
        for m in range(3, 5):
            gather.unpack(SQ_AT[m], 1, sq, m)
    split_heads(wvh, sq[3])

    gain_acc = r.gain_acc
    gain_acc[...] = jnp.zeros_like(gain_acc)
    blocks = [pl.ds(i * ROWS, ROWS) for i in range(tokens // ROWS)]
    for rows in blocks:
        mixed = dot(r.u[rows, :], wvh[...]).astype(BF16)
        r.mixed[rows, :] = mixed
        resid = r.acts_v[rows, :] + dot(mixed, sq[4])
        r.resid[rows, :] = resid
        hat, scale = normalize(resid)
        r.hat_two[rows, :] = hat
        r.rstd_two[rows, :] = scale
        r.second[rows, :] = (hat * g2).astype(BF16)
    arrive(5)
    r.out_low[...] = r.cot_v[...].astype(BF16)
    if remote:
        gather.last(0, 1)
        gather.unpack(0, 4, mlp, 0)
    wide_blocks = [pl.ds(c * 256, 256) for c in range(wide // 256)]
    for rows in blocks:
        for columns in wide_blocks:
            v = dot(r.second[rows, :], mlp[0, :, columns])
            square = v * v
            t = jnp.tanh(0.7978845608 * (v + 0.044715 * square * v))
            r.active[rows, columns] = (0.5 * v * (1.0 + t)).astype(BF16)
            slope = 0.5 * (1.0 + t) + 0.5 * v * (1.0 - t * t) * (0.7978845608 * (1.0 + 0.134145 * square))
            r.slope[rows, columns] = slope

    grads = r.grads

    def put(base, tiles, value):
        for j in range(tiles):
            part = value[:, j * LANES : (j + 1) * LANES].reshape(GRID + (TILE, LANES))
            grads[:, :, :, :, pl.ds(base + j * TILE, TILE), :] = part

    def by_head(left, right):
        turned = left.T
        parts = [
            dot(turned[h * head_dim : (h + 1) * head_dim, :], right[:, pl.ds(h * width, width)])
            for h in range(HEADS)
        ]
        return jnp.concatenate(parts, axis=0).T

    put(MLP_ROWS, 8, dot(r.out_low[...], r.active[...], TN))
    if remote:
        update.start(2)
        update.start(3)
        gather.last(2, 3)
        gather.unpack(MLP_ROWS, 4, mlp, 1)
    for rows in blocks:
        for columns in wide_blocks:
            slope = r.slope[rows, columns]
            r.dhidden[rows, columns] = (slope * dot(r.out_low[rows, :], mlp[1, :, columns])).astype(BF16)
    put(0, 8, dot(r.second[...], r.dhidden[...], TN))
    if remote:
        update.start(0)
        update.start(1)
        update.one(2, 3)
    for i, rows in enumerate(blocks):
        r.out_v[rows, :] = r.resid[rows, :] + dot(r.active[rows, :], mlp[1], NT)
        grad_second = dot(r.dhidden[rows, :], mlp[0], NT)
        hat = r.hat_two[rows, :]
        gain_acc[1:2, :] += jnp.sum(grad_second * hat, 0, keepdims=True)
        dres = r.cot_v[rows, :] + norm_back(grad_second * g2, hat, r.rstd_two[rows, :])
        r.dres[rows, :] = dres
        low = dres.astype(BF16)
        r.dres_low[rows, :] = low
        gm = dot(low, sq[4], NT).astype(BF16)
        r.dmixed[rows, :] = gm
        here = pl.ds(i * per, per)
        for h in range(HEADS):
            wv = wvh[pl.ds(h * width, width), :]
            sides[here, pl.ds(h * ACT, ACT), :] = dot(gm, wv, NT).astype(BF16).reshape(per, ACT, width)
    keep_out = pltpu.make_async_copy(r.out_v, r.output, out_sems.at[0])
    keep_out.start()
    if remote:
        update.one(0, 1)
    put(SQ_AT[4], 2, dot(r.mixed[...], r.dres_low[...], TN))
    put(SQ_AT[3], 2, by_head(r.dmixed[...], r.u))
    if remote:
        update.start(4)

    def attend_back(g, _):
        ids = [g * GROUP + k for k in range(GROUP)]
        rises = [dot(sides[s, low_rows, :], mem[s], NT) for s in ids]
        for s, rise in zip(ids, rises):
            probs = r.probs[s]
            both = probs * rise
            weights[s, high_rows, :] = (both - probs * jnp.sum(both, -1, keepdims=True)).astype(BF16)
        for s in ids:
            dq = (dot(weights[s, high_rows, :], mem[s]) * 0.125).astype(BF16)
            rows = pl.ds(pl.multiple_of(s * ACT, ACT), ACT)
            for h in range(HEADS):
                r.dq_wide[rows, pl.ds(h * width, width)] = dq[h * ACT : (h + 1) * ACT, :]
            end = dot(weights[s, :, LANES:KEYS_PAD], sides[s], TN)
            r.stamps[s] = end[64:72, :]
        return 0

    lax.fori_loop(0, groups // 2, attend_back, 0)
    if remote:
        update.two(2, 3)
        update.one(4)
        update.two(0, 1)
    lax.fori_loop(groups // 2, groups, attend_back, 0)
    if remote:
        update.three(2, 3)
        update.two(4)
    put(SQ_AT[2], 2, by_head(r.query[...], r.dq_wide))
    stamp_low = r.stamps[:, 4:5, :].reshape(samples, width).astype(BF16)
    put(SQ_AT[0], 2, dot(r.embed[...], stamp_low, TN))
    if remote:
        update.start(5)
        update.three(0, 1)

    def memory_back(low, high):
        for s in range(2 * low, 2 * high):
            mem[s] = dot(weights[s], sides[s], TN).astype(BF16)

    def keep_og(part):
        here = pl.ds(part * batch, batch)
        return pltpu.make_async_copy(obs_v.at[pl.ds(0, keys), here], r.og.at[:, here], out_sems.at[2 + part])

    def turn_back(part, low, high):
        def one(j):
            at = pl.ds(pl.multiple_of(j * batch, batch), batch)
            here = pl.ds(part * batch, batch)
            block = mem[here, at, :].reshape(batch * batch, width)
            value = dot(swap[...], block).astype(BF16).reshape(batch, batch, width)
            obs_v[at, here, :] = value

        for j in range(low, high):
            one(j)
        if high == chunks:
            keep_og(part).start()

    def queries_back(i, _):
        rows = pl.ds(pl.multiple_of(i * ROWS, ROWS), ROWS)
        r.dquery[rows, :] = dot(r.dq_wide[rows, :], wkh[...]).astype(BF16)
        return 0

    lax.fori_loop(0, tokens // ROWS, queries_back, 0)
    put(SQ_AT[1], 2, dot(r.first[...], r.dquery[...], TN))
    if remote:
        update.start(6)
        update.one(5)

    def acts_back(i, _):
        rows = pl.ds(pl.multiple_of(i * ROWS, ROWS), ROWS)
        grad_first = dot(r.dquery[rows, :], sq[1], NT)
        hat = r.xhat[rows, :]
        gain_acc[0:1, :] += jnp.sum(grad_first * hat, 0, keepdims=True)
        r.ag_v[rows, :] = r.dres[rows, :] + norm_back(grad_first * g1, hat, r.rstd[rows, :])
        return 0

    def finish_acts():
        lax.fori_loop(0, tokens // ROWS, acts_back, 0)
        for norm in range(2):
            for j in range(2):
                row = gain_acc[norm : norm + 1, j * LANES : (j + 1) * LANES]
                at = GAIN_BASE + norm * 2 + j
                value = jnp.broadcast_to(row.reshape(1, 1, 1, 1, 1, LANES), GRID + (1, LANES))
                grads[:, :, :, :, at : at + 1, :] = value
        rest = WIRE - GAIN_BASE - 4
        grads[:, :, :, :, GAIN_BASE + 4 : WIRE, :] = jnp.zeros(GRID + (rest, LANES), F32)

    keep_ag = pltpu.make_async_copy(r.ag_v, r.ag, out_sems.at[1])
    if remote:
        pairs = samples // 2
        finish_acts()
        keep_ag.start()
        update.start(7)
        update.one(6)
        update.three(4)
        memory_back(0, pairs // 2)
        update.four(2, 3)
        update.two(5)
        update.one(7)
        update.two(6)
        memory_back(pairs // 2, pairs)
        update.four(0, 1)
        update.three(5)
        update.two(7)
        update.three(6)
        turn_back(0, 0, chunks // 2)
        update.orthogonalize()
        update.give_all()
        update.three(7)
        turn_back(0, chunks // 2, chunks)
        update.four(4, 5, 6)
        turn_back(1, 0, chunks)
        update.four(7)
        out = r.out
        out[1, :, :] = r.moment[...]
        out[2, pl.ds(GAIN_BASE, 16), :] = jnp.zeros((16, LANES), F32)
        gather.drain()
        update.drain()
        update.take_all()
        update.drain_owner()
    else:
        finish_acts()
        keep_ag.start()
        memory_back(0, samples // 2)
        for part in range(samples // batch):
            turn_back(part, 0, chunks)
    for copy in (keep_out, keep_ag, *(keep_og(part) for part in range(samples // batch))):
        copy.wait()


def block_and_back(remote, acts, obs, flags, levels, cot, sqw, mlpw, gain, sqm=None, mlpm=None):
    tokens, width = acts.shape
    keys, samples = obs.shape[0], obs.shape[1]
    rows = HEADS * ACT
    wide = mlpw.shape[2]
    any_space = pl.BlockSpec(memory_space=pl.ANY)
    in_vmem = pl.BlockSpec(memory_space=VMEM)
    sem = pltpu.SemaphoreType.DMA
    ins = dict(flags=flags, levels=levels, acts=acts, obs=obs, cot=cot, sqw=sqw, mlpw=mlpw, gain=gain)
    outs = dict(
        output=jax.ShapeDtypeStruct(acts.shape, F32),
        ag=jax.ShapeDtypeStruct(acts.shape, F32),
        og=jax.ShapeDtypeStruct(obs.shape, BF16),
    )
    grads = GRID + (WIRE, LANES)
    scratch = dict(
        obs_v=VMEM((KEYS_PAD, samples, width), BF16),
        acts_v=VMEM(acts.shape, F32),
        cot_v=VMEM(acts.shape, F32),
        mem=VMEM((samples, KEYS_PAD, width), BF16),
        swap=VMEM((256, 256), BF16),
        sq_all=VMEM((5, width, width), BF16),
        mlp_all=VMEM((2, width, wide), BF16),
        gain_all=VMEM((2, width), F32),
        wkh=VMEM((HEADS * width, width), BF16),
        wvh=VMEM((HEADS * width, width), BF16),
        first=VMEM((tokens, width), BF16),
        query=VMEM((tokens, width), BF16),
        xhat=VMEM((tokens, width), F32),
        rstd=VMEM((tokens, 1), F32),
        probs=VMEM((samples, rows, KEYS_PAD), F32),
        pds_v=VMEM((samples, 2 * rows, KEYS_PAD), BF16),
        sides_v=VMEM((samples, 2 * rows, width), BF16),
        u=VMEM((tokens, HEADS * width), BF16),
        dq_wide=VMEM((tokens, HEADS * width), BF16),
        mixed=VMEM((tokens, width), BF16),
        second=VMEM((tokens, width), BF16),
        active=VMEM((tokens, wide), BF16),
        dhidden=VMEM((tokens, wide), BF16),
        out_low=VMEM((tokens, width), BF16),
        dres_low=VMEM((tokens, width), BF16),
        dres=VMEM((tokens, width), F32),
        resid=VMEM((tokens, width), F32),
        hat_two=VMEM((tokens, width), F32),
        rstd_two=VMEM((tokens, 1), F32),
        slope=VMEM((tokens, wide), F32),
        dmixed=VMEM((tokens, width), BF16),
        dquery=VMEM((tokens, width), BF16),
        out_v=VMEM((tokens, width), F32),
        ag_v=VMEM((tokens, width), F32),
        angle=VMEM((samples, width // 2), F32),
        embed=VMEM((samples, width), BF16),
        stamps=VMEM((samples, 8, width), F32),
        gain_acc=VMEM((8, width), F32),
        flags_s=pltpu.SMEM(flags.shape, jnp.int32),
        levels_s=pltpu.SMEM(levels.shape, jnp.int32),
        in_sems=sem((10,)),
        out_sems=sem((2 + samples // 16,)),
    )
    extra = {}
    if remote:
        ins.update(sqm=sqm, mlpm=mlpm)
        outs.update(out=jax.ShapeDtypeStruct((3, WIRE, LANES), F32))
        chunks = len(CHUNKS)
        scratch.update(
            grads=VMEM(grads, F32),
            sqw_v=VMEM(sqw.shape, F32),
            mlpw_v=VMEM(mlpw.shape, F32),
            gain_v=VMEM(gain.shape, F32),
            sqm_v=VMEM(sqm.shape, F32),
            mlpm_v=VMEM(mlpm.shape, F32),
            wire=VMEM(grads, BF16),
            edge=VMEM((16, LANES), F32),
            gsend=sem((len(PIECES), 6)),
            grecv=sem((len(PIECES), 6)),
            send0=VMEM((4, 2, 2, WIRE, LANES), BF16),
            got_core=VMEM((4, 2, 2, WIRE, LANES), BF16),
            sum1=VMEM((4, 2, 2, WIRE, LANES), F32),
            send1=VMEM((4, 2, WIRE, LANES), BF16),
            got1=VMEM((4, 2, WIRE, LANES), BF16),
            sum2=VMEM((4, 2, WIRE, LANES), F32),
            send2=VMEM((4, WIRE, LANES), BF16),
            got2=VMEM((4, WIRE, LANES), BF16),
            sum3=VMEM((4, WIRE, LANES), F32),
            send3=VMEM((4, WIRE, LANES), BF16),
            got3=VMEM((3, WIRE, LANES), BF16),
            moment=VMEM((WIRE, LANES), F32),
            slabs_sq=VMEM((4, 8, 4, SQ_ROWS, LANES), BF16),
            slabs_mlp=VMEM((32, MLP_ROWS, LANES), BF16),
            moment_low=VMEM((2 * MLP_ROWS, LANES), BF16),
            back_mlp=VMEM((2, MLP_ROWS, LANES), BF16),
            back_sq=VMEM((5, SQ_ROWS, LANES), BF16),
            result_sq=VMEM((32, SQ_ROWS, LANES), BF16),
            result_mlp=VMEM((32, MLP_ROWS, LANES), BF16),
            cur=VMEM((width, wide), F32),
            cur_low=VMEM((width, wide), BF16),
            send=sem((chunks, 6)),
            recv=sem((chunks, 6)),
            own_send=sem((len(PARTS_OUT),)),
            own_recv=sem((1,)),
            back_send=sem((32,)),
            back_recv=sem((7,)),
        )
        extra = dict(collective_id=0, has_side_effects=True)
        outs = {name: VMEM(like.shape, like.dtype) for name, like in outs.items()}
    else:
        outs.update(grads=jax.ShapeDtypeStruct(grads, F32))
    names = tuple(ins) + tuple(outs) + tuple(scratch)
    stay = [pltpu.with_memory_space_constraint(value, pltpu.HBM) for value in ins.values()]
    results = pl.pallas_call(
        functools.partial(block_kernel, names, remote),
        out_shape=tuple(outs.values()),
        in_specs=[any_space] * len(ins),
        out_specs=[any_space] * 3 + [in_vmem],
        scratch_shapes=list(scratch.values()),
        compiler_params=pltpu.CompilerParams(vmem_limit_bytes=52 << 20, **extra),
        name="block_and_back",
    )(*stay)
    return Refs(zip(outs, results))


PARTS = 7


def finish_kernel(names, rate, *args):
    r = Refs(zip(names, args))
    sems = r.sems
    keys = r.og.shape[0]
    step = keys // PARTS

    def leave(part):
        block = pl.ds(part * step, step)
        return pltpu.make_async_copy(r.og_v.at[block], r.og.at[block], sems.at[part])

    more = PARTS
    moves = []
    if hasattr(r, "wire"):
        pairs = [(r.sqw, r.sqw_v), (r.mlpw, r.mlpw_v), (r.gain, r.gain_v), (r.gainm, r.gainm_v)]
        pairs += [(r.output, r.output_f), (r.ag, r.ag_f)]
        for source, target in pairs:
            moves.append(pltpu.make_async_copy(source, target, sems.at[more]))
            moves[-1].start()
            more += 1
    for part in range(PARTS):

        def widen(j, _):
            r.og_v[j] = r.low[j].astype(F32)
            return 0

        lax.fori_loop(part * step, (part + 1) * step, widen, 0, unroll=4)
        leave(part).start()
    for copy in moves[:4]:
        copy.wait()
    if hasattr(r, "wire"):
        finish_weights(r, rate)
    for part in range(PARTS):
        leave(part).wait()
    for copy in moves[4:]:
        copy.wait()


def finish_weights(r, rate):
    wire = r.wire
    me = lax.axis_index("dp")
    for m in range(5):
        for j in range(2):
            rows, columns = pl.ds(SQ_AT[m] + j * TILE, TILE), pl.ds(j * LANES, LANES)
            r.sqg[m, :, columns] = wire[0, rows, :]
            r.sqm[m, :, columns] = wire[1, rows, :]
            r.sqn[m, :, columns] = r.sqw_v[m, :, columns] - SQ_RATES[m] * wire[2, rows, :]
    r.sqc[...] = r.sqn[...].astype(BF16)
    for m in range(2):
        for j in range(8):
            rows, columns = pl.ds(m * MLP_ROWS + j * TILE, TILE), pl.ds(j * LANES, LANES)
            r.mlpg[m, :, columns] = wire[0, rows, :]
            r.mlpm[m, :, columns] = wire[1, rows, :]
            r.mlpn[m, :, columns] = r.mlpw_v[m, :, columns] - MLP_RATES[m] * wire[2, rows, :]
    r.mlpc[...] = r.mlpn[...].astype(BF16)
    tile = wire[0, pl.ds(GAIN_BASE, TILE), :]
    turned = pltpu.roll(tile, (LANES - (me % 16) * TILE) % LANES, 1)
    at = me // 16
    for norm in range(2):
        pair = turned[2 * norm : 2 * norm + 2, 0:TILE]
        row = jnp.where(at == 0, pair[0:1, :], pair[1:2, :])
        new = 0.5 * r.gainm_v[norm : norm + 1, :] + row
        r.gg[norm : norm + 1, :] = row
        r.gm[norm : norm + 1, :] = new
        r.gn[norm : norm + 1, :] = r.gain_v[norm : norm + 1, :] - rate * new


def finish(rate, made, sqw=None, mlpw=None, gain=None, gainm=None):
    any_space = pl.BlockSpec(memory_space=pl.ANY)
    in_vmem = pl.BlockSpec(memory_space=VMEM)
    ins = dict(low=made.og)
    outs = dict(og=jax.ShapeDtypeStruct(made.og.shape, F32))
    near, far = 1, 1
    if hasattr(made, "out"):
        ins.update(output=made.output, ag=made.ag, wire=made.out, sqw=sqw, mlpw=mlpw, gain=gain, gainm=gainm)
        like = jax.ShapeDtypeStruct
        near, far = 4, 3
        outs.update(
            output_f=like(made.output.shape, F32),
            ag_f=like(made.ag.shape, F32),
            sqg=like(sqw.shape, F32),
            sqm=like(sqw.shape, F32),
            sqn=like(sqw.shape, F32),
            sqc=like(sqw.shape, BF16),
            mlpg=like(mlpw.shape, F32),
            mlpm=like(mlpw.shape, F32),
            mlpn=like(mlpw.shape, F32),
            mlpc=like(mlpw.shape, BF16),
            gg=like(gain.shape, F32),
            gm=like(gain.shape, F32),
            gn=like(gain.shape, F32),
        )
    scratch = dict(
        og_v=VMEM(made.og.shape, F32),
        sems=pltpu.SemaphoreType.DMA((PARTS + 6,)),
    )
    if hasattr(made, "out"):
        scratch.update(
            sqw_v=VMEM(sqw.shape, F32),
            mlpw_v=VMEM(mlpw.shape, F32),
            gain_v=VMEM(gain.shape, F32),
            gainm_v=VMEM(gainm.shape, F32),
        )
    names = tuple(ins) + tuple(outs) + tuple(scratch)
    made_here = list(ins.values())
    stay = [pltpu.with_memory_space_constraint(value, pltpu.HBM) for value in made_here[near:]]
    results = pl.pallas_call(
        functools.partial(finish_kernel, names, rate),
        out_shape=tuple(outs.values()),
        in_specs=[in_vmem] * near + [any_space] * (len(ins) - near),
        out_specs=[any_space] * far + [in_vmem] * (len(outs) - far),
        scratch_shapes=list(scratch.values()),
        compiler_params=pltpu.CompilerParams(vmem_limit_bytes=16 << 20),
        name="finish",
    )(*made_here[:near], *stay)
    return Refs(zip(outs, results))


HIGH_PRECISION = lax.Precision.HIGHEST


def plain_orthogonalize(matrix):
    current = matrix / (jnp.sqrt(jnp.sum(matrix * matrix)) + 1e-07)
    for turn in range(5):
        gram = jnp.dot(current, current.T, precision=HIGH_PRECISION)
        poly = COEF_B * gram + COEF_C * jnp.dot(gram, gram, precision=HIGH_PRECISION)
        current = COEF_A * current + jnp.dot(poly, current, precision=HIGH_PRECISION)
    return current


def pick_owned(stack, owners, device):
    chosen = jnp.zeros_like(stack[0])
    for index in range(len(owners)):
        chosen = jnp.where(device == owners[index], stack[index], chosen)
    return chosen


def is_owner(owners, device):
    flag = device < 0
    for owner in owners:
        flag = jnp.logical_or(flag, device == owner)
    return flag


def from_wire(grads):
    def matrix(base, tiles):
        part = grads[:, base : base + tiles * TILE, :].reshape(-1, tiles, TILE, LANES)
        return part.transpose(0, 2, 1, 3).reshape(-1, tiles * LANES)

    square = jnp.stack([matrix(SQ_AT[m], 2) for m in range(5)])
    mlp = jnp.stack([matrix(m * MLP_ROWS, 8) for m in range(2)])
    return square, mlp, grads[0, GAIN_BASE : GAIN_BASE + 4, :].reshape(2, 2 * LANES)


def update_by_collectives(
    grads, square_weights, mlp_weights, gains, square_moment, mlp_moment, gain_moment, rate
):
    square_local, mlp_local, gain_local = from_wire(grads)
    square_grad, mlp_grad, gain_grad = (
        lax.psum_scatter(square_local, "dp", scatter_dimension=1, tiled=True),
        lax.psum_scatter(mlp_local, "dp", scatter_dimension=1, tiled=True),
        lax.psum_scatter(gain_local, "dp", scatter_dimension=1, tiled=True),
    )
    square_moment_new = 0.5 * square_moment + square_grad
    mlp_moment_new = 0.5 * mlp_moment + mlp_grad
    gain_moment_new = 0.5 * gain_moment + gain_grad
    device = lax.axis_index("dp")
    count = lax.axis_size("dp")
    square_owners = [index * count // 7 for index in range(5)]
    mlp_owners = [(index + 5) * count // 7 for index in range(2)]
    square_full, mlp_full = (
        lax.all_gather(square_moment_new, "dp", axis=1, tiled=True),
        lax.all_gather(mlp_moment_new, "dp", axis=1, tiled=True),
    )
    mine_square = pick_owned(square_full, square_owners, device)
    mine_mlp = pick_owned(mlp_full, mlp_owners, device)
    made_square = lax.cond(
        is_owner(square_owners, device), plain_orthogonalize, jnp.zeros_like, mine_square
    )
    made_mlp = lax.cond(is_owner(mlp_owners, device), plain_orthogonalize, jnp.zeros_like, mine_mlp)
    stack_square = jnp.stack(
        [jnp.where(device == owner, made_square, 0.0) for owner in square_owners]
    )
    stack_mlp = jnp.stack([jnp.where(device == owner, made_mlp, 0.0) for owner in mlp_owners])
    square_ortho, mlp_ortho = (
        lax.psum_scatter(stack_square, "dp", scatter_dimension=1, tiled=True),
        lax.psum_scatter(stack_mlp, "dp", scatter_dimension=1, tiled=True),
    )
    square_new = square_weights - jnp.array(SQ_RATES, F32)[:, None, None] * square_ortho
    mlp_new = mlp_weights - jnp.array(MLP_RATES, F32)[:, None, None] * mlp_ortho
    gains_new = gains - rate * gain_moment_new
    return (
        square_grad,
        square_moment_new,
        square_new,
        square_new.astype(BF16),
        mlp_grad,
        mlp_moment_new,
        mlp_new,
        mlp_new.astype(BF16),
        gain_grad,
        gain_moment_new,
        gains_new,
    )


def per_device(
    actions,
    observed,
    camera_flags,
    noise_levels,
    cotangent,
    square_weights,
    mlp_weights,
    gains,
    square_moment,
    mlp_moment,
    gain_moment,
):
    count = lax.axis_size("dp")
    rate = 0.1 / math.sqrt(actions.shape[0] * count)
    by_key = observed.transpose(1, 0, 2)
    ins = (actions, by_key, camera_flags, noise_levels, cotangent)
    if count == math.prod(GRID):
        made = block_and_back(True, *ins, square_weights, mlp_weights, gains, square_moment, mlp_moment)
        done = finish(rate, made, square_weights, mlp_weights, gains, gain_moment)
        output, actions_grad = done.output_f, done.ag_f
        d = done
        rest = (d.sqg, d.sqm, d.sqn, d.sqc, d.mlpg, d.mlpm, d.mlpn, d.mlpc, d.gg, d.gm, d.gn)
    else:
        square_all, mlp_all = (
            lax.all_gather(square_weights.astype(BF16), "dp", axis=1, tiled=True),
            lax.all_gather(mlp_weights.astype(BF16), "dp", axis=1, tiled=True),
        )
        gain_all = lax.all_gather(gains, "dp", axis=1, tiled=True)
        made = block_and_back(False, *ins, square_all, mlp_all, gain_all)
        done = finish(rate, made)
        output, actions_grad = made.output, made.ag
        grads = made.grads.reshape(-1, WIRE, LANES)
        rest = update_by_collectives(
            grads, square_weights, mlp_weights, gains, square_moment, mlp_moment, gain_moment, rate
        )
    observed_grad = done.og.transpose(1, 0, 2)
    return (output, actions_grad, observed_grad) + tuple(rest)


def solution(mesh):
    rows, cube, flat = P("dp", None), P("dp", None, None), P("dp")
    stacked, pair = P(None, "dp", None), P(None, "dp")
    return jax.shard_map(
        per_device,
        mesh=mesh,
        in_specs=(rows, cube, flat, flat, rows, stacked, stacked, pair, stacked, stacked, pair),
        out_specs=(rows, rows, cube) + (stacked,) * 8 + (pair,) * 3,
        check_vma=False,
    )
```

```python
import functools
import math

import jax
import jax.numpy as jnp
from jax import lax
from jax.experimental import pallas as pl
from jax.experimental.pallas import tpu as pltpu
from jax.sharding import PartitionSpec as P

HEADS = 4
ACT = 16
OBS_FULL = 196
OBS_FEW = 49
COEF_A = 3.4445
COEF_B = -4.775
COEF_C = 2.0315
F32 = jnp.float32
BF16 = jnp.bfloat16
MESH = pl.DeviceIdType.MESH
VMEM = pltpu.VMEM
NN = (((1,), (0,)), ((), ()))
NT = (((1,), (1,)), ((), ()))
TN = (((0,), (0,)), ((), ()))

LANES = 128
TILE = 8
MLP_ROWS = 64
SQ_ROWS = 16
SQ_AT = (160, 192, 176, 128, 144)
GAIN_BASE = 208
WIRE = 224
PIECES = ((0, 32), (32, 32), (64, 32), (96, 32), (128, 32), (160, 32), (192, 32))
PIECE_X_FIRST = (True, False, True, False, True, True, False)
CHUNKS = ((0, 32), (32, 32), (64, 32), (96, 32), (128, 32), (160, 32), (192, 16), (208, 16))
X_FIRST = (True, False, True, False, True, False, True, False)
PARTS_OUT = (
    (0, 0, 0, 32, 0),
    (1, 0, 32, 32, 32),
    (2, 1, 64, 32, 0),
    (3, 1, 96, 32, 32),
    (4, 5, 128, 16, 0),
    (4, 6, 144, 16, 0),
    (5, 2, 160, 16, 0),
    (5, 4, 176, 16, 0),
    (6, 3, 192, 16, 0),
)
MLP_RATES = (1.0, 0.5)
SQ_RATES = (0.5, 0.5, 0.5, 0.5, 4.0)
GRID = (4, 2, 2, 2)
OWNERS = (8, 22, 14, 16, 11, 21, 13)
SHIFTS = (0.0, 0.0, 0.4, 0.8, 0.8)
KEYS_PAD = 208
GROUP = 16
ROWS = 512


class Refs:
    def __init__(self, pairs):
        self.__dict__.update(pairs)


def dot(left, right, dims=NN):
    return lax.dot_general(left, right, dims, preferred_element_type=F32)


def place():
    me = lax.axis_index("dp")
    return me, me // 8, (me // 4) % 2, (me // 2) % 2, me % 2


def device_at(z, y, x, c):
    return ((z * 2 + y) * 2 + x) * 2 + c


def link(src, dst, send, recv, device):
    return pltpu.make_async_remote_copy(
        src_ref=src,
        dst_ref=dst,
        send_sem=send,
        recv_sem=recv,
        device_id=(device,),
        device_id_type=MESH,
    )


def greet(device):
    pl.semaphore_signal(
        pltpu.get_barrier_semaphore(), inc=1, device_id=(device,), device_id_type=MESH
    )


def normalize(values):
    centred = values - jnp.mean(values, -1, keepdims=True)
    scale = lax.rsqrt(jnp.mean(centred * centred, -1, keepdims=True) + 1e-05)
    return centred * scale, scale


def norm_back(grad, hat, scale):
    mean_one = jnp.mean(grad, -1, keepdims=True)
    mean_two = jnp.mean(grad * hat, -1, keepdims=True)
    return scale * (grad - mean_one - hat * mean_two)


class Gather:
    def __init__(self, r):
        self.r = r
        self.me, self.z, self.y, self.x, self.c = place()

    def hop(self, k, step, part, device):
        return link(part, part, self.r.gsend.at[k, step], self.r.grecv.at[k, step], device)

    def along_z(self, k, step):
        part = self.r.wire.at[self.z, self.y, self.x, self.c, pl.ds(*PIECES[k])]
        return self.hop(k, step, part, device_at((self.z + step + 1) % 4, self.y, self.x, self.c))

    def from_z(self, k, step):
        there = (self.z + 3 - step) % 4
        part = self.r.wire.at[there, self.y, self.x, self.c, pl.ds(*PIECES[k])]
        return self.hop(k, step, part, device_at(there, self.y, self.x, self.c))

    def plane(self, k, second, mine):
        z, y, x, c = self.z, self.y, self.x, self.c
        rows, wire = pl.ds(*PIECES[k]), self.r.wire
        py, px = (y, x) if mine else (1 - y, 1 - x)
        along_x = PIECE_X_FIRST[k] == second
        if along_x:
            part = wire.at[:, y, px, c, rows] if second else wire.at[:, :, px, c, rows]
            return self.hop(k, 3 if second else 4, part, device_at(z, y, 1 - x, c))
        part = wire.at[:, py, x, c, rows] if second else wire.at[:, py, :, c, rows]
        return self.hop(k, 3 if second else 4, part, device_at(z, 1 - y, x, c))

    def core(self, k, mine):
        part = self.r.wire.at[:, :, :, self.c if mine else 1 - self.c, pl.ds(*PIECES[k])]
        return self.hop(k, 5, part, device_at(self.z, self.y, self.x, 1 - self.c))

    def first(self, *chunks):
        for k in chunks:
            for step in range(3):
                self.along_z(k, step).start()

    def second(self, *chunks):
        for k in chunks:
            for step in range(3):
                self.from_z(k, step).wait_recv()
            self.plane(k, True, True).start()

    def third(self, *chunks):
        for k in chunks:
            self.plane(k, True, False).wait_recv()
            self.plane(k, False, True).start()

    def fourth(self, *chunks):
        for k in chunks:
            self.plane(k, False, False).wait_recv()
            self.core(k, True).start()

    def last(self, *chunks):
        for k in chunks:
            self.core(k, False).wait_recv()

    def drain(self):
        for k in range(len(PIECES)):
            for step in range(3):
                self.along_z(k, step).wait_send()
            self.plane(k, True, True).wait_send()
            self.plane(k, False, True).wait_send()
            self.core(k, True).wait_send()

    def fill(self):
        r = self.r
        spot = (self.z, self.y, self.x, self.c)

        def tiles(source, m, base, number):
            for j in range(number):
                pair = [source[m, :, pl.ds((2 * j + k) * LANES, LANES)] for k in range(2)]
                r.wire[spot + (pl.ds(base + j * 16, 16),)] = jnp.concatenate(pair, axis=0).astype(BF16)

        for m in range(5):
            tiles(r.sqw_v, m, SQ_AT[m], 1)
        for m in range(2):
            tiles(r.mlpw_v, m, m * MLP_ROWS, 4)
        gains, edge = r.gain_v[...], r.edge
        high = gains.astype(BF16).astype(F32)
        middle = (gains - high).astype(BF16).astype(F32)
        edge[...] = jnp.zeros_like(edge)
        edge[0:2, 0:TILE] = high
        edge[2:4, 0:TILE] = middle
        edge[4:6, 0:TILE] = (gains - high - middle).astype(BF16).astype(F32)
        r.wire[spot + (pl.ds(GAIN_BASE, 16),)] = edge[...].astype(BF16)

    def unpack(self, base, number, out, m):
        for j in range(number):
            block = self.r.wire[:, :, :, :, pl.ds(base + j * 16, 16), :].reshape(32, 16, LANES).astype(F32)
            for half in range(2):
                columns = pl.ds((2 * j + half) * LANES, LANES)
                out[m, :, columns] = block[:, half * 8 : half * 8 + 8, :].reshape(256, LANES).astype(BF16)

    def unpack_gains(self):
        edge, wire = self.r.edge, self.r.wire
        for half in range(2):
            total = jnp.zeros((16, LANES), F32)
            for at in range(16):
                d = half * 16 + at
                tile = wire[d // 8, (d // 4) % 2, (d // 2) % 2, d % 2, pl.ds(GAIN_BASE, 16), :].astype(F32)
                total = total + (tile if at == 0 else pltpu.roll(tile, at * TILE, 1))
            edge[...] = total
            self.r.gain_all[:, pl.ds(half * LANES, LANES)] = edge[0:2, :] + edge[2:4, :] + edge[4:6, :]


class Update:
    def __init__(self, r):
        self.r = r
        self.me, self.z, self.y, self.x, self.c = place()

    def hop(self, k, step, src, dst, device):
        return link(src, dst, self.r.send.at[k, step], self.r.recv.at[k, step], device)

    def core(self, k):
        rows = pl.ds(*CHUNKS[k])
        src, dst = self.r.send0.at[:, :, :, rows], self.r.got_core.at[:, :, :, rows]
        return self.hop(k, 0, src, dst, device_at(self.z, self.y, self.x, 1 - self.c))

    def plane(self, k, first):
        rows = pl.ds(*CHUNKS[k])
        to = (self.z, self.y, 1 - self.x, self.c) if X_FIRST[k] == first else (self.z, 1 - self.y, self.x, self.c)
        if first:
            src, dst = self.r.send1.at[:, :, rows], self.r.got1.at[:, :, rows]
        else:
            src, dst = self.r.send2.at[:, rows], self.r.got2.at[:, rows]
        return self.hop(k, 1 if first else 2, src, dst, device_at(*to))

    def along_z(self, k, step):
        rows = pl.ds(*CHUNKS[k])
        there = (self.z + step + 1) % 4
        src, dst = self.r.send3.at[there, rows], self.r.got3.at[step, rows]
        return self.hop(k, 3 + step, src, dst, device_at(there, self.y, self.x, self.c))

    def start(self, k):
        rows = pl.ds(*CHUNKS[k])
        self.r.send0[:, :, :, rows, :] = self.r.grads[:, :, :, 1 - self.c, rows, :].astype(BF16)
        self.core(k).start()

    def one(self, *chunks):
        r = self.r
        for k in chunks:
            rows = pl.ds(*CHUNKS[k])
            self.core(k).wait_recv()
            sum1 = r.sum1
            sum1[:, :, :, rows, :] = r.grads[:, :, :, self.c, rows, :] + r.got_core[:, :, :, rows, :].astype(F32)
            other = sum1[:, :, 1 - self.x, rows, :] if X_FIRST[k] else sum1[:, 1 - self.y, :, rows, :]
            r.send1[:, :, rows, :] = other.astype(BF16)
            self.plane(k, True).start()

    def two(self, *chunks):
        r = self.r
        for k in chunks:
            rows = pl.ds(*CHUNKS[k])
            self.plane(k, True).wait_recv()
            sum1, sum2 = r.sum1, r.sum2
            mine = sum1[:, :, self.x, rows, :] if X_FIRST[k] else sum1[:, self.y, :, rows, :]
            sum2[:, :, rows, :] = mine + r.got1[:, :, rows, :].astype(F32)
            other = 1 - self.y if X_FIRST[k] else 1 - self.x
            r.send2[:, rows, :] = sum2[:, other, rows, :].astype(BF16)
            self.plane(k, False).start()

    def three(self, *chunks):
        r = self.r
        for k in chunks:
            rows = pl.ds(*CHUNKS[k])
            self.plane(k, False).wait_recv()
            mine = self.y if X_FIRST[k] else self.x
            total = r.sum2[:, mine, rows, :] + r.got2[:, rows, :].astype(F32)
            r.sum3[:, rows, :] = total
            r.send3[:, rows, :] = total.astype(BF16)
            if k >= 4:
                own = r.sum3[self.z, rows, :] + 0.5 * r.moment[rows, :]
                r.send3[self.z, rows, :] = own.astype(BF16)
                self.parts_to_owners(k)
            for step in range(3):
                self.along_z(k, step).start()

    def parts_to_owners(self, k):
        for part, (chunk, index, *_) in enumerate(PARTS_OUT):
            if chunk != k:
                continue

            @pl.when(self.me != OWNERS[index])
            def _():
                self.to_owner(part).start()

            @pl.when(self.me == OWNERS[index])
            def _():
                src, dst = self.own_part(part)
                pltpu.make_async_copy(src, dst, self.r.own_recv.at[0]).start()

    def result(self, index):
        return self.r.result_mlp if index < 2 else self.r.result_sq

    def own_part(self, part):
        _, index, base, number, place = PARTS_OUT[part]
        if index < 2:
            return self.r.moment_low.at[pl.ds(base, number)], self.r.slabs_mlp.at[self.me, pl.ds(place, number)]
        return self.r.send3.at[:, pl.ds(base, number)], self.r.slabs_sq.at[self.z, self.me % 8]

    def to_owner(self, part):
        src, dst = self.own_part(part)
        return link(src, dst, self.r.own_send.at[part], self.r.own_recv.at[0], OWNERS[PARTS_OUT[part][1]])

    def four(self, *chunks):
        r = self.r
        moment, out = r.moment, r.out
        for k in chunks:
            rows = pl.ds(*CHUNKS[k])
            total = r.sum3[self.z, rows, :]
            for step in range(3):
                self.along_z(k, step).wait_recv()
                total = total + r.got3[step, rows, :].astype(F32)
            out[0, rows, :] = total
            new = 0.5 * moment[rows, :] + total
            moment[rows, :] = new
            if k < 4:
                r.moment_low[rows, :] = new.astype(BF16)
            if k < 4:
                self.parts_to_owners(k)

    def old_moment(self):
        r = self.r
        moment = r.moment
        for m in range(2):
            for j in range(8):
                moment[pl.ds(m * MLP_ROWS + j * TILE, TILE), :] = r.mlpm_v[m, :, pl.ds(j * LANES, LANES)]
        for m in range(5):
            for j in range(2):
                moment[pl.ds(SQ_AT[m] + j * TILE, TILE), :] = r.sqm_v[m, :, pl.ds(j * LANES, LANES)]
        moment[pl.ds(GAIN_BASE, 16), :] = jnp.zeros((16, LANES), F32)

    def orthogonalize(self):
        r = self.r
        cur = r.cur
        rows = lax.broadcasted_iota(jnp.int32, (256, 256), 0)
        diagonal = rows == lax.broadcasted_iota(jnp.int32, (256, 256), 1)

        low = r.cur_low

        def load(rows, j, pair):
            for side in range(2):
                columns = pl.ds((2 * j + side) * LANES, LANES)
                part = pair[:, side * TILE : (side + 1) * TILE, :].reshape(-1, LANES)
                cur[rows, columns] = part
                low[rows, columns] = part.astype(BF16)

        def load_mlp():
            for j in range(4):
                load(pl.ds(0, 256), j, r.slabs_mlp[:, pl.ds(j * 16, 16), :].astype(F32))

        def load_sq():
            for to in range(4):
                pair = r.slabs_sq[0, :, to].astype(F32)
                for plane in range(1, 4):
                    pair = pair + r.slabs_sq[plane, :, to].astype(F32)
                load(pl.ds(to * 64, 64), 0, pair)

        def run(slabs, fetch, result, tiles):
            pltpu.make_async_copy(slabs, slabs, r.own_recv.at[0]).wait()
            fetch()
            scale = 1.0
            for turn, shift in enumerate(SHIFTS):
                whole = low[:, 0 : tiles * LANES]
                off = dot(whole, whole, NT)
                if turn == 0:
                    norm = jnp.sum(jnp.sum(jnp.where(diagonal, off, 0.0), axis=0, keepdims=True), axis=1, keepdims=True)
                    scale = 1.0 / (jnp.sqrt(norm) + 1e-07)
                    off = off * (scale * scale)
                if shift:
                    off = off - jnp.where(diagonal, shift, 0.0)
                off_low = off.astype(BF16)
                poly = (COEF_B + 2.0 * COEF_C * shift) * off + COEF_C * dot(off_low, off_low)
                poly = poly.astype(BF16)
                keep = COEF_A + shift * (COEF_B + COEF_C * shift)
                for j in range(tiles // 2):
                    columns = pl.ds(j * 2 * LANES, 2 * LANES)
                    now = keep * cur[:, columns] + dot(poly, low[:, columns])
                    if turn == 0:
                        now = now * scale
                    if turn < len(SHIFTS) - 1:
                        cur[:, columns] = now
                        low[:, columns] = now.astype(BF16)
                    else:
                        parts = [now[:, side * LANES : (side + 1) * LANES].reshape(32, TILE, LANES) for side in range(2)]
                        result[:, pl.ds(j * 16, 16), :] = jnp.concatenate(parts, axis=1).astype(result.dtype)

        mine_mlp = jnp.logical_or(self.me == OWNERS[0], self.me == OWNERS[1])
        mine_sq = self.me < 0
        for device in OWNERS[2:]:
            mine_sq = jnp.logical_or(mine_sq, self.me == device)

        @pl.when(mine_mlp)
        def _():
            run(r.slabs_mlp, load_mlp, r.result_mlp, 8)

        @pl.when(mine_sq)
        def _():
            run(r.slabs_sq, load_sq, r.result_sq, 2)

    def landing(self, index):
        if index < 2:
            return self.r.back_mlp.at[index]
        return self.r.back_sq.at[index - 2]

    def give_back(self, index, device):
        result = self.result(index)
        return link(
            result.at[device], self.landing(index),
            self.r.back_send.at[device], self.r.back_recv.at[index], device,
        )

    def give_all(self):
        r = self.r
        for index in range(7):
            result = self.result(index)

            @pl.when(self.me == OWNERS[index])
            def _():
                def send_one(step, _):
                    self.give_back(index, step + (step + 32 - self.me) // 32).start()
                    return 0

                lax.fori_loop(0, 31, send_one, 0)
                pltpu.make_async_copy(result.at[self.me], self.landing(index), r.back_recv.at[index]).start()

    def take_all(self):
        for index in range(7):
            result = self.result(index)
            pltpu.make_async_copy(result.at[0], self.landing(index), self.r.back_recv.at[index]).wait()
        for index in range(2):
            rows = pl.ds(index * MLP_ROWS, MLP_ROWS)
            self.r.out[2, rows, :] = self.r.back_mlp[index].astype(F32)
        for index in range(5):
            self.r.out[2, pl.ds(SQ_AT[index], SQ_ROWS), :] = self.r.back_sq[index].astype(F32)

    def drain(self):
        for k in range(len(CHUNKS)):
            self.core(k).wait_send()
            self.plane(k, True).wait_send()
            self.plane(k, False).wait_send()
            for step in range(3):
                self.along_z(k, step).wait_send()
        for part in range(len(PARTS_OUT)):

            @pl.when(self.me != OWNERS[PARTS_OUT[part][1]])
            def _():
                self.to_owner(part).wait_send()

    def drain_owner(self):
        for index in range(7):

            @pl.when(self.me == OWNERS[index])
            def _():
                def wait_one(step, _):
                    self.give_back(index, step + (step + 32 - self.me) // 32).wait_send()
                    return 0

                lax.fori_loop(0, 31, wait_one, 0)


def greet_all():
    me, z, y, x, c = place()
    greet(device_at(z, y, x, 1 - c))
    greet(device_at(z, y, 1 - x, c))
    greet(device_at(z, 1 - y, x, c))
    for step in range(1, 4):
        greet(device_at((z + step) % 4, y, x, c))
    owner = me < 0
    for device in OWNERS:
        owner = jnp.logical_or(owner, me == device)

        @pl.when(me != device)
        def _():
            greet(device)

    @pl.when(owner)
    def _():
        def greet_other(step, _):
            greet((me + step) % 32)
            return 0

        lax.fori_loop(1, 32, greet_other, 0)

    is_owner = owner.astype(jnp.int32)
    return 6 + 7 - is_owner + 31 * is_owner


def block_kernel(names, remote, *args):
    r = Refs(zip(names, args))
    keys, samples = r.obs.shape[0], r.obs.shape[1]
    tokens, width = r.acts.shape
    head_dim, half, per = width // HEADS, width // 2, ROWS // ACT
    wide = r.mlp_all.shape[2]
    groups = samples // GROUP
    in_sems, out_sems = r.in_sems, r.out_sems

    if remote:
        own = (r.sqw_v, r.mlpw_v, r.gain_v)
    else:
        own = (r.sq_all, r.mlp_all, r.gain_all)
    loads = list(zip((r.sqw, r.mlpw, r.gain), own))
    loads += [(r.acts, r.acts_v), (r.obs, r.obs_v.at[pl.ds(0, keys)]), (r.cot, r.cot_v)]
    if remote:
        loads += [(r.sqm, r.sqm_v), (r.mlpm, r.mlpm_v)]
    loads += [(r.flags, r.flags_s), (r.levels, r.levels_s)]
    copies = [pltpu.make_async_copy(a, b, in_sems.at[i]) for i, (a, b) in enumerate(loads)]

    def arrive(*which):
        for i in which:
            copies[i].wait()

    for copy in copies:
        copy.start()
    if remote:
        gather, update = Gather(r), Update(r)
        expected = greet_all()
        arrive(0, 1, 2)
        gather.fill()
        pl.semaphore_wait(pltpu.get_barrier_semaphore(), expected)
        gather.first(5, 6, 4, 0, 1, 2, 3)

    arrive(3)

    def hats(i, _):
        rows = pl.ds(pl.multiple_of(i * ROWS, ROWS), ROWS)
        hat, scale = normalize(r.acts_v[rows, :])
        r.xhat[rows, :] = hat
        r.rstd[rows, :] = scale
        return 0

    lax.fori_loop(0, tokens // ROWS, hats, 0)

    mem, obs_v = r.mem, r.obs_v
    batch = 16
    chunks = KEYS_PAD // batch
    swap = r.swap
    row = lax.broadcasted_iota(jnp.int32, swap.shape, 0)
    column = lax.broadcasted_iota(jnp.int32, swap.shape, 1)
    swap[...] = jnp.where(column == (row % batch) * batch + row // batch, 1.0, 0.0).astype(BF16)

    def turn(part, low, high):
        def one(j, _):
            at = pl.ds(pl.multiple_of(j * batch, batch), batch)
            here = pl.ds(part * batch, batch)
            block = obs_v[at, here, :].reshape(batch * batch, width)
            mem[here, at, :] = dot(swap[...], block).astype(BF16).reshape(batch, batch, width)
            return 0

        lax.fori_loop(low, high, one, 0, unroll=high - low)

    whole = chunks - 1
    arrive(4)
    turn(0, 0, whole // 2)
    if remote:
        gather.second(5, 6)
    turn(0, whole // 2, whole)
    if remote:
        gather.third(5, 6)
    turn(1, 0, whole // 2)
    if remote:
        gather.second(4, 0, 1)
        gather.fourth(5, 6)
    turn(1, whole // 2, whole)
    if remote:
        gather.second(2, 3)
    arrive(len(copies) - 1, len(copies) - 2)
    freqs = jnp.exp(
        lax.broadcasted_iota(jnp.int32, (1, half), 1).astype(F32) * F32(-math.log(10000.0)) / half
    )
    for s in range(samples):
        r.angle[s : s + 1, :] = r.levels_s[s].astype(F32) * freqs
    r.embed[:, 0:half] = jnp.sin(r.angle[...]).astype(BF16)
    r.embed[:, half:width] = jnp.cos(r.angle[...]).astype(BF16)
    if remote:
        arrive(6, 7)
        update.old_moment()
        gather.third(4, 0, 1)
        gather.last(5, 6)
        for m in range(3):
            gather.unpack(SQ_AT[m], 1, r.sq_all, m)
        gather.unpack_gains()
    else:
        arrive(0, 1, 2)

    sq, mlp = r.sq_all, r.mlp_all
    wkh, wvh = r.wkh, r.wvh
    lane = lax.broadcasted_iota(jnp.int32, (width, width), 1)

    def split_heads(out, weight):
        weight = weight.astype(F32)
        for h in range(HEADS):
            out[pl.ds(h * width, width), :] = jnp.where(lane // head_dim == h, weight, 0.0).astype(BF16)

    split_heads(wkh, sq[2])
    g1, g2 = r.gain_all[0:1, :], r.gain_all[1:2, :]

    obs_v[keys] = dot(r.embed[...], sq[0]).astype(BF16)
    obs_v[keys + 1 :] = jnp.zeros((KEYS_PAD - keys - 1, samples, width), BF16)
    for part in range(samples // batch):
        turn(part, whole, chunks)

    sides, weights = r.sides_v, r.pds_v

    def make_queries(i, _):
        rows = pl.ds(pl.multiple_of(i * ROWS, ROWS), ROWS)
        first = (r.xhat[rows, :] * g1).astype(BF16)
        r.first[rows, :] = first
        q = dot(first, sq[1]).astype(BF16)
        r.query[rows, :] = q
        here = pl.ds(i * per, per)
        for h in range(HEADS):
            wk = wkh[pl.ds(h * width, width), :]
            value = (dot(q, wk, NT) * 0.125).astype(BF16).reshape(per, ACT, width)
            sides[here, pl.ds((HEADS + h) * ACT, ACT), :] = value
        return 0

    lax.fori_loop(0, tokens // ROWS, make_queries, 0)

    key = lax.broadcasted_iota(jnp.int32, (1, KEYS_PAD), 1)
    low_rows, high_rows = pl.ds(0, HEADS * ACT), pl.ds(HEADS * ACT, HEADS * ACT)

    def attend(g, _):
        ids = [g * GROUP + k for k in range(GROUP)]
        scores = [dot(sides[s, high_rows, :], mem[s], NT) for s in ids]
        lows = []
        for s, score in zip(ids, scores):
            count = OBS_FEW + (OBS_FULL - OBS_FEW) * r.flags_s[s]
            score = score + jnp.where((key < count) | (key == OBS_FULL), 0.0, -1000000000.0)
            expo = jnp.exp(score - jnp.max(score, -1, keepdims=True))
            probs = expo * (1.0 / jnp.sum(expo, -1, keepdims=True))
            r.probs[s] = probs
            low = probs.astype(BF16)
            weights[s, low_rows, :] = low
            lows.append(low)
        for s, low in zip(ids, lows):
            u = dot(low, mem[s]).astype(BF16)
            rows = pl.ds(pl.multiple_of(s * ACT, ACT), ACT)
            for h in range(HEADS):
                r.u[rows, pl.ds(h * width, width)] = u[h * ACT : (h + 1) * ACT, :]
        return 0

    lax.fori_loop(0, groups // 2, attend, 0)
    if remote:
        gather.third(2, 3)
        gather.fourth(4, 0, 1)
    lax.fori_loop(groups // 2, groups, attend, 0)
    if remote:
        gather.fourth(2, 3)
        gather.last(4)
        for m in range(3, 5):
            gather.unpack(SQ_AT[m], 1, sq, m)
    split_heads(wvh, sq[3])

    gain_acc = r.gain_acc
    gain_acc[...] = jnp.zeros_like(gain_acc)
    blocks = [pl.ds(i * ROWS, ROWS) for i in range(tokens // ROWS)]
    for rows in blocks:
        mixed = dot(r.u[rows, :], wvh[...]).astype(BF16)
        r.mixed[rows, :] = mixed
        resid = r.acts_v[rows, :] + dot(mixed, sq[4])
        r.resid[rows, :] = resid
        hat, scale = normalize(resid)
        r.hat_two[rows, :] = hat
        r.rstd_two[rows, :] = scale
        r.second[rows, :] = (hat * g2).astype(BF16)
    arrive(5)
    r.out_low[...] = r.cot_v[...].astype(BF16)
    if remote:
        gather.last(0, 1)
        gather.unpack(0, 4, mlp, 0)
    wide_blocks = [pl.ds(c * 256, 256) for c in range(wide // 256)]
    for rows in blocks:
        for columns in wide_blocks:
            v = dot(r.second[rows, :], mlp[0, :, columns])
            square = v * v
            t = jnp.tanh(0.7978845608 * (v + 0.044715 * square * v))
            r.active[rows, columns] = (0.5 * v * (1.0 + t)).astype(BF16)
            slope = 0.5 * (1.0 + t) + 0.5 * v * (1.0 - t * t) * (0.7978845608 * (1.0 + 0.134145 * square))
            r.slope[rows, columns] = slope

    grads = r.grads

    def put(base, tiles, value):
        for j in range(tiles):
            part = value[:, j * LANES : (j + 1) * LANES].reshape(GRID + (TILE, LANES))
            grads[:, :, :, :, pl.ds(base + j * TILE, TILE), :] = part

    def by_head(left, right):
        turned = left.T
        parts = [
            dot(turned[h * head_dim : (h + 1) * head_dim, :], right[:, pl.ds(h * width, width)])
            for h in range(HEADS)
        ]
        return jnp.concatenate(parts, axis=0).T

    put(MLP_ROWS, 8, dot(r.out_low[...], r.active[...], TN))
    if remote:
        update.start(2)
        update.start(3)
        gather.last(2, 3)
        gather.unpack(MLP_ROWS, 4, mlp, 1)
    for rows in blocks:
        for columns in wide_blocks:
            slope = r.slope[rows, columns]
            r.dhidden[rows, columns] = (slope * dot(r.out_low[rows, :], mlp[1, :, columns])).astype(BF16)
    put(0, 8, dot(r.second[...], r.dhidden[...], TN))
    if remote:
        update.start(0)
        update.start(1)
        update.one(2, 3)
    for i, rows in enumerate(blocks):
        r.out_v[rows, :] = r.resid[rows, :] + dot(r.active[rows, :], mlp[1], NT)
        grad_second = dot(r.dhidden[rows, :], mlp[0], NT)
        hat = r.hat_two[rows, :]
        gain_acc[1:2, :] += jnp.sum(grad_second * hat, 0, keepdims=True)
        dres = r.cot_v[rows, :] + norm_back(grad_second * g2, hat, r.rstd_two[rows, :])
        r.dres[rows, :] = dres
        low = dres.astype(BF16)
        r.dres_low[rows, :] = low
        gm = dot(low, sq[4], NT).astype(BF16)
        r.dmixed[rows, :] = gm
        here = pl.ds(i * per, per)
        for h in range(HEADS):
            wv = wvh[pl.ds(h * width, width), :]
            sides[here, pl.ds(h * ACT, ACT), :] = dot(gm, wv, NT).astype(BF16).reshape(per, ACT, width)
    keep_out = pltpu.make_async_copy(r.out_v, r.output, out_sems.at[0])
    keep_out.start()
    if remote:
        update.one(0, 1)
    put(SQ_AT[4], 2, dot(r.mixed[...], r.dres_low[...], TN))
    put(SQ_AT[3], 2, by_head(r.dmixed[...], r.u))
    if remote:
        update.start(4)

    def attend_back(g, _):
        ids = [g * GROUP + k for k in range(GROUP)]
        rises = [dot(sides[s, low_rows, :], mem[s], NT) for s in ids]
        for s, rise in zip(ids, rises):
            probs = r.probs[s]
            both = probs * rise
            weights[s, high_rows, :] = (both - probs * jnp.sum(both, -1, keepdims=True)).astype(BF16)
        for s in ids:
            dq = (dot(weights[s, high_rows, :], mem[s]) * 0.125).astype(BF16)
            rows = pl.ds(pl.multiple_of(s * ACT, ACT), ACT)
            for h in range(HEADS):
                r.dq_wide[rows, pl.ds(h * width, width)] = dq[h * ACT : (h + 1) * ACT, :]
            end = dot(weights[s, :, LANES:KEYS_PAD], sides[s], TN)
            r.stamps[s] = end[64:72, :]
        return 0

    lax.fori_loop(0, groups // 2, attend_back, 0)
    if remote:
        update.two(2, 3)
        update.one(4)
        update.two(0, 1)
    lax.fori_loop(groups // 2, groups, attend_back, 0)
    if remote:
        update.three(2, 3)
        update.two(4)
    put(SQ_AT[2], 2, by_head(r.query[...], r.dq_wide))
    stamp_low = r.stamps[:, 4:5, :].reshape(samples, width).astype(BF16)
    put(SQ_AT[0], 2, dot(r.embed[...], stamp_low, TN))
    if remote:
        update.start(5)
        update.three(0, 1)

    def memory_back(low, high):
        for s in range(2 * low, 2 * high):
            mem[s] = dot(weights[s], sides[s], TN).astype(BF16)

    def keep_og(part):
        here = pl.ds(part * batch, batch)
        return pltpu.make_async_copy(obs_v.at[pl.ds(0, keys), here], r.og.at[:, here], out_sems.at[2 + part])

    def turn_back(part, low, high):
        def one(j):
            at = pl.ds(pl.multiple_of(j * batch, batch), batch)
            here = pl.ds(part * batch, batch)
            block = mem[here, at, :].reshape(batch * batch, width)
            value = dot(swap[...], block).astype(BF16).reshape(batch, batch, width)
            obs_v[at, here, :] = value

        for j in range(low, high):
            one(j)
        if high == chunks:
            keep_og(part).start()

    def queries_back(i, _):
        rows = pl.ds(pl.multiple_of(i * ROWS, ROWS), ROWS)
        r.dquery[rows, :] = dot(r.dq_wide[rows, :], wkh[...]).astype(BF16)
        return 0

    lax.fori_loop(0, tokens // ROWS, queries_back, 0)
    put(SQ_AT[1], 2, dot(r.first[...], r.dquery[...], TN))
    if remote:
        update.start(6)
        update.one(5)

    def acts_back(i, _):
        rows = pl.ds(pl.multiple_of(i * ROWS, ROWS), ROWS)
        grad_first = dot(r.dquery[rows, :], sq[1], NT)
        hat = r.xhat[rows, :]
        gain_acc[0:1, :] += jnp.sum(grad_first * hat, 0, keepdims=True)
        r.ag_v[rows, :] = r.dres[rows, :] + norm_back(grad_first * g1, hat, r.rstd[rows, :])
        return 0

    def finish_acts():
        lax.fori_loop(0, tokens // ROWS, acts_back, 0)
        for norm in range(2):
            for j in range(2):
                row = gain_acc[norm : norm + 1, j * LANES : (j + 1) * LANES]
                at = GAIN_BASE + norm * 2 + j
                value = jnp.broadcast_to(row.reshape(1, 1, 1, 1, 1, LANES), GRID + (1, LANES))
                grads[:, :, :, :, at : at + 1, :] = value
        rest = WIRE - GAIN_BASE - 4
        grads[:, :, :, :, GAIN_BASE + 4 : WIRE, :] = jnp.zeros(GRID + (rest, LANES), F32)

    keep_ag = pltpu.make_async_copy(r.ag_v, r.ag, out_sems.at[1])
    if remote:
        pairs = samples // 2
        finish_acts()
        keep_ag.start()
        update.start(7)
        update.one(6)
        update.three(4)
        memory_back(0, pairs // 2)
        update.four(2, 3)
        update.two(5)
        update.one(7)
        update.two(6)
        memory_back(pairs // 2, pairs)
        update.four(0, 1)
        update.three(5)
        update.two(7)
        update.three(6)
        turn_back(0, 0, chunks // 2)
        update.three(7)
        update.orthogonalize()
        update.give_all()
        turn_back(0, chunks // 2, chunks)
        update.four(4, 5, 6)
        turn_back(1, 0, chunks)
        update.four(7)
        out = r.out
        out[1, :, :] = r.moment[...]
        out[2, pl.ds(GAIN_BASE, 16), :] = jnp.zeros((16, LANES), F32)
        gather.drain()
        update.drain()
        update.take_all()
        update.drain_owner()
    else:
        finish_acts()
        keep_ag.start()
        memory_back(0, samples // 2)
        for part in range(samples // batch):
            turn_back(part, 0, chunks)
    for copy in (keep_out, keep_ag, *(keep_og(part) for part in range(samples // batch))):
        copy.wait()


def block_and_back(remote, acts, obs, flags, levels, cot, sqw, mlpw, gain, sqm=None, mlpm=None):
    tokens, width = acts.shape
    keys, samples = obs.shape[0], obs.shape[1]
    rows = HEADS * ACT
    wide = mlpw.shape[2]
    any_space = pl.BlockSpec(memory_space=pl.ANY)
    in_vmem = pl.BlockSpec(memory_space=VMEM)
    sem = pltpu.SemaphoreType.DMA
    ins = dict(flags=flags, levels=levels, acts=acts, obs=obs, cot=cot, sqw=sqw, mlpw=mlpw, gain=gain)
    outs = dict(
        output=jax.ShapeDtypeStruct(acts.shape, F32),
        ag=jax.ShapeDtypeStruct(acts.shape, F32),
        og=jax.ShapeDtypeStruct(obs.shape, BF16),
    )
    grads = GRID + (WIRE, LANES)
    scratch = dict(
        obs_v=VMEM((KEYS_PAD, samples, width), BF16),
        acts_v=VMEM(acts.shape, F32),
        cot_v=VMEM(acts.shape, F32),
        mem=VMEM((samples, KEYS_PAD, width), BF16),
        swap=VMEM((256, 256), BF16),
        sq_all=VMEM((5, width, width), BF16),
        mlp_all=VMEM((2, width, wide), BF16),
        gain_all=VMEM((2, width), F32),
        wkh=VMEM((HEADS * width, width), BF16),
        wvh=VMEM((HEADS * width, width), BF16),
        first=VMEM((tokens, width), BF16),
        query=VMEM((tokens, width), BF16),
        xhat=VMEM((tokens, width), F32),
        rstd=VMEM((tokens, 1), F32),
        probs=VMEM((samples, rows, KEYS_PAD), F32),
        pds_v=VMEM((samples, 2 * rows, KEYS_PAD), BF16),
        sides_v=VMEM((samples, 2 * rows, width), BF16),
        u=VMEM((tokens, HEADS * width), BF16),
        dq_wide=VMEM((tokens, HEADS * width), BF16),
        mixed=VMEM((tokens, width), BF16),
        second=VMEM((tokens, width), BF16),
        active=VMEM((tokens, wide), BF16),
        dhidden=VMEM((tokens, wide), BF16),
        out_low=VMEM((tokens, width), BF16),
        dres_low=VMEM((tokens, width), BF16),
        dres=VMEM((tokens, width), F32),
        resid=VMEM((tokens, width), F32),
        hat_two=VMEM((tokens, width), F32),
        rstd_two=VMEM((tokens, 1), F32),
        slope=VMEM((tokens, wide), F32),
        dmixed=VMEM((tokens, width), BF16),
        dquery=VMEM((tokens, width), BF16),
        out_v=VMEM((tokens, width), F32),
        ag_v=VMEM((tokens, width), F32),
        angle=VMEM((samples, width // 2), F32),
        embed=VMEM((samples, width), BF16),
        stamps=VMEM((samples, 8, width), F32),
        gain_acc=VMEM((8, width), F32),
        flags_s=pltpu.SMEM(flags.shape, jnp.int32),
        levels_s=pltpu.SMEM(levels.shape, jnp.int32),
        in_sems=sem((10,)),
        out_sems=sem((2 + samples // 16,)),
    )
    extra = {}
    if remote:
        ins.update(sqm=sqm, mlpm=mlpm)
        outs.update(out=jax.ShapeDtypeStruct((3, WIRE, LANES), F32))
        chunks = len(CHUNKS)
        scratch.update(
            grads=VMEM(grads, F32),
            sqw_v=VMEM(sqw.shape, F32),
            mlpw_v=VMEM(mlpw.shape, F32),
            gain_v=VMEM(gain.shape, F32),
            sqm_v=VMEM(sqm.shape, F32),
            mlpm_v=VMEM(mlpm.shape, F32),
            wire=VMEM(grads, BF16),
            edge=VMEM((16, LANES), F32),
            gsend=sem((len(PIECES), 6)),
            grecv=sem((len(PIECES), 6)),
            send0=VMEM((4, 2, 2, WIRE, LANES), BF16),
            got_core=VMEM((4, 2, 2, WIRE, LANES), BF16),
            sum1=VMEM((4, 2, 2, WIRE, LANES), F32),
            send1=VMEM((4, 2, WIRE, LANES), BF16),
            got1=VMEM((4, 2, WIRE, LANES), BF16),
            sum2=VMEM((4, 2, WIRE, LANES), F32),
            send2=VMEM((4, WIRE, LANES), BF16),
            got2=VMEM((4, WIRE, LANES), BF16),
            sum3=VMEM((4, WIRE, LANES), F32),
            send3=VMEM((4, WIRE, LANES), BF16),
            got3=VMEM((3, WIRE, LANES), BF16),
            moment=VMEM((WIRE, LANES), F32),
            slabs_sq=VMEM((4, 8, 4, SQ_ROWS, LANES), BF16),
            slabs_mlp=VMEM((32, MLP_ROWS, LANES), BF16),
            moment_low=VMEM((2 * MLP_ROWS, LANES), BF16),
            back_mlp=VMEM((2, MLP_ROWS, LANES), BF16),
            back_sq=VMEM((5, SQ_ROWS, LANES), BF16),
            result_sq=VMEM((32, SQ_ROWS, LANES), BF16),
            result_mlp=VMEM((32, MLP_ROWS, LANES), BF16),
            cur=VMEM((width, wide), F32),
            cur_low=VMEM((width, wide), BF16),
            send=sem((chunks, 6)),
            recv=sem((chunks, 6)),
            own_send=sem((len(PARTS_OUT),)),
            own_recv=sem((1,)),
            back_send=sem((32,)),
            back_recv=sem((7,)),
        )
        extra = dict(collective_id=0, has_side_effects=True)
        outs = {name: VMEM(like.shape, like.dtype) for name, like in outs.items()}
    else:
        outs.update(grads=jax.ShapeDtypeStruct(grads, F32))
    names = tuple(ins) + tuple(outs) + tuple(scratch)
    stay = [pltpu.with_memory_space_constraint(value, pltpu.HBM) for value in ins.values()]
    results = pl.pallas_call(
        functools.partial(block_kernel, names, remote),
        out_shape=tuple(outs.values()),
        in_specs=[any_space] * len(ins),
        out_specs=[any_space] * 3 + [in_vmem],
        scratch_shapes=list(scratch.values()),
        compiler_params=pltpu.CompilerParams(vmem_limit_bytes=52 << 20, **extra),
        name="block_and_back",
    )(*stay)
    return Refs(zip(outs, results))


PARTS = 7


def finish_kernel(names, rate, *args):
    r = Refs(zip(names, args))
    sems = r.sems
    keys = r.og.shape[0]
    step = keys // PARTS

    def leave(part):
        block = pl.ds(part * step, step)
        return pltpu.make_async_copy(r.og_v.at[block], r.og.at[block], sems.at[part])

    more = PARTS
    moves = []
    if hasattr(r, "wire"):
        pairs = [(r.sqw, r.sqw_v), (r.mlpw, r.mlpw_v), (r.gain, r.gain_v), (r.gainm, r.gainm_v)]
        pairs += [(r.output, r.output_f), (r.ag, r.ag_f)]
        for source, target in pairs:
            moves.append(pltpu.make_async_copy(source, target, sems.at[more]))
            moves[-1].start()
            more += 1
    for part in range(PARTS):

        def widen(j, _):
            r.og_v[j] = r.low[j].astype(F32)
            return 0

        lax.fori_loop(part * step, (part + 1) * step, widen, 0, unroll=4)
        leave(part).start()
    for copy in moves[:4]:
        copy.wait()
    if hasattr(r, "wire"):
        finish_weights(r, rate)
    for part in range(PARTS):
        leave(part).wait()
    for copy in moves[4:]:
        copy.wait()


def finish_weights(r, rate):
    wire = r.wire
    me = lax.axis_index("dp")
    for m in range(5):
        for j in range(2):
            rows, columns = pl.ds(SQ_AT[m] + j * TILE, TILE), pl.ds(j * LANES, LANES)
            r.sqg[m, :, columns] = wire[0, rows, :]
            r.sqm[m, :, columns] = wire[1, rows, :]
            r.sqn[m, :, columns] = r.sqw_v[m, :, columns] - SQ_RATES[m] * wire[2, rows, :]
    r.sqc[...] = r.sqn[...].astype(BF16)
    for m in range(2):
        for j in range(8):
            rows, columns = pl.ds(m * MLP_ROWS + j * TILE, TILE), pl.ds(j * LANES, LANES)
            r.mlpg[m, :, columns] = wire[0, rows, :]
            r.mlpm[m, :, columns] = wire[1, rows, :]
            r.mlpn[m, :, columns] = r.mlpw_v[m, :, columns] - MLP_RATES[m] * wire[2, rows, :]
    r.mlpc[...] = r.mlpn[...].astype(BF16)
    tile = wire[0, pl.ds(GAIN_BASE, TILE), :]
    turned = pltpu.roll(tile, (LANES - (me % 16) * TILE) % LANES, 1)
    at = me // 16
    for norm in range(2):
        pair = turned[2 * norm : 2 * norm + 2, 0:TILE]
        row = jnp.where(at == 0, pair[0:1, :], pair[1:2, :])
        new = 0.5 * r.gainm_v[norm : norm + 1, :] + row
        r.gg[norm : norm + 1, :] = row
        r.gm[norm : norm + 1, :] = new
        r.gn[norm : norm + 1, :] = r.gain_v[norm : norm + 1, :] - rate * new


def finish(rate, made, sqw=None, mlpw=None, gain=None, gainm=None):
    any_space = pl.BlockSpec(memory_space=pl.ANY)
    in_vmem = pl.BlockSpec(memory_space=VMEM)
    ins = dict(low=made.og)
    outs = dict(og=jax.ShapeDtypeStruct(made.og.shape, F32))
    near, far = 1, 1
    if hasattr(made, "out"):
        ins.update(output=made.output, ag=made.ag, wire=made.out, sqw=sqw, mlpw=mlpw, gain=gain, gainm=gainm)
        like = jax.ShapeDtypeStruct
        near, far = 4, 3
        outs.update(
            output_f=like(made.output.shape, F32),
            ag_f=like(made.ag.shape, F32),
            sqg=like(sqw.shape, F32),
            sqm=like(sqw.shape, F32),
            sqn=like(sqw.shape, F32),
            sqc=like(sqw.shape, BF16),
            mlpg=like(mlpw.shape, F32),
            mlpm=like(mlpw.shape, F32),
            mlpn=like(mlpw.shape, F32),
            mlpc=like(mlpw.shape, BF16),
            gg=like(gain.shape, F32),
            gm=like(gain.shape, F32),
            gn=like(gain.shape, F32),
        )
    scratch = dict(
        og_v=VMEM(made.og.shape, F32),
        sems=pltpu.SemaphoreType.DMA((PARTS + 6,)),
    )
    if hasattr(made, "out"):
        scratch.update(
            sqw_v=VMEM(sqw.shape, F32),
            mlpw_v=VMEM(mlpw.shape, F32),
            gain_v=VMEM(gain.shape, F32),
            gainm_v=VMEM(gainm.shape, F32),
        )
    names = tuple(ins) + tuple(outs) + tuple(scratch)
    made_here = list(ins.values())
    stay = [pltpu.with_memory_space_constraint(value, pltpu.HBM) for value in made_here[near:]]
    results = pl.pallas_call(
        functools.partial(finish_kernel, names, rate),
        out_shape=tuple(outs.values()),
        in_specs=[in_vmem] * near + [any_space] * (len(ins) - near),
        out_specs=[any_space] * far + [in_vmem] * (len(outs) - far),
        scratch_shapes=list(scratch.values()),
        compiler_params=pltpu.CompilerParams(vmem_limit_bytes=16 << 20),
        name="finish",
    )(*made_here[:near], *stay)
    return Refs(zip(outs, results))


HIGH_PRECISION = lax.Precision.HIGHEST


def plain_orthogonalize(matrix):
    current = matrix / (jnp.sqrt(jnp.sum(matrix * matrix)) + 1e-07)
    for turn in range(5):
        gram = jnp.dot(current, current.T, precision=HIGH_PRECISION)
        poly = COEF_B * gram + COEF_C * jnp.dot(gram, gram, precision=HIGH_PRECISION)
        current = COEF_A * current + jnp.dot(poly, current, precision=HIGH_PRECISION)
    return current


def pick_owned(stack, owners, device):
    chosen = jnp.zeros_like(stack[0])
    for index in range(len(owners)):
        chosen = jnp.where(device == owners[index], stack[index], chosen)
    return chosen


def is_owner(owners, device):
    flag = device < 0
    for owner in owners:
        flag = jnp.logical_or(flag, device == owner)
    return flag


def from_wire(grads):
    def matrix(base, tiles):
        part = grads[:, base : base + tiles * TILE, :].reshape(-1, tiles, TILE, LANES)
        return part.transpose(0, 2, 1, 3).reshape(-1, tiles * LANES)

    square = jnp.stack([matrix(SQ_AT[m], 2) for m in range(5)])
    mlp = jnp.stack([matrix(m * MLP_ROWS, 8) for m in range(2)])
    return square, mlp, grads[0, GAIN_BASE : GAIN_BASE + 4, :].reshape(2, 2 * LANES)


def update_by_collectives(
    grads, square_weights, mlp_weights, gains, square_moment, mlp_moment, gain_moment, rate
):
    square_local, mlp_local, gain_local = from_wire(grads)
    square_grad, mlp_grad, gain_grad = (
        lax.psum_scatter(square_local, "dp", scatter_dimension=1, tiled=True),
        lax.psum_scatter(mlp_local, "dp", scatter_dimension=1, tiled=True),
        lax.psum_scatter(gain_local, "dp", scatter_dimension=1, tiled=True),
    )
    square_moment_new = 0.5 * square_moment + square_grad
    mlp_moment_new = 0.5 * mlp_moment + mlp_grad
    gain_moment_new = 0.5 * gain_moment + gain_grad
    device = lax.axis_index("dp")
    count = lax.axis_size("dp")
    square_owners = [index * count // 7 for index in range(5)]
    mlp_owners = [(index + 5) * count // 7 for index in range(2)]
    square_full, mlp_full = (
        lax.all_gather(square_moment_new, "dp", axis=1, tiled=True),
        lax.all_gather(mlp_moment_new, "dp", axis=1, tiled=True),
    )
    mine_square = pick_owned(square_full, square_owners, device)
    mine_mlp = pick_owned(mlp_full, mlp_owners, device)
    made_square = lax.cond(
        is_owner(square_owners, device), plain_orthogonalize, jnp.zeros_like, mine_square
    )
    made_mlp = lax.cond(is_owner(mlp_owners, device), plain_orthogonalize, jnp.zeros_like, mine_mlp)
    stack_square = jnp.stack(
        [jnp.where(device == owner, made_square, 0.0) for owner in square_owners]
    )
    stack_mlp = jnp.stack([jnp.where(device == owner, made_mlp, 0.0) for owner in mlp_owners])
    square_ortho, mlp_ortho = (
        lax.psum_scatter(stack_square, "dp", scatter_dimension=1, tiled=True),
        lax.psum_scatter(stack_mlp, "dp", scatter_dimension=1, tiled=True),
    )
    square_new = square_weights - jnp.array(SQ_RATES, F32)[:, None, None] * square_ortho
    mlp_new = mlp_weights - jnp.array(MLP_RATES, F32)[:, None, None] * mlp_ortho
    gains_new = gains - rate * gain_moment_new
    return (
        square_grad,
        square_moment_new,
        square_new,
        square_new.astype(BF16),
        mlp_grad,
        mlp_moment_new,
        mlp_new,
        mlp_new.astype(BF16),
        gain_grad,
        gain_moment_new,
        gains_new,
    )


def per_device(
    actions,
    observed,
    camera_flags,
    noise_levels,
    cotangent,
    square_weights,
    mlp_weights,
    gains,
    square_moment,
    mlp_moment,
    gain_moment,
):
    count = lax.axis_size("dp")
    rate = 0.1 / math.sqrt(actions.shape[0] * count)
    by_key = observed.transpose(1, 0, 2)
    ins = (actions, by_key, camera_flags, noise_levels, cotangent)
    if count == math.prod(GRID):
        made = block_and_back(True, *ins, square_weights, mlp_weights, gains, square_moment, mlp_moment)
        done = finish(rate, made, square_weights, mlp_weights, gains, gain_moment)
        output, actions_grad = done.output_f, done.ag_f
        d = done
        rest = (d.sqg, d.sqm, d.sqn, d.sqc, d.mlpg, d.mlpm, d.mlpn, d.mlpc, d.gg, d.gm, d.gn)
    else:
        square_all, mlp_all = (
            lax.all_gather(square_weights.astype(BF16), "dp", axis=1, tiled=True),
            lax.all_gather(mlp_weights.astype(BF16), "dp", axis=1, tiled=True),
        )
        gain_all = lax.all_gather(gains, "dp", axis=1, tiled=True)
        made = block_and_back(False, *ins, square_all, mlp_all, gain_all)
        done = finish(rate, made)
        output, actions_grad = made.output, made.ag
        grads = made.grads.reshape(-1, WIRE, LANES)
        rest = update_by_collectives(
            grads, square_weights, mlp_weights, gains, square_moment, mlp_moment, gain_moment, rate
        )
    observed_grad = done.og.transpose(1, 0, 2)
    return (output, actions_grad, observed_grad) + tuple(rest)


def solution(mesh):
    rows, cube, flat = P("dp", None), P("dp", None, None), P("dp")
    stacked, pair = P(None, "dp", None), P(None, "dp")
    return jax.shard_map(
        per_device,
        mesh=mesh,
        in_specs=(rows, cube, flat, flat, rows, stacked, stacked, pair, stacked, stacked, pair),
        out_specs=(rows, rows, cube) + (stacked,) * 8 + (pair,) * 3,
        check_vma=False,
    )
```

```python
import functools
import math

import jax
import jax.numpy as jnp
from jax import lax
from jax.experimental import pallas as pl
from jax.experimental.pallas import tpu as pltpu
from jax.sharding import PartitionSpec as P

HEADS = 4
ACT = 16
OBS_FULL = 196
OBS_FEW = 49
COEF_A = 3.4445
COEF_B = -4.775
COEF_C = 2.0315
F32 = jnp.float32
BF16 = jnp.bfloat16
MESH = pl.DeviceIdType.MESH
VMEM = pltpu.VMEM
NN = (((1,), (0,)), ((), ()))
NT = (((1,), (1,)), ((), ()))
TN = (((0,), (0,)), ((), ()))

LANES = 128
TILE = 8
MLP_ROWS = 64
SQ_ROWS = 16
SQ_AT = (160, 192, 176, 128, 144)
GAIN_BASE = 208
WIRE = 224
PIECES = ((0, 32), (32, 32), (64, 32), (96, 32), (128, 32), (160, 32), (192, 32))
PIECE_X_FIRST = (True, False, True, False, True, True, False)
CHUNKS = ((0, 32), (32, 32), (64, 32), (96, 32), (128, 32), (160, 32), (192, 16), (208, 16))
X_FIRST = (True, False, True, False, True, False, True, False)
PARTS_OUT = (
    (0, 0, 0, 32, 0),
    (1, 0, 32, 32, 32),
    (2, 1, 64, 32, 0),
    (3, 1, 96, 32, 32),
    (4, 5, 128, 16, 0),
    (4, 6, 144, 16, 0),
    (5, 2, 160, 16, 0),
    (5, 4, 176, 16, 0),
    (6, 3, 192, 16, 0),
)
MLP_RATES = (1.0, 0.5)
SQ_RATES = (0.5, 0.5, 0.5, 0.5, 4.0)
GRID = (4, 2, 2, 2)
OWNERS = (8, 22, 14, 16, 11, 21, 13)
SHIFTS = (0.0, 0.0, 0.4, 0.8, 0.8)
KEYS_PAD = 208
GROUP = 16
ROWS = 512


class Refs:
    def __init__(self, pairs):
        self.__dict__.update(pairs)


def dot(left, right, dims=NN):
    return lax.dot_general(left, right, dims, preferred_element_type=F32)


def place():
    me = lax.axis_index("dp")
    return me, me // 8, (me // 4) % 2, (me // 2) % 2, me % 2


def device_at(z, y, x, c):
    return ((z * 2 + y) * 2 + x) * 2 + c


def link(src, dst, send, recv, device):
    return pltpu.make_async_remote_copy(
        src_ref=src,
        dst_ref=dst,
        send_sem=send,
        recv_sem=recv,
        device_id=(device,),
        device_id_type=MESH,
    )


def greet(device):
    pl.semaphore_signal(
        pltpu.get_barrier_semaphore(), inc=1, device_id=(device,), device_id_type=MESH
    )


def normalize(values):
    centred = values - jnp.mean(values, -1, keepdims=True)
    scale = lax.rsqrt(jnp.mean(centred * centred, -1, keepdims=True) + 1e-05)
    return centred * scale, scale


def norm_back(grad, hat, scale):
    mean_one = jnp.mean(grad, -1, keepdims=True)
    mean_two = jnp.mean(grad * hat, -1, keepdims=True)
    return scale * (grad - mean_one - hat * mean_two)


class Gather:
    def __init__(self, r):
        self.r = r
        self.me, self.z, self.y, self.x, self.c = place()

    def hop(self, k, step, part, device):
        return link(part, part, self.r.gsend.at[k, step], self.r.grecv.at[k, step], device)

    def along_z(self, k, step):
        part = self.r.wire.at[self.z, self.y, self.x, self.c, pl.ds(*PIECES[k])]
        return self.hop(k, step, part, device_at((self.z + step + 1) % 4, self.y, self.x, self.c))

    def from_z(self, k, step):
        there = (self.z + 3 - step) % 4
        part = self.r.wire.at[there, self.y, self.x, self.c, pl.ds(*PIECES[k])]
        return self.hop(k, step, part, device_at(there, self.y, self.x, self.c))

    def plane(self, k, second, mine):
        z, y, x, c = self.z, self.y, self.x, self.c
        rows, wire = pl.ds(*PIECES[k]), self.r.wire
        py, px = (y, x) if mine else (1 - y, 1 - x)
        along_x = PIECE_X_FIRST[k] == second
        if along_x:
            part = wire.at[:, y, px, c, rows] if second else wire.at[:, :, px, c, rows]
            return self.hop(k, 3 if second else 4, part, device_at(z, y, 1 - x, c))
        part = wire.at[:, py, x, c, rows] if second else wire.at[:, py, :, c, rows]
        return self.hop(k, 3 if second else 4, part, device_at(z, 1 - y, x, c))

    def core(self, k, mine):
        part = self.r.wire.at[:, :, :, self.c if mine else 1 - self.c, pl.ds(*PIECES[k])]
        return self.hop(k, 5, part, device_at(self.z, self.y, self.x, 1 - self.c))

    def first(self, *chunks):
        for k in chunks:
            for step in range(3):
                self.along_z(k, step).start()

    def second(self, *chunks):
        for k in chunks:
            for step in range(3):
                self.from_z(k, step).wait_recv()
            self.plane(k, True, True).start()

    def third(self, *chunks):
        for k in chunks:
            self.plane(k, True, False).wait_recv()
            self.plane(k, False, True).start()

    def fourth(self, *chunks):
        for k in chunks:
            self.plane(k, False, False).wait_recv()
            self.core(k, True).start()

    def last(self, *chunks):
        for k in chunks:
            self.core(k, False).wait_recv()

    def drain(self):
        for k in range(len(PIECES)):
            for step in range(3):
                self.along_z(k, step).wait_send()
            self.plane(k, True, True).wait_send()
            self.plane(k, False, True).wait_send()
            self.core(k, True).wait_send()

    def fill(self, square):
        r = self.r
        spot = (self.z, self.y, self.x, self.c)

        def tiles(source, m, base, number):
            for j in range(number):
                pair = [source[m, :, pl.ds((2 * j + k) * LANES, LANES)] for k in range(2)]
                r.wire[spot + (pl.ds(base + j * 16, 16),)] = jnp.concatenate(pair, axis=0).astype(BF16)

        if not square:
            for m in range(2):
                tiles(r.mlpw_v, m, m * MLP_ROWS, 4)
            return
        for m in range(5):
            tiles(r.sqw_v, m, SQ_AT[m], 1)
        gains, edge = r.gain_v[...], r.edge
        high = gains.astype(BF16).astype(F32)
        middle = (gains - high).astype(BF16).astype(F32)
        edge[...] = jnp.zeros_like(edge)
        edge[0:2, 0:TILE] = high
        edge[2:4, 0:TILE] = middle
        edge[4:6, 0:TILE] = (gains - high - middle).astype(BF16).astype(F32)
        r.wire[spot + (pl.ds(GAIN_BASE, 16),)] = edge[...].astype(BF16)

    def unpack(self, base, number, out, m):
        for j in range(number):
            block = self.r.wire[:, :, :, :, pl.ds(base + j * 16, 16), :].reshape(32, 16, LANES).astype(F32)
            for half in range(2):
                columns = pl.ds((2 * j + half) * LANES, LANES)
                out[m, :, columns] = block[:, half * 8 : half * 8 + 8, :].reshape(256, LANES).astype(BF16)

    def unpack_gains(self):
        edge, wire = self.r.edge, self.r.wire
        for half in range(2):
            total = jnp.zeros((16, LANES), F32)
            for at in range(16):
                d = half * 16 + at
                tile = wire[d // 8, (d // 4) % 2, (d // 2) % 2, d % 2, pl.ds(GAIN_BASE, 16), :].astype(F32)
                total = total + (tile if at == 0 else pltpu.roll(tile, at * TILE, 1))
            edge[...] = total
            self.r.gain_all[:, pl.ds(half * LANES, LANES)] = edge[0:2, :] + edge[2:4, :] + edge[4:6, :]


class Update:
    def __init__(self, r):
        self.r = r
        self.me, self.z, self.y, self.x, self.c = place()

    def hop(self, k, step, src, dst, device):
        return link(src, dst, self.r.send.at[k, step], self.r.recv.at[k, step], device)

    def core(self, k):
        rows = pl.ds(*CHUNKS[k])
        src, dst = self.r.send0.at[:, :, :, rows], self.r.got_core.at[:, :, :, rows]
        return self.hop(k, 0, src, dst, device_at(self.z, self.y, self.x, 1 - self.c))

    def plane(self, k, first):
        rows = pl.ds(*CHUNKS[k])
        to = (self.z, self.y, 1 - self.x, self.c) if X_FIRST[k] == first else (self.z, 1 - self.y, self.x, self.c)
        if first:
            src, dst = self.r.send1.at[:, :, rows], self.r.got1.at[:, :, rows]
        else:
            src, dst = self.r.send2.at[:, rows], self.r.got2.at[:, rows]
        return self.hop(k, 1 if first else 2, src, dst, device_at(*to))

    def along_z(self, k, step):
        rows = pl.ds(*CHUNKS[k])
        there = (self.z + step + 1) % 4
        src, dst = self.r.send3.at[there, rows], self.r.got3.at[step, rows]
        return self.hop(k, 3 + step, src, dst, device_at(there, self.y, self.x, self.c))

    def start(self, k):
        rows = pl.ds(*CHUNKS[k])
        self.r.send0[:, :, :, rows, :] = self.r.grads[:, :, :, 1 - self.c, rows, :].astype(BF16)
        self.core(k).start()

    def one(self, *chunks):
        r = self.r
        for k in chunks:
            rows = pl.ds(*CHUNKS[k])
            self.core(k).wait_recv()
            sum1 = r.sum1
            sum1[:, :, :, rows, :] = r.grads[:, :, :, self.c, rows, :] + r.got_core[:, :, :, rows, :].astype(F32)
            other = sum1[:, :, 1 - self.x, rows, :] if X_FIRST[k] else sum1[:, 1 - self.y, :, rows, :]
            r.send1[:, :, rows, :] = other.astype(BF16)
            self.plane(k, True).start()

    def two(self, *chunks):
        r = self.r
        for k in chunks:
            rows = pl.ds(*CHUNKS[k])
            self.plane(k, True).wait_recv()
            sum1, sum2 = r.sum1, r.sum2
            mine = sum1[:, :, self.x, rows, :] if X_FIRST[k] else sum1[:, self.y, :, rows, :]
            sum2[:, :, rows, :] = mine + r.got1[:, :, rows, :].astype(F32)
            other = 1 - self.y if X_FIRST[k] else 1 - self.x
            r.send2[:, rows, :] = sum2[:, other, rows, :].astype(BF16)
            self.plane(k, False).start()

    def three(self, *chunks):
        r = self.r
        for k in chunks:
            rows = pl.ds(*CHUNKS[k])
            self.plane(k, False).wait_recv()
            mine = self.y if X_FIRST[k] else self.x
            total = r.sum2[:, mine, rows, :] + r.got2[:, rows, :].astype(F32)
            r.sum3[:, rows, :] = total
            r.send3[:, rows, :] = total.astype(BF16)
            if k >= 4:
                own = r.sum3[self.z, rows, :] + 0.5 * r.moment[rows, :]
                r.send3[self.z, rows, :] = own.astype(BF16)
                self.parts_to_owners(k)
            for step in range(3):
                self.along_z(k, step).start()

    def parts_to_owners(self, k):
        for part, (chunk, index, *_) in enumerate(PARTS_OUT):
            if chunk != k:
                continue

            @pl.when(self.me != OWNERS[index])
            def _():
                self.to_owner(part).start()

            @pl.when(self.me == OWNERS[index])
            def _():
                src, dst = self.own_part(part)
                pltpu.make_async_copy(src, dst, self.r.own_recv.at[0]).start()

    def result(self, index):
        return self.r.result_mlp if index < 2 else self.r.result_sq

    def own_part(self, part):
        _, index, base, number, place = PARTS_OUT[part]
        if index < 2:
            return self.r.moment_low.at[pl.ds(base, number)], self.r.slabs_mlp.at[self.me, pl.ds(place, number)]
        return self.r.send3.at[:, pl.ds(base, number)], self.r.slabs_sq.at[self.z, self.me % 8]

    def to_owner(self, part):
        src, dst = self.own_part(part)
        return link(src, dst, self.r.own_send.at[part], self.r.own_recv.at[0], OWNERS[PARTS_OUT[part][1]])

    def four(self, *chunks):
        r = self.r
        moment, out = r.moment, r.out
        for k in chunks:
            rows = pl.ds(*CHUNKS[k])
            total = r.sum3[self.z, rows, :]
            for step in range(3):
                self.along_z(k, step).wait_recv()
                total = total + r.got3[step, rows, :].astype(F32)
            out[0, rows, :] = total
            new = 0.5 * moment[rows, :] + total
            moment[rows, :] = new
            if k < 4:
                r.moment_low[rows, :] = new.astype(BF16)
            if k < 4:
                self.parts_to_owners(k)

    def old_moment(self):
        r = self.r
        moment = r.moment
        for m in range(2):
            for j in range(8):
                moment[pl.ds(m * MLP_ROWS + j * TILE, TILE), :] = r.mlpm_v[m, :, pl.ds(j * LANES, LANES)]
        for m in range(5):
            for j in range(2):
                moment[pl.ds(SQ_AT[m] + j * TILE, TILE), :] = r.sqm_v[m, :, pl.ds(j * LANES, LANES)]
        moment[pl.ds(GAIN_BASE, 16), :] = jnp.zeros((16, LANES), F32)

    def orthogonalize(self):
        r = self.r
        cur = r.cur
        rows = lax.broadcasted_iota(jnp.int32, (256, 256), 0)
        diagonal = rows == lax.broadcasted_iota(jnp.int32, (256, 256), 1)

        low = r.cur_low

        def load(rows, j, pair):
            for side in range(2):
                columns = pl.ds((2 * j + side) * LANES, LANES)
                part = pair[:, side * TILE : (side + 1) * TILE, :].reshape(-1, LANES)
                cur[rows, columns] = part
                low[rows, columns] = part.astype(BF16)

        def load_mlp():
            for j in range(4):
                load(pl.ds(0, 256), j, r.slabs_mlp[:, pl.ds(j * 16, 16), :].astype(F32))

        def load_sq():
            for to in range(4):
                pair = r.slabs_sq[0, :, to].astype(F32)
                for plane in range(1, 4):
                    pair = pair + r.slabs_sq[plane, :, to].astype(F32)
                load(pl.ds(to * 64, 64), 0, pair)

        def run(slabs, fetch, result, tiles):
            pltpu.make_async_copy(slabs, slabs, r.own_recv.at[0]).wait()
            fetch()
            scale = 1.0
            for turn, shift in enumerate(SHIFTS):
                whole = low[:, 0 : tiles * LANES]
                off = dot(whole, whole, NT)
                if turn == 0:
                    norm = jnp.sum(jnp.sum(jnp.where(diagonal, off, 0.0), axis=0, keepdims=True), axis=1, keepdims=True)
                    scale = 1.0 / (jnp.sqrt(norm) + 1e-07)
                    off = off * (scale * scale)
                if shift:
                    off = off - jnp.where(diagonal, shift, 0.0)
                off_low = off.astype(BF16)
                poly = (COEF_B + 2.0 * COEF_C * shift) * off + COEF_C * dot(off_low, off_low)
                poly = poly.astype(BF16)
                keep = COEF_A + shift * (COEF_B + COEF_C * shift)
                for j in range(tiles // 2):
                    columns = pl.ds(j * 2 * LANES, 2 * LANES)
                    now = keep * cur[:, columns] + dot(poly, low[:, columns])
                    if turn == 0:
                        now = now * scale
                    if turn < len(SHIFTS) - 1:
                        cur[:, columns] = now
                        low[:, columns] = now.astype(BF16)
                    else:
                        parts = [now[:, side * LANES : (side + 1) * LANES].reshape(32, TILE, LANES) for side in range(2)]
                        result[:, pl.ds(j * 16, 16), :] = jnp.concatenate(parts, axis=1).astype(result.dtype)

        mine_mlp = jnp.logical_or(self.me == OWNERS[0], self.me == OWNERS[1])
        mine_sq = self.me < 0
        for device in OWNERS[2:]:
            mine_sq = jnp.logical_or(mine_sq, self.me == device)

        @pl.when(mine_mlp)
        def _():
            run(r.slabs_mlp, load_mlp, r.result_mlp, 8)

        @pl.when(mine_sq)
        def _():
            run(r.slabs_sq, load_sq, r.result_sq, 2)

    def landing(self, index):
        if index < 2:
            return self.r.back_mlp.at[index]
        return self.r.back_sq.at[index - 2]

    def give_back(self, index, device):
        result = self.result(index)
        return link(
            result.at[device], self.landing(index),
            self.r.back_send.at[device], self.r.back_recv.at[index], device,
        )

    def give_all(self):
        r = self.r
        for index in range(7):
            result = self.result(index)

            @pl.when(self.me == OWNERS[index])
            def _():
                def send_one(step, _):
                    self.give_back(index, step + (step + 32 - self.me) // 32).start()
                    return 0

                lax.fori_loop(0, 31, send_one, 0)
                pltpu.make_async_copy(result.at[self.me], self.landing(index), r.back_recv.at[index]).start()

    def take_all(self):
        for index in range(7):
            result = self.result(index)
            pltpu.make_async_copy(result.at[0], self.landing(index), self.r.back_recv.at[index]).wait()
        for index in range(2):
            rows = pl.ds(index * MLP_ROWS, MLP_ROWS)
            self.r.out[2, rows, :] = self.r.back_mlp[index].astype(F32)
        for index in range(5):
            self.r.out[2, pl.ds(SQ_AT[index], SQ_ROWS), :] = self.r.back_sq[index].astype(F32)

    def drain(self):
        for k in range(len(CHUNKS)):
            self.core(k).wait_send()
            self.plane(k, True).wait_send()
            self.plane(k, False).wait_send()
            for step in range(3):
                self.along_z(k, step).wait_send()
        for part in range(len(PARTS_OUT)):

            @pl.when(self.me != OWNERS[PARTS_OUT[part][1]])
            def _():
                self.to_owner(part).wait_send()

    def drain_owner(self):
        for index in range(7):

            @pl.when(self.me == OWNERS[index])
            def _():
                def wait_one(step, _):
                    self.give_back(index, step + (step + 32 - self.me) // 32).wait_send()
                    return 0

                lax.fori_loop(0, 31, wait_one, 0)


def greet_all():
    me, z, y, x, c = place()
    greet(device_at(z, y, x, 1 - c))
    greet(device_at(z, y, 1 - x, c))
    greet(device_at(z, 1 - y, x, c))
    for step in range(1, 4):
        greet(device_at((z + step) % 4, y, x, c))
    owner = me < 0
    for device in OWNERS:
        owner = jnp.logical_or(owner, me == device)

        @pl.when(me != device)
        def _():
            greet(device)

    @pl.when(owner)
    def _():
        def greet_other(step, _):
            greet((me + step) % 32)
            return 0

        lax.fori_loop(1, 32, greet_other, 0)

    is_owner = owner.astype(jnp.int32)
    return 6 + 7 - is_owner + 31 * is_owner


def block_kernel(names, remote, *args):
    r = Refs(zip(names, args))
    keys, samples = r.obs.shape[0], r.obs.shape[1]
    tokens, width = r.acts.shape
    head_dim, half, per = width // HEADS, width // 2, ROWS // ACT
    wide = r.mlp_all.shape[2]
    groups = samples // GROUP
    in_sems, out_sems = r.in_sems, r.out_sems

    if remote:
        own = (r.sqw_v, r.mlpw_v, r.gain_v)
    else:
        own = (r.sq_all, r.mlp_all, r.gain_all)
    loads = list(zip((r.sqw, r.mlpw, r.gain), own))
    loads += [(r.acts, r.acts_v), (r.obs, r.obs_v.at[pl.ds(0, keys)]), (r.cot, r.cot_v)]
    if remote:
        loads += [(r.sqm, r.sqm_v), (r.mlpm, r.mlpm_v)]
    loads += [(r.flags, r.flags_s), (r.levels, r.levels_s)]
    copies = [pltpu.make_async_copy(a, b, in_sems.at[i]) for i, (a, b) in enumerate(loads)]

    def arrive(*which):
        for i in which:
            copies[i].wait()

    for copy in copies:
        copy.start()
    if remote:
        gather, update = Gather(r), Update(r)
        expected = greet_all()
        arrive(0, 2)
        gather.fill(True)
        pl.semaphore_wait(pltpu.get_barrier_semaphore(), expected)
        gather.first(5, 6, 4)
        arrive(1)
        gather.fill(False)
        gather.first(0, 1, 2, 3)

    arrive(3)

    def hats(i, _):
        rows = pl.ds(pl.multiple_of(i * ROWS, ROWS), ROWS)
        hat, scale = normalize(r.acts_v[rows, :])
        r.xhat[rows, :] = hat
        r.rstd[rows, :] = scale
        return 0

    lax.fori_loop(0, tokens // ROWS, hats, 0)

    mem, obs_v = r.mem, r.obs_v
    batch = 16
    chunks = KEYS_PAD // batch
    swap = r.swap
    row = lax.broadcasted_iota(jnp.int32, swap.shape, 0)
    column = lax.broadcasted_iota(jnp.int32, swap.shape, 1)
    swap[...] = jnp.where(column == (row % batch) * batch + row // batch, 1.0, 0.0).astype(BF16)

    def turn(part, low, high):
        def one(j, _):
            at = pl.ds(pl.multiple_of(j * batch, batch), batch)
            here = pl.ds(part * batch, batch)
            block = obs_v[at, here, :].reshape(batch * batch, width)
            mem[here, at, :] = dot(swap[...], block).astype(BF16).reshape(batch, batch, width)
            return 0

        lax.fori_loop(low, high, one, 0, unroll=high - low)

    whole = chunks - 1
    arrive(4)
    turn(0, 0, whole // 2)
    if remote:
        gather.second(5, 6)
    turn(0, whole // 2, whole)
    if remote:
        gather.third(5, 6)
    turn(1, 0, whole // 2)
    if remote:
        gather.second(4, 0, 1)
        gather.fourth(5, 6)
    turn(1, whole // 2, whole)
    if remote:
        gather.second(2, 3)
    arrive(len(copies) - 1, len(copies) - 2)
    freqs = jnp.exp(
        lax.broadcasted_iota(jnp.int32, (1, half), 1).astype(F32) * F32(-math.log(10000.0)) / half
    )
    for s in range(samples):
        r.angle[s : s + 1, :] = r.levels_s[s].astype(F32) * freqs
    r.embed[:, 0:half] = jnp.sin(r.angle[...]).astype(BF16)
    r.embed[:, half:width] = jnp.cos(r.angle[...]).astype(BF16)
    if remote:
        arrive(6, 7)
        update.old_moment()
        gather.third(4, 0, 1)
        gather.last(5, 6)
        for m in range(3):
            gather.unpack(SQ_AT[m], 1, r.sq_all, m)
        gather.unpack_gains()
    else:
        arrive(0, 1, 2)

    sq, mlp = r.sq_all, r.mlp_all
    wkh, wvh = r.wkh, r.wvh
    lane = lax.broadcasted_iota(jnp.int32, (width, width), 1)

    def split_heads(out, weight):
        weight = weight.astype(F32)
        for h in range(HEADS):
            out[pl.ds(h * width, width), :] = jnp.where(lane // head_dim == h, weight, 0.0).astype(BF16)

    split_heads(wkh, sq[2])
    g1, g2 = r.gain_all[0:1, :], r.gain_all[1:2, :]

    obs_v[keys] = dot(r.embed[...], sq[0]).astype(BF16)
    obs_v[keys + 1 :] = jnp.zeros((KEYS_PAD - keys - 1, samples, width), BF16)
    for part in range(samples // batch):
        turn(part, whole, chunks)

    sides, weights = r.sides_v, r.pds_v

    def make_queries(i, _):
        rows = pl.ds(pl.multiple_of(i * ROWS, ROWS), ROWS)
        first = (r.xhat[rows, :] * g1).astype(BF16)
        r.first[rows, :] = first
        q = dot(first, sq[1]).astype(BF16)
        r.query[rows, :] = q
        here = pl.ds(i * per, per)
        for h in range(HEADS):
            wk = wkh[pl.ds(h * width, width), :]
            value = (dot(q, wk, NT) * 0.125).astype(BF16).reshape(per, ACT, width)
            sides[here, pl.ds((HEADS + h) * ACT, ACT), :] = value
        return 0

    lax.fori_loop(0, tokens // ROWS, make_queries, 0)

    key = lax.broadcasted_iota(jnp.int32, (1, KEYS_PAD), 1)
    low_rows, high_rows = pl.ds(0, HEADS * ACT), pl.ds(HEADS * ACT, HEADS * ACT)

    def attend(g, _):
        ids = [g * GROUP + k for k in range(GROUP)]
        scores = [dot(sides[s, high_rows, :], mem[s], NT) for s in ids]
        lows = []
        for s, score in zip(ids, scores):
            count = OBS_FEW + (OBS_FULL - OBS_FEW) * r.flags_s[s]
            score = score + jnp.where((key < count) | (key == OBS_FULL), 0.0, -1000000000.0)
            expo = jnp.exp(score - jnp.max(score, -1, keepdims=True))
            probs = expo * (1.0 / jnp.sum(expo, -1, keepdims=True))
            r.probs[s] = probs
            low = probs.astype(BF16)
            weights[s, low_rows, :] = low
            lows.append(low)
        for s, low in zip(ids, lows):
            u = dot(low, mem[s]).astype(BF16)
            rows = pl.ds(pl.multiple_of(s * ACT, ACT), ACT)
            for h in range(HEADS):
                r.u[rows, pl.ds(h * width, width)] = u[h * ACT : (h + 1) * ACT, :]
        return 0

    lax.fori_loop(0, groups // 2, attend, 0)
    if remote:
        gather.third(2, 3)
        gather.fourth(4, 0, 1)
    lax.fori_loop(groups // 2, groups, attend, 0)
    if remote:
        gather.fourth(2, 3)
        gather.last(4)
        for m in range(3, 5):
            gather.unpack(SQ_AT[m], 1, sq, m)
    split_heads(wvh, sq[3])

    gain_acc = r.gain_acc
    gain_acc[...] = jnp.zeros_like(gain_acc)
    blocks = [pl.ds(i * ROWS, ROWS) for i in range(tokens // ROWS)]
    for rows in blocks:
        mixed = dot(r.u[rows, :], wvh[...]).astype(BF16)
        r.mixed[rows, :] = mixed
        resid = r.acts_v[rows, :] + dot(mixed, sq[4])
        r.resid[rows, :] = resid
        hat, scale = normalize(resid)
        r.hat_two[rows, :] = hat
        r.rstd_two[rows, :] = scale
        r.second[rows, :] = (hat * g2).astype(BF16)
    arrive(5)
    r.out_low[...] = r.cot_v[...].astype(BF16)
    if remote:
        gather.last(0, 1)
        gather.unpack(0, 4, mlp, 0)
    wide_blocks = [pl.ds(c * 256, 256) for c in range(wide // 256)]
    for rows in blocks:
        for columns in wide_blocks:
            v = dot(r.second[rows, :], mlp[0, :, columns])
            square = v * v
            t = jnp.tanh(0.7978845608 * (v + 0.044715 * square * v))
            r.active[rows, columns] = (0.5 * v * (1.0 + t)).astype(BF16)
            slope = 0.5 * (1.0 + t) + 0.5 * v * (1.0 - t * t) * (0.7978845608 * (1.0 + 0.134145 * square))
            r.slope[rows, columns] = slope

    grads = r.grads

    def put(base, tiles, value):
        for j in range(tiles):
            part = value[:, j * LANES : (j + 1) * LANES].reshape(GRID + (TILE, LANES))
            grads[:, :, :, :, pl.ds(base + j * TILE, TILE), :] = part

    def by_head(left, right):
        turned = left.T
        parts = [
            dot(turned[h * head_dim : (h + 1) * head_dim, :], right[:, pl.ds(h * width, width)])
            for h in range(HEADS)
        ]
        return jnp.concatenate(parts, axis=0).T

    put(MLP_ROWS, 8, dot(r.out_low[...], r.active[...], TN))
    if remote:
        update.start(2)
        update.start(3)
        gather.last(2, 3)
        gather.unpack(MLP_ROWS, 4, mlp, 1)
    for rows in blocks:
        for columns in wide_blocks:
            slope = r.slope[rows, columns]
            r.dhidden[rows, columns] = (slope * dot(r.out_low[rows, :], mlp[1, :, columns])).astype(BF16)
    put(0, 8, dot(r.second[...], r.dhidden[...], TN))
    if remote:
        update.start(0)
        update.start(1)
        update.one(2, 3)
    for i, rows in enumerate(blocks):
        r.out_v[rows, :] = r.resid[rows, :] + dot(r.active[rows, :], mlp[1], NT)
        grad_second = dot(r.dhidden[rows, :], mlp[0], NT)
        hat = r.hat_two[rows, :]
        gain_acc[1:2, :] += jnp.sum(grad_second * hat, 0, keepdims=True)
        dres = r.cot_v[rows, :] + norm_back(grad_second * g2, hat, r.rstd_two[rows, :])
        r.dres[rows, :] = dres
        low = dres.astype(BF16)
        r.dres_low[rows, :] = low
        gm = dot(low, sq[4], NT).astype(BF16)
        r.dmixed[rows, :] = gm
        here = pl.ds(i * per, per)
        for h in range(HEADS):
            wv = wvh[pl.ds(h * width, width), :]
            sides[here, pl.ds(h * ACT, ACT), :] = dot(gm, wv, NT).astype(BF16).reshape(per, ACT, width)
    keep_out = pltpu.make_async_copy(r.out_v, r.output, out_sems.at[0])
    keep_out.start()
    if remote:
        update.one(0, 1)
    put(SQ_AT[4], 2, dot(r.mixed[...], r.dres_low[...], TN))
    put(SQ_AT[3], 2, by_head(r.dmixed[...], r.u))
    if remote:
        update.start(4)

    def attend_back(g, _):
        ids = [g * GROUP + k for k in range(GROUP)]
        rises = [dot(sides[s, low_rows, :], mem[s], NT) for s in ids]
        for s, rise in zip(ids, rises):
            probs = r.probs[s]
            both = probs * rise
            weights[s, high_rows, :] = (both - probs * jnp.sum(both, -1, keepdims=True)).astype(BF16)
        for s in ids:
            dq = (dot(weights[s, high_rows, :], mem[s]) * 0.125).astype(BF16)
            rows = pl.ds(pl.multiple_of(s * ACT, ACT), ACT)
            for h in range(HEADS):
                r.dq_wide[rows, pl.ds(h * width, width)] = dq[h * ACT : (h + 1) * ACT, :]
            end = dot(weights[s, :, LANES:KEYS_PAD], sides[s], TN)
            r.stamps[s] = end[64:72, :]
        return 0

    lax.fori_loop(0, groups // 2, attend_back, 0)
    if remote:
        update.two(2, 3)
        update.one(4)
        update.two(0, 1)
    lax.fori_loop(groups // 2, groups, attend_back, 0)
    if remote:
        update.three(2, 3)
        update.two(4)
    put(SQ_AT[2], 2, by_head(r.query[...], r.dq_wide))
    stamp_low = r.stamps[:, 4:5, :].reshape(samples, width).astype(BF16)
    put(SQ_AT[0], 2, dot(r.embed[...], stamp_low, TN))
    if remote:
        update.start(5)
        update.three(0, 1)

    def memory_back(low, high):
        for s in range(2 * low, 2 * high):
            mem[s] = dot(weights[s], sides[s], TN).astype(BF16)

    def keep_og(part):
        here = pl.ds(part * batch, batch)
        return pltpu.make_async_copy(obs_v.at[pl.ds(0, keys), here], r.og.at[:, here], out_sems.at[2 + part])

    def turn_back(part, low, high):
        def one(j):
            at = pl.ds(pl.multiple_of(j * batch, batch), batch)
            here = pl.ds(part * batch, batch)
            block = mem[here, at, :].reshape(batch * batch, width)
            value = dot(swap[...], block).astype(BF16).reshape(batch, batch, width)
            obs_v[at, here, :] = value

        for j in range(low, high):
            one(j)
        if high == chunks:
            keep_og(part).start()

    def queries_back(i, _):
        rows = pl.ds(pl.multiple_of(i * ROWS, ROWS), ROWS)
        r.dquery[rows, :] = dot(r.dq_wide[rows, :], wkh[...]).astype(BF16)
        return 0

    lax.fori_loop(0, tokens // ROWS, queries_back, 0)
    put(SQ_AT[1], 2, dot(r.first[...], r.dquery[...], TN))
    if remote:
        update.start(6)
        update.one(5)

    def acts_back(i, _):
        rows = pl.ds(pl.multiple_of(i * ROWS, ROWS), ROWS)
        grad_first = dot(r.dquery[rows, :], sq[1], NT)
        hat = r.xhat[rows, :]
        gain_acc[0:1, :] += jnp.sum(grad_first * hat, 0, keepdims=True)
        r.ag_v[rows, :] = r.dres[rows, :] + norm_back(grad_first * g1, hat, r.rstd[rows, :])
        return 0

    def finish_acts():
        lax.fori_loop(0, tokens // ROWS, acts_back, 0)
        for norm in range(2):
            for j in range(2):
                row = gain_acc[norm : norm + 1, j * LANES : (j + 1) * LANES]
                at = GAIN_BASE + norm * 2 + j
                value = jnp.broadcast_to(row.reshape(1, 1, 1, 1, 1, LANES), GRID + (1, LANES))
                grads[:, :, :, :, at : at + 1, :] = value
        rest = WIRE - GAIN_BASE - 4
        grads[:, :, :, :, GAIN_BASE + 4 : WIRE, :] = jnp.zeros(GRID + (rest, LANES), F32)

    keep_ag = pltpu.make_async_copy(r.ag_v, r.ag, out_sems.at[1])
    if remote:
        pairs = samples // 2
        finish_acts()
        keep_ag.start()
        update.start(7)
        update.one(6)
        update.three(4)
        memory_back(0, 6)
        update.four(2, 3)
        update.two(5)
        update.one(7)
        update.two(6)
        memory_back(6, 11)
        update.four(0, 1)
        update.three(5)
        update.two(7)
        update.three(6)
        memory_back(11, pairs)
        update.three(7)
        update.orthogonalize()
        update.give_all()
        turn_back(0, 0, chunks // 2)
        turn_back(0, chunks // 2, chunks)
        update.four(4, 5, 6)
        turn_back(1, 0, chunks)
        update.four(7)
        out = r.out
        out[1, :, :] = r.moment[...]
        out[2, pl.ds(GAIN_BASE, 16), :] = jnp.zeros((16, LANES), F32)
        gather.drain()
        update.drain()
        update.take_all()
        update.drain_owner()
    else:
        finish_acts()
        keep_ag.start()
        memory_back(0, samples // 2)
        for part in range(samples // batch):
            turn_back(part, 0, chunks)
    for copy in (keep_out, keep_ag, *(keep_og(part) for part in range(samples // batch))):
        copy.wait()


def block_and_back(remote, acts, obs, flags, levels, cot, sqw, mlpw, gain, sqm=None, mlpm=None):
    tokens, width = acts.shape
    keys, samples = obs.shape[0], obs.shape[1]
    rows = HEADS * ACT
    wide = mlpw.shape[2]
    any_space = pl.BlockSpec(memory_space=pl.ANY)
    in_vmem = pl.BlockSpec(memory_space=VMEM)
    sem = pltpu.SemaphoreType.DMA
    ins = dict(flags=flags, levels=levels, acts=acts, obs=obs, cot=cot, sqw=sqw, mlpw=mlpw, gain=gain)
    outs = dict(
        output=jax.ShapeDtypeStruct(acts.shape, F32),
        ag=jax.ShapeDtypeStruct(acts.shape, F32),
        og=jax.ShapeDtypeStruct(obs.shape, BF16),
    )
    grads = GRID + (WIRE, LANES)
    scratch = dict(
        obs_v=VMEM((KEYS_PAD, samples, width), BF16),
        acts_v=VMEM(acts.shape, F32),
        cot_v=VMEM(acts.shape, F32),
        mem=VMEM((samples, KEYS_PAD, width), BF16),
        swap=VMEM((256, 256), BF16),
        sq_all=VMEM((5, width, width), BF16),
        mlp_all=VMEM((2, width, wide), BF16),
        gain_all=VMEM((2, width), F32),
        wkh=VMEM((HEADS * width, width), BF16),
        wvh=VMEM((HEADS * width, width), BF16),
        first=VMEM((tokens, width), BF16),
        query=VMEM((tokens, width), BF16),
        xhat=VMEM((tokens, width), F32),
        rstd=VMEM((tokens, 1), F32),
        probs=VMEM((samples, rows, KEYS_PAD), F32),
        pds_v=VMEM((samples, 2 * rows, KEYS_PAD), BF16),
        sides_v=VMEM((samples, 2 * rows, width), BF16),
        u=VMEM((tokens, HEADS * width), BF16),
        dq_wide=VMEM((tokens, HEADS * width), BF16),
        mixed=VMEM((tokens, width), BF16),
        second=VMEM((tokens, width), BF16),
        active=VMEM((tokens, wide), BF16),
        dhidden=VMEM((tokens, wide), BF16),
        out_low=VMEM((tokens, width), BF16),
        dres_low=VMEM((tokens, width), BF16),
        dres=VMEM((tokens, width), F32),
        resid=VMEM((tokens, width), F32),
        hat_two=VMEM((tokens, width), F32),
        rstd_two=VMEM((tokens, 1), F32),
        slope=VMEM((tokens, wide), F32),
        dmixed=VMEM((tokens, width), BF16),
        dquery=VMEM((tokens, width), BF16),
        out_v=VMEM((tokens, width), F32),
        ag_v=VMEM((tokens, width), F32),
        angle=VMEM((samples, width // 2), F32),
        embed=VMEM((samples, width), BF16),
        stamps=VMEM((samples, 8, width), F32),
        gain_acc=VMEM((8, width), F32),
        flags_s=pltpu.SMEM(flags.shape, jnp.int32),
        levels_s=pltpu.SMEM(levels.shape, jnp.int32),
        in_sems=sem((10,)),
        out_sems=sem((2 + samples // 16,)),
    )
    extra = {}
    if remote:
        ins.update(sqm=sqm, mlpm=mlpm)
        outs.update(out=jax.ShapeDtypeStruct((3, WIRE, LANES), F32))
        chunks = len(CHUNKS)
        scratch.update(
            grads=VMEM(grads, F32),
            sqw_v=VMEM(sqw.shape, F32),
            mlpw_v=VMEM(mlpw.shape, F32),
            gain_v=VMEM(gain.shape, F32),
            sqm_v=VMEM(sqm.shape, F32),
            mlpm_v=VMEM(mlpm.shape, F32),
            wire=VMEM(grads, BF16),
            edge=VMEM((16, LANES), F32),
            gsend=sem((len(PIECES), 6)),
            grecv=sem((len(PIECES), 6)),
            send0=VMEM((4, 2, 2, WIRE, LANES), BF16),
            got_core=VMEM((4, 2, 2, WIRE, LANES), BF16),
            sum1=VMEM((4, 2, 2, WIRE, LANES), F32),
            send1=VMEM((4, 2, WIRE, LANES), BF16),
            got1=VMEM((4, 2, WIRE, LANES), BF16),
            sum2=VMEM((4, 2, WIRE, LANES), F32),
            send2=VMEM((4, WIRE, LANES), BF16),
            got2=VMEM((4, WIRE, LANES), BF16),
            sum3=VMEM((4, WIRE, LANES), F32),
            send3=VMEM((4, WIRE, LANES), BF16),
            got3=VMEM((3, WIRE, LANES), BF16),
            moment=VMEM((WIRE, LANES), F32),
            slabs_sq=VMEM((4, 8, 4, SQ_ROWS, LANES), BF16),
            slabs_mlp=VMEM((32, MLP_ROWS, LANES), BF16),
            moment_low=VMEM((2 * MLP_ROWS, LANES), BF16),
            back_mlp=VMEM((2, MLP_ROWS, LANES), BF16),
            back_sq=VMEM((5, SQ_ROWS, LANES), BF16),
            result_sq=VMEM((32, SQ_ROWS, LANES), BF16),
            result_mlp=VMEM((32, MLP_ROWS, LANES), BF16),
            cur=VMEM((width, wide), F32),
            cur_low=VMEM((width, wide), BF16),
            send=sem((chunks, 6)),
            recv=sem((chunks, 6)),
            own_send=sem((len(PARTS_OUT),)),
            own_recv=sem((1,)),
            back_send=sem((32,)),
            back_recv=sem((7,)),
        )
        extra = dict(collective_id=0, has_side_effects=True)
        outs = {name: VMEM(like.shape, like.dtype) for name, like in outs.items()}
    else:
        outs.update(grads=jax.ShapeDtypeStruct(grads, F32))
    names = tuple(ins) + tuple(outs) + tuple(scratch)
    stay = [pltpu.with_memory_space_constraint(value, pltpu.HBM) for value in ins.values()]
    results = pl.pallas_call(
        functools.partial(block_kernel, names, remote),
        out_shape=tuple(outs.values()),
        in_specs=[any_space] * len(ins),
        out_specs=[any_space] * 3 + [in_vmem],
        scratch_shapes=list(scratch.values()),
        compiler_params=pltpu.CompilerParams(vmem_limit_bytes=52 << 20, **extra),
        name="block_and_back",
    )(*stay)
    return Refs(zip(outs, results))


PARTS = 14


def finish_kernel(names, rate, *args):
    r = Refs(zip(names, args))
    sems = r.sems
    keys = r.og.shape[0]
    step = keys // PARTS

    def leave(part):
        block = pl.ds(part * step, step)
        return pltpu.make_async_copy(r.og_v.at[block], r.og.at[block], sems.at[part])

    more = PARTS
    moves = []
    if hasattr(r, "wire"):
        pairs = [(r.sqw, r.sqw_v), (r.mlpw, r.mlpw_v), (r.gain, r.gain_v), (r.gainm, r.gainm_v)]
        pairs += [(r.output, r.output_f), (r.ag, r.ag_f)]
        for source, target in pairs:
            moves.append(pltpu.make_async_copy(source, target, sems.at[more]))
            moves[-1].start()
            more += 1
    for part in range(PARTS):

        def widen(j, _):
            r.og_v[j] = r.low[j].astype(F32)
            return 0

        lax.fori_loop(part * step, (part + 1) * step, widen, 0, unroll=4)
        leave(part).start()
    for copy in moves[:4]:
        copy.wait()
    if hasattr(r, "wire"):
        finish_weights(r, rate)
    for part in range(PARTS):
        leave(part).wait()
    for copy in moves[4:]:
        copy.wait()


def finish_weights(r, rate):
    wire = r.wire
    me = lax.axis_index("dp")
    for m in range(5):
        for j in range(2):
            rows, columns = pl.ds(SQ_AT[m] + j * TILE, TILE), pl.ds(j * LANES, LANES)
            r.sqg[m, :, columns] = wire[0, rows, :]
            r.sqm[m, :, columns] = wire[1, rows, :]
            r.sqn[m, :, columns] = r.sqw_v[m, :, columns] - SQ_RATES[m] * wire[2, rows, :]
    r.sqc[...] = r.sqn[...].astype(BF16)
    for m in range(2):
        for j in range(8):
            rows, columns = pl.ds(m * MLP_ROWS + j * TILE, TILE), pl.ds(j * LANES, LANES)
            r.mlpg[m, :, columns] = wire[0, rows, :]
            r.mlpm[m, :, columns] = wire[1, rows, :]
            r.mlpn[m, :, columns] = r.mlpw_v[m, :, columns] - MLP_RATES[m] * wire[2, rows, :]
    r.mlpc[...] = r.mlpn[...].astype(BF16)
    tile = wire[0, pl.ds(GAIN_BASE, TILE), :]
    turned = pltpu.roll(tile, (LANES - (me % 16) * TILE) % LANES, 1)
    at = me // 16
    for norm in range(2):
        pair = turned[2 * norm : 2 * norm + 2, 0:TILE]
        row = jnp.where(at == 0, pair[0:1, :], pair[1:2, :])
        new = 0.5 * r.gainm_v[norm : norm + 1, :] + row
        r.gg[norm : norm + 1, :] = row
        r.gm[norm : norm + 1, :] = new
        r.gn[norm : norm + 1, :] = r.gain_v[norm : norm + 1, :] - rate * new


def finish(rate, made, sqw=None, mlpw=None, gain=None, gainm=None):
    any_space = pl.BlockSpec(memory_space=pl.ANY)
    in_vmem = pl.BlockSpec(memory_space=VMEM)
    ins = dict(low=made.og)
    outs = dict(og=jax.ShapeDtypeStruct(made.og.shape, F32))
    near, far = 1, 1
    if hasattr(made, "out"):
        ins.update(output=made.output, ag=made.ag, wire=made.out, sqw=sqw, mlpw=mlpw, gain=gain, gainm=gainm)
        like = jax.ShapeDtypeStruct
        near, far = 4, 3
        outs.update(
            output_f=like(made.output.shape, F32),
            ag_f=like(made.ag.shape, F32),
            sqg=like(sqw.shape, F32),
            sqm=like(sqw.shape, F32),
            sqn=like(sqw.shape, F32),
            sqc=like(sqw.shape, BF16),
            mlpg=like(mlpw.shape, F32),
            mlpm=like(mlpw.shape, F32),
            mlpn=like(mlpw.shape, F32),
            mlpc=like(mlpw.shape, BF16),
            gg=like(gain.shape, F32),
            gm=like(gain.shape, F32),
            gn=like(gain.shape, F32),
        )
    scratch = dict(
        og_v=VMEM(made.og.shape, F32),
        sems=pltpu.SemaphoreType.DMA((PARTS + 6,)),
    )
    if hasattr(made, "out"):
        scratch.update(
            sqw_v=VMEM(sqw.shape, F32),
            mlpw_v=VMEM(mlpw.shape, F32),
            gain_v=VMEM(gain.shape, F32),
            gainm_v=VMEM(gainm.shape, F32),
        )
    names = tuple(ins) + tuple(outs) + tuple(scratch)
    made_here = list(ins.values())
    stay = [pltpu.with_memory_space_constraint(value, pltpu.HBM) for value in made_here[near:]]
    results = pl.pallas_call(
        functools.partial(finish_kernel, names, rate),
        out_shape=tuple(outs.values()),
        in_specs=[in_vmem] * near + [any_space] * (len(ins) - near),
        out_specs=[any_space] * far + [in_vmem] * (len(outs) - far),
        scratch_shapes=list(scratch.values()),
        compiler_params=pltpu.CompilerParams(vmem_limit_bytes=16 << 20),
        name="finish",
    )(*made_here[:near], *stay)
    return Refs(zip(outs, results))


HIGH_PRECISION = lax.Precision.HIGHEST


def plain_orthogonalize(matrix):
    current = matrix / (jnp.sqrt(jnp.sum(matrix * matrix)) + 1e-07)
    for turn in range(5):
        gram = jnp.dot(current, current.T, precision=HIGH_PRECISION)
        poly = COEF_B * gram + COEF_C * jnp.dot(gram, gram, precision=HIGH_PRECISION)
        current = COEF_A * current + jnp.dot(poly, current, precision=HIGH_PRECISION)
    return current


def pick_owned(stack, owners, device):
    chosen = jnp.zeros_like(stack[0])
    for index in range(len(owners)):
        chosen = jnp.where(device == owners[index], stack[index], chosen)
    return chosen


def is_owner(owners, device):
    flag = device < 0
    for owner in owners:
        flag = jnp.logical_or(flag, device == owner)
    return flag


def from_wire(grads):
    def matrix(base, tiles):
        part = grads[:, base : base + tiles * TILE, :].reshape(-1, tiles, TILE, LANES)
        return part.transpose(0, 2, 1, 3).reshape(-1, tiles * LANES)

    square = jnp.stack([matrix(SQ_AT[m], 2) for m in range(5)])
    mlp = jnp.stack([matrix(m * MLP_ROWS, 8) for m in range(2)])
    return square, mlp, grads[0, GAIN_BASE : GAIN_BASE + 4, :].reshape(2, 2 * LANES)


def update_by_collectives(
    grads, square_weights, mlp_weights, gains, square_moment, mlp_moment, gain_moment, rate
):
    square_local, mlp_local, gain_local = from_wire(grads)
    square_grad, mlp_grad, gain_grad = (
        lax.psum_scatter(square_local, "dp", scatter_dimension=1, tiled=True),
        lax.psum_scatter(mlp_local, "dp", scatter_dimension=1, tiled=True),
        lax.psum_scatter(gain_local, "dp", scatter_dimension=1, tiled=True),
    )
    square_moment_new = 0.5 * square_moment + square_grad
    mlp_moment_new = 0.5 * mlp_moment + mlp_grad
    gain_moment_new = 0.5 * gain_moment + gain_grad
    device = lax.axis_index("dp")
    count = lax.axis_size("dp")
    square_owners = [index * count // 7 for index in range(5)]
    mlp_owners = [(index + 5) * count // 7 for index in range(2)]
    square_full, mlp_full = (
        lax.all_gather(square_moment_new, "dp", axis=1, tiled=True),
        lax.all_gather(mlp_moment_new, "dp", axis=1, tiled=True),
    )
    mine_square = pick_owned(square_full, square_owners, device)
    mine_mlp = pick_owned(mlp_full, mlp_owners, device)
    made_square = lax.cond(
        is_owner(square_owners, device), plain_orthogonalize, jnp.zeros_like, mine_square
    )
    made_mlp = lax.cond(is_owner(mlp_owners, device), plain_orthogonalize, jnp.zeros_like, mine_mlp)
    stack_square = jnp.stack(
        [jnp.where(device == owner, made_square, 0.0) for owner in square_owners]
    )
    stack_mlp = jnp.stack([jnp.where(device == owner, made_mlp, 0.0) for owner in mlp_owners])
    square_ortho, mlp_ortho = (
        lax.psum_scatter(stack_square, "dp", scatter_dimension=1, tiled=True),
        lax.psum_scatter(stack_mlp, "dp", scatter_dimension=1, tiled=True),
    )
    square_new = square_weights - jnp.array(SQ_RATES, F32)[:, None, None] * square_ortho
    mlp_new = mlp_weights - jnp.array(MLP_RATES, F32)[:, None, None] * mlp_ortho
    gains_new = gains - rate * gain_moment_new
    return (
        square_grad,
        square_moment_new,
        square_new,
        square_new.astype(BF16),
        mlp_grad,
        mlp_moment_new,
        mlp_new,
        mlp_new.astype(BF16),
        gain_grad,
        gain_moment_new,
        gains_new,
    )


def per_device(
    actions,
    observed,
    camera_flags,
    noise_levels,
    cotangent,
    square_weights,
    mlp_weights,
    gains,
    square_moment,
    mlp_moment,
    gain_moment,
):
    count = lax.axis_size("dp")
    rate = 0.1 / math.sqrt(actions.shape[0] * count)
    by_key = observed.transpose(1, 0, 2)
    ins = (actions, by_key, camera_flags, noise_levels, cotangent)
    if count == math.prod(GRID):
        made = block_and_back(True, *ins, square_weights, mlp_weights, gains, square_moment, mlp_moment)
        done = finish(rate, made, square_weights, mlp_weights, gains, gain_moment)
        output, actions_grad = done.output_f, done.ag_f
        d = done
        rest = (d.sqg, d.sqm, d.sqn, d.sqc, d.mlpg, d.mlpm, d.mlpn, d.mlpc, d.gg, d.gm, d.gn)
    else:
        square_all, mlp_all = (
            lax.all_gather(square_weights.astype(BF16), "dp", axis=1, tiled=True),
            lax.all_gather(mlp_weights.astype(BF16), "dp", axis=1, tiled=True),
        )
        gain_all = lax.all_gather(gains, "dp", axis=1, tiled=True)
        made = block_and_back(False, *ins, square_all, mlp_all, gain_all)
        done = finish(rate, made)
        output, actions_grad = made.output, made.ag
        grads = made.grads.reshape(-1, WIRE, LANES)
        rest = update_by_collectives(
            grads, square_weights, mlp_weights, gains, square_moment, mlp_moment, gain_moment, rate
        )
    observed_grad = done.og.transpose(1, 0, 2)
    return (output, actions_grad, observed_grad) + tuple(rest)


def solution(mesh):
    rows, cube, flat = P("dp", None), P("dp", None, None), P("dp")
    stacked, pair = P(None, "dp", None), P(None, "dp")
    return jax.shard_map(
        per_device,
        mesh=mesh,
        in_specs=(rows, cube, flat, flat, rows, stacked, stacked, pair, stacked, stacked, pair),
        out_specs=(rows, rows, cube) + (stacked,) * 8 + (pair,) * 3,
        check_vma=False,
    )
```
